32 devices in a mesh: replica: 16 (over z, y, x), tensor: 2 (over core).
Axes of the slice: x: 2, y: 2, z: 4, core: 2. Of those that a mesh axis runs over, the one named last changes fastest.
Arguments:
- hidden: bfloat16 [512, 1536], P(('replica', 'tensor')), may hold values from -6 to 6
- attn_gain: float32 [1536], replicated, may hold values from 0.25 to 1.75
- w_query: bfloat16 [1536, 1536], P(None, 'tensor'), may hold values from -0.625 to 0.625
- w_keyvalue: bfloat16 [1536, 8, 128], P(None, 'tensor'), may hold values from -0.4375 to 0.4375
- w_output: bfloat16 [1536, 1536], P('tensor'), may hold values from -0.625 to 0.625
- cache: bfloat16 [768, 128, 8, 128], P('replica', None, 'tensor')
- page_table: int32 [512, 16], P('replica'), may hold values from -1 to 79, as said below
- ctx_len: int32 [512], P('replica'), may hold values from 1 to 2048, as said below
- move_dest: int32 [128], P('replica'), may hold values from 0 to 15, as said below
- ffn_gain: float32 [1536], replicated, may hold values from 0.25 to 1.75
- router: bfloat16 [1536, 40], replicated, may hold values from -0.15625 to 0.15625
- routes: int32 [512, 8], P('replica'), may hold values from 0 to 39, all different within a row
- w_in: bfloat16 [1536, 2, 1024], P(None, None, 'tensor'), may hold values from -0.15625 to 0.15625
- w_down: bfloat16 [1024, 1536], P('tensor'), may hold values from -0.25 to 0.25
Outputs:
- attended: bfloat16 [512, 1536], P(('replica', 'tensor'))
- experts_out: bfloat16 [512, 1536], P(('replica', 'tensor'))
The draws below stay inside these ranges and needn't reach their ends.
Inputs may be any that keep to these rules, and one draw needn't show every extreme that they name: `move_dest`: replica r's 8 entries name where its pool rows 40 to 47 go, in order: 4 other replicas, 2 pages each, never r itself; one replica drawn from the seed receives pages from every other. `page_table`: row i holds request i's pages in order and -1 after its last page; each request has one page or more; every lent page is used by exactly one request of the replica it goes to, and no pool page twice. `ctx_len`: with n pages in its row, a request holds between (n - 1) * 128 + 1 and n * 128 cached tokens. `routes`: each row names 8 different experts.
All inputs are finite; a program needn't handle non-finite values.
Results may differ from the reference program's by a relative error of at most 0.02.
Values may be sent and summed in bfloat16 or wider, within the bound.
No kernel may reach another device: no remote copies, remote signals or barrier semaphores. Data moves between devices by JAX's collectives and lax.ppermute only.
A program may use at most 64 MiB of HBM per device.

```python
import math
import jax
import jax.numpy as jnp
from jax import lax

D = 1536
QHEADS = 24
KVHEADS = 8
HEAD_DIM = 64
EXPERTS = 40
TOPK = 8
FF = 512
WINDOW_EXPERTS = 2
PAGE = 128
MAXPAGES = 16
CAP = 2
REQ_REP = 32
LOCAL_PAGES = 40
FANOUT = 4
OUTGOING = 8
POOL = 48
REQS = 512


def overflow_plan(key):
    replicas = REQS // REQ_REP
    hottest = jax.random.randint(jax.random.fold_in(key, 11), (), 0, replicas)
    replica_ids = jnp.arange(replicas, dtype=jnp.int32)

    def one_source(sender):
        subkey = jax.random.fold_in(jax.random.fold_in(key, 12), sender)
        jitter = jax.random.randint(subkey, (replicas,), 0, 4096)
        scores = jitter * replicas + replica_ids + 1
        scores = jnp.where(replica_ids == hottest, 0, scores)
        scores = jnp.where(replica_ids == sender, 4097 * replicas + 1, scores)
        ranking = jnp.argsort(scores, stable=True)
        chosen = jnp.sort(ranking[:FANOUT])
        return jnp.repeat(chosen, CAP, total_repeat_length=FANOUT * CAP).astype(jnp.int32)
    return jax.vmap(one_source)(replica_ids)


def page_plan(key):
    replicas = REQS // REQ_REP
    layout = overflow_plan(key)
    out_slots = jnp.arange(OUTGOING, dtype=jnp.int32)
    earlier = (layout[:, None, :] == layout[:, :, None]) & (out_slots[None, None, :] < out_slots[None, :, None])
    order_rank = jnp.sum(earlier, axis=2).astype(jnp.int32)
    senders = jnp.arange(replicas, dtype=jnp.int32)[:, None]
    remote_value = (POOL + senders * CAP + order_rank).reshape(-1)
    remote_dest = layout.reshape(-1)
    candidates = replicas * OUTGOING + LOCAL_PAGES
    listing = jnp.concatenate([remote_value, jnp.arange(LOCAL_PAGES, dtype=jnp.int32)])

    def one_replica(replica):
        subkey = jax.random.fold_in(jax.random.fold_in(key, 13), replica)
        key_a, key_b, key_c, key_d = jax.random.split(subkey, 4)
        category = jnp.concatenate([jnp.where(remote_dest == replica, 0, 2).astype(jnp.int32), jnp.ones((LOCAL_PAGES,), jnp.int32)])
        jitter = jax.random.randint(key_a, (candidates,), 0, 4096)
        scores = category * 16777216 + jitter * 4096 + jnp.arange(candidates, dtype=jnp.int32)
        listed = listing[jnp.argsort(scores, stable=True)]
        available = LOCAL_PAGES + jnp.sum((remote_dest == replica).astype(jnp.int32))
        halving = jax.random.randint(key_b, (REQ_REP,), 0, 3)
        capacity = jnp.right_shift(jnp.full((REQ_REP,), MAXPAGES, jnp.int32), halving)
        shuffle = jax.random.permutation(key_c, REQ_REP)
        standing = jnp.argsort(shuffle)
        surplus = (capacity - 1)[shuffle]
        before = (jnp.cumsum(surplus) - surplus)[standing]
        slot_grid = jnp.arange(MAXPAGES, dtype=jnp.int32)[None, :]
        order_pos = jnp.where(slot_grid == 0, standing[:, None], REQ_REP + before[:, None] + slot_grid - 1)
        occupied = (slot_grid < capacity[:, None]) & (order_pos < available)
        slot_table = jnp.where(occupied, listed[jnp.clip(order_pos, 0, candidates - 1)], -1)
        page_count = jnp.sum(occupied.astype(jnp.int32), axis=1)
        last_fill = jax.random.randint(key_d, (REQ_REP,), 1, PAGE + 1)
        return (slot_table.astype(jnp.int32), ((page_count - 1) * PAGE + last_fill).astype(jnp.int32))
    tables, lengths = jax.vmap(one_replica)(jnp.arange(replicas, dtype=jnp.int32))
    return (tables.reshape(REQS, MAXPAGES), lengths.reshape(REQS))


def draw_move_dest(key, part):
    return overflow_plan(key).reshape(-1)


def draw_page_table(key, part):
    return page_plan(key)[0]


def draw_ctx_len(key, part):
    return page_plan(key)[1]


def draw_cache(key, part):
    replicas = REQS // REQ_REP
    array_shape = (replicas * POOL, PAGE, KVHEADS, 2 * HEAD_DIM)
    subkey = jax.random.fold_in(key, 14)
    key_a = jax.random.fold_in(subkey, 0)
    key_lane = jnp.arange(2 * HEAD_DIM) < HEAD_DIM
    spread = jnp.where(key_lane, 3.0, 1.0).astype(jnp.float32)
    normal_draw = jax.random.normal(key_a, array_shape, jnp.float32)
    return (normal_draw * spread).astype(jnp.bfloat16)


def levels(rng, extent, cuts, smallest, largest):
    def one(position, parts):
        steps = jax.random.uniform(jax.random.fold_in(jax.random.fold_in(rng, 6), position), (parts,), jnp.float32, smallest / len(cuts), largest / len(cuts))
        return jnp.repeat(jnp.exp(steps), extent[position] // parts).reshape((-1,) + (1,) * (len(extent) - position - 1))

    factor_of = one(*cuts[0])
    for cut in cuts[1:]:
        factor_of = factor_of * one(*cut)
    return factor_of


def picks_of(rng, rows, number_of, top, lift):
    sequence = jax.random.permutation(jax.random.fold_in(rng, 1), number_of)
    boost = sequence
    for power in range(3):
        boost = boost * boost // number_of
    boost = boost * lift // number_of
    lots = jax.random.randint(jax.random.fold_in(rng, 2), (rows, number_of), 0, 4096) + boost
    fixed_rows = jax.random.permutation(jax.random.fold_in(rng, 3), rows)[jnp.arange(number_of) % rows]
    lots = jnp.where(jnp.arange(rows)[:, None] == fixed_rows[None, :], 1 << 14, lots)
    priority = lots * number_of + jnp.arange(number_of)
    return lax.top_k(priority.astype(jnp.int32), top)[1].astype(jnp.int32)


def scatter_about(key, shape, scale, bound, cuts=(), kind=jnp.bfloat16):
    result = jax.random.normal(key, shape, jnp.float32) * scale
    if len(cuts) > 0:
        result = levels(key, shape, cuts, -0.22, 0.18) * result
    return jnp.clip(result, min=-bound, max=bound).astype(kind)


def setup_inputs(seed: int = 0) -> dict:
    seeds = jax.random.split(jax.random.key(seed), 15)
    hidden = scatter_about(seeds[0], (REQS, D), 1.0, 6.0, ((0, 32),))
    attn_gain = jnp.clip(1.0 + 0.15 * jax.random.normal(seeds[1], (D,), jnp.float32), 0.25, 1.75)
    w_query = scatter_about(seeds[2], (D, QHEADS * HEAD_DIM), (D // 16) ** -0.5, 0.625, ((1, 2),))
    w_keyvalue = scatter_about(seeds[3], (D, KVHEADS, 2 * HEAD_DIM), (D // 9) ** -0.5, 0.4375, ((1, 2),))
    w_output = scatter_about(seeds[4], (QHEADS * HEAD_DIM, D), (QHEADS * HEAD_DIM // 16) ** -0.5, 0.625, ((0, 2),))
    cache = draw_cache(jax.random.fold_in(seeds[14], 71), 0)
    page_table = draw_page_table(jax.random.fold_in(seeds[14], 71), 0)
    ctx_len = draw_ctx_len(jax.random.fold_in(seeds[14], 71), 0)
    move_dest = draw_move_dest(jax.random.fold_in(seeds[14], 71), 0)
    ffn_gain = jnp.clip(1.0 + 0.15 * jax.random.normal(seeds[9], (D,), jnp.float32), 0.25, 1.75)
    router = scatter_about(seeds[10], (D, EXPERTS), D ** -0.5, 0.15625)
    routes = picks_of(seeds[11], REQS, EXPERTS, TOPK, 1638)
    w_in = scatter_about(seeds[12], (D, 2, WINDOW_EXPERTS * FF), D ** -0.5, 0.15625, ((2, 2),))
    w_down = scatter_about(seeds[13], (WINDOW_EXPERTS * FF, D), FF ** -0.5, 0.25, ((0, 2),))
    return {"hidden": hidden, "attn_gain": attn_gain, "w_query": w_query, "w_keyvalue": w_keyvalue, "w_output": w_output, "cache": cache, "page_table": page_table, "ctx_len": ctx_len, "move_dest": move_dest, "ffn_gain": ffn_gain, "router": router, "routes": routes, "w_in": w_in, "w_down": w_down}


ATTN_SCALE = 0.015625
RESID_SCALE = 0.22
ROPE_BASE = 10000.0
EPSILON = 1e-06
NEG_FILL = -1e+30

def rms_norm(row_block, gain):
    values = row_block.astype(jnp.float32)
    factor = lax.rsqrt(lax.optimization_barrier(jnp.mean(values * values, axis=-1, keepdims=True)) + EPSILON)
    return (values * factor * gain.astype(jnp.float32)).astype(jnp.bfloat16)

def rotate(values, positions):
    lanes = values.shape[-1]
    halfway = lanes // 2
    indices = jnp.arange(halfway, dtype=jnp.float32)
    inverse = jnp.exp(indices * (-2.0 * math.log(ROPE_BASE) / lanes))
    angles = positions.astype(jnp.float32)[:, None] * inverse[None, :]
    cosine = jnp.concatenate([jnp.cos(angles), jnp.cos(angles)], axis=-1)[:, None, :]
    sine_rep = jnp.concatenate([jnp.sin(angles), jnp.sin(angles)], axis=-1)[:, None, :]
    turned = jnp.concatenate([-values[..., halfway:], values[..., :halfway]], axis=-1)
    return values * cosine + turned * sine_rep

def page_partials(queries, page_rows, spans):
    head_dim = queries.shape[-1]
    keys_part = page_rows[..., :head_dim].astype(jnp.float32)
    values_part = page_rows[..., head_dim:].astype(jnp.float32)
    scores = jnp.einsum('pkgh,ptkh->pkgt', queries.astype(jnp.float32), keys_part) * ATTN_SCALE
    in_range = (jnp.arange(page_rows.shape[1], dtype=jnp.int32)[None, :] < spans[:, None])[:, None, None, :]
    scores = jnp.where(in_range, scores, NEG_FILL)
    part_max = lax.optimization_barrier(jnp.max(scores, axis=-1))
    weights = jnp.where(in_range, jnp.exp(scores - part_max[..., None]), 0.0)
    part_sum = lax.optimization_barrier(jnp.sum(weights, axis=-1))
    rounded = lax.optimization_barrier(weights.astype(jnp.bfloat16)).astype(jnp.float32)
    part_out = jnp.einsum('pkgt,ptkh->pkgh', rounded, values_part)
    return (part_max, part_sum, part_out)

def inbox_sources(move_dest, replica):
    replicas = move_dest.shape[0] // OUTGOING
    layout = move_dest.reshape(replicas, OUTGOING)
    out_slots = jnp.arange(OUTGOING, dtype=jnp.int32)
    earlier = (layout[:, None, :] == layout[:, :, None]) & (out_slots[None, None, :] < out_slots[None, :, None])
    order_rank = lax.optimization_barrier(jnp.sum(earlier, axis=2)).astype(jnp.int32)
    senders = jnp.arange(replicas, dtype=jnp.int32)[:, None]
    target = senders * CAP + order_rank
    rows_global = senders * POOL + LOCAL_PAGES + out_slots[None, :]
    matches = (layout == replica)[None] & (target[None] == jnp.arange(replicas * CAP, dtype=jnp.int32)[:, None, None])
    return lax.optimization_barrier(jnp.sum(jnp.where(matches, rows_global[None], 0), axis=(1, 2))).astype(jnp.int32)

def one_replica(replica, row_block, slot_table, lengths, chosen_ids, cache, move_dest, attn_gain, w_query, w_keyvalue, w_output, ffn_gain, router, w_in, w_down):
    requests = row_block.shape[0]
    groups = QHEADS // KVHEADS
    normed = rms_norm(row_block, attn_gain)
    queries = jnp.dot(normed, w_query, preferred_element_type=jnp.float32).reshape(requests, QHEADS, HEAD_DIM)
    queries = rotate(queries, lengths).astype(jnp.bfloat16).reshape(requests, KVHEADS, groups, HEAD_DIM)
    projected = jnp.dot(normed, w_keyvalue.reshape(D, KVHEADS * 2 * HEAD_DIM), preferred_element_type=jnp.float32).reshape(requests, KVHEADS, 2 * HEAD_DIM)
    new_key = rotate(projected[..., :HEAD_DIM], lengths).astype(jnp.bfloat16)
    new_value = projected[..., HEAD_DIM:].astype(jnp.bfloat16)
    entries = slot_table.reshape(-1).astype(jnp.int32)
    positions = jnp.arange(entries.shape[0], dtype=jnp.int32)
    owners = positions // MAXPAGES
    slot_idx = positions % MAXPAGES
    spans = jnp.where(entries >= 0, jnp.clip(lengths[owners] - slot_idx * PAGE, 0, PAGE), 0).astype(jnp.int32)
    inbox_rows = inbox_sources(move_dest, replica)
    inbox_index = jnp.clip(entries - POOL, 0, inbox_rows.shape[0] - 1)
    page_source = jnp.where(entries < POOL, replica * POOL + entries, inbox_rows[inbox_index])
    page_source = jnp.where(entries >= 0, page_source, 0).astype(jnp.int32)
    part_max, part_sum, part_out = page_partials(queries[owners], cache[page_source], spans)
    part_max = part_max.reshape(requests, MAXPAGES, KVHEADS, groups)
    part_sum = part_sum.reshape(requests, MAXPAGES, KVHEADS, groups)
    part_out = part_out.reshape(requests, MAXPAGES, KVHEADS, groups, HEAD_DIM)
    new_score = jnp.einsum('rkgh,rkh->rkg', queries.astype(jnp.float32), new_key.astype(jnp.float32)) * ATTN_SCALE
    highest = jnp.maximum(new_score, lax.optimization_barrier(jnp.max(part_max, axis=1)))
    rescale = jnp.exp(part_max - highest[:, None])
    fresh_weight = jnp.exp(new_score - highest)
    denominator = lax.optimization_barrier(jnp.sum(rescale * part_sum, axis=1)) + fresh_weight
    numerator = lax.optimization_barrier(jnp.sum(rescale[..., None] * part_out, axis=1)) + fresh_weight[..., None] * new_value.astype(jnp.float32)[:, :, None, :]
    attention = (numerator / denominator[..., None]).astype(jnp.bfloat16).reshape(requests, QHEADS * HEAD_DIM)
    summed = jnp.dot(attention, w_output, preferred_element_type=jnp.float32)
    attended = (row_block.astype(jnp.float32) + RESID_SCALE * summed).astype(jnp.bfloat16)
    ffn_input = rms_norm(attended, ffn_gain)
    logits = jnp.dot(ffn_input, router, preferred_element_type=jnp.float32)
    gate_weights = jax.nn.softmax(jnp.take_along_axis(logits, chosen_ids, axis=1), axis=-1)
    unit_expert = jnp.arange(WINDOW_EXPERTS * FF, dtype=jnp.int32) // FF
    spread = lax.optimization_barrier(jnp.sum(jnp.where(chosen_ids[:, :, None] == unit_expert[None, None, :], gate_weights[:, :, None], 0.0), axis=1))
    lifted = jnp.dot(ffn_input, w_in.reshape(D, 2 * WINDOW_EXPERTS * FF), preferred_element_type=jnp.float32).reshape(requests, 2, WINDOW_EXPERTS * FF)
    active = (jax.nn.silu(lifted[:, 0]) * lifted[:, 1] * spread).astype(jnp.bfloat16)
    experts_out = jnp.dot(active, w_down, preferred_element_type=jnp.float32).astype(jnp.bfloat16)
    return (attended, experts_out)

def reference(hidden, attn_gain, w_query, w_keyvalue, w_output, cache, page_table, ctx_len, move_dest, ffn_gain, router, routes, w_in, w_down):
    replicas = hidden.shape[0] // REQ_REP

    def per_replica(pieces):
        replica, row_block, slot_table, lengths, chosen_ids = pieces
        return one_replica(replica, row_block, slot_table, lengths, chosen_ids, cache, move_dest, attn_gain, w_query, w_keyvalue, w_output, ffn_gain, router, w_in, w_down)
    attended, experts_out = lax.map(per_replica, (jnp.arange(replicas, dtype=jnp.int32), hidden.reshape(replicas, REQ_REP, D), page_table.reshape(replicas, REQ_REP, MAXPAGES), ctx_len.reshape(replicas, REQ_REP), routes.reshape(replicas, REQ_REP, TOPK)))
    return (attended.reshape(REQS, D), experts_out.reshape(REQS, D))
```

```python
import functools
import math

import jax
import jax.numpy as jnp
from jax import lax
from jax.experimental import pallas as pl
from jax.experimental.pallas import tpu as pltpu
from jax.sharding import PartitionSpec as P

HEAD_DIM = 64
EXPERTS = 40
FF = 512
CAP = 2
LANES = 128
SLOT = 8
ROWS = 16
META = 6

ATTN_SCALE = 0.015625
RESID_SCALE = 0.22
ROPE_BASE = 10000.0
EPSILON = 1e-06
NEG_FILL = -1e30

F32 = jnp.float32
BF16 = jnp.bfloat16
VMEM = pl.BlockSpec(memory_space=pltpu.VMEM)
SMEM = pl.BlockSpec(memory_space=pltpu.SMEM)
ANY = pl.BlockSpec(memory_space=pl.ANY)
NT = (((1,), (1,)), ((), ()))
TN = (((0,), (0,)), ((), ()))


def iota(shape, axis):
    return lax.broadcasted_iota(jnp.int32, shape, axis)


def norm_rows(values, gain):
    factor = lax.rsqrt(jnp.mean(values * values, axis=-1, keepdims=True) + EPSILON)
    return (values * factor * gain).astype(BF16)


def rope_tables(ctx_row, requests):
    diagonal = iota((requests, requests), 0) == iota((requests, requests), 1)
    ctx = jnp.broadcast_to(ctx_row.astype(F32), (requests, requests))
    ctx = jnp.sum(jnp.where(diagonal, ctx, 0.0), axis=1, keepdims=True)
    lane = iota((requests, LANES), 1)
    index = (lane % (HEAD_DIM // 2)).astype(F32)
    inverse = jnp.exp(index * (-2.0 * math.log(ROPE_BASE) / HEAD_DIM))
    angles = ctx * inverse
    sign = jnp.where(lane % HEAD_DIM < HEAD_DIM // 2, -1.0, 1.0)
    return jnp.cos(angles), jnp.sin(angles) * sign


def rotate(chunk, cosine, sine):
    lane = iota(chunk.shape, 1)
    ahead = pltpu.roll(chunk, LANES - HEAD_DIM // 2, 1)
    behind = pltpu.roll(chunk, HEAD_DIM // 2, 1)
    turned = jnp.where(lane % HEAD_DIM < HEAD_DIM // 2, ahead, behind)
    return chunk * cosine + turned * sine


def query_kernel(
    pool, inbox, hidden_ref, gain_ref, wq_ref, ctx_ref, table_ref,
    normed_ref, packed_ref, send_ref, meta_ref, scratch, sends,
):
    requests = hidden_ref.shape[0]
    entries = meta_ref.shape[1]
    width = wq_ref.shape[1]
    chunks = -(-width // LANES)
    values = iota((entries, requests), 0)
    held = jnp.zeros((entries, requests), F32)
    spans = jnp.zeros((entries, requests), F32)
    ctx_row = ctx_ref[...]
    for k in range(table_ref.shape[0]):
        match = table_ref[k : k + 1, :] == values
        filled = jnp.clip(ctx_row - k * 128, 0, 128).astype(F32)
        held = jnp.where(match, 1.0, held)
        spans = jnp.where(match, filled, spans)
    held16 = held.astype(BF16)
    numbers = (iota((SLOT, requests), 1) + 1).astype(BF16)
    ones = jnp.ones((SLOT, requests), BF16)
    holder = lax.dot_general(numbers, held16, NT, preferred_element_type=F32)
    covered = lax.dot_general(ones, spans.astype(BF16), NT, preferred_element_type=F32)
    meta_ref[0:1, :] = holder[0:1, :].astype(jnp.int32) - 1
    meta_ref[1:2, :] = covered[0:1, :].astype(jnp.int32)

    normed = norm_rows(hidden_ref[...].astype(F32), gain_ref[...])
    normed_ref[...] = normed
    queries = jnp.dot(normed, wq_ref[...], preferred_element_type=F32)
    if chunks * LANES > width:
        pad = jnp.zeros((requests, chunks * LANES - width), F32)
        queries = jnp.concatenate([queries, pad], axis=1)
    cosine, sine = rope_tables(ctx_row, requests)
    away = held16[pool : pool + inbox, :]
    away_span = jnp.sum(spans[pool : pool + inbox, :], axis=1, keepdims=True)
    zeros = jnp.zeros((requests, LANES), F32)
    nothing = jnp.zeros((inbox, LANES), F32)
    for j in range(SLOT):
        here = pl.ds(j, requests, stride=SLOT)
        there = pl.ds(j, inbox, stride=SLOT)
        if j < chunks:
            chunk = rotate(queries[:, j * LANES : (j + 1) * LANES], cosine, sine)
            chunk = (chunk.astype(BF16).astype(F32) * ATTN_SCALE).astype(BF16)
            scratch[here, :] = chunk.astype(F32)
            sends[there, :] = jnp.dot(away, chunk, preferred_element_type=F32)
        else:
            scratch[here, :] = zeros
            sends[there, :] = nothing + away_span if j == META else nothing
    packed_ref[...] = scratch[...]
    send_ref[...] = sends[...].astype(BF16)


def unpack(packed):
    low = iota(packed.shape, 1) < HEAD_DIM
    even = jnp.where(low, packed, 0.0)
    odd = jnp.where(low, pltpu.roll(packed, HEAD_DIM, 1), 0.0)
    return jnp.concatenate([even, odd], axis=0)


def head_rows(heads):
    return [(h // 2) + SLOT * (h % 2) for h in range(heads)]


def token_of_column(heads, kv_local, columns):
    row = iota((ROWS, columns), 0)
    column = iota((ROWS, columns), 1)
    wanted = jnp.full((ROWS, columns), kv_local, jnp.int32)
    for h, place in enumerate(head_rows(heads)):
        wanted = jnp.where(row == place, h // (heads // kv_local), wanted)
    return jnp.where(column % kv_local == wanted, column // kv_local, 1 << 20)


def attend(queries, block, tokens, span):
    scores = lax.dot_general(queries, block, NT, preferred_element_type=F32)
    scores = jnp.where(tokens < span, scores, NEG_FILL)
    top = jnp.max(scores, axis=1, keepdims=True)
    weights = jnp.exp(scores - top)
    total = jnp.sum(weights, axis=1, keepdims=True)
    out = jnp.dot(weights.astype(BF16), block, preferred_element_type=F32)
    return top, total, out


def local_kernel(
    heads, group, local_pages, meta_ref, packed_ref, kv_ref, ctx_ref, cache_ref,
    top_ref, acc_ref, pages, queries, fresh, tops, sums, sems,
):
    requests = ctx_ref.shape[1]
    kv_local = kv_ref.shape[0]
    columns = cache_ref.shape[1]
    groups = local_pages // group

    def fetch(g):
        rows = pl.ds(g * group, group)
        return pltpu.make_async_copy(cache_ref.at[rows], pages.at[rows], sems.at[g])

    for g in range(groups):
        fetch(g).start()
    low = iota((requests, LANES), 1) < HEAD_DIM
    cosine, sine = rope_tables(ctx_ref[...], requests)
    cosine = jnp.where(low, cosine, 1.0)
    sine = jnp.where(low, sine, 0.0)
    packed = packed_ref[...].reshape(requests, SLOT, LANES)
    low3 = iota(packed.shape, 2) < HEAD_DIM
    queries[:, 0:SLOT, :] = jnp.where(low3, packed, 0.0)
    queries[:, SLOT:ROWS, :] = jnp.where(low3, pltpu.roll(packed, HEAD_DIM, 2), 0.0)
    new = [
        rotate(kv_ref[k], cosine, sine).astype(BF16).astype(F32) for k in range(kv_local)
    ]
    fresh[...] = jnp.zeros(fresh.shape, F32)
    for h, place in enumerate(head_rows(heads)):
        fresh[pl.ds(place, requests, stride=ROWS), :] = new[h // (heads // kv_local)]
    added = fresh[...].reshape(requests, ROWS, LANES)
    low16 = iota(added.shape, 2) < HEAD_DIM
    score = jnp.sum(queries[...] * added, axis=2, keepdims=True)
    top_ref[0:requests] = jnp.broadcast_to(score, added.shape)
    start = jnp.where(low16, 1.0, added)

    tokens = token_of_column(heads, kv_local, columns)
    lower = iota((ROWS, LANES), 1) < HEAD_DIM

    def work(g, carry):
        fetch(g).wait()
        for u in range(group):
            p = g * group + u
            owner = jnp.maximum(meta_ref[0, p], 0)
            query = queries[owner].astype(BF16)
            top, total, out = attend(query, pages[p], tokens, meta_ref[1, p])
            tops[p] = jnp.broadcast_to(top, (ROWS, LANES))
            sums[p] = jnp.where(lower, total, out)
        return carry

    lax.fori_loop(0, groups, work, 0)

    def place_of(p):
        owner = meta_ref[0, p]
        return jnp.where(owner < 0, requests, owner)

    before = top_ref[0:requests]
    for p in range(local_pages):
        place = place_of(p)
        top_ref[place] = jnp.maximum(top_ref[place], tops[p])
    acc_ref[0:requests] = start * jnp.exp(before - top_ref[0:requests])
    for p in range(local_pages):
        place = place_of(p)
        acc_ref[place] = acc_ref[place] + sums[p] * jnp.exp(tops[p] - top_ref[place])


def lent_kernel(
    heads, kv_local, local_pages, dest_ref, asked_ref, cache_ref,
    reply_ref, pages, asked, reply, sems,
):
    outgoing = dest_ref.shape[0]
    columns = cache_ref.shape[1]

    def fetch(j):
        return pltpu.make_async_copy(
            cache_ref.at[local_pages + j], pages.at[j], sems.at[j]
        )

    for j in range(outgoing):
        fetch(j).start()
    asked[...] = asked_ref[...].astype(F32)
    reply[...] = jnp.zeros(reply.shape, F32)
    tokens = token_of_column(heads, kv_local, columns).astype(F32)
    low = iota((SLOT, LANES), 1) < HEAD_DIM
    lane = iota((SLOT, LANES), 1)
    row = iota((SLOT, LANES), 0)

    def terms(total, offset):
        first = total.astype(BF16).astype(F32)
        rest = total - first
        second = rest.astype(BF16).astype(F32)
        third = rest - second
        spot = lane - offset - 3 * row
        placed = jnp.where(spot == 0, first, 0.0)
        placed = jnp.where(spot == 1, second, placed)
        return jnp.where(spot == 2, third, placed)

    for j in range(outgoing):
        dest = dest_ref[j]
        rank = jnp.int32(0)
        for e in range(j):
            rank = rank + (dest_ref[e] == dest).astype(jnp.int32)
        rows = pl.ds(pl.multiple_of((dest * CAP + rank) * SLOT, SLOT), SLOT)
        packed = asked[rows, :]
        query = unpack(packed).astype(BF16)
        fetch(j).wait()
        top, total, out = attend(query, pages[j], tokens, packed[META : META + 1, 0:1])
        out = out / total
        logs = top + jnp.log(total)
        even = pltpu.roll(out[0:SLOT], HEAD_DIM, 1)
        both = jnp.where(low, even, out[SLOT:ROWS])
        line = jnp.sum(
            terms(logs[0:SLOT], 0) + terms(logs[SLOT:ROWS], HEAD_DIM), axis=0, keepdims=True
        )
        reply[rows, :] = jnp.where(row == META, line, both)
    reply_ref[...] = reply[...].astype(BF16)


def combine_kernel(
    heads, pool, meta_ref, top_ref, acc_ref, reply_ref, wo_ref,
    part_ref, tops, accs, reply, finals,
):
    requests = top_ref.shape[0] - 1
    inbox = reply_ref.shape[0] // SLOT
    chunks = -(-heads // 2)
    reply[...] = reply_ref[...].astype(F32)
    tops[...] = top_ref[...]
    low = iota((SLOT, LANES), 1) < HEAD_DIM
    lane = iota((SLOT, LANES), 1)
    row = iota((SLOT, LANES), 0)
    mine = (lane % HEAD_DIM) // 3 == row

    def place_of(s):
        owner = meta_ref[0, pool + s]
        return jnp.where(owner < 0, requests, owner)

    def logs_of(s):
        line = reply[s * SLOT + META : s * SLOT + META + 1, :]
        line = jnp.where(mine, jnp.broadcast_to(line, (SLOT, LANES)), 0.0)
        even = jnp.sum(jnp.where(low, line, 0.0), axis=1, keepdims=True)
        odd = jnp.sum(jnp.where(low, 0.0, line), axis=1, keepdims=True)
        logs = jnp.concatenate([even, odd], axis=0)
        return jnp.broadcast_to(logs, (ROWS, LANES))

    logs = [logs_of(s) for s in range(inbox)]
    for s in range(inbox):
        place = place_of(s)
        tops[place] = jnp.maximum(tops[place], logs[s])
    accs[0:requests] = acc_ref[0:requests] * jnp.exp(
        top_ref[0:requests] - tops[0:requests]
    )
    for s in range(inbox):
        place = place_of(s)
        packed = reply[s * SLOT : (s + 1) * SLOT, :]
        even = jnp.where(low, 1.0, pltpu.roll(packed, HEAD_DIM, 1))
        odd = jnp.where(low, 1.0, packed)
        both = jnp.concatenate([even, odd], axis=0)
        accs[place] = accs[place] + both * jnp.exp(logs[s] - tops[place])
    whole = accs[0:requests]
    finals[...] = (whole / pltpu.roll(whole, HEAD_DIM, 2)).reshape(
        requests * ROWS, LANES
    )
    wide = iota((requests, LANES), 1) < HEAD_DIM
    parts = []
    for j in range(chunks):
        even = finals[pl.ds(j, requests, stride=ROWS), :]
        odd = finals[pl.ds(SLOT + j, requests, stride=ROWS), :]
        parts.append(jnp.where(wide, pltpu.roll(even, HEAD_DIM, 1), odd).astype(BF16))
    attention = jnp.concatenate(parts, axis=1)[:, : heads * HEAD_DIM]
    part_ref[...] = jnp.dot(
        attention, wo_ref[...], preferred_element_type=F32
    ).astype(BF16)


def gate_kernel(
    tp, units, rank_ref, hidden_ref, parts_ref, gain_ref, router_ref, routes_ref,
    attended_ref, input_ref, spread_ref,
):
    requests = hidden_ref.shape[0]
    summed = parts_ref[0:requests, :].astype(F32)
    for t in range(1, tp):
        summed = summed + parts_ref[t * requests : (t + 1) * requests, :].astype(F32)
    attended = (hidden_ref[...].astype(F32) + RESID_SCALE * summed).astype(BF16)
    attended_ref[...] = attended
    ffn_input = norm_rows(attended.astype(F32), gain_ref[...])
    input_ref[...] = ffn_input
    logits = lax.dot_general(router_ref[...], ffn_input, NT, preferred_element_type=F32)
    expert = iota(logits.shape, 0)
    named = jnp.zeros(logits.shape, F32)
    for k in range(routes_ref.shape[0]):
        named = jnp.where(routes_ref[k : k + 1, :] == expert, 1.0, named)
    chosen = named > 0.5
    top = jnp.max(jnp.where(chosen, logits, NEG_FILL), axis=0, keepdims=True)
    weights = jnp.where(chosen, jnp.exp(logits - top), 0.0)
    gates = weights / jnp.sum(weights, axis=0, keepdims=True)
    unit = iota((EXPERTS, units), 1) + rank_ref[0] * units
    owner = (unit // FF == iota((EXPERTS, units), 0)).astype(F32)
    spread_ref[...] = lax.dot_general(
        gates, owner, TN, preferred_element_type=F32, precision=lax.Precision.HIGHEST
    )


def expert_kernel(lifted_ref, spread_ref, wd_ref, out_ref):
    gate = lifted_ref[0]
    active = gate / (1.0 + jnp.exp(-gate)) * lifted_ref[1] * spread_ref[...]
    out_ref[...] = jnp.dot(
        active.astype(BF16), wd_ref[...], preferred_element_type=F32
    ).astype(BF16)


def call(body, outs, in_specs, scratch=(), limit=16, flops=0, moved=0, out_specs=None):
    single = not isinstance(outs, (list, tuple))
    return pl.pallas_call(
        body,
        out_shape=outs,
        in_specs=in_specs,
        out_specs=VMEM if single else [VMEM] * len(outs),
        scratch_shapes=list(scratch),
        compiler_params=pltpu.CompilerParams(vmem_limit_bytes=limit << 20),
        cost_estimate=pl.CostEstimate(
            flops=flops, bytes_accessed=moved, transcendentals=0
        ),
    )


def on_device(
    hidden,
    attn_gain,
    w_query,
    w_keyvalue,
    w_output,
    cache,
    page_table,
    ctx_len,
    move_dest,
    ffn_gain,
    router,
    routes,
    w_in,
    w_down,
):
    replicas = lax.axis_size("replica")
    tp = lax.axis_size("tensor")
    rank = lax.axis_index("tensor").astype(jnp.int32)
    rows, width = hidden.shape
    pool, page_len, kv_local, _ = cache.shape
    outgoing = move_dest.shape[0]
    local_pages = pool - outgoing
    requests = page_table.shape[0]
    heads = w_query.shape[1] // HEAD_DIM
    inbox = replicas * CAP
    units = w_down.shape[0]
    columns = page_len * kv_local
    entries = -(-(pool + inbox) // LANES) * LANES
    struct = jax.ShapeDtypeStruct

    ctx_row = ctx_len.reshape(1, requests)
    table = page_table.T
    blocks = cache.reshape(pool, columns, LANES)
    hidden_all = lax.all_gather(hidden, "tensor", axis=0, tiled=True)
    normed, packed, sends, meta = call(
        functools.partial(query_kernel, pool, inbox),
        [
            struct((requests, width), BF16),
            struct((requests * SLOT, LANES), F32),
            struct((inbox * SLOT, LANES), BF16),
            struct((2, entries), jnp.int32),
        ],
        [VMEM] * 5,
        [
            pltpu.VMEM((requests * SLOT, LANES), F32),
            pltpu.VMEM((inbox * SLOT, LANES), F32),
        ],
        flops=4 * requests * width * w_query.shape[1],
        moved=2 * w_query.size,
    )(hidden_all, attn_gain.reshape(1, width), w_query, ctx_row, table)
    asked = lax.all_to_all(
        sends.reshape(replicas, CAP * SLOT, LANES),
        "replica",
        split_axis=0,
        concat_axis=0,
        tiled=True,
    )
    projected = jnp.einsum(
        "rd,dkc->krc", normed, w_keyvalue, preferred_element_type=F32
    )
    group = next(g for g in (8, 4, 2, 1) if local_pages % g == 0)
    top, acc = call(
        functools.partial(local_kernel, heads, group, local_pages),
        [struct((requests + 1, ROWS, LANES), F32)] * 2,
        [SMEM, VMEM, VMEM, VMEM, ANY],
        [
            pltpu.VMEM((local_pages, columns, LANES), BF16),
            pltpu.VMEM((requests, ROWS, LANES), F32),
            pltpu.VMEM((requests * ROWS, LANES), F32),
            pltpu.VMEM((local_pages, ROWS, LANES), F32),
            pltpu.VMEM((local_pages, ROWS, LANES), F32),
            pltpu.SemaphoreType.DMA((local_pages // group,)),
        ],
        flops=4 * ROWS * columns * LANES * local_pages,
        moved=2 * columns * LANES * local_pages,
    )(meta, packed, projected, ctx_row, blocks)
    replies = call(
        functools.partial(lent_kernel, heads, kv_local, local_pages),
        struct((inbox * SLOT, LANES), BF16),
        [SMEM, VMEM, ANY],
        [
            pltpu.VMEM((outgoing, columns, LANES), BF16),
            pltpu.VMEM((inbox * SLOT, LANES), F32),
            pltpu.VMEM((inbox * SLOT, LANES), F32),
            pltpu.SemaphoreType.DMA((outgoing,)),
        ],
        flops=4 * ROWS * columns * LANES * outgoing,
        moved=2 * columns * LANES * outgoing,
    )(move_dest, asked.reshape(inbox * SLOT, LANES), blocks)
    returned = lax.all_to_all(
        replies.reshape(replicas, CAP * SLOT, LANES),
        "replica",
        split_axis=0,
        concat_axis=0,
        tiled=True,
    )
    partial_sum = call(
        functools.partial(combine_kernel, heads, pool),
        struct((requests, width), BF16),
        [SMEM, VMEM, VMEM, VMEM, VMEM],
        [
            pltpu.VMEM((requests + 1, ROWS, LANES), F32),
            pltpu.VMEM((requests + 1, ROWS, LANES), F32),
            pltpu.VMEM((inbox * SLOT, LANES), F32),
            pltpu.VMEM((requests * ROWS, LANES), F32),
        ],
        flops=2 * requests * w_output.size,
        moved=2 * w_output.size,
    )(meta, top, acc, returned.reshape(inbox * SLOT, LANES), w_output)
    parts = lax.all_gather(partial_sum, "tensor", axis=0, tiled=True)
    attended, ffn_input, spread = call(
        functools.partial(gate_kernel, tp, units),
        [
            struct((requests, width), BF16),
            struct((requests, width), BF16),
            struct((requests, units), F32),
        ],
        [SMEM] + [VMEM] * 5,
        flops=2 * requests * router.size,
        moved=2 * router.size,
    )(rank.reshape(1), hidden_all, parts, ffn_gain.reshape(1, width), router.T, routes.T)
    lifted = jnp.einsum("rd,dsu->sru", ffn_input, w_in, preferred_element_type=F32)
    share = call(
        expert_kernel,
        struct((requests, width), BF16),
        [VMEM] * 3,
        flops=2 * requests * w_down.size,
        moved=2 * w_down.size,
    )(lifted, spread, w_down)
    shares = lax.all_gather(share, "tensor", axis=0)
    mine = lax.dynamic_slice_in_dim(shares, rank * rows, rows, axis=1)
    experts_out = jnp.sum(mine.astype(F32), axis=0).astype(BF16)
    attended = lax.dynamic_slice_in_dim(attended, rank * rows, rows, axis=0)
    return attended, experts_out


def solution(mesh):
    placed = (
        P(("replica", "tensor"), None),
        P(),
        P(None, "tensor"),
        P(None, "tensor", None),
        P("tensor", None),
        P("replica", None, "tensor", None),
        P("replica", None),
        P("replica"),
        P("replica"),
        P(),
        P(),
        P("replica", None),
        P(None, None, "tensor"),
        P("tensor", None),
    )
    return jax.shard_map(
        on_device,
        mesh=mesh,
        in_specs=placed,
        out_specs=(P(("replica", "tensor"), None), P(("replica", "tensor"), None)),
        check_vma=False,
    )
```

```python
import functools
import math

import jax
import jax.numpy as jnp
from jax import lax
from jax.experimental import pallas as pl
from jax.experimental.pallas import tpu as pltpu
from jax.sharding import PartitionSpec as P

HEAD_DIM = 64
EXPERTS = 40
FF = 512
CAP = 2
LANES = 128
SLOT = 8
ROWS = 16
META = 6

ATTN_SCALE = 0.015625
RESID_SCALE = 0.22
ROPE_BASE = 10000.0
EPSILON = 1e-06
NEG_FILL = -1e30

F32 = jnp.float32
BF16 = jnp.bfloat16
VMEM = pl.BlockSpec(memory_space=pltpu.VMEM)
SMEM = pl.BlockSpec(memory_space=pltpu.SMEM)
ANY = pl.BlockSpec(memory_space=pl.ANY)
HBM = pl.BlockSpec(memory_space=pltpu.HBM)
NT = (((1,), (1,)), ((), ()))
TN = (((0,), (0,)), ((), ()))


def iota(shape, axis):
    return lax.broadcasted_iota(jnp.int32, shape, axis)


def norm_rows(values, gain):
    factor = lax.rsqrt(jnp.mean(values * values, axis=-1, keepdims=True) + EPSILON)
    return (values * factor * gain).astype(BF16)


def rope_tables(ctx_row, requests):
    diagonal = iota((requests, requests), 0) == iota((requests, requests), 1)
    ctx = jnp.broadcast_to(ctx_row.astype(F32), (requests, requests))
    ctx = jnp.sum(jnp.where(diagonal, ctx, 0.0), axis=1, keepdims=True)
    lane = iota((requests, LANES), 1)
    index = (lane % (HEAD_DIM // 2)).astype(F32)
    inverse = jnp.exp(index * (-2.0 * math.log(ROPE_BASE) / HEAD_DIM))
    angles = ctx * inverse
    sign = jnp.where(lane % HEAD_DIM < HEAD_DIM // 2, -1.0, 1.0)
    return jnp.cos(angles), jnp.sin(angles) * sign


def rotate(chunk, cosine, sine):
    lane = iota(chunk.shape, 1)
    ahead = pltpu.roll(chunk, LANES - HEAD_DIM // 2, 1)
    behind = pltpu.roll(chunk, HEAD_DIM // 2, 1)
    turned = jnp.where(lane % HEAD_DIM < HEAD_DIM // 2, ahead, behind)
    return chunk * cosine + turned * sine


def copy_of(source, target, sem):
    return pltpu.make_async_copy(source, target, sem)


def prepare_kernel(
    pool, inbox, ctx_hbm, table_hbm, attn_gain_hbm, ffn_gain_hbm, wq_hbm, wkv_hbm,
    wq_ref, wkv_ref, gains_ref, cosine_ref, sine_ref, away_ref, span_ref, meta_ref,
    ctx, table, gain_a, gain_f, raw, wide, sems,
):
    requests = ctx.shape[1]
    entries = meta_ref.shape[1]
    depth = wkv_ref.shape[0]
    kv_local = raw.shape[0] // depth
    small = [
        copy_of(ctx_hbm, ctx, sems.at[0]),
        copy_of(table_hbm, table, sems.at[1]),
        copy_of(attn_gain_hbm, gain_a, sems.at[2]),
        copy_of(ffn_gain_hbm, gain_f, sems.at[3]),
    ]
    raw_copy = copy_of(wkv_hbm, raw, sems.at[4])
    wq_copy = copy_of(wq_hbm, wq_ref, sems.at[5])
    for copy in small + [raw_copy, wq_copy]:
        copy.start()
    for copy in small:
        copy.wait()
    gains_ref[0:1, :] = gain_a[...].reshape(1, gain_a.shape[0])
    gains_ref[1:2, :] = gain_f[...].reshape(1, gain_f.shape[0])
    values = iota((entries, requests), 0)
    held = jnp.zeros((entries, requests), F32)
    spans = jnp.zeros((entries, requests), F32)
    ctx_row = ctx[...]
    for k in range(table.shape[0]):
        match = table[k : k + 1, :] == values
        filled = jnp.clip(ctx_row - k * 128, 0, 128).astype(F32)
        held = jnp.where(match, 1.0, held)
        spans = jnp.where(match, filled, spans)
    held16 = held.astype(BF16)
    numbers = (iota((SLOT, requests), 1) + 1).astype(BF16)
    ones = jnp.ones((SLOT, requests), BF16)
    holder = lax.dot_general(numbers, held16, NT, preferred_element_type=F32)
    covered = lax.dot_general(ones, spans.astype(BF16), NT, preferred_element_type=F32)
    meta_ref[0:1, :] = holder[0:1, :].astype(jnp.int32) - 1
    meta_ref[1:2, :] = covered[0:1, :].astype(jnp.int32)
    away_ref[...] = held16[pool : pool + inbox, :]
    away_span = jnp.sum(spans[pool : pool + inbox, :], axis=1, keepdims=True)
    span_ref[...] = jnp.broadcast_to(away_span, span_ref.shape)
    cosine, sine = rope_tables(ctx_row, requests)
    cosine_ref[...] = cosine
    sine_ref[...] = sine
    raw_copy.wait()
    if kv_local == 1:
        wkv_ref[...] = raw[...]
    else:
        wide[...] = raw[...].astype(F32)
        for k in range(kv_local):
            wkv_ref[:, k * LANES : (k + 1) * LANES] = wide[
                pl.ds(k, depth, stride=kv_local), :
            ].astype(BF16)
    wq_copy.wait()


def query_kernel(
    count, rank_ref, *refs,
):
    pieces = refs[:count]
    (gains_ref, wq_ref, cosine_ref, sine_ref, away_ref, span_ref,
     hidden_ref, normed_ref, packed_ref, send_ref, scratch, sends) = refs[count:]
    requests = hidden_ref.shape[0]
    inbox = span_ref.shape[0]
    width = wq_ref.shape[1]
    chunks = -(-width // LANES)
    if count == 1:
        hidden = pieces[0][...]
    else:
        own, other = pieces[0][...], pieces[1][...]
        first = rank_ref[0] == 0
        hidden = jnp.concatenate(
            [jnp.where(first, own, other), jnp.where(first, other, own)], axis=0
        )
    hidden_ref[...] = hidden
    normed = norm_rows(hidden.astype(F32), gains_ref[0:1, :])
    normed_ref[...] = normed
    queries = jnp.dot(normed, wq_ref[...], preferred_element_type=F32)
    if chunks * LANES > width:
        pad = jnp.zeros((requests, chunks * LANES - width), F32)
        queries = jnp.concatenate([queries, pad], axis=1)
    cosine, sine = cosine_ref[...], sine_ref[...]
    zeros = jnp.zeros((requests, LANES), F32)
    nothing = jnp.zeros((inbox, LANES), F32)
    for j in range(SLOT):
        here = pl.ds(j, requests, stride=SLOT)
        there = pl.ds(j, inbox, stride=SLOT)
        if j < chunks:
            chunk = rotate(queries[:, j * LANES : (j + 1) * LANES], cosine, sine)
            chunk = (chunk.astype(BF16).astype(F32) * ATTN_SCALE).astype(BF16)
            scratch[here, :] = chunk.astype(F32)
            sends[there, :] = jnp.dot(away_ref[...], chunk, preferred_element_type=F32)
        else:
            scratch[here, :] = zeros
            sends[there, :] = span_ref[...] if j == META else nothing
    packed_ref[...] = scratch[...]
    send_ref[...] = sends[...].astype(BF16)


def unpack(packed):
    low = iota(packed.shape, 1) < HEAD_DIM
    even = jnp.where(low, packed, 0.0)
    odd = jnp.where(low, pltpu.roll(packed, HEAD_DIM, 1), 0.0)
    return jnp.concatenate([even, odd], axis=0)


def head_rows(heads):
    return [(h // 2) + SLOT * (h % 2) for h in range(heads)]


def token_of_column(heads, kv_local, columns):
    row = iota((ROWS, columns), 0)
    column = iota((ROWS, columns), 1)
    wanted = jnp.full((ROWS, columns), kv_local, jnp.int32)
    for h, place in enumerate(head_rows(heads)):
        wanted = jnp.where(row == place, h // (heads // kv_local), wanted)
    return jnp.where(column % kv_local == wanted, column // kv_local, 1 << 20)


def score_page(query, block):
    return lax.dot_general(query, block, NT, preferred_element_type=F32)


def weigh_page(scores, tokens, span):
    scores = jnp.where(tokens < span, scores, NEG_FILL)
    top = jnp.max(scores, axis=1, keepdims=True)
    weights = jnp.exp(scores - top)
    return top, jnp.sum(weights, axis=1, keepdims=True), weights.astype(BF16)


def value_page(weights, block):
    return jnp.dot(weights, block, preferred_element_type=F32)


def attend_pages(count, stage, query_of, block_of, span_of, tokens, keep):
    stages = [range(i, min(i + stage, count)) for i in range(0, count, stage)]
    scores = {p: score_page(query_of(p), block_of(p)) for p in stages[0]}
    for i, pages in enumerate(stages):
        if i + 1 < len(stages):
            ahead = {p: score_page(query_of(p), block_of(p)) for p in stages[i + 1]}
        weighed = {p: weigh_page(scores[p], tokens, span_of(p)) for p in pages}
        outs = {p: value_page(weighed[p][2], block_of(p)) for p in pages}
        for p in pages:
            keep(p, weighed[p][0], weighed[p][1], outs[p])
        if i + 1 < len(stages):
            scores = ahead


def first_kernel(
    heads, kv_local, first, local_pages, meta_ref, packed_ref, normed_ref, wkv_ref,
    cosine_ref, sine_ref, cache_hbm,
    queries_ref, fresh_ref, tops_ref, sums_ref, later_ref, lent_ref,
    pages, sems,
):
    requests = cosine_ref.shape[0]
    columns = pages.shape[1]
    lent = lent_ref.shape[0]
    mine = copy_of(cache_hbm.at[pl.ds(0, first)], pages, sems.at[0])
    lending = copy_of(cache_hbm.at[pl.ds(local_pages, lent)], lent_ref, sems.at[1])
    rest = copy_of(
        cache_hbm.at[pl.ds(first, local_pages - first)], later_ref, sems.at[2]
    )
    for copy in (mine, lending, rest):
        copy.start()
    low = iota((requests, LANES), 1) < HEAD_DIM
    cosine = jnp.where(low, cosine_ref[...], 1.0)
    sine = jnp.where(low, sine_ref[...], 0.0)
    packed = packed_ref[...].reshape(requests, SLOT, LANES)
    low3 = iota(packed.shape, 2) < HEAD_DIM
    queries_ref[:, 0:SLOT, :] = jnp.where(low3, packed, 0.0)
    queries_ref[:, SLOT:ROWS, :] = jnp.where(low3, pltpu.roll(packed, HEAD_DIM, 2), 0.0)
    projected = jnp.dot(normed_ref[...], wkv_ref[...], preferred_element_type=F32)
    new = [
        rotate(projected[:, k * LANES : (k + 1) * LANES], cosine, sine)
        .astype(BF16)
        .astype(F32)
        for k in range(kv_local)
    ]
    used = {place: h for h, place in enumerate(head_rows(heads))}
    for place in range(ROWS):
        value = jnp.zeros((requests, LANES), F32)
        if place in used:
            value = new[used[place] // (heads // kv_local)]
        fresh_ref[pl.ds(place, requests, stride=ROWS), :] = value
    tokens = token_of_column(heads, kv_local, columns)
    lower = iota((ROWS, LANES), 1) < HEAD_DIM
    mine.wait()

    def keep(p, top, total, out):
        tops_ref[p] = jnp.broadcast_to(top, (ROWS, LANES))
        sums_ref[p] = jnp.where(lower, total, out)

    attend_pages(
        first,
        4,
        lambda p: queries_ref[jnp.maximum(meta_ref[0, p], 0)].astype(BF16),
        lambda p: pages[p],
        lambda p: meta_ref[1, p],
        tokens,
        keep,
    )
    lending.wait()
    rest.wait()


def second_kernel(
    heads, kv_local, first, meta_ref, queries_ref, fresh_ref, tops_ref, sums_ref,
    pages_ref, order_hbm, wo_hbm, wd_hbm, router_hbm, routes_hbm,
    top_ref, acc_ref, wo_ref, wd_ref, router_ref, routes_ref,
    tops, sums, sems,
):
    del order_hbm
    requests = queries_ref.shape[0]
    count, columns, _ = pages_ref.shape
    local_pages = first + count
    copies = [
        copy_of(wo_hbm, wo_ref, sems.at[0]),
        copy_of(router_hbm, router_ref, sems.at[1]),
        copy_of(routes_hbm, routes_ref, sems.at[2]),
        copy_of(wd_hbm, wd_ref, sems.at[3]),
    ]
    for copy in copies:
        copy.start()
    tokens = token_of_column(heads, kv_local, columns)
    lower = iota((ROWS, LANES), 1) < HEAD_DIM
    added = fresh_ref[...].reshape(requests, ROWS, LANES)
    low16 = iota(added.shape, 2) < HEAD_DIM
    score = jnp.sum(queries_ref[...] * added, axis=2, keepdims=True)
    before = jnp.broadcast_to(score, added.shape)
    start = jnp.where(low16, 1.0, added)

    def keep(p, top, total, out):
        tops[p] = jnp.broadcast_to(top, (ROWS, LANES))
        sums[p] = jnp.where(lower, total, out)

    attend_pages(
        count,
        4,
        lambda p: queries_ref[jnp.maximum(meta_ref[0, first + p], 0)].astype(BF16),
        lambda p: pages_ref[p],
        lambda p: meta_ref[1, first + p],
        tokens,
        keep,
    )

    def place_of(p):
        owner = meta_ref[0, p]
        return jnp.where(owner < 0, requests, owner)

    def top_of(p):
        return tops_ref[p] if p < first else tops[p - first]

    def sum_of(p):
        return sums_ref[p] if p < first else sums[p - first]

    top_ref[0:requests] = before
    for p in range(local_pages):
        place = place_of(p)
        top_ref[place] = jnp.maximum(top_ref[place], top_of(p))
    acc_ref[0:requests] = start * jnp.exp(before - top_ref[0:requests])
    for p in range(local_pages):
        place = place_of(p)
        acc_ref[place] = acc_ref[place] + sum_of(p) * jnp.exp(top_of(p) - top_ref[place])
    for copy in copies:
        copy.wait()


def lent_kernel(
    heads, kv_local, dest_ref, asked_ref, pages_ref, reply_ref, asked, reply,
):
    outgoing, columns, _ = pages_ref.shape
    asked[...] = asked_ref[...].astype(F32)
    reply[...] = jnp.zeros(reply.shape, F32)
    tokens = token_of_column(heads, kv_local, columns).astype(F32)
    low = iota((SLOT, LANES), 1) < HEAD_DIM
    lane = iota((SLOT, LANES), 1)
    row = iota((SLOT, LANES), 0)

    def terms(total, offset):
        leading = total.astype(BF16).astype(F32)
        rest = total - leading
        second = rest.astype(BF16).astype(F32)
        third = rest - second
        spot = lane - offset - 3 * row
        placed = jnp.where(spot == 0, leading, 0.0)
        placed = jnp.where(spot == 1, second, placed)
        return jnp.where(spot == 2, third, placed)

    def rows_of(j):
        dest = dest_ref[j]
        rank = jnp.int32(0)
        for e in range(j):
            rank = rank + (dest_ref[e] == dest).astype(jnp.int32)
        return pl.ds(pl.multiple_of((dest * CAP + rank) * SLOT, SLOT), SLOT)

    places = [rows_of(j) for j in range(outgoing)]
    packed = [asked[rows, :] for rows in places]
    replies = {}

    def keep(j, top, total, out):
        out = out / total
        logs = top + jnp.log(total)
        even = pltpu.roll(out[0:SLOT], HEAD_DIM, 1)
        both = jnp.where(low, even, out[SLOT:ROWS])
        line = jnp.sum(
            terms(logs[0:SLOT], 0) + terms(logs[SLOT:ROWS], HEAD_DIM), axis=0, keepdims=True
        )
        replies[j] = jnp.where(row == META, line, both)

    attend_pages(
        outgoing,
        4,
        lambda j: unpack(packed[j]).astype(BF16),
        lambda j: pages_ref[j],
        lambda j: packed[j][META : META + 1, 0:1],
        tokens,
        keep,
    )
    for j in range(outgoing):
        reply[places[j], :] = replies[j]
    reply_ref[...] = reply[...].astype(BF16)


def combine_kernel(
    heads, pool, meta_ref, top_ref, acc_ref, reply_ref, wo_ref,
    part_ref, tops, accs, reply, finals,
):
    requests = top_ref.shape[0] - 1
    inbox = reply_ref.shape[0] // SLOT
    chunks = -(-heads // 2)
    reply[...] = reply_ref[...].astype(F32)
    tops[...] = top_ref[...]
    low = iota((SLOT, LANES), 1) < HEAD_DIM
    lane = iota((SLOT, LANES), 1)
    row = iota((SLOT, LANES), 0)
    mine = (lane % HEAD_DIM) // 3 == row

    def place_of(s):
        owner = meta_ref[0, pool + s]
        return jnp.where(owner < 0, requests, owner)

    def logs_of(s):
        line = reply[s * SLOT + META : s * SLOT + META + 1, :]
        line = jnp.where(mine, jnp.broadcast_to(line, (SLOT, LANES)), 0.0)
        even = jnp.sum(jnp.where(low, line, 0.0), axis=1, keepdims=True)
        odd = jnp.sum(jnp.where(low, 0.0, line), axis=1, keepdims=True)
        logs = jnp.concatenate([even, odd], axis=0)
        return jnp.broadcast_to(logs, (ROWS, LANES))

    logs = [logs_of(s) for s in range(inbox)]
    for s in range(inbox):
        place = place_of(s)
        tops[place] = jnp.maximum(tops[place], logs[s])
    accs[0:requests] = acc_ref[0:requests] * jnp.exp(
        top_ref[0:requests] - tops[0:requests]
    )
    for s in range(inbox):
        place = place_of(s)
        packed = reply[s * SLOT : (s + 1) * SLOT, :]
        even = jnp.where(low, 1.0, pltpu.roll(packed, HEAD_DIM, 1))
        odd = jnp.where(low, 1.0, packed)
        both = jnp.concatenate([even, odd], axis=0)
        accs[place] = accs[place] + both * jnp.exp(logs[s] - tops[place])
    whole = accs[0:requests]
    finals[...] = (whole / pltpu.roll(whole, HEAD_DIM, 2)).reshape(
        requests * ROWS, LANES
    )
    wide = iota((requests, LANES), 1) < HEAD_DIM
    parts = []
    for j in range(chunks):
        even = finals[pl.ds(j, requests, stride=ROWS), :]
        odd = finals[pl.ds(SLOT + j, requests, stride=ROWS), :]
        parts.append(jnp.where(wide, pltpu.roll(even, HEAD_DIM, 1), odd).astype(BF16))
    attention = jnp.concatenate(parts, axis=1)[:, : heads * HEAD_DIM]
    part_ref[...] = jnp.dot(
        attention, wo_ref[...], preferred_element_type=F32
    ).astype(BF16)


def own_rows(values, first):
    half = values.shape[0] // 2
    return jnp.where(first, values[:half], values[half:])


def gate_kernel(
    tp, units, count, rank_ref, hidden_ref, *refs,
):
    pieces = refs[:count]
    (gains_ref, router_ref, routes_ref, attended_ref, input_ref, spread_ref) = refs[count:]
    requests = hidden_ref.shape[0]
    if count == 2:
        summed = pieces[0][...].astype(F32) + pieces[1][...].astype(F32)
    else:
        summed = pieces[0][0:requests, :].astype(F32)
        for t in range(1, tp):
            part = pieces[0][t * requests : (t + 1) * requests, :]
            summed = summed + part.astype(F32)
    attended = (hidden_ref[...].astype(F32) + RESID_SCALE * summed).astype(BF16)
    if count == 2:
        attended_ref[...] = own_rows(attended, rank_ref[0] == 0)
    else:
        attended_ref[...] = attended
    ffn_input = norm_rows(attended.astype(F32), gains_ref[1:2, :])
    input_ref[...] = ffn_input
    logits = lax.dot_general(router_ref[...], ffn_input, NT, preferred_element_type=F32)
    expert = iota(logits.shape, 0)
    named = jnp.zeros(logits.shape, F32)
    for k in range(routes_ref.shape[0]):
        named = jnp.where(routes_ref[k : k + 1, :] == expert, 1.0, named)
    chosen = named > 0.5
    top = jnp.max(jnp.where(chosen, logits, NEG_FILL), axis=0, keepdims=True)
    weights = jnp.where(chosen, jnp.exp(logits - top), 0.0)
    gates = weights / jnp.sum(weights, axis=0, keepdims=True)
    unit = iota((EXPERTS, units), 1) + rank_ref[0] * units
    owner = (unit // FF == iota((EXPERTS, units), 0)).astype(F32)
    spread_ref[...] = lax.dot_general(
        gates, owner, TN, preferred_element_type=F32, precision=lax.Precision.HIGHEST
    )


def expert_kernel(rank_ref, lifted_ref, spread_ref, wd_ref, *outs):
    gate = lifted_ref[0]
    active = gate / (1.0 + jnp.exp(-gate)) * lifted_ref[1] * spread_ref[...]
    share = jnp.dot(active.astype(BF16), wd_ref[...], preferred_element_type=F32)
    if len(outs) == 2:
        first = rank_ref[0] == 0
        outs[0][...] = own_rows(share, first)
        outs[1][...] = own_rows(share, jnp.logical_not(first)).astype(BF16)
    else:
        outs[0][...] = share.astype(BF16)


def call(body, outs, in_specs, scratch=(), limit=16, flops=0, moved=0):
    return pl.pallas_call(
        body,
        out_shape=outs,
        in_specs=in_specs,
        out_specs=[VMEM] * len(outs),
        scratch_shapes=list(scratch),
        compiler_params=pltpu.CompilerParams(vmem_limit_bytes=limit << 20),
        cost_estimate=pl.CostEstimate(
            flops=flops, bytes_accessed=moved, transcendentals=0
        ),
    )


def swap(values):
    return lax.ppermute(values, "tensor", [(0, 1), (1, 0)])


def on_device(
    hidden,
    attn_gain,
    w_query,
    w_keyvalue,
    w_output,
    cache,
    page_table,
    ctx_len,
    move_dest,
    ffn_gain,
    router,
    routes,
    w_in,
    w_down,
):
    replicas = lax.axis_size("replica")
    tp = lax.axis_size("tensor")
    rank = lax.axis_index("tensor").astype(jnp.int32)
    rows, width = hidden.shape
    pool, page_len, kv_local, _ = cache.shape
    outgoing = move_dest.shape[0]
    local_pages = pool - outgoing
    requests = page_table.shape[0]
    heads = w_query.shape[1] // HEAD_DIM
    inbox = replicas * CAP
    units = w_down.shape[0]
    columns = page_len * kv_local
    entries = -(-(pool + inbox) // LANES) * LANES
    first = local_pages // 2
    struct = jax.ShapeDtypeStruct
    pair = tp == 2
    here = rank.reshape(1)

    blocks = cache.reshape(pool, columns, LANES)
    if pair:
        pieces = [hidden, swap(hidden)]
    else:
        pieces = [lax.all_gather(hidden, "tensor", axis=0, tiled=True)]
    wq, wkv, gains, cosine, sine, away, away_span, meta = call(
        functools.partial(prepare_kernel, pool, inbox),
        [
            struct(w_query.shape, BF16),
            struct((width, kv_local * LANES), BF16),
            struct((2, width), F32),
            struct((requests, LANES), F32),
            struct((requests, LANES), F32),
            struct((inbox, requests), BF16),
            struct((inbox, LANES), F32),
            struct((2, entries), jnp.int32),
        ],
        [HBM] * 6,
        [
            pltpu.VMEM((1, requests), jnp.int32),
            pltpu.VMEM((page_table.shape[1], requests), jnp.int32),
            pltpu.VMEM((width,), F32),
            pltpu.VMEM((width,), F32),
            pltpu.VMEM((width * kv_local, LANES), BF16),
            pltpu.VMEM((width * kv_local, LANES), F32),
            pltpu.SemaphoreType.DMA((6,)),
        ],
        moved=2 * (w_query.size + w_keyvalue.size),
    )(
        ctx_len.reshape(1, requests),
        page_table.T,
        attn_gain,
        ffn_gain,
        w_query,
        w_keyvalue.reshape(width * kv_local, LANES),
    )
    hidden_all, normed, packed, sends = call(
        functools.partial(query_kernel, len(pieces)),
        [
            struct((requests, width), BF16),
            struct((requests, width), BF16),
            struct((requests * SLOT, LANES), F32),
            struct((inbox * SLOT, LANES), BF16),
        ],
        [SMEM] + [VMEM] * (len(pieces) + 6),
        [
            pltpu.VMEM((requests * SLOT, LANES), F32),
            pltpu.VMEM((inbox * SLOT, LANES), F32),
        ],
        flops=4 * requests * width * w_query.shape[1],
        moved=2 * w_query.size,
    )(here, *pieces, gains, wq, cosine, sine, away, away_span)
    asked = lax.all_to_all(
        sends.reshape(replicas, CAP * SLOT, LANES),
        "replica",
        split_axis=0,
        concat_axis=0,
        tiled=True,
    )
    partials = [struct((first, ROWS, LANES), F32)] * 2
    queries, fresh, tops, sums, later, lent = call(
        functools.partial(first_kernel, heads, kv_local, first, local_pages),
        [
            struct((requests, ROWS, LANES), F32),
            struct((requests * ROWS, LANES), F32),
            *partials,
            struct((local_pages - first, columns, LANES), BF16),
            struct((outgoing, columns, LANES), BF16),
        ],
        [SMEM] + [VMEM] * 5 + [HBM],
        [
            pltpu.VMEM((first, columns, LANES), BF16),
            pltpu.SemaphoreType.DMA((3,)),
        ],
        flops=4 * ROWS * columns * LANES * first,
        moved=2 * columns * LANES * pool,
    )(meta, packed, normed, wkv, cosine, sine, blocks)
    (replies,) = call(
        functools.partial(lent_kernel, heads, kv_local),
        [struct((inbox * SLOT, LANES), BF16)],
        [SMEM, VMEM, VMEM],
        [
            pltpu.VMEM((inbox * SLOT, LANES), F32),
            pltpu.VMEM((inbox * SLOT, LANES), F32),
        ],
        flops=4 * ROWS * columns * LANES * outgoing,
        moved=2 * columns * LANES * outgoing,
    )(move_dest, asked.reshape(inbox * SLOT, LANES), lent)
    returned = lax.all_to_all(
        replies.reshape(replicas, CAP * SLOT, LANES),
        "replica",
        split_axis=0,
        concat_axis=0,
        tiled=True,
    )
    top, acc, wo, wd, router_t, routes_t = call(
        functools.partial(second_kernel, heads, kv_local, first),
        [
            struct((requests + 1, ROWS, LANES), F32),
            struct((requests + 1, ROWS, LANES), F32),
            struct(w_output.shape, BF16),
            struct(w_down.shape, BF16),
            struct(router.shape[::-1], BF16),
            struct(routes.shape[::-1], jnp.int32),
        ],
        [SMEM] + [VMEM] * 5 + [ANY] + [HBM] * 4,
        [
            pltpu.VMEM((local_pages - first, ROWS, LANES), F32),
            pltpu.VMEM((local_pages - first, ROWS, LANES), F32),
            pltpu.SemaphoreType.DMA((4,)),
        ],
        flops=4 * ROWS * columns * LANES * (local_pages - first),
        moved=2 * (w_output.size + w_down.size + router.size),
    )(
        meta, queries, fresh, tops, sums, later,
        replies, w_output, w_down, router.T, routes.T,
    )
    (part,) = call(
        functools.partial(combine_kernel, heads, pool),
        [struct((requests, width), BF16)],
        [SMEM, VMEM, VMEM, VMEM, VMEM],
        [
            pltpu.VMEM((requests + 1, ROWS, LANES), F32),
            pltpu.VMEM((requests + 1, ROWS, LANES), F32),
            pltpu.VMEM((inbox * SLOT, LANES), F32),
            pltpu.VMEM((requests * ROWS, LANES), F32),
        ],
        flops=2 * requests * w_output.size,
        moved=2 * w_output.size,
    )(meta, top, acc, returned.reshape(inbox * SLOT, LANES), wo)
    if pair:
        parts = [part, swap(part)]
    else:
        parts = [lax.all_gather(part, "tensor", axis=0, tiled=True)]
    attended, ffn_input, spread = call(
        functools.partial(gate_kernel, tp, units, len(parts)),
        [
            struct((rows if pair else requests, width), BF16),
            struct((requests, width), BF16),
            struct((requests, units), F32),
        ],
        [SMEM] + [VMEM] * (len(parts) + 4),
        flops=2 * requests * router.size,
        moved=2 * router.size,
    )(here, hidden_all, *parts, gains, router_t, routes_t)
    lifted = jnp.einsum("rd,dsu->sru", ffn_input, w_in, preferred_element_type=F32)
    shapes = [struct((requests, width), BF16)]
    if pair:
        shapes = [struct((rows, width), F32), struct((rows, width), BF16)]
    shares = call(
        expert_kernel,
        shapes,
        [SMEM] + [VMEM] * 3,
        flops=2 * requests * w_down.size,
        moved=2 * w_down.size,
    )(here, lifted, spread, wd)
    if pair:
        return attended, (shares[0] + swap(shares[1]).astype(F32)).astype(BF16)
    shares = lax.all_gather(shares[0], "tensor", axis=0)
    mine = lax.dynamic_slice_in_dim(shares, rank * rows, rows, axis=1)
    experts_out = jnp.sum(mine.astype(F32), axis=0).astype(BF16)
    attended = lax.dynamic_slice_in_dim(attended, rank * rows, rows, axis=0)
    return attended, experts_out


def solution(mesh):
    placed = (
        P(("replica", "tensor"), None),
        P(),
        P(None, "tensor"),
        P(None, "tensor", None),
        P("tensor", None),
        P("replica", None, "tensor", None),
        P("replica", None),
        P("replica"),
        P("replica"),
        P(),
        P(),
        P("replica", None),
        P(None, None, "tensor"),
        P("tensor", None),
    )
    return jax.shard_map(
        on_device,
        mesh=mesh,
        in_specs=placed,
        out_specs=(P(("replica", "tensor"), None), P(("replica", "tensor"), None)),
        check_vma=False,
    )
```

```python
import functools
import math

import jax
import jax.numpy as jnp
from jax import lax
from jax.experimental import pallas as pl
from jax.experimental.pallas import tpu as pltpu
from jax.sharding import PartitionSpec as P

HEAD_DIM = 64
EXPERTS = 40
FF = 512
CAP = 2
LANES = 128
SLOT = 8
ROWS = 16
META = 6

ATTN_SCALE = 0.015625
RESID_SCALE = 0.22
ROPE_BASE = 10000.0
EPSILON = 1e-06
NEG_FILL = -1e30

F32 = jnp.float32
BF16 = jnp.bfloat16
VMEM = pl.BlockSpec(memory_space=pltpu.VMEM)
SMEM = pl.BlockSpec(memory_space=pltpu.SMEM)
ANY = pl.BlockSpec(memory_space=pl.ANY)
HBM = pl.BlockSpec(memory_space=pltpu.HBM)
NT = (((1,), (1,)), ((), ()))
TN = (((0,), (0,)), ((), ()))


def iota(shape, axis):
    return lax.broadcasted_iota(jnp.int32, shape, axis)


def norm_rows(values, gain):
    factor = lax.rsqrt(jnp.mean(values * values, axis=-1, keepdims=True) + EPSILON)
    return (values * factor * gain).astype(BF16)


def rope_tables(ctx_row, requests):
    diagonal = iota((requests, requests), 0) == iota((requests, requests), 1)
    ctx = jnp.broadcast_to(ctx_row.astype(F32), (requests, requests))
    ctx = jnp.sum(jnp.where(diagonal, ctx, 0.0), axis=1, keepdims=True)
    lane = iota((requests, LANES), 1)
    index = (lane % (HEAD_DIM // 2)).astype(F32)
    inverse = jnp.exp(index * (-2.0 * math.log(ROPE_BASE) / HEAD_DIM))
    angles = ctx * inverse
    sign = jnp.where(lane % HEAD_DIM < HEAD_DIM // 2, -1.0, 1.0)
    return jnp.cos(angles), jnp.sin(angles) * sign


def rotate(chunk, cosine, sine):
    lane = iota(chunk.shape, 1)
    ahead = pltpu.roll(chunk, LANES - HEAD_DIM // 2, 1)
    behind = pltpu.roll(chunk, HEAD_DIM // 2, 1)
    turned = jnp.where(lane % HEAD_DIM < HEAD_DIM // 2, ahead, behind)
    return chunk * cosine + turned * sine


def copy_of(source, target, sem):
    return pltpu.make_async_copy(source, target, sem)


def prepare_kernel(
    pool, replicas, ids_ref, hidden_hbm, ctx_hbm, table_hbm, dest_hbm, attn_gain_hbm,
    ffn_gain_hbm, wq_hbm, wkv_hbm,
    hidden_ref, wq_ref, wkv_ref, gains_ref, cosine_ref, sine_ref, away_ref, span_ref,
    meta_ref, ctx, table, dest, gain_a, gain_f, raw, wide, sems,
):
    inbox = replicas * CAP
    requests = ctx.shape[1]
    entries = meta_ref.shape[1]
    depth = wkv_ref.shape[0]
    kv_local = raw.shape[0] // depth
    small = [
        copy_of(ctx_hbm, ctx, sems.at[0]),
        copy_of(table_hbm, table, sems.at[1]),
        copy_of(attn_gain_hbm, gain_a, sems.at[2]),
        copy_of(ffn_gain_hbm, gain_f, sems.at[3]),
        copy_of(dest_hbm, dest, sems.at[6]),
        copy_of(hidden_hbm, hidden_ref, sems.at[7]),
    ]
    raw_copy = copy_of(wkv_hbm, raw, sems.at[4])
    wq_copy = copy_of(wq_hbm, wq_ref, sems.at[5])
    for copy in small + [raw_copy, wq_copy]:
        copy.start()
    for copy in small:
        copy.wait()
    gains_ref[0:1, :] = gain_a[...].reshape(1, gain_a.shape[0])
    gains_ref[1:2, :] = gain_f[...].reshape(1, gain_f.shape[0])
    values = iota((entries, requests), 0)
    held = jnp.zeros((entries, requests), F32)
    spans = jnp.zeros((entries, requests), F32)
    ctx_row = ctx[...]
    for k in range(table.shape[0]):
        match = table[k : k + 1, :] == values
        filled = jnp.clip(ctx_row - k * 128, 0, 128).astype(F32)
        held = jnp.where(match, 1.0, held)
        spans = jnp.where(match, filled, spans)
    held16 = held.astype(BF16)
    numbers = (iota((SLOT, requests), 1) + 1).astype(BF16)
    ones = jnp.ones((SLOT, requests), BF16)
    holder = lax.dot_general(numbers, held16, NT, preferred_element_type=F32)
    covered = lax.dot_general(ones, spans.astype(BF16), NT, preferred_element_type=F32)
    meta_ref[0:1, :] = holder[0:1, :].astype(jnp.int32) - 1
    meta_ref[1:2, :] = covered[0:1, :].astype(jnp.int32)
    meta_ref[2:3, :] = jnp.zeros((1, entries), jnp.int32)
    meta_ref[2:3, 0 : dest.shape[1]] = dest[...]
    meta_ref[3:4, :] = jnp.full((1, entries), ids_ref[0], jnp.int32)
    slot = iota((inbox, requests), 0)
    lender = lax.rem(ids_ref[1] + slot // CAP, replicas)
    values = pool + lender * CAP + slot % CAP
    held = jnp.zeros((inbox, requests), F32)
    spans = jnp.zeros((inbox, requests), F32)
    for k in range(table.shape[0]):
        match = table[k : k + 1, :] == values
        filled = jnp.clip(ctx_row - k * 128, 0, 128).astype(F32)
        held = jnp.where(match, 1.0, held)
        spans = jnp.where(match, filled, spans)
    away_ref[...] = held.astype(BF16)
    away_span = jnp.sum(spans, axis=1, keepdims=True)
    span_ref[...] = jnp.broadcast_to(away_span, span_ref.shape)
    cosine, sine = rope_tables(ctx_row, requests)
    cosine_ref[...] = cosine
    sine_ref[...] = sine
    raw_copy.wait()
    if kv_local == 1:
        wkv_ref[...] = raw[...]
    else:
        wide[...] = raw[...].astype(F32)
        for k in range(kv_local):
            wkv_ref[:, k * LANES : (k + 1) * LANES] = wide[
                pl.ds(k, depth, stride=kv_local), :
            ].astype(BF16)
    wq_copy.wait()


def query_kernel(
    count, meta_ref, *refs,
):
    pieces = refs[:count]
    (gains_ref, wq_ref, cosine_ref, sine_ref, away_ref, span_ref,
     hidden_ref, normed_ref, packed_ref, *send_refs, scratch, sends) = refs[count:]
    requests = hidden_ref.shape[0]
    inbox = span_ref.shape[0]
    width = wq_ref.shape[1]
    chunks = -(-width // LANES)
    if count == 1:
        hidden = pieces[0][...]
    else:
        own, other = pieces[0][...], pieces[1][...]
        first = meta_ref[3:4, 0:1] == 0
        hidden = jnp.concatenate(
            [jnp.where(first, own, other), jnp.where(first, other, own)], axis=0
        )
    hidden_ref[...] = hidden
    normed = norm_rows(hidden.astype(F32), gains_ref[0:1, :])
    normed_ref[...] = normed
    queries = jnp.dot(normed, wq_ref[...], preferred_element_type=F32)
    if chunks * LANES > width:
        pad = jnp.zeros((requests, chunks * LANES - width), F32)
        queries = jnp.concatenate([queries, pad], axis=1)
    cosine, sine = cosine_ref[...], sine_ref[...]
    zeros = jnp.zeros((requests, LANES), F32)
    nothing = jnp.zeros((inbox, LANES), F32)
    for j in range(SLOT):
        here = pl.ds(j, requests, stride=SLOT)
        there = pl.ds(j, inbox, stride=SLOT)
        if j < chunks:
            chunk = rotate(queries[:, j * LANES : (j + 1) * LANES], cosine, sine)
            chunk = (chunk.astype(BF16).astype(F32) * ATTN_SCALE).astype(BF16)
            scratch[here, :] = chunk.astype(F32)
            sends[there, :] = jnp.dot(away_ref[...], chunk, preferred_element_type=F32)
        else:
            scratch[here, :] = zeros
            sends[there, :] = span_ref[...] if j == META else nothing
    packed_ref[...] = scratch[...]
    for d, send_ref in enumerate(send_refs):
        rows = (d + 1) * CAP * SLOT
        send_ref[...] = sends[rows : rows + CAP * SLOT, :].astype(BF16)


def unpack(packed):
    low = iota(packed.shape, 1) < HEAD_DIM
    even = jnp.where(low, packed, 0.0)
    odd = jnp.where(low, pltpu.roll(packed, HEAD_DIM, 1), 0.0)
    return jnp.concatenate([even, odd], axis=0)


def head_rows(heads):
    return [(h // 2) + SLOT * (h % 2) for h in range(heads)]


def token_of_column(heads, kv_local, columns):
    row = iota((ROWS, columns), 0)
    column = iota((ROWS, columns), 1)
    wanted = jnp.full((ROWS, columns), kv_local, jnp.int32)
    for h, place in enumerate(head_rows(heads)):
        wanted = jnp.where(row == place, h // (heads // kv_local), wanted)
    return jnp.where(column % kv_local == wanted, column // kv_local, 1 << 20)


def score_page(query, block):
    return lax.dot_general(query, block, NT, preferred_element_type=F32)


def weigh_page(scores, tokens, span):
    scores = jnp.where(tokens < span, scores, NEG_FILL)
    top = jnp.max(scores, axis=1, keepdims=True)
    weights = jnp.exp(scores - top)
    return top, jnp.sum(weights, axis=1, keepdims=True), weights.astype(BF16)


def value_page(weights, block):
    return jnp.dot(weights, block, preferred_element_type=F32)


def attend_pages(count, stage, query_of, block_of, span_of, tokens, keep):
    stages = [range(i, min(i + stage, count)) for i in range(0, count, stage)]
    scores = {p: score_page(query_of(p), block_of(p)) for p in stages[0]}
    for i, pages in enumerate(stages):
        if i + 1 < len(stages):
            ahead = {p: score_page(query_of(p), block_of(p)) for p in stages[i + 1]}
        weighed = {p: weigh_page(scores[p], tokens, span_of(p)) for p in pages}
        outs = {p: value_page(weighed[p][2], block_of(p)) for p in pages}
        for p in pages:
            keep(p, weighed[p][0], weighed[p][1], outs[p])
        if i + 1 < len(stages):
            scores = ahead


def first_kernel(
    heads, kv_local, first, local_pages, meta_ref, packed_ref, normed_ref, wkv_ref,
    cosine_ref, sine_ref, cache_hbm,
    queries_ref, fresh_ref, tops_ref, sums_ref, later_ref, lent_ref,
    pages, sems,
):
    requests = cosine_ref.shape[0]
    columns = pages.shape[1]
    lent = lent_ref.shape[0]
    mine = copy_of(cache_hbm.at[pl.ds(0, first)], pages, sems.at[0])
    lending = copy_of(cache_hbm.at[pl.ds(local_pages, lent)], lent_ref, sems.at[1])
    rest = copy_of(
        cache_hbm.at[pl.ds(first, local_pages - first)], later_ref, sems.at[2]
    )
    for copy in (mine, lending, rest):
        copy.start()
    low = iota((requests, LANES), 1) < HEAD_DIM
    cosine = jnp.where(low, cosine_ref[...], 1.0)
    sine = jnp.where(low, sine_ref[...], 0.0)
    packed = packed_ref[...].reshape(requests, SLOT, LANES)
    low3 = iota(packed.shape, 2) < HEAD_DIM
    queries_ref[:, 0:SLOT, :] = jnp.where(low3, packed, 0.0)
    queries_ref[:, SLOT:ROWS, :] = jnp.where(low3, pltpu.roll(packed, HEAD_DIM, 2), 0.0)
    projected = jnp.dot(normed_ref[...], wkv_ref[...], preferred_element_type=F32)
    new = [
        rotate(projected[:, k * LANES : (k + 1) * LANES], cosine, sine)
        .astype(BF16)
        .astype(F32)
        for k in range(kv_local)
    ]
    used = {place: h for h, place in enumerate(head_rows(heads))}
    for place in range(ROWS):
        value = jnp.zeros((requests, LANES), F32)
        if place in used:
            value = new[used[place] // (heads // kv_local)]
        fresh_ref[pl.ds(place, requests, stride=ROWS), :] = value
    tokens = token_of_column(heads, kv_local, columns)
    lower = iota((ROWS, LANES), 1) < HEAD_DIM
    mine.wait()

    def keep(p, top, total, out):
        tops_ref[p] = jnp.broadcast_to(top, (ROWS, LANES))
        sums_ref[p] = jnp.where(lower, total, out)

    attend_pages(
        first,
        4,
        lambda p: queries_ref[jnp.maximum(meta_ref[0, p], 0)].astype(BF16),
        lambda p: pages[p],
        lambda p: meta_ref[1, p],
        tokens,
        keep,
    )
    lending.wait()
    rest.wait()


def second_kernel(
    heads, kv_local, first, meta_ref, queries_ref, fresh_ref, tops_ref, sums_ref,
    pages_ref, order_hbm, wo_hbm, wd_hbm, router_hbm, routes_hbm,
    top_ref, acc_ref, wo_ref, wd_ref, router_ref, routes_ref,
    tops, sums, sems,
):
    del order_hbm
    requests = queries_ref.shape[0]
    count, columns, _ = pages_ref.shape
    local_pages = first + count
    copies = [
        copy_of(wo_hbm, wo_ref, sems.at[0]),
        copy_of(router_hbm, router_ref, sems.at[1]),
        copy_of(routes_hbm, routes_ref, sems.at[2]),
        copy_of(wd_hbm, wd_ref, sems.at[3]),
    ]
    for copy in copies:
        copy.start()
    tokens = token_of_column(heads, kv_local, columns)
    lower = iota((ROWS, LANES), 1) < HEAD_DIM
    added = fresh_ref[...].reshape(requests, ROWS, LANES)
    low16 = iota(added.shape, 2) < HEAD_DIM
    score = jnp.sum(queries_ref[...] * added, axis=2, keepdims=True)
    before = jnp.broadcast_to(score, added.shape)
    start = jnp.where(low16, 1.0, added)

    def keep(p, top, total, out):
        tops[p] = jnp.broadcast_to(top, (ROWS, LANES))
        sums[p] = jnp.where(lower, total, out)

    attend_pages(
        count,
        4,
        lambda p: queries_ref[jnp.maximum(meta_ref[0, first + p], 0)].astype(BF16),
        lambda p: pages_ref[p],
        lambda p: meta_ref[1, first + p],
        tokens,
        keep,
    )

    def place_of(p):
        owner = meta_ref[0, p]
        return jnp.where(owner < 0, requests, owner)

    def top_of(p):
        return tops_ref[p] if p < first else tops[p - first]

    def sum_of(p):
        return sums_ref[p] if p < first else sums[p - first]

    top_ref[0:requests] = before
    for p in range(local_pages):
        place = place_of(p)
        top_ref[place] = jnp.maximum(top_ref[place], top_of(p))
    acc_ref[0:requests] = start * jnp.exp(before - top_ref[0:requests])
    for p in range(local_pages):
        place = place_of(p)
        acc_ref[place] = acc_ref[place] + sum_of(p) * jnp.exp(top_of(p) - top_ref[place])
    for copy in copies:
        copy.wait()


def lent_kernel(
    heads, kv_local, replicas, meta_ref, ids_ref, pages_ref, *refs,
):
    asked_refs, reply_refs = refs[: replicas - 1], refs[replicas - 1 : -2]
    asked, reply = refs[-2:]
    outgoing, columns, _ = pages_ref.shape
    block = CAP * SLOT
    for d, asked_ref in enumerate(asked_refs):
        asked[(d + 1) * block : (d + 2) * block, :] = asked_ref[...].astype(F32)
    reply[...] = jnp.zeros(reply.shape, F32)
    tokens = token_of_column(heads, kv_local, columns).astype(F32)
    low = iota((SLOT, LANES), 1) < HEAD_DIM
    lane = iota((SLOT, LANES), 1)
    row = iota((SLOT, LANES), 0)

    def terms(total, offset):
        leading = total.astype(BF16).astype(F32)
        rest = total - leading
        second = rest.astype(BF16).astype(F32)
        third = rest - second
        spot = lane - offset - 3 * row
        placed = jnp.where(spot == 0, leading, 0.0)
        placed = jnp.where(spot == 1, second, placed)
        return jnp.where(spot == 2, third, placed)

    def rows_of(j):
        dest = meta_ref[2, j]
        rank = jnp.int32(0)
        for e in range(j):
            rank = rank + (meta_ref[2, e] == dest).astype(jnp.int32)
        away = dest - ids_ref[1]
        away = jnp.where(away < 0, away + replicas, away)
        back = jnp.where(away == 0, 0, replicas - away)
        return [
            pl.ds(pl.multiple_of((x * CAP + rank) * SLOT, SLOT), SLOT) for x in (back, away)
        ]

    places = [rows_of(j) for j in range(outgoing)]
    packed = [asked[rows[0], :] for rows in places]
    replies = {}

    def keep(j, top, total, out):
        out = out / total
        logs = top + jnp.log(total)
        even = pltpu.roll(out[0:SLOT], HEAD_DIM, 1)
        both = jnp.where(low, even, out[SLOT:ROWS])
        line = jnp.sum(
            terms(logs[0:SLOT], 0) + terms(logs[SLOT:ROWS], HEAD_DIM), axis=0, keepdims=True
        )
        replies[j] = jnp.where(row == META, line, both)

    attend_pages(
        outgoing,
        4,
        lambda j: unpack(packed[j]).astype(BF16),
        lambda j: pages_ref[j],
        lambda j: packed[j][META : META + 1, 0:1],
        tokens,
        keep,
    )
    for j in range(outgoing):
        reply[places[j][1], :] = replies[j]
    for d, reply_ref in enumerate(reply_refs):
        reply_ref[...] = reply[(d + 1) * block : (d + 2) * block, :].astype(BF16)


def combine_kernel(
    heads, pool, replicas, meta_ref, ids_ref, top_ref, acc_ref, wo_ref, *refs,
):
    reply_refs = refs[: replicas - 1]
    part_ref, tops, accs, reply, finals = refs[replicas - 1 :]
    requests = top_ref.shape[0] - 1
    inbox = (replicas - 1) * CAP
    chunks = -(-heads // 2)
    block = CAP * SLOT
    for d, reply_ref in enumerate(reply_refs):
        reply[d * block : (d + 1) * block, :] = reply_ref[...].astype(F32)
    tops[...] = top_ref[...]
    low = iota((SLOT, LANES), 1) < HEAD_DIM
    lane = iota((SLOT, LANES), 1)
    row = iota((SLOT, LANES), 0)
    mine = (lane % HEAD_DIM) // 3 == row

    def place_of(s):
        lender = ids_ref[1] - (s // CAP + 1)
        lender = jnp.where(lender < 0, lender + replicas, lender)
        owner = meta_ref[0, pool + lender * CAP + s % CAP]
        return jnp.where(owner < 0, requests, owner)

    def logs_of(s):
        line = reply[s * SLOT + META : s * SLOT + META + 1, :]
        line = jnp.where(mine, jnp.broadcast_to(line, (SLOT, LANES)), 0.0)
        even = jnp.sum(jnp.where(low, line, 0.0), axis=1, keepdims=True)
        odd = jnp.sum(jnp.where(low, 0.0, line), axis=1, keepdims=True)
        logs = jnp.concatenate([even, odd], axis=0)
        return jnp.broadcast_to(logs, (ROWS, LANES))

    logs = [logs_of(s) for s in range(inbox)]
    for s in range(inbox):
        place = place_of(s)
        tops[place] = jnp.maximum(tops[place], logs[s])
    accs[0:requests] = acc_ref[0:requests] * jnp.exp(
        top_ref[0:requests] - tops[0:requests]
    )
    for s in range(inbox):
        place = place_of(s)
        packed = reply[s * SLOT : (s + 1) * SLOT, :]
        even = jnp.where(low, 1.0, pltpu.roll(packed, HEAD_DIM, 1))
        odd = jnp.where(low, 1.0, packed)
        both = jnp.concatenate([even, odd], axis=0)
        accs[place] = accs[place] + both * jnp.exp(logs[s] - tops[place])
    whole = accs[0:requests]
    finals[...] = (whole / pltpu.roll(whole, HEAD_DIM, 2)).reshape(
        requests * ROWS, LANES
    )
    wide = iota((requests, LANES), 1) < HEAD_DIM
    parts = []
    for j in range(chunks):
        even = finals[pl.ds(j, requests, stride=ROWS), :]
        odd = finals[pl.ds(SLOT + j, requests, stride=ROWS), :]
        parts.append(jnp.where(wide, pltpu.roll(even, HEAD_DIM, 1), odd).astype(BF16))
    attention = jnp.concatenate(parts, axis=1)[:, : heads * HEAD_DIM]
    part_ref[...] = jnp.dot(
        attention, wo_ref[...], preferred_element_type=F32
    ).astype(BF16)


def own_rows(values, first):
    half = values.shape[0] // 2
    return jnp.where(first, values[:half], values[half:])


def gate_kernel(
    tp, units, count, meta_ref, hidden_ref, *refs,
):
    pieces = refs[:count]
    (gains_ref, router_ref, routes_ref, attended_ref, input_ref, spread_ref) = refs[count:]
    requests = hidden_ref.shape[0]
    if count == 2:
        summed = pieces[0][...].astype(F32) + pieces[1][...].astype(F32)
    else:
        summed = pieces[0][0:requests, :].astype(F32)
        for t in range(1, tp):
            part = pieces[0][t * requests : (t + 1) * requests, :]
            summed = summed + part.astype(F32)
    attended = (hidden_ref[...].astype(F32) + RESID_SCALE * summed).astype(BF16)
    if count == 2:
        attended_ref[...] = own_rows(attended, meta_ref[3:4, 0:1] == 0)
    else:
        attended_ref[...] = attended
    ffn_input = norm_rows(attended.astype(F32), gains_ref[1:2, :])
    input_ref[...] = ffn_input
    logits = lax.dot_general(router_ref[...], ffn_input, NT, preferred_element_type=F32)
    expert = iota(logits.shape, 0)
    named = jnp.zeros(logits.shape, F32)
    for k in range(routes_ref.shape[0]):
        named = jnp.where(routes_ref[k : k + 1, :] == expert, 1.0, named)
    chosen = named > 0.5
    top = jnp.max(jnp.where(chosen, logits, NEG_FILL), axis=0, keepdims=True)
    weights = jnp.where(chosen, jnp.exp(logits - top), 0.0)
    gates = weights / jnp.sum(weights, axis=0, keepdims=True)
    unit = iota((EXPERTS, units), 1) + meta_ref[3:4, 0:1] * units
    owner = (unit // FF == iota((EXPERTS, units), 0)).astype(F32)
    spread_ref[...] = lax.dot_general(
        gates, owner, TN, preferred_element_type=F32, precision=lax.Precision.HIGHEST
    )


def expert_kernel(meta_ref, lifted_ref, spread_ref, wd_ref, *outs):
    gate = lifted_ref[0]
    active = gate / (1.0 + jnp.exp(-gate)) * lifted_ref[1] * spread_ref[...]
    share = jnp.dot(active.astype(BF16), wd_ref[...], preferred_element_type=F32)
    if len(outs) == 2:
        first = meta_ref[3:4, 0:1] == 0
        outs[0][...] = own_rows(share, first)
        outs[1][...] = own_rows(share, jnp.logical_not(first)).astype(BF16)
    else:
        outs[0][...] = share.astype(BF16)


def call(body, outs, in_specs, scratch=(), limit=16, flops=0, moved=0):
    return pl.pallas_call(
        body,
        out_shape=outs,
        in_specs=in_specs,
        out_specs=[VMEM] * len(outs),
        scratch_shapes=list(scratch),
        compiler_params=pltpu.CompilerParams(vmem_limit_bytes=limit << 20),
        cost_estimate=pl.CostEstimate(
            flops=flops, bytes_accessed=moved, transcendentals=0
        ),
    )


def swap(values):
    return lax.ppermute(values, "tensor", [(0, 1), (1, 0)])


def on_device(
    hidden,
    attn_gain,
    w_query,
    w_keyvalue,
    w_output,
    cache,
    page_table,
    ctx_len,
    move_dest,
    ffn_gain,
    router,
    routes,
    w_in,
    w_down,
):
    replicas = lax.axis_size("replica")
    tp = lax.axis_size("tensor")
    rank = lax.axis_index("tensor").astype(jnp.int32)
    rows, width = hidden.shape
    pool, page_len, kv_local, _ = cache.shape
    outgoing = move_dest.shape[0]
    local_pages = pool - outgoing
    requests = page_table.shape[0]
    heads = w_query.shape[1] // HEAD_DIM
    inbox = replicas * CAP
    units = w_down.shape[0]
    columns = page_len * kv_local
    entries = -(-(pool + inbox) // LANES) * LANES
    first = local_pages // 2
    struct = jax.ShapeDtypeStruct
    pair = tp == 2
    ids = jnp.stack([rank, lax.axis_index("replica").astype(jnp.int32)])
    hops = range(1, replicas)

    def pin(values):
        return pltpu.with_memory_space_constraint(values, pltpu.HBM)

    def send(blocks):
        return [
            lax.ppermute(block, "replica", [(r, (r + d) % replicas) for r in range(replicas)])
            for d, block in zip(hops, blocks)
        ]

    blocks = pin(cache.reshape(pool, columns, LANES))
    if pair:
        pieces = [hidden, swap(hidden)]
    else:
        pieces = [lax.all_gather(hidden, "tensor", axis=0, tiled=True)]
    own, wq, wkv, gains, cosine, sine, away, away_span, meta = call(
        functools.partial(prepare_kernel, pool, replicas),
        [
            struct(hidden.shape, BF16),
            struct(w_query.shape, BF16),
            struct((width, kv_local * LANES), BF16),
            struct((2, width), F32),
            struct((requests, LANES), F32),
            struct((requests, LANES), F32),
            struct((inbox, requests), BF16),
            struct((inbox, LANES), F32),
            struct((4, entries), jnp.int32),
        ],
        [SMEM] + [HBM] * 8,
        [
            pltpu.VMEM((1, requests), jnp.int32),
            pltpu.VMEM((page_table.shape[1], requests), jnp.int32),
            pltpu.VMEM((1, outgoing), jnp.int32),
            pltpu.VMEM((width,), F32),
            pltpu.VMEM((width,), F32),
            pltpu.VMEM((width * kv_local, LANES), BF16),
            pltpu.VMEM((width * kv_local, LANES), F32),
            pltpu.SemaphoreType.DMA((8,)),
        ],
        moved=2 * (w_query.size + w_keyvalue.size),
    )(
        ids,
        pin(hidden),
        pin(ctx_len.reshape(1, requests)),
        pin(page_table.T),
        pin(move_dest.reshape(1, outgoing)),
        pin(attn_gain),
        pin(ffn_gain),
        pin(w_query),
        pin(w_keyvalue.reshape(width * kv_local, LANES)),
    )
    if pair:
        pieces[0] = own
    block = struct((CAP * SLOT, LANES), BF16)
    hidden_all, normed, packed, *sends = call(
        functools.partial(query_kernel, len(pieces)),
        [
            struct((requests, width), BF16),
            struct((requests, width), BF16),
            struct((requests * SLOT, LANES), F32),
            *[block for _ in hops],
        ],
        [VMEM] * (len(pieces) + 7),
        [
            pltpu.VMEM((requests * SLOT, LANES), F32),
            pltpu.VMEM((inbox * SLOT, LANES), F32),
        ],
        flops=4 * requests * width * w_query.shape[1],
        moved=2 * w_query.size,
    )(meta, *pieces, gains, wq, cosine, sine, away, away_span)
    asked = send(sends)
    partials = [struct((first, ROWS, LANES), F32)] * 2
    queries, fresh, tops, sums, later, lent = call(
        functools.partial(first_kernel, heads, kv_local, first, local_pages),
        [
            struct((requests, ROWS, LANES), F32),
            struct((requests * ROWS, LANES), F32),
            *partials,
            struct((local_pages - first, columns, LANES), BF16),
            struct((outgoing, columns, LANES), BF16),
        ],
        [SMEM] + [VMEM] * 5 + [HBM],
        [
            pltpu.VMEM((first, columns, LANES), BF16),
            pltpu.SemaphoreType.DMA((3,)),
        ],
        flops=4 * ROWS * columns * LANES * first,
        moved=2 * columns * LANES * pool,
    )(meta, packed, normed, wkv, cosine, sine, blocks)
    replies = call(
        functools.partial(lent_kernel, heads, kv_local, replicas),
        [block for _ in hops],
        [SMEM, SMEM, VMEM] + [VMEM for _ in hops],
        [
            pltpu.VMEM((inbox * SLOT, LANES), F32),
            pltpu.VMEM((inbox * SLOT, LANES), F32),
        ],
        flops=4 * ROWS * columns * LANES * outgoing,
        moved=2 * columns * LANES * outgoing,
    )(meta, ids, lent, *asked)
    returned = send(replies)
    top, acc, wo, wd, router_t, routes_t = call(
        functools.partial(second_kernel, heads, kv_local, first),
        [
            struct((requests + 1, ROWS, LANES), F32),
            struct((requests + 1, ROWS, LANES), F32),
            struct(w_output.shape, BF16),
            struct(w_down.shape, BF16),
            struct(router.shape[::-1], BF16),
            struct(routes.shape[::-1], jnp.int32),
        ],
        [SMEM] + [VMEM] * 5 + [ANY] + [HBM] * 4,
        [
            pltpu.VMEM((local_pages - first, ROWS, LANES), F32),
            pltpu.VMEM((local_pages - first, ROWS, LANES), F32),
            pltpu.SemaphoreType.DMA((4,)),
        ],
        flops=4 * ROWS * columns * LANES * (local_pages - first),
        moved=2 * (w_output.size + w_down.size + router.size),
    )(
        meta, queries, fresh, tops, sums, later,
        replies[0], pin(w_output), pin(w_down), pin(router.T), pin(routes.T),
    )
    (part,) = call(
        functools.partial(combine_kernel, heads, pool, replicas),
        [struct((requests, width), BF16)],
        [SMEM, SMEM, VMEM, VMEM, VMEM] + [VMEM for _ in hops],
        [
            pltpu.VMEM((requests + 1, ROWS, LANES), F32),
            pltpu.VMEM((requests + 1, ROWS, LANES), F32),
            pltpu.VMEM((inbox * SLOT, LANES), F32),
            pltpu.VMEM((requests * ROWS, LANES), F32),
        ],
        flops=2 * requests * w_output.size,
        moved=2 * w_output.size,
    )(meta, ids, top, acc, wo, *returned)
    if pair:
        parts = [part, swap(part)]
    else:
        parts = [lax.all_gather(part, "tensor", axis=0, tiled=True)]
    attended, ffn_input, spread = call(
        functools.partial(gate_kernel, tp, units, len(parts)),
        [
            struct((rows if pair else requests, width), BF16),
            struct((requests, width), BF16),
            struct((requests, units), F32),
        ],
        [VMEM] * (len(parts) + 5),
        flops=2 * requests * router.size,
        moved=2 * router.size,
    )(meta, hidden_all, *parts, gains, router_t, routes_t)
    lifted = jnp.einsum("rd,dsu->sru", ffn_input, w_in, preferred_element_type=F32)
    shapes = [struct((requests, width), BF16)]
    if pair:
        shapes = [struct((rows, width), F32), struct((rows, width), BF16)]
    shares = call(
        expert_kernel,
        shapes,
        [VMEM] * 4,
        flops=2 * requests * w_down.size,
        moved=2 * w_down.size,
    )(meta, lifted, spread, wd)
    if pair:
        return attended, (shares[0] + swap(shares[1]).astype(F32)).astype(BF16)
    shares = lax.all_gather(shares[0], "tensor", axis=0)
    mine = lax.dynamic_slice_in_dim(shares, rank * rows, rows, axis=1)
    experts_out = jnp.sum(mine.astype(F32), axis=0).astype(BF16)
    attended = lax.dynamic_slice_in_dim(attended, rank * rows, rows, axis=0)
    return attended, experts_out


def solution(mesh):
    placed = (
        P(("replica", "tensor"), None),
        P(),
        P(None, "tensor"),
        P(None, "tensor", None),
        P("tensor", None),
        P("replica", None, "tensor", None),
        P("replica", None),
        P("replica"),
        P("replica"),
        P(),
        P(),
        P("replica", None),
        P(None, None, "tensor"),
        P("tensor", None),
    )
    return jax.shard_map(
        on_device,
        mesh=mesh,
        in_specs=placed,
        out_specs=(P(("replica", "tensor"), None), P(("replica", "tensor"), None)),
        check_vma=False,
    )
```

```python
import functools
import math

import jax
import jax.numpy as jnp
from jax import lax
from jax.experimental import pallas as pl
from jax.experimental.pallas import tpu as pltpu
from jax.sharding import PartitionSpec as P

HEAD_DIM = 64
EXPERTS = 40
FF = 512
CAP = 2
LANES = 128
SLOT = 8
ROWS = 16
META = 6

ATTN_SCALE = 0.015625
RESID_SCALE = 0.22
ROPE_BASE = 10000.0
EPSILON = 1e-06
NEG_FILL = -1e30

F32 = jnp.float32
BF16 = jnp.bfloat16
VMEM = pl.BlockSpec(memory_space=pltpu.VMEM)
SMEM = pl.BlockSpec(memory_space=pltpu.SMEM)
ANY = pl.BlockSpec(memory_space=pl.ANY)
HBM = pl.BlockSpec(memory_space=pltpu.HBM)
NT = (((1,), (1,)), ((), ()))
TN = (((0,), (0,)), ((), ()))


def iota(shape, axis):
    return lax.broadcasted_iota(jnp.int32, shape, axis)


def norm_rows(values, gain):
    factor = lax.rsqrt(jnp.mean(values * values, axis=-1, keepdims=True) + EPSILON)
    return (values * factor * gain).astype(BF16)


def rope_tables(ctx_row, requests):
    diagonal = iota((requests, requests), 0) == iota((requests, requests), 1)
    ctx = jnp.broadcast_to(ctx_row.astype(F32), (requests, requests))
    ctx = jnp.sum(jnp.where(diagonal, ctx, 0.0), axis=1, keepdims=True)
    lane = iota((requests, LANES), 1)
    index = (lane % (HEAD_DIM // 2)).astype(F32)
    inverse = jnp.exp(index * (-2.0 * math.log(ROPE_BASE) / HEAD_DIM))
    angles = ctx * inverse
    sign = jnp.where(lane % HEAD_DIM < HEAD_DIM // 2, -1.0, 1.0)
    return jnp.cos(angles), jnp.sin(angles) * sign


def rotate(chunk, cosine, sine):
    lane = iota(chunk.shape, 1)
    ahead = pltpu.roll(chunk, LANES - HEAD_DIM // 2, 1)
    behind = pltpu.roll(chunk, HEAD_DIM // 2, 1)
    turned = jnp.where(lane % HEAD_DIM < HEAD_DIM // 2, ahead, behind)
    return chunk * cosine + turned * sine


def copy_of(source, target, sem):
    return pltpu.make_async_copy(source, target, sem)


def prepare_kernel(
    pool, replicas, ids_ref, hidden_hbm, ctx_hbm, table_hbm, dest_hbm, attn_gain_hbm,
    wq_hbm,
    hidden_ref, wq_ref, gain_ref, tables_ref, away_ref, span_ref, meta_ref,
    tables_hbm, meta_hbm, ctx, table, dest, gain, sems,
):
    inbox = replicas * CAP
    requests = ctx.shape[1]
    entries = meta_ref.shape[1]
    small = [
        copy_of(ctx_hbm, ctx, sems.at[0]),
        copy_of(table_hbm, table, sems.at[1]),
        copy_of(dest_hbm, dest, sems.at[2]),
        copy_of(attn_gain_hbm, gain, sems.at[3]),
    ]
    large = [
        copy_of(hidden_hbm, hidden_ref, sems.at[4]),
        copy_of(wq_hbm, wq_ref, sems.at[5]),
    ]
    for copy in small + large:
        copy.start()
    for copy in small:
        copy.wait()
    gain_ref[...] = gain[...].reshape(1, gain.shape[0])
    ctx_row = ctx[...]

    def claims(values):
        held = jnp.zeros(values.shape, F32)
        spans = jnp.zeros(values.shape, F32)
        for k in range(table.shape[0]):
            match = table[k : k + 1, :] == values
            filled = jnp.clip(ctx_row - k * 128, 0, 128).astype(F32)
            held = jnp.where(match, 1.0, held)
            spans = jnp.where(match, filled, spans)
        return held.astype(BF16), spans

    held, spans = claims(iota((entries, requests), 0))
    numbers = (iota((SLOT, requests), 1) + 1).astype(BF16)
    ones = jnp.ones((SLOT, requests), BF16)
    holder = lax.dot_general(numbers, held, NT, preferred_element_type=F32)
    covered = lax.dot_general(ones, spans.astype(BF16), NT, preferred_element_type=F32)
    meta_ref[0:1, :] = holder[0:1, :].astype(jnp.int32) - 1
    meta_ref[1:2, :] = covered[0:1, :].astype(jnp.int32)
    meta_ref[2:3, :] = jnp.zeros((1, entries), jnp.int32)
    meta_ref[2:3, 0 : dest.shape[1]] = dest[...]
    meta_ref[3:4, :] = jnp.full((1, entries), ids_ref[0], jnp.int32)
    cosine, sine = rope_tables(ctx_row, requests)
    tables_ref[0] = cosine
    tables_ref[1] = sine
    parked = [
        copy_of(tables_ref, tables_hbm, sems.at[6]),
        copy_of(meta_ref, meta_hbm, sems.at[7]),
    ]
    for copy in parked:
        copy.start()
    held, spans = claims(pool + iota((inbox, requests), 0))
    away_ref[...] = held
    away_span = jnp.sum(spans, axis=1, keepdims=True)
    span_ref[...] = jnp.broadcast_to(away_span, span_ref.shape)
    for copy in large + parked:
        copy.wait()


def query_kernel(
    count, meta_ref, *refs,
):
    pieces = refs[:count]
    (gain_ref, wq_ref, tables_ref, away_ref, span_ref,
     hidden_hbm, normed_hbm, packed_hbm, send_hbm,
     hiddens, norms, packs, sends, sends16, sems) = refs[count:]
    requests = hiddens.shape[0]
    inbox = span_ref.shape[0]
    width = wq_ref.shape[1]
    chunks = -(-width // LANES)
    if count == 1:
        hidden = pieces[0][...]
    else:
        own, other = pieces[0][...], pieces[1][...]
        first = meta_ref[3:4, 0:1] == 0
        hidden = jnp.concatenate(
            [jnp.where(first, own, other), jnp.where(first, other, own)], axis=0
        )
    hiddens[...] = hidden
    normed = norm_rows(hidden.astype(F32), gain_ref[...])
    norms[...] = normed
    early = [
        copy_of(hiddens, hidden_hbm, sems.at[0]),
        copy_of(norms, normed_hbm, sems.at[1]),
    ]
    for copy in early:
        copy.start()
    queries = jnp.dot(normed, wq_ref[...], preferred_element_type=F32)
    if chunks * LANES > width:
        pad = jnp.zeros((requests, chunks * LANES - width), F32)
        queries = jnp.concatenate([queries, pad], axis=1)
    cosine, sine = tables_ref[0], tables_ref[1]
    zeros = jnp.zeros((requests, LANES), F32)
    nothing = jnp.zeros((inbox, LANES), F32)
    for j in range(SLOT):
        here = pl.ds(j, requests, stride=SLOT)
        there = pl.ds(j, inbox, stride=SLOT)
        if j < chunks:
            chunk = rotate(queries[:, j * LANES : (j + 1) * LANES], cosine, sine)
            chunk = (chunk.astype(BF16).astype(F32) * ATTN_SCALE).astype(BF16)
            packs[here, :] = chunk.astype(F32)
            sends[there, :] = jnp.dot(away_ref[...], chunk, preferred_element_type=F32)
        else:
            packs[here, :] = zeros
            sends[there, :] = span_ref[...] if j == META else nothing
    sends16[...] = sends[...].astype(BF16)
    late = [
        copy_of(sends16, send_hbm, sems.at[2]),
        copy_of(packs, packed_hbm, sems.at[3]),
    ]
    for copy in late:
        copy.start()
    for copy in early + late:
        copy.wait()


def unpack(packed):
    low = iota(packed.shape, 1) < HEAD_DIM
    even = jnp.where(low, packed, 0.0)
    odd = jnp.where(low, pltpu.roll(packed, HEAD_DIM, 1), 0.0)
    return jnp.concatenate([even, odd], axis=0)


def head_rows(heads):
    return [(h // 2) + SLOT * (h % 2) for h in range(heads)]


def token_of_column(heads, kv_local, columns):
    row = iota((ROWS, columns), 0)
    column = iota((ROWS, columns), 1)
    wanted = jnp.full((ROWS, columns), kv_local, jnp.int32)
    for h, place in enumerate(head_rows(heads)):
        wanted = jnp.where(row == place, h // (heads // kv_local), wanted)
    return jnp.where(column % kv_local == wanted, column // kv_local, 1 << 20)


def score_page(query, block):
    return lax.dot_general(query, block, NT, preferred_element_type=F32)


def weigh_page(scores, tokens, span):
    scores = jnp.where(tokens < span, scores, NEG_FILL)
    top = jnp.max(scores, axis=1, keepdims=True)
    weights = jnp.exp(scores - top)
    return top, jnp.sum(weights, axis=1, keepdims=True), weights.astype(BF16)


def value_page(weights, block):
    return jnp.dot(weights, block, preferred_element_type=F32)


def attend_pages(count, stage, query_of, block_of, span_of, tokens, keep):
    stages = [range(i, min(i + stage, count)) for i in range(0, count, stage)]
    scores = {p: score_page(query_of(p), block_of(p)) for p in stages[0]}
    for i, pages in enumerate(stages):
        if i + 1 < len(stages):
            ahead = {p: score_page(query_of(p), block_of(p)) for p in stages[i + 1]}
        weighed = {p: weigh_page(scores[p], tokens, span_of(p)) for p in pages}
        outs = {p: value_page(weighed[p][2], block_of(p)) for p in pages}
        for p in pages:
            keep(p, weighed[p][0], weighed[p][1], outs[p])
        if i + 1 < len(stages):
            scores = ahead


def spread_queries(target, packed):
    low = iota(packed.shape, 2) < HEAD_DIM
    target[:, 0:SLOT, :] = jnp.where(low, packed, 0.0)
    target[:, SLOT:ROWS, :] = jnp.where(low, pltpu.roll(packed, HEAD_DIM, 2), 0.0)


def first_kernel(
    heads, kv_local, meta_hbm, packed_hbm, normed_hbm, wkv_hbm, tables_hbm, cache_hbm,
    new_hbm, tops_hbm, sums_hbm,
    meta, packed, normed, raw, wide, tables, pages, queries, new, tops, sums, sems,
):
    requests, depth = normed.shape
    count, columns, _ = pages.shape
    small = [
        copy_of(meta_hbm, meta, sems.at[0]),
        copy_of(packed_hbm, packed, sems.at[1]),
        copy_of(normed_hbm, normed, sems.at[2]),
        copy_of(tables_hbm, tables, sems.at[3]),
    ]
    weights = copy_of(wkv_hbm, raw, sems.at[4])
    paging = copy_of(cache_hbm.at[pl.ds(0, count)], pages, sems.at[5])
    for copy in small + [weights, paging]:
        copy.start()
    for copy in small:
        copy.wait()
    spread_queries(queries, packed[...].reshape(requests, SLOT, LANES))
    tokens = token_of_column(heads, kv_local, columns)
    lower = iota((ROWS, LANES), 1) < HEAD_DIM
    low = iota((requests, LANES), 1) < HEAD_DIM
    cosine = jnp.where(low, tables[0], 1.0)
    sine = jnp.where(low, tables[1], 0.0)
    weights.wait()
    if kv_local > 1:
        wide[...] = raw[...].astype(F32)
    for k in range(kv_local):
        if kv_local > 1:
            weight = wide[pl.ds(k, depth, stride=kv_local), :].astype(BF16)
        else:
            weight = raw[...]
        projected = jnp.dot(normed[...], weight, preferred_element_type=F32)
        new[k] = rotate(projected, cosine, sine).astype(BF16).astype(F32)
    paging.wait()

    def keep(p, top, total, out):
        tops[p] = jnp.broadcast_to(top, (ROWS, LANES))
        sums[p] = jnp.where(lower, total, out)

    attend_pages(
        count,
        4,
        lambda p: queries[jnp.maximum(meta[0, p], 0)].astype(BF16),
        lambda p: pages[p],
        lambda p: meta[1, p],
        tokens,
        keep,
    )
    parked = [
        copy_of(new, new_hbm, sems.at[6]),
        copy_of(tops, tops_hbm, sems.at[7]),
        copy_of(sums, sums_hbm, sems.at[8]),
    ]
    for copy in parked:
        copy.start()
    for copy in parked:
        copy.wait()


def second_kernel(
    heads, kv_local, first, meta_hbm, packed_hbm, new_hbm, tops_hbm, sums_hbm,
    cache_hbm, order_hbm, hidden_hbm, gain_hbm, wo_hbm, wd_hbm, router_hbm, routes_hbm,
    top_ref, acc_ref, meta_ref, hidden_ref, gain_ref, wo_ref, wd_ref, router_ref,
    routes_ref,
    meta, packed, new, tops, sums, gain, pages, queries, fresh, sems,
):
    del order_hbm
    requests = queries.shape[0]
    local_pages, columns, _ = pages.shape
    count = local_pages - first
    rest = pl.ds(first, count)
    small = [
        copy_of(meta_hbm, meta, sems.at[0]),
        copy_of(packed_hbm, packed, sems.at[1]),
        copy_of(new_hbm, new, sems.at[2]),
    ]
    paging = copy_of(cache_hbm.at[rest], pages.at[rest], sems.at[3])
    earlier = [
        copy_of(tops_hbm, tops.at[pl.ds(0, first)], sems.at[4]),
        copy_of(sums_hbm, sums.at[pl.ds(0, first)], sems.at[5]),
        copy_of(gain_hbm, gain, sems.at[6]),
    ]
    later = [
        copy_of(wo_hbm, wo_ref, sems.at[7]),
        copy_of(meta_hbm, meta_ref, sems.at[8]),
        copy_of(hidden_hbm, hidden_ref, sems.at[9]),
        copy_of(router_hbm, router_ref, sems.at[10]),
        copy_of(routes_hbm, routes_ref, sems.at[11]),
        copy_of(wd_hbm, wd_ref, sems.at[12]),
    ]
    for copy in small + [paging] + earlier + later:
        copy.start()
    for copy in small:
        copy.wait()
    spread_queries(queries, packed[...].reshape(requests, SLOT, LANES))
    used = {place: h for h, place in enumerate(head_rows(heads))}
    for place in range(ROWS):
        value = jnp.zeros((requests, LANES), F32)
        if place in used:
            value = new[used[place] // (heads // kv_local)]
        fresh[pl.ds(place, requests, stride=ROWS), :] = value
    tokens = token_of_column(heads, kv_local, columns)
    lower = iota((ROWS, LANES), 1) < HEAD_DIM
    added = fresh[...].reshape(requests, ROWS, LANES)
    low16 = iota(added.shape, 2) < HEAD_DIM
    score = jnp.sum(queries[...] * added, axis=2, keepdims=True)
    before = jnp.broadcast_to(score, added.shape)
    start = jnp.where(low16, 1.0, added)
    top_ref[0:requests] = before
    paging.wait()

    def keep(p, top, total, out):
        tops[first + p] = jnp.broadcast_to(top, (ROWS, LANES))
        sums[first + p] = jnp.where(lower, total, out)

    attend_pages(
        count,
        4,
        lambda p: queries[jnp.maximum(meta[0, first + p], 0)].astype(BF16),
        lambda p: pages[first + p],
        lambda p: meta[1, first + p],
        tokens,
        keep,
    )
    for copy in earlier:
        copy.wait()
    gain_ref[...] = gain[...].reshape(1, gain.shape[0])

    def place_of(p):
        owner = meta[0, p]
        return jnp.where(owner < 0, requests, owner)

    for p in range(local_pages):
        place = place_of(p)
        top_ref[place] = jnp.maximum(top_ref[place], tops[p])
    acc_ref[0:requests] = start * jnp.exp(before - top_ref[0:requests])
    for p in range(local_pages):
        place = place_of(p)
        acc_ref[place] = acc_ref[place] + sums[p] * jnp.exp(tops[p] - top_ref[place])
    for copy in later:
        copy.wait()


def lent_kernel(
    heads, kv_local, local_pages, meta_hbm, asked_ref, cache_hbm, reply_ref,
    meta, pages, asked, reply, sems,
):
    outgoing, columns, _ = pages.shape
    meta_copy = copy_of(meta_hbm, meta, sems.at[0])
    paging = copy_of(cache_hbm.at[pl.ds(local_pages, outgoing)], pages, sems.at[1])
    meta_copy.start()
    paging.start()
    asked[...] = asked_ref[...].astype(F32)
    reply[...] = jnp.zeros(reply.shape, F32)
    tokens = token_of_column(heads, kv_local, columns).astype(F32)
    low = iota((SLOT, LANES), 1) < HEAD_DIM
    lane = iota((SLOT, LANES), 1)
    row = iota((SLOT, LANES), 0)

    def terms(total, offset):
        leading = total.astype(BF16).astype(F32)
        rest = total - leading
        second = rest.astype(BF16).astype(F32)
        third = rest - second
        spot = lane - offset - 3 * row
        placed = jnp.where(spot == 0, leading, 0.0)
        placed = jnp.where(spot == 1, second, placed)
        return jnp.where(spot == 2, third, placed)

    def rows_of(j):
        dest = meta[2, j]
        rank = jnp.int32(0)
        for e in range(j):
            rank = rank + (meta[2, e] == dest).astype(jnp.int32)
        return pl.ds(pl.multiple_of((dest * CAP + rank) * SLOT, SLOT), SLOT)

    meta_copy.wait()
    places = [rows_of(j) for j in range(outgoing)]
    packed = [asked[rows, :] for rows in places]
    replies = {}

    def keep(j, top, total, out):
        out = out / total
        logs = top + jnp.log(total)
        even = pltpu.roll(out[0:SLOT], HEAD_DIM, 1)
        both = jnp.where(low, even, out[SLOT:ROWS])
        line = jnp.sum(
            terms(logs[0:SLOT], 0) + terms(logs[SLOT:ROWS], HEAD_DIM), axis=0, keepdims=True
        )
        replies[j] = jnp.where(row == META, line, both)

    paging.wait()
    attend_pages(
        outgoing,
        4,
        lambda j: unpack(packed[j]).astype(BF16),
        lambda j: pages[j],
        lambda j: packed[j][META : META + 1, 0:1],
        tokens,
        keep,
    )
    for j in range(outgoing):
        reply[places[j], :] = replies[j]
    reply_ref[...] = reply[...].astype(BF16)


def combine_kernel(
    heads, pool, meta_ref, top_ref, acc_ref, reply_ref, wo_ref,
    part_ref, tops, accs, reply, finals,
):
    requests = top_ref.shape[0] - 1
    inbox = reply_ref.shape[0] // SLOT
    chunks = -(-heads // 2)
    reply[...] = reply_ref[...].astype(F32)
    tops[...] = top_ref[...]
    low = iota((SLOT, LANES), 1) < HEAD_DIM
    lane = iota((SLOT, LANES), 1)
    row = iota((SLOT, LANES), 0)
    mine = (lane % HEAD_DIM) // 3 == row

    def place_of(s):
        owner = meta_ref[0, pool + s]
        return jnp.where(owner < 0, requests, owner)

    def logs_of(s):
        line = reply[s * SLOT + META : s * SLOT + META + 1, :]
        line = jnp.where(mine, jnp.broadcast_to(line, (SLOT, LANES)), 0.0)
        even = jnp.sum(jnp.where(low, line, 0.0), axis=1, keepdims=True)
        odd = jnp.sum(jnp.where(low, 0.0, line), axis=1, keepdims=True)
        logs = jnp.concatenate([even, odd], axis=0)
        return jnp.broadcast_to(logs, (ROWS, LANES))

    logs = [logs_of(s) for s in range(inbox)]
    for s in range(inbox):
        place = place_of(s)
        tops[place] = jnp.maximum(tops[place], logs[s])
    accs[0:requests] = acc_ref[0:requests] * jnp.exp(
        top_ref[0:requests] - tops[0:requests]
    )
    for s in range(inbox):
        place = place_of(s)
        packed = reply[s * SLOT : (s + 1) * SLOT, :]
        even = jnp.where(low, 1.0, pltpu.roll(packed, HEAD_DIM, 1))
        odd = jnp.where(low, 1.0, packed)
        both = jnp.concatenate([even, odd], axis=0)
        accs[place] = accs[place] + both * jnp.exp(logs[s] - tops[place])
    whole = accs[0:requests]
    finals[...] = (whole / pltpu.roll(whole, HEAD_DIM, 2)).reshape(
        requests * ROWS, LANES
    )
    wide = iota((requests, LANES), 1) < HEAD_DIM
    parts = []
    for j in range(chunks):
        even = finals[pl.ds(j, requests, stride=ROWS), :]
        odd = finals[pl.ds(SLOT + j, requests, stride=ROWS), :]
        parts.append(jnp.where(wide, pltpu.roll(even, HEAD_DIM, 1), odd).astype(BF16))
    attention = jnp.concatenate(parts, axis=1)[:, : heads * HEAD_DIM]
    part_ref[...] = jnp.dot(
        attention, wo_ref[...], preferred_element_type=F32
    ).astype(BF16)


def own_rows(values, first):
    half = values.shape[0] // 2
    return jnp.where(first, values[:half], values[half:])


def gate_kernel(
    tp, units, count, meta_ref, hidden_ref, *refs,
):
    pieces = refs[:count]
    (gain_ref, router_ref, routes_ref, attended_ref, input_ref, spread_ref) = refs[count:]
    requests = hidden_ref.shape[0]
    if count == 2:
        summed = pieces[0][...].astype(F32) + pieces[1][...].astype(F32)
    else:
        summed = pieces[0][0:requests, :].astype(F32)
        for t in range(1, tp):
            part = pieces[0][t * requests : (t + 1) * requests, :]
            summed = summed + part.astype(F32)
    attended = (hidden_ref[...].astype(F32) + RESID_SCALE * summed).astype(BF16)
    if count == 2:
        attended_ref[...] = own_rows(attended, meta_ref[3:4, 0:1] == 0)
    else:
        attended_ref[...] = attended
    ffn_input = norm_rows(attended.astype(F32), gain_ref[...])
    input_ref[...] = ffn_input
    logits = lax.dot_general(router_ref[...], ffn_input, NT, preferred_element_type=F32)
    expert = iota(logits.shape, 0)
    named = jnp.zeros(logits.shape, F32)
    for k in range(routes_ref.shape[0]):
        named = jnp.where(routes_ref[k : k + 1, :] == expert, 1.0, named)
    chosen = named > 0.5
    top = jnp.max(jnp.where(chosen, logits, NEG_FILL), axis=0, keepdims=True)
    weights = jnp.where(chosen, jnp.exp(logits - top), 0.0)
    gates = weights / jnp.sum(weights, axis=0, keepdims=True)
    unit = iota((EXPERTS, units), 1) + meta_ref[3:4, 0:1] * units
    owner = (unit // FF == iota((EXPERTS, units), 0)).astype(F32)
    spread_ref[...] = lax.dot_general(
        gates, owner, TN, preferred_element_type=F32, precision=lax.Precision.HIGHEST
    )


def expert_kernel(meta_ref, lifted_ref, spread_ref, wd_ref, *outs):
    gate = lifted_ref[0]
    active = gate / (1.0 + jnp.exp(-gate)) * lifted_ref[1] * spread_ref[...]
    share = jnp.dot(active.astype(BF16), wd_ref[...], preferred_element_type=F32)
    if len(outs) == 2:
        first = meta_ref[3:4, 0:1] == 0
        outs[0][...] = own_rows(share, first)
        outs[1][...] = own_rows(share, jnp.logical_not(first)).astype(BF16)
    else:
        outs[0][...] = share.astype(BF16)


def call(body, outs, in_specs, scratch=(), limit=16, flops=0, moved=0):
    return pl.pallas_call(
        body,
        out_shape=outs,
        in_specs=in_specs,
        out_specs=[VMEM if isinstance(o, jax.ShapeDtypeStruct) else HBM for o in outs],
        scratch_shapes=list(scratch),
        compiler_params=pltpu.CompilerParams(vmem_limit_bytes=limit << 20),
        cost_estimate=pl.CostEstimate(
            flops=flops, bytes_accessed=moved, transcendentals=0
        ),
    )


def swap(values):
    return lax.ppermute(values, "tensor", [(0, 1), (1, 0)])


def on_device(
    hidden,
    attn_gain,
    w_query,
    w_keyvalue,
    w_output,
    cache,
    page_table,
    ctx_len,
    move_dest,
    ffn_gain,
    router,
    routes,
    w_in,
    w_down,
):
    replicas = lax.axis_size("replica")
    tp = lax.axis_size("tensor")
    rank = lax.axis_index("tensor").astype(jnp.int32)
    rows, width = hidden.shape
    pool, page_len, kv_local, _ = cache.shape
    outgoing = move_dest.shape[0]
    local_pages = pool - outgoing
    requests = page_table.shape[0]
    heads = w_query.shape[1] // HEAD_DIM
    inbox = replicas * CAP
    units = w_down.shape[0]
    columns = page_len * kv_local
    entries = -(-(pool + inbox) // LANES) * LANES
    first = local_pages // 2
    struct = jax.ShapeDtypeStruct
    pair = tp == 2
    ids = rank.reshape(1)

    def pin(values):
        return pltpu.with_memory_space_constraint(values, pltpu.HBM)

    def exchange(blocks):
        blocks = blocks.reshape(replicas, CAP * SLOT, LANES)
        blocks = lax.all_to_all(blocks, "replica", split_axis=0, concat_axis=0, tiled=True)
        return blocks.reshape(inbox * SLOT, LANES)

    blocks = pin(cache.reshape(pool, columns, LANES))
    if pair:
        pieces = [hidden, swap(hidden)]
    else:
        pieces = [lax.all_gather(hidden, "tensor", axis=0, tiled=True)]
    meta_shape = (4, entries)
    tables_shape = (2, requests, LANES)
    own, wq, gain, tables, away, away_span, meta, tables_far, meta_far = call(
        functools.partial(prepare_kernel, pool, replicas),
        [
            struct(hidden.shape, BF16),
            struct(w_query.shape, BF16),
            struct((1, width), F32),
            struct(tables_shape, F32),
            struct((inbox, requests), BF16),
            struct((inbox, LANES), F32),
            struct(meta_shape, jnp.int32),
            pltpu.HBM(tables_shape, F32),
            pltpu.HBM(meta_shape, jnp.int32),
        ],
        [SMEM] + [HBM] * 6,
        [
            pltpu.VMEM((1, requests), jnp.int32),
            pltpu.VMEM((page_table.shape[1], requests), jnp.int32),
            pltpu.VMEM((1, outgoing), jnp.int32),
            pltpu.VMEM((width,), F32),
            pltpu.SemaphoreType.DMA((8,)),
        ],
        moved=2 * w_query.size,
    )(
        ids,
        pin(hidden),
        pin(ctx_len.reshape(1, requests)),
        pin(page_table.T),
        pin(move_dest.reshape(1, outgoing)),
        pin(attn_gain),
        pin(w_query),
    )
    if pair:
        pieces[0] = own
    hidden_far, normed, packed, sends = call(
        functools.partial(query_kernel, len(pieces)),
        [
            pltpu.HBM((requests, width), BF16),
            pltpu.HBM((requests, width), BF16),
            pltpu.HBM((requests * SLOT, LANES), F32),
            pltpu.HBM((inbox * SLOT, LANES), BF16),
        ],
        [VMEM] * (len(pieces) + 6),
        [
            pltpu.VMEM((requests, width), BF16),
            pltpu.VMEM((requests, width), BF16),
            pltpu.VMEM((requests * SLOT, LANES), F32),
            pltpu.VMEM((inbox * SLOT, LANES), F32),
            pltpu.VMEM((inbox * SLOT, LANES), BF16),
            pltpu.SemaphoreType.DMA((4,)),
        ],
        flops=4 * requests * width * w_query.shape[1],
        moved=2 * w_query.size,
    )(meta, *pieces, gain, wq, tables, away, away_span)
    asked = exchange(sends)
    new, tops, sums = call(
        functools.partial(first_kernel, heads, kv_local),
        [
            pltpu.HBM((kv_local, requests, LANES), F32),
            pltpu.HBM((first, ROWS, LANES), F32),
            pltpu.HBM((first, ROWS, LANES), F32),
        ],
        [HBM] * 6,
        [
            pltpu.SMEM(meta_shape, jnp.int32),
            pltpu.VMEM((requests * SLOT, LANES), F32),
            pltpu.VMEM((requests, width), BF16),
            pltpu.VMEM((width * kv_local, LANES), BF16),
            pltpu.VMEM((width * kv_local, LANES), F32),
            pltpu.VMEM(tables_shape, F32),
            pltpu.VMEM((first, columns, LANES), BF16),
            pltpu.VMEM((requests, ROWS, LANES), F32),
            pltpu.VMEM((kv_local, requests, LANES), F32),
            pltpu.VMEM((first, ROWS, LANES), F32),
            pltpu.VMEM((first, ROWS, LANES), F32),
            pltpu.SemaphoreType.DMA((9,)),
        ],
        flops=4 * ROWS * columns * LANES * first,
        moved=2 * columns * LANES * first,
    )(
        pin(meta_far),
        pin(packed),
        pin(normed),
        pin(w_keyvalue.reshape(width * kv_local, LANES)),
        pin(tables_far),
        blocks,
    )
    (replies,) = call(
        functools.partial(lent_kernel, heads, kv_local, local_pages),
        [struct((inbox * SLOT, LANES), BF16)],
        [HBM, VMEM, HBM],
        [
            pltpu.SMEM(meta_shape, jnp.int32),
            pltpu.VMEM((outgoing, columns, LANES), BF16),
            pltpu.VMEM((inbox * SLOT, LANES), F32),
            pltpu.VMEM((inbox * SLOT, LANES), F32),
            pltpu.SemaphoreType.DMA((2,)),
        ],
        flops=4 * ROWS * columns * LANES * outgoing,
        moved=2 * columns * LANES * outgoing,
    )(pin(meta_far), asked, blocks)
    returned = exchange(replies)
    top, acc, meta, hidden_all, gain, wo, wd, router_t, routes_t = call(
        functools.partial(second_kernel, heads, kv_local, first),
        [
            struct((requests + 1, ROWS, LANES), F32),
            struct((requests + 1, ROWS, LANES), F32),
            struct(meta_shape, jnp.int32),
            struct((requests, width), BF16),
            struct((1, width), F32),
            struct(w_output.shape, BF16),
            struct(w_down.shape, BF16),
            struct(router.shape[::-1], BF16),
            struct(routes.shape[::-1], jnp.int32),
        ],
        [HBM] * 6 + [ANY] + [HBM] * 6,
        [
            pltpu.SMEM(meta_shape, jnp.int32),
            pltpu.VMEM((requests * SLOT, LANES), F32),
            pltpu.VMEM((kv_local, requests, LANES), F32),
            pltpu.VMEM((local_pages, ROWS, LANES), F32),
            pltpu.VMEM((local_pages, ROWS, LANES), F32),
            pltpu.VMEM((width,), F32),
            pltpu.VMEM((local_pages, columns, LANES), BF16),
            pltpu.VMEM((requests, ROWS, LANES), F32),
            pltpu.VMEM((requests * ROWS, LANES), F32),
            pltpu.SemaphoreType.DMA((13,)),
        ],
        limit=32,
        flops=4 * ROWS * columns * LANES * (local_pages - first),
        moved=2 * (w_output.size + w_down.size + router.size),
    )(
        pin(meta_far), pin(packed), pin(new), pin(tops), pin(sums), blocks,
        replies, pin(hidden_far), pin(ffn_gain), pin(w_output), pin(w_down),
        pin(router.T), pin(routes.T),
    )
    (part,) = call(
        functools.partial(combine_kernel, heads, pool),
        [struct((requests, width), BF16)],
        [SMEM, VMEM, VMEM, VMEM, VMEM],
        [
            pltpu.VMEM((requests + 1, ROWS, LANES), F32),
            pltpu.VMEM((requests + 1, ROWS, LANES), F32),
            pltpu.VMEM((inbox * SLOT, LANES), F32),
            pltpu.VMEM((requests * ROWS, LANES), F32),
        ],
        flops=2 * requests * w_output.size,
        moved=2 * w_output.size,
    )(meta, top, acc, returned, wo)
    if pair:
        parts = [part, swap(part)]
    else:
        parts = [lax.all_gather(part, "tensor", axis=0, tiled=True)]
    attended, ffn_input, spread = call(
        functools.partial(gate_kernel, tp, units, len(parts)),
        [
            struct((rows if pair else requests, width), BF16),
            struct((requests, width), BF16),
            struct((requests, units), F32),
        ],
        [VMEM] * (len(parts) + 5),
        flops=2 * requests * router.size,
        moved=2 * router.size,
    )(meta, hidden_all, *parts, gain, router_t, routes_t)
    lifted = jnp.einsum("rd,dsu->sru", ffn_input, w_in, preferred_element_type=F32)
    shapes = [struct((requests, width), BF16)]
    if pair:
        shapes = [struct((rows, width), F32), struct((rows, width), BF16)]
    shares = call(
        expert_kernel,
        shapes,
        [VMEM] * 4,
        flops=2 * requests * w_down.size,
        moved=2 * w_down.size,
    )(meta, lifted, spread, wd)
    if pair:
        return attended, (shares[0] + swap(shares[1]).astype(F32)).astype(BF16)
    shares = lax.all_gather(shares[0], "tensor", axis=0)
    mine = lax.dynamic_slice_in_dim(shares, rank * rows, rows, axis=1)
    experts_out = jnp.sum(mine.astype(F32), axis=0).astype(BF16)
    attended = lax.dynamic_slice_in_dim(attended, rank * rows, rows, axis=0)
    return attended, experts_out


def solution(mesh):
    placed = (
        P(("replica", "tensor"), None),
        P(),
        P(None, "tensor"),
        P(None, "tensor", None),
        P("tensor", None),
        P("replica", None, "tensor", None),
        P("replica", None),
        P("replica"),
        P("replica"),
        P(),
        P(),
        P("replica", None),
        P(None, None, "tensor"),
        P("tensor", None),
    )
    return jax.shard_map(
        on_device,
        mesh=mesh,
        in_specs=placed,
        out_specs=(P(("replica", "tensor"), None), P(("replica", "tensor"), None)),
        check_vma=False,
    )
```

```python
import functools
import math

import jax
import jax.numpy as jnp
from jax import lax
from jax.experimental import pallas as pl
from jax.experimental.pallas import tpu as pltpu
from jax.sharding import PartitionSpec as P

HEAD_DIM = 64
EXPERTS = 40
FF = 512
CAP = 2
LANES = 128
SLOT = 8
ROWS = 16
META = 6

ATTN_SCALE = 0.015625
RESID_SCALE = 0.22
ROPE_BASE = 10000.0
EPSILON = 1e-06
NEG_FILL = -1e30

F32 = jnp.float32
BF16 = jnp.bfloat16
VMEM = pl.BlockSpec(memory_space=pltpu.VMEM)
SMEM = pl.BlockSpec(memory_space=pltpu.SMEM)
ANY = pl.BlockSpec(memory_space=pl.ANY)
HBM = pl.BlockSpec(memory_space=pltpu.HBM)
NT = (((1,), (1,)), ((), ()))
TN = (((0,), (0,)), ((), ()))


def iota(shape, axis):
    return lax.broadcasted_iota(jnp.int32, shape, axis)


def norm_rows(values, gain):
    factor = lax.rsqrt(jnp.mean(values * values, axis=-1, keepdims=True) + EPSILON)
    return (values * factor * gain).astype(BF16)


def rope_tables(ctx_row, requests):
    diagonal = iota((requests, requests), 0) == iota((requests, requests), 1)
    ctx = jnp.broadcast_to(ctx_row.astype(F32), (requests, requests))
    ctx = jnp.sum(jnp.where(diagonal, ctx, 0.0), axis=1, keepdims=True)
    lane = iota((requests, LANES), 1)
    index = (lane % (HEAD_DIM // 2)).astype(F32)
    inverse = jnp.exp(index * (-2.0 * math.log(ROPE_BASE) / HEAD_DIM))
    angles = ctx * inverse
    sign = jnp.where(lane % HEAD_DIM < HEAD_DIM // 2, -1.0, 1.0)
    return jnp.cos(angles), jnp.sin(angles) * sign


def rotate(chunk, cosine, sine):
    lane = iota(chunk.shape, 1)
    ahead = pltpu.roll(chunk, LANES - HEAD_DIM // 2, 1)
    behind = pltpu.roll(chunk, HEAD_DIM // 2, 1)
    turned = jnp.where(lane % HEAD_DIM < HEAD_DIM // 2, ahead, behind)
    return chunk * cosine + turned * sine


def copy_of(source, target, sem):
    return pltpu.make_async_copy(source, target, sem)


def page_copies(cache_hbm, first, pages, place, count, sems, base):
    return [
        copy_of(cache_hbm.at[first + p], pages.at[place + p], sems.at[base + p])
        for p in range(count)
    ]


def prepare_kernel(
    pool, replicas, ids_ref, hidden_hbm, ctx_hbm, table_hbm, dest_hbm, attn_gain_hbm,
    wq_hbm,
    hidden_ref, wq_ref, gain_ref, tables_ref, away_ref, span_ref, meta_ref,
    tables_hbm, meta_hbm, ctx, table, dest, gain, sems,
):
    inbox = replicas * CAP
    requests = ctx.shape[1]
    entries = meta_ref.shape[1]
    small = [
        copy_of(ctx_hbm, ctx, sems.at[0]),
        copy_of(table_hbm, table, sems.at[1]),
        copy_of(dest_hbm, dest, sems.at[2]),
        copy_of(attn_gain_hbm, gain, sems.at[3]),
    ]
    large = [
        copy_of(hidden_hbm, hidden_ref, sems.at[4]),
        copy_of(wq_hbm, wq_ref, sems.at[5]),
    ]
    for copy in small + large:
        copy.start()
    for copy in small:
        copy.wait()
    gain_ref[...] = gain[...].reshape(1, gain.shape[0])
    ctx_row = ctx[...]

    def claims(values):
        held = jnp.zeros(values.shape, F32)
        spans = jnp.zeros(values.shape, F32)
        for k in range(table.shape[0]):
            match = table[k : k + 1, :] == values
            filled = jnp.clip(ctx_row - k * 128, 0, 128).astype(F32)
            held = jnp.where(match, 1.0, held)
            spans = jnp.where(match, filled, spans)
        return held.astype(BF16), spans

    held, spans = claims(iota((entries, requests), 0))
    numbers = (iota((SLOT, requests), 1) + 1).astype(BF16)
    ones = jnp.ones((SLOT, requests), BF16)
    holder = lax.dot_general(numbers, held, NT, preferred_element_type=F32)
    covered = lax.dot_general(ones, spans.astype(BF16), NT, preferred_element_type=F32)
    meta_ref[0:1, :] = holder[0:1, :].astype(jnp.int32) - 1
    meta_ref[1:2, :] = covered[0:1, :].astype(jnp.int32)
    meta_ref[2:3, :] = jnp.zeros((1, entries), jnp.int32)
    meta_ref[2:3, 0 : dest.shape[1]] = dest[...]
    meta_ref[3:4, :] = jnp.full((1, entries), ids_ref[0], jnp.int32)
    cosine, sine = rope_tables(ctx_row, requests)
    tables_ref[0] = cosine
    tables_ref[1] = sine
    parked = [
        copy_of(tables_ref, tables_hbm, sems.at[6]),
        copy_of(meta_ref, meta_hbm, sems.at[7]),
    ]
    for copy in parked:
        copy.start()
    held, spans = claims(pool + iota((inbox, requests), 0))
    away_ref[...] = held
    away_span = jnp.sum(spans, axis=1, keepdims=True)
    span_ref[...] = jnp.broadcast_to(away_span, span_ref.shape)
    for copy in large + parked:
        copy.wait()


def query_kernel(
    count, meta_ref, *refs,
):
    pieces = refs[:count]
    (gain_ref, wq_ref, tables_ref, away_ref, span_ref,
     hidden_hbm, normed_hbm, packed_hbm, send_hbm,
     hiddens, norms, packs, sends, sends16, sems) = refs[count:]
    requests = hiddens.shape[0]
    inbox = span_ref.shape[0]
    width = wq_ref.shape[1]
    chunks = -(-width // LANES)
    if count == 1:
        hidden = pieces[0][...]
    else:
        own, other = pieces[0][...], pieces[1][...]
        first = meta_ref[3:4, 0:1] == 0
        hidden = jnp.concatenate(
            [jnp.where(first, own, other), jnp.where(first, other, own)], axis=0
        )
    hiddens[...] = hidden
    normed = norm_rows(hidden.astype(F32), gain_ref[...])
    norms[...] = normed
    early = [
        copy_of(hiddens, hidden_hbm, sems.at[0]),
        copy_of(norms, normed_hbm, sems.at[1]),
    ]
    for copy in early:
        copy.start()
    queries = jnp.dot(normed, wq_ref[...], preferred_element_type=F32)
    if chunks * LANES > width:
        pad = jnp.zeros((requests, chunks * LANES - width), F32)
        queries = jnp.concatenate([queries, pad], axis=1)
    cosine, sine = tables_ref[0], tables_ref[1]
    zeros = jnp.zeros((requests, LANES), F32)
    nothing = jnp.zeros((inbox, LANES), F32)
    for j in range(SLOT):
        here = pl.ds(j, requests, stride=SLOT)
        there = pl.ds(j, inbox, stride=SLOT)
        if j < chunks:
            chunk = rotate(queries[:, j * LANES : (j + 1) * LANES], cosine, sine)
            chunk = (chunk.astype(BF16).astype(F32) * ATTN_SCALE).astype(BF16)
            packs[here, :] = chunk.astype(F32)
            sends[there, :] = jnp.dot(away_ref[...], chunk, preferred_element_type=F32)
        else:
            packs[here, :] = zeros
            sends[there, :] = span_ref[...] if j == META else nothing
    sends16[...] = sends[...].astype(BF16)
    late = [
        copy_of(sends16, send_hbm, sems.at[2]),
        copy_of(packs, packed_hbm, sems.at[3]),
    ]
    for copy in late:
        copy.start()
    for copy in early + late:
        copy.wait()


def unpack(packed):
    low = iota(packed.shape, 1) < HEAD_DIM
    even = jnp.where(low, packed, 0.0)
    odd = jnp.where(low, pltpu.roll(packed, HEAD_DIM, 1), 0.0)
    return jnp.concatenate([even, odd], axis=0)


def head_rows(heads):
    return [(h // 2) + SLOT * (h % 2) for h in range(heads)]


def token_of_column(heads, kv_local, columns):
    row = iota((ROWS, columns), 0)
    column = iota((ROWS, columns), 1)
    wanted = jnp.full((ROWS, columns), kv_local, jnp.int32)
    for h, place in enumerate(head_rows(heads)):
        wanted = jnp.where(row == place, h // (heads // kv_local), wanted)
    return jnp.where(column % kv_local == wanted, column // kv_local, 1 << 20)


def score_page(query, block):
    return lax.dot_general(query, block, NT, preferred_element_type=F32)


def weigh_page(scores, tokens, span):
    scores = jnp.where(tokens < span, scores, NEG_FILL)
    top = jnp.max(scores, axis=1, keepdims=True)
    weights = jnp.exp(scores - top)
    return top, jnp.sum(weights, axis=1, keepdims=True), weights.astype(BF16)


def value_page(weights, block):
    return jnp.dot(weights, block, preferred_element_type=F32)


def attend_pages(count, stage, query_of, block_of, span_of, tokens, keep):
    stages = [range(i, min(i + stage, count)) for i in range(0, count, stage)]
    scores = {p: score_page(query_of(p), block_of(p)) for p in stages[0]}
    for i, pages in enumerate(stages):
        if i + 1 < len(stages):
            ahead = {p: score_page(query_of(p), block_of(p)) for p in stages[i + 1]}
        weighed = {p: weigh_page(scores[p], tokens, span_of(p)) for p in pages}
        outs = {p: value_page(weighed[p][2], block_of(p)) for p in pages}
        for p in pages:
            keep(p, weighed[p][0], weighed[p][1], outs[p])
        if i + 1 < len(stages):
            scores = ahead


def spread_queries(target, packed):
    low = iota(packed.shape, 2) < HEAD_DIM
    target[:, 0:SLOT, :] = jnp.where(low, packed, 0.0)
    target[:, SLOT:ROWS, :] = jnp.where(low, pltpu.roll(packed, HEAD_DIM, 2), 0.0)


def first_kernel(
    heads, kv_local, meta_hbm, packed_hbm, normed_hbm, wkv_hbm, tables_hbm, cache_hbm,
    new_hbm, tops_hbm, sums_hbm,
    meta, packed, normed, raw, wide, tables, pages, queries, new, tops, sums, sems,
):
    requests, depth = normed.shape
    count, columns, _ = pages.shape
    small = [
        copy_of(meta_hbm, meta, sems.at[0]),
        copy_of(packed_hbm, packed, sems.at[1]),
        copy_of(normed_hbm, normed, sems.at[2]),
        copy_of(tables_hbm, tables, sems.at[3]),
    ]
    weights = copy_of(wkv_hbm, raw, sems.at[4])
    paging = page_copies(cache_hbm, 0, pages, 0, count, sems, 9)
    for copy in small + [weights] + paging:
        copy.start()
    for copy in small:
        copy.wait()
    spread_queries(queries, packed[...].reshape(requests, SLOT, LANES))
    tokens = token_of_column(heads, kv_local, columns)
    lower = iota((ROWS, LANES), 1) < HEAD_DIM
    low = iota((requests, LANES), 1) < HEAD_DIM
    cosine = jnp.where(low, tables[0], 1.0)
    sine = jnp.where(low, tables[1], 0.0)
    weights.wait()
    if kv_local > 1:
        wide[...] = raw[...].astype(F32)
    for k in range(kv_local):
        if kv_local > 1:
            weight = wide[pl.ds(k, depth, stride=kv_local), :].astype(BF16)
        else:
            weight = raw[...]
        projected = jnp.dot(normed[...], weight, preferred_element_type=F32)
        new[k] = rotate(projected, cosine, sine).astype(BF16).astype(F32)
    for copy in paging:
        copy.wait()

    def keep(p, top, total, out):
        tops[p] = jnp.broadcast_to(top, (ROWS, LANES))
        sums[p] = jnp.where(lower, total, out)

    attend_pages(
        count,
        4,
        lambda p: queries[jnp.maximum(meta[0, p], 0)].astype(BF16),
        lambda p: pages[p],
        lambda p: meta[1, p],
        tokens,
        keep,
    )
    parked = [
        copy_of(new, new_hbm, sems.at[6]),
        copy_of(tops, tops_hbm, sems.at[7]),
        copy_of(sums, sums_hbm, sems.at[8]),
    ]
    for copy in parked:
        copy.start()
    for copy in parked:
        copy.wait()


def second_kernel(
    heads, kv_local, first, meta_hbm, packed_hbm, new_hbm, tops_hbm, sums_hbm,
    cache_hbm, order_hbm, state_hbm,
    meta, packed, new, tops, sums, pages, queries, fresh, top, acc, sems,
):
    del order_hbm
    requests = queries.shape[0]
    local_pages = tops.shape[0]
    count, columns, _ = pages.shape
    small = [
        copy_of(meta_hbm, meta, sems.at[0]),
        copy_of(packed_hbm, packed, sems.at[1]),
        copy_of(new_hbm, new, sems.at[2]),
    ]
    earlier = [
        copy_of(tops_hbm, tops.at[pl.ds(0, first)], sems.at[3]),
        copy_of(sums_hbm, sums.at[pl.ds(0, first)], sems.at[4]),
    ]
    paging = page_copies(cache_hbm, first, pages, 0, count, sems, 6)
    for copy in small + paging + earlier:
        copy.start()
    for copy in small:
        copy.wait()
    spread_queries(queries, packed[...].reshape(requests, SLOT, LANES))
    used = {place: h for h, place in enumerate(head_rows(heads))}
    for place in range(ROWS):
        value = jnp.zeros((requests, LANES), F32)
        if place in used:
            value = new[used[place] // (heads // kv_local)]
        fresh[pl.ds(place, requests, stride=ROWS), :] = value
    tokens = token_of_column(heads, kv_local, columns)
    lower = iota((ROWS, LANES), 1) < HEAD_DIM
    added = fresh[...].reshape(requests, ROWS, LANES)
    low16 = iota(added.shape, 2) < HEAD_DIM
    score = jnp.sum(queries[...] * added, axis=2, keepdims=True)
    before = jnp.broadcast_to(score, added.shape)
    start = jnp.where(low16, 1.0, added)
    top[0:requests] = before
    for copy in paging:
        copy.wait()

    def keep(p, top, total, out):
        tops[first + p] = jnp.broadcast_to(top, (ROWS, LANES))
        sums[first + p] = jnp.where(lower, total, out)

    attend_pages(
        count,
        4,
        lambda p: queries[jnp.maximum(meta[0, first + p], 0)].astype(BF16),
        lambda p: pages[p],
        lambda p: meta[1, first + p],
        tokens,
        keep,
    )
    for copy in earlier:
        copy.wait()

    def place_of(p):
        owner = meta[0, p]
        return jnp.where(owner < 0, requests, owner)

    for p in range(local_pages):
        place = place_of(p)
        top[place] = jnp.maximum(top[place], tops[p])
    acc[0:requests] = start * jnp.exp(before - top[0:requests])
    for p in range(local_pages):
        place = place_of(p)
        acc[place] = acc[place] + sums[p] * jnp.exp(tops[p] - top[place])
    whole = acc[0:requests]
    acc[0:requests] = jnp.where(
        low16, top[0:requests] + jnp.log(whole), whole / pltpu.roll(whole, HEAD_DIM, 2)
    )
    parked = copy_of(acc.at[pl.ds(0, requests)], state_hbm, sems.at[5])
    parked.start()
    parked.wait()


def lent_kernel(
    heads, kv_local, local_pages, meta_hbm, asked_ref, cache_hbm, order_hbm, reply_ref,
    meta, pages, asked, reply, sems,
):
    del order_hbm
    outgoing, columns, _ = pages.shape
    meta_copy = copy_of(meta_hbm, meta, sems.at[0])
    paging = page_copies(cache_hbm, local_pages, pages, 0, outgoing, sems, 1)
    for copy in [meta_copy] + paging:
        copy.start()
    asked[...] = asked_ref[...].astype(F32)
    reply[...] = jnp.zeros(reply.shape, F32)
    tokens = token_of_column(heads, kv_local, columns).astype(F32)
    low = iota((SLOT, LANES), 1) < HEAD_DIM
    lane = iota((SLOT, LANES), 1)
    row = iota((SLOT, LANES), 0)

    def terms(total, offset):
        leading = total.astype(BF16).astype(F32)
        rest = total - leading
        second = rest.astype(BF16).astype(F32)
        third = rest - second
        spot = lane - offset - 3 * row
        placed = jnp.where(spot == 0, leading, 0.0)
        placed = jnp.where(spot == 1, second, placed)
        return jnp.where(spot == 2, third, placed)

    def rows_of(j):
        dest = meta[2, j]
        rank = jnp.int32(0)
        for e in range(j):
            rank = rank + (meta[2, e] == dest).astype(jnp.int32)
        return pl.ds(pl.multiple_of((dest * CAP + rank) * SLOT, SLOT), SLOT)

    meta_copy.wait()
    places = [rows_of(j) for j in range(outgoing)]
    packed = [asked[rows, :] for rows in places]
    replies = {}

    def keep(j, top, total, out):
        out = out / total
        logs = top + jnp.log(total)
        even = pltpu.roll(out[0:SLOT], HEAD_DIM, 1)
        both = jnp.where(low, even, out[SLOT:ROWS])
        line = jnp.sum(
            terms(logs[0:SLOT], 0) + terms(logs[SLOT:ROWS], HEAD_DIM), axis=0, keepdims=True
        )
        replies[j] = jnp.where(row == META, line, both)

    for copy in paging:
        copy.wait()
    attend_pages(
        outgoing,
        4,
        lambda j: unpack(packed[j]).astype(BF16),
        lambda j: pages[j],
        lambda j: packed[j][META : META + 1, 0:1],
        tokens,
        keep,
    )
    for j in range(outgoing):
        reply[places[j], :] = replies[j]
    reply_ref[...] = reply[...].astype(BF16)


def combine_kernel(
    heads, pool, meta_hbm, state_hbm, wo_hbm, hidden_hbm, gain_hbm, router_hbm,
    routes_hbm, wd_hbm, reply_ref,
    part_ref, meta_ref, hidden_ref, gain_ref, router_ref, routes_ref, wd_ref,
    meta, state, wo, gain, tops, accs, reply, finals, sems,
):
    requests = state.shape[0]
    inbox = reply_ref.shape[0] // SLOT
    chunks = -(-heads // 2)
    small = [
        copy_of(meta_hbm, meta, sems.at[0]),
        copy_of(state_hbm, state, sems.at[1]),
    ]
    weights = copy_of(wo_hbm, wo, sems.at[2])
    gaining = copy_of(gain_hbm, gain, sems.at[3])
    later = [
        copy_of(meta_hbm, meta_ref, sems.at[4]),
        copy_of(hidden_hbm, hidden_ref, sems.at[5]),
        copy_of(router_hbm, router_ref, sems.at[6]),
        copy_of(routes_hbm, routes_ref, sems.at[7]),
        copy_of(wd_hbm, wd_ref, sems.at[8]),
    ]
    for copy in small + [weights, gaining] + later:
        copy.start()
    reply[...] = reply_ref[...].astype(F32)
    low = iota((SLOT, LANES), 1) < HEAD_DIM
    lane = iota((SLOT, LANES), 1)
    row = iota((SLOT, LANES), 0)
    mine = (lane % HEAD_DIM) // 3 == row

    def place_of(s):
        owner = meta[0, pool + s]
        return jnp.where(owner < 0, requests, owner)

    def logs_of(s):
        line = reply[s * SLOT + META : s * SLOT + META + 1, :]
        line = jnp.where(mine, jnp.broadcast_to(line, (SLOT, LANES)), 0.0)
        even = jnp.sum(jnp.where(low, line, 0.0), axis=1, keepdims=True)
        odd = jnp.sum(jnp.where(low, 0.0, line), axis=1, keepdims=True)
        logs = jnp.concatenate([even, odd], axis=0)
        return jnp.broadcast_to(logs, (ROWS, LANES))

    logs = [logs_of(s) for s in range(inbox)]
    for copy in small:
        copy.wait()
    low16 = iota(state.shape, 2) < HEAD_DIM
    start = state[...]
    before = jnp.where(low16, start, pltpu.roll(start, HEAD_DIM, 2))
    tops[0:requests] = before
    for s in range(inbox):
        place = place_of(s)
        tops[place] = jnp.maximum(tops[place], logs[s])
    accs[0:requests] = jnp.where(low16, 1.0, start) * jnp.exp(before - tops[0:requests])
    for s in range(inbox):
        place = place_of(s)
        packed = reply[s * SLOT : (s + 1) * SLOT, :]
        even = jnp.where(low, 1.0, pltpu.roll(packed, HEAD_DIM, 1))
        odd = jnp.where(low, 1.0, packed)
        both = jnp.concatenate([even, odd], axis=0)
        accs[place] = accs[place] + both * jnp.exp(logs[s] - tops[place])
    whole = accs[0:requests]
    finals[...] = (whole / pltpu.roll(whole, HEAD_DIM, 2)).reshape(
        requests * ROWS, LANES
    )
    wide = iota((requests, LANES), 1) < HEAD_DIM
    parts = []
    for j in range(chunks):
        even = finals[pl.ds(j, requests, stride=ROWS), :]
        odd = finals[pl.ds(SLOT + j, requests, stride=ROWS), :]
        parts.append(jnp.where(wide, pltpu.roll(even, HEAD_DIM, 1), odd).astype(BF16))
    attention = jnp.concatenate(parts, axis=1)[:, : heads * HEAD_DIM]
    weights.wait()
    part_ref[...] = jnp.dot(attention, wo[...], preferred_element_type=F32).astype(BF16)
    gaining.wait()
    gain_ref[...] = gain[...].reshape(1, gain.shape[0])
    for copy in later:
        copy.wait()


def own_rows(values, first):
    half = values.shape[0] // 2
    return jnp.where(first, values[:half], values[half:])


def gate_kernel(
    tp, units, count, meta_ref, hidden_ref, *refs,
):
    pieces = refs[:count]
    (gain_ref, router_ref, routes_ref, attended_ref, input_ref, spread_ref) = refs[count:]
    requests = hidden_ref.shape[0]
    if count == 2:
        summed = pieces[0][...].astype(F32) + pieces[1][...].astype(F32)
    else:
        summed = pieces[0][0:requests, :].astype(F32)
        for t in range(1, tp):
            part = pieces[0][t * requests : (t + 1) * requests, :]
            summed = summed + part.astype(F32)
    attended = (hidden_ref[...].astype(F32) + RESID_SCALE * summed).astype(BF16)
    if count == 2:
        attended_ref[...] = own_rows(attended, meta_ref[3:4, 0:1] == 0)
    else:
        attended_ref[...] = attended
    ffn_input = norm_rows(attended.astype(F32), gain_ref[...])
    input_ref[...] = ffn_input
    logits = lax.dot_general(router_ref[...], ffn_input, NT, preferred_element_type=F32)
    expert = iota(logits.shape, 0)
    named = jnp.zeros(logits.shape, F32)
    for k in range(routes_ref.shape[0]):
        named = jnp.where(routes_ref[k : k + 1, :] == expert, 1.0, named)
    chosen = named > 0.5
    top = jnp.max(jnp.where(chosen, logits, NEG_FILL), axis=0, keepdims=True)
    weights = jnp.where(chosen, jnp.exp(logits - top), 0.0)
    gates = weights / jnp.sum(weights, axis=0, keepdims=True)
    unit = iota((EXPERTS, units), 1) + meta_ref[3:4, 0:1] * units
    owner = (unit // FF == iota((EXPERTS, units), 0)).astype(F32)
    spread_ref[...] = lax.dot_general(
        gates, owner, TN, preferred_element_type=F32, precision=lax.Precision.HIGHEST
    )


def expert_kernel(meta_ref, lifted_ref, spread_ref, wd_ref, *outs):
    gate = lifted_ref[0]
    active = gate / (1.0 + jnp.exp(-gate)) * lifted_ref[1] * spread_ref[...]
    share = jnp.dot(active.astype(BF16), wd_ref[...], preferred_element_type=F32)
    if len(outs) == 2:
        first = meta_ref[3:4, 0:1] == 0
        outs[0][...] = own_rows(share, first)
        outs[1][...] = own_rows(share, jnp.logical_not(first)).astype(BF16)
    else:
        outs[0][...] = share.astype(BF16)


def call(body, outs, in_specs, scratch=(), limit=16, flops=0, moved=0):
    return pl.pallas_call(
        body,
        out_shape=outs,
        in_specs=in_specs,
        out_specs=[VMEM if isinstance(o, jax.ShapeDtypeStruct) else HBM for o in outs],
        scratch_shapes=list(scratch),
        compiler_params=pltpu.CompilerParams(vmem_limit_bytes=limit << 20),
        cost_estimate=pl.CostEstimate(
            flops=flops, bytes_accessed=moved, transcendentals=0
        ),
    )


def swap(values):
    return lax.ppermute(values, "tensor", [(0, 1), (1, 0)])


def on_device(
    hidden,
    attn_gain,
    w_query,
    w_keyvalue,
    w_output,
    cache,
    page_table,
    ctx_len,
    move_dest,
    ffn_gain,
    router,
    routes,
    w_in,
    w_down,
):
    replicas = lax.axis_size("replica")
    tp = lax.axis_size("tensor")
    rank = lax.axis_index("tensor").astype(jnp.int32)
    rows, width = hidden.shape
    pool, page_len, kv_local, _ = cache.shape
    outgoing = move_dest.shape[0]
    local_pages = pool - outgoing
    requests = page_table.shape[0]
    heads = w_query.shape[1] // HEAD_DIM
    inbox = replicas * CAP
    units = w_down.shape[0]
    columns = page_len * kv_local
    entries = -(-(pool + inbox) // LANES) * LANES
    first = local_pages // 2
    struct = jax.ShapeDtypeStruct
    pair = tp == 2
    ids = rank.reshape(1)

    def pin(values):
        return pltpu.with_memory_space_constraint(values, pltpu.HBM)

    def exchange(blocks):
        blocks = blocks.reshape(replicas, CAP * SLOT, LANES)
        blocks = lax.all_to_all(blocks, "replica", split_axis=0, concat_axis=0, tiled=True)
        return blocks.reshape(inbox * SLOT, LANES)

    blocks = pin(cache.reshape(pool, columns, LANES))
    if pair:
        pieces = [hidden, swap(hidden)]
    else:
        pieces = [lax.all_gather(hidden, "tensor", axis=0, tiled=True)]
    meta_shape = (4, entries)
    tables_shape = (2, requests, LANES)
    own, wq, gain, tables, away, away_span, meta, tables_far, meta_far = call(
        functools.partial(prepare_kernel, pool, replicas),
        [
            struct(hidden.shape, BF16),
            struct(w_query.shape, BF16),
            struct((1, width), F32),
            struct(tables_shape, F32),
            struct((inbox, requests), BF16),
            struct((inbox, LANES), F32),
            struct(meta_shape, jnp.int32),
            pltpu.HBM(tables_shape, F32),
            pltpu.HBM(meta_shape, jnp.int32),
        ],
        [SMEM] + [HBM] * 6,
        [
            pltpu.VMEM((1, requests), jnp.int32),
            pltpu.VMEM((page_table.shape[1], requests), jnp.int32),
            pltpu.VMEM((1, outgoing), jnp.int32),
            pltpu.VMEM((width,), F32),
            pltpu.SemaphoreType.DMA((8,)),
        ],
        moved=2 * w_query.size,
    )(
        ids,
        pin(hidden),
        pin(ctx_len.reshape(1, requests)),
        pin(page_table.T),
        pin(move_dest.reshape(1, outgoing)),
        pin(attn_gain),
        pin(w_query),
    )
    if pair:
        pieces[0] = own
    hidden_far, normed, packed, sends = call(
        functools.partial(query_kernel, len(pieces)),
        [
            pltpu.HBM((requests, width), BF16),
            pltpu.HBM((requests, width), BF16),
            pltpu.HBM((requests * SLOT, LANES), F32),
            pltpu.HBM((inbox * SLOT, LANES), BF16),
        ],
        [VMEM] * (len(pieces) + 6),
        [
            pltpu.VMEM((requests, width), BF16),
            pltpu.VMEM((requests, width), BF16),
            pltpu.VMEM((requests * SLOT, LANES), F32),
            pltpu.VMEM((inbox * SLOT, LANES), F32),
            pltpu.VMEM((inbox * SLOT, LANES), BF16),
            pltpu.SemaphoreType.DMA((4,)),
        ],
        flops=4 * requests * width * w_query.shape[1],
        moved=2 * w_query.size,
    )(meta, *pieces, gain, wq, tables, away, away_span)
    asked = exchange(sends)
    new, tops, sums = call(
        functools.partial(first_kernel, heads, kv_local),
        [
            pltpu.HBM((kv_local, requests, LANES), F32),
            pltpu.HBM((first, ROWS, LANES), F32),
            pltpu.HBM((first, ROWS, LANES), F32),
        ],
        [HBM] * 6,
        [
            pltpu.SMEM(meta_shape, jnp.int32),
            pltpu.VMEM((requests * SLOT, LANES), F32),
            pltpu.VMEM((requests, width), BF16),
            pltpu.VMEM((width * kv_local, LANES), BF16),
            pltpu.VMEM((width * kv_local, LANES), F32),
            pltpu.VMEM(tables_shape, F32),
            pltpu.VMEM((first, columns, LANES), BF16),
            pltpu.VMEM((requests, ROWS, LANES), F32),
            pltpu.VMEM((kv_local, requests, LANES), F32),
            pltpu.VMEM((first, ROWS, LANES), F32),
            pltpu.VMEM((first, ROWS, LANES), F32),
            pltpu.SemaphoreType.DMA((9 + first,)),
        ],
        flops=4 * ROWS * columns * LANES * first,
        moved=2 * columns * LANES * first,
    )(
        pin(meta_far),
        pin(packed),
        pin(normed),
        pin(w_keyvalue.reshape(width * kv_local, LANES)),
        pin(tables_far),
        blocks,
    )
    (replies,) = call(
        functools.partial(lent_kernel, heads, kv_local, local_pages),
        [struct((inbox * SLOT, LANES), BF16)],
        [HBM, VMEM, HBM, HBM],
        [
            pltpu.SMEM(meta_shape, jnp.int32),
            pltpu.VMEM((outgoing, columns, LANES), BF16),
            pltpu.VMEM((inbox * SLOT, LANES), F32),
            pltpu.VMEM((inbox * SLOT, LANES), F32),
            pltpu.SemaphoreType.DMA((1 + outgoing,)),
        ],
        flops=4 * ROWS * columns * LANES * outgoing,
        moved=2 * columns * LANES * outgoing,
    )(pin(meta_far), asked, blocks, pin(tops))
    returned = exchange(replies)
    (state,) = call(
        functools.partial(second_kernel, heads, kv_local, first),
        [pltpu.HBM((requests, ROWS, LANES), F32)],
        [HBM] * 6 + [ANY],
        [
            pltpu.SMEM(meta_shape, jnp.int32),
            pltpu.VMEM((requests * SLOT, LANES), F32),
            pltpu.VMEM((kv_local, requests, LANES), F32),
            pltpu.VMEM((local_pages, ROWS, LANES), F32),
            pltpu.VMEM((local_pages, ROWS, LANES), F32),
            pltpu.VMEM((local_pages - first, columns, LANES), BF16),
            pltpu.VMEM((requests, ROWS, LANES), F32),
            pltpu.VMEM((requests * ROWS, LANES), F32),
            pltpu.VMEM((requests + 1, ROWS, LANES), F32),
            pltpu.VMEM((requests + 1, ROWS, LANES), F32),
            pltpu.SemaphoreType.DMA((6 + local_pages - first,)),
        ],
        flops=4 * ROWS * columns * LANES * (local_pages - first),
        moved=2 * columns * LANES * (local_pages - first),
    )(pin(meta_far), pin(packed), pin(new), pin(tops), pin(sums), blocks, replies)
    part, meta, hidden_all, gain, router_t, routes_t, wd = call(
        functools.partial(combine_kernel, heads, pool),
        [
            struct((requests, width), BF16),
            struct(meta_shape, jnp.int32),
            struct((requests, width), BF16),
            struct((1, width), F32),
            struct(router.shape[::-1], BF16),
            struct(routes.shape[::-1], jnp.int32),
            struct(w_down.shape, BF16),
        ],
        [HBM] * 8 + [VMEM],
        [
            pltpu.SMEM(meta_shape, jnp.int32),
            pltpu.VMEM((requests, ROWS, LANES), F32),
            pltpu.VMEM(w_output.shape, BF16),
            pltpu.VMEM((width,), F32),
            pltpu.VMEM((requests + 1, ROWS, LANES), F32),
            pltpu.VMEM((requests + 1, ROWS, LANES), F32),
            pltpu.VMEM((inbox * SLOT, LANES), F32),
            pltpu.VMEM((requests * ROWS, LANES), F32),
            pltpu.SemaphoreType.DMA((9,)),
        ],
        flops=2 * requests * w_output.size,
        moved=2 * (w_output.size + w_down.size),
    )(
        pin(meta_far), pin(state), pin(w_output), pin(hidden_far), pin(ffn_gain),
        pin(router.T), pin(routes.T), pin(w_down), returned,
    )
    if pair:
        parts = [part, swap(part)]
    else:
        parts = [lax.all_gather(part, "tensor", axis=0, tiled=True)]
    attended, ffn_input, spread = call(
        functools.partial(gate_kernel, tp, units, len(parts)),
        [
            struct((rows if pair else requests, width), BF16),
            struct((requests, width), BF16),
            struct((requests, units), F32),
        ],
        [VMEM] * (len(parts) + 5),
        flops=2 * requests * router.size,
        moved=2 * router.size,
    )(meta, hidden_all, *parts, gain, router_t, routes_t)
    lifted = jnp.einsum("rd,dsu->sru", ffn_input, w_in, preferred_element_type=F32)
    shapes = [struct((requests, width), BF16)]
    if pair:
        shapes = [struct((rows, width), F32), struct((rows, width), BF16)]
    shares = call(
        expert_kernel,
        shapes,
        [VMEM] * 4,
        flops=2 * requests * w_down.size,
        moved=2 * w_down.size,
    )(meta, lifted, spread, wd)
    if pair:
        return attended, (shares[0] + swap(shares[1]).astype(F32)).astype(BF16)
    shares = lax.all_gather(shares[0], "tensor", axis=0)
    mine = lax.dynamic_slice_in_dim(shares, rank * rows, rows, axis=1)
    experts_out = jnp.sum(mine.astype(F32), axis=0).astype(BF16)
    attended = lax.dynamic_slice_in_dim(attended, rank * rows, rows, axis=0)
    return attended, experts_out


def solution(mesh):
    placed = (
        P(("replica", "tensor"), None),
        P(),
        P(None, "tensor"),
        P(None, "tensor", None),
        P("tensor", None),
        P("replica", None, "tensor", None),
        P("replica", None),
        P("replica"),
        P("replica"),
        P(),
        P(),
        P("replica", None),
        P(None, None, "tensor"),
        P("tensor", None),
    )
    return jax.shard_map(
        on_device,
        mesh=mesh,
        in_specs=placed,
        out_specs=(P(("replica", "tensor"), None), P(("replica", "tensor"), None)),
        check_vma=False,
    )
```

```python
import functools
import math

import jax
import jax.numpy as jnp
from jax import lax
from jax.experimental import pallas as pl
from jax.experimental.pallas import tpu as pltpu
from jax.sharding import PartitionSpec as P

HEAD_DIM = 64
EXPERTS = 40
FF = 512
CAP = 2
LANES = 128
SLOT = 8
ROWS = 16
META = 6

ATTN_SCALE = 0.015625
RESID_SCALE = 0.22
ROPE_BASE = 10000.0
EPSILON = 1e-06
NEG_FILL = -1e30

F32 = jnp.float32
BF16 = jnp.bfloat16
VMEM = pl.BlockSpec(memory_space=pltpu.VMEM)
SMEM = pl.BlockSpec(memory_space=pltpu.SMEM)
ANY = pl.BlockSpec(memory_space=pl.ANY)
HBM = pl.BlockSpec(memory_space=pltpu.HBM)
NT = (((1,), (1,)), ((), ()))


def iota(shape, axis):
    return lax.broadcasted_iota(jnp.int32, shape, axis)


def norm_rows(values, gain):
    factor = lax.rsqrt(jnp.mean(values * values, axis=-1, keepdims=True) + EPSILON)
    return (values * factor * gain).astype(BF16)


def rope_tables(ctx_row, requests):
    diagonal = iota((requests, requests), 0) == iota((requests, requests), 1)
    ctx = jnp.broadcast_to(ctx_row.astype(F32), (requests, requests))
    ctx = jnp.sum(jnp.where(diagonal, ctx, 0.0), axis=1, keepdims=True)
    lane = iota((requests, LANES), 1)
    index = (lane % (HEAD_DIM // 2)).astype(F32)
    inverse = jnp.exp(index * (-2.0 * math.log(ROPE_BASE) / HEAD_DIM))
    angles = ctx * inverse
    sign = jnp.where(lane % HEAD_DIM < HEAD_DIM // 2, -1.0, 1.0)
    return jnp.cos(angles), jnp.sin(angles) * sign


def rotate(chunk, cosine, sine):
    lane = iota(chunk.shape, 1)
    ahead = pltpu.roll(chunk, LANES - HEAD_DIM // 2, 1)
    behind = pltpu.roll(chunk, HEAD_DIM // 2, 1)
    turned = jnp.where(lane % HEAD_DIM < HEAD_DIM // 2, ahead, behind)
    return chunk * cosine + turned * sine


def copy_of(source, target, sem):
    return pltpu.make_async_copy(source, target, sem)


def page_copies(cache_hbm, first, pages, place, count, sems, base):
    return [
        copy_of(cache_hbm.at[first + p], pages.at[place + p], sems.at[base + p])
        for p in range(count)
    ]


def prepare_kernel(
    pool, replicas, ids_ref, hidden_hbm, ctx_hbm, table_hbm, dest_hbm, attn_gain_hbm,
    wq_hbm,
    hidden_ref, wq_ref, gain_ref, tables_ref, away_ref, span_ref, meta_ref,
    ctx, table, dest, gain, sems,
):
    inbox = replicas * CAP
    requests = ctx.shape[1]
    entries = meta_ref.shape[1]
    small = [
        copy_of(ctx_hbm, ctx, sems.at[0]),
        copy_of(table_hbm, table, sems.at[1]),
        copy_of(dest_hbm, dest, sems.at[2]),
        copy_of(attn_gain_hbm, gain, sems.at[3]),
    ]
    large = [
        copy_of(hidden_hbm, hidden_ref, sems.at[4]),
        copy_of(wq_hbm, wq_ref, sems.at[5]),
    ]
    for copy in small + large:
        copy.start()
    for copy in small:
        copy.wait()
    gain_ref[...] = gain[...].reshape(1, gain.shape[0])
    ctx_row = ctx[...]

    def claims(values):
        held = jnp.zeros(values.shape, F32)
        spans = jnp.zeros(values.shape, F32)
        for k in range(table.shape[0]):
            match = table[k : k + 1, :] == values
            filled = jnp.clip(ctx_row - k * 128, 0, 128).astype(F32)
            held = jnp.where(match, 1.0, held)
            spans = jnp.where(match, filled, spans)
        return held.astype(BF16), spans

    held, spans = claims(iota((entries, requests), 0))
    numbers = (iota((SLOT, requests), 1) + 1).astype(BF16)
    ones = jnp.ones((SLOT, requests), BF16)
    holder = lax.dot_general(numbers, held, NT, preferred_element_type=F32)
    covered = lax.dot_general(ones, spans.astype(BF16), NT, preferred_element_type=F32)
    meta_ref[0:1, :] = holder[0:1, :].astype(jnp.int32) - 1
    meta_ref[1:2, :] = covered[0:1, :].astype(jnp.int32)
    meta_ref[2:3, :] = jnp.zeros((1, entries), jnp.int32)
    meta_ref[2:3, 0 : dest.shape[1]] = dest[...]
    meta_ref[3:4, :] = jnp.full((1, entries), ids_ref[0], jnp.int32)
    cosine, sine = rope_tables(ctx_row, requests)
    tables_ref[0] = cosine
    tables_ref[1] = sine
    held, spans = claims(pool + iota((inbox, requests), 0))
    away_ref[...] = held
    away_span = jnp.sum(spans, axis=1, keepdims=True)
    span_ref[...] = jnp.broadcast_to(away_span, span_ref.shape)
    for copy in large:
        copy.wait()


def query_kernel(
    count, meta_ref, *refs,
):
    pieces = refs[:count]
    (gain_ref, wq_ref, tables_ref, away_ref, span_ref,
     hidden_hbm, normed_hbm, packed_hbm, send_hbm, tables_hbm, meta_hbm,
     hiddens, norms, packs, sends, sends16, sems) = refs[count:]
    requests = hiddens.shape[0]
    inbox = span_ref.shape[0]
    width = wq_ref.shape[1]
    chunks = -(-width // LANES)
    if count == 1:
        hidden = pieces[0][...]
    else:
        own, other = pieces[0][...], pieces[1][...]
        first = meta_ref[3:4, 0:1] == 0
        hidden = jnp.concatenate(
            [jnp.where(first, own, other), jnp.where(first, other, own)], axis=0
        )
    hiddens[...] = hidden
    normed = norm_rows(hidden.astype(F32), gain_ref[...])
    norms[...] = normed
    early = [
        copy_of(hiddens, hidden_hbm, sems.at[0]),
        copy_of(norms, normed_hbm, sems.at[1]),
        copy_of(tables_ref, tables_hbm, sems.at[4]),
        copy_of(meta_ref, meta_hbm, sems.at[5]),
    ]
    for copy in early:
        copy.start()
    queries = jnp.dot(normed, wq_ref[...], preferred_element_type=F32)
    if chunks * LANES > width:
        pad = jnp.zeros((requests, chunks * LANES - width), F32)
        queries = jnp.concatenate([queries, pad], axis=1)
    cosine, sine = tables_ref[0], tables_ref[1]
    zeros = jnp.zeros((requests, LANES), F32)
    nothing = jnp.zeros((inbox, LANES), F32)
    for j in range(SLOT):
        here = pl.ds(j, requests, stride=SLOT)
        there = pl.ds(j, inbox, stride=SLOT)
        if j < chunks:
            chunk = rotate(queries[:, j * LANES : (j + 1) * LANES], cosine, sine)
            chunk = (chunk.astype(BF16).astype(F32) * ATTN_SCALE).astype(BF16)
            packs[here, :] = chunk.astype(F32)
            sends[there, :] = jnp.dot(away_ref[...], chunk, preferred_element_type=F32)
        else:
            packs[here, :] = zeros
            sends[there, :] = span_ref[...] if j == META else nothing
    sends16[...] = sends[...].astype(BF16)
    late = [
        copy_of(sends16, send_hbm, sems.at[2]),
        copy_of(packs, packed_hbm, sems.at[3]),
    ]
    for copy in late:
        copy.start()
    for copy in early + late:
        copy.wait()


def unpack(packed):
    low = iota(packed.shape, 1) < HEAD_DIM
    even = jnp.where(low, packed, 0.0)
    odd = jnp.where(low, pltpu.roll(packed, HEAD_DIM, 1), 0.0)
    return jnp.concatenate([even, odd], axis=0)


def head_rows(heads):
    return [(h // 2) + SLOT * (h % 2) for h in range(heads)]


def token_of_column(heads, kv_local, columns):
    row = iota((ROWS, columns), 0)
    column = iota((ROWS, columns), 1)
    wanted = jnp.full((ROWS, columns), kv_local, jnp.int32)
    for h, place in enumerate(head_rows(heads)):
        wanted = jnp.where(row == place, h // (heads // kv_local), wanted)
    return jnp.where(column % kv_local == wanted, column // kv_local, 1 << 20)


def score_page(query, block):
    return lax.dot_general(query, block, NT, preferred_element_type=F32)


def weigh_page(scores, tokens, span):
    scores = jnp.where(tokens < span, scores, NEG_FILL)
    top = jnp.max(scores, axis=1, keepdims=True)
    weights = jnp.exp(scores - top)
    return top, jnp.sum(weights, axis=1, keepdims=True), weights.astype(BF16)


def value_page(weights, block):
    return jnp.dot(weights, block, preferred_element_type=F32)


def attend_pages(
    count, stage, copies, query_of, block_of, span_of, tokens, keep, aside=None
):
    stages = [range(i, min(i + stage, count)) for i in range(0, count, stage)]

    def score_stage(pages):
        for p in pages:
            copies[p].wait()
        return {p: score_page(query_of(p), block_of(p)) for p in pages}

    scores = score_stage(stages[0])
    for i, pages in enumerate(stages):
        if i + 1 < len(stages):
            ahead = score_stage(stages[i + 1])
        if aside is not None:
            aside(i, len(stages))
        weighed = {p: weigh_page(scores[p], tokens, span_of(p)) for p in pages}
        outs = {p: value_page(weighed[p][2], block_of(p)) for p in pages}
        for p in pages:
            keep(p, weighed[p][0], weighed[p][1], outs[p])
        if i + 1 < len(stages):
            scores = ahead


def spread_queries(target, packed):
    low = iota(packed.shape, 2) < HEAD_DIM
    target[:, 0:SLOT, :] = jnp.where(low, packed, 0.0)
    target[:, SLOT:ROWS, :] = jnp.where(low, pltpu.roll(packed, HEAD_DIM, 2), 0.0)


def first_kernel(
    heads, kv_local, meta_hbm, packed_hbm, normed_hbm, wkv_hbm, tables_hbm, cache_hbm,
    new_hbm, tops_hbm, sums_hbm,
    meta, packed, normed, raw, wide, tables, pages, queries, new, tops, sums, sems,
):
    requests, depth = normed.shape
    count, columns, _ = pages.shape
    small = [
        copy_of(meta_hbm, meta, sems.at[0]),
        copy_of(packed_hbm, packed, sems.at[1]),
        copy_of(normed_hbm, normed, sems.at[2]),
        copy_of(tables_hbm, tables, sems.at[3]),
    ]
    weights = copy_of(wkv_hbm, raw, sems.at[4])
    paging = page_copies(cache_hbm, 0, pages, 0, count, sems, 9)
    for copy in small + paging[:8] + [weights] + paging[8:]:
        copy.start()
    for copy in small:
        copy.wait()
    spread_queries(queries, packed[...].reshape(requests, SLOT, LANES))
    tokens = token_of_column(heads, kv_local, columns)
    lower = iota((ROWS, LANES), 1) < HEAD_DIM
    low = iota((requests, LANES), 1) < HEAD_DIM
    cosine = jnp.where(low, tables[0], 1.0)
    sine = jnp.where(low, tables[1], 0.0)

    def project(stage, stages):
        if stage == 0:
            weights.wait()
            if kv_local > 1:
                wide[...] = raw[...].astype(F32)
            return
        for k in range(stage - 1, kv_local, stages - 1):
            if kv_local > 1:
                weight = wide[pl.ds(k, depth, stride=kv_local), :].astype(BF16)
            else:
                weight = raw[...]
            projected = jnp.dot(normed[...], weight, preferred_element_type=F32)
            new[k] = rotate(projected, cosine, sine).astype(BF16).astype(F32)

    def keep(p, top, total, out):
        tops[p] = jnp.broadcast_to(top, (ROWS, LANES))
        sums[p] = jnp.where(lower, total, out)

    attend_pages(
        count,
        4,
        paging,
        lambda p: queries[jnp.maximum(meta[0, p], 0)].astype(BF16),
        lambda p: pages[p],
        lambda p: meta[1, p],
        tokens,
        keep,
        project,
    )
    parked = [
        copy_of(new, new_hbm, sems.at[6]),
        copy_of(tops, tops_hbm, sems.at[7]),
        copy_of(sums, sums_hbm, sems.at[8]),
    ]
    for copy in parked:
        copy.start()
    for copy in parked:
        copy.wait()


def merge_pages(places, top_of, sum_of, top, acc, scaled, start, before):
    requests = start.shape[0]
    for p, place in enumerate(places):
        top[place] = jnp.maximum(top[place], top_of(p))
    acc[0:requests] = start * jnp.exp(before - top[0:requests])
    for p, place in enumerate(places):
        scaled[p] = sum_of(p) * jnp.exp(top_of(p) - top[place])
    for p, place in enumerate(places):
        acc[place] = acc[place] + scaled[p]


def second_kernel(
    heads, kv_local, first, meta_hbm, packed_hbm, new_hbm, tops_hbm, sums_hbm,
    cache_hbm, order_hbm, state_hbm,
    meta, packed, new, tops, sums, pages, queries, fresh, top, acc, scaled, sems,
):
    del order_hbm
    requests = queries.shape[0]
    local_pages = tops.shape[0]
    count, columns, _ = pages.shape
    small = [
        copy_of(meta_hbm, meta, sems.at[0]),
        copy_of(packed_hbm, packed, sems.at[1]),
        copy_of(new_hbm, new, sems.at[2]),
    ]
    earlier = [
        copy_of(tops_hbm, tops.at[pl.ds(0, first)], sems.at[3]),
        copy_of(sums_hbm, sums.at[pl.ds(0, first)], sems.at[4]),
    ]
    paging = page_copies(cache_hbm, first, pages, 0, count, sems, 6)
    for copy in small + paging + earlier:
        copy.start()
    for copy in small:
        copy.wait()
    spread_queries(queries, packed[...].reshape(requests, SLOT, LANES))
    used = {place: h for h, place in enumerate(head_rows(heads))}
    for place in range(ROWS):
        value = jnp.zeros((requests, LANES), F32)
        if place in used:
            value = new[used[place] // (heads // kv_local)]
        fresh[pl.ds(place, requests, stride=ROWS), :] = value
    tokens = token_of_column(heads, kv_local, columns)
    lower = iota((ROWS, LANES), 1) < HEAD_DIM
    added = fresh[...].reshape(requests, ROWS, LANES)
    low16 = iota(added.shape, 2) < HEAD_DIM
    score = jnp.sum(queries[...] * added, axis=2, keepdims=True)
    before = jnp.broadcast_to(score, added.shape)
    start = jnp.where(low16, 1.0, added)
    top[0:requests] = before

    def keep(p, top, total, out):
        tops[first + p] = jnp.broadcast_to(top, (ROWS, LANES))
        sums[first + p] = jnp.where(lower, total, out)

    attend_pages(
        count,
        4,
        paging,
        lambda p: queries[jnp.maximum(meta[0, first + p], 0)].astype(BF16),
        lambda p: pages[p],
        lambda p: meta[1, first + p],
        tokens,
        keep,
    )
    for copy in earlier:
        copy.wait()

    def place_of(p):
        owner = meta[0, p]
        return jnp.where(owner < 0, requests, owner)

    places = [place_of(p) for p in range(local_pages)]
    merge_pages(
        places, lambda p: tops[p], lambda p: sums[p], top, acc, scaled, start, before
    )
    whole = acc[0:requests]
    acc[0:requests] = jnp.where(
        low16, top[0:requests] + jnp.log(whole), whole / pltpu.roll(whole, HEAD_DIM, 2)
    )
    parked = copy_of(acc.at[pl.ds(0, requests)], state_hbm, sems.at[5])
    parked.start()
    parked.wait()


def lent_kernel(
    heads, kv_local, local_pages, meta_hbm, asked_ref, cache_hbm, order_hbm, reply_ref,
    meta, pages, asked, reply, sems,
):
    del order_hbm
    outgoing, columns, _ = pages.shape
    meta_copy = copy_of(meta_hbm, meta, sems.at[0])
    paging = page_copies(cache_hbm, local_pages, pages, 0, outgoing, sems, 1)
    for copy in [meta_copy] + paging:
        copy.start()
    asked[...] = asked_ref[...].astype(F32)
    reply[...] = jnp.zeros(reply.shape, F32)
    tokens = token_of_column(heads, kv_local, columns).astype(F32)
    low = iota((SLOT, LANES), 1) < HEAD_DIM
    lane = iota((SLOT, LANES), 1)
    row = iota((SLOT, LANES), 0)

    def terms(total, offset):
        leading = total.astype(BF16).astype(F32)
        rest = total - leading
        second = rest.astype(BF16).astype(F32)
        third = rest - second
        spot = lane - offset - 3 * row
        placed = jnp.where(spot == 0, leading, 0.0)
        placed = jnp.where(spot == 1, second, placed)
        return jnp.where(spot == 2, third, placed)

    def rows_of(j):
        dest = meta[2, j]
        rank = jnp.int32(0)
        for e in range(j):
            rank = rank + (meta[2, e] == dest).astype(jnp.int32)
        return pl.ds(pl.multiple_of((dest * CAP + rank) * SLOT, SLOT), SLOT)

    meta_copy.wait()
    places = [rows_of(j) for j in range(outgoing)]
    packed = [asked[rows, :] for rows in places]
    replies = {}

    def keep(j, top, total, out):
        out = out / total
        logs = top + jnp.log(total)
        even = pltpu.roll(out[0:SLOT], HEAD_DIM, 1)
        both = jnp.where(low, even, out[SLOT:ROWS])
        line = jnp.sum(
            terms(logs[0:SLOT], 0) + terms(logs[SLOT:ROWS], HEAD_DIM), axis=0, keepdims=True
        )
        replies[j] = jnp.where(row == META, line, both)

    attend_pages(
        outgoing,
        4,
        paging,
        lambda j: unpack(packed[j]).astype(BF16),
        lambda j: pages[j],
        lambda j: packed[j][META : META + 1, 0:1],
        tokens,
        keep,
    )
    for j in range(outgoing):
        reply[places[j], :] = replies[j]
    reply_ref[...] = reply[...].astype(BF16)


def combine_kernel(
    heads, pool, meta_hbm, state_hbm, wo_hbm, hidden_hbm, gain_hbm, router_hbm,
    routes_hbm, wd_hbm, reply_ref,
    part_ref, meta_ref, hidden_ref, gain_ref, router_ref, routes_ref, wd_ref,
    meta, state, wo, gain, tops, accs, scaled, reply, finals, sems,
):
    requests = state.shape[0]
    inbox = reply_ref.shape[0] // SLOT
    chunks = -(-heads // 2)
    small = [
        copy_of(meta_hbm, meta, sems.at[0]),
        copy_of(state_hbm, state, sems.at[1]),
    ]
    weights = copy_of(wo_hbm, wo, sems.at[2])
    gaining = copy_of(gain_hbm, gain, sems.at[3])
    later = [
        copy_of(meta_hbm, meta_ref, sems.at[4]),
        copy_of(hidden_hbm, hidden_ref, sems.at[5]),
        copy_of(router_hbm, router_ref, sems.at[6]),
        copy_of(routes_hbm, routes_ref, sems.at[7]),
        copy_of(wd_hbm, wd_ref, sems.at[8]),
    ]
    for copy in small + [weights, gaining] + later:
        copy.start()
    reply[...] = reply_ref[...].astype(F32)
    low = iota((SLOT, LANES), 1) < HEAD_DIM
    lane = iota((SLOT, LANES), 1)
    row = iota((SLOT, LANES), 0)
    mine = (lane % HEAD_DIM) // 3 == row

    def place_of(s):
        owner = meta[0, pool + s]
        return jnp.where(owner < 0, requests, owner)

    def logs_of(s):
        line = reply[s * SLOT + META : s * SLOT + META + 1, :]
        line = jnp.where(mine, jnp.broadcast_to(line, (SLOT, LANES)), 0.0)
        even = jnp.sum(jnp.where(low, line, 0.0), axis=1, keepdims=True)
        odd = jnp.sum(jnp.where(low, 0.0, line), axis=1, keepdims=True)
        logs = jnp.concatenate([even, odd], axis=0)
        return jnp.broadcast_to(logs, (ROWS, LANES))

    logs = [logs_of(s) for s in range(inbox)]
    for copy in small:
        copy.wait()
    low16 = iota(state.shape, 2) < HEAD_DIM
    start = state[...]
    before = jnp.where(low16, start, pltpu.roll(start, HEAD_DIM, 2))
    tops[0:requests] = before

    def sum_of(s):
        packed = reply[s * SLOT : (s + 1) * SLOT, :]
        even = jnp.where(low, 1.0, pltpu.roll(packed, HEAD_DIM, 1))
        odd = jnp.where(low, 1.0, packed)
        return jnp.concatenate([even, odd], axis=0)

    merge_pages(
        [place_of(s) for s in range(inbox)],
        lambda s: logs[s],
        sum_of,
        tops,
        accs,
        scaled,
        jnp.where(low16, 1.0, start),
        before,
    )
    whole = accs[0:requests]
    finals[...] = (whole / pltpu.roll(whole, HEAD_DIM, 2)).reshape(
        requests * ROWS, LANES
    )
    wide = iota((requests, LANES), 1) < HEAD_DIM
    parts = []
    for j in range(chunks):
        even = finals[pl.ds(j, requests, stride=ROWS), :]
        odd = finals[pl.ds(SLOT + j, requests, stride=ROWS), :]
        parts.append(jnp.where(wide, pltpu.roll(even, HEAD_DIM, 1), odd).astype(BF16))
    attention = jnp.concatenate(parts, axis=1)[:, : heads * HEAD_DIM]
    weights.wait()
    part_ref[...] = jnp.dot(attention, wo[...], preferred_element_type=F32).astype(BF16)
    gaining.wait()
    gain_ref[...] = gain[...].reshape(1, gain.shape[0])
    for copy in later:
        copy.wait()


def own_rows(values, first):
    half = values.shape[0] // 2
    return jnp.where(first, values[:half], values[half:])


def gate_kernel(
    tp, units, count, meta_ref, hidden_ref, *refs,
):
    pieces = refs[:count]
    (gain_ref, router_ref, routes_ref, attended_ref, input_ref, spread_ref) = refs[count:]
    requests = hidden_ref.shape[0]
    if count == 2:
        summed = pieces[0][...].astype(F32) + pieces[1][...].astype(F32)
    else:
        summed = pieces[0][0:requests, :].astype(F32)
        for t in range(1, tp):
            part = pieces[0][t * requests : (t + 1) * requests, :]
            summed = summed + part.astype(F32)
    attended = (hidden_ref[...].astype(F32) + RESID_SCALE * summed).astype(BF16)
    if count == 2:
        attended_ref[...] = own_rows(attended, meta_ref[3:4, 0:1] == 0)
    else:
        attended_ref[...] = attended
    ffn_input = norm_rows(attended.astype(F32), gain_ref[...])
    input_ref[...] = ffn_input
    logits = lax.dot_general(router_ref[...], ffn_input, NT, preferred_element_type=F32)
    expert = iota(logits.shape, 0)
    named = jnp.zeros(logits.shape, F32)
    for k in range(routes_ref.shape[0]):
        named = jnp.where(routes_ref[k : k + 1, :] == expert, 1.0, named)
    chosen = named > 0.5
    top = jnp.max(jnp.where(chosen, logits, NEG_FILL), axis=0, keepdims=True)
    weights = jnp.where(chosen, jnp.exp(logits - top), 0.0)
    gates = weights / jnp.sum(weights, axis=0, keepdims=True)
    mine = expert == meta_ref[3:4, 0:1] * units // FF
    line = jnp.sum(jnp.where(mine, gates, 0.0), axis=0, keepdims=True)
    diagonal = iota((requests, requests), 0) == iota((requests, requests), 1)
    line = jnp.where(diagonal, jnp.broadcast_to(line, (requests, requests)), 0.0)
    column = jnp.sum(line, axis=1, keepdims=True)
    spread_ref[...] = jnp.broadcast_to(column, spread_ref.shape)


def expert_kernel(meta_ref, lifted_ref, spread_ref, wd_ref, *outs):
    gate = lifted_ref[0]
    active = gate / (1.0 + jnp.exp(-gate)) * lifted_ref[1] * spread_ref[:, 0:1]
    share = jnp.dot(active.astype(BF16), wd_ref[...], preferred_element_type=F32)
    if len(outs) == 2:
        first = meta_ref[3:4, 0:1] == 0
        outs[0][...] = own_rows(share, first)
        outs[1][...] = own_rows(share, jnp.logical_not(first)).astype(BF16)
    else:
        outs[0][...] = share.astype(BF16)


def call(body, outs, in_specs, scratch=(), limit=16, flops=0, moved=0):
    return pl.pallas_call(
        body,
        out_shape=outs,
        in_specs=in_specs,
        out_specs=[VMEM if isinstance(o, jax.ShapeDtypeStruct) else HBM for o in outs],
        scratch_shapes=list(scratch),
        compiler_params=pltpu.CompilerParams(vmem_limit_bytes=limit << 20),
        cost_estimate=pl.CostEstimate(
            flops=flops, bytes_accessed=moved, transcendentals=0
        ),
    )


def swap(values):
    return lax.ppermute(values, "tensor", [(0, 1), (1, 0)])


def on_device(
    hidden,
    attn_gain,
    w_query,
    w_keyvalue,
    w_output,
    cache,
    page_table,
    ctx_len,
    move_dest,
    ffn_gain,
    router,
    routes,
    w_in,
    w_down,
):
    replicas = lax.axis_size("replica")
    tp = lax.axis_size("tensor")
    rank = lax.axis_index("tensor").astype(jnp.int32)
    rows, width = hidden.shape
    pool, page_len, kv_local, _ = cache.shape
    outgoing = move_dest.shape[0]
    local_pages = pool - outgoing
    requests = page_table.shape[0]
    heads = w_query.shape[1] // HEAD_DIM
    inbox = replicas * CAP
    units = w_down.shape[0]
    assert FF % units == 0
    columns = page_len * kv_local
    entries = -(-(pool + inbox) // LANES) * LANES
    first = local_pages // 2
    struct = jax.ShapeDtypeStruct
    pair = tp == 2
    ids = rank.reshape(1)

    def pin(values):
        return pltpu.with_memory_space_constraint(values, pltpu.HBM)

    def exchange(blocks):
        blocks = blocks.reshape(replicas, CAP * SLOT, LANES)
        blocks = lax.all_to_all(blocks, "replica", split_axis=0, concat_axis=0, tiled=True)
        return blocks.reshape(inbox * SLOT, LANES)

    blocks = pin(cache.reshape(pool, columns, LANES))
    if pair:
        pieces = [hidden, swap(hidden)]
    else:
        pieces = [lax.all_gather(hidden, "tensor", axis=0, tiled=True)]
    meta_shape = (4, entries)
    tables_shape = (2, requests, LANES)
    own, wq, gain, tables, away, away_span, meta = call(
        functools.partial(prepare_kernel, pool, replicas),
        [
            struct(hidden.shape, BF16),
            struct(w_query.shape, BF16),
            struct((1, width), F32),
            struct(tables_shape, F32),
            struct((inbox, requests), BF16),
            struct((inbox, LANES), F32),
            struct(meta_shape, jnp.int32),
        ],
        [SMEM] + [HBM] * 6,
        [
            pltpu.VMEM((1, requests), jnp.int32),
            pltpu.VMEM((page_table.shape[1], requests), jnp.int32),
            pltpu.VMEM((1, outgoing), jnp.int32),
            pltpu.VMEM((width,), F32),
            pltpu.SemaphoreType.DMA((6,)),
        ],
        moved=2 * w_query.size,
    )(
        ids,
        pin(hidden),
        pin(ctx_len.reshape(1, requests)),
        pin(page_table.T),
        pin(move_dest.reshape(1, outgoing)),
        pin(attn_gain),
        pin(w_query),
    )
    if pair:
        pieces[0] = own
    hidden_far, normed, packed, sends, tables_far, meta_far = call(
        functools.partial(query_kernel, len(pieces)),
        [
            pltpu.HBM((requests, width), BF16),
            pltpu.HBM((requests, width), BF16),
            pltpu.HBM((requests * SLOT, LANES), F32),
            pltpu.HBM((inbox * SLOT, LANES), BF16),
            pltpu.HBM(tables_shape, F32),
            pltpu.HBM(meta_shape, jnp.int32),
        ],
        [VMEM] * (len(pieces) + 6),
        [
            pltpu.VMEM((requests, width), BF16),
            pltpu.VMEM((requests, width), BF16),
            pltpu.VMEM((requests * SLOT, LANES), F32),
            pltpu.VMEM((inbox * SLOT, LANES), F32),
            pltpu.VMEM((inbox * SLOT, LANES), BF16),
            pltpu.SemaphoreType.DMA((6,)),
        ],
        flops=4 * requests * width * w_query.shape[1],
        moved=2 * w_query.size,
    )(meta, *pieces, gain, wq, tables, away, away_span)
    asked = exchange(sends)
    new, tops, sums = call(
        functools.partial(first_kernel, heads, kv_local),
        [
            pltpu.HBM((kv_local, requests, LANES), F32),
            pltpu.HBM((first, ROWS, LANES), F32),
            pltpu.HBM((first, ROWS, LANES), F32),
        ],
        [HBM] * 6,
        [
            pltpu.SMEM(meta_shape, jnp.int32),
            pltpu.VMEM((requests * SLOT, LANES), F32),
            pltpu.VMEM((requests, width), BF16),
            pltpu.VMEM((width * kv_local, LANES), BF16),
            pltpu.VMEM((width * kv_local, LANES), F32),
            pltpu.VMEM(tables_shape, F32),
            pltpu.VMEM((first, columns, LANES), BF16),
            pltpu.VMEM((requests, ROWS, LANES), F32),
            pltpu.VMEM((kv_local, requests, LANES), F32),
            pltpu.VMEM((first, ROWS, LANES), F32),
            pltpu.VMEM((first, ROWS, LANES), F32),
            pltpu.SemaphoreType.DMA((9 + first,)),
        ],
        flops=4 * ROWS * columns * LANES * first,
        moved=2 * columns * LANES * first,
    )(
        pin(meta_far),
        pin(packed),
        pin(normed),
        pin(w_keyvalue.reshape(width * kv_local, LANES)),
        pin(tables_far),
        blocks,
    )
    (replies,) = call(
        functools.partial(lent_kernel, heads, kv_local, local_pages),
        [struct((inbox * SLOT, LANES), BF16)],
        [HBM, VMEM, HBM, HBM],
        [
            pltpu.SMEM(meta_shape, jnp.int32),
            pltpu.VMEM((outgoing, columns, LANES), BF16),
            pltpu.VMEM((inbox * SLOT, LANES), F32),
            pltpu.VMEM((inbox * SLOT, LANES), F32),
            pltpu.SemaphoreType.DMA((1 + outgoing,)),
        ],
        flops=4 * ROWS * columns * LANES * outgoing,
        moved=2 * columns * LANES * outgoing,
    )(pin(meta_far), asked, blocks, pin(tops))
    returned = exchange(replies)
    (state,) = call(
        functools.partial(second_kernel, heads, kv_local, first),
        [pltpu.HBM((requests, ROWS, LANES), F32)],
        [HBM] * 6 + [ANY],
        [
            pltpu.SMEM(meta_shape, jnp.int32),
            pltpu.VMEM((requests * SLOT, LANES), F32),
            pltpu.VMEM((kv_local, requests, LANES), F32),
            pltpu.VMEM((local_pages, ROWS, LANES), F32),
            pltpu.VMEM((local_pages, ROWS, LANES), F32),
            pltpu.VMEM((local_pages - first, columns, LANES), BF16),
            pltpu.VMEM((requests, ROWS, LANES), F32),
            pltpu.VMEM((requests * ROWS, LANES), F32),
            pltpu.VMEM((requests + 1, ROWS, LANES), F32),
            pltpu.VMEM((requests + 1, ROWS, LANES), F32),
            pltpu.VMEM((local_pages, ROWS, LANES), F32),
            pltpu.SemaphoreType.DMA((6 + local_pages - first,)),
        ],
        flops=4 * ROWS * columns * LANES * (local_pages - first),
        moved=2 * columns * LANES * (local_pages - first),
    )(pin(meta_far), pin(packed), pin(new), pin(tops), pin(sums), blocks, replies)
    part, meta, hidden_all, gain, router_t, routes_t, wd = call(
        functools.partial(combine_kernel, heads, pool),
        [
            struct((requests, width), BF16),
            struct(meta_shape, jnp.int32),
            struct((requests, width), BF16),
            struct((1, width), F32),
            struct(router.shape[::-1], BF16),
            struct(routes.shape[::-1], jnp.int32),
            struct(w_down.shape, BF16),
        ],
        [HBM] * 8 + [VMEM],
        [
            pltpu.SMEM(meta_shape, jnp.int32),
            pltpu.VMEM((requests, ROWS, LANES), F32),
            pltpu.VMEM(w_output.shape, BF16),
            pltpu.VMEM((width,), F32),
            pltpu.VMEM((requests + 1, ROWS, LANES), F32),
            pltpu.VMEM((requests + 1, ROWS, LANES), F32),
            pltpu.VMEM((inbox, ROWS, LANES), F32),
            pltpu.VMEM((inbox * SLOT, LANES), F32),
            pltpu.VMEM((requests * ROWS, LANES), F32),
            pltpu.SemaphoreType.DMA((9,)),
        ],
        flops=2 * requests * w_output.size,
        moved=2 * (w_output.size + w_down.size),
    )(
        pin(meta_far), pin(state), pin(w_output), pin(hidden_far), pin(ffn_gain),
        pin(router.T), pin(routes.T), pin(w_down), returned,
    )
    if pair:
        parts = [part, swap(part)]
    else:
        parts = [lax.all_gather(part, "tensor", axis=0, tiled=True)]
    attended, ffn_input, spread = call(
        functools.partial(gate_kernel, tp, units, len(parts)),
        [
            struct((rows if pair else requests, width), BF16),
            struct((requests, width), BF16),
            struct((requests, LANES), F32),
        ],
        [VMEM] * (len(parts) + 5),
        flops=2 * requests * router.size,
        moved=2 * router.size,
    )(meta, hidden_all, *parts, gain, router_t, routes_t)
    lifted = jnp.einsum("rd,dsu->sru", ffn_input, w_in, preferred_element_type=F32)
    shapes = [struct((requests, width), BF16)]
    if pair:
        shapes = [struct((rows, width), F32), struct((rows, width), BF16)]
    shares = call(
        expert_kernel,
        shapes,
        [VMEM] * 4,
        flops=2 * requests * w_down.size,
        moved=2 * w_down.size,
    )(meta, lifted, spread, wd)
    if pair:
        return attended, (shares[0] + swap(shares[1]).astype(F32)).astype(BF16)
    shares = lax.all_gather(shares[0], "tensor", axis=0)
    mine = lax.dynamic_slice_in_dim(shares, rank * rows, rows, axis=1)
    experts_out = jnp.sum(mine.astype(F32), axis=0).astype(BF16)
    attended = lax.dynamic_slice_in_dim(attended, rank * rows, rows, axis=0)
    return attended, experts_out


def solution(mesh):
    placed = (
        P(("replica", "tensor"), None),
        P(),
        P(None, "tensor"),
        P(None, "tensor", None),
        P("tensor", None),
        P("replica", None, "tensor", None),
        P("replica", None),
        P("replica"),
        P("replica"),
        P(),
        P(),
        P("replica", None),
        P(None, None, "tensor"),
        P("tensor", None),
    )
    return jax.shard_map(
        on_device,
        mesh=mesh,
        in_specs=placed,
        out_specs=(P(("replica", "tensor"), None), P(("replica", "tensor"), None)),
        check_vma=False,
    )
```

```python
import functools
import math

import jax
import jax.numpy as jnp
from jax import lax
from jax.experimental import pallas as pl
from jax.experimental.pallas import tpu as pltpu
from jax.sharding import PartitionSpec as P

HEAD_DIM = 64
EXPERTS = 40
FF = 512
CAP = 2
LANES = 128
SLOT = 8
ROWS = 16
META = 6

ATTN_SCALE = 0.015625
RESID_SCALE = 0.22
ROPE_BASE = 10000.0
EPSILON = 1e-06
NEG_FILL = -1e30

F32 = jnp.float32
BF16 = jnp.bfloat16
VMEM = pl.BlockSpec(memory_space=pltpu.VMEM)
SMEM = pl.BlockSpec(memory_space=pltpu.SMEM)
ANY = pl.BlockSpec(memory_space=pl.ANY)
HBM = pl.BlockSpec(memory_space=pltpu.HBM)
NT = (((1,), (1,)), ((), ()))


def iota(shape, axis):
    return lax.broadcasted_iota(jnp.int32, shape, axis)


def norm_rows(values, gain):
    factor = lax.rsqrt(jnp.mean(values * values, axis=-1, keepdims=True) + EPSILON)
    return (values * factor * gain).astype(BF16)


def rope_tables(ctx_row, requests):
    diagonal = iota((requests, requests), 0) == iota((requests, requests), 1)
    ctx = jnp.broadcast_to(ctx_row.astype(F32), (requests, requests))
    ctx = jnp.sum(jnp.where(diagonal, ctx, 0.0), axis=1, keepdims=True)
    lane = iota((requests, LANES), 1)
    index = (lane % (HEAD_DIM // 2)).astype(F32)
    inverse = jnp.exp(index * (-2.0 * math.log(ROPE_BASE) / HEAD_DIM))
    angles = ctx * inverse
    sign = jnp.where(lane % HEAD_DIM < HEAD_DIM // 2, -1.0, 1.0)
    return jnp.cos(angles), jnp.sin(angles) * sign


def rotate(chunk, cosine, sine):
    lane = iota(chunk.shape, 1)
    ahead = pltpu.roll(chunk, LANES - HEAD_DIM // 2, 1)
    behind = pltpu.roll(chunk, HEAD_DIM // 2, 1)
    turned = jnp.where(lane % HEAD_DIM < HEAD_DIM // 2, ahead, behind)
    return chunk * cosine + turned * sine


def copy_of(source, target, sem):
    return pltpu.make_async_copy(source, target, sem)


def copies_of(source, target, sems, base):
    step = source.shape[0] // 4
    return [
        copy_of(
            source.at[pl.ds(i * step, step)], target.at[pl.ds(i * step, step)], sems.at[base + i]
        )
        for i in range(4)
    ]


def page_copies(cache_hbm, first, pages, place, count, sems, base):
    return [
        copy_of(cache_hbm.at[first + p], pages.at[place + p], sems.at[base + p])
        for p in range(count)
    ]


def prepare_kernel(
    pool, replicas, ids_ref, hidden_hbm, ctx_hbm, table_hbm, dest_hbm, attn_gain_hbm,
    wq_hbm,
    hidden_ref, wq_ref, gain_ref, tables_ref, away_ref, span_ref, meta_ref,
    ctx, table, dest, gain, sems,
):
    inbox = replicas * CAP
    requests = ctx.shape[1]
    entries = meta_ref.shape[1]
    small = [
        copy_of(ctx_hbm, ctx, sems.at[0]),
        copy_of(table_hbm, table, sems.at[1]),
        copy_of(dest_hbm, dest, sems.at[2]),
        copy_of(attn_gain_hbm, gain, sems.at[3]),
    ]
    large = [copy_of(hidden_hbm, hidden_ref, sems.at[4])]
    large += copies_of(wq_hbm, wq_ref, sems, 5)
    for copy in small + large:
        copy.start()
    for copy in small:
        copy.wait()
    gain_ref[...] = gain[...].reshape(1, gain.shape[0])
    ctx_row = ctx[...]

    def claims(values):
        held = jnp.zeros(values.shape, F32)
        spans = jnp.zeros(values.shape, F32)
        for k in range(table.shape[0]):
            match = table[k : k + 1, :] == values
            filled = jnp.clip(ctx_row - k * 128, 0, 128).astype(F32)
            held = jnp.where(match, 1.0, held)
            spans = jnp.where(match, filled, spans)
        return held.astype(BF16), spans

    held, spans = claims(iota((entries, requests), 0))
    numbers = (iota((SLOT, requests), 1) + 1).astype(BF16)
    ones = jnp.ones((SLOT, requests), BF16)
    holder = lax.dot_general(numbers, held, NT, preferred_element_type=F32)
    covered = lax.dot_general(ones, spans.astype(BF16), NT, preferred_element_type=F32)
    meta_ref[0:1, :] = holder[0:1, :].astype(jnp.int32) - 1
    meta_ref[1:2, :] = covered[0:1, :].astype(jnp.int32)
    meta_ref[2:3, :] = jnp.zeros((1, entries), jnp.int32)
    meta_ref[2:3, 0 : dest.shape[1]] = dest[...]
    meta_ref[3:4, :] = jnp.full((1, entries), ids_ref[0], jnp.int32)
    cosine, sine = rope_tables(ctx_row, requests)
    tables_ref[0] = cosine
    tables_ref[1] = sine
    held, spans = claims(pool + iota((inbox, requests), 0))
    away_ref[...] = held
    away_span = jnp.sum(spans, axis=1, keepdims=True)
    span_ref[...] = jnp.broadcast_to(away_span, span_ref.shape)
    for copy in large:
        copy.wait()


def query_kernel(
    count, meta_ref, *refs,
):
    pieces = refs[:count]
    (gain_ref, wq_ref, tables_ref, away_ref, span_ref,
     hidden_hbm, normed_hbm, packed_hbm, send_hbm, tables_hbm, meta_hbm,
     hiddens, norms, packs, sends, sends16, sems) = refs[count:]
    requests = hiddens.shape[0]
    inbox = span_ref.shape[0]
    width = wq_ref.shape[1]
    chunks = -(-width // LANES)
    if count == 1:
        hidden = pieces[0][...]
    else:
        own, other = pieces[0][...], pieces[1][...]
        first = meta_ref[3:4, 0:1] == 0
        hidden = jnp.concatenate(
            [jnp.where(first, own, other), jnp.where(first, other, own)], axis=0
        )
    hiddens[...] = hidden
    normed = norm_rows(hidden.astype(F32), gain_ref[...])
    norms[...] = normed
    early = [
        copy_of(hiddens, hidden_hbm, sems.at[0]),
        copy_of(norms, normed_hbm, sems.at[1]),
        copy_of(tables_ref, tables_hbm, sems.at[4]),
        copy_of(meta_ref, meta_hbm, sems.at[5]),
    ]
    for copy in early:
        copy.start()
    queries = jnp.dot(normed, wq_ref[...], preferred_element_type=F32)
    if chunks * LANES > width:
        pad = jnp.zeros((requests, chunks * LANES - width), F32)
        queries = jnp.concatenate([queries, pad], axis=1)
    cosine, sine = tables_ref[0], tables_ref[1]
    zeros = jnp.zeros((requests, LANES), F32)
    nothing = jnp.zeros((inbox, LANES), F32)
    for j in range(SLOT):
        here = pl.ds(j, requests, stride=SLOT)
        there = pl.ds(j, inbox, stride=SLOT)
        if j < chunks:
            chunk = rotate(queries[:, j * LANES : (j + 1) * LANES], cosine, sine)
            chunk = (chunk.astype(BF16).astype(F32) * ATTN_SCALE).astype(BF16)
            packs[here, :] = chunk.astype(F32)
            sends[there, :] = jnp.dot(away_ref[...], chunk, preferred_element_type=F32)
        else:
            packs[here, :] = zeros
            sends[there, :] = span_ref[...] if j == META else nothing
    sends16[...] = sends[...].astype(BF16)
    late = [
        copy_of(sends16, send_hbm, sems.at[2]),
        copy_of(packs, packed_hbm, sems.at[3]),
    ]
    for copy in late:
        copy.start()
    for copy in early + late:
        copy.wait()


def unpack(packed):
    low = iota(packed.shape, 1) < HEAD_DIM
    even = jnp.where(low, packed, 0.0)
    odd = jnp.where(low, pltpu.roll(packed, HEAD_DIM, 1), 0.0)
    return jnp.concatenate([even, odd], axis=0)


def head_rows(heads):
    return [(h // 2) + SLOT * (h % 2) for h in range(heads)]


def token_of_column(heads, kv_local, columns):
    row = iota((ROWS, columns), 0)
    column = iota((ROWS, columns), 1)
    wanted = jnp.full((ROWS, columns), kv_local, jnp.int32)
    for h, place in enumerate(head_rows(heads)):
        wanted = jnp.where(row == place, h // (heads // kv_local), wanted)
    return jnp.where(column % kv_local == wanted, column // kv_local, 1 << 20)


def attend_pages(count, stage, copies, query_of, block_of, span_of, tokens, keep):
    pairs = [(p, p + 1) for p in range(0, count, 2)]
    stages = [pairs[i : i + stage] for i in range(0, len(pairs), stage)]
    empty = jnp.zeros((ROWS, LANES), BF16)

    def blocks_of(pair):
        return jnp.concatenate([block_of(p) for p in pair], axis=1)

    def score_stage(pairs):
        for pair in pairs:
            for p in pair:
                copies[p].wait()
        scores = {}
        for a, b in pairs:
            top = jnp.concatenate([query_of(a), empty], axis=1)
            low = jnp.concatenate([empty, query_of(b)], axis=1)
            query = jnp.concatenate([top, low], axis=0)
            scores[a, b] = lax.dot_general(
                query, blocks_of((a, b)), NT, preferred_element_type=F32
            )
        return scores

    def weigh(scores, span):
        scores = jnp.where(tokens < span, scores, NEG_FILL)
        top = jnp.max(scores, axis=1, keepdims=True)
        weights = jnp.exp(scores - top)
        return top, jnp.sum(weights, axis=1, keepdims=True), weights.astype(BF16)

    scores = score_stage(stages[0])
    for i, pairs in enumerate(stages):
        if i + 1 < len(stages):
            ahead = score_stage(stages[i + 1])
        for a, b in pairs:
            first = weigh(scores[a, b][:ROWS], span_of(a))
            second = weigh(scores[a, b][ROWS:], span_of(b))
            weights = jnp.concatenate([first[2], second[2]], axis=0)
            outs = jnp.dot(weights, blocks_of((a, b)), preferred_element_type=F32)
            keep(a, first[0], first[1], outs[:ROWS, :LANES])
            keep(b, second[0], second[1], outs[ROWS:, LANES:])
        if i + 1 < len(stages):
            scores = ahead


def spread_queries(target, packed):
    low = iota(packed.shape, 2) < HEAD_DIM
    target[:, 0:SLOT, :] = jnp.where(low, packed, 0.0)
    target[:, SLOT:ROWS, :] = jnp.where(low, pltpu.roll(packed, HEAD_DIM, 2), 0.0)


def first_kernel(
    heads, kv_local, meta_hbm, packed_hbm, normed_hbm, wkv_hbm, tables_hbm, cache_hbm,
    new_hbm, tops_hbm, sums_hbm,
    meta, packed, normed, raw, wide, tables, pages, queries, new, tops, sums, sems,
):
    requests, depth = normed.shape
    count, columns, _ = pages.shape
    small = [
        copy_of(meta_hbm, meta, sems.at[0]),
        copy_of(packed_hbm, packed, sems.at[1]),
        copy_of(normed_hbm, normed, sems.at[2]),
        copy_of(tables_hbm, tables, sems.at[3]),
    ]
    weights = copy_of(wkv_hbm, raw, sems.at[4])
    paging = page_copies(cache_hbm, 0, pages, 0, count, sems, 9)
    for copy in small + [weights] + paging:
        copy.start()
    for copy in small:
        copy.wait()
    spread_queries(queries, packed[...].reshape(requests, SLOT, LANES))
    tokens = token_of_column(heads, kv_local, columns)
    lower = iota((ROWS, LANES), 1) < HEAD_DIM
    low = iota((requests, LANES), 1) < HEAD_DIM
    cosine = jnp.where(low, tables[0], 1.0)
    sine = jnp.where(low, tables[1], 0.0)
    weights.wait()
    if kv_local > 1:
        wide[...] = raw[...].astype(F32)
    for k in range(kv_local):
        if kv_local > 1:
            weight = wide[pl.ds(k, depth, stride=kv_local), :].astype(BF16)
        else:
            weight = raw[...]
        projected = jnp.dot(normed[...], weight, preferred_element_type=F32)
        new[k] = rotate(projected, cosine, sine).astype(BF16).astype(F32)

    def keep(p, top, total, out):
        tops[p] = jnp.broadcast_to(top, (ROWS, LANES))
        sums[p] = jnp.where(lower, total, out)

    attend_pages(
        count,
        2,
        paging,
        lambda p: queries[jnp.maximum(meta[0, p], 0)].astype(BF16),
        lambda p: pages[p],
        lambda p: meta[1, p],
        tokens,
        keep,
    )
    parked = [
        copy_of(new, new_hbm, sems.at[6]),
        copy_of(tops, tops_hbm, sems.at[7]),
        copy_of(sums, sums_hbm, sems.at[8]),
    ]
    for copy in parked:
        copy.start()
    for copy in parked:
        copy.wait()


def merge_pages(places, top_of, sum_of, top, acc, scaled, start, before):
    requests = start.shape[0]
    for p, place in enumerate(places):
        top[place] = jnp.maximum(top[place], top_of(p))
    acc[0:requests] = start * jnp.exp(before - top[0:requests])
    for p, place in enumerate(places):
        scaled[p] = sum_of(p) * jnp.exp(top_of(p) - top[place])
    for p, place in enumerate(places):
        acc[place] = acc[place] + scaled[p]


def second_kernel(
    heads, kv_local, first, meta_hbm, packed_hbm, new_hbm, tops_hbm, sums_hbm,
    cache_hbm, order_hbm, state_hbm,
    meta, packed, new, tops, sums, pages, queries, fresh, top, acc, scaled, sems,
):
    del order_hbm
    requests = queries.shape[0]
    local_pages = tops.shape[0]
    count, columns, _ = pages.shape
    small = [
        copy_of(meta_hbm, meta, sems.at[0]),
        copy_of(packed_hbm, packed, sems.at[1]),
        copy_of(new_hbm, new, sems.at[2]),
    ]
    earlier = [
        copy_of(tops_hbm, tops.at[pl.ds(0, first)], sems.at[3]),
        copy_of(sums_hbm, sums.at[pl.ds(0, first)], sems.at[4]),
    ]
    paging = page_copies(cache_hbm, first, pages, 0, count, sems, 6)
    for copy in small + paging + earlier:
        copy.start()
    for copy in small:
        copy.wait()
    spread_queries(queries, packed[...].reshape(requests, SLOT, LANES))
    used = {place: h for h, place in enumerate(head_rows(heads))}
    for place in range(ROWS):
        value = jnp.zeros((requests, LANES), F32)
        if place in used:
            value = new[used[place] // (heads // kv_local)]
        fresh[pl.ds(place, requests, stride=ROWS), :] = value
    tokens = token_of_column(heads, kv_local, columns)
    lower = iota((ROWS, LANES), 1) < HEAD_DIM
    added = fresh[...].reshape(requests, ROWS, LANES)
    low16 = iota(added.shape, 2) < HEAD_DIM
    score = jnp.sum(queries[...] * added, axis=2, keepdims=True)
    before = jnp.broadcast_to(score, added.shape)
    start = jnp.where(low16, 1.0, added)
    top[0:requests] = before

    def keep(p, top, total, out):
        tops[first + p] = jnp.broadcast_to(top, (ROWS, LANES))
        sums[first + p] = jnp.where(lower, total, out)

    attend_pages(
        count,
        2,
        paging,
        lambda p: queries[jnp.maximum(meta[0, first + p], 0)].astype(BF16),
        lambda p: pages[p],
        lambda p: meta[1, first + p],
        tokens,
        keep,
    )
    for copy in earlier:
        copy.wait()

    def place_of(p):
        owner = meta[0, p]
        return jnp.where(owner < 0, requests, owner)

    places = [place_of(p) for p in range(local_pages)]
    merge_pages(
        places, lambda p: tops[p], lambda p: sums[p], top, acc, scaled, start, before
    )
    whole = acc[0:requests]
    acc[0:requests] = jnp.where(
        low16, top[0:requests] + jnp.log(whole), whole / pltpu.roll(whole, HEAD_DIM, 2)
    )
    parked = copy_of(acc.at[pl.ds(0, requests)], state_hbm, sems.at[5])
    parked.start()
    parked.wait()


def lent_kernel(
    heads, kv_local, local_pages, meta_hbm, asked_ref, cache_hbm, order_hbm, reply_ref,
    meta, pages, asked, reply, sems,
):
    del order_hbm
    outgoing, columns, _ = pages.shape
    meta_copy = copy_of(meta_hbm, meta, sems.at[0])
    paging = page_copies(cache_hbm, local_pages, pages, 0, outgoing, sems, 1)
    for copy in [meta_copy] + paging:
        copy.start()
    asked[...] = asked_ref[...].astype(F32)
    reply[...] = jnp.zeros(reply.shape, F32)
    tokens = token_of_column(heads, kv_local, columns).astype(F32)
    low = iota((SLOT, LANES), 1) < HEAD_DIM
    lane = iota((SLOT, LANES), 1)
    row = iota((SLOT, LANES), 0)

    def terms(total, offset):
        leading = total.astype(BF16).astype(F32)
        rest = total - leading
        second = rest.astype(BF16).astype(F32)
        third = rest - second
        spot = lane - offset - 3 * row
        placed = jnp.where(spot == 0, leading, 0.0)
        placed = jnp.where(spot == 1, second, placed)
        return jnp.where(spot == 2, third, placed)

    def rows_of(j):
        dest = meta[2, j]
        rank = jnp.int32(0)
        for e in range(j):
            rank = rank + (meta[2, e] == dest).astype(jnp.int32)
        return pl.ds(pl.multiple_of((dest * CAP + rank) * SLOT, SLOT), SLOT)

    meta_copy.wait()
    places = [rows_of(j) for j in range(outgoing)]
    packed = [asked[rows, :] for rows in places]
    replies = {}

    def keep(j, top, total, out):
        out = out / total
        logs = top + jnp.log(total)
        even = pltpu.roll(out[0:SLOT], HEAD_DIM, 1)
        both = jnp.where(low, even, out[SLOT:ROWS])
        line = jnp.sum(
            terms(logs[0:SLOT], 0) + terms(logs[SLOT:ROWS], HEAD_DIM), axis=0, keepdims=True
        )
        replies[j] = jnp.where(row == META, line, both)

    attend_pages(
        outgoing,
        2,
        paging,
        lambda j: unpack(packed[j]).astype(BF16),
        lambda j: pages[j],
        lambda j: packed[j][META : META + 1, 0:1],
        tokens,
        keep,
    )
    for j in range(outgoing):
        reply[places[j], :] = replies[j]
    reply_ref[...] = reply[...].astype(BF16)


def combine_kernel(
    heads, pool, meta_hbm, state_hbm, wo_hbm, reply_ref,
    part_ref, meta, state, wo, tops, accs, scaled, reply, finals, sems,
):
    requests = state.shape[0]
    inbox = reply_ref.shape[0] // SLOT
    chunks = -(-heads // 2)
    small = [
        copy_of(meta_hbm, meta, sems.at[0]),
        copy_of(state_hbm, state, sems.at[1]),
    ]
    weights = copies_of(wo_hbm, wo, sems, 2)
    for copy in small + weights:
        copy.start()
    reply[...] = reply_ref[...].astype(F32)
    low = iota((SLOT, LANES), 1) < HEAD_DIM
    lane = iota((SLOT, LANES), 1)
    row = iota((SLOT, LANES), 0)
    mine = (lane % HEAD_DIM) // 3 == row

    def place_of(s):
        owner = meta[0, pool + s]
        return jnp.where(owner < 0, requests, owner)

    def logs_of(s):
        line = reply[s * SLOT + META : s * SLOT + META + 1, :]
        line = jnp.where(mine, jnp.broadcast_to(line, (SLOT, LANES)), 0.0)
        even = jnp.sum(jnp.where(low, line, 0.0), axis=1, keepdims=True)
        odd = jnp.sum(jnp.where(low, 0.0, line), axis=1, keepdims=True)
        logs = jnp.concatenate([even, odd], axis=0)
        return jnp.broadcast_to(logs, (ROWS, LANES))

    logs = [logs_of(s) for s in range(inbox)]
    for copy in small:
        copy.wait()
    low16 = iota(state.shape, 2) < HEAD_DIM
    start = state[...]
    before = jnp.where(low16, start, pltpu.roll(start, HEAD_DIM, 2))
    tops[0:requests] = before

    def sum_of(s):
        packed = reply[s * SLOT : (s + 1) * SLOT, :]
        even = jnp.where(low, 1.0, pltpu.roll(packed, HEAD_DIM, 1))
        odd = jnp.where(low, 1.0, packed)
        return jnp.concatenate([even, odd], axis=0)

    merge_pages(
        [place_of(s) for s in range(inbox)],
        lambda s: logs[s],
        sum_of,
        tops,
        accs,
        scaled,
        jnp.where(low16, 1.0, start),
        before,
    )
    whole = accs[0:requests]
    finals[...] = (whole / pltpu.roll(whole, HEAD_DIM, 2)).reshape(
        requests * ROWS, LANES
    )
    wide = iota((requests, LANES), 1) < HEAD_DIM
    parts = []
    for j in range(chunks):
        even = finals[pl.ds(j, requests, stride=ROWS), :]
        odd = finals[pl.ds(SLOT + j, requests, stride=ROWS), :]
        parts.append(jnp.where(wide, pltpu.roll(even, HEAD_DIM, 1), odd).astype(BF16))
    attention = jnp.concatenate(parts, axis=1)[:, : heads * HEAD_DIM]
    for copy in weights:
        copy.wait()
    part_ref[...] = jnp.dot(attention, wo[...], preferred_element_type=F32).astype(BF16)


def load_kernel(
    meta_hbm, hidden_hbm, gain_hbm, router_hbm, routes_hbm, wd_hbm, order_hbm,
    meta_ref, hidden_ref, gain_ref, router_ref, routes_ref, wd_ref, gain, sems,
):
    del order_hbm
    gaining = copy_of(gain_hbm, gain, sems.at[0])
    others = [
        copy_of(meta_hbm, meta_ref, sems.at[1]),
        copy_of(hidden_hbm, hidden_ref, sems.at[2]),
        copy_of(router_hbm, router_ref, sems.at[3]),
        copy_of(routes_hbm, routes_ref, sems.at[4]),
    ]
    others += copies_of(wd_hbm, wd_ref, sems, 5)
    for copy in [gaining] + others:
        copy.start()
    gaining.wait()
    gain_ref[...] = gain[...].reshape(1, gain.shape[0])
    for copy in others:
        copy.wait()


def own_rows(values, first):
    half = values.shape[0] // 2
    return jnp.where(first, values[:half], values[half:])


def gate_kernel(
    tp, units, count, meta_ref, hidden_ref, *refs,
):
    pieces = refs[:count]
    (gain_ref, router_ref, routes_ref, attended_ref, input_ref, spread_ref) = refs[count:]
    requests = hidden_ref.shape[0]
    if count == 2:
        summed = pieces[0][...].astype(F32) + pieces[1][...].astype(F32)
    else:
        summed = pieces[0][0:requests, :].astype(F32)
        for t in range(1, tp):
            part = pieces[0][t * requests : (t + 1) * requests, :]
            summed = summed + part.astype(F32)
    attended = (hidden_ref[...].astype(F32) + RESID_SCALE * summed).astype(BF16)
    if count == 2:
        attended_ref[...] = own_rows(attended, meta_ref[3:4, 0:1] == 0)
    else:
        attended_ref[...] = attended
    ffn_input = norm_rows(attended.astype(F32), gain_ref[...])
    input_ref[...] = ffn_input
    logits = lax.dot_general(router_ref[...], ffn_input, NT, preferred_element_type=F32)
    expert = iota(logits.shape, 0)
    named = jnp.zeros(logits.shape, F32)
    for k in range(routes_ref.shape[0]):
        named = jnp.where(routes_ref[k : k + 1, :] == expert, 1.0, named)
    chosen = named > 0.5
    top = jnp.max(jnp.where(chosen, logits, NEG_FILL), axis=0, keepdims=True)
    weights = jnp.where(chosen, jnp.exp(logits - top), 0.0)
    gates = weights / jnp.sum(weights, axis=0, keepdims=True)
    mine = expert == meta_ref[3:4, 0:1] * units // FF
    line = jnp.sum(jnp.where(mine, gates, 0.0), axis=0, keepdims=True)
    diagonal = iota((requests, requests), 0) == iota((requests, requests), 1)
    line = jnp.where(diagonal, jnp.broadcast_to(line, (requests, requests)), 0.0)
    column = jnp.sum(line, axis=1, keepdims=True)
    spread_ref[...] = jnp.broadcast_to(column, spread_ref.shape)


def expert_kernel(meta_ref, lifted_ref, spread_ref, wd_ref, *outs):
    gate = lifted_ref[0]
    active = gate / (1.0 + jnp.exp(-gate)) * lifted_ref[1] * spread_ref[:, 0:1]
    share = jnp.dot(active.astype(BF16), wd_ref[...], preferred_element_type=F32)
    if len(outs) == 2:
        first = meta_ref[3:4, 0:1] == 0
        outs[0][...] = own_rows(share, first)
        outs[1][...] = own_rows(share, jnp.logical_not(first)).astype(BF16)
    else:
        outs[0][...] = share.astype(BF16)


def call(body, outs, in_specs, scratch=(), limit=16, flops=0, moved=0):
    return pl.pallas_call(
        body,
        out_shape=outs,
        in_specs=in_specs,
        out_specs=[VMEM if isinstance(o, jax.ShapeDtypeStruct) else HBM for o in outs],
        scratch_shapes=list(scratch),
        compiler_params=pltpu.CompilerParams(vmem_limit_bytes=limit << 20),
        cost_estimate=pl.CostEstimate(
            flops=flops, bytes_accessed=moved, transcendentals=0
        ),
    )


def swap(values):
    return lax.ppermute(values, "tensor", [(0, 1), (1, 0)])


def on_device(
    hidden,
    attn_gain,
    w_query,
    w_keyvalue,
    w_output,
    cache,
    page_table,
    ctx_len,
    move_dest,
    ffn_gain,
    router,
    routes,
    w_in,
    w_down,
):
    replicas = lax.axis_size("replica")
    tp = lax.axis_size("tensor")
    rank = lax.axis_index("tensor").astype(jnp.int32)
    rows, width = hidden.shape
    pool, page_len, kv_local, _ = cache.shape
    outgoing = move_dest.shape[0]
    local_pages = pool - outgoing
    requests = page_table.shape[0]
    heads = w_query.shape[1] // HEAD_DIM
    inbox = replicas * CAP
    units = w_down.shape[0]
    assert FF % units == 0
    columns = page_len * kv_local
    entries = -(-(pool + inbox) // LANES) * LANES
    first = local_pages // 2
    struct = jax.ShapeDtypeStruct
    pair = tp == 2
    ids = rank.reshape(1)

    def pin(values):
        return pltpu.with_memory_space_constraint(values, pltpu.HBM)

    def exchange(blocks):
        blocks = blocks.reshape(replicas, CAP * SLOT, LANES)
        blocks = lax.all_to_all(blocks, "replica", split_axis=0, concat_axis=0, tiled=True)
        return blocks.reshape(inbox * SLOT, LANES)

    blocks = pin(cache.reshape(pool, columns, LANES))
    if pair:
        pieces = [hidden, swap(hidden)]
    else:
        pieces = [lax.all_gather(hidden, "tensor", axis=0, tiled=True)]
    meta_shape = (4, entries)
    tables_shape = (2, requests, LANES)
    own, wq, gain, tables, away, away_span, meta = call(
        functools.partial(prepare_kernel, pool, replicas),
        [
            struct(hidden.shape, BF16),
            struct(w_query.shape, BF16),
            struct((1, width), F32),
            struct(tables_shape, F32),
            struct((inbox, requests), BF16),
            struct((inbox, LANES), F32),
            struct(meta_shape, jnp.int32),
        ],
        [SMEM] + [HBM] * 6,
        [
            pltpu.VMEM((1, requests), jnp.int32),
            pltpu.VMEM((page_table.shape[1], requests), jnp.int32),
            pltpu.VMEM((1, outgoing), jnp.int32),
            pltpu.VMEM((width,), F32),
            pltpu.SemaphoreType.DMA((9,)),
        ],
        moved=2 * w_query.size,
    )(
        ids,
        pin(hidden),
        pin(ctx_len.reshape(1, requests)),
        pin(page_table.T),
        pin(move_dest.reshape(1, outgoing)),
        pin(attn_gain),
        pin(w_query),
    )
    if pair:
        pieces[0] = own
    hidden_far, normed, packed, sends, tables_far, meta_far = call(
        functools.partial(query_kernel, len(pieces)),
        [
            pltpu.HBM((requests, width), BF16),
            pltpu.HBM((requests, width), BF16),
            pltpu.HBM((requests * SLOT, LANES), F32),
            pltpu.HBM((inbox * SLOT, LANES), BF16),
            pltpu.HBM(tables_shape, F32),
            pltpu.HBM(meta_shape, jnp.int32),
        ],
        [VMEM] * (len(pieces) + 6),
        [
            pltpu.VMEM((requests, width), BF16),
            pltpu.VMEM((requests, width), BF16),
            pltpu.VMEM((requests * SLOT, LANES), F32),
            pltpu.VMEM((inbox * SLOT, LANES), F32),
            pltpu.VMEM((inbox * SLOT, LANES), BF16),
            pltpu.SemaphoreType.DMA((6,)),
        ],
        flops=4 * requests * width * w_query.shape[1],
        moved=2 * w_query.size,
    )(meta, *pieces, gain, wq, tables, away, away_span)
    asked = exchange(sends)
    new, tops, sums = call(
        functools.partial(first_kernel, heads, kv_local),
        [
            pltpu.HBM((kv_local, requests, LANES), F32),
            pltpu.HBM((first, ROWS, LANES), F32),
            pltpu.HBM((first, ROWS, LANES), F32),
        ],
        [HBM] * 6,
        [
            pltpu.SMEM(meta_shape, jnp.int32),
            pltpu.VMEM((requests * SLOT, LANES), F32),
            pltpu.VMEM((requests, width), BF16),
            pltpu.VMEM((width * kv_local, LANES), BF16),
            pltpu.VMEM((width * kv_local, LANES), F32),
            pltpu.VMEM(tables_shape, F32),
            pltpu.VMEM((first, columns, LANES), BF16),
            pltpu.VMEM((requests, ROWS, LANES), F32),
            pltpu.VMEM((kv_local, requests, LANES), F32),
            pltpu.VMEM((first, ROWS, LANES), F32),
            pltpu.VMEM((first, ROWS, LANES), F32),
            pltpu.SemaphoreType.DMA((9 + first,)),
        ],
        flops=4 * ROWS * columns * LANES * first,
        moved=2 * columns * LANES * first,
    )(
        pin(meta_far),
        pin(packed),
        pin(normed),
        pin(w_keyvalue.reshape(width * kv_local, LANES)),
        pin(tables_far),
        blocks,
    )
    (replies,) = call(
        functools.partial(lent_kernel, heads, kv_local, local_pages),
        [struct((inbox * SLOT, LANES), BF16)],
        [HBM, VMEM, HBM, HBM],
        [
            pltpu.SMEM(meta_shape, jnp.int32),
            pltpu.VMEM((outgoing, columns, LANES), BF16),
            pltpu.VMEM((inbox * SLOT, LANES), F32),
            pltpu.VMEM((inbox * SLOT, LANES), F32),
            pltpu.SemaphoreType.DMA((1 + outgoing,)),
        ],
        flops=4 * ROWS * columns * LANES * outgoing,
        moved=2 * columns * LANES * outgoing,
    )(pin(meta_far), asked, blocks, pin(tops))
    returned = exchange(replies)
    (state,) = call(
        functools.partial(second_kernel, heads, kv_local, first),
        [pltpu.HBM((requests, ROWS, LANES), F32)],
        [HBM] * 6 + [ANY],
        [
            pltpu.SMEM(meta_shape, jnp.int32),
            pltpu.VMEM((requests * SLOT, LANES), F32),
            pltpu.VMEM((kv_local, requests, LANES), F32),
            pltpu.VMEM((local_pages, ROWS, LANES), F32),
            pltpu.VMEM((local_pages, ROWS, LANES), F32),
            pltpu.VMEM((local_pages - first, columns, LANES), BF16),
            pltpu.VMEM((requests, ROWS, LANES), F32),
            pltpu.VMEM((requests * ROWS, LANES), F32),
            pltpu.VMEM((requests + 1, ROWS, LANES), F32),
            pltpu.VMEM((requests + 1, ROWS, LANES), F32),
            pltpu.VMEM((local_pages, ROWS, LANES), F32),
            pltpu.SemaphoreType.DMA((6 + local_pages - first,)),
        ],
        flops=4 * ROWS * columns * LANES * (local_pages - first),
        moved=2 * columns * LANES * (local_pages - first),
    )(pin(meta_far), pin(packed), pin(new), pin(tops), pin(sums), blocks, replies)
    (part,) = call(
        functools.partial(combine_kernel, heads, pool),
        [struct((requests, width), BF16)],
        [HBM] * 3 + [VMEM],
        [
            pltpu.SMEM(meta_shape, jnp.int32),
            pltpu.VMEM((requests, ROWS, LANES), F32),
            pltpu.VMEM(w_output.shape, BF16),
            pltpu.VMEM((requests + 1, ROWS, LANES), F32),
            pltpu.VMEM((requests + 1, ROWS, LANES), F32),
            pltpu.VMEM((inbox, ROWS, LANES), F32),
            pltpu.VMEM((inbox * SLOT, LANES), F32),
            pltpu.VMEM((requests * ROWS, LANES), F32),
            pltpu.SemaphoreType.DMA((6,)),
        ],
        flops=2 * requests * w_output.size,
        moved=2 * w_output.size,
    )(pin(meta_far), pin(state), pin(w_output), returned)
    if pair:
        parts = [part, swap(part)]
    else:
        parts = [lax.all_gather(part, "tensor", axis=0, tiled=True)]
    meta, hidden_all, gain, router_t, routes_t, wd = call(
        load_kernel,
        [
            struct(meta_shape, jnp.int32),
            struct((requests, width), BF16),
            struct((1, width), F32),
            struct(router.shape[::-1], BF16),
            struct(routes.shape[::-1], jnp.int32),
            struct(w_down.shape, BF16),
        ],
        [HBM] * 6 + [ANY],
        [pltpu.VMEM((width,), F32), pltpu.SemaphoreType.DMA((9,))],
        moved=2 * w_down.size,
    )(
        pin(meta_far), pin(hidden_far), pin(ffn_gain), pin(router.T), pin(routes.T),
        pin(w_down), part,
    )
    attended, ffn_input, spread = call(
        functools.partial(gate_kernel, tp, units, len(parts)),
        [
            struct((rows if pair else requests, width), BF16),
            struct((requests, width), BF16),
            struct((requests, LANES), F32),
        ],
        [VMEM] * (len(parts) + 5),
        flops=2 * requests * router.size,
        moved=2 * router.size,
    )(meta, hidden_all, *parts, gain, router_t, routes_t)
    lifted = jnp.einsum("rd,dsu->sru", ffn_input, w_in, preferred_element_type=F32)
    shapes = [struct((requests, width), BF16)]
    if pair:
        shapes = [struct((rows, width), F32), struct((rows, width), BF16)]
    shares = call(
        expert_kernel,
        shapes,
        [VMEM] * 4,
        flops=2 * requests * w_down.size,
        moved=2 * w_down.size,
    )(meta, lifted, spread, wd)
    if pair:
        return attended, (shares[0] + swap(shares[1]).astype(F32)).astype(BF16)
    shares = lax.all_gather(shares[0], "tensor", axis=0)
    mine = lax.dynamic_slice_in_dim(shares, rank * rows, rows, axis=1)
    experts_out = jnp.sum(mine.astype(F32), axis=0).astype(BF16)
    attended = lax.dynamic_slice_in_dim(attended, rank * rows, rows, axis=0)
    return attended, experts_out


def solution(mesh):
    placed = (
        P(("replica", "tensor"), None),
        P(),
        P(None, "tensor"),
        P(None, "tensor", None),
        P("tensor", None),
        P("replica", None, "tensor", None),
        P("replica", None),
        P("replica"),
        P("replica"),
        P(),
        P(),
        P("replica", None),
        P(None, None, "tensor"),
        P("tensor", None),
    )
    return jax.shard_map(
        on_device,
        mesh=mesh,
        in_specs=placed,
        out_specs=(P(("replica", "tensor"), None), P(("replica", "tensor"), None)),
        check_vma=False,
    )
```

```python
import functools
import math

import jax
import jax.numpy as jnp
from jax import lax
from jax.experimental import pallas as pl
from jax.experimental.pallas import tpu as pltpu
from jax.sharding import PartitionSpec as P

HEAD_DIM = 64
EXPERTS = 40
FF = 512
CAP = 2
LANES = 128
SLOT = 8
ROWS = 16
META = 6

ATTN_SCALE = 0.015625
RESID_SCALE = 0.22
ROPE_BASE = 10000.0
EPSILON = 1e-06
NEG_FILL = -1e30

F32 = jnp.float32
BF16 = jnp.bfloat16
VMEM = pl.BlockSpec(memory_space=pltpu.VMEM)
SMEM = pl.BlockSpec(memory_space=pltpu.SMEM)
ANY = pl.BlockSpec(memory_space=pl.ANY)
HBM = pl.BlockSpec(memory_space=pltpu.HBM)
NT = (((1,), (1,)), ((), ()))


def iota(shape, axis):
    return lax.broadcasted_iota(jnp.int32, shape, axis)


def norm_rows(values, gain):
    factor = lax.rsqrt(jnp.mean(values * values, axis=-1, keepdims=True) + EPSILON)
    return (values * factor * gain).astype(BF16)


def rope_tables(ctx_row, requests):
    diagonal = iota((requests, requests), 0) == iota((requests, requests), 1)
    ctx = jnp.broadcast_to(ctx_row.astype(F32), (requests, requests))
    ctx = jnp.sum(jnp.where(diagonal, ctx, 0.0), axis=1, keepdims=True)
    lane = iota((requests, LANES), 1)
    index = (lane % (HEAD_DIM // 2)).astype(F32)
    inverse = jnp.exp(index * (-2.0 * math.log(ROPE_BASE) / HEAD_DIM))
    angles = ctx * inverse
    sign = jnp.where(lane % HEAD_DIM < HEAD_DIM // 2, -1.0, 1.0)
    return jnp.cos(angles), jnp.sin(angles) * sign


def rotate(chunk, cosine, sine):
    lane = iota(chunk.shape, 1)
    ahead = pltpu.roll(chunk, LANES - HEAD_DIM // 2, 1)
    behind = pltpu.roll(chunk, HEAD_DIM // 2, 1)
    turned = jnp.where(lane % HEAD_DIM < HEAD_DIM // 2, ahead, behind)
    return chunk * cosine + turned * sine


def copy_of(source, target, sem):
    return pltpu.make_async_copy(source, target, sem)


def copies_of(source, target, sems, base):
    step = source.shape[0] // 4
    return [
        copy_of(
            source.at[pl.ds(i * step, step)], target.at[pl.ds(i * step, step)], sems.at[base + i]
        )
        for i in range(4)
    ]


def page_copies(cache_hbm, first, pages, place, count, sems, base):
    return [
        copy_of(cache_hbm.at[first + p], pages.at[place + p], sems.at[base + p])
        for p in range(count)
    ]


def prepare_kernel(
    pool, replicas, ids_ref, hidden_hbm, ctx_hbm, table_hbm, dest_hbm, attn_gain_hbm,
    wq_hbm, cache_hbm,
    hidden_ref, wq_ref, gain_ref, tables_ref, away_ref, span_ref, meta_ref, lent_ref,
    ctx, table, dest, gain, sems,
):
    inbox = replicas * CAP
    requests = ctx.shape[1]
    entries = meta_ref.shape[1]
    small = [
        copy_of(ctx_hbm, ctx, sems.at[0]),
        copy_of(table_hbm, table, sems.at[1]),
        copy_of(dest_hbm, dest, sems.at[2]),
        copy_of(attn_gain_hbm, gain, sems.at[3]),
    ]
    large = [copy_of(hidden_hbm, hidden_ref, sems.at[4])]
    large += copies_of(wq_hbm, wq_ref, sems, 5)
    lent = lent_ref.shape[0]
    large.append(copy_of(cache_hbm.at[pl.ds(pool - lent, lent)], lent_ref, sems.at[9]))
    for copy in small + large:
        copy.start()
    for copy in small:
        copy.wait()
    gain_ref[...] = gain[...].reshape(1, gain.shape[0])
    ctx_row = ctx[...]

    def claims(values):
        held = jnp.zeros(values.shape, F32)
        spans = jnp.zeros(values.shape, F32)
        for k in range(table.shape[0]):
            match = table[k : k + 1, :] == values
            filled = jnp.clip(ctx_row - k * 128, 0, 128).astype(F32)
            held = jnp.where(match, 1.0, held)
            spans = jnp.where(match, filled, spans)
        return held.astype(BF16), spans

    held, spans = claims(iota((entries, requests), 0))
    numbers = (iota((SLOT, requests), 1) + 1).astype(BF16)
    ones = jnp.ones((SLOT, requests), BF16)
    holder = lax.dot_general(numbers, held, NT, preferred_element_type=F32)
    covered = lax.dot_general(ones, spans.astype(BF16), NT, preferred_element_type=F32)
    meta_ref[0:1, :] = holder[0:1, :].astype(jnp.int32) - 1
    meta_ref[1:2, :] = covered[0:1, :].astype(jnp.int32)
    meta_ref[2:3, :] = jnp.zeros((1, entries), jnp.int32)
    meta_ref[2:3, 0 : dest.shape[1]] = dest[...]
    meta_ref[3:4, :] = jnp.full((1, entries), ids_ref[0], jnp.int32)
    cosine, sine = rope_tables(ctx_row, requests)
    tables_ref[0] = cosine
    tables_ref[1] = sine
    held, spans = claims(pool + iota((inbox, requests), 0))
    away_ref[...] = held
    away_span = jnp.sum(spans, axis=1, keepdims=True)
    span_ref[...] = jnp.broadcast_to(away_span, span_ref.shape)
    for copy in large:
        copy.wait()


def query_kernel(
    count, meta_ref, *refs,
):
    pieces = refs[:count]
    (gain_ref, wq_ref, tables_ref, away_ref, span_ref,
     hidden_ref, normed_ref, packed_ref, send_ref, packs, sends) = refs[count:]
    requests = hidden_ref.shape[0]
    inbox = span_ref.shape[0]
    width = wq_ref.shape[1]
    chunks = -(-width // LANES)
    if count == 1:
        hidden = pieces[0][...]
    else:
        own, other = pieces[0][...], pieces[1][...]
        first = meta_ref[3:4, 0:1] == 0
        hidden = jnp.concatenate(
            [jnp.where(first, own, other), jnp.where(first, other, own)], axis=0
        )
    hidden_ref[...] = hidden
    normed = norm_rows(hidden.astype(F32), gain_ref[...])
    normed_ref[...] = normed
    queries = jnp.dot(normed, wq_ref[...], preferred_element_type=F32)
    if chunks * LANES > width:
        pad = jnp.zeros((requests, chunks * LANES - width), F32)
        queries = jnp.concatenate([queries, pad], axis=1)
    cosine, sine = tables_ref[0], tables_ref[1]
    zeros = jnp.zeros((requests, LANES), F32)
    nothing = jnp.zeros((inbox, LANES), F32)
    for j in range(SLOT):
        here = pl.ds(j, requests, stride=SLOT)
        there = pl.ds(j, inbox, stride=SLOT)
        if j < chunks:
            chunk = rotate(queries[:, j * LANES : (j + 1) * LANES], cosine, sine)
            chunk = (chunk.astype(BF16).astype(F32) * ATTN_SCALE).astype(BF16)
            packs[here, :] = chunk.astype(F32)
            sends[there, :] = jnp.dot(away_ref[...], chunk, preferred_element_type=F32)
        else:
            packs[here, :] = zeros
            sends[there, :] = span_ref[...] if j == META else nothing
    packed_ref[...] = packs[...]
    send_ref[...] = sends[...].astype(BF16)


def unpack(packed):
    low = iota(packed.shape, 1) < HEAD_DIM
    even = jnp.where(low, packed, 0.0)
    odd = jnp.where(low, pltpu.roll(packed, HEAD_DIM, 1), 0.0)
    return jnp.concatenate([even, odd], axis=0)


def head_rows(heads):
    return [(h // 2) + SLOT * (h % 2) for h in range(heads)]


def token_of_column(heads, kv_local, columns):
    row = iota((ROWS, columns), 0)
    column = iota((ROWS, columns), 1)
    wanted = jnp.full((ROWS, columns), kv_local, jnp.int32)
    for h, place in enumerate(head_rows(heads)):
        wanted = jnp.where(row == place, h // (heads // kv_local), wanted)
    return jnp.where(column % kv_local == wanted, column // kv_local, 1 << 20)


def score_page(query, block):
    return lax.dot_general(query, block, NT, preferred_element_type=F32)


def weigh_page(scores, tokens, span):
    scores = jnp.where(tokens < span, scores, NEG_FILL)
    top = jnp.max(scores, axis=1, keepdims=True)
    weights = jnp.exp(scores - top)
    return top, jnp.sum(weights, axis=1, keepdims=True), weights.astype(BF16)


def attend_pages(count, stage, copies, query_of, block_of, span_of, tokens, keep):
    stages = [range(i, min(i + stage, count)) for i in range(0, count, stage)]

    def score_stage(pages):
        for p in pages:
            if copies is not None:
                copies[p].wait()
        return {p: score_page(query_of(p), block_of(p)) for p in pages}

    scores = score_stage(stages[0])
    for i, pages in enumerate(stages):
        if i + 1 < len(stages):
            ahead = score_stage(stages[i + 1])
        weighed = {p: weigh_page(scores[p], tokens, span_of(p)) for p in pages}
        outs = {
            p: jnp.dot(weighed[p][2], block_of(p), preferred_element_type=F32)
            for p in pages
        }
        for p in pages:
            keep(p, weighed[p][0], weighed[p][1], outs[p])
        if i + 1 < len(stages):
            scores = ahead


def spread_queries(target, packed):
    low = iota(packed.shape, 2) < HEAD_DIM
    target[:, 0:SLOT, :] = jnp.where(low, packed, 0.0)
    target[:, SLOT:ROWS, :] = jnp.where(low, pltpu.roll(packed, HEAD_DIM, 2), 0.0)


def merge_pages(places, top_of, sum_of, top, acc, scaled, start, before):
    requests = start.shape[0]
    for p, place in enumerate(places):
        top[place] = jnp.maximum(top[place], top_of(p))
    acc[0:requests] = start * jnp.exp(before - top[0:requests])
    for p, place in enumerate(places):
        scaled[p] = sum_of(p) * jnp.exp(top_of(p) - top[place])
    for p, place in enumerate(places):
        acc[place] = acc[place] + scaled[p]


def local_kernel(
    heads, kv_local, meta_hbm, packed_hbm, normed_hbm, wkv_hbm, tables_hbm, cache_hbm,
    state_hbm,
    meta, packed, normed, raw, wide, tables, pages, queries, fresh, tops, sums, top,
    acc, scaled, sems,
):
    requests, depth = normed.shape
    count, columns, _ = pages.shape
    small = [
        copy_of(meta_hbm, meta, sems.at[0]),
        copy_of(packed_hbm, packed, sems.at[1]),
        copy_of(normed_hbm, normed, sems.at[2]),
        copy_of(tables_hbm, tables, sems.at[3]),
    ]
    weights = copy_of(wkv_hbm, raw, sems.at[4])
    paging = page_copies(cache_hbm, 0, pages, 0, count, sems, 6)
    for copy in small + [weights] + paging:
        copy.start()
    for copy in small:
        copy.wait()
    spread_queries(queries, packed[...].reshape(requests, SLOT, LANES))
    tokens = token_of_column(heads, kv_local, columns)
    lower = iota((ROWS, LANES), 1) < HEAD_DIM
    low = iota((requests, LANES), 1) < HEAD_DIM
    cosine = jnp.where(low, tables[0], 1.0)
    sine = jnp.where(low, tables[1], 0.0)
    weights.wait()
    if kv_local > 1:
        wide[...] = raw[...].astype(F32)
    new = []
    for k in range(kv_local):
        if kv_local > 1:
            weight = wide[pl.ds(k, depth, stride=kv_local), :].astype(BF16)
        else:
            weight = raw[...]
        projected = jnp.dot(normed[...], weight, preferred_element_type=F32)
        new.append(rotate(projected, cosine, sine).astype(BF16).astype(F32))
    used = {place: h for h, place in enumerate(head_rows(heads))}
    for place in range(ROWS):
        value = jnp.zeros((requests, LANES), F32)
        if place in used:
            value = new[used[place] // (heads // kv_local)]
        fresh[pl.ds(place, requests, stride=ROWS), :] = value

    def keep(p, page_top, total, out):
        tops[p] = jnp.broadcast_to(page_top, (ROWS, LANES))
        sums[p] = jnp.where(lower, total, out)

    attend_pages(
        count,
        4,
        paging,
        lambda p: queries[jnp.maximum(meta[0, p], 0)].astype(BF16),
        lambda p: pages[p],
        lambda p: meta[1, p],
        tokens,
        keep,
    )
    added = fresh[...].reshape(requests, ROWS, LANES)
    low16 = iota(added.shape, 2) < HEAD_DIM
    score = jnp.sum(queries[...] * added, axis=2, keepdims=True)
    before = jnp.broadcast_to(score, added.shape)
    start = jnp.where(low16, 1.0, added)
    top[0:requests] = before

    def place_of(p):
        owner = meta[0, p]
        return jnp.where(owner < 0, requests, owner)

    merge_pages(
        [place_of(p) for p in range(count)],
        lambda p: tops[p],
        lambda p: sums[p],
        top,
        acc,
        scaled,
        start,
        before,
    )
    whole = acc[0:requests]
    acc[0:requests] = jnp.where(
        low16, top[0:requests] + jnp.log(whole), whole / pltpu.roll(whole, HEAD_DIM, 2)
    )
    parked = copy_of(acc.at[pl.ds(0, requests)], state_hbm, sems.at[5])
    parked.start()
    parked.wait()


def lent_kernel(
    heads, kv_local, meta, asked_ref, pages, meta_ref, packed_ref, normed_ref,
    tables_ref, hidden_ref,
    reply_hbm, meta_hbm, packed_hbm, normed_hbm, tables_hbm, hidden_hbm,
    asked, reply, reply16, sems,
):
    outgoing, columns, _ = pages.shape
    parked = [
        copy_of(packed_ref, packed_hbm, sems.at[0]),
        copy_of(normed_ref, normed_hbm, sems.at[1]),
        copy_of(hidden_ref, hidden_hbm, sems.at[2]),
        copy_of(tables_ref, tables_hbm, sems.at[3]),
        copy_of(meta_ref, meta_hbm, sems.at[4]),
    ]
    for copy in parked:
        copy.start()
    asked[...] = asked_ref[...].astype(F32)
    reply[...] = jnp.zeros(reply.shape, F32)
    tokens = token_of_column(heads, kv_local, columns).astype(F32)
    low = iota((SLOT, LANES), 1) < HEAD_DIM
    lane = iota((SLOT, LANES), 1)
    row = iota((SLOT, LANES), 0)

    def terms(total, offset):
        leading = total.astype(BF16).astype(F32)
        rest = total - leading
        second = rest.astype(BF16).astype(F32)
        third = rest - second
        spot = lane - offset - 3 * row
        placed = jnp.where(spot == 0, leading, 0.0)
        placed = jnp.where(spot == 1, second, placed)
        return jnp.where(spot == 2, third, placed)

    def rows_of(j):
        dest = meta[2, j]
        rank = jnp.int32(0)
        for e in range(j):
            rank = rank + (meta[2, e] == dest).astype(jnp.int32)
        return pl.ds(pl.multiple_of((dest * CAP + rank) * SLOT, SLOT), SLOT)

    places = [rows_of(j) for j in range(outgoing)]
    packed = [asked[rows, :] for rows in places]
    replies = {}

    def keep(j, top, total, out):
        out = out / total
        logs = top + jnp.log(total)
        even = pltpu.roll(out[0:SLOT], HEAD_DIM, 1)
        both = jnp.where(low, even, out[SLOT:ROWS])
        line = jnp.sum(
            terms(logs[0:SLOT], 0) + terms(logs[SLOT:ROWS], HEAD_DIM), axis=0, keepdims=True
        )
        replies[j] = jnp.where(row == META, line, both)

    attend_pages(
        outgoing,
        4,
        None,
        lambda j: unpack(packed[j]).astype(BF16),
        lambda j: pages[j],
        lambda j: packed[j][META : META + 1, 0:1],
        tokens,
        keep,
    )
    for j in range(outgoing):
        reply[places[j], :] = replies[j]
    reply16[...] = reply[...].astype(BF16)
    replying = copy_of(reply16, reply_hbm, sems.at[5])
    replying.start()
    for copy in parked + [replying]:
        copy.wait()


def combine_kernel(
    heads, pool, meta_hbm, state_hbm, wo_hbm, hidden_hbm, gain_hbm, router_hbm,
    routes_hbm, reply_ref,
    part_ref, meta_ref, hidden_ref, gain_ref, router_ref, routes_ref,
    meta, state, wo, gain, tops, accs, scaled, reply, finals, sems,
):
    requests = state.shape[0]
    inbox = reply_ref.shape[0] // SLOT
    chunks = -(-heads // 2)
    small = [
        copy_of(meta_hbm, meta, sems.at[0]),
        copy_of(state_hbm, state, sems.at[1]),
    ]
    weights = copies_of(wo_hbm, wo, sems, 2)
    gaining = copy_of(gain_hbm, gain, sems.at[6])
    later = [
        copy_of(meta_hbm, meta_ref, sems.at[7]),
        copy_of(hidden_hbm, hidden_ref, sems.at[8]),
        copy_of(router_hbm, router_ref, sems.at[9]),
        copy_of(routes_hbm, routes_ref, sems.at[10]),
    ]
    for copy in small + weights + [gaining] + later:
        copy.start()
    reply[...] = reply_ref[...].astype(F32)
    low = iota((SLOT, LANES), 1) < HEAD_DIM
    lane = iota((SLOT, LANES), 1)
    row = iota((SLOT, LANES), 0)
    mine = (lane % HEAD_DIM) // 3 == row

    def place_of(s):
        owner = meta[0, pool + s]
        return jnp.where(owner < 0, requests, owner)

    def logs_of(s):
        line = reply[s * SLOT + META : s * SLOT + META + 1, :]
        line = jnp.where(mine, jnp.broadcast_to(line, (SLOT, LANES)), 0.0)
        even = jnp.sum(jnp.where(low, line, 0.0), axis=1, keepdims=True)
        odd = jnp.sum(jnp.where(low, 0.0, line), axis=1, keepdims=True)
        logs = jnp.concatenate([even, odd], axis=0)
        return jnp.broadcast_to(logs, (ROWS, LANES))

    logs = [logs_of(s) for s in range(inbox)]
    for copy in small:
        copy.wait()
    low16 = iota(state.shape, 2) < HEAD_DIM
    start = state[...]
    before = jnp.where(low16, start, pltpu.roll(start, HEAD_DIM, 2))
    tops[0:requests] = before

    def sum_of(s):
        packed = reply[s * SLOT : (s + 1) * SLOT, :]
        even = jnp.where(low, 1.0, pltpu.roll(packed, HEAD_DIM, 1))
        odd = jnp.where(low, 1.0, packed)
        return jnp.concatenate([even, odd], axis=0)

    merge_pages(
        [place_of(s) for s in range(inbox)],
        lambda s: logs[s],
        sum_of,
        tops,
        accs,
        scaled,
        jnp.where(low16, 1.0, start),
        before,
    )
    whole = accs[0:requests]
    finals[...] = (whole / pltpu.roll(whole, HEAD_DIM, 2)).reshape(
        requests * ROWS, LANES
    )
    wide = iota((requests, LANES), 1) < HEAD_DIM
    parts = []
    for j in range(chunks):
        even = finals[pl.ds(j, requests, stride=ROWS), :]
        odd = finals[pl.ds(SLOT + j, requests, stride=ROWS), :]
        parts.append(jnp.where(wide, pltpu.roll(even, HEAD_DIM, 1), odd).astype(BF16))
    attention = jnp.concatenate(parts, axis=1)[:, : heads * HEAD_DIM]
    for copy in weights:
        copy.wait()
    part_ref[...] = jnp.dot(attention, wo[...], preferred_element_type=F32).astype(BF16)
    gaining.wait()
    gain_ref[...] = gain[...].reshape(1, gain.shape[0])
    for copy in later:
        copy.wait()


def load_kernel(wd_hbm, order_hbm, wd_ref, sems):
    del order_hbm
    copies = copies_of(wd_hbm, wd_ref, sems, 0)
    for copy in copies:
        copy.start()
    for copy in copies:
        copy.wait()


def finish_kernel(attended_ref, order_ref, out_ref):
    del order_ref
    out_ref[...] = attended_ref[...]


def own_rows(values, first):
    half = values.shape[0] // 2
    return jnp.where(first, values[:half], values[half:])


def gate_kernel(
    tp, units, count, meta_ref, hidden_ref, *refs,
):
    pieces = refs[:count]
    (gain_ref, router_ref, routes_ref, attended_ref, input_ref, spread_ref) = refs[count:]
    requests = hidden_ref.shape[0]
    if count == 2:
        summed = pieces[0][...].astype(F32) + pieces[1][...].astype(F32)
    else:
        summed = pieces[0][0:requests, :].astype(F32)
        for t in range(1, tp):
            part = pieces[0][t * requests : (t + 1) * requests, :]
            summed = summed + part.astype(F32)
    attended = (hidden_ref[...].astype(F32) + RESID_SCALE * summed).astype(BF16)
    if count == 2:
        attended_ref[...] = own_rows(attended, meta_ref[3:4, 0:1] == 0)
    else:
        attended_ref[...] = attended
    ffn_input = norm_rows(attended.astype(F32), gain_ref[...])
    input_ref[...] = ffn_input
    logits = lax.dot_general(router_ref[...], ffn_input, NT, preferred_element_type=F32)
    expert = iota(logits.shape, 0)
    named = jnp.zeros(logits.shape, F32)
    for k in range(routes_ref.shape[0]):
        named = jnp.where(routes_ref[k : k + 1, :] == expert, 1.0, named)
    chosen = named > 0.5
    top = jnp.max(jnp.where(chosen, logits, NEG_FILL), axis=0, keepdims=True)
    weights = jnp.where(chosen, jnp.exp(logits - top), 0.0)
    gates = weights / jnp.sum(weights, axis=0, keepdims=True)
    mine = expert == meta_ref[3:4, 0:1] * units // FF
    line = jnp.sum(jnp.where(mine, gates, 0.0), axis=0, keepdims=True)
    diagonal = iota((requests, requests), 0) == iota((requests, requests), 1)
    line = jnp.where(diagonal, jnp.broadcast_to(line, (requests, requests)), 0.0)
    column = jnp.sum(line, axis=1, keepdims=True)
    spread_ref[...] = jnp.broadcast_to(column, spread_ref.shape)


def expert_kernel(meta_ref, lifted_ref, spread_ref, wd_ref, *outs):
    gate = lifted_ref[0]
    active = gate / (1.0 + jnp.exp(-gate)) * lifted_ref[1] * spread_ref[:, 0:1]
    share = jnp.dot(active.astype(BF16), wd_ref[...], preferred_element_type=F32)
    if len(outs) == 2:
        first = meta_ref[3:4, 0:1] == 0
        outs[0][...] = own_rows(share, first)
        outs[1][...] = own_rows(share, jnp.logical_not(first)).astype(BF16)
    else:
        outs[0][...] = share.astype(BF16)


def call(body, outs, in_specs, scratch=(), limit=16, flops=0, moved=0):
    return pl.pallas_call(
        body,
        out_shape=outs,
        in_specs=in_specs,
        out_specs=[VMEM if isinstance(o, jax.ShapeDtypeStruct) else HBM for o in outs],
        scratch_shapes=list(scratch),
        compiler_params=pltpu.CompilerParams(vmem_limit_bytes=limit << 20),
        cost_estimate=pl.CostEstimate(
            flops=flops, bytes_accessed=moved, transcendentals=0
        ),
    )


def swap(values):
    return lax.ppermute(values, "tensor", [(0, 1), (1, 0)])


def on_device(
    hidden,
    attn_gain,
    w_query,
    w_keyvalue,
    w_output,
    cache,
    page_table,
    ctx_len,
    move_dest,
    ffn_gain,
    router,
    routes,
    w_in,
    w_down,
):
    replicas = lax.axis_size("replica")
    tp = lax.axis_size("tensor")
    rank = lax.axis_index("tensor").astype(jnp.int32)
    rows, width = hidden.shape
    pool, page_len, kv_local, _ = cache.shape
    outgoing = move_dest.shape[0]
    local_pages = pool - outgoing
    requests = page_table.shape[0]
    heads = w_query.shape[1] // HEAD_DIM
    inbox = replicas * CAP
    units = w_down.shape[0]
    assert FF % units == 0
    columns = page_len * kv_local
    entries = -(-(pool + inbox) // LANES) * LANES
    struct = jax.ShapeDtypeStruct
    pair = tp == 2
    ids = rank.reshape(1)

    def pin(values):
        return pltpu.with_memory_space_constraint(values, pltpu.HBM)

    def exchange(blocks):
        blocks = blocks.reshape(replicas, CAP * SLOT, LANES)
        blocks = lax.all_to_all(blocks, "replica", split_axis=0, concat_axis=0, tiled=True)
        return blocks.reshape(inbox * SLOT, LANES)

    blocks = pin(cache.reshape(pool, columns, LANES))
    if pair:
        pieces = [hidden, swap(hidden)]
    else:
        pieces = [lax.all_gather(hidden, "tensor", axis=0, tiled=True)]
    meta_shape = (4, entries)
    tables_shape = (2, requests, LANES)
    own, wq, gain, tables, away, away_span, meta, lent = call(
        functools.partial(prepare_kernel, pool, replicas),
        [
            struct(hidden.shape, BF16),
            struct(w_query.shape, BF16),
            struct((1, width), F32),
            struct(tables_shape, F32),
            struct((inbox, requests), BF16),
            struct((inbox, LANES), F32),
            struct(meta_shape, jnp.int32),
            struct((outgoing, columns, LANES), BF16),
        ],
        [SMEM] + [HBM] * 7,
        [
            pltpu.VMEM((1, requests), jnp.int32),
            pltpu.VMEM((page_table.shape[1], requests), jnp.int32),
            pltpu.VMEM((1, outgoing), jnp.int32),
            pltpu.VMEM((width,), F32),
            pltpu.SemaphoreType.DMA((10,)),
        ],
        moved=2 * w_query.size,
    )(
        ids,
        pin(hidden),
        pin(ctx_len.reshape(1, requests)),
        pin(page_table.T),
        pin(move_dest.reshape(1, outgoing)),
        pin(attn_gain),
        pin(w_query),
        blocks,
    )
    if pair:
        pieces[0] = own
    hidden_all, normed, packed, sends = call(
        functools.partial(query_kernel, len(pieces)),
        [
            struct((requests, width), BF16),
            struct((requests, width), BF16),
            struct((requests * SLOT, LANES), F32),
            struct((inbox * SLOT, LANES), BF16),
        ],
        [VMEM] * (len(pieces) + 6),
        [
            pltpu.VMEM((requests * SLOT, LANES), F32),
            pltpu.VMEM((inbox * SLOT, LANES), F32),
        ],
        flops=4 * requests * width * w_query.shape[1],
        moved=2 * w_query.size,
    )(meta, *pieces, gain, wq, tables, away, away_span)
    asked = exchange(sends)
    replies, meta_far, packed_far, normed_far, tables_far, hidden_far = call(
        functools.partial(lent_kernel, heads, kv_local),
        [
            pltpu.HBM((inbox * SLOT, LANES), BF16),
            pltpu.HBM(meta_shape, jnp.int32),
            pltpu.HBM((requests * SLOT, LANES), F32),
            pltpu.HBM((requests, width), BF16),
            pltpu.HBM(tables_shape, F32),
            pltpu.HBM((requests, width), BF16),
        ],
        [SMEM] + [VMEM] * 7,
        [
            pltpu.VMEM((inbox * SLOT, LANES), F32),
            pltpu.VMEM((inbox * SLOT, LANES), F32),
            pltpu.VMEM((inbox * SLOT, LANES), BF16),
            pltpu.SemaphoreType.DMA((6,)),
        ],
        flops=4 * ROWS * columns * LANES * outgoing,
        moved=2 * columns * LANES * outgoing,
    )(meta, asked, lent, meta, packed, normed, tables, hidden_all)
    returned = exchange(replies)
    (state,) = call(
        functools.partial(local_kernel, heads, kv_local),
        [pltpu.HBM((requests, ROWS, LANES), F32)],
        [HBM] * 6,
        [
            pltpu.SMEM(meta_shape, jnp.int32),
            pltpu.VMEM((requests * SLOT, LANES), F32),
            pltpu.VMEM((requests, width), BF16),
            pltpu.VMEM((width * kv_local, LANES), BF16),
            pltpu.VMEM((width * kv_local, LANES), F32),
            pltpu.VMEM(tables_shape, F32),
            pltpu.VMEM((local_pages, columns, LANES), BF16),
            pltpu.VMEM((requests, ROWS, LANES), F32),
            pltpu.VMEM((requests * ROWS, LANES), F32),
            pltpu.VMEM((local_pages, ROWS, LANES), F32),
            pltpu.VMEM((local_pages, ROWS, LANES), F32),
            pltpu.VMEM((requests + 1, ROWS, LANES), F32),
            pltpu.VMEM((requests + 1, ROWS, LANES), F32),
            pltpu.VMEM((local_pages, ROWS, LANES), F32),
            pltpu.SemaphoreType.DMA((6 + local_pages,)),
        ],
        limit=24,
        flops=4 * ROWS * columns * LANES * local_pages,
        moved=2 * columns * LANES * local_pages,
    )(
        pin(meta_far),
        pin(packed_far),
        pin(normed_far),
        pin(w_keyvalue.reshape(width * kv_local, LANES)),
        pin(tables_far),
        blocks,
    )
    part, meta, hidden_all, gain, router_t, routes_t = call(
        functools.partial(combine_kernel, heads, pool),
        [
            struct((requests, width), BF16),
            struct(meta_shape, jnp.int32),
            struct((requests, width), BF16),
            struct((1, width), F32),
            struct(router.shape[::-1], BF16),
            struct(routes.shape[::-1], jnp.int32),
        ],
        [HBM] * 7 + [VMEM],
        [
            pltpu.SMEM(meta_shape, jnp.int32),
            pltpu.VMEM((requests, ROWS, LANES), F32),
            pltpu.VMEM(w_output.shape, BF16),
            pltpu.VMEM((width,), F32),
            pltpu.VMEM((requests + 1, ROWS, LANES), F32),
            pltpu.VMEM((requests + 1, ROWS, LANES), F32),
            pltpu.VMEM((inbox, ROWS, LANES), F32),
            pltpu.VMEM((inbox * SLOT, LANES), F32),
            pltpu.VMEM((requests * ROWS, LANES), F32),
            pltpu.SemaphoreType.DMA((11,)),
        ],
        flops=2 * requests * w_output.size,
        moved=2 * w_output.size,
    )(
        pin(meta_far), pin(state), pin(w_output), pin(hidden_far), pin(ffn_gain),
        pin(router.T), pin(routes.T), returned,
    )
    if pair:
        parts = [part, swap(part)]
    else:
        parts = [lax.all_gather(part, "tensor", axis=0, tiled=True)]
    (wd,) = call(
        load_kernel,
        [struct(w_down.shape, BF16)],
        [HBM, ANY],
        [pltpu.SemaphoreType.DMA((4,))],
        moved=2 * w_down.size,
    )(pin(w_down), part)
    attended, ffn_input, spread = call(
        functools.partial(gate_kernel, tp, units, len(parts)),
        [
            struct((rows if pair else requests, width), BF16),
            struct((requests, width), BF16),
            struct((requests, LANES), F32),
        ],
        [VMEM] * (len(parts) + 5),
        flops=2 * requests * router.size,
        moved=2 * router.size,
    )(meta, hidden_all, *parts, gain, router_t, routes_t)
    lifted = jnp.einsum("rd,dsu->sru", ffn_input, w_in, preferred_element_type=F32)
    shapes = [struct((requests, width), BF16)]
    if pair:
        shapes = [struct((rows, width), F32), struct((rows, width), BF16)]
    shares = call(
        expert_kernel,
        shapes,
        [VMEM] * 4,
        flops=2 * requests * w_down.size,
        moved=2 * w_down.size,
    )(meta, lifted, spread, wd)
    if pair:
        (attended,) = call(
            finish_kernel, [struct((rows, width), BF16)], [VMEM, ANY], moved=4 * attended.size
        )(attended, shares[1])
        return attended, (shares[0] + swap(shares[1]).astype(F32)).astype(BF16)
    shares = lax.all_gather(shares[0], "tensor", axis=0)
    mine = lax.dynamic_slice_in_dim(shares, rank * rows, rows, axis=1)
    experts_out = jnp.sum(mine.astype(F32), axis=0).astype(BF16)
    attended = lax.dynamic_slice_in_dim(attended, rank * rows, rows, axis=0)
    return attended, experts_out


def solution(mesh):
    placed = (
        P(("replica", "tensor"), None),
        P(),
        P(None, "tensor"),
        P(None, "tensor", None),
        P("tensor", None),
        P("replica", None, "tensor", None),
        P("replica", None),
        P("replica"),
        P("replica"),
        P(),
        P(),
        P("replica", None),
        P(None, None, "tensor"),
        P("tensor", None),
    )
    return jax.shard_map(
        on_device,
        mesh=mesh,
        in_specs=placed,
        out_specs=(P(("replica", "tensor"), None), P(("replica", "tensor"), None)),
        check_vma=False,
    )
```

```python
import functools
import math

import jax
import jax.numpy as jnp
from jax import lax
from jax.experimental import pallas as pl
from jax.experimental.pallas import tpu as pltpu
from jax.sharding import PartitionSpec as P

HEAD_DIM = 64
EXPERTS = 40
FF = 512
CAP = 2
LANES = 128
SLOT = 8
ROWS = 16
META = 6

ATTN_SCALE = 0.015625
RESID_SCALE = 0.22
ROPE_BASE = 10000.0
EPSILON = 1e-06
NEG_FILL = -1e30

F32 = jnp.float32
BF16 = jnp.bfloat16
VMEM = pl.BlockSpec(memory_space=pltpu.VMEM)
SMEM = pl.BlockSpec(memory_space=pltpu.SMEM)
ANY = pl.BlockSpec(memory_space=pl.ANY)
HBM = pl.BlockSpec(memory_space=pltpu.HBM)
NT = (((1,), (1,)), ((), ()))


def iota(shape, axis):
    return lax.broadcasted_iota(jnp.int32, shape, axis)


def norm_rows(values, gain):
    factor = lax.rsqrt(jnp.mean(values * values, axis=-1, keepdims=True) + EPSILON)
    return (values * factor * gain).astype(BF16)


def rope_tables(ctx_row, requests):
    diagonal = iota((requests, requests), 0) == iota((requests, requests), 1)
    ctx = jnp.broadcast_to(ctx_row.astype(F32), (requests, requests))
    ctx = jnp.sum(jnp.where(diagonal, ctx, 0.0), axis=1, keepdims=True)
    lane = iota((requests, LANES), 1)
    index = (lane % (HEAD_DIM // 2)).astype(F32)
    inverse = jnp.exp(index * (-2.0 * math.log(ROPE_BASE) / HEAD_DIM))
    angles = ctx * inverse
    sign = jnp.where(lane % HEAD_DIM < HEAD_DIM // 2, -1.0, 1.0)
    return jnp.cos(angles), jnp.sin(angles) * sign


def rotate(chunk, cosine, sine):
    lane = iota(chunk.shape, 1)
    ahead = pltpu.roll(chunk, LANES - HEAD_DIM // 2, 1)
    behind = pltpu.roll(chunk, HEAD_DIM // 2, 1)
    turned = jnp.where(lane % HEAD_DIM < HEAD_DIM // 2, ahead, behind)
    return chunk * cosine + turned * sine


def copy_of(source, target, sem):
    return pltpu.make_async_copy(source, target, sem)


def copies_of(source, target, sems, base):
    step = source.shape[0] // 4
    return [
        copy_of(
            source.at[pl.ds(i * step, step)], target.at[pl.ds(i * step, step)], sems.at[base + i]
        )
        for i in range(4)
    ]


def page_copies(cache_hbm, first, pages, place, count, sems, base):
    return [
        copy_of(cache_hbm.at[first + p], pages.at[place + p], sems.at[base + p])
        for p in range(count)
    ]


def prepare_kernel(
    pool, replicas, ids_ref, hidden_hbm, ctx_hbm, table_hbm, dest_hbm, attn_gain_hbm,
    wq_hbm,
    hidden_ref, wq_ref, gain_ref, tables_ref, away_ref, span_ref, meta_ref,
    ctx, table, dest, gain, sems,
):
    inbox = replicas * CAP
    requests = ctx.shape[1]
    entries = meta_ref.shape[1]
    small = [
        copy_of(ctx_hbm, ctx, sems.at[0]),
        copy_of(table_hbm, table, sems.at[1]),
        copy_of(dest_hbm, dest, sems.at[2]),
        copy_of(attn_gain_hbm, gain, sems.at[3]),
    ]
    large = [copy_of(hidden_hbm, hidden_ref, sems.at[4])]
    large += copies_of(wq_hbm, wq_ref, sems, 5)
    for copy in small + large:
        copy.start()
    for copy in small:
        copy.wait()
    gain_ref[...] = gain[...].reshape(1, gain.shape[0])
    ctx_row = ctx[...]

    def claims(values):
        held = jnp.zeros(values.shape, F32)
        spans = jnp.zeros(values.shape, F32)
        for k in range(table.shape[0]):
            match = table[k : k + 1, :] == values
            filled = jnp.clip(ctx_row - k * 128, 0, 128).astype(F32)
            held = jnp.where(match, 1.0, held)
            spans = jnp.where(match, filled, spans)
        return held.astype(BF16), spans

    held, spans = claims(iota((entries, requests), 0))
    numbers = (iota((SLOT, requests), 1) + 1).astype(BF16)
    ones = jnp.ones((SLOT, requests), BF16)
    holder = lax.dot_general(numbers, held, NT, preferred_element_type=F32)
    covered = lax.dot_general(ones, spans.astype(BF16), NT, preferred_element_type=F32)
    meta_ref[0:1, :] = holder[0:1, :].astype(jnp.int32) - 1
    meta_ref[1:2, :] = covered[0:1, :].astype(jnp.int32)
    meta_ref[2:3, :] = jnp.zeros((1, entries), jnp.int32)
    lent = dest.shape[1]
    across = jnp.broadcast_to(dest[...].astype(F32), (lent, lent))
    row, lane = iota((lent, lent), 0), iota((lent, lent), 1)
    down = jnp.sum(jnp.where(row == lane, across, 0.0), axis=1, keepdims=True)
    same = jnp.where((across == down) & (row < lane), 1.0, 0.0)
    rank = jnp.sum(same, axis=0, keepdims=True)
    slots = dest[...] * CAP + rank.astype(jnp.int32)
    meta_ref[2:3, 0:lent] = slots
    meta_ref[3:4, :] = jnp.full((1, entries), ids_ref[0], jnp.int32)
    cosine, sine = rope_tables(ctx_row, requests)
    tables_ref[0] = cosine
    tables_ref[1] = sine
    held, spans = claims(pool + iota((inbox, requests), 0))
    away_ref[...] = held
    away_span = jnp.sum(spans, axis=1, keepdims=True)
    span_ref[...] = jnp.broadcast_to(away_span, span_ref.shape)
    for copy in large:
        copy.wait()


def query_kernel(
    count, local_pages, meta_ref, *refs,
):
    pieces = refs[:count]
    (gain_ref, wq_ref, tables_ref, away_ref, span_ref, cache_hbm,
     hidden_ref, normed_ref, packed_ref, send_ref, lent_ref, packs, sends, sems) = refs[count:]
    requests = hidden_ref.shape[0]
    lending = page_copies(cache_hbm, local_pages, lent_ref, 0, lent_ref.shape[0], sems, 0)
    for copy in lending:
        copy.start()
    inbox = span_ref.shape[0]
    width = wq_ref.shape[1]
    chunks = -(-width // LANES)
    if count == 1:
        hidden = pieces[0][...]
    else:
        own, other = pieces[0][...], pieces[1][...]
        first = meta_ref[3:4, 0:1] == 0
        hidden = jnp.concatenate(
            [jnp.where(first, own, other), jnp.where(first, other, own)], axis=0
        )
    hidden_ref[...] = hidden
    normed = norm_rows(hidden.astype(F32), gain_ref[...])
    normed_ref[...] = normed
    queries = jnp.dot(normed, wq_ref[...], preferred_element_type=F32)
    if chunks * LANES > width:
        pad = jnp.zeros((requests, chunks * LANES - width), F32)
        queries = jnp.concatenate([queries, pad], axis=1)
    cosine, sine = tables_ref[0], tables_ref[1]
    zeros = jnp.zeros((requests, LANES), F32)
    nothing = jnp.zeros((inbox, LANES), F32)
    for j in range(SLOT):
        here = pl.ds(j, requests, stride=SLOT)
        there = pl.ds(j, inbox, stride=SLOT)
        if j < chunks:
            chunk = rotate(queries[:, j * LANES : (j + 1) * LANES], cosine, sine)
            chunk = (chunk.astype(BF16).astype(F32) * ATTN_SCALE).astype(BF16)
            packs[here, :] = chunk.astype(F32)
            sends[there, :] = jnp.dot(away_ref[...], chunk, preferred_element_type=F32)
        else:
            packs[here, :] = zeros
            sends[there, :] = span_ref[...] if j == META else nothing
    packed_ref[...] = packs[...]
    send_ref[...] = sends[...].astype(BF16)
    for copy in lending:
        copy.wait()


def unpack(packed):
    low = iota(packed.shape, 1) < HEAD_DIM
    even = jnp.where(low, packed, 0.0)
    odd = jnp.where(low, pltpu.roll(packed, HEAD_DIM, 1), 0.0)
    return jnp.concatenate([even, odd], axis=0)


def head_rows(heads):
    return [(h // 2) + SLOT * (h % 2) for h in range(heads)]


def token_of_column(heads, kv_local, columns):
    row = iota((ROWS, columns), 0)
    column = iota((ROWS, columns), 1)
    wanted = jnp.full((ROWS, columns), kv_local, jnp.int32)
    for h, place in enumerate(head_rows(heads)):
        wanted = jnp.where(row == place, h // (heads // kv_local), wanted)
    return jnp.where(column % kv_local == wanted, column // kv_local, 1 << 20)


def score_page(query, block):
    return lax.dot_general(query, block, NT, preferred_element_type=F32)


def weigh_page(scores, tokens, span):
    scores = jnp.where(tokens < span, scores, NEG_FILL)
    top = jnp.max(scores, axis=1, keepdims=True)
    weights = jnp.exp(scores - top)
    return top, jnp.sum(weights, axis=1, keepdims=True), weights.astype(BF16)


def attend_pages(count, stage, copies, query_of, block_of, span_of, tokens, keep):
    stages = [range(i, min(i + stage, count)) for i in range(0, count, stage)]

    def score_stage(pages):
        for p in pages:
            if copies is not None:
                copies[p].wait()
        return {p: score_page(query_of(p), block_of(p)) for p in pages}

    scores = score_stage(stages[0])
    for i, pages in enumerate(stages):
        if i + 1 < len(stages):
            ahead = score_stage(stages[i + 1])
        weighed = {p: weigh_page(scores[p], tokens, span_of(p)) for p in pages}
        outs = {
            p: jnp.dot(weighed[p][2], block_of(p), preferred_element_type=F32)
            for p in pages
        }
        for p in pages:
            keep(p, weighed[p][0], weighed[p][1], outs[p])
        if i + 1 < len(stages):
            scores = ahead


def spread_queries(target, packed):
    low = iota(packed.shape, 2) < HEAD_DIM
    target[:, 0:SLOT, :] = jnp.where(low, packed, 0.0)
    target[:, SLOT:ROWS, :] = jnp.where(low, pltpu.roll(packed, HEAD_DIM, 2), 0.0)


def merge_pages(places, top_of, sum_of, top, acc, scaled, start_of):
    for p, place in enumerate(places):
        top[place] = jnp.maximum(top[place], top_of(p))
    start_of()
    for p, place in enumerate(places):
        scaled[p] = sum_of(p) * jnp.exp(top_of(p) - top[place])
    for p, place in enumerate(places):
        acc[place] = acc[place] + scaled[p]


def local_kernel(
    heads, kv_local, meta_hbm, packed_hbm, normed_hbm, wkv_hbm, tables_hbm, cache_hbm,
    top_hbm, acc_hbm,
    meta, packed, normed, raw, wide, tables, pages, queries, fresh, tops, sums, top,
    acc, scaled, sems,
):
    requests, depth = normed.shape
    count, columns, _ = pages.shape
    small = [
        copy_of(meta_hbm, meta, sems.at[0]),
        copy_of(packed_hbm, packed, sems.at[1]),
        copy_of(normed_hbm, normed, sems.at[2]),
        copy_of(tables_hbm, tables, sems.at[3]),
    ]
    weights = copy_of(wkv_hbm, raw, sems.at[4])
    paging = page_copies(cache_hbm, 0, pages, 0, count, sems, 6)
    for copy in small + [weights] + paging:
        copy.start()
    for copy in small:
        copy.wait()
    spread_queries(queries, packed[...].reshape(requests, SLOT, LANES))
    tokens = token_of_column(heads, kv_local, columns)
    lower = iota((ROWS, LANES), 1) < HEAD_DIM
    low = iota((requests, LANES), 1) < HEAD_DIM
    cosine = jnp.where(low, tables[0], 1.0)
    sine = jnp.where(low, tables[1], 0.0)
    weights.wait()
    if kv_local > 1:
        wide[...] = raw[...].astype(F32)
    new = []
    for k in range(kv_local):
        if kv_local > 1:
            weight = wide[pl.ds(k, depth, stride=kv_local), :].astype(BF16)
        else:
            weight = raw[...]
        projected = jnp.dot(normed[...], weight, preferred_element_type=F32)
        new.append(rotate(projected, cosine, sine).astype(BF16).astype(F32))
    used = {place: h for h, place in enumerate(head_rows(heads))}
    for place in range(ROWS):
        value = jnp.zeros((requests, LANES), F32)
        if place in used:
            value = new[used[place] // (heads // kv_local)]
        fresh[pl.ds(place, requests, stride=ROWS), :] = value

    def keep(p, page_top, total, out):
        tops[p] = jnp.broadcast_to(page_top, (ROWS, LANES))
        sums[p] = jnp.where(lower, total, out)

    attend_pages(
        count,
        4,
        paging,
        lambda p: queries[jnp.maximum(meta[0, p], 0)].astype(BF16),
        lambda p: pages[p],
        lambda p: meta[1, p],
        tokens,
        keep,
    )
    added = fresh[...].reshape(requests, ROWS, LANES)
    low16 = iota(added.shape, 2) < HEAD_DIM
    score = jnp.sum(queries[...] * added, axis=2, keepdims=True)
    before = jnp.broadcast_to(score, added.shape)
    start = jnp.where(low16, 1.0, added)
    top[0:requests] = before

    def start_of():
        acc[0:requests] = start * jnp.exp(before - top[0:requests])

    def place_of(p):
        owner = meta[0, p]
        return jnp.where(owner < 0, requests, owner)

    merge_pages(
        [place_of(p) for p in range(count)],
        lambda p: tops[p],
        lambda p: sums[p],
        top,
        acc,
        scaled,
        start_of,
    )
    whole = pl.ds(0, requests)
    parked = [
        copy_of(top.at[whole], top_hbm, sems.at[5]),
        copy_of(acc.at[whole], acc_hbm, sems.at[6 + count]),
    ]
    for copy in parked:
        copy.start()
    for copy in parked:
        copy.wait()


def lent_kernel(
    heads, kv_local, meta, asked_ref, pages, meta_ref, packed_ref, normed_ref,
    tables_ref, hidden_ref,
    reply_hbm, meta_hbm, packed_hbm, normed_hbm, tables_hbm, hidden_hbm,
    reply, reply16, sems,
):
    outgoing, columns, _ = pages.shape
    parked = [
        copy_of(packed_ref, packed_hbm, sems.at[0]),
        copy_of(normed_ref, normed_hbm, sems.at[1]),
        copy_of(hidden_ref, hidden_hbm, sems.at[2]),
        copy_of(tables_ref, tables_hbm, sems.at[3]),
        copy_of(meta_ref, meta_hbm, sems.at[4]),
    ]
    for copy in parked:
        copy.start()
    reply[...] = jnp.zeros(reply.shape, F32)
    tokens = token_of_column(heads, kv_local, columns).astype(F32)
    low = iota((SLOT, LANES), 1) < HEAD_DIM
    lane = iota((SLOT, LANES), 1)
    row = iota((SLOT, LANES), 0)

    def terms(total, offset):
        leading = total.astype(BF16).astype(F32)
        rest = total - leading
        second = rest.astype(BF16).astype(F32)
        third = rest - second
        spot = lane - offset - 3 * row
        placed = jnp.where(spot == 0, leading, 0.0)
        placed = jnp.where(spot == 1, second, placed)
        return jnp.where(spot == 2, third, placed)

    slots = [meta[2, j] for j in range(outgoing)]

    def asked_of(slot):
        rows = pl.ds(pl.multiple_of((slot // CAP) * CAP * SLOT, CAP * SLOT), CAP * SLOT)
        both = asked_ref[rows, :].astype(F32)
        return jnp.where(slot % CAP == 0, both[:SLOT], both[SLOT:])

    packed = [asked_of(slot) for slot in slots]
    replies = {}

    def keep(j, top, total, out):
        out = out / total
        logs = top + jnp.log(total)
        even = pltpu.roll(out[0:SLOT], HEAD_DIM, 1)
        both = jnp.where(low, even, out[SLOT:ROWS])
        line = jnp.sum(
            terms(logs[0:SLOT], 0) + terms(logs[SLOT:ROWS], HEAD_DIM), axis=0, keepdims=True
        )
        replies[j] = jnp.where(row == META, line, both)

    attend_pages(
        outgoing,
        8,
        None,
        lambda j: unpack(packed[j]).astype(BF16),
        lambda j: pages[j],
        lambda j: packed[j][META : META + 1, 0:1],
        tokens,
        keep,
    )
    for j in range(outgoing):
        reply[pl.ds(pl.multiple_of(slots[j] * SLOT, SLOT), SLOT), :] = replies[j]
    reply16[...] = reply[...].astype(BF16)
    replying = copy_of(reply16, reply_hbm, sems.at[5])
    replying.start()
    for copy in parked + [replying]:
        copy.wait()


def combine_kernel(
    heads, pool, meta_hbm, top_hbm, acc_hbm, wo_hbm, hidden_hbm, gain_hbm, router_hbm,
    routes_hbm, reply_ref,
    part_ref, meta_ref, hidden_ref, gain_ref, router_ref, routes_ref,
    meta, wo, gain, before, tops, accs, scaled, reply, finals, sems,
):
    requests = before.shape[0]
    whole = pl.ds(0, requests)
    inbox = reply_ref.shape[0] // SLOT
    chunks = -(-heads // 2)
    small = [
        copy_of(meta_hbm, meta, sems.at[0]),
        copy_of(top_hbm, before, sems.at[1]),
        copy_of(top_hbm, tops.at[whole], sems.at[11]),
        copy_of(acc_hbm, accs.at[whole], sems.at[12]),
    ]
    weights = copies_of(wo_hbm, wo, sems, 2)
    gaining = copy_of(gain_hbm, gain, sems.at[6])
    later = [
        copy_of(meta_hbm, meta_ref, sems.at[7]),
        copy_of(hidden_hbm, hidden_ref, sems.at[8]),
        copy_of(router_hbm, router_ref, sems.at[9]),
        copy_of(routes_hbm, routes_ref, sems.at[10]),
    ]
    for copy in small + weights + [gaining] + later:
        copy.start()
    reply[...] = reply_ref[...].astype(F32)
    low = iota((SLOT, LANES), 1) < HEAD_DIM
    lane = iota((SLOT, LANES), 1)
    row = iota((SLOT, LANES), 0)
    mine = (lane % HEAD_DIM) // 3 == row

    def place_of(s):
        owner = meta[0, pool + s]
        return jnp.where(owner < 0, requests, owner)

    def logs_of(s):
        line = reply[s * SLOT + META : s * SLOT + META + 1, :]
        line = jnp.where(mine, jnp.broadcast_to(line, (SLOT, LANES)), 0.0)
        even = jnp.sum(jnp.where(low, line, 0.0), axis=1, keepdims=True)
        odd = jnp.sum(jnp.where(low, 0.0, line), axis=1, keepdims=True)
        logs = jnp.concatenate([even, odd], axis=0)
        return jnp.broadcast_to(logs, (ROWS, LANES))

    logs = [logs_of(s) for s in range(inbox)]
    for copy in small:
        copy.wait()

    def start_of():
        accs[0:requests] = accs[0:requests] * jnp.exp(before[...] - tops[0:requests])

    def sum_of(s):
        packed = reply[s * SLOT : (s + 1) * SLOT, :]
        even = jnp.where(low, 1.0, pltpu.roll(packed, HEAD_DIM, 1))
        odd = jnp.where(low, 1.0, packed)
        return jnp.concatenate([even, odd], axis=0)

    merge_pages(
        [place_of(s) for s in range(inbox)],
        lambda s: logs[s],
        sum_of,
        tops,
        accs,
        scaled,
        start_of,
    )
    merged = accs[0:requests]
    finals[...] = (merged / pltpu.roll(merged, HEAD_DIM, 2)).reshape(
        requests * ROWS, LANES
    )
    wide = iota((requests, LANES), 1) < HEAD_DIM
    parts = []
    for j in range(chunks):
        even = finals[pl.ds(j, requests, stride=ROWS), :]
        odd = finals[pl.ds(SLOT + j, requests, stride=ROWS), :]
        parts.append(jnp.where(wide, pltpu.roll(even, HEAD_DIM, 1), odd).astype(BF16))
    attention = jnp.concatenate(parts, axis=1)[:, : heads * HEAD_DIM]
    for copy in weights:
        copy.wait()
    part_ref[...] = jnp.dot(attention, wo[...], preferred_element_type=F32).astype(BF16)
    gaining.wait()
    gain_ref[...] = gain[...].reshape(1, gain.shape[0])
    for copy in later:
        copy.wait()


def load_kernel(wd_hbm, order_hbm, wd_ref, sems):
    del order_hbm
    copies = copies_of(wd_hbm, wd_ref, sems, 0)
    for copy in copies:
        copy.start()
    for copy in copies:
        copy.wait()


def finish_kernel(attended_ref, order_ref, out_ref):
    del order_ref
    out_ref[...] = attended_ref[...]


def own_rows(values, first):
    half = values.shape[0] // 2
    return jnp.where(first, values[:half], values[half:])


def gate_kernel(
    tp, units, count, meta_ref, hidden_ref, *refs,
):
    pieces = refs[:count]
    (gain_ref, router_ref, routes_ref, attended_ref, input_ref, spread_ref) = refs[count:]
    requests = hidden_ref.shape[0]
    if count == 2:
        summed = pieces[0][...].astype(F32) + pieces[1][...].astype(F32)
    else:
        summed = pieces[0][0:requests, :].astype(F32)
        for t in range(1, tp):
            part = pieces[0][t * requests : (t + 1) * requests, :]
            summed = summed + part.astype(F32)
    attended = (hidden_ref[...].astype(F32) + RESID_SCALE * summed).astype(BF16)
    if count == 2:
        attended_ref[...] = own_rows(attended, meta_ref[3:4, 0:1] == 0)
    else:
        attended_ref[...] = attended
    ffn_input = norm_rows(attended.astype(F32), gain_ref[...])
    input_ref[...] = ffn_input
    logits = lax.dot_general(router_ref[...], ffn_input, NT, preferred_element_type=F32)
    expert = iota(logits.shape, 0)
    named = jnp.zeros(logits.shape, F32)
    for k in range(routes_ref.shape[0]):
        named = jnp.where(routes_ref[k : k + 1, :] == expert, 1.0, named)
    chosen = named > 0.5
    top = jnp.max(jnp.where(chosen, logits, NEG_FILL), axis=0, keepdims=True)
    weights = jnp.where(chosen, jnp.exp(logits - top), 0.0)
    gates = weights / jnp.sum(weights, axis=0, keepdims=True)
    mine = expert == meta_ref[3:4, 0:1] * units // FF
    line = jnp.sum(jnp.where(mine, gates, 0.0), axis=0, keepdims=True)
    diagonal = iota((requests, requests), 0) == iota((requests, requests), 1)
    line = jnp.where(diagonal, jnp.broadcast_to(line, (requests, requests)), 0.0)
    column = jnp.sum(line, axis=1, keepdims=True)
    spread_ref[...] = jnp.broadcast_to(column, spread_ref.shape)


def expert_kernel(meta_ref, lifted_ref, spread_ref, wd_ref, *outs):
    gate = lifted_ref[0]
    active = gate / (1.0 + jnp.exp(-gate)) * lifted_ref[1] * spread_ref[:, 0:1]
    share = jnp.dot(active.astype(BF16), wd_ref[...], preferred_element_type=F32)
    if len(outs) == 2:
        first = meta_ref[3:4, 0:1] == 0
        outs[0][...] = own_rows(share, first)
        outs[1][...] = own_rows(share, jnp.logical_not(first)).astype(BF16)
    else:
        outs[0][...] = share.astype(BF16)


def call(body, outs, in_specs, scratch=(), limit=16, flops=0, moved=0):
    return pl.pallas_call(
        body,
        out_shape=outs,
        in_specs=in_specs,
        out_specs=[VMEM if isinstance(o, jax.ShapeDtypeStruct) else HBM for o in outs],
        scratch_shapes=list(scratch),
        compiler_params=pltpu.CompilerParams(vmem_limit_bytes=limit << 20),
        cost_estimate=pl.CostEstimate(
            flops=flops, bytes_accessed=moved, transcendentals=0
        ),
    )


def swap(values):
    return lax.ppermute(values, "tensor", [(0, 1), (1, 0)])


def on_device(
    hidden,
    attn_gain,
    w_query,
    w_keyvalue,
    w_output,
    cache,
    page_table,
    ctx_len,
    move_dest,
    ffn_gain,
    router,
    routes,
    w_in,
    w_down,
):
    replicas = lax.axis_size("replica")
    tp = lax.axis_size("tensor")
    rank = lax.axis_index("tensor").astype(jnp.int32)
    rows, width = hidden.shape
    pool, page_len, kv_local, _ = cache.shape
    outgoing = move_dest.shape[0]
    local_pages = pool - outgoing
    requests = page_table.shape[0]
    heads = w_query.shape[1] // HEAD_DIM
    inbox = replicas * CAP
    units = w_down.shape[0]
    assert FF % units == 0
    columns = page_len * kv_local
    entries = -(-(pool + inbox) // LANES) * LANES
    struct = jax.ShapeDtypeStruct
    pair = tp == 2
    ids = rank.reshape(1)

    def pin(values):
        return pltpu.with_memory_space_constraint(values, pltpu.HBM)

    def exchange(blocks):
        blocks = blocks.reshape(replicas, CAP * SLOT, LANES)
        blocks = lax.all_to_all(blocks, "replica", split_axis=0, concat_axis=0, tiled=True)
        return blocks.reshape(inbox * SLOT, LANES)

    blocks = pin(cache.reshape(pool, columns, LANES))
    if pair:
        pieces = [hidden, swap(hidden)]
    else:
        pieces = [lax.all_gather(hidden, "tensor", axis=0, tiled=True)]
    meta_shape = (4, entries)
    tables_shape = (2, requests, LANES)
    own, wq, gain, tables, away, away_span, meta = call(
        functools.partial(prepare_kernel, pool, replicas),
        [
            struct(hidden.shape, BF16),
            struct(w_query.shape, BF16),
            struct((1, width), F32),
            struct(tables_shape, F32),
            struct((inbox, requests), BF16),
            struct((inbox, LANES), F32),
            struct(meta_shape, jnp.int32),
        ],
        [SMEM] + [HBM] * 6,
        [
            pltpu.VMEM((1, requests), jnp.int32),
            pltpu.VMEM((page_table.shape[1], requests), jnp.int32),
            pltpu.VMEM((1, outgoing), jnp.int32),
            pltpu.VMEM((width,), F32),
            pltpu.SemaphoreType.DMA((9,)),
        ],
        moved=2 * w_query.size,
    )(
        ids,
        pin(hidden),
        pin(ctx_len.reshape(1, requests)),
        pin(page_table.T),
        pin(move_dest.reshape(1, outgoing)),
        pin(attn_gain),
        pin(w_query),
    )
    if pair:
        pieces[0] = own
    hidden_all, normed, packed, sends, lent = call(
        functools.partial(query_kernel, len(pieces), local_pages),
        [
            struct((requests, width), BF16),
            struct((requests, width), BF16),
            struct((requests * SLOT, LANES), F32),
            struct((inbox * SLOT, LANES), BF16),
            struct((outgoing, columns, LANES), BF16),
        ],
        [VMEM] * (len(pieces) + 6) + [HBM],
        [
            pltpu.VMEM((requests * SLOT, LANES), F32),
            pltpu.VMEM((inbox * SLOT, LANES), F32),
            pltpu.SemaphoreType.DMA((outgoing,)),
        ],
        flops=4 * requests * width * w_query.shape[1],
        moved=2 * w_query.size,
    )(meta, *pieces, gain, wq, tables, away, away_span, blocks)
    asked = exchange(sends)
    replies, meta_far, packed_far, normed_far, tables_far, hidden_far = call(
        functools.partial(lent_kernel, heads, kv_local),
        [
            pltpu.HBM((inbox * SLOT, LANES), BF16),
            pltpu.HBM(meta_shape, jnp.int32),
            pltpu.HBM((requests * SLOT, LANES), F32),
            pltpu.HBM((requests, width), BF16),
            pltpu.HBM(tables_shape, F32),
            pltpu.HBM((requests, width), BF16),
        ],
        [SMEM] + [VMEM] * 7,
        [
            pltpu.VMEM((inbox * SLOT, LANES), F32),
            pltpu.VMEM((inbox * SLOT, LANES), BF16),
            pltpu.SemaphoreType.DMA((6,)),
        ],
        flops=4 * ROWS * columns * LANES * outgoing,
        moved=2 * columns * LANES * outgoing,
    )(meta, asked, lent, meta, packed, normed, tables, hidden_all)
    returned = exchange(replies)
    top, acc = call(
        functools.partial(local_kernel, heads, kv_local),
        [pltpu.HBM((requests, ROWS, LANES), F32)] * 2,
        [HBM] * 6,
        [
            pltpu.SMEM(meta_shape, jnp.int32),
            pltpu.VMEM((requests * SLOT, LANES), F32),
            pltpu.VMEM((requests, width), BF16),
            pltpu.VMEM((width * kv_local, LANES), BF16),
            pltpu.VMEM((width * kv_local, LANES), F32),
            pltpu.VMEM(tables_shape, F32),
            pltpu.VMEM((local_pages, columns, LANES), BF16),
            pltpu.VMEM((requests, ROWS, LANES), F32),
            pltpu.VMEM((requests * ROWS, LANES), F32),
            pltpu.VMEM((local_pages, ROWS, LANES), F32),
            pltpu.VMEM((local_pages, ROWS, LANES), F32),
            pltpu.VMEM((requests + 1, ROWS, LANES), F32),
            pltpu.VMEM((requests + 1, ROWS, LANES), F32),
            pltpu.VMEM((local_pages, ROWS, LANES), F32),
            pltpu.SemaphoreType.DMA((7 + local_pages,)),
        ],
        limit=24,
        flops=4 * ROWS * columns * LANES * local_pages,
        moved=2 * columns * LANES * local_pages,
    )(
        pin(meta_far),
        pin(packed_far),
        pin(normed_far),
        pin(w_keyvalue.reshape(width * kv_local, LANES)),
        pin(tables_far),
        blocks,
    )
    part, meta, hidden_all, gain, router_t, routes_t = call(
        functools.partial(combine_kernel, heads, pool),
        [
            struct((requests, width), BF16),
            struct(meta_shape, jnp.int32),
            struct((requests, width), BF16),
            struct((1, width), F32),
            struct(router.shape[::-1], BF16),
            struct(routes.shape[::-1], jnp.int32),
        ],
        [HBM] * 8 + [VMEM],
        [
            pltpu.SMEM(meta_shape, jnp.int32),
            pltpu.VMEM(w_output.shape, BF16),
            pltpu.VMEM((width,), F32),
            pltpu.VMEM((requests, ROWS, LANES), F32),
            pltpu.VMEM((requests + 1, ROWS, LANES), F32),
            pltpu.VMEM((requests + 1, ROWS, LANES), F32),
            pltpu.VMEM((inbox, ROWS, LANES), F32),
            pltpu.VMEM((inbox * SLOT, LANES), F32),
            pltpu.VMEM((requests * ROWS, LANES), F32),
            pltpu.SemaphoreType.DMA((13,)),
        ],
        flops=2 * requests * w_output.size,
        moved=2 * w_output.size,
    )(
        pin(meta_far), pin(top), pin(acc), pin(w_output), pin(hidden_far), pin(ffn_gain),
        pin(router.T), pin(routes.T), returned,
    )
    if pair:
        parts = [part, swap(part)]
    else:
        parts = [lax.all_gather(part, "tensor", axis=0, tiled=True)]
    (wd,) = call(
        load_kernel,
        [struct(w_down.shape, BF16)],
        [HBM, ANY],
        [pltpu.SemaphoreType.DMA((4,))],
        moved=2 * w_down.size,
    )(pin(w_down), part)
    attended, ffn_input, spread = call(
        functools.partial(gate_kernel, tp, units, len(parts)),
        [
            struct((rows if pair else requests, width), BF16),
            struct((requests, width), BF16),
            struct((requests, LANES), F32),
        ],
        [VMEM] * (len(parts) + 5),
        flops=2 * requests * router.size,
        moved=2 * router.size,
    )(meta, hidden_all, *parts, gain, router_t, routes_t)
    lifted = jnp.einsum("rd,dsu->sru", ffn_input, w_in, preferred_element_type=F32)
    shapes = [struct((requests, width), BF16)]
    if pair:
        shapes = [struct((rows, width), F32), struct((rows, width), BF16)]
    shares = call(
        expert_kernel,
        shapes,
        [VMEM] * 4,
        flops=2 * requests * w_down.size,
        moved=2 * w_down.size,
    )(meta, lifted, spread, wd)
    if pair:
        (attended,) = call(
            finish_kernel, [struct((rows, width), BF16)], [VMEM, ANY], moved=4 * attended.size
        )(attended, shares[1])
        return attended, (shares[0] + swap(shares[1]).astype(F32)).astype(BF16)
    shares = lax.all_gather(shares[0], "tensor", axis=0)
    mine = lax.dynamic_slice_in_dim(shares, rank * rows, rows, axis=1)
    experts_out = jnp.sum(mine.astype(F32), axis=0).astype(BF16)
    attended = lax.dynamic_slice_in_dim(attended, rank * rows, rows, axis=0)
    return attended, experts_out


def solution(mesh):
    placed = (
        P(("replica", "tensor"), None),
        P(),
        P(None, "tensor"),
        P(None, "tensor", None),
        P("tensor", None),
        P("replica", None, "tensor", None),
        P("replica", None),
        P("replica"),
        P("replica"),
        P(),
        P(),
        P("replica", None),
        P(None, None, "tensor"),
        P("tensor", None),
    )
    return jax.shard_map(
        on_device,
        mesh=mesh,
        in_specs=placed,
        out_specs=(P(("replica", "tensor"), None), P(("replica", "tensor"), None)),
        check_vma=False,
    )
```

```python
import functools
import math

import jax
import jax.numpy as jnp
from jax import lax
from jax.experimental import pallas as pl
from jax.experimental.pallas import tpu as pltpu
from jax.sharding import PartitionSpec as P

HEAD_DIM = 64
EXPERTS = 40
FF = 512
CAP = 2
LANES = 128
SLOT = 8
ROWS = 16
META = 6

ATTN_SCALE = 0.015625
RESID_SCALE = 0.22
ROPE_BASE = 10000.0
EPSILON = 1e-06
NEG_FILL = -1e30

F32 = jnp.float32
BF16 = jnp.bfloat16
VMEM = pl.BlockSpec(memory_space=pltpu.VMEM)
SMEM = pl.BlockSpec(memory_space=pltpu.SMEM)
ANY = pl.BlockSpec(memory_space=pl.ANY)
HBM = pl.BlockSpec(memory_space=pltpu.HBM)
NT = (((1,), (1,)), ((), ()))


def iota(shape, axis):
    return lax.broadcasted_iota(jnp.int32, shape, axis)


def norm_rows(values, gain):
    factor = lax.rsqrt(jnp.mean(values * values, axis=-1, keepdims=True) + EPSILON)
    return (values * factor * gain).astype(BF16)


def rope_tables(ctx_row, requests):
    diagonal = iota((requests, requests), 0) == iota((requests, requests), 1)
    ctx = jnp.broadcast_to(ctx_row.astype(F32), (requests, requests))
    ctx = jnp.sum(jnp.where(diagonal, ctx, 0.0), axis=1, keepdims=True)
    lane = iota((requests, LANES), 1)
    index = (lane % (HEAD_DIM // 2)).astype(F32)
    inverse = jnp.exp(index * (-2.0 * math.log(ROPE_BASE) / HEAD_DIM))
    angles = ctx * inverse
    sign = jnp.where(lane % HEAD_DIM < HEAD_DIM // 2, -1.0, 1.0)
    return jnp.cos(angles), jnp.sin(angles) * sign


def rotate(chunk, cosine, sine):
    lane = iota(chunk.shape, 1)
    ahead = pltpu.roll(chunk, LANES - HEAD_DIM // 2, 1)
    behind = pltpu.roll(chunk, HEAD_DIM // 2, 1)
    turned = jnp.where(lane % HEAD_DIM < HEAD_DIM // 2, ahead, behind)
    return chunk * cosine + turned * sine


def copy_of(source, target, sem):
    return pltpu.make_async_copy(source, target, sem)


def copies_of(source, target, sems, base):
    step = source.shape[0] // 4
    return [
        copy_of(
            source.at[pl.ds(i * step, step)], target.at[pl.ds(i * step, step)], sems.at[base + i]
        )
        for i in range(4)
    ]


def page_copies(cache_hbm, first, pages, place, count, sems, base):
    return [
        copy_of(cache_hbm.at[first + p], pages.at[place + p], sems.at[base + p])
        for p in range(count)
    ]


def prepare_kernel(
    pool, replicas, ids_ref, hidden_hbm, ctx_hbm, table_hbm, dest_hbm, attn_gain_hbm,
    wq_hbm, cache_hbm,
    hidden_ref, wq_ref, gain_ref, tables_ref, away_ref, span_ref, meta_ref, lent_ref,
    pick_ref, drop_ref,
    ctx, table, dest, gain, sems,
):
    inbox = replicas * CAP
    requests = ctx.shape[1]
    entries = meta_ref.shape[1]
    small = [
        copy_of(ctx_hbm, ctx, sems.at[0]),
        copy_of(table_hbm, table, sems.at[1]),
        copy_of(dest_hbm, dest, sems.at[2]),
        copy_of(attn_gain_hbm, gain, sems.at[3]),
    ]
    large = [copy_of(hidden_hbm, hidden_ref, sems.at[4])]
    large += copies_of(wq_hbm, wq_ref, sems, 5)
    lending = pl.ds(pool - lent_ref.shape[0], lent_ref.shape[0])
    large.append(copy_of(cache_hbm.at[lending], lent_ref, sems.at[9]))
    for copy in small + large:
        copy.start()
    for copy in small:
        copy.wait()
    gain_ref[...] = gain[...].reshape(1, gain.shape[0])
    ctx_row = ctx[...]

    def claims(values):
        held = jnp.zeros(values.shape, F32)
        spans = jnp.zeros(values.shape, F32)
        for k in range(table.shape[0]):
            match = table[k : k + 1, :] == values
            filled = jnp.clip(ctx_row - k * 128, 0, 128).astype(F32)
            held = jnp.where(match, 1.0, held)
            spans = jnp.where(match, filled, spans)
        return held.astype(BF16), spans

    held, spans = claims(iota((entries, requests), 0))
    numbers = (iota((SLOT, requests), 1) + 1).astype(BF16)
    ones = jnp.ones((SLOT, requests), BF16)
    holder = lax.dot_general(numbers, held, NT, preferred_element_type=F32)
    covered = lax.dot_general(ones, spans.astype(BF16), NT, preferred_element_type=F32)
    meta_ref[0:1, :] = holder[0:1, :].astype(jnp.int32) - 1
    meta_ref[1:2, :] = covered[0:1, :].astype(jnp.int32)
    meta_ref[2:3, :] = jnp.zeros((1, entries), jnp.int32)
    lent = dest.shape[1]
    across = jnp.broadcast_to(dest[...].astype(F32), (lent, lent))
    row, lane = iota((lent, lent), 0), iota((lent, lent), 1)
    down = jnp.sum(jnp.where(row == lane, across, 0.0), axis=1, keepdims=True)
    same = across == down
    before = jnp.sum(jnp.where(same & (lane < row), 1.0, 0.0), axis=1, keepdims=True)
    column = jnp.broadcast_to(down * CAP + before, (lent, LANES)).astype(BF16)
    before = jnp.sum(jnp.where(same & (row < lane), 1.0, 0.0), axis=0, keepdims=True)
    line = (across * CAP + before).astype(BF16)
    expand = iota((lent * SLOT, lent), 0) // SLOT == iota((lent * SLOT, lent), 1)
    expand = jnp.where(expand, 1.0, 0.0).astype(BF16)
    column = jnp.dot(expand, column, preferred_element_type=F32).astype(jnp.int32)
    pick_ref[...] = column * SLOT + iota(column.shape, 0) % SLOT
    line = lax.dot_general(line, expand, NT, preferred_element_type=F32).astype(jnp.int32)
    drop_ref[...] = line * SLOT + iota(line.shape, 1) % SLOT
    meta_ref[3:4, :] = jnp.full((1, entries), ids_ref[0], jnp.int32)
    cosine, sine = rope_tables(ctx_row, requests)
    tables_ref[0] = cosine
    tables_ref[1] = sine
    held, spans = claims(pool + iota((inbox, requests), 0))
    away_ref[...] = held
    away_span = jnp.sum(spans, axis=1, keepdims=True)
    span_ref[...] = jnp.broadcast_to(away_span, span_ref.shape)
    for copy in large:
        copy.wait()


def query_kernel(
    count, meta_ref, *refs,
):
    pieces = refs[:count]
    (gain_ref, wq_ref, tables_ref, away_ref, span_ref,
     hidden_ref, normed_ref, packed_ref, send_ref, packs, sends) = refs[count:]
    requests = hidden_ref.shape[0]
    inbox = span_ref.shape[0]
    width = wq_ref.shape[1]
    chunks = -(-width // LANES)
    if count == 1:
        hidden = pieces[0][...]
    else:
        own, other = pieces[0][...], pieces[1][...]
        first = meta_ref[3:4, 0:1] == 0
        hidden = jnp.concatenate(
            [jnp.where(first, own, other), jnp.where(first, other, own)], axis=0
        )
    hidden_ref[...] = hidden
    normed = norm_rows(hidden.astype(F32), gain_ref[...])
    normed_ref[...] = normed
    queries = jnp.dot(normed, wq_ref[...], preferred_element_type=F32)
    if chunks * LANES > width:
        pad = jnp.zeros((requests, chunks * LANES - width), F32)
        queries = jnp.concatenate([queries, pad], axis=1)
    cosine, sine = tables_ref[0], tables_ref[1]
    zeros = jnp.zeros((requests, LANES), F32)
    nothing = jnp.zeros((inbox, LANES), F32)
    for j in range(SLOT):
        here = pl.ds(j, requests, stride=SLOT)
        there = pl.ds(j, inbox, stride=SLOT)
        if j < chunks:
            chunk = rotate(queries[:, j * LANES : (j + 1) * LANES], cosine, sine)
            chunk = (chunk.astype(BF16).astype(F32) * ATTN_SCALE).astype(BF16)
            packs[here, :] = chunk.astype(F32)
            sends[there, :] = jnp.dot(away_ref[...], chunk, preferred_element_type=F32)
        else:
            packs[here, :] = zeros
            sends[there, :] = span_ref[...] if j == META else nothing
    packed_ref[...] = packs[...]
    send_ref[...] = sends[...].astype(BF16)


def unpack(packed):
    low = iota(packed.shape, 1) < HEAD_DIM
    even = jnp.where(low, packed, 0.0)
    odd = jnp.where(low, pltpu.roll(packed, HEAD_DIM, 1), 0.0)
    return jnp.concatenate([even, odd], axis=0)


def head_rows(heads):
    return [(h // 2) + SLOT * (h % 2) for h in range(heads)]


def token_of_column(heads, kv_local, columns):
    row = iota((ROWS, columns), 0)
    column = iota((ROWS, columns), 1)
    wanted = jnp.full((ROWS, columns), kv_local, jnp.int32)
    for h, place in enumerate(head_rows(heads)):
        wanted = jnp.where(row == place, h // (heads // kv_local), wanted)
    return jnp.where(column % kv_local == wanted, column // kv_local, 1 << 20)


def score_page(query, block):
    return lax.dot_general(query, block, NT, preferred_element_type=F32)


def weigh_page(scores, tokens, span):
    scores = jnp.where(tokens < span, scores, NEG_FILL)
    top = jnp.max(scores, axis=1, keepdims=True)
    weights = jnp.exp(scores - top)
    return top, jnp.sum(weights, axis=1, keepdims=True), weights.astype(BF16)


def attend_pages(count, stage, copies, query_of, block_of, span_of, tokens, keep):
    stages = [range(i, min(i + stage, count)) for i in range(0, count, stage)]

    def score_stage(pages):
        for p in pages:
            if copies is not None:
                copies[p].wait()
        return {p: score_page(query_of(p), block_of(p)) for p in pages}

    scores = score_stage(stages[0])
    for i, pages in enumerate(stages):
        if i + 1 < len(stages):
            ahead = score_stage(stages[i + 1])
        weighed = {p: weigh_page(scores[p], tokens, span_of(p)) for p in pages}
        outs = {
            p: jnp.dot(weighed[p][2], block_of(p), preferred_element_type=F32)
            for p in pages
        }
        for p in pages:
            keep(p, weighed[p][0], weighed[p][1], outs[p])
        if i + 1 < len(stages):
            scores = ahead


def spread_queries(target, packed):
    low = iota(packed.shape, 2) < HEAD_DIM
    target[:, 0:SLOT, :] = jnp.where(low, packed, 0.0)
    target[:, SLOT:ROWS, :] = jnp.where(low, pltpu.roll(packed, HEAD_DIM, 2), 0.0)


def merge_pages(places, top_of, sum_of, top, acc, scaled, start, before):
    requests = start.shape[0]
    for p, place in enumerate(places):
        top[place] = jnp.maximum(top[place], top_of(p))
    acc[0:requests] = start * jnp.exp(before - top[0:requests])
    for p, place in enumerate(places):
        scaled[p] = sum_of(p) * jnp.exp(top_of(p) - top[place])
    for p, place in enumerate(places):
        acc[place] = acc[place] + scaled[p]


def local_kernel(
    heads, kv_local, meta_hbm, packed_hbm, normed_hbm, wkv_hbm, tables_hbm, cache_hbm,
    state_hbm,
    meta, packed, normed, raw, wide, tables, pages, queries, fresh, tops, sums, top,
    acc, scaled, sems,
):
    requests, depth = normed.shape
    count, columns, _ = pages.shape
    small = [
        copy_of(meta_hbm, meta, sems.at[0]),
        copy_of(packed_hbm, packed, sems.at[1]),
        copy_of(normed_hbm, normed, sems.at[2]),
        copy_of(tables_hbm, tables, sems.at[3]),
    ]
    weights = copy_of(wkv_hbm, raw, sems.at[4])
    paging = page_copies(cache_hbm, 0, pages, 0, count, sems, 6)
    for copy in small + [weights] + paging:
        copy.start()
    for copy in small:
        copy.wait()
    spread_queries(queries, packed[...].reshape(requests, SLOT, LANES))
    tokens = token_of_column(heads, kv_local, columns)
    lower = iota((ROWS, LANES), 1) < HEAD_DIM
    low = iota((requests, LANES), 1) < HEAD_DIM
    cosine = jnp.where(low, tables[0], 1.0)
    sine = jnp.where(low, tables[1], 0.0)
    weights.wait()
    if kv_local > 1:
        wide[...] = raw[...].astype(F32)
    new = []
    for k in range(kv_local):
        if kv_local > 1:
            weight = wide[pl.ds(k, depth, stride=kv_local), :].astype(BF16)
        else:
            weight = raw[...]
        projected = jnp.dot(normed[...], weight, preferred_element_type=F32)
        new.append(rotate(projected, cosine, sine).astype(BF16).astype(F32))
    used = {place: h for h, place in enumerate(head_rows(heads))}
    for place in range(ROWS):
        value = jnp.zeros((requests, LANES), F32)
        if place in used:
            value = new[used[place] // (heads // kv_local)]
        fresh[pl.ds(place, requests, stride=ROWS), :] = value

    def keep(p, page_top, total, out):
        tops[p] = jnp.broadcast_to(page_top, (ROWS, LANES))
        sums[p] = jnp.where(lower, total, out)

    attend_pages(
        count,
        4,
        paging,
        lambda p: queries[jnp.maximum(meta[0, p], 0)].astype(BF16),
        lambda p: pages[p],
        lambda p: meta[1, p],
        tokens,
        keep,
    )
    added = fresh[...].reshape(requests, ROWS, LANES)
    low16 = iota(added.shape, 2) < HEAD_DIM
    score = jnp.sum(queries[...] * added, axis=2, keepdims=True)
    before = jnp.broadcast_to(score, added.shape)
    start = jnp.where(low16, 1.0, added)
    top[0:requests] = before

    def place_of(p):
        owner = meta[0, p]
        return jnp.where(owner < 0, requests, owner)

    merge_pages(
        [place_of(p) for p in range(count)],
        lambda p: tops[p],
        lambda p: sums[p],
        top,
        acc,
        scaled,
        start,
        before,
    )
    whole = acc[0:requests]
    acc[0:requests] = jnp.where(
        low16, top[0:requests] + jnp.log(whole), whole / pltpu.roll(whole, HEAD_DIM, 2)
    )
    parked = copy_of(acc.at[pl.ds(0, requests)], state_hbm, sems.at[5])
    parked.start()
    parked.wait()


def lent_kernel(
    heads, kv_local, asked_ref, pages, pick_ref, drop_ref, meta_ref, packed_ref,
    normed_ref, tables_ref, hidden_ref,
    reply_hbm, meta_hbm, packed_hbm, normed_hbm, tables_hbm, hidden_hbm,
    reply16, sems,
):
    outgoing, columns, _ = pages.shape
    parked = [
        copy_of(packed_ref, packed_hbm, sems.at[0]),
        copy_of(normed_ref, normed_hbm, sems.at[1]),
        copy_of(hidden_ref, hidden_hbm, sems.at[2]),
        copy_of(tables_ref, tables_hbm, sems.at[3]),
        copy_of(meta_ref, meta_hbm, sems.at[4]),
    ]
    for copy in parked:
        copy.start()
    slot_rows = asked_ref.shape[0]
    shape = (outgoing * SLOT, slot_rows)
    chosen = jnp.where(pick_ref[:, 0:1] == iota(shape, 1), 1.0, 0.0).astype(BF16)
    asked = jnp.dot(chosen, asked_ref[...], preferred_element_type=F32)
    tokens = token_of_column(heads, kv_local, columns).astype(F32)
    low = iota((SLOT, LANES), 1) < HEAD_DIM
    lane = iota((SLOT, LANES), 1)
    row = iota((SLOT, LANES), 0)

    def terms(total, offset):
        leading = total.astype(BF16).astype(F32)
        rest = total - leading
        second = rest.astype(BF16).astype(F32)
        third = rest - second
        spot = lane - offset - 3 * row
        placed = jnp.where(spot == 0, leading, 0.0)
        placed = jnp.where(spot == 1, second, placed)
        return jnp.where(spot == 2, third, placed)

    packed = [asked[j * SLOT : (j + 1) * SLOT] for j in range(outgoing)]
    replies = {}

    def keep(j, top, total, out):
        out = out / total
        logs = top + jnp.log(total)
        even = pltpu.roll(out[0:SLOT], HEAD_DIM, 1)
        both = jnp.where(low, even, out[SLOT:ROWS])
        line = jnp.sum(
            terms(logs[0:SLOT], 0) + terms(logs[SLOT:ROWS], HEAD_DIM), axis=0, keepdims=True
        )
        replies[j] = jnp.where(row == META, line, both)

    attend_pages(
        outgoing,
        8,
        None,
        lambda j: unpack(packed[j]).astype(BF16),
        lambda j: pages[j],
        lambda j: packed[j][META : META + 1, 0:1],
        tokens,
        keep,
    )
    shape = (slot_rows, outgoing * SLOT)
    placed = jnp.where(drop_ref[0:1, :] == iota(shape, 0), 1.0, 0.0).astype(BF16)
    every = jnp.concatenate([replies[j] for j in range(outgoing)], axis=0).astype(BF16)
    reply = jnp.dot(placed, every, preferred_element_type=F32)
    reply16[...] = reply.astype(BF16)
    replying = copy_of(reply16, reply_hbm, sems.at[5])
    replying.start()
    for copy in parked + [replying]:
        copy.wait()


def combine_kernel(
    heads, pool, meta_hbm, state_hbm, wo_hbm, hidden_hbm, gain_hbm, router_hbm,
    routes_hbm, wd_hbm, reply_ref,
    part_ref, meta_ref, hidden_ref, gain_ref, router_ref, routes_ref, wd_ref,
    meta, state, wo, gain, tops, accs, scaled, reply, finals, sems,
):
    requests = state.shape[0]
    inbox = reply_ref.shape[0] // SLOT
    chunks = -(-heads // 2)
    small = [
        copy_of(meta_hbm, meta, sems.at[0]),
        copy_of(state_hbm, state, sems.at[1]),
    ]
    weights = copies_of(wo_hbm, wo, sems, 2)
    gaining = copy_of(gain_hbm, gain, sems.at[6])
    later = [
        copy_of(meta_hbm, meta_ref, sems.at[7]),
        copy_of(hidden_hbm, hidden_ref, sems.at[8]),
        copy_of(router_hbm, router_ref, sems.at[9]),
        copy_of(routes_hbm, routes_ref, sems.at[10]),
        copy_of(wd_hbm, wd_ref, sems.at[11]),
    ]
    for copy in small + weights + [gaining] + later:
        copy.start()
    reply[...] = reply_ref[...].astype(F32)
    low = iota((SLOT, LANES), 1) < HEAD_DIM
    lane = iota((SLOT, LANES), 1)
    row = iota((SLOT, LANES), 0)
    mine = (lane % HEAD_DIM) // 3 == row

    def place_of(s):
        owner = meta[0, pool + s]
        return jnp.where(owner < 0, requests, owner)

    def logs_of(s):
        line = reply[s * SLOT + META : s * SLOT + META + 1, :]
        line = jnp.where(mine, jnp.broadcast_to(line, (SLOT, LANES)), 0.0)
        even = jnp.sum(jnp.where(low, line, 0.0), axis=1, keepdims=True)
        odd = jnp.sum(jnp.where(low, 0.0, line), axis=1, keepdims=True)
        logs = jnp.concatenate([even, odd], axis=0)
        return jnp.broadcast_to(logs, (ROWS, LANES))

    logs = [logs_of(s) for s in range(inbox)]
    for copy in small:
        copy.wait()
    low16 = iota(state.shape, 2) < HEAD_DIM
    start = state[...]
    before = jnp.where(low16, start, pltpu.roll(start, HEAD_DIM, 2))
    tops[0:requests] = before

    def sum_of(s):
        packed = reply[s * SLOT : (s + 1) * SLOT, :]
        even = jnp.where(low, 1.0, pltpu.roll(packed, HEAD_DIM, 1))
        odd = jnp.where(low, 1.0, packed)
        return jnp.concatenate([even, odd], axis=0)

    merge_pages(
        [place_of(s) for s in range(inbox)],
        lambda s: logs[s],
        sum_of,
        tops,
        accs,
        scaled,
        jnp.where(low16, 1.0, start),
        before,
    )
    whole = accs[0:requests]
    finals[...] = (whole / pltpu.roll(whole, HEAD_DIM, 2)).reshape(
        requests * ROWS, LANES
    )
    wide = iota((requests, LANES), 1) < HEAD_DIM
    parts = []
    for j in range(chunks):
        even = finals[pl.ds(j, requests, stride=ROWS), :]
        odd = finals[pl.ds(SLOT + j, requests, stride=ROWS), :]
        parts.append(jnp.where(wide, pltpu.roll(even, HEAD_DIM, 1), odd).astype(BF16))
    attention = jnp.concatenate(parts, axis=1)[:, : heads * HEAD_DIM]
    for copy in weights:
        copy.wait()
    part_ref[...] = jnp.dot(attention, wo[...], preferred_element_type=F32).astype(BF16)
    gaining.wait()
    gain_ref[...] = gain[...].reshape(1, gain.shape[0])
    for copy in later:
        copy.wait()


def load_kernel(win_hbm, order_hbm, win_ref, sems):
    del order_hbm
    copies = copies_of(win_hbm, win_ref, sems, 0)
    for copy in copies:
        copy.start()
    for copy in copies:
        copy.wait()


def finish_kernel(attended_ref, own_ref, other_ref, attended_out, experts_out):
    attended_out[...] = attended_ref[...]
    experts_out[...] = (own_ref[...] + other_ref[...].astype(F32)).astype(BF16)


def own_rows(values, first):
    half = values.shape[0] // 2
    return jnp.where(first, values[:half], values[half:])


def gate_kernel(
    tp, units, count, meta_ref, hidden_ref, *refs,
):
    pieces = refs[:count]
    (gain_ref, router_ref, routes_ref, attended_ref, input_ref, spread_ref) = refs[count:]
    requests = hidden_ref.shape[0]
    if count == 2:
        summed = pieces[0][...].astype(F32) + pieces[1][...].astype(F32)
    else:
        summed = pieces[0][0:requests, :].astype(F32)
        for t in range(1, tp):
            part = pieces[0][t * requests : (t + 1) * requests, :]
            summed = summed + part.astype(F32)
    attended = (hidden_ref[...].astype(F32) + RESID_SCALE * summed).astype(BF16)
    if count == 2:
        attended_ref[...] = own_rows(attended, meta_ref[3:4, 0:1] == 0)
    else:
        attended_ref[...] = attended
    ffn_input = norm_rows(attended.astype(F32), gain_ref[...])
    input_ref[...] = ffn_input
    logits = lax.dot_general(router_ref[...], ffn_input, NT, preferred_element_type=F32)
    expert = iota(logits.shape, 0)
    named = jnp.zeros(logits.shape, F32)
    for k in range(routes_ref.shape[0]):
        named = jnp.where(routes_ref[k : k + 1, :] == expert, 1.0, named)
    chosen = named > 0.5
    top = jnp.max(jnp.where(chosen, logits, NEG_FILL), axis=0, keepdims=True)
    weights = jnp.where(chosen, jnp.exp(logits - top), 0.0)
    gates = weights / jnp.sum(weights, axis=0, keepdims=True)
    mine = expert == meta_ref[3:4, 0:1] * units // FF
    line = jnp.sum(jnp.where(mine, gates, 0.0), axis=0, keepdims=True)
    diagonal = iota((requests, requests), 0) == iota((requests, requests), 1)
    line = jnp.where(diagonal, jnp.broadcast_to(line, (requests, requests)), 0.0)
    column = jnp.sum(line, axis=1, keepdims=True)
    spread_ref[...] = jnp.broadcast_to(column, spread_ref.shape)


def expert_kernel(meta_ref, lifted_ref, spread_ref, wd_ref, *outs):
    gate = lifted_ref[0]
    active = gate / (1.0 + jnp.exp(-gate)) * lifted_ref[1] * spread_ref[:, 0:1]
    share = jnp.dot(active.astype(BF16), wd_ref[...], preferred_element_type=F32)
    if len(outs) == 2:
        first = meta_ref[3:4, 0:1] == 0
        outs[0][...] = own_rows(share, first)
        outs[1][...] = own_rows(share, jnp.logical_not(first)).astype(BF16)
    else:
        outs[0][...] = share.astype(BF16)


def call(body, outs, in_specs, scratch=(), limit=16, flops=0, moved=0):
    return pl.pallas_call(
        body,
        out_shape=outs,
        in_specs=in_specs,
        out_specs=[VMEM if isinstance(o, jax.ShapeDtypeStruct) else HBM for o in outs],
        scratch_shapes=list(scratch),
        compiler_params=pltpu.CompilerParams(vmem_limit_bytes=limit << 20),
        cost_estimate=pl.CostEstimate(
            flops=flops, bytes_accessed=moved, transcendentals=0
        ),
    )


def swap(values):
    return lax.ppermute(values, "tensor", [(0, 1), (1, 0)])


def on_device(
    hidden,
    attn_gain,
    w_query,
    w_keyvalue,
    w_output,
    cache,
    page_table,
    ctx_len,
    move_dest,
    ffn_gain,
    router,
    routes,
    w_in,
    w_down,
):
    replicas = lax.axis_size("replica")
    tp = lax.axis_size("tensor")
    rank = lax.axis_index("tensor").astype(jnp.int32)
    rows, width = hidden.shape
    pool, page_len, kv_local, _ = cache.shape
    outgoing = move_dest.shape[0]
    local_pages = pool - outgoing
    requests = page_table.shape[0]
    heads = w_query.shape[1] // HEAD_DIM
    inbox = replicas * CAP
    units = w_down.shape[0]
    assert FF % units == 0
    columns = page_len * kv_local
    entries = -(-(pool + inbox) // LANES) * LANES
    struct = jax.ShapeDtypeStruct
    pair = tp == 2
    ids = rank.reshape(1)

    def pin(values):
        return pltpu.with_memory_space_constraint(values, pltpu.HBM)

    def exchange(blocks):
        blocks = blocks.reshape(replicas, CAP * SLOT, LANES)
        blocks = lax.all_to_all(blocks, "replica", split_axis=0, concat_axis=0, tiled=True)
        return blocks.reshape(inbox * SLOT, LANES)

    blocks = pin(cache.reshape(pool, columns, LANES))
    if pair:
        pieces = [hidden, swap(hidden)]
    else:
        pieces = [lax.all_gather(hidden, "tensor", axis=0, tiled=True)]
    meta_shape = (4, entries)
    tables_shape = (2, requests, LANES)
    own, wq, gain, tables, away, away_span, meta, lent, pick, drop = call(
        functools.partial(prepare_kernel, pool, replicas),
        [
            struct(hidden.shape, BF16),
            struct(w_query.shape, BF16),
            struct((1, width), F32),
            struct(tables_shape, F32),
            struct((inbox, requests), BF16),
            struct((inbox, LANES), F32),
            struct(meta_shape, jnp.int32),
            struct((outgoing, columns, LANES), BF16),
            struct((outgoing * SLOT, LANES), jnp.int32),
            struct((outgoing, outgoing * SLOT), jnp.int32),
        ],
        [SMEM] + [HBM] * 7,
        [
            pltpu.VMEM((1, requests), jnp.int32),
            pltpu.VMEM((page_table.shape[1], requests), jnp.int32),
            pltpu.VMEM((1, outgoing), jnp.int32),
            pltpu.VMEM((width,), F32),
            pltpu.SemaphoreType.DMA((10,)),
        ],
        moved=2 * w_query.size,
    )(
        ids,
        pin(hidden),
        pin(ctx_len.reshape(1, requests)),
        pin(page_table.T),
        pin(move_dest.reshape(1, outgoing)),
        pin(attn_gain),
        pin(w_query),
        blocks,
    )
    if pair:
        pieces[0] = own
    hidden_all, normed, packed, sends = call(
        functools.partial(query_kernel, len(pieces)),
        [
            struct((requests, width), BF16),
            struct((requests, width), BF16),
            struct((requests * SLOT, LANES), F32),
            struct((inbox * SLOT, LANES), BF16),
        ],
        [VMEM] * (len(pieces) + 6),
        [
            pltpu.VMEM((requests * SLOT, LANES), F32),
            pltpu.VMEM((inbox * SLOT, LANES), F32),
        ],
        flops=4 * requests * width * w_query.shape[1],
        moved=2 * w_query.size,
    )(meta, *pieces, gain, wq, tables, away, away_span)
    asked = exchange(sends)
    replies, meta_far, packed_far, normed_far, tables_far, hidden_far = call(
        functools.partial(lent_kernel, heads, kv_local),
        [
            pltpu.HBM((inbox * SLOT, LANES), BF16),
            pltpu.HBM(meta_shape, jnp.int32),
            pltpu.HBM((requests * SLOT, LANES), F32),
            pltpu.HBM((requests, width), BF16),
            pltpu.HBM(tables_shape, F32),
            pltpu.HBM((requests, width), BF16),
        ],
        [VMEM] * 9,
        [
            pltpu.VMEM((inbox * SLOT, LANES), BF16),
            pltpu.SemaphoreType.DMA((6,)),
        ],
        flops=4 * ROWS * columns * LANES * outgoing,
        moved=2 * columns * LANES * outgoing,
    )(asked, lent, pick, drop, meta, packed, normed, tables, hidden_all)
    returned = exchange(replies)
    (state,) = call(
        functools.partial(local_kernel, heads, kv_local),
        [pltpu.HBM((requests, ROWS, LANES), F32)],
        [HBM] * 6,
        [
            pltpu.SMEM(meta_shape, jnp.int32),
            pltpu.VMEM((requests * SLOT, LANES), F32),
            pltpu.VMEM((requests, width), BF16),
            pltpu.VMEM((width * kv_local, LANES), BF16),
            pltpu.VMEM((width * kv_local, LANES), F32),
            pltpu.VMEM(tables_shape, F32),
            pltpu.VMEM((local_pages, columns, LANES), BF16),
            pltpu.VMEM((requests, ROWS, LANES), F32),
            pltpu.VMEM((requests * ROWS, LANES), F32),
            pltpu.VMEM((local_pages, ROWS, LANES), F32),
            pltpu.VMEM((local_pages, ROWS, LANES), F32),
            pltpu.VMEM((requests + 1, ROWS, LANES), F32),
            pltpu.VMEM((requests + 1, ROWS, LANES), F32),
            pltpu.VMEM((local_pages, ROWS, LANES), F32),
            pltpu.SemaphoreType.DMA((6 + local_pages,)),
        ],
        limit=24,
        flops=4 * ROWS * columns * LANES * local_pages,
        moved=2 * columns * LANES * local_pages,
    )(
        pin(meta_far),
        pin(packed_far),
        pin(normed_far),
        pin(w_keyvalue.reshape(width * kv_local, LANES)),
        pin(tables_far),
        blocks,
    )
    part, meta, hidden_all, gain, router_t, routes_t, wd = call(
        functools.partial(combine_kernel, heads, pool),
        [
            struct((requests, width), BF16),
            struct(meta_shape, jnp.int32),
            struct((requests, width), BF16),
            struct((1, width), F32),
            struct(router.shape[::-1], BF16),
            struct(routes.shape[::-1], jnp.int32),
            struct(w_down.shape, BF16),
        ],
        [HBM] * 8 + [VMEM],
        [
            pltpu.SMEM(meta_shape, jnp.int32),
            pltpu.VMEM((requests, ROWS, LANES), F32),
            pltpu.VMEM(w_output.shape, BF16),
            pltpu.VMEM((width,), F32),
            pltpu.VMEM((requests + 1, ROWS, LANES), F32),
            pltpu.VMEM((requests + 1, ROWS, LANES), F32),
            pltpu.VMEM((inbox, ROWS, LANES), F32),
            pltpu.VMEM((inbox * SLOT, LANES), F32),
            pltpu.VMEM((requests * ROWS, LANES), F32),
            pltpu.SemaphoreType.DMA((12,)),
        ],
        flops=2 * requests * w_output.size,
        moved=2 * (w_output.size + w_down.size),
    )(
        pin(meta_far), pin(state), pin(w_output), pin(hidden_far), pin(ffn_gain),
        pin(router.T), pin(routes.T), pin(w_down), returned,
    )
    if pair:
        parts = [part, swap(part)]
    else:
        parts = [lax.all_gather(part, "tensor", axis=0, tiled=True)]
    (w_first,) = call(
        load_kernel,
        [struct(w_in.shape, BF16)],
        [HBM, ANY],
        [pltpu.SemaphoreType.DMA((4,))],
        moved=2 * w_in.size,
    )(pin(w_in), part)
    attended, ffn_input, spread = call(
        functools.partial(gate_kernel, tp, units, len(parts)),
        [
            struct((rows if pair else requests, width), BF16),
            struct((requests, width), BF16),
            struct((requests, LANES), F32),
        ],
        [VMEM] * (len(parts) + 5),
        flops=2 * requests * router.size,
        moved=2 * router.size,
    )(meta, hidden_all, *parts, gain, router_t, routes_t)
    lifted = jnp.einsum("rd,dsu->sru", ffn_input, w_first, preferred_element_type=F32)
    shapes = [struct((requests, width), BF16)]
    if pair:
        shapes = [struct((rows, width), F32), struct((rows, width), BF16)]
    shares = call(
        expert_kernel,
        shapes,
        [VMEM] * 4,
        flops=2 * requests * w_down.size,
        moved=2 * w_down.size,
    )(meta, lifted, spread, wd)
    if pair:
        out = struct((rows, width), BF16)
        return tuple(
            call(finish_kernel, [out, out], [VMEM] * 3)(attended, shares[0], swap(shares[1]))
        )
    shares = lax.all_gather(shares[0], "tensor", axis=0)
    mine = lax.dynamic_slice_in_dim(shares, rank * rows, rows, axis=1)
    experts_out = jnp.sum(mine.astype(F32), axis=0).astype(BF16)
    attended = lax.dynamic_slice_in_dim(attended, rank * rows, rows, axis=0)
    return attended, experts_out


def solution(mesh):
    placed = (
        P(("replica", "tensor"), None),
        P(),
        P(None, "tensor"),
        P(None, "tensor", None),
        P("tensor", None),
        P("replica", None, "tensor", None),
        P("replica", None),
        P("replica"),
        P("replica"),
        P(),
        P(),
        P("replica", None),
        P(None, None, "tensor"),
        P("tensor", None),
    )
    return jax.shard_map(
        on_device,
        mesh=mesh,
        in_specs=placed,
        out_specs=(P(("replica", "tensor"), None), P(("replica", "tensor"), None)),
        check_vma=False,
    )
```

```python
import functools
import math

import jax
import jax.numpy as jnp
from jax import lax
from jax.experimental import pallas as pl
from jax.experimental.pallas import tpu as pltpu
from jax.sharding import PartitionSpec as P

HEAD_DIM = 64
EXPERTS = 40
FF = 512
CAP = 2
LANES = 128
SLOT = 8
ROWS = 16
META = 6

ATTN_SCALE = 0.015625
RESID_SCALE = 0.22
ROPE_BASE = 10000.0
EPSILON = 1e-06
NEG_FILL = -1e30

F32 = jnp.float32
BF16 = jnp.bfloat16
VMEM = pl.BlockSpec(memory_space=pltpu.VMEM)
SMEM = pl.BlockSpec(memory_space=pltpu.SMEM)
ANY = pl.BlockSpec(memory_space=pl.ANY)
HBM = pl.BlockSpec(memory_space=pltpu.HBM)
NT = (((1,), (1,)), ((), ()))


def iota(shape, axis):
    return lax.broadcasted_iota(jnp.int32, shape, axis)


def norm_rows(values, gain):
    factor = lax.rsqrt(jnp.mean(values * values, axis=-1, keepdims=True) + EPSILON)
    return (values * factor * gain).astype(BF16)


def rope_tables(ctx_row, requests):
    diagonal = iota((requests, requests), 0) == iota((requests, requests), 1)
    ctx = jnp.broadcast_to(ctx_row.astype(F32), (requests, requests))
    ctx = jnp.sum(jnp.where(diagonal, ctx, 0.0), axis=1, keepdims=True)
    lane = iota((requests, LANES), 1)
    index = (lane % (HEAD_DIM // 2)).astype(F32)
    inverse = jnp.exp(index * (-2.0 * math.log(ROPE_BASE) / HEAD_DIM))
    angles = ctx * inverse
    sign = jnp.where(lane % HEAD_DIM < HEAD_DIM // 2, -1.0, 1.0)
    return jnp.cos(angles), jnp.sin(angles) * sign


def rotate(chunk, cosine, sine):
    lane = iota(chunk.shape, 1)
    ahead = pltpu.roll(chunk, LANES - HEAD_DIM // 2, 1)
    behind = pltpu.roll(chunk, HEAD_DIM // 2, 1)
    turned = jnp.where(lane % HEAD_DIM < HEAD_DIM // 2, ahead, behind)
    return chunk * cosine + turned * sine


def copy_of(source, target, sem):
    return pltpu.make_async_copy(source, target, sem)


def copies_of(source, target, sems, base):
    step = source.shape[0] // 4
    return [
        copy_of(
            source.at[pl.ds(i * step, step)], target.at[pl.ds(i * step, step)], sems.at[base + i]
        )
        for i in range(4)
    ]


def page_copies(cache_hbm, first, pages, place, count, sems, base):
    return [
        copy_of(cache_hbm.at[first + p], pages.at[place + p], sems.at[base + p])
        for p in range(count)
    ]


def prepare_kernel(
    pool, replicas, ids_ref, hidden_hbm, ctx_hbm, table_hbm, dest_hbm, attn_gain_hbm,
    wq_hbm, cache_hbm,
    hidden_ref, wq_ref, gain_ref, tables_ref, away_ref, span_ref, meta_ref, lent_ref,
    pick_ref, drop_ref,
    ctx, table, dest, gain, sems,
):
    inbox = replicas * CAP
    requests = ctx.shape[1]
    entries = meta_ref.shape[1]
    small = [
        copy_of(ctx_hbm, ctx, sems.at[0]),
        copy_of(table_hbm, table, sems.at[1]),
        copy_of(dest_hbm, dest, sems.at[2]),
        copy_of(attn_gain_hbm, gain, sems.at[3]),
    ]
    large = [copy_of(hidden_hbm, hidden_ref, sems.at[4])]
    large += copies_of(wq_hbm, wq_ref, sems, 5)
    lending = pl.ds(pool - lent_ref.shape[0], lent_ref.shape[0])
    large.append(copy_of(cache_hbm.at[lending], lent_ref, sems.at[9]))
    for copy in small + large:
        copy.start()
    for copy in small:
        copy.wait()
    gain_ref[...] = gain[...].reshape(1, gain.shape[0])
    ctx_row = ctx[...]

    def claims(values):
        held = jnp.zeros(values.shape, F32)
        spans = jnp.zeros(values.shape, F32)
        for k in range(table.shape[0]):
            match = table[k : k + 1, :] == values
            filled = jnp.clip(ctx_row - k * 128, 0, 128).astype(F32)
            held = jnp.where(match, 1.0, held)
            spans = jnp.where(match, filled, spans)
        return held.astype(BF16), spans

    held, spans = claims(iota((entries, requests), 0))
    numbers = (iota((SLOT, requests), 1) + 1).astype(BF16)
    ones = jnp.ones((SLOT, requests), BF16)
    holder = lax.dot_general(numbers, held, NT, preferred_element_type=F32)
    covered = lax.dot_general(ones, spans.astype(BF16), NT, preferred_element_type=F32)
    meta_ref[0:1, :] = holder[0:1, :].astype(jnp.int32) - 1
    meta_ref[1:2, :] = covered[0:1, :].astype(jnp.int32)
    meta_ref[2:3, :] = jnp.zeros((1, entries), jnp.int32)
    lent = dest.shape[1]
    across = jnp.broadcast_to(dest[...].astype(F32), (lent, lent))
    row, lane = iota((lent, lent), 0), iota((lent, lent), 1)
    down = jnp.sum(jnp.where(row == lane, across, 0.0), axis=1, keepdims=True)
    same = across == down
    before = jnp.sum(jnp.where(same & (lane < row), 1.0, 0.0), axis=1, keepdims=True)
    column = jnp.broadcast_to(down * CAP + before, (lent, LANES)).astype(BF16)
    before = jnp.sum(jnp.where(same & (row < lane), 1.0, 0.0), axis=0, keepdims=True)
    line = (across * CAP + before).astype(BF16)
    expand = iota((lent * SLOT, lent), 0) // SLOT == iota((lent * SLOT, lent), 1)
    expand = jnp.where(expand, 1.0, 0.0).astype(BF16)
    column = jnp.dot(expand, column, preferred_element_type=F32).astype(jnp.int32)
    pick_ref[...] = column * SLOT + iota(column.shape, 0) % SLOT
    line = lax.dot_general(line, expand, NT, preferred_element_type=F32).astype(jnp.int32)
    drop_ref[...] = line * SLOT + iota(line.shape, 1) % SLOT
    meta_ref[3:4, :] = jnp.full((1, entries), ids_ref[0], jnp.int32)
    cosine, sine = rope_tables(ctx_row, requests)
    tables_ref[0] = cosine
    tables_ref[1] = sine
    held, spans = claims(pool + iota((inbox, requests), 0))
    away_ref[...] = held
    away_span = jnp.sum(spans, axis=1, keepdims=True)
    span_ref[...] = jnp.broadcast_to(away_span, span_ref.shape)
    for copy in large:
        copy.wait()


def query_kernel(
    count, meta_ref, *refs,
):
    pieces = refs[:count]
    (gain_ref, wq_ref, tables_ref, away_ref, span_ref,
     hidden_ref, normed_ref, packed_ref, send_ref, packs, sends) = refs[count:]
    requests = hidden_ref.shape[0]
    inbox = span_ref.shape[0]
    width = wq_ref.shape[1]
    chunks = -(-width // LANES)
    if count == 1:
        hidden = pieces[0][...]
    else:
        own, other = pieces[0][...], pieces[1][...]
        first = meta_ref[3:4, 0:1] == 0
        hidden = jnp.concatenate(
            [jnp.where(first, own, other), jnp.where(first, other, own)], axis=0
        )
    hidden_ref[...] = hidden
    normed = norm_rows(hidden.astype(F32), gain_ref[...])
    normed_ref[...] = normed
    queries = jnp.dot(normed, wq_ref[...], preferred_element_type=F32)
    if chunks * LANES > width:
        pad = jnp.zeros((requests, chunks * LANES - width), F32)
        queries = jnp.concatenate([queries, pad], axis=1)
    cosine, sine = tables_ref[0], tables_ref[1]
    zeros = jnp.zeros((requests, LANES), F32)
    nothing = jnp.zeros((inbox, LANES), F32)
    for j in range(SLOT):
        here = pl.ds(j, requests, stride=SLOT)
        there = pl.ds(j, inbox, stride=SLOT)
        if j < chunks:
            chunk = rotate(queries[:, j * LANES : (j + 1) * LANES], cosine, sine)
            chunk = (chunk.astype(BF16).astype(F32) * ATTN_SCALE).astype(BF16)
            packs[here, :] = chunk.astype(F32)
            sends[there, :] = jnp.dot(away_ref[...], chunk, preferred_element_type=F32)
        else:
            packs[here, :] = zeros
            sends[there, :] = span_ref[...] if j == META else nothing
    packed_ref[...] = packs[...]
    send_ref[...] = sends[...].astype(BF16)


def unpack(packed):
    low = iota(packed.shape, 1) < HEAD_DIM
    even = jnp.where(low, packed, 0.0)
    odd = jnp.where(low, pltpu.roll(packed, HEAD_DIM, 1), 0.0)
    return jnp.concatenate([even, odd], axis=0)


def head_rows(heads):
    return [(h // 2) + SLOT * (h % 2) for h in range(heads)]


def token_of_column(heads, kv_local, columns):
    row = iota((ROWS, columns), 0)
    column = iota((ROWS, columns), 1)
    wanted = jnp.full((ROWS, columns), kv_local, jnp.int32)
    for h, place in enumerate(head_rows(heads)):
        wanted = jnp.where(row == place, h // (heads // kv_local), wanted)
    return jnp.where(column % kv_local == wanted, column // kv_local, 1 << 20)


def score_page(query, block):
    return lax.dot_general(query, block, NT, preferred_element_type=F32)


def weigh_page(scores, tokens, span):
    scores = jnp.where(tokens < span, scores, NEG_FILL)
    top = jnp.max(scores, axis=1, keepdims=True)
    weights = jnp.exp(scores - top)
    return top, jnp.sum(weights, axis=1, keepdims=True), weights.astype(BF16)


def attend_pages(count, stage, copies, query_of, block_of, span_of, tokens, keep):
    stages = [range(i, min(i + stage, count)) for i in range(0, count, stage)]

    def score_stage(pages):
        for p in pages:
            if copies is not None:
                copies[p].wait()
        return {p: score_page(query_of(p), block_of(p)) for p in pages}

    scores = score_stage(stages[0])
    for i, pages in enumerate(stages):
        if i + 1 < len(stages):
            ahead = score_stage(stages[i + 1])
        weighed = {p: weigh_page(scores[p], tokens, span_of(p)) for p in pages}
        outs = {
            p: jnp.dot(weighed[p][2], block_of(p), preferred_element_type=F32)
            for p in pages
        }
        for p in pages:
            keep(p, weighed[p][0], weighed[p][1], outs[p])
        if i + 1 < len(stages):
            scores = ahead


def spread_queries(target, packed):
    low = iota(packed.shape, 2) < HEAD_DIM
    target[:, 0:SLOT, :] = jnp.where(low, packed, 0.0)
    target[:, SLOT:ROWS, :] = jnp.where(low, pltpu.roll(packed, HEAD_DIM, 2), 0.0)


def merge_pages(places, top_of, sum_of, top, acc, scaled, start, before):
    requests = start.shape[0]
    for p, place in enumerate(places):
        top[place] = jnp.maximum(top[place], top_of(p))
    acc[0:requests] = start * jnp.exp(before - top[0:requests])
    for p, place in enumerate(places):
        scaled[p] = sum_of(p) * jnp.exp(top_of(p) - top[place])
    for p, place in enumerate(places):
        acc[place] = acc[place] + scaled[p]


def local_kernel(
    heads, kv_local, meta_hbm, packed_hbm, normed_hbm, wkv_hbm, tables_hbm, cache_hbm,
    state_hbm,
    meta, packed, normed, raw, wide, tables, pages, queries, fresh, tops, sums, top,
    acc, scaled, sems,
):
    requests, depth = normed.shape
    count, columns, _ = pages.shape
    small = [
        copy_of(meta_hbm, meta, sems.at[0]),
        copy_of(packed_hbm, packed, sems.at[1]),
        copy_of(normed_hbm, normed, sems.at[2]),
        copy_of(tables_hbm, tables, sems.at[3]),
    ]
    weights = copy_of(wkv_hbm, raw, sems.at[4])
    paging = page_copies(cache_hbm, 0, pages, 0, count, sems, 6)
    for copy in small + paging + [weights]:
        copy.start()
    for copy in small:
        copy.wait()
    spread_queries(queries, packed[...].reshape(requests, SLOT, LANES))
    tokens = token_of_column(heads, kv_local, columns)
    lower = iota((ROWS, LANES), 1) < HEAD_DIM
    low = iota((requests, LANES), 1) < HEAD_DIM
    cosine = jnp.where(low, tables[0], 1.0)
    sine = jnp.where(low, tables[1], 0.0)

    def keep(p, page_top, total, out):
        tops[p] = jnp.broadcast_to(page_top, (ROWS, LANES))
        sums[p] = jnp.where(lower, total, out)

    attend_pages(
        count,
        4,
        paging,
        lambda p: queries[jnp.maximum(meta[0, p], 0)].astype(BF16),
        lambda p: pages[p],
        lambda p: meta[1, p],
        tokens,
        keep,
    )
    weights.wait()
    if kv_local > 1:
        wide[...] = raw[...].astype(F32)
    new = []
    for k in range(kv_local):
        if kv_local > 1:
            weight = wide[pl.ds(k, depth, stride=kv_local), :].astype(BF16)
        else:
            weight = raw[...]
        projected = jnp.dot(normed[...], weight, preferred_element_type=F32)
        new.append(rotate(projected, cosine, sine).astype(BF16).astype(F32))
    used = {place: h for h, place in enumerate(head_rows(heads))}
    for place in range(ROWS):
        value = jnp.zeros((requests, LANES), F32)
        if place in used:
            value = new[used[place] // (heads // kv_local)]
        fresh[pl.ds(place, requests, stride=ROWS), :] = value

    added = fresh[...].reshape(requests, ROWS, LANES)
    low16 = iota(added.shape, 2) < HEAD_DIM
    score = jnp.sum(queries[...] * added, axis=2, keepdims=True)
    before = jnp.broadcast_to(score, added.shape)
    start = jnp.where(low16, 1.0, added)
    top[0:requests] = before

    def place_of(p):
        owner = meta[0, p]
        return jnp.where(owner < 0, requests, owner)

    merge_pages(
        [place_of(p) for p in range(count)],
        lambda p: tops[p],
        lambda p: sums[p],
        top,
        acc,
        scaled,
        start,
        before,
    )
    whole = acc[0:requests]
    acc[0:requests] = jnp.where(
        low16, top[0:requests] + jnp.log(whole), whole / pltpu.roll(whole, HEAD_DIM, 2)
    )
    parked = copy_of(acc.at[pl.ds(0, requests)], state_hbm, sems.at[5])
    parked.start()
    parked.wait()


def lent_kernel(
    heads, kv_local, asked_ref, pages, pick_ref, drop_ref, meta_ref, packed_ref,
    normed_ref, tables_ref, hidden_ref,
    reply_hbm, meta_hbm, packed_hbm, normed_hbm, tables_hbm, hidden_hbm,
    reply16, sems,
):
    outgoing, columns, _ = pages.shape
    parked = [
        copy_of(packed_ref, packed_hbm, sems.at[0]),
        copy_of(normed_ref, normed_hbm, sems.at[1]),
        copy_of(hidden_ref, hidden_hbm, sems.at[2]),
        copy_of(tables_ref, tables_hbm, sems.at[3]),
        copy_of(meta_ref, meta_hbm, sems.at[4]),
    ]
    for copy in parked:
        copy.start()
    slot_rows = asked_ref.shape[0]
    shape = (outgoing * SLOT, slot_rows)
    chosen = jnp.where(pick_ref[:, 0:1] == iota(shape, 1), 1.0, 0.0).astype(BF16)
    asked = jnp.dot(chosen, asked_ref[...], preferred_element_type=F32)
    tokens = token_of_column(heads, kv_local, columns).astype(F32)
    low = iota((SLOT, LANES), 1) < HEAD_DIM
    lane = iota((SLOT, LANES), 1)
    row = iota((SLOT, LANES), 0)

    def terms(total, offset):
        leading = total.astype(BF16).astype(F32)
        rest = total - leading
        second = rest.astype(BF16).astype(F32)
        third = rest - second
        spot = lane - offset - 3 * row
        placed = jnp.where(spot == 0, leading, 0.0)
        placed = jnp.where(spot == 1, second, placed)
        return jnp.where(spot == 2, third, placed)

    packed = [asked[j * SLOT : (j + 1) * SLOT] for j in range(outgoing)]
    replies = {}

    def keep(j, top, total, out):
        out = out / total
        logs = top + jnp.log(total)
        even = pltpu.roll(out[0:SLOT], HEAD_DIM, 1)
        both = jnp.where(low, even, out[SLOT:ROWS])
        line = jnp.sum(
            terms(logs[0:SLOT], 0) + terms(logs[SLOT:ROWS], HEAD_DIM), axis=0, keepdims=True
        )
        replies[j] = jnp.where(row == META, line, both)

    attend_pages(
        outgoing,
        8,
        None,
        lambda j: unpack(packed[j]).astype(BF16),
        lambda j: pages[j],
        lambda j: packed[j][META : META + 1, 0:1],
        tokens,
        keep,
    )
    shape = (slot_rows, outgoing * SLOT)
    placed = jnp.where(drop_ref[0:1, :] == iota(shape, 0), 1.0, 0.0).astype(BF16)
    every = jnp.concatenate([replies[j] for j in range(outgoing)], axis=0).astype(BF16)
    reply = jnp.dot(placed, every, preferred_element_type=F32)
    reply16[...] = reply.astype(BF16)
    replying = copy_of(reply16, reply_hbm, sems.at[5])
    replying.start()
    for copy in parked + [replying]:
        copy.wait()


def combine_kernel(
    heads, pool, meta_hbm, state_hbm, wo_hbm, hidden_hbm, gain_hbm, router_hbm,
    routes_hbm, reply_ref,
    part_ref, meta_ref, hidden_ref, gain_ref, router_ref, routes_ref,
    meta, state, wo, gain, tops, accs, scaled, reply, finals, sems,
):
    requests = state.shape[0]
    inbox = reply_ref.shape[0] // SLOT
    chunks = -(-heads // 2)
    small = [
        copy_of(meta_hbm, meta, sems.at[0]),
        copy_of(state_hbm, state, sems.at[1]),
    ]
    weights = copies_of(wo_hbm, wo, sems, 2)
    gaining = copy_of(gain_hbm, gain, sems.at[6])
    later = [
        copy_of(meta_hbm, meta_ref, sems.at[7]),
        copy_of(hidden_hbm, hidden_ref, sems.at[8]),
        copy_of(router_hbm, router_ref, sems.at[9]),
        copy_of(routes_hbm, routes_ref, sems.at[10]),
    ]
    for copy in small + weights + [gaining] + later:
        copy.start()
    reply[...] = reply_ref[...].astype(F32)
    low = iota((SLOT, LANES), 1) < HEAD_DIM
    lane = iota((SLOT, LANES), 1)
    row = iota((SLOT, LANES), 0)
    mine = (lane % HEAD_DIM) // 3 == row

    def place_of(s):
        owner = meta[0, pool + s]
        return jnp.where(owner < 0, requests, owner)

    def logs_of(s):
        line = reply[s * SLOT + META : s * SLOT + META + 1, :]
        line = jnp.where(mine, jnp.broadcast_to(line, (SLOT, LANES)), 0.0)
        even = jnp.sum(jnp.where(low, line, 0.0), axis=1, keepdims=True)
        odd = jnp.sum(jnp.where(low, 0.0, line), axis=1, keepdims=True)
        logs = jnp.concatenate([even, odd], axis=0)
        return jnp.broadcast_to(logs, (ROWS, LANES))

    logs = [logs_of(s) for s in range(inbox)]
    for copy in small:
        copy.wait()
    low16 = iota(state.shape, 2) < HEAD_DIM
    start = state[...]
    before = jnp.where(low16, start, pltpu.roll(start, HEAD_DIM, 2))
    tops[0:requests] = before

    def sum_of(s):
        packed = reply[s * SLOT : (s + 1) * SLOT, :]
        even = jnp.where(low, 1.0, pltpu.roll(packed, HEAD_DIM, 1))
        odd = jnp.where(low, 1.0, packed)
        return jnp.concatenate([even, odd], axis=0)

    merge_pages(
        [place_of(s) for s in range(inbox)],
        lambda s: logs[s],
        sum_of,
        tops,
        accs,
        scaled,
        jnp.where(low16, 1.0, start),
        before,
    )
    whole = accs[0:requests]
    finals[...] = (whole / pltpu.roll(whole, HEAD_DIM, 2)).reshape(
        requests * ROWS, LANES
    )
    wide = iota((requests, LANES), 1) < HEAD_DIM
    parts = []
    for j in range(chunks):
        even = finals[pl.ds(j, requests, stride=ROWS), :]
        odd = finals[pl.ds(SLOT + j, requests, stride=ROWS), :]
        parts.append(jnp.where(wide, pltpu.roll(even, HEAD_DIM, 1), odd).astype(BF16))
    attention = jnp.concatenate(parts, axis=1)[:, : heads * HEAD_DIM]
    for copy in weights:
        copy.wait()
    part_ref[...] = jnp.dot(attention, wo[...], preferred_element_type=F32).astype(BF16)
    gaining.wait()
    gain_ref[...] = gain[...].reshape(1, gain.shape[0])
    for copy in later:
        copy.wait()


def load_kernel(wd_hbm, order_hbm, wd_ref, sems):
    del order_hbm
    copies = copies_of(wd_hbm, wd_ref, sems, 0)
    for copy in copies:
        copy.start()
    for copy in copies:
        copy.wait()


def finish_kernel(attended_ref, own_ref, other_ref, attended_out, experts_out):
    attended_out[...] = attended_ref[...]
    experts_out[...] = (own_ref[...] + other_ref[...].astype(F32)).astype(BF16)


def own_rows(values, first):
    half = values.shape[0] // 2
    return jnp.where(first, values[:half], values[half:])


def residual_kernel(
    tp, count, meta_ref, hidden_ref, *refs,
):
    pieces = refs[:count]
    gain_ref, attended_ref, input_ref, again_ref = refs[count:]
    requests = hidden_ref.shape[0]
    if count == 2:
        summed = pieces[0][...].astype(F32) + pieces[1][...].astype(F32)
    else:
        summed = pieces[0][0:requests, :].astype(F32)
        for t in range(1, tp):
            part = pieces[0][t * requests : (t + 1) * requests, :]
            summed = summed + part.astype(F32)
    attended = (hidden_ref[...].astype(F32) + RESID_SCALE * summed).astype(BF16)
    if count == 2:
        attended_ref[...] = own_rows(attended, meta_ref[3:4, 0:1] == 0)
    else:
        attended_ref[...] = attended
    ffn_input = norm_rows(attended.astype(F32), gain_ref[...])
    input_ref[...] = ffn_input
    again_ref[...] = ffn_input


def gate_column(units, meta_ref, input_ref, router_ref, routes_ref):
    ffn_input = input_ref[...]
    requests = ffn_input.shape[0]
    logits = lax.dot_general(router_ref[...], ffn_input, NT, preferred_element_type=F32)
    expert = iota(logits.shape, 0)
    named = jnp.zeros(logits.shape, F32)
    for k in range(routes_ref.shape[0]):
        named = jnp.where(routes_ref[k : k + 1, :] == expert, 1.0, named)
    chosen = named > 0.5
    top = jnp.max(jnp.where(chosen, logits, NEG_FILL), axis=0, keepdims=True)
    weights = jnp.where(chosen, jnp.exp(logits - top), 0.0)
    total = jnp.sum(weights, axis=0, keepdims=True)
    mine = expert == meta_ref[3:4, 0:1] * units // FF
    line = jnp.sum(jnp.where(mine, weights, 0.0), axis=0, keepdims=True) / total
    diagonal = iota((requests, requests), 0) == iota((requests, requests), 1)
    line = jnp.where(diagonal, jnp.broadcast_to(line, (requests, requests)), 0.0)
    return jnp.sum(line, axis=1, keepdims=True)


def expert_kernel(
    units, meta_ref, lifted_ref, input_ref, router_ref, routes_ref, wd_ref, *outs
):
    column = gate_column(units, meta_ref, input_ref, router_ref, routes_ref)
    gate = lifted_ref[0]
    active = gate / (1.0 + jnp.exp(-gate)) * lifted_ref[1] * column
    share = jnp.dot(active.astype(BF16), wd_ref[...], preferred_element_type=F32)
    if len(outs) == 2:
        first = meta_ref[3:4, 0:1] == 0
        outs[0][...] = own_rows(share, first)
        outs[1][...] = own_rows(share, jnp.logical_not(first)).astype(BF16)
    else:
        outs[0][...] = share.astype(BF16)


def call(body, outs, in_specs, scratch=(), limit=16, flops=0, moved=0):
    return pl.pallas_call(
        body,
        out_shape=outs,
        in_specs=in_specs,
        out_specs=[VMEM if isinstance(o, jax.ShapeDtypeStruct) else HBM for o in outs],
        scratch_shapes=list(scratch),
        compiler_params=pltpu.CompilerParams(vmem_limit_bytes=limit << 20),
        cost_estimate=pl.CostEstimate(
            flops=flops, bytes_accessed=moved, transcendentals=0
        ),
    )


def swap(values):
    return lax.ppermute(values, "tensor", [(0, 1), (1, 0)])


def on_device(
    hidden,
    attn_gain,
    w_query,
    w_keyvalue,
    w_output,
    cache,
    page_table,
    ctx_len,
    move_dest,
    ffn_gain,
    router,
    routes,
    w_in,
    w_down,
):
    replicas = lax.axis_size("replica")
    tp = lax.axis_size("tensor")
    rank = lax.axis_index("tensor").astype(jnp.int32)
    rows, width = hidden.shape
    pool, page_len, kv_local, _ = cache.shape
    outgoing = move_dest.shape[0]
    local_pages = pool - outgoing
    requests = page_table.shape[0]
    heads = w_query.shape[1] // HEAD_DIM
    inbox = replicas * CAP
    units = w_down.shape[0]
    assert FF % units == 0
    columns = page_len * kv_local
    entries = -(-(pool + inbox) // LANES) * LANES
    struct = jax.ShapeDtypeStruct
    pair = tp == 2
    ids = rank.reshape(1)

    def pin(values):
        return pltpu.with_memory_space_constraint(values, pltpu.HBM)

    def exchange(blocks):
        blocks = blocks.reshape(replicas, CAP * SLOT, LANES)
        blocks = lax.all_to_all(blocks, "replica", split_axis=0, concat_axis=0, tiled=True)
        return blocks.reshape(inbox * SLOT, LANES)

    blocks = pin(cache.reshape(pool, columns, LANES))
    if pair:
        pieces = [hidden, swap(hidden)]
    else:
        pieces = [lax.all_gather(hidden, "tensor", axis=0, tiled=True)]
    meta_shape = (4, entries)
    tables_shape = (2, requests, LANES)
    own, wq, gain, tables, away, away_span, meta, lent, pick, drop = call(
        functools.partial(prepare_kernel, pool, replicas),
        [
            struct(hidden.shape, BF16),
            struct(w_query.shape, BF16),
            struct((1, width), F32),
            struct(tables_shape, F32),
            struct((inbox, requests), BF16),
            struct((inbox, LANES), F32),
            struct(meta_shape, jnp.int32),
            struct((outgoing, columns, LANES), BF16),
            struct((outgoing * SLOT, LANES), jnp.int32),
            struct((outgoing, outgoing * SLOT), jnp.int32),
        ],
        [SMEM] + [HBM] * 7,
        [
            pltpu.VMEM((1, requests), jnp.int32),
            pltpu.VMEM((page_table.shape[1], requests), jnp.int32),
            pltpu.VMEM((1, outgoing), jnp.int32),
            pltpu.VMEM((width,), F32),
            pltpu.SemaphoreType.DMA((10,)),
        ],
        moved=2 * w_query.size,
    )(
        ids,
        pin(hidden),
        pin(ctx_len.reshape(1, requests)),
        pin(page_table.T),
        pin(move_dest.reshape(1, outgoing)),
        pin(attn_gain),
        pin(w_query),
        blocks,
    )
    if pair:
        pieces[0] = own
    hidden_all, normed, packed, sends = call(
        functools.partial(query_kernel, len(pieces)),
        [
            struct((requests, width), BF16),
            struct((requests, width), BF16),
            struct((requests * SLOT, LANES), F32),
            struct((inbox * SLOT, LANES), BF16),
        ],
        [VMEM] * (len(pieces) + 6),
        [
            pltpu.VMEM((requests * SLOT, LANES), F32),
            pltpu.VMEM((inbox * SLOT, LANES), F32),
        ],
        flops=4 * requests * width * w_query.shape[1],
        moved=2 * w_query.size,
    )(meta, *pieces, gain, wq, tables, away, away_span)
    asked = exchange(sends)
    replies, meta_far, packed_far, normed_far, tables_far, hidden_far = call(
        functools.partial(lent_kernel, heads, kv_local),
        [
            pltpu.HBM((inbox * SLOT, LANES), BF16),
            pltpu.HBM(meta_shape, jnp.int32),
            pltpu.HBM((requests * SLOT, LANES), F32),
            pltpu.HBM((requests, width), BF16),
            pltpu.HBM(tables_shape, F32),
            pltpu.HBM((requests, width), BF16),
        ],
        [VMEM] * 9,
        [
            pltpu.VMEM((inbox * SLOT, LANES), BF16),
            pltpu.SemaphoreType.DMA((6,)),
        ],
        flops=4 * ROWS * columns * LANES * outgoing,
        moved=2 * columns * LANES * outgoing,
    )(asked, lent, pick, drop, meta, packed, normed, tables, hidden_all)
    returned = exchange(replies)
    (state,) = call(
        functools.partial(local_kernel, heads, kv_local),
        [pltpu.HBM((requests, ROWS, LANES), F32)],
        [HBM] * 6,
        [
            pltpu.SMEM(meta_shape, jnp.int32),
            pltpu.VMEM((requests * SLOT, LANES), F32),
            pltpu.VMEM((requests, width), BF16),
            pltpu.VMEM((width * kv_local, LANES), BF16),
            pltpu.VMEM((width * kv_local, LANES), F32),
            pltpu.VMEM(tables_shape, F32),
            pltpu.VMEM((local_pages, columns, LANES), BF16),
            pltpu.VMEM((requests, ROWS, LANES), F32),
            pltpu.VMEM((requests * ROWS, LANES), F32),
            pltpu.VMEM((local_pages, ROWS, LANES), F32),
            pltpu.VMEM((local_pages, ROWS, LANES), F32),
            pltpu.VMEM((requests + 1, ROWS, LANES), F32),
            pltpu.VMEM((requests + 1, ROWS, LANES), F32),
            pltpu.VMEM((local_pages, ROWS, LANES), F32),
            pltpu.SemaphoreType.DMA((6 + local_pages,)),
        ],
        limit=24,
        flops=4 * ROWS * columns * LANES * local_pages,
        moved=2 * columns * LANES * local_pages,
    )(
        pin(meta_far),
        pin(packed_far),
        pin(normed_far),
        pin(w_keyvalue.reshape(width * kv_local, LANES)),
        pin(tables_far),
        blocks,
    )
    part, meta, hidden_all, gain, router_t, routes_t = call(
        functools.partial(combine_kernel, heads, pool),
        [
            struct((requests, width), BF16),
            struct(meta_shape, jnp.int32),
            struct((requests, width), BF16),
            struct((1, width), F32),
            struct(router.shape[::-1], BF16),
            struct(routes.shape[::-1], jnp.int32),
        ],
        [HBM] * 7 + [VMEM],
        [
            pltpu.SMEM(meta_shape, jnp.int32),
            pltpu.VMEM((requests, ROWS, LANES), F32),
            pltpu.VMEM(w_output.shape, BF16),
            pltpu.VMEM((width,), F32),
            pltpu.VMEM((requests + 1, ROWS, LANES), F32),
            pltpu.VMEM((requests + 1, ROWS, LANES), F32),
            pltpu.VMEM((inbox, ROWS, LANES), F32),
            pltpu.VMEM((inbox * SLOT, LANES), F32),
            pltpu.VMEM((requests * ROWS, LANES), F32),
            pltpu.SemaphoreType.DMA((11,)),
        ],
        flops=2 * requests * w_output.size,
        moved=2 * w_output.size,
    )(
        pin(meta_far), pin(state), pin(w_output), pin(hidden_far), pin(ffn_gain),
        pin(router.T), pin(routes.T), returned,
    )
    if pair:
        parts = [part, swap(part)]
    else:
        parts = [lax.all_gather(part, "tensor", axis=0, tiled=True)]
    (wd,) = call(
        load_kernel,
        [struct(w_down.shape, BF16)],
        [HBM, ANY],
        [pltpu.SemaphoreType.DMA((4,))],
        moved=2 * w_down.size,
    )(pin(w_down), part)
    attended, ffn_input, ffn_again = call(
        functools.partial(residual_kernel, tp, len(parts)),
        [
            struct((rows if pair else requests, width), BF16),
            struct((requests, width), BF16),
            struct((requests, width), BF16),
        ],
        [VMEM] * (len(parts) + 3),
        flops=2 * requests * width,
        moved=8 * requests * width,
    )(meta, hidden_all, *parts, gain)
    lifted = jnp.einsum("rd,dsu->sru", ffn_input, w_in, preferred_element_type=F32)
    shapes = [struct((requests, width), BF16)]
    if pair:
        shapes = [struct((rows, width), F32), struct((rows, width), BF16)]
    shares = call(
        functools.partial(expert_kernel, units),
        shapes,
        [VMEM] * 6,
        flops=2 * requests * w_down.size,
        moved=2 * w_down.size,
    )(meta, lifted, ffn_again, router_t, routes_t, wd)
    if pair:
        out = struct((rows, width), BF16)
        return tuple(
            call(finish_kernel, [out, out], [VMEM] * 3)(attended, shares[0], swap(shares[1]))
        )
    shares = lax.all_gather(shares[0], "tensor", axis=0)
    mine = lax.dynamic_slice_in_dim(shares, rank * rows, rows, axis=1)
    experts_out = jnp.sum(mine.astype(F32), axis=0).astype(BF16)
    attended = lax.dynamic_slice_in_dim(attended, rank * rows, rows, axis=0)
    return attended, experts_out


def solution(mesh):
    placed = (
        P(("replica", "tensor"), None),
        P(),
        P(None, "tensor"),
        P(None, "tensor", None),
        P("tensor", None),
        P("replica", None, "tensor", None),
        P("replica", None),
        P("replica"),
        P("replica"),
        P(),
        P(),
        P("replica", None),
        P(None, None, "tensor"),
        P("tensor", None),
    )
    return jax.shard_map(
        on_device,
        mesh=mesh,
        in_specs=placed,
        out_specs=(P(("replica", "tensor"), None), P(("replica", "tensor"), None)),
        check_vma=False,
    )
```

```python
import functools
import math

import jax
import jax.numpy as jnp
from jax import lax
from jax.experimental import pallas as pl
from jax.experimental.pallas import tpu as pltpu
from jax.sharding import PartitionSpec as P

HEAD_DIM = 64
EXPERTS = 40
FF = 512
CAP = 2
LANES = 128
SLOT = 8
ROWS = 16
META = 6

ATTN_SCALE = 0.015625
RESID_SCALE = 0.22
ROPE_BASE = 10000.0
EPSILON = 1e-06
NEG_FILL = -1e30

F32 = jnp.float32
BF16 = jnp.bfloat16
VMEM = pl.BlockSpec(memory_space=pltpu.VMEM)
SMEM = pl.BlockSpec(memory_space=pltpu.SMEM)
ANY = pl.BlockSpec(memory_space=pl.ANY)
HBM = pl.BlockSpec(memory_space=pltpu.HBM)
NT = (((1,), (1,)), ((), ()))


def iota(shape, axis):
    return lax.broadcasted_iota(jnp.int32, shape, axis)


def norm_rows(values, gain):
    factor = lax.rsqrt(jnp.mean(values * values, axis=-1, keepdims=True) + EPSILON)
    return (values * factor * gain).astype(BF16)


def rope_tables(ctx_row, requests):
    diagonal = iota((requests, requests), 0) == iota((requests, requests), 1)
    ctx = jnp.broadcast_to(ctx_row.astype(F32), (requests, requests))
    ctx = jnp.sum(jnp.where(diagonal, ctx, 0.0), axis=1, keepdims=True)
    lane = iota((requests, LANES), 1)
    index = (lane % (HEAD_DIM // 2)).astype(F32)
    inverse = jnp.exp(index * (-2.0 * math.log(ROPE_BASE) / HEAD_DIM))
    angles = ctx * inverse
    sign = jnp.where(lane % HEAD_DIM < HEAD_DIM // 2, -1.0, 1.0)
    return jnp.cos(angles), jnp.sin(angles) * sign


def rotate(chunk, cosine, sine):
    lane = iota(chunk.shape, 1)
    ahead = pltpu.roll(chunk, LANES - HEAD_DIM // 2, 1)
    behind = pltpu.roll(chunk, HEAD_DIM // 2, 1)
    turned = jnp.where(lane % HEAD_DIM < HEAD_DIM // 2, ahead, behind)
    return chunk * cosine + turned * sine


def copy_of(source, target, sem):
    return pltpu.make_async_copy(source, target, sem)


def copies_of(source, target, sems, base):
    step = source.shape[0] // 4
    return [
        copy_of(
            source.at[pl.ds(i * step, step)], target.at[pl.ds(i * step, step)], sems.at[base + i]
        )
        for i in range(4)
    ]


def page_copies(cache_hbm, first, pages, place, count, sems, base):
    return [
        copy_of(cache_hbm.at[first + p], pages.at[place + p], sems.at[base + p])
        for p in range(count)
    ]


def prepare_kernel(
    pool, replicas, ids_ref, hidden_hbm, ctx_hbm, table_hbm, dest_hbm, attn_gain_hbm,
    wq_hbm, cache_hbm,
    hidden_ref, wq_ref, gain_ref, tables_ref, away_ref, span_ref, meta_ref, lent_ref,
    pick_ref, drop_ref,
    ctx, table, dest, gain, sems,
):
    inbox = replicas * CAP
    requests = ctx.shape[1]
    entries = meta_ref.shape[1]
    small = [
        copy_of(ctx_hbm, ctx, sems.at[0]),
        copy_of(table_hbm, table, sems.at[1]),
        copy_of(dest_hbm, dest, sems.at[2]),
        copy_of(attn_gain_hbm, gain, sems.at[3]),
    ]
    large = [copy_of(hidden_hbm, hidden_ref, sems.at[4])]
    large += copies_of(wq_hbm, wq_ref, sems, 5)
    lending = pl.ds(pool - lent_ref.shape[0], lent_ref.shape[0])
    large.append(copy_of(cache_hbm.at[lending], lent_ref, sems.at[9]))
    for copy in small + large:
        copy.start()
    for copy in small:
        copy.wait()
    gain_ref[...] = gain[...].reshape(1, gain.shape[0])
    ctx_row = ctx[...]

    def claims(values):
        held = jnp.zeros(values.shape, F32)
        spans = jnp.zeros(values.shape, F32)
        for k in range(table.shape[0]):
            match = table[k : k + 1, :] == values
            filled = jnp.clip(ctx_row - k * 128, 0, 128).astype(F32)
            held = jnp.where(match, 1.0, held)
            spans = jnp.where(match, filled, spans)
        return held.astype(BF16), spans

    held, spans = claims(iota((entries, requests), 0))
    numbers = (iota((SLOT, requests), 1) + 1).astype(BF16)
    ones = jnp.ones((SLOT, requests), BF16)
    holder = lax.dot_general(numbers, held, NT, preferred_element_type=F32)
    covered = lax.dot_general(ones, spans.astype(BF16), NT, preferred_element_type=F32)
    meta_ref[0:1, :] = holder[0:1, :].astype(jnp.int32) - 1
    meta_ref[1:2, :] = covered[0:1, :].astype(jnp.int32)
    meta_ref[2:3, :] = jnp.zeros((1, entries), jnp.int32)
    lent = dest.shape[1]
    across = jnp.broadcast_to(dest[...].astype(F32), (lent, lent))
    row, lane = iota((lent, lent), 0), iota((lent, lent), 1)
    down = jnp.sum(jnp.where(row == lane, across, 0.0), axis=1, keepdims=True)
    same = across == down
    before = jnp.sum(jnp.where(same & (lane < row), 1.0, 0.0), axis=1, keepdims=True)
    column = (replicas - 1 - down) * CAP + before
    column = jnp.broadcast_to(column, (lent, LANES)).astype(BF16)
    before = jnp.sum(jnp.where(same & (row < lane), 1.0, 0.0), axis=0, keepdims=True)
    line = (across * CAP + before).astype(BF16)
    expand = iota((lent * SLOT, lent), 0) // SLOT == iota((lent * SLOT, lent), 1)
    expand = jnp.where(expand, 1.0, 0.0).astype(BF16)
    column = jnp.dot(expand, column, preferred_element_type=F32).astype(jnp.int32)
    pick_ref[...] = column * SLOT + iota(column.shape, 0) % SLOT
    line = lax.dot_general(line, expand, NT, preferred_element_type=F32).astype(jnp.int32)
    drop_ref[...] = line * SLOT + iota(line.shape, 1) % SLOT
    meta_ref[3:4, :] = jnp.full((1, entries), ids_ref[0], jnp.int32)
    cosine, sine = rope_tables(ctx_row, requests)
    tables_ref[0] = cosine
    tables_ref[1] = sine
    slot = iota((inbox, requests), 0)
    lender = replicas - 1 - slot // CAP
    held, spans = claims(pool + lender * CAP + slot % CAP)
    away_ref[...] = held
    away_span = jnp.sum(spans, axis=1, keepdims=True)
    span_ref[...] = jnp.broadcast_to(away_span, span_ref.shape)
    for copy in large:
        copy.wait()


def query_kernel(
    count, meta_ref, *refs,
):
    pieces = refs[:count]
    (gain_ref, wq_ref, tables_ref, away_ref, span_ref,
     hidden_ref, normed_ref, packed_ref, send_ref, packs, sends) = refs[count:]
    requests = hidden_ref.shape[0]
    inbox = span_ref.shape[0]
    width = wq_ref.shape[1]
    chunks = -(-width // LANES)
    if count == 1:
        hidden = pieces[0][...]
    else:
        own, other = pieces[0][...], pieces[1][...]
        first = meta_ref[3:4, 0:1] == 0
        hidden = jnp.concatenate(
            [jnp.where(first, own, other), jnp.where(first, other, own)], axis=0
        )
    hidden_ref[...] = hidden
    normed = norm_rows(hidden.astype(F32), gain_ref[...])
    normed_ref[...] = normed
    queries = jnp.dot(normed, wq_ref[...], preferred_element_type=F32)
    if chunks * LANES > width:
        pad = jnp.zeros((requests, chunks * LANES - width), F32)
        queries = jnp.concatenate([queries, pad], axis=1)
    cosine, sine = tables_ref[0], tables_ref[1]
    zeros = jnp.zeros((requests, LANES), F32)
    nothing = jnp.zeros((inbox, LANES), F32)
    for j in range(SLOT):
        here = pl.ds(j, requests, stride=SLOT)
        there = pl.ds(j, inbox, stride=SLOT)
        if j < chunks:
            chunk = rotate(queries[:, j * LANES : (j + 1) * LANES], cosine, sine)
            chunk = (chunk.astype(BF16).astype(F32) * ATTN_SCALE).astype(BF16)
            packs[here, :] = chunk.astype(F32)
            sends[there, :] = jnp.dot(away_ref[...], chunk, preferred_element_type=F32)
        else:
            packs[here, :] = zeros
            sends[there, :] = span_ref[...] if j == META else nothing
    packed_ref[...] = packs[...]
    send_ref[...] = sends[...].astype(BF16)


def unpack(packed):
    low = iota(packed.shape, 1) < HEAD_DIM
    even = jnp.where(low, packed, 0.0)
    odd = jnp.where(low, pltpu.roll(packed, HEAD_DIM, 1), 0.0)
    return jnp.concatenate([even, odd], axis=0)


def head_rows(heads):
    return [(h // 2) + SLOT * (h % 2) for h in range(heads)]


def token_of_column(heads, kv_local, columns):
    row = iota((ROWS, columns), 0)
    column = iota((ROWS, columns), 1)
    wanted = jnp.full((ROWS, columns), kv_local, jnp.int32)
    for h, place in enumerate(head_rows(heads)):
        wanted = jnp.where(row == place, h // (heads // kv_local), wanted)
    return jnp.where(column % kv_local == wanted, column // kv_local, 1 << 20)


def score_page(query, block):
    return lax.dot_general(query, block, NT, preferred_element_type=F32)


def weigh_page(scores, tokens, span):
    scores = jnp.where(tokens < span, scores, NEG_FILL)
    top = jnp.max(scores, axis=1, keepdims=True)
    weights = jnp.exp(scores - top)
    return top, jnp.sum(weights, axis=1, keepdims=True), weights.astype(BF16)


def attend_pages(count, stage, copies, query_of, block_of, span_of, tokens, keep):
    stages = [range(i, min(i + stage, count)) for i in range(0, count, stage)]

    def score_stage(pages):
        for p in pages:
            if copies is not None:
                copies[p].wait()
        return {p: score_page(query_of(p), block_of(p)) for p in pages}

    scores = score_stage(stages[0])
    for i, pages in enumerate(stages):
        if i + 1 < len(stages):
            ahead = score_stage(stages[i + 1])
        weighed = {p: weigh_page(scores[p], tokens, span_of(p)) for p in pages}
        outs = {
            p: jnp.dot(weighed[p][2], block_of(p), preferred_element_type=F32)
            for p in pages
        }
        for p in pages:
            keep(p, weighed[p][0], weighed[p][1], outs[p])
        if i + 1 < len(stages):
            scores = ahead


def spread_queries(target, packed):
    low = iota(packed.shape, 2) < HEAD_DIM
    target[:, 0:SLOT, :] = jnp.where(low, packed, 0.0)
    target[:, SLOT:ROWS, :] = jnp.where(low, pltpu.roll(packed, HEAD_DIM, 2), 0.0)


def merge_pages(places, top_of, sum_of, top, acc, scaled, start, before):
    requests = start.shape[0]
    for p, place in enumerate(places):
        top[place] = jnp.maximum(top[place], top_of(p))
    acc[0:requests] = start * jnp.exp(before - top[0:requests])
    for p, place in enumerate(places):
        scaled[p] = sum_of(p) * jnp.exp(top_of(p) - top[place])
    for p, place in enumerate(places):
        acc[place] = acc[place] + scaled[p]


def local_kernel(
    heads, kv_local, meta_hbm, packed_hbm, normed_hbm, wkv_hbm, tables_hbm, cache_hbm,
    state_hbm,
    meta, packed, normed, raw, wide, tables, pages, queries, fresh, tops, sums, top,
    acc, scaled, sems,
):
    requests, depth = normed.shape
    count, columns, _ = pages.shape
    small = [
        copy_of(meta_hbm, meta, sems.at[0]),
        copy_of(packed_hbm, packed, sems.at[1]),
        copy_of(normed_hbm, normed, sems.at[2]),
        copy_of(tables_hbm, tables, sems.at[3]),
    ]
    weights = copy_of(wkv_hbm, raw, sems.at[4])
    paging = page_copies(cache_hbm, 0, pages, 0, count, sems, 6)
    for copy in small + paging + [weights]:
        copy.start()
    for copy in small:
        copy.wait()
    spread_queries(queries, packed[...].reshape(requests, SLOT, LANES))
    tokens = token_of_column(heads, kv_local, columns)
    lower = iota((ROWS, LANES), 1) < HEAD_DIM
    low = iota((requests, LANES), 1) < HEAD_DIM
    cosine = jnp.where(low, tables[0], 1.0)
    sine = jnp.where(low, tables[1], 0.0)

    def keep(p, page_top, total, out):
        tops[p] = jnp.broadcast_to(page_top, (ROWS, LANES))
        sums[p] = jnp.where(lower, total, out)

    attend_pages(
        count,
        4,
        paging,
        lambda p: queries[jnp.maximum(meta[0, p], 0)].astype(BF16),
        lambda p: pages[p],
        lambda p: meta[1, p],
        tokens,
        keep,
    )
    weights.wait()
    if kv_local > 1:
        wide[...] = raw[...].astype(F32)
    new = []
    for k in range(kv_local):
        if kv_local > 1:
            weight = wide[pl.ds(k, depth, stride=kv_local), :].astype(BF16)
        else:
            weight = raw[...]
        projected = jnp.dot(normed[...], weight, preferred_element_type=F32)
        new.append(rotate(projected, cosine, sine).astype(BF16).astype(F32))
    used = {place: h for h, place in enumerate(head_rows(heads))}
    for place in range(ROWS):
        value = jnp.zeros((requests, LANES), F32)
        if place in used:
            value = new[used[place] // (heads // kv_local)]
        fresh[pl.ds(place, requests, stride=ROWS), :] = value

    added = fresh[...].reshape(requests, ROWS, LANES)
    low16 = iota(added.shape, 2) < HEAD_DIM
    score = jnp.sum(queries[...] * added, axis=2, keepdims=True)
    before = jnp.broadcast_to(score, added.shape)
    start = jnp.where(low16, 1.0, added)
    top[0:requests] = before

    def place_of(p):
        owner = meta[0, p]
        return jnp.where(owner < 0, requests, owner)

    merge_pages(
        [place_of(p) for p in range(count)],
        lambda p: tops[p],
        lambda p: sums[p],
        top,
        acc,
        scaled,
        start,
        before,
    )
    whole = acc[0:requests]
    acc[0:requests] = jnp.where(
        low16, top[0:requests] + jnp.log(whole), whole / pltpu.roll(whole, HEAD_DIM, 2)
    )
    parked = copy_of(acc.at[pl.ds(0, requests)], state_hbm, sems.at[5])
    parked.start()
    parked.wait()


def lent_kernel(
    heads, kv_local, asked_ref, pages, pick_ref, drop_ref, meta_ref, packed_ref,
    normed_ref, tables_ref, hidden_ref,
    reply_hbm, meta_hbm, packed_hbm, normed_hbm, tables_hbm, hidden_hbm,
    reply16, sems,
):
    outgoing, columns, _ = pages.shape
    parked = [
        copy_of(packed_ref, packed_hbm, sems.at[0]),
        copy_of(normed_ref, normed_hbm, sems.at[1]),
        copy_of(hidden_ref, hidden_hbm, sems.at[2]),
        copy_of(tables_ref, tables_hbm, sems.at[3]),
        copy_of(meta_ref, meta_hbm, sems.at[4]),
    ]
    for copy in parked:
        copy.start()
    slot_rows = asked_ref.shape[0]
    shape = (outgoing * SLOT, slot_rows)
    chosen = jnp.where(pick_ref[:, 0:1] == iota(shape, 1), 1.0, 0.0).astype(BF16)
    asked = jnp.dot(chosen, asked_ref[...], preferred_element_type=F32)
    tokens = token_of_column(heads, kv_local, columns).astype(F32)
    low = iota((SLOT, LANES), 1) < HEAD_DIM
    lane = iota((SLOT, LANES), 1)
    row = iota((SLOT, LANES), 0)

    def terms(total, offset):
        leading = total.astype(BF16).astype(F32)
        rest = total - leading
        second = rest.astype(BF16).astype(F32)
        third = rest - second
        spot = lane - offset - 3 * row
        placed = jnp.where(spot == 0, leading, 0.0)
        placed = jnp.where(spot == 1, second, placed)
        return jnp.where(spot == 2, third, placed)

    packed = [asked[j * SLOT : (j + 1) * SLOT] for j in range(outgoing)]
    replies = {}

    def keep(j, top, total, out):
        out = out / total
        logs = top + jnp.log(total)
        even = pltpu.roll(out[0:SLOT], HEAD_DIM, 1)
        both = jnp.where(low, even, out[SLOT:ROWS])
        line = jnp.sum(
            terms(logs[0:SLOT], 0) + terms(logs[SLOT:ROWS], HEAD_DIM), axis=0, keepdims=True
        )
        replies[j] = jnp.where(row == META, line, both)

    attend_pages(
        outgoing,
        8,
        None,
        lambda j: unpack(packed[j]).astype(BF16),
        lambda j: pages[j],
        lambda j: packed[j][META : META + 1, 0:1],
        tokens,
        keep,
    )
    shape = (slot_rows, outgoing * SLOT)
    placed = jnp.where(drop_ref[0:1, :] == iota(shape, 0), 1.0, 0.0).astype(BF16)
    every = jnp.concatenate([replies[j] for j in range(outgoing)], axis=0).astype(BF16)
    reply = jnp.dot(placed, every, preferred_element_type=F32)
    reply16[...] = reply.astype(BF16)
    replying = copy_of(reply16, reply_hbm, sems.at[5])
    replying.start()
    for copy in parked + [replying]:
        copy.wait()


def combine_kernel(
    heads, pool, meta_hbm, state_hbm, wo_hbm, hidden_hbm, gain_hbm, router_hbm,
    routes_hbm, reply_ref,
    part_ref, meta_ref, hidden_ref, gain_ref, router_ref, routes_ref,
    meta, state, wo, gain, tops, accs, scaled, reply, finals, sems,
):
    requests = state.shape[0]
    inbox = reply_ref.shape[0] // SLOT
    chunks = -(-heads // 2)
    small = [
        copy_of(meta_hbm, meta, sems.at[0]),
        copy_of(state_hbm, state, sems.at[1]),
    ]
    weights = copies_of(wo_hbm, wo, sems, 2)
    gaining = copy_of(gain_hbm, gain, sems.at[6])
    later = [
        copy_of(meta_hbm, meta_ref, sems.at[7]),
        copy_of(hidden_hbm, hidden_ref, sems.at[8]),
        copy_of(router_hbm, router_ref, sems.at[9]),
        copy_of(routes_hbm, routes_ref, sems.at[10]),
    ]
    for copy in small + weights + [gaining] + later:
        copy.start()
    reply[...] = reply_ref[...].astype(F32)
    low = iota((SLOT, LANES), 1) < HEAD_DIM
    lane = iota((SLOT, LANES), 1)
    row = iota((SLOT, LANES), 0)
    mine = (lane % HEAD_DIM) // 3 == row

    def place_of(s):
        owner = meta[0, pool + s]
        return jnp.where(owner < 0, requests, owner)

    def logs_of(s):
        line = reply[s * SLOT + META : s * SLOT + META + 1, :]
        line = jnp.where(mine, jnp.broadcast_to(line, (SLOT, LANES)), 0.0)
        even = jnp.sum(jnp.where(low, line, 0.0), axis=1, keepdims=True)
        odd = jnp.sum(jnp.where(low, 0.0, line), axis=1, keepdims=True)
        logs = jnp.concatenate([even, odd], axis=0)
        return jnp.broadcast_to(logs, (ROWS, LANES))

    logs = [logs_of(s) for s in range(inbox)]
    for copy in small:
        copy.wait()
    low16 = iota(state.shape, 2) < HEAD_DIM
    start = state[...]
    before = jnp.where(low16, start, pltpu.roll(start, HEAD_DIM, 2))
    tops[0:requests] = before

    def sum_of(s):
        packed = reply[s * SLOT : (s + 1) * SLOT, :]
        even = jnp.where(low, 1.0, pltpu.roll(packed, HEAD_DIM, 1))
        odd = jnp.where(low, 1.0, packed)
        return jnp.concatenate([even, odd], axis=0)

    merge_pages(
        [place_of(s) for s in range(inbox)],
        lambda s: logs[s],
        sum_of,
        tops,
        accs,
        scaled,
        jnp.where(low16, 1.0, start),
        before,
    )
    whole = accs[0:requests]
    finals[...] = (whole / pltpu.roll(whole, HEAD_DIM, 2)).reshape(
        requests * ROWS, LANES
    )
    wide = iota((requests, LANES), 1) < HEAD_DIM
    parts = []
    for j in range(chunks):
        even = finals[pl.ds(j, requests, stride=ROWS), :]
        odd = finals[pl.ds(SLOT + j, requests, stride=ROWS), :]
        parts.append(jnp.where(wide, pltpu.roll(even, HEAD_DIM, 1), odd).astype(BF16))
    attention = jnp.concatenate(parts, axis=1)[:, : heads * HEAD_DIM]
    for copy in weights:
        copy.wait()
    part_ref[...] = jnp.dot(attention, wo[...], preferred_element_type=F32).astype(BF16)
    gaining.wait()
    gain_ref[...] = gain[...].reshape(1, gain.shape[0])
    for copy in later:
        copy.wait()


def load_kernel(wd_hbm, order_hbm, wd_ref, sems):
    del order_hbm
    copies = copies_of(wd_hbm, wd_ref, sems, 0)
    for copy in copies:
        copy.start()
    for copy in copies:
        copy.wait()


def finish_kernel(attended_ref, own_ref, other_ref, attended_out, experts_out):
    attended_out[...] = attended_ref[...]
    experts_out[...] = (own_ref[...] + other_ref[...].astype(F32)).astype(BF16)


def own_rows(values, first):
    half = values.shape[0] // 2
    return jnp.where(first, values[:half], values[half:])


def residual_kernel(
    tp, count, meta_ref, hidden_ref, *refs,
):
    pieces = refs[:count]
    gain_ref, attended_ref, input_ref, again_ref = refs[count:]
    requests = hidden_ref.shape[0]
    if count == 2:
        summed = pieces[0][...].astype(F32) + pieces[1][...].astype(F32)
    else:
        summed = pieces[0][0:requests, :].astype(F32)
        for t in range(1, tp):
            part = pieces[0][t * requests : (t + 1) * requests, :]
            summed = summed + part.astype(F32)
    attended = (hidden_ref[...].astype(F32) + RESID_SCALE * summed).astype(BF16)
    if count == 2:
        attended_ref[...] = own_rows(attended, meta_ref[3:4, 0:1] == 0)
    else:
        attended_ref[...] = attended
    ffn_input = norm_rows(attended.astype(F32), gain_ref[...])
    input_ref[...] = ffn_input
    again_ref[...] = ffn_input


def gate_column(units, meta_ref, input_ref, router_ref, routes_ref):
    ffn_input = input_ref[...]
    requests = ffn_input.shape[0]
    logits = lax.dot_general(router_ref[...], ffn_input, NT, preferred_element_type=F32)
    expert = iota(logits.shape, 0)
    named = jnp.zeros(logits.shape, F32)
    for k in range(routes_ref.shape[0]):
        named = jnp.where(routes_ref[k : k + 1, :] == expert, 1.0, named)
    chosen = named > 0.5
    top = jnp.max(jnp.where(chosen, logits, NEG_FILL), axis=0, keepdims=True)
    weights = jnp.where(chosen, jnp.exp(logits - top), 0.0)
    total = jnp.sum(weights, axis=0, keepdims=True)
    mine = expert == meta_ref[3:4, 0:1] * units // FF
    line = jnp.sum(jnp.where(mine, weights, 0.0), axis=0, keepdims=True) / total
    diagonal = iota((requests, requests), 0) == iota((requests, requests), 1)
    line = jnp.where(diagonal, jnp.broadcast_to(line, (requests, requests)), 0.0)
    return jnp.sum(line, axis=1, keepdims=True)


def expert_kernel(
    units, meta_ref, lifted_ref, input_ref, router_ref, routes_ref, wd_ref, *outs
):
    column = gate_column(units, meta_ref, input_ref, router_ref, routes_ref)
    gate = lifted_ref[0]
    active = gate / (1.0 + jnp.exp(-gate)) * lifted_ref[1] * column
    share = jnp.dot(active.astype(BF16), wd_ref[...], preferred_element_type=F32)
    if len(outs) == 2:
        first = meta_ref[3:4, 0:1] == 0
        outs[0][...] = own_rows(share, first)
        outs[1][...] = own_rows(share, jnp.logical_not(first)).astype(BF16)
    else:
        outs[0][...] = share.astype(BF16)


def call(body, outs, in_specs, scratch=(), limit=16, flops=0, moved=0):
    return pl.pallas_call(
        body,
        out_shape=outs,
        in_specs=in_specs,
        out_specs=[VMEM if isinstance(o, jax.ShapeDtypeStruct) else HBM for o in outs],
        scratch_shapes=list(scratch),
        compiler_params=pltpu.CompilerParams(vmem_limit_bytes=limit << 20),
        cost_estimate=pl.CostEstimate(
            flops=flops, bytes_accessed=moved, transcendentals=0
        ),
    )


def swap(values):
    return lax.ppermute(values, "tensor", [(0, 1), (1, 0)])


def on_device(
    hidden,
    attn_gain,
    w_query,
    w_keyvalue,
    w_output,
    cache,
    page_table,
    ctx_len,
    move_dest,
    ffn_gain,
    router,
    routes,
    w_in,
    w_down,
):
    replicas = lax.axis_size("replica")
    tp = lax.axis_size("tensor")
    rank = lax.axis_index("tensor").astype(jnp.int32)
    rows, width = hidden.shape
    pool, page_len, kv_local, _ = cache.shape
    outgoing = move_dest.shape[0]
    local_pages = pool - outgoing
    requests = page_table.shape[0]
    heads = w_query.shape[1] // HEAD_DIM
    inbox = replicas * CAP
    units = w_down.shape[0]
    assert FF % units == 0
    columns = page_len * kv_local
    entries = -(-(pool + inbox) // LANES) * LANES
    struct = jax.ShapeDtypeStruct
    pair = tp == 2
    ids = rank.reshape(1)

    def pin(values):
        return pltpu.with_memory_space_constraint(values, pltpu.HBM)

    def exchange(blocks, order):
        blocks = blocks.reshape(replicas, CAP * SLOT, LANES)
        blocks = lax.all_to_all(
            blocks,
            "replica",
            split_axis=0,
            concat_axis=0,
            tiled=True,
            axis_index_groups=[list(order)],
        )
        return blocks.reshape(inbox * SLOT, LANES)

    blocks = pin(cache.reshape(pool, columns, LANES))
    if pair:
        pieces = [hidden, swap(hidden)]
    else:
        pieces = [lax.all_gather(hidden, "tensor", axis=0, tiled=True)]
    meta_shape = (4, entries)
    tables_shape = (2, requests, LANES)
    own, wq, gain, tables, away, away_span, meta, lent, pick, drop = call(
        functools.partial(prepare_kernel, pool, replicas),
        [
            struct(hidden.shape, BF16),
            struct(w_query.shape, BF16),
            struct((1, width), F32),
            struct(tables_shape, F32),
            struct((inbox, requests), BF16),
            struct((inbox, LANES), F32),
            struct(meta_shape, jnp.int32),
            struct((outgoing, columns, LANES), BF16),
            struct((outgoing * SLOT, LANES), jnp.int32),
            struct((outgoing, outgoing * SLOT), jnp.int32),
        ],
        [SMEM] + [HBM] * 7,
        [
            pltpu.VMEM((1, requests), jnp.int32),
            pltpu.VMEM((page_table.shape[1], requests), jnp.int32),
            pltpu.VMEM((1, outgoing), jnp.int32),
            pltpu.VMEM((width,), F32),
            pltpu.SemaphoreType.DMA((10,)),
        ],
        moved=2 * w_query.size,
    )(
        ids,
        pin(hidden),
        pin(ctx_len.reshape(1, requests)),
        pin(page_table.T),
        pin(move_dest.reshape(1, outgoing)),
        pin(attn_gain),
        pin(w_query),
        blocks,
    )
    if pair:
        pieces[0] = own
    hidden_all, normed, packed, sends = call(
        functools.partial(query_kernel, len(pieces)),
        [
            struct((requests, width), BF16),
            struct((requests, width), BF16),
            struct((requests * SLOT, LANES), F32),
            struct((inbox * SLOT, LANES), BF16),
        ],
        [VMEM] * (len(pieces) + 6),
        [
            pltpu.VMEM((requests * SLOT, LANES), F32),
            pltpu.VMEM((inbox * SLOT, LANES), F32),
        ],
        flops=4 * requests * width * w_query.shape[1],
        moved=2 * w_query.size,
    )(meta, *pieces, gain, wq, tables, away, away_span)
    asked = exchange(sends, range(replicas)[::-1])
    replies, meta_far, packed_far, normed_far, tables_far, hidden_far = call(
        functools.partial(lent_kernel, heads, kv_local),
        [
            pltpu.HBM((inbox * SLOT, LANES), BF16),
            pltpu.HBM(meta_shape, jnp.int32),
            pltpu.HBM((requests * SLOT, LANES), F32),
            pltpu.HBM((requests, width), BF16),
            pltpu.HBM(tables_shape, F32),
            pltpu.HBM((requests, width), BF16),
        ],
        [VMEM] * 9,
        [
            pltpu.VMEM((inbox * SLOT, LANES), BF16),
            pltpu.SemaphoreType.DMA((6,)),
        ],
        flops=4 * ROWS * columns * LANES * outgoing,
        moved=2 * columns * LANES * outgoing,
    )(asked, lent, pick, drop, meta, packed, normed, tables, hidden_all)
    returned = exchange(replies, range(replicas))
    (state,) = call(
        functools.partial(local_kernel, heads, kv_local),
        [pltpu.HBM((requests, ROWS, LANES), F32)],
        [HBM] * 6,
        [
            pltpu.SMEM(meta_shape, jnp.int32),
            pltpu.VMEM((requests * SLOT, LANES), F32),
            pltpu.VMEM((requests, width), BF16),
            pltpu.VMEM((width * kv_local, LANES), BF16),
            pltpu.VMEM((width * kv_local, LANES), F32),
            pltpu.VMEM(tables_shape, F32),
            pltpu.VMEM((local_pages, columns, LANES), BF16),
            pltpu.VMEM((requests, ROWS, LANES), F32),
            pltpu.VMEM((requests * ROWS, LANES), F32),
            pltpu.VMEM((local_pages, ROWS, LANES), F32),
            pltpu.VMEM((local_pages, ROWS, LANES), F32),
            pltpu.VMEM((requests + 1, ROWS, LANES), F32),
            pltpu.VMEM((requests + 1, ROWS, LANES), F32),
            pltpu.VMEM((local_pages, ROWS, LANES), F32),
            pltpu.SemaphoreType.DMA((6 + local_pages,)),
        ],
        limit=24,
        flops=4 * ROWS * columns * LANES * local_pages,
        moved=2 * columns * LANES * local_pages,
    )(
        pin(meta_far),
        pin(packed_far),
        pin(normed_far),
        pin(w_keyvalue.reshape(width * kv_local, LANES)),
        pin(tables_far),
        blocks,
    )
    part, meta, hidden_all, gain, router_t, routes_t = call(
        functools.partial(combine_kernel, heads, pool),
        [
            struct((requests, width), BF16),
            struct(meta_shape, jnp.int32),
            struct((requests, width), BF16),
            struct((1, width), F32),
            struct(router.shape[::-1], BF16),
            struct(routes.shape[::-1], jnp.int32),
        ],
        [HBM] * 7 + [VMEM],
        [
            pltpu.SMEM(meta_shape, jnp.int32),
            pltpu.VMEM((requests, ROWS, LANES), F32),
            pltpu.VMEM(w_output.shape, BF16),
            pltpu.VMEM((width,), F32),
            pltpu.VMEM((requests + 1, ROWS, LANES), F32),
            pltpu.VMEM((requests + 1, ROWS, LANES), F32),
            pltpu.VMEM((inbox, ROWS, LANES), F32),
            pltpu.VMEM((inbox * SLOT, LANES), F32),
            pltpu.VMEM((requests * ROWS, LANES), F32),
            pltpu.SemaphoreType.DMA((11,)),
        ],
        flops=2 * requests * w_output.size,
        moved=2 * w_output.size,
    )(
        pin(meta_far), pin(state), pin(w_output), pin(hidden_far), pin(ffn_gain),
        pin(router.T), pin(routes.T), returned,
    )
    if pair:
        parts = [part, swap(part)]
    else:
        parts = [lax.all_gather(part, "tensor", axis=0, tiled=True)]
    (wd,) = call(
        load_kernel,
        [struct(w_down.shape, BF16)],
        [HBM, ANY],
        [pltpu.SemaphoreType.DMA((4,))],
        moved=2 * w_down.size,
    )(pin(w_down), part)
    attended, ffn_input, ffn_again = call(
        functools.partial(residual_kernel, tp, len(parts)),
        [
            struct((rows if pair else requests, width), BF16),
            struct((requests, width), BF16),
            struct((requests, width), BF16),
        ],
        [VMEM] * (len(parts) + 3),
        flops=2 * requests * width,
        moved=8 * requests * width,
    )(meta, hidden_all, *parts, gain)
    lifted = jnp.einsum("rd,dsu->sru", ffn_input, w_in, preferred_element_type=F32)
    shapes = [struct((requests, width), BF16)]
    if pair:
        shapes = [struct((rows, width), F32), struct((rows, width), BF16)]
    shares = call(
        functools.partial(expert_kernel, units),
        shapes,
        [VMEM] * 6,
        flops=2 * requests * w_down.size,
        moved=2 * w_down.size,
    )(meta, lifted, ffn_again, router_t, routes_t, wd)
    if pair:
        out = struct((rows, width), BF16)
        return tuple(
            call(finish_kernel, [out, out], [VMEM] * 3)(attended, shares[0], swap(shares[1]))
        )
    shares = lax.all_gather(shares[0], "tensor", axis=0)
    mine = lax.dynamic_slice_in_dim(shares, rank * rows, rows, axis=1)
    experts_out = jnp.sum(mine.astype(F32), axis=0).astype(BF16)
    attended = lax.dynamic_slice_in_dim(attended, rank * rows, rows, axis=0)
    return attended, experts_out


def solution(mesh):
    placed = (
        P(("replica", "tensor"), None),
        P(),
        P(None, "tensor"),
        P(None, "tensor", None),
        P("tensor", None),
        P("replica", None, "tensor", None),
        P("replica", None),
        P("replica"),
        P("replica"),
        P(),
        P(),
        P("replica", None),
        P(None, None, "tensor"),
        P("tensor", None),
    )
    return jax.shard_map(
        on_device,
        mesh=mesh,
        in_specs=placed,
        out_specs=(P(("replica", "tensor"), None), P(("replica", "tensor"), None)),
        check_vma=False,
    )
```

```python
import functools
import math

import jax
import jax.numpy as jnp
from jax import lax
from jax.experimental import pallas as pl
from jax.experimental.pallas import tpu as pltpu
from jax.sharding import PartitionSpec as P

HEAD_DIM = 64
EXPERTS = 40
FF = 512
CAP = 2
LANES = 128
SLOT = 8
ROWS = 16
META = 6

ATTN_SCALE = 0.015625
RESID_SCALE = 0.22
ROPE_BASE = 10000.0
EPSILON = 1e-06
NEG_FILL = -1e30

F32 = jnp.float32
BF16 = jnp.bfloat16
VMEM = pl.BlockSpec(memory_space=pltpu.VMEM)
SMEM = pl.BlockSpec(memory_space=pltpu.SMEM)
ANY = pl.BlockSpec(memory_space=pl.ANY)
HBM = pl.BlockSpec(memory_space=pltpu.HBM)
NT = (((1,), (1,)), ((), ()))


def iota(shape, axis):
    return lax.broadcasted_iota(jnp.int32, shape, axis)


def norm_rows(values, gain):
    factor = lax.rsqrt(jnp.mean(values * values, axis=-1, keepdims=True) + EPSILON)
    return (values * factor * gain).astype(BF16)


def rope_tables(ctx_row, requests):
    diagonal = iota((requests, requests), 0) == iota((requests, requests), 1)
    ctx = jnp.broadcast_to(ctx_row.astype(F32), (requests, requests))
    ctx = jnp.sum(jnp.where(diagonal, ctx, 0.0), axis=1, keepdims=True)
    lane = iota((requests, LANES), 1)
    index = (lane % (HEAD_DIM // 2)).astype(F32)
    inverse = jnp.exp(index * (-2.0 * math.log(ROPE_BASE) / HEAD_DIM))
    angles = ctx * inverse
    sign = jnp.where(lane % HEAD_DIM < HEAD_DIM // 2, -1.0, 1.0)
    return jnp.cos(angles), jnp.sin(angles) * sign


def rotate(chunk, cosine, sine):
    lane = iota(chunk.shape, 1)
    ahead = pltpu.roll(chunk, LANES - HEAD_DIM // 2, 1)
    behind = pltpu.roll(chunk, HEAD_DIM // 2, 1)
    turned = jnp.where(lane % HEAD_DIM < HEAD_DIM // 2, ahead, behind)
    return chunk * cosine + turned * sine


def copy_of(source, target, sem):
    return pltpu.make_async_copy(source, target, sem)


def copies_of(source, target, sems, base):
    step = source.shape[0] // 4
    return [
        copy_of(
            source.at[pl.ds(i * step, step)], target.at[pl.ds(i * step, step)], sems.at[base + i]
        )
        for i in range(4)
    ]


def page_copies(cache_hbm, first, pages, place, count, sems, base):
    return [
        copy_of(cache_hbm.at[first + p], pages.at[place + p], sems.at[base + p])
        for p in range(count)
    ]


def prepare_kernel(
    pool, replicas, ids_ref, hidden_hbm, ctx_hbm, table_hbm, dest_hbm, attn_gain_hbm,
    wq_hbm, cache_hbm,
    hidden_ref, wq_ref, gain_ref, tables_ref, away_ref, span_ref, meta_ref, lent_ref,
    pick_ref, drop_ref,
    ctx, table, dest, gain, sems,
):
    inbox = replicas * CAP
    requests = ctx.shape[1]
    entries = meta_ref.shape[1]
    small = [
        copy_of(ctx_hbm, ctx, sems.at[0]),
        copy_of(table_hbm, table, sems.at[1]),
        copy_of(dest_hbm, dest, sems.at[2]),
        copy_of(attn_gain_hbm, gain, sems.at[3]),
    ]
    large = [copy_of(hidden_hbm, hidden_ref, sems.at[4])]
    large += copies_of(wq_hbm, wq_ref, sems, 5)
    lending = pl.ds(pool - lent_ref.shape[0], lent_ref.shape[0])
    large.append(copy_of(cache_hbm.at[lending], lent_ref, sems.at[9]))
    for copy in small + large:
        copy.start()
    for copy in small:
        copy.wait()
    gain_ref[...] = gain[...].reshape(1, gain.shape[0])
    ctx_row = ctx[...]

    def claims(values):
        held = jnp.zeros(values.shape, F32)
        spans = jnp.zeros(values.shape, F32)
        for k in range(table.shape[0]):
            match = table[k : k + 1, :] == values
            filled = jnp.clip(ctx_row - k * 128, 0, 128).astype(F32)
            held = jnp.where(match, 1.0, held)
            spans = jnp.where(match, filled, spans)
        return held.astype(BF16), spans

    held, spans = claims(iota((entries, requests), 0))
    numbers = (iota((SLOT, requests), 1) + 1).astype(BF16)
    ones = jnp.ones((SLOT, requests), BF16)
    holder = lax.dot_general(numbers, held, NT, preferred_element_type=F32)
    covered = lax.dot_general(ones, spans.astype(BF16), NT, preferred_element_type=F32)
    meta_ref[0:1, :] = holder[0:1, :].astype(jnp.int32) - 1
    meta_ref[1:2, :] = covered[0:1, :].astype(jnp.int32)
    meta_ref[2:3, :] = jnp.zeros((1, entries), jnp.int32)
    lent = dest.shape[1]
    across = jnp.broadcast_to(dest[...].astype(F32), (lent, lent))
    row, lane = iota((lent, lent), 0), iota((lent, lent), 1)
    down = jnp.sum(jnp.where(row == lane, across, 0.0), axis=1, keepdims=True)
    same = across == down
    before = jnp.sum(jnp.where(same & (lane < row), 1.0, 0.0), axis=1, keepdims=True)
    column = (replicas - 1 - down) * CAP + before
    column = jnp.broadcast_to(column, (lent, LANES)).astype(BF16)
    before = jnp.sum(jnp.where(same & (row < lane), 1.0, 0.0), axis=0, keepdims=True)
    line = dest[...] ^ replicas // 2
    line = jnp.broadcast_to(line.astype(F32), (lent, lent))
    line = (line * CAP + before).astype(BF16)
    expand = iota((lent * SLOT, lent), 0) // SLOT == iota((lent * SLOT, lent), 1)
    expand = jnp.where(expand, 1.0, 0.0).astype(BF16)
    column = jnp.dot(expand, column, preferred_element_type=F32).astype(jnp.int32)
    pick_ref[...] = column * SLOT + iota(column.shape, 0) % SLOT
    line = lax.dot_general(line, expand, NT, preferred_element_type=F32).astype(jnp.int32)
    drop_ref[...] = line * SLOT + iota(line.shape, 1) % SLOT
    meta_ref[3:4, :] = jnp.full((1, entries), ids_ref[0], jnp.int32)
    cosine, sine = rope_tables(ctx_row, requests)
    tables_ref[0] = cosine
    tables_ref[1] = sine
    slot = iota((inbox, requests), 0)
    lender = replicas - 1 - slot // CAP
    held, spans = claims(pool + lender * CAP + slot % CAP)
    away_ref[...] = held
    away_span = jnp.sum(spans, axis=1, keepdims=True)
    span_ref[...] = jnp.broadcast_to(away_span, span_ref.shape)
    for copy in large:
        copy.wait()


def query_kernel(
    count, meta_ref, *refs,
):
    pieces = refs[:count]
    (gain_ref, wq_ref, tables_ref, away_ref, span_ref,
     hidden_ref, normed_ref, packed_ref, send_ref, packs, sends) = refs[count:]
    requests = hidden_ref.shape[0]
    inbox = span_ref.shape[0]
    width = wq_ref.shape[1]
    chunks = -(-width // LANES)
    if count == 1:
        hidden = pieces[0][...]
    else:
        own, other = pieces[0][...], pieces[1][...]
        first = meta_ref[3:4, 0:1] == 0
        hidden = jnp.concatenate(
            [jnp.where(first, own, other), jnp.where(first, other, own)], axis=0
        )
    hidden_ref[...] = hidden
    normed = norm_rows(hidden.astype(F32), gain_ref[...])
    normed_ref[...] = normed
    queries = jnp.dot(normed, wq_ref[...], preferred_element_type=F32)
    if chunks * LANES > width:
        pad = jnp.zeros((requests, chunks * LANES - width), F32)
        queries = jnp.concatenate([queries, pad], axis=1)
    cosine, sine = tables_ref[0], tables_ref[1]
    zeros = jnp.zeros((requests, LANES), F32)
    nothing = jnp.zeros((inbox, LANES), F32)
    for j in range(SLOT):
        here = pl.ds(j, requests, stride=SLOT)
        there = pl.ds(j, inbox, stride=SLOT)
        if j < chunks:
            chunk = rotate(queries[:, j * LANES : (j + 1) * LANES], cosine, sine)
            chunk = (chunk.astype(BF16).astype(F32) * ATTN_SCALE).astype(BF16)
            packs[here, :] = chunk.astype(F32)
            sends[there, :] = jnp.dot(away_ref[...], chunk, preferred_element_type=F32)
        else:
            packs[here, :] = zeros
            sends[there, :] = span_ref[...] if j == META else nothing
    packed_ref[...] = packs[...]
    send_ref[...] = sends[...].astype(BF16)


def unpack(packed):
    low = iota(packed.shape, 1) < HEAD_DIM
    even = jnp.where(low, packed, 0.0)
    odd = jnp.where(low, pltpu.roll(packed, HEAD_DIM, 1), 0.0)
    return jnp.concatenate([even, odd], axis=0)


def head_rows(heads):
    return [(h // 2) + SLOT * (h % 2) for h in range(heads)]


def token_of_column(heads, kv_local, columns):
    row = iota((ROWS, columns), 0)
    column = iota((ROWS, columns), 1)
    wanted = jnp.full((ROWS, columns), kv_local, jnp.int32)
    for h, place in enumerate(head_rows(heads)):
        wanted = jnp.where(row == place, h // (heads // kv_local), wanted)
    return jnp.where(column % kv_local == wanted, column // kv_local, 1 << 20)


def score_page(query, block):
    return lax.dot_general(query, block, NT, preferred_element_type=F32)


def weigh_page(scores, tokens, span):
    scores = jnp.where(tokens < span, scores, NEG_FILL)
    top = jnp.max(scores, axis=1, keepdims=True)
    weights = jnp.exp(scores - top)
    return top, jnp.sum(weights, axis=1, keepdims=True), weights.astype(BF16)


def attend_pages(count, stage, copies, query_of, block_of, span_of, tokens, keep):
    stages = [range(i, min(i + stage, count)) for i in range(0, count, stage)]

    def score_stage(pages):
        for p in pages:
            if copies is not None:
                copies[p].wait()
        return {p: score_page(query_of(p), block_of(p)) for p in pages}

    scores = score_stage(stages[0])
    for i, pages in enumerate(stages):
        if i + 1 < len(stages):
            ahead = score_stage(stages[i + 1])
        weighed = {p: weigh_page(scores[p], tokens, span_of(p)) for p in pages}
        outs = {
            p: jnp.dot(weighed[p][2], block_of(p), preferred_element_type=F32)
            for p in pages
        }
        for p in pages:
            keep(p, weighed[p][0], weighed[p][1], outs[p])
        if i + 1 < len(stages):
            scores = ahead


def spread_queries(target, packed):
    low = iota(packed.shape, 2) < HEAD_DIM
    target[:, 0:SLOT, :] = jnp.where(low, packed, 0.0)
    target[:, SLOT:ROWS, :] = jnp.where(low, pltpu.roll(packed, HEAD_DIM, 2), 0.0)


def merge_pages(places, top_of, sum_of, top, acc, scaled, start, before):
    requests = start.shape[0]
    for p, place in enumerate(places):
        top[place] = jnp.maximum(top[place], top_of(p))
    acc[0:requests] = start * jnp.exp(before - top[0:requests])
    for p, place in enumerate(places):
        scaled[p] = sum_of(p) * jnp.exp(top_of(p) - top[place])
    for p, place in enumerate(places):
        acc[place] = acc[place] + scaled[p]


def project_heads(values, weights_ref, heads):
    if heads == 1:
        return jnp.dot(values, weights_ref[...], preferred_element_type=F32)
    rows, depth = values.shape
    wide = 1024
    part = wide // heads
    repeat = iota((part, wide), 1) // heads == iota((part, wide), 0)
    repeat = jnp.where(repeat, 1.0, 0.0).astype(BF16)
    parts = [values[:, i : i + part] for i in range(0, depth, part)]
    spread = jnp.dot(
        jnp.concatenate(parts, axis=0), repeat, preferred_element_type=F32
    ).astype(BF16)
    lane = iota((1, wide), 1) % heads
    masks = [jnp.where(lane == k, 1.0, 0.0).astype(BF16) for k in range(heads)]
    total = jnp.zeros((heads * rows, LANES), F32)
    for i in range(len(parts)):
        piece = spread[i * rows : (i + 1) * rows]
        piece = jnp.concatenate([piece * mask for mask in masks], axis=0)
        total += jnp.dot(
            piece, weights_ref[i * wide : (i + 1) * wide, :], preferred_element_type=F32
        )
    return total


def local_kernel(
    heads, kv_local, meta_hbm, packed_hbm, normed_hbm, wkv_hbm, tables_hbm, cache_hbm,
    state_hbm,
    meta, packed, normed, raw, tables, pages, queries, fresh, tops, sums, top,
    acc, scaled, sems,
):
    requests = normed.shape[0]
    count, columns, _ = pages.shape
    small = [
        copy_of(meta_hbm, meta, sems.at[0]),
        copy_of(packed_hbm, packed, sems.at[1]),
        copy_of(normed_hbm, normed, sems.at[2]),
        copy_of(tables_hbm, tables, sems.at[3]),
    ]
    weights = copy_of(wkv_hbm, raw, sems.at[4])
    paging = page_copies(cache_hbm, 0, pages, 0, count, sems, 6)
    for copy in small + paging + [weights]:
        copy.start()
    for copy in small:
        copy.wait()
    spread_queries(queries, packed[...].reshape(requests, SLOT, LANES))
    tokens = token_of_column(heads, kv_local, columns)
    lower = iota((ROWS, LANES), 1) < HEAD_DIM
    low = iota((requests, LANES), 1) < HEAD_DIM
    cosine = jnp.where(low, tables[0], 1.0)
    sine = jnp.where(low, tables[1], 0.0)

    def keep(p, page_top, total, out):
        tops[p] = jnp.broadcast_to(page_top, (ROWS, LANES))
        sums[p] = jnp.where(lower, total, out)

    attend_pages(
        count,
        8,
        paging,
        lambda p: queries[jnp.maximum(meta[0, p], 0)].astype(BF16),
        lambda p: pages[p],
        lambda p: meta[1, p],
        tokens,
        keep,
    )
    weights.wait()
    projected = project_heads(normed[...], raw, kv_local)
    new = [
        rotate(projected[k * requests : (k + 1) * requests], cosine, sine)
        .astype(BF16)
        .astype(F32)
        for k in range(kv_local)
    ]
    used = {place: h for h, place in enumerate(head_rows(heads))}
    for place in range(ROWS):
        value = jnp.zeros((requests, LANES), F32)
        if place in used:
            value = new[used[place] // (heads // kv_local)]
        fresh[pl.ds(place, requests, stride=ROWS), :] = value

    added = fresh[...].reshape(requests, ROWS, LANES)
    low16 = iota(added.shape, 2) < HEAD_DIM
    score = jnp.sum(queries[...] * added, axis=2, keepdims=True)
    before = jnp.broadcast_to(score, added.shape)
    start = jnp.where(low16, 1.0, added)
    top[0:requests] = before

    def place_of(p):
        owner = meta[0, p]
        return jnp.where(owner < 0, requests, owner)

    merge_pages(
        [place_of(p) for p in range(count)],
        lambda p: tops[p],
        lambda p: sums[p],
        top,
        acc,
        scaled,
        start,
        before,
    )
    whole = acc[0:requests]
    acc[0:requests] = jnp.where(
        low16, top[0:requests] + jnp.log(whole), whole / pltpu.roll(whole, HEAD_DIM, 2)
    )
    parked = copy_of(acc.at[pl.ds(0, requests)], state_hbm, sems.at[5])
    parked.start()
    parked.wait()


def lent_kernel(
    heads, kv_local, asked_ref, pages, pick_ref, drop_ref, meta_ref, packed_ref,
    normed_ref, tables_ref, hidden_ref,
    reply_hbm, meta_hbm, packed_hbm, normed_hbm, tables_hbm, hidden_hbm,
    reply16, sems,
):
    outgoing, columns, _ = pages.shape
    parked = [
        copy_of(packed_ref, packed_hbm, sems.at[0]),
        copy_of(normed_ref, normed_hbm, sems.at[1]),
        copy_of(hidden_ref, hidden_hbm, sems.at[2]),
        copy_of(tables_ref, tables_hbm, sems.at[3]),
        copy_of(meta_ref, meta_hbm, sems.at[4]),
    ]
    for copy in parked:
        copy.start()
    slot_rows = asked_ref.shape[0]
    shape = (outgoing * SLOT, slot_rows)
    chosen = jnp.where(pick_ref[:, 0:1] == iota(shape, 1), 1.0, 0.0).astype(BF16)
    asked = jnp.dot(chosen, asked_ref[...], preferred_element_type=F32)
    tokens = token_of_column(heads, kv_local, columns).astype(F32)
    low = iota((SLOT, LANES), 1) < HEAD_DIM
    lane = iota((SLOT, LANES), 1)
    row = iota((SLOT, LANES), 0)

    def terms(total, offset):
        leading = total.astype(BF16).astype(F32)
        rest = total - leading
        second = rest.astype(BF16).astype(F32)
        third = rest - second
        spot = lane - offset - 3 * row
        placed = jnp.where(spot == 0, leading, 0.0)
        placed = jnp.where(spot == 1, second, placed)
        return jnp.where(spot == 2, third, placed)

    packed = [asked[j * SLOT : (j + 1) * SLOT] for j in range(outgoing)]
    replies = {}

    def keep(j, top, total, out):
        out = out / total
        logs = top + jnp.log(total)
        even = pltpu.roll(out[0:SLOT], HEAD_DIM, 1)
        both = jnp.where(low, even, out[SLOT:ROWS])
        line = jnp.sum(
            terms(logs[0:SLOT], 0) + terms(logs[SLOT:ROWS], HEAD_DIM), axis=0, keepdims=True
        )
        replies[j] = jnp.where(row == META, line, both)

    attend_pages(
        outgoing,
        8,
        None,
        lambda j: unpack(packed[j]).astype(BF16),
        lambda j: pages[j],
        lambda j: packed[j][META : META + 1, 0:1],
        tokens,
        keep,
    )
    shape = (slot_rows, outgoing * SLOT)
    placed = jnp.where(drop_ref[0:1, :] == iota(shape, 0), 1.0, 0.0).astype(BF16)
    every = jnp.concatenate([replies[j] for j in range(outgoing)], axis=0).astype(BF16)
    reply = jnp.dot(placed, every, preferred_element_type=F32)
    reply16[...] = reply.astype(BF16)
    replying = copy_of(reply16, reply_hbm, sems.at[5])
    replying.start()
    for copy in parked + [replying]:
        copy.wait()


def combine_kernel(
    heads, pool, meta_hbm, state_hbm, wo_hbm, hidden_hbm, gain_hbm, router_hbm,
    routes_hbm, reply_ref,
    part_ref, meta_ref, hidden_ref, gain_ref, router_ref, routes_ref,
    meta, state, wo, gain, tops, accs, scaled, reply, finals, sems,
):
    requests = state.shape[0]
    inbox = reply_ref.shape[0] // SLOT
    chunks = -(-heads // 2)
    small = [
        copy_of(meta_hbm, meta, sems.at[0]),
        copy_of(state_hbm, state, sems.at[1]),
    ]
    weights = copies_of(wo_hbm, wo, sems, 2)
    gaining = copy_of(gain_hbm, gain, sems.at[6])
    later = [
        copy_of(meta_hbm, meta_ref, sems.at[7]),
        copy_of(hidden_hbm, hidden_ref, sems.at[8]),
        copy_of(router_hbm, router_ref, sems.at[9]),
        copy_of(routes_hbm, routes_ref, sems.at[10]),
    ]
    for copy in small + weights + [gaining] + later:
        copy.start()
    reply[...] = reply_ref[...].astype(F32)
    low = iota((SLOT, LANES), 1) < HEAD_DIM
    lane = iota((SLOT, LANES), 1)
    row = iota((SLOT, LANES), 0)
    mine = (lane % HEAD_DIM) // 3 == row

    def place_of(s):
        lender = s // CAP ^ (inbox // CAP // 2)
        owner = meta[0, pool + lender * CAP + s % CAP]
        return jnp.where(owner < 0, requests, owner)

    def logs_of(s):
        line = reply[s * SLOT + META : s * SLOT + META + 1, :]
        line = jnp.where(mine, jnp.broadcast_to(line, (SLOT, LANES)), 0.0)
        even = jnp.sum(jnp.where(low, line, 0.0), axis=1, keepdims=True)
        odd = jnp.sum(jnp.where(low, 0.0, line), axis=1, keepdims=True)
        logs = jnp.concatenate([even, odd], axis=0)
        return jnp.broadcast_to(logs, (ROWS, LANES))

    logs = [logs_of(s) for s in range(inbox)]
    for copy in small:
        copy.wait()
    low16 = iota(state.shape, 2) < HEAD_DIM
    start = state[...]
    before = jnp.where(low16, start, pltpu.roll(start, HEAD_DIM, 2))
    tops[0:requests] = before

    def sum_of(s):
        packed = reply[s * SLOT : (s + 1) * SLOT, :]
        even = jnp.where(low, 1.0, pltpu.roll(packed, HEAD_DIM, 1))
        odd = jnp.where(low, 1.0, packed)
        return jnp.concatenate([even, odd], axis=0)

    merge_pages(
        [place_of(s) for s in range(inbox)],
        lambda s: logs[s],
        sum_of,
        tops,
        accs,
        scaled,
        jnp.where(low16, 1.0, start),
        before,
    )
    whole = accs[0:requests]
    finals[...] = (whole / pltpu.roll(whole, HEAD_DIM, 2)).reshape(
        requests * ROWS, LANES
    )
    wide = iota((requests, LANES), 1) < HEAD_DIM
    parts = []
    for j in range(chunks):
        even = finals[pl.ds(j, requests, stride=ROWS), :]
        odd = finals[pl.ds(SLOT + j, requests, stride=ROWS), :]
        parts.append(jnp.where(wide, pltpu.roll(even, HEAD_DIM, 1), odd).astype(BF16))
    attention = jnp.concatenate(parts, axis=1)[:, : heads * HEAD_DIM]
    for copy in weights:
        copy.wait()
    part_ref[...] = jnp.dot(attention, wo[...], preferred_element_type=F32).astype(BF16)
    gaining.wait()
    gain_ref[...] = gain[...].reshape(1, gain.shape[0])
    for copy in later:
        copy.wait()


def load_kernel(wd_hbm, order_hbm, wd_ref, sems):
    del order_hbm
    copies = copies_of(wd_hbm, wd_ref, sems, 0)
    for copy in copies:
        copy.start()
    for copy in copies:
        copy.wait()


def finish_kernel(attended_ref, own_ref, other_ref, attended_out, experts_out):
    attended_out[...] = attended_ref[...]
    experts_out[...] = (own_ref[...] + other_ref[...].astype(F32)).astype(BF16)


def own_rows(values, first):
    half = values.shape[0] // 2
    return jnp.where(first, values[:half], values[half:])


def residual_kernel(
    tp, count, meta_ref, hidden_ref, *refs,
):
    pieces = refs[:count]
    gain_ref, attended_ref, input_ref, again_ref = refs[count:]
    requests = hidden_ref.shape[0]
    if count == 2:
        summed = pieces[0][...].astype(F32) + pieces[1][...].astype(F32)
    else:
        summed = pieces[0][0:requests, :].astype(F32)
        for t in range(1, tp):
            part = pieces[0][t * requests : (t + 1) * requests, :]
            summed = summed + part.astype(F32)
    attended = (hidden_ref[...].astype(F32) + RESID_SCALE * summed).astype(BF16)
    if count == 2:
        attended_ref[...] = own_rows(attended, meta_ref[3:4, 0:1] == 0)
    else:
        attended_ref[...] = attended
    ffn_input = norm_rows(attended.astype(F32), gain_ref[...])
    input_ref[...] = ffn_input
    again_ref[...] = ffn_input


def gate_column(units, meta_ref, input_ref, router_ref, routes_ref):
    ffn_input = input_ref[...]
    requests = ffn_input.shape[0]
    logits = lax.dot_general(router_ref[...], ffn_input, NT, preferred_element_type=F32)
    expert = iota(logits.shape, 0)
    named = jnp.zeros(logits.shape, F32)
    for k in range(routes_ref.shape[0]):
        named = jnp.where(routes_ref[k : k + 1, :] == expert, 1.0, named)
    chosen = named > 0.5
    top = jnp.max(jnp.where(chosen, logits, NEG_FILL), axis=0, keepdims=True)
    weights = jnp.where(chosen, jnp.exp(logits - top), 0.0)
    total = jnp.sum(weights, axis=0, keepdims=True)
    mine = expert == meta_ref[3:4, 0:1] * units // FF
    line = jnp.sum(jnp.where(mine, weights, 0.0), axis=0, keepdims=True) / total
    diagonal = iota((requests, requests), 0) == iota((requests, requests), 1)
    line = jnp.where(diagonal, jnp.broadcast_to(line, (requests, requests)), 0.0)
    return jnp.sum(line, axis=1, keepdims=True)


def expert_kernel(
    units, meta_ref, lifted_ref, input_ref, router_ref, routes_ref, wd_ref, *outs
):
    column = gate_column(units, meta_ref, input_ref, router_ref, routes_ref)
    gate = lifted_ref[0]
    active = gate / (1.0 + jnp.exp(-gate)) * lifted_ref[1] * column
    share = jnp.dot(active.astype(BF16), wd_ref[...], preferred_element_type=F32)
    if len(outs) == 2:
        first = meta_ref[3:4, 0:1] == 0
        outs[0][...] = own_rows(share, first)
        outs[1][...] = own_rows(share, jnp.logical_not(first)).astype(BF16)
    else:
        outs[0][...] = share.astype(BF16)


def call(body, outs, in_specs, scratch=(), limit=16, flops=0, moved=0):
    return pl.pallas_call(
        body,
        out_shape=outs,
        in_specs=in_specs,
        out_specs=[VMEM if isinstance(o, jax.ShapeDtypeStruct) else HBM for o in outs],
        scratch_shapes=list(scratch),
        compiler_params=pltpu.CompilerParams(vmem_limit_bytes=limit << 20),
        cost_estimate=pl.CostEstimate(
            flops=flops, bytes_accessed=moved, transcendentals=0
        ),
    )


def swap(values):
    return lax.ppermute(values, "tensor", [(0, 1), (1, 0)])


def on_device(
    hidden,
    attn_gain,
    w_query,
    w_keyvalue,
    w_output,
    cache,
    page_table,
    ctx_len,
    move_dest,
    ffn_gain,
    router,
    routes,
    w_in,
    w_down,
):
    replicas = lax.axis_size("replica")
    tp = lax.axis_size("tensor")
    rank = lax.axis_index("tensor").astype(jnp.int32)
    rows, width = hidden.shape
    pool, page_len, kv_local, _ = cache.shape
    outgoing = move_dest.shape[0]
    local_pages = pool - outgoing
    requests = page_table.shape[0]
    heads = w_query.shape[1] // HEAD_DIM
    inbox = replicas * CAP
    units = w_down.shape[0]
    assert FF % units == 0
    columns = page_len * kv_local
    entries = -(-(pool + inbox) // LANES) * LANES
    struct = jax.ShapeDtypeStruct
    pair = tp == 2
    ids = rank.reshape(1)

    def pin(values):
        return pltpu.with_memory_space_constraint(values, pltpu.HBM)

    def exchange(blocks, order):
        blocks = blocks.reshape(replicas, CAP * SLOT, LANES)
        blocks = lax.all_to_all(
            blocks,
            "replica",
            split_axis=0,
            concat_axis=0,
            tiled=True,
            axis_index_groups=[list(order)],
        )
        return blocks.reshape(inbox * SLOT, LANES)

    blocks = pin(cache.reshape(pool, columns, LANES))
    if pair:
        pieces = [hidden, swap(hidden)]
    else:
        pieces = [lax.all_gather(hidden, "tensor", axis=0, tiled=True)]
    meta_shape = (4, entries)
    tables_shape = (2, requests, LANES)
    own, wq, gain, tables, away, away_span, meta, lent, pick, drop = call(
        functools.partial(prepare_kernel, pool, replicas),
        [
            struct(hidden.shape, BF16),
            struct(w_query.shape, BF16),
            struct((1, width), F32),
            struct(tables_shape, F32),
            struct((inbox, requests), BF16),
            struct((inbox, LANES), F32),
            struct(meta_shape, jnp.int32),
            struct((outgoing, columns, LANES), BF16),
            struct((outgoing * SLOT, LANES), jnp.int32),
            struct((outgoing, outgoing * SLOT), jnp.int32),
        ],
        [SMEM] + [HBM] * 7,
        [
            pltpu.VMEM((1, requests), jnp.int32),
            pltpu.VMEM((page_table.shape[1], requests), jnp.int32),
            pltpu.VMEM((1, outgoing), jnp.int32),
            pltpu.VMEM((width,), F32),
            pltpu.SemaphoreType.DMA((10,)),
        ],
        moved=2 * w_query.size,
    )(
        ids,
        pin(hidden),
        pin(ctx_len.reshape(1, requests)),
        pin(page_table.T),
        pin(move_dest.reshape(1, outgoing)),
        pin(attn_gain),
        pin(w_query),
        blocks,
    )
    if pair:
        pieces[0] = own
    hidden_all, normed, packed, sends = call(
        functools.partial(query_kernel, len(pieces)),
        [
            struct((requests, width), BF16),
            struct((requests, width), BF16),
            struct((requests * SLOT, LANES), F32),
            struct((inbox * SLOT, LANES), BF16),
        ],
        [VMEM] * (len(pieces) + 6),
        [
            pltpu.VMEM((requests * SLOT, LANES), F32),
            pltpu.VMEM((inbox * SLOT, LANES), F32),
        ],
        flops=4 * requests * width * w_query.shape[1],
        moved=2 * w_query.size,
    )(meta, *pieces, gain, wq, tables, away, away_span)
    asked = exchange(sends, range(replicas)[::-1])
    replies, meta_far, packed_far, normed_far, tables_far, hidden_far = call(
        functools.partial(lent_kernel, heads, kv_local),
        [
            pltpu.HBM((inbox * SLOT, LANES), BF16),
            pltpu.HBM(meta_shape, jnp.int32),
            pltpu.HBM((requests * SLOT, LANES), F32),
            pltpu.HBM((requests, width), BF16),
            pltpu.HBM(tables_shape, F32),
            pltpu.HBM((requests, width), BF16),
        ],
        [VMEM] * 9,
        [
            pltpu.VMEM((inbox * SLOT, LANES), BF16),
            pltpu.SemaphoreType.DMA((6,)),
        ],
        flops=4 * ROWS * columns * LANES * outgoing,
        moved=2 * columns * LANES * outgoing,
    )(asked, lent, pick, drop, meta, packed, normed, tables, hidden_all)
    returned = exchange(replies, [r ^ replicas // 2 for r in range(replicas)])
    (state,) = call(
        functools.partial(local_kernel, heads, kv_local),
        [pltpu.HBM((requests, ROWS, LANES), F32)],
        [HBM] * 6,
        [
            pltpu.SMEM(meta_shape, jnp.int32),
            pltpu.VMEM((requests * SLOT, LANES), F32),
            pltpu.VMEM((requests, width), BF16),
            pltpu.VMEM((width * kv_local, LANES), BF16),
            pltpu.VMEM(tables_shape, F32),
            pltpu.VMEM((local_pages, columns, LANES), BF16),
            pltpu.VMEM((requests, ROWS, LANES), F32),
            pltpu.VMEM((requests * ROWS, LANES), F32),
            pltpu.VMEM((local_pages, ROWS, LANES), F32),
            pltpu.VMEM((local_pages, ROWS, LANES), F32),
            pltpu.VMEM((requests + 1, ROWS, LANES), F32),
            pltpu.VMEM((requests + 1, ROWS, LANES), F32),
            pltpu.VMEM((local_pages, ROWS, LANES), F32),
            pltpu.SemaphoreType.DMA((6 + local_pages,)),
        ],
        limit=24,
        flops=4 * ROWS * columns * LANES * local_pages,
        moved=2 * columns * LANES * local_pages,
    )(
        pin(meta_far),
        pin(packed_far),
        pin(normed_far),
        pin(w_keyvalue.reshape(width * kv_local, LANES)),
        pin(tables_far),
        blocks,
    )
    part, meta, hidden_all, gain, router_t, routes_t = call(
        functools.partial(combine_kernel, heads, pool),
        [
            struct((requests, width), BF16),
            struct(meta_shape, jnp.int32),
            struct((requests, width), BF16),
            struct((1, width), F32),
            struct(router.shape[::-1], BF16),
            struct(routes.shape[::-1], jnp.int32),
        ],
        [HBM] * 7 + [VMEM],
        [
            pltpu.SMEM(meta_shape, jnp.int32),
            pltpu.VMEM((requests, ROWS, LANES), F32),
            pltpu.VMEM(w_output.shape, BF16),
            pltpu.VMEM((width,), F32),
            pltpu.VMEM((requests + 1, ROWS, LANES), F32),
            pltpu.VMEM((requests + 1, ROWS, LANES), F32),
            pltpu.VMEM((inbox, ROWS, LANES), F32),
            pltpu.VMEM((inbox * SLOT, LANES), F32),
            pltpu.VMEM((requests * ROWS, LANES), F32),
            pltpu.SemaphoreType.DMA((11,)),
        ],
        flops=2 * requests * w_output.size,
        moved=2 * w_output.size,
    )(
        pin(meta_far), pin(state), pin(w_output), pin(hidden_far), pin(ffn_gain),
        pin(router.T), pin(routes.T), returned,
    )
    if pair:
        parts = [part, swap(part)]
    else:
        parts = [lax.all_gather(part, "tensor", axis=0, tiled=True)]
    (wd,) = call(
        load_kernel,
        [struct(w_down.shape, BF16)],
        [HBM, ANY],
        [pltpu.SemaphoreType.DMA((4,))],
        moved=2 * w_down.size,
    )(pin(w_down), part)
    attended, ffn_input, ffn_again = call(
        functools.partial(residual_kernel, tp, len(parts)),
        [
            struct((rows if pair else requests, width), BF16),
            struct((requests, width), BF16),
            struct((requests, width), BF16),
        ],
        [VMEM] * (len(parts) + 3),
        flops=2 * requests * width,
        moved=8 * requests * width,
    )(meta, hidden_all, *parts, gain)
    lifted = jnp.einsum("rd,dsu->sru", ffn_input, w_in, preferred_element_type=F32)
    shapes = [struct((requests, width), BF16)]
    if pair:
        shapes = [struct((rows, width), F32), struct((rows, width), BF16)]
    shares = call(
        functools.partial(expert_kernel, units),
        shapes,
        [VMEM] * 6,
        flops=2 * requests * w_down.size,
        moved=2 * w_down.size,
    )(meta, lifted, ffn_again, router_t, routes_t, wd)
    if pair:
        out = struct((rows, width), BF16)
        return tuple(
            call(finish_kernel, [out, out], [VMEM] * 3)(attended, shares[0], swap(shares[1]))
        )
    shares = lax.all_gather(shares[0], "tensor", axis=0)
    mine = lax.dynamic_slice_in_dim(shares, rank * rows, rows, axis=1)
    experts_out = jnp.sum(mine.astype(F32), axis=0).astype(BF16)
    attended = lax.dynamic_slice_in_dim(attended, rank * rows, rows, axis=0)
    return attended, experts_out


def solution(mesh):
    placed = (
        P(("replica", "tensor"), None),
        P(),
        P(None, "tensor"),
        P(None, "tensor", None),
        P("tensor", None),
        P("replica", None, "tensor", None),
        P("replica", None),
        P("replica"),
        P("replica"),
        P(),
        P(),
        P("replica", None),
        P(None, None, "tensor"),
        P("tensor", None),
    )
    return jax.shard_map(
        on_device,
        mesh=mesh,
        in_specs=placed,
        out_specs=(P(("replica", "tensor"), None), P(("replica", "tensor"), None)),
        check_vma=False,
    )
```

```python
import functools
import math

import jax
import jax.numpy as jnp
from jax import lax
from jax.experimental import pallas as pl
from jax.experimental.pallas import tpu as pltpu
from jax.sharding import PartitionSpec as P

HEAD_DIM = 64
EXPERTS = 40
FF = 512
CAP = 2
LANES = 128
SLOT = 8
ROWS = 16
META = 6

ATTN_SCALE = 0.015625
RESID_SCALE = 0.22
ROPE_BASE = 10000.0
EPSILON = 1e-06
NEG_FILL = -1e30

F32 = jnp.float32
BF16 = jnp.bfloat16
VMEM = pl.BlockSpec(memory_space=pltpu.VMEM)
SMEM = pl.BlockSpec(memory_space=pltpu.SMEM)
ANY = pl.BlockSpec(memory_space=pl.ANY)
HBM = pl.BlockSpec(memory_space=pltpu.HBM)
NT = (((1,), (1,)), ((), ()))


def iota(shape, axis):
    return lax.broadcasted_iota(jnp.int32, shape, axis)


def norm_rows(values, gain):
    factor = lax.rsqrt(jnp.mean(values * values, axis=-1, keepdims=True) + EPSILON)
    return (values * factor * gain).astype(BF16)


def rope_tables(ctx_row, requests):
    diagonal = iota((requests, requests), 0) == iota((requests, requests), 1)
    ctx = jnp.broadcast_to(ctx_row.astype(F32), (requests, requests))
    ctx = jnp.sum(jnp.where(diagonal, ctx, 0.0), axis=1, keepdims=True)
    lane = iota((requests, LANES), 1)
    index = (lane % (HEAD_DIM // 2)).astype(F32)
    inverse = jnp.exp(index * (-2.0 * math.log(ROPE_BASE) / HEAD_DIM))
    angles = ctx * inverse
    sign = jnp.where(lane % HEAD_DIM < HEAD_DIM // 2, -1.0, 1.0)
    return jnp.cos(angles), jnp.sin(angles) * sign


def rotate(chunk, cosine, sine):
    lane = iota(chunk.shape, 1)
    ahead = pltpu.roll(chunk, LANES - HEAD_DIM // 2, 1)
    behind = pltpu.roll(chunk, HEAD_DIM // 2, 1)
    turned = jnp.where(lane % HEAD_DIM < HEAD_DIM // 2, ahead, behind)
    return chunk * cosine + turned * sine


def copy_of(source, target, sem):
    return pltpu.make_async_copy(source, target, sem)


def copies_of(source, target, sems, base):
    step = source.shape[0] // 4
    return [
        copy_of(
            source.at[pl.ds(i * step, step)], target.at[pl.ds(i * step, step)], sems.at[base + i]
        )
        for i in range(4)
    ]


def page_copies(cache_hbm, first, pages, place, count, sems, base):
    return [
        copy_of(cache_hbm.at[first + p], pages.at[place + p], sems.at[base + p])
        for p in range(count)
    ]


def prepare_kernel(
    pool, replicas, ids_ref, hidden_hbm, ctx_hbm, table_hbm, dest_hbm, attn_gain_hbm,
    wq_hbm, cache_hbm,
    hidden_ref, wq_ref, gain_ref, tables_ref, away_ref, span_ref, meta_ref, lent_ref,
    pick_ref, drop_ref,
    ctx, table, dest, gain, sems,
):
    inbox = replicas * CAP
    requests = ctx.shape[1]
    entries = meta_ref.shape[1]
    small = [
        copy_of(ctx_hbm, ctx, sems.at[0]),
        copy_of(table_hbm, table, sems.at[1]),
        copy_of(dest_hbm, dest, sems.at[2]),
        copy_of(attn_gain_hbm, gain, sems.at[3]),
    ]
    large = [copy_of(hidden_hbm, hidden_ref, sems.at[4])]
    large += copies_of(wq_hbm, wq_ref, sems, 5)
    lending = pl.ds(pool - lent_ref.shape[0], lent_ref.shape[0])
    large.append(copy_of(cache_hbm.at[lending], lent_ref, sems.at[9]))
    for copy in small + large:
        copy.start()
    for copy in small:
        copy.wait()
    gain_ref[...] = gain[...].reshape(1, gain.shape[0])
    ctx_row = ctx[...]

    def claims(values):
        held = jnp.zeros(values.shape, F32)
        spans = jnp.zeros(values.shape, F32)
        for k in range(table.shape[0]):
            match = table[k : k + 1, :] == values
            filled = jnp.clip(ctx_row - k * 128, 0, 128).astype(F32)
            held = jnp.where(match, 1.0, held)
            spans = jnp.where(match, filled, spans)
        return held.astype(BF16), spans

    held, spans = claims(iota((entries, requests), 0))
    numbers = (iota((SLOT, requests), 1) + 1).astype(BF16)
    ones = jnp.ones((SLOT, requests), BF16)
    holder = lax.dot_general(numbers, held, NT, preferred_element_type=F32)
    covered = lax.dot_general(ones, spans.astype(BF16), NT, preferred_element_type=F32)
    meta_ref[0:1, :] = holder[0:1, :].astype(jnp.int32) - 1
    meta_ref[1:2, :] = covered[0:1, :].astype(jnp.int32)
    meta_ref[2:3, :] = jnp.zeros((1, entries), jnp.int32)
    lent = dest.shape[1]
    across = jnp.broadcast_to(dest[...].astype(F32), (lent, lent))
    row, lane = iota((lent, lent), 0), iota((lent, lent), 1)
    down = jnp.sum(jnp.where(row == lane, across, 0.0), axis=1, keepdims=True)
    same = across == down
    before = jnp.sum(jnp.where(same & (lane < row), 1.0, 0.0), axis=1, keepdims=True)
    column = (replicas - 1 - down) * CAP + before
    column = jnp.broadcast_to(column, (lent, LANES)).astype(BF16)
    before = jnp.sum(jnp.where(same & (row < lane), 1.0, 0.0), axis=0, keepdims=True)
    line = dest[...] ^ replicas // 2
    line = jnp.broadcast_to(line.astype(F32), (lent, lent))
    line = (line * CAP + before).astype(BF16)
    expand = iota((lent * SLOT, lent), 0) // SLOT == iota((lent * SLOT, lent), 1)
    expand = jnp.where(expand, 1.0, 0.0).astype(BF16)
    column = jnp.dot(expand, column, preferred_element_type=F32).astype(jnp.int32)
    pick_ref[...] = column * SLOT + iota(column.shape, 0) % SLOT
    line = lax.dot_general(line, expand, NT, preferred_element_type=F32).astype(jnp.int32)
    drop_ref[...] = line * SLOT + iota(line.shape, 1) % SLOT
    meta_ref[3:4, :] = jnp.full((1, entries), ids_ref[0], jnp.int32)
    cosine, sine = rope_tables(ctx_row, requests)
    tables_ref[0] = cosine
    tables_ref[1] = sine
    slot = iota((inbox, requests), 0)
    lender = replicas - 1 - slot // CAP
    held, spans = claims(pool + lender * CAP + slot % CAP)
    away_ref[...] = held
    away_span = jnp.sum(spans, axis=1, keepdims=True)
    span_ref[...] = jnp.broadcast_to(away_span, span_ref.shape)
    for copy in large:
        copy.wait()


def query_kernel(
    count, meta_ref, *refs,
):
    pieces = refs[:count]
    (gain_ref, wq_ref, tables_ref, away_ref, span_ref,
     hidden_ref, normed_ref, packed_ref, send_ref, packs, sends) = refs[count:]
    requests = hidden_ref.shape[0]
    inbox = span_ref.shape[0]
    width = wq_ref.shape[1]
    chunks = -(-width // LANES)
    if count == 1:
        hidden = pieces[0][...]
    else:
        own, other = pieces[0][...], pieces[1][...]
        first = meta_ref[3:4, 0:1] == 0
        hidden = jnp.concatenate(
            [jnp.where(first, own, other), jnp.where(first, other, own)], axis=0
        )
    hidden_ref[...] = hidden
    normed = norm_rows(hidden.astype(F32), gain_ref[...])
    normed_ref[...] = normed
    queries = jnp.dot(normed, wq_ref[...], preferred_element_type=F32)
    if chunks * LANES > width:
        pad = jnp.zeros((requests, chunks * LANES - width), F32)
        queries = jnp.concatenate([queries, pad], axis=1)
    cosine, sine = tables_ref[0], tables_ref[1]
    zeros = jnp.zeros((requests, LANES), F32)
    nothing = jnp.zeros((inbox, LANES), F32)
    for j in range(SLOT):
        here = pl.ds(j, requests, stride=SLOT)
        there = pl.ds(j, inbox, stride=SLOT)
        if j < chunks:
            chunk = rotate(queries[:, j * LANES : (j + 1) * LANES], cosine, sine)
            chunk = (chunk.astype(BF16).astype(F32) * ATTN_SCALE).astype(BF16)
            packs[here, :] = chunk.astype(F32)
            sends[there, :] = jnp.dot(away_ref[...], chunk, preferred_element_type=F32)
        else:
            packs[here, :] = zeros
            sends[there, :] = span_ref[...] if j == META else nothing
    packed_ref[...] = packs[...]
    send_ref[...] = sends[...].astype(BF16)


def unpack(packed):
    low = iota(packed.shape, 1) < HEAD_DIM
    even = jnp.where(low, packed, 0.0)
    odd = jnp.where(low, pltpu.roll(packed, HEAD_DIM, 1), 0.0)
    return jnp.concatenate([even, odd], axis=0)


def head_rows(heads):
    return [(h // 2) + SLOT * (h % 2) for h in range(heads)]


def token_of_column(heads, kv_local, columns):
    row = iota((ROWS, columns), 0)
    column = iota((ROWS, columns), 1)
    wanted = jnp.full((ROWS, columns), kv_local, jnp.int32)
    for h, place in enumerate(head_rows(heads)):
        wanted = jnp.where(row == place, h // (heads // kv_local), wanted)
    return jnp.where(column % kv_local == wanted, column // kv_local, 1 << 20)


def score_page(query, block):
    return lax.dot_general(query, block, NT, preferred_element_type=F32)


def weigh_page(scores, tokens, span):
    scores = jnp.where(tokens < span, scores, NEG_FILL)
    top = jnp.max(scores, axis=1, keepdims=True)
    weights = jnp.exp(scores - top)
    return top, jnp.sum(weights, axis=1, keepdims=True), weights.astype(BF16)


def attend_pages(
    count, stage, copies, query_of, block_of, span_of, tokens, keep, last=None
):
    stages = [range(i, min(i + stage, count)) for i in range(0, count, stage)]

    def score_stage(pages):
        for p in pages:
            if copies is not None:
                copies[p].wait()
            if last is not None and p == count - 1:
                last.wait()
        return {p: score_page(query_of(p), block_of(p)) for p in pages}

    scores = score_stage(stages[0])
    for i, pages in enumerate(stages):
        if i + 1 < len(stages):
            ahead = score_stage(stages[i + 1])
        weighed = {p: weigh_page(scores[p], tokens, span_of(p)) for p in pages}
        outs = {
            p: jnp.dot(weighed[p][2], block_of(p), preferred_element_type=F32)
            for p in pages
        }
        for p in pages:
            keep(p, weighed[p][0], weighed[p][1], outs[p])
        if i + 1 < len(stages):
            scores = ahead


def spread_queries(target, packed):
    low = iota(packed.shape, 2) < HEAD_DIM
    target[:, 0:SLOT, :] = jnp.where(low, packed, 0.0)
    target[:, SLOT:ROWS, :] = jnp.where(low, pltpu.roll(packed, HEAD_DIM, 2), 0.0)


def merge_pages(places, top_of, sum_of, top, acc, scaled, start, before):
    requests = start.shape[0]
    for p, place in enumerate(places):
        top[place] = jnp.maximum(top[place], top_of(p))
    acc[0:requests] = start * jnp.exp(before - top[0:requests])
    for p, place in enumerate(places):
        scaled[p] = sum_of(p) * jnp.exp(top_of(p) - top[place])
    for p, place in enumerate(places):
        acc[place] = acc[place] + scaled[p]


def project_heads(values, weights_ref, heads):
    if heads == 1:
        return jnp.dot(values, weights_ref[...], preferred_element_type=F32)
    rows, depth = values.shape
    wide = 1024
    part = wide // heads
    repeat = iota((part, wide), 1) // heads == iota((part, wide), 0)
    repeat = jnp.where(repeat, 1.0, 0.0).astype(BF16)
    parts = [values[:, i : i + part] for i in range(0, depth, part)]
    spread = jnp.dot(
        jnp.concatenate(parts, axis=0), repeat, preferred_element_type=F32
    ).astype(BF16)
    lane = iota((1, wide), 1) % heads
    masks = [jnp.where(lane == k, 1.0, 0.0).astype(BF16) for k in range(heads)]
    total = jnp.zeros((heads * rows, LANES), F32)
    for i in range(len(parts)):
        piece = spread[i * rows : (i + 1) * rows]
        piece = jnp.concatenate([piece * mask for mask in masks], axis=0)
        total += jnp.dot(
            piece, weights_ref[i * wide : (i + 1) * wide, :], preferred_element_type=F32
        )
    return total


def local_kernel(
    heads, kv_local, meta_hbm, packed_hbm, normed_hbm, wkv_hbm, tables_hbm, cache_hbm,
    state_hbm,
    meta, packed, normed, raw, tables, pages, queries, fresh, tops, sums, top, acc,
    scaled, sems,
):
    requests = normed.shape[0]
    count, columns, _ = pages.shape
    small = [
        copy_of(meta_hbm, meta, sems.at[0]),
        copy_of(packed_hbm, packed, sems.at[1]),
        copy_of(normed_hbm, normed, sems.at[2]),
        copy_of(tables_hbm, tables, sems.at[3]),
    ]
    weights = copy_of(wkv_hbm, raw, sems.at[4])
    paging = page_copies(cache_hbm, 0, pages, 0, count, sems, 6)
    for copy in small + paging + [weights]:
        copy.start()
    tokens = token_of_column(heads, kv_local, columns)
    lower = iota((ROWS, LANES), 1) < HEAD_DIM
    low = iota((requests, LANES), 1) < HEAD_DIM
    low16 = iota((requests, ROWS, LANES), 2) < HEAD_DIM
    top[...] = jnp.full(top.shape, NEG_FILL, F32)
    acc[...] = jnp.zeros(acc.shape, F32)
    for copy in small:
        copy.wait()
    spread_queries(queries, packed[...].reshape(requests, SLOT, LANES))

    def place_of(p):
        owner = meta[0, p]
        return jnp.where(owner < 0, requests, owner)

    places = [place_of(p) for p in range(count)]

    def keep(p, page_top, total, out):
        tops[p] = jnp.broadcast_to(page_top, (ROWS, LANES))
        sums[p] = jnp.where(lower, total, out)
        top[places[p]] = jnp.maximum(top[places[p]], tops[p])

    attend_pages(
        count,
        8,
        paging,
        lambda p: queries[jnp.maximum(meta[0, p], 0)].astype(BF16),
        lambda p: pages[p],
        lambda p: meta[1, p],
        tokens,
        keep,
        weights,
    )
    cosine = jnp.where(low, tables[0], 1.0)
    sine = jnp.where(low, tables[1], 0.0)
    projected = project_heads(normed[...], raw, kv_local)
    new = [
        rotate(projected[k * requests : (k + 1) * requests], cosine, sine)
        .astype(BF16)
        .astype(F32)
        for k in range(kv_local)
    ]
    used = {place: h for h, place in enumerate(head_rows(heads))}
    for place in range(ROWS):
        value = jnp.zeros((requests, LANES), F32)
        if place in used:
            value = new[used[place] // (heads // kv_local)]
        fresh[pl.ds(place, requests, stride=ROWS), :] = value
    for p, place in enumerate(places):
        scaled[p] = sums[p] * jnp.exp(tops[p] - top[place])
    for p, place in enumerate(places):
        acc[place] = acc[place] + scaled[p]
    added = fresh[...].reshape(requests, ROWS, LANES)
    score = jnp.sum(queries[...] * added, axis=2, keepdims=True)
    score = jnp.broadcast_to(score, added.shape)
    before = top[0:requests]
    highest = jnp.maximum(before, score)
    whole = acc[0:requests] * jnp.exp(before - highest)
    whole = whole + jnp.where(low16, 1.0, added) * jnp.exp(score - highest)
    acc[0:requests] = jnp.where(
        low16, highest + jnp.log(whole), whole / pltpu.roll(whole, HEAD_DIM, 2)
    )
    parked = copy_of(acc.at[pl.ds(0, requests)], state_hbm, sems.at[5])
    parked.start()
    parked.wait()


def lent_kernel(
    heads, kv_local, asked_ref, pages, pick_ref, drop_ref, meta_ref, packed_ref,
    normed_ref, tables_ref, hidden_ref,
    reply_hbm, meta_hbm, packed_hbm, normed_hbm, tables_hbm, hidden_hbm,
    reply16, sems,
):
    outgoing, columns, _ = pages.shape
    parked = [
        copy_of(packed_ref, packed_hbm, sems.at[0]),
        copy_of(normed_ref, normed_hbm, sems.at[1]),
        copy_of(hidden_ref, hidden_hbm, sems.at[2]),
        copy_of(tables_ref, tables_hbm, sems.at[3]),
        copy_of(meta_ref, meta_hbm, sems.at[4]),
    ]
    for copy in parked:
        copy.start()
    slot_rows = asked_ref.shape[0]
    shape = (outgoing * SLOT, slot_rows)
    chosen = jnp.where(pick_ref[:, 0:1] == iota(shape, 1), 1.0, 0.0).astype(BF16)
    asked = jnp.dot(chosen, asked_ref[...], preferred_element_type=F32)
    tokens = token_of_column(heads, kv_local, columns).astype(F32)
    low = iota((SLOT, LANES), 1) < HEAD_DIM
    lane = iota((SLOT, LANES), 1)
    row = iota((SLOT, LANES), 0)

    def terms(total, offset):
        leading = total.astype(BF16).astype(F32)
        rest = total - leading
        second = rest.astype(BF16).astype(F32)
        third = rest - second
        spot = lane - offset - 3 * row
        placed = jnp.where(spot == 0, leading, 0.0)
        placed = jnp.where(spot == 1, second, placed)
        return jnp.where(spot == 2, third, placed)

    packed = [asked[j * SLOT : (j + 1) * SLOT] for j in range(outgoing)]
    replies = {}

    def keep(j, top, total, out):
        out = out / total
        logs = top + jnp.log(total)
        even = pltpu.roll(out[0:SLOT], HEAD_DIM, 1)
        both = jnp.where(low, even, out[SLOT:ROWS])
        line = jnp.sum(
            terms(logs[0:SLOT], 0) + terms(logs[SLOT:ROWS], HEAD_DIM), axis=0, keepdims=True
        )
        replies[j] = jnp.where(row == META, line, both)

    attend_pages(
        outgoing,
        8,
        None,
        lambda j: unpack(packed[j]).astype(BF16),
        lambda j: pages[j],
        lambda j: packed[j][META : META + 1, 0:1],
        tokens,
        keep,
    )
    shape = (slot_rows, outgoing * SLOT)
    placed = jnp.where(drop_ref[0:1, :] == iota(shape, 0), 1.0, 0.0).astype(BF16)
    every = jnp.concatenate([replies[j] for j in range(outgoing)], axis=0).astype(BF16)
    reply = jnp.dot(placed, every, preferred_element_type=F32)
    reply16[...] = reply.astype(BF16)
    replying = copy_of(reply16, reply_hbm, sems.at[5])
    replying.start()
    for copy in parked + [replying]:
        copy.wait()


def combine_kernel(
    heads, pool, meta_hbm, state_hbm, wo_hbm, hidden_hbm, gain_hbm, router_hbm,
    routes_hbm, reply_ref,
    part_ref, meta_ref, hidden_ref, gain_ref, router_ref, routes_ref,
    meta, state, wo, gain, tops, accs, scaled, reply, finals, sems,
):
    requests = state.shape[0]
    inbox = reply_ref.shape[0] // SLOT
    chunks = -(-heads // 2)
    small = [
        copy_of(meta_hbm, meta, sems.at[0]),
        copy_of(state_hbm, state, sems.at[1]),
    ]
    weights = copies_of(wo_hbm, wo, sems, 2)
    gaining = copy_of(gain_hbm, gain, sems.at[6])
    later = [
        copy_of(meta_hbm, meta_ref, sems.at[7]),
        copy_of(hidden_hbm, hidden_ref, sems.at[8]),
        copy_of(router_hbm, router_ref, sems.at[9]),
        copy_of(routes_hbm, routes_ref, sems.at[10]),
    ]
    for copy in small + weights + [gaining] + later:
        copy.start()
    reply[...] = reply_ref[...].astype(F32)
    low = iota((SLOT, LANES), 1) < HEAD_DIM
    lane = iota((SLOT, LANES), 1)
    row = iota((SLOT, LANES), 0)
    mine = (lane % HEAD_DIM) // 3 == row

    def place_of(s):
        lender = s // CAP ^ (inbox // CAP // 2)
        owner = meta[0, pool + lender * CAP + s % CAP]
        return jnp.where(owner < 0, requests, owner)

    def logs_of(s):
        line = reply[s * SLOT + META : s * SLOT + META + 1, :]
        line = jnp.where(mine, jnp.broadcast_to(line, (SLOT, LANES)), 0.0)
        even = jnp.sum(jnp.where(low, line, 0.0), axis=1, keepdims=True)
        odd = jnp.sum(jnp.where(low, 0.0, line), axis=1, keepdims=True)
        logs = jnp.concatenate([even, odd], axis=0)
        return jnp.broadcast_to(logs, (ROWS, LANES))

    logs = [logs_of(s) for s in range(inbox)]
    for copy in small:
        copy.wait()
    low16 = iota(state.shape, 2) < HEAD_DIM
    start = state[...]
    before = jnp.where(low16, start, pltpu.roll(start, HEAD_DIM, 2))
    tops[0:requests] = before

    def sum_of(s):
        packed = reply[s * SLOT : (s + 1) * SLOT, :]
        even = jnp.where(low, 1.0, pltpu.roll(packed, HEAD_DIM, 1))
        odd = jnp.where(low, 1.0, packed)
        return jnp.concatenate([even, odd], axis=0)

    merge_pages(
        [place_of(s) for s in range(inbox)],
        lambda s: logs[s],
        sum_of,
        tops,
        accs,
        scaled,
        jnp.where(low16, 1.0, start),
        before,
    )
    whole = accs[0:requests]
    finals[...] = (whole / pltpu.roll(whole, HEAD_DIM, 2)).reshape(
        requests * ROWS, LANES
    )
    wide = iota((requests, LANES), 1) < HEAD_DIM
    parts = []
    for j in range(chunks):
        even = finals[pl.ds(j, requests, stride=ROWS), :]
        odd = finals[pl.ds(SLOT + j, requests, stride=ROWS), :]
        parts.append(jnp.where(wide, pltpu.roll(even, HEAD_DIM, 1), odd).astype(BF16))
    attention = jnp.concatenate(parts, axis=1)[:, : heads * HEAD_DIM]
    for copy in weights:
        copy.wait()
    part_ref[...] = jnp.dot(attention, wo[...], preferred_element_type=F32).astype(BF16)
    gaining.wait()
    gain_ref[...] = gain[...].reshape(1, gain.shape[0])
    for copy in later:
        copy.wait()


def load_kernel(wd_hbm, order_hbm, wd_ref, sems):
    del order_hbm
    copies = copies_of(wd_hbm, wd_ref, sems, 0)
    for copy in copies:
        copy.start()
    for copy in copies:
        copy.wait()


def finish_kernel(attended_ref, own_ref, other_ref, attended_out, experts_out):
    attended_out[...] = attended_ref[...]
    experts_out[...] = (own_ref[...] + other_ref[...].astype(F32)).astype(BF16)


def own_rows(values, first):
    half = values.shape[0] // 2
    return jnp.where(first, values[:half], values[half:])


def residual_kernel(
    tp, count, meta_ref, hidden_ref, *refs,
):
    pieces = refs[:count]
    gain_ref, attended_ref, input_ref, again_ref = refs[count:]
    requests = hidden_ref.shape[0]
    if count == 2:
        summed = pieces[0][...].astype(F32) + pieces[1][...].astype(F32)
    else:
        summed = pieces[0][0:requests, :].astype(F32)
        for t in range(1, tp):
            part = pieces[0][t * requests : (t + 1) * requests, :]
            summed = summed + part.astype(F32)
    attended = (hidden_ref[...].astype(F32) + RESID_SCALE * summed).astype(BF16)
    if count == 2:
        attended_ref[...] = own_rows(attended, meta_ref[3:4, 0:1] == 0)
    else:
        attended_ref[...] = attended
    ffn_input = norm_rows(attended.astype(F32), gain_ref[...])
    input_ref[...] = ffn_input
    again_ref[...] = ffn_input


def gate_column(units, meta_ref, input_ref, router_ref, routes_ref):
    ffn_input = input_ref[...]
    requests = ffn_input.shape[0]
    logits = lax.dot_general(router_ref[...], ffn_input, NT, preferred_element_type=F32)
    expert = iota(logits.shape, 0)
    named = jnp.zeros(logits.shape, F32)
    for k in range(routes_ref.shape[0]):
        named = jnp.where(routes_ref[k : k + 1, :] == expert, 1.0, named)
    chosen = named > 0.5
    top = jnp.max(jnp.where(chosen, logits, NEG_FILL), axis=0, keepdims=True)
    weights = jnp.where(chosen, jnp.exp(logits - top), 0.0)
    total = jnp.sum(weights, axis=0, keepdims=True)
    mine = expert == meta_ref[3:4, 0:1] * units // FF
    line = jnp.sum(jnp.where(mine, weights, 0.0), axis=0, keepdims=True) / total
    diagonal = iota((requests, requests), 0) == iota((requests, requests), 1)
    line = jnp.where(diagonal, jnp.broadcast_to(line, (requests, requests)), 0.0)
    return jnp.sum(line, axis=1, keepdims=True)


def expert_kernel(
    units, meta_ref, lifted_ref, input_ref, router_ref, routes_ref, wd_ref, *outs
):
    column = gate_column(units, meta_ref, input_ref, router_ref, routes_ref)
    gate = lifted_ref[0]
    active = gate / (1.0 + jnp.exp(-gate)) * lifted_ref[1] * column
    share = jnp.dot(active.astype(BF16), wd_ref[...], preferred_element_type=F32)
    if len(outs) == 2:
        first = meta_ref[3:4, 0:1] == 0
        outs[0][...] = own_rows(share, first)
        outs[1][...] = own_rows(share, jnp.logical_not(first)).astype(BF16)
    else:
        outs[0][...] = share.astype(BF16)


def call(body, outs, in_specs, scratch=(), limit=16, flops=0, moved=0):
    return pl.pallas_call(
        body,
        out_shape=outs,
        in_specs=in_specs,
        out_specs=[VMEM if isinstance(o, jax.ShapeDtypeStruct) else HBM for o in outs],
        scratch_shapes=list(scratch),
        compiler_params=pltpu.CompilerParams(vmem_limit_bytes=limit << 20),
        cost_estimate=pl.CostEstimate(
            flops=flops, bytes_accessed=moved, transcendentals=0
        ),
    )


def swap(values):
    return lax.ppermute(values, "tensor", [(0, 1), (1, 0)])


def on_device(
    hidden,
    attn_gain,
    w_query,
    w_keyvalue,
    w_output,
    cache,
    page_table,
    ctx_len,
    move_dest,
    ffn_gain,
    router,
    routes,
    w_in,
    w_down,
):
    replicas = lax.axis_size("replica")
    tp = lax.axis_size("tensor")
    rank = lax.axis_index("tensor").astype(jnp.int32)
    rows, width = hidden.shape
    pool, page_len, kv_local, _ = cache.shape
    outgoing = move_dest.shape[0]
    local_pages = pool - outgoing
    requests = page_table.shape[0]
    heads = w_query.shape[1] // HEAD_DIM
    inbox = replicas * CAP
    units = w_down.shape[0]
    assert FF % units == 0
    columns = page_len * kv_local
    entries = -(-(pool + inbox) // LANES) * LANES
    struct = jax.ShapeDtypeStruct
    pair = tp == 2
    ids = rank.reshape(1)

    def pin(values):
        return pltpu.with_memory_space_constraint(values, pltpu.HBM)

    def exchange(blocks, order):
        blocks = blocks.reshape(replicas, CAP * SLOT, LANES)
        blocks = lax.all_to_all(
            blocks,
            "replica",
            split_axis=0,
            concat_axis=0,
            tiled=True,
            axis_index_groups=[list(order)],
        )
        return blocks.reshape(inbox * SLOT, LANES)

    blocks = pin(cache.reshape(pool, columns, LANES))
    if pair:
        pieces = [hidden, swap(hidden)]
    else:
        pieces = [lax.all_gather(hidden, "tensor", axis=0, tiled=True)]
    meta_shape = (4, entries)
    tables_shape = (2, requests, LANES)
    own, wq, gain, tables, away, away_span, meta, lent, pick, drop = call(
        functools.partial(prepare_kernel, pool, replicas),
        [
            struct(hidden.shape, BF16),
            struct(w_query.shape, BF16),
            struct((1, width), F32),
            struct(tables_shape, F32),
            struct((inbox, requests), BF16),
            struct((inbox, LANES), F32),
            struct(meta_shape, jnp.int32),
            struct((outgoing, columns, LANES), BF16),
            struct((outgoing * SLOT, LANES), jnp.int32),
            struct((outgoing, outgoing * SLOT), jnp.int32),
        ],
        [SMEM] + [HBM] * 7,
        [
            pltpu.VMEM((1, requests), jnp.int32),
            pltpu.VMEM((page_table.shape[1], requests), jnp.int32),
            pltpu.VMEM((1, outgoing), jnp.int32),
            pltpu.VMEM((width,), F32),
            pltpu.SemaphoreType.DMA((10,)),
        ],
        moved=2 * w_query.size,
    )(
        ids,
        pin(hidden),
        pin(ctx_len.reshape(1, requests)),
        pin(page_table.T),
        pin(move_dest.reshape(1, outgoing)),
        pin(attn_gain),
        pin(w_query),
        blocks,
    )
    if pair:
        pieces[0] = own
    hidden_all, normed, packed, sends = call(
        functools.partial(query_kernel, len(pieces)),
        [
            struct((requests, width), BF16),
            struct((requests, width), BF16),
            struct((requests * SLOT, LANES), F32),
            struct((inbox * SLOT, LANES), BF16),
        ],
        [VMEM] * (len(pieces) + 6),
        [
            pltpu.VMEM((requests * SLOT, LANES), F32),
            pltpu.VMEM((inbox * SLOT, LANES), F32),
        ],
        flops=4 * requests * width * w_query.shape[1],
        moved=2 * w_query.size,
    )(meta, *pieces, gain, wq, tables, away, away_span)
    asked = exchange(sends, range(replicas)[::-1])
    replies, meta_far, packed_far, normed_far, tables_far, hidden_far = call(
        functools.partial(lent_kernel, heads, kv_local),
        [
            pltpu.HBM((inbox * SLOT, LANES), BF16),
            pltpu.HBM(meta_shape, jnp.int32),
            pltpu.HBM((requests * SLOT, LANES), F32),
            pltpu.HBM((requests, width), BF16),
            pltpu.HBM(tables_shape, F32),
            pltpu.HBM((requests, width), BF16),
        ],
        [VMEM] * 9,
        [
            pltpu.VMEM((inbox * SLOT, LANES), BF16),
            pltpu.SemaphoreType.DMA((6,)),
        ],
        flops=4 * ROWS * columns * LANES * outgoing,
        moved=2 * columns * LANES * outgoing,
    )(asked, lent, pick, drop, meta, packed, normed, tables, hidden_all)
    returned = exchange(replies, [r ^ replicas // 2 for r in range(replicas)])
    (state,) = call(
        functools.partial(local_kernel, heads, kv_local),
        [pltpu.HBM((requests, ROWS, LANES), F32)],
        [HBM] * 6,
        [
            pltpu.SMEM(meta_shape, jnp.int32),
            pltpu.VMEM((requests * SLOT, LANES), F32),
            pltpu.VMEM((requests, width), BF16),
            pltpu.VMEM((width * kv_local, LANES), BF16),
            pltpu.VMEM(tables_shape, F32),
            pltpu.VMEM((local_pages, columns, LANES), BF16),
            pltpu.VMEM((requests, ROWS, LANES), F32),
            pltpu.VMEM((requests * ROWS, LANES), F32),
            pltpu.VMEM((local_pages, ROWS, LANES), F32),
            pltpu.VMEM((local_pages, ROWS, LANES), F32),
            pltpu.VMEM((requests + 1, ROWS, LANES), F32),
            pltpu.VMEM((requests + 1, ROWS, LANES), F32),
            pltpu.VMEM((local_pages, ROWS, LANES), F32),
            pltpu.SemaphoreType.DMA((6 + local_pages,)),
        ],
        limit=24,
        flops=4 * ROWS * columns * LANES * local_pages,
        moved=2 * columns * LANES * local_pages,
    )(
        pin(meta_far),
        pin(packed_far),
        pin(normed_far),
        pin(w_keyvalue.reshape(width * kv_local, LANES)),
        pin(tables_far),
        blocks,
    )
    part, meta, hidden_all, gain, router_t, routes_t = call(
        functools.partial(combine_kernel, heads, pool),
        [
            struct((requests, width), BF16),
            struct(meta_shape, jnp.int32),
            struct((requests, width), BF16),
            struct((1, width), F32),
            struct(router.shape[::-1], BF16),
            struct(routes.shape[::-1], jnp.int32),
        ],
        [HBM] * 7 + [VMEM],
        [
            pltpu.SMEM(meta_shape, jnp.int32),
            pltpu.VMEM((requests, ROWS, LANES), F32),
            pltpu.VMEM(w_output.shape, BF16),
            pltpu.VMEM((width,), F32),
            pltpu.VMEM((requests + 1, ROWS, LANES), F32),
            pltpu.VMEM((requests + 1, ROWS, LANES), F32),
            pltpu.VMEM((inbox, ROWS, LANES), F32),
            pltpu.VMEM((inbox * SLOT, LANES), F32),
            pltpu.VMEM((requests * ROWS, LANES), F32),
            pltpu.SemaphoreType.DMA((11,)),
        ],
        flops=2 * requests * w_output.size,
        moved=2 * w_output.size,
    )(
        pin(meta_far), pin(state), pin(w_output), pin(hidden_far), pin(ffn_gain),
        pin(router.T), pin(routes.T), returned,
    )
    if pair:
        parts = [part, swap(part)]
    else:
        parts = [lax.all_gather(part, "tensor", axis=0, tiled=True)]
    (wd,) = call(
        load_kernel,
        [struct(w_down.shape, BF16)],
        [HBM, ANY],
        [pltpu.SemaphoreType.DMA((4,))],
        moved=2 * w_down.size,
    )(pin(w_down), part)
    attended, ffn_input, ffn_again = call(
        functools.partial(residual_kernel, tp, len(parts)),
        [
            struct((rows if pair else requests, width), BF16),
            struct((requests, width), BF16),
            struct((requests, width), BF16),
        ],
        [VMEM] * (len(parts) + 3),
        flops=2 * requests * width,
        moved=8 * requests * width,
    )(meta, hidden_all, *parts, gain)
    lifted = jnp.einsum("rd,dsu->sru", ffn_input, w_in, preferred_element_type=F32)
    shapes = [struct((requests, width), BF16)]
    if pair:
        shapes = [struct((rows, width), F32), struct((rows, width), BF16)]
    shares = call(
        functools.partial(expert_kernel, units),
        shapes,
        [VMEM] * 6,
        flops=2 * requests * w_down.size,
        moved=2 * w_down.size,
    )(meta, lifted, ffn_again, router_t, routes_t, wd)
    if pair:
        out = struct((rows, width), BF16)
        return tuple(
            call(finish_kernel, [out, out], [VMEM] * 3)(attended, shares[0], swap(shares[1]))
        )
    shares = lax.all_gather(shares[0], "tensor", axis=0)
    mine = lax.dynamic_slice_in_dim(shares, rank * rows, rows, axis=1)
    experts_out = jnp.sum(mine.astype(F32), axis=0).astype(BF16)
    attended = lax.dynamic_slice_in_dim(attended, rank * rows, rows, axis=0)
    return attended, experts_out


def solution(mesh):
    placed = (
        P(("replica", "tensor"), None),
        P(),
        P(None, "tensor"),
        P(None, "tensor", None),
        P("tensor", None),
        P("replica", None, "tensor", None),
        P("replica", None),
        P("replica"),
        P("replica"),
        P(),
        P(),
        P("replica", None),
        P(None, None, "tensor"),
        P("tensor", None),
    )
    return jax.shard_map(
        on_device,
        mesh=mesh,
        in_specs=placed,
        out_specs=(P(("replica", "tensor"), None), P(("replica", "tensor"), None)),
        check_vma=False,
    )
```

```python
import functools
import math

import jax
import jax.numpy as jnp
from jax import lax
from jax.experimental import pallas as pl
from jax.experimental.pallas import tpu as pltpu
from jax.sharding import PartitionSpec as P

HEAD_DIM = 64
EXPERTS = 40
FF = 512
CAP = 2
LANES = 128
SLOT = 8
ROWS = 16
META = 6

ATTN_SCALE = 0.015625
RESID_SCALE = 0.22
ROPE_BASE = 10000.0
EPSILON = 1e-06
NEG_FILL = -1e30

F32 = jnp.float32
BF16 = jnp.bfloat16
VMEM = pl.BlockSpec(memory_space=pltpu.VMEM)
SMEM = pl.BlockSpec(memory_space=pltpu.SMEM)
ANY = pl.BlockSpec(memory_space=pl.ANY)
HBM = pl.BlockSpec(memory_space=pltpu.HBM)
NT = (((1,), (1,)), ((), ()))


def iota(shape, axis):
    return lax.broadcasted_iota(jnp.int32, shape, axis)


def norm_rows(values, gain):
    factor = lax.rsqrt(jnp.mean(values * values, axis=-1, keepdims=True) + EPSILON)
    return (values * factor * gain).astype(BF16)


def rope_tables(ctx_row, requests):
    diagonal = iota((requests, requests), 0) == iota((requests, requests), 1)
    ctx = jnp.broadcast_to(ctx_row.astype(F32), (requests, requests))
    ctx = jnp.sum(jnp.where(diagonal, ctx, 0.0), axis=1, keepdims=True)
    lane = iota((requests, LANES), 1)
    index = (lane % (HEAD_DIM // 2)).astype(F32)
    inverse = jnp.exp(index * (-2.0 * math.log(ROPE_BASE) / HEAD_DIM))
    angles = ctx * inverse
    sign = jnp.where(lane % HEAD_DIM < HEAD_DIM // 2, -1.0, 1.0)
    return jnp.cos(angles), jnp.sin(angles) * sign


def rotate(chunk, cosine, sine):
    lane = iota(chunk.shape, 1)
    ahead = pltpu.roll(chunk, LANES - HEAD_DIM // 2, 1)
    behind = pltpu.roll(chunk, HEAD_DIM // 2, 1)
    turned = jnp.where(lane % HEAD_DIM < HEAD_DIM // 2, ahead, behind)
    return chunk * cosine + turned * sine


def copy_of(source, target, sem):
    return pltpu.make_async_copy(source, target, sem)


def copies_of(source, target, sems, base):
    step = source.shape[0] // 4
    return [
        copy_of(
            source.at[pl.ds(i * step, step)], target.at[pl.ds(i * step, step)], sems.at[base + i]
        )
        for i in range(4)
    ]


def page_copies(cache_hbm, pages, stage, sems, base):
    starts = range(0, pages.shape[0], stage)
    return [
        copy_of(cache_hbm.at[pl.ds(p, stage)], pages.at[pl.ds(p, stage)], sems.at[base + i])
        for i, p in enumerate(starts)
    ]


def prepare_kernel(
    pool, replicas, ids_ref, hidden_hbm, ctx_hbm, table_hbm, dest_hbm, attn_gain_hbm,
    wq_hbm, cache_hbm,
    hidden_ref, wq_ref, gain_ref, tables_ref, away_ref, span_ref, meta_ref, lent_ref,
    pick_ref, drop_ref,
    ctx, table, dest, gain, sems,
):
    inbox = replicas * CAP
    requests = ctx.shape[1]
    entries = meta_ref.shape[1]
    small = [
        copy_of(ctx_hbm, ctx, sems.at[0]),
        copy_of(table_hbm, table, sems.at[1]),
        copy_of(dest_hbm, dest, sems.at[2]),
        copy_of(attn_gain_hbm, gain, sems.at[3]),
    ]
    large = [copy_of(hidden_hbm, hidden_ref, sems.at[4])]
    large += copies_of(wq_hbm, wq_ref, sems, 5)
    lending = pl.ds(pool - lent_ref.shape[0], lent_ref.shape[0])
    large.append(copy_of(cache_hbm.at[lending], lent_ref, sems.at[9]))
    for copy in small + large:
        copy.start()
    for copy in small:
        copy.wait()
    gain_ref[...] = gain[...].reshape(1, gain.shape[0])
    ctx_row = ctx[...]

    def claims(values):
        held = jnp.zeros(values.shape, F32)
        spans = jnp.zeros(values.shape, F32)
        for k in range(table.shape[0]):
            match = table[k : k + 1, :] == values
            filled = jnp.clip(ctx_row - k * 128, 0, 128).astype(F32)
            held = jnp.where(match, 1.0, held)
            spans = jnp.where(match, filled, spans)
        return held.astype(BF16), spans

    held, spans = claims(iota((entries, requests), 0))
    numbers = (iota((SLOT, requests), 1) + 1).astype(BF16)
    ones = jnp.ones((SLOT, requests), BF16)
    holder = lax.dot_general(numbers, held, NT, preferred_element_type=F32)
    covered = lax.dot_general(ones, spans.astype(BF16), NT, preferred_element_type=F32)
    meta_ref[0:1, :] = holder[0:1, :].astype(jnp.int32) - 1
    meta_ref[1:2, :] = covered[0:1, :].astype(jnp.int32)
    meta_ref[2:3, :] = jnp.zeros((1, entries), jnp.int32)
    lent = dest.shape[1]
    across = jnp.broadcast_to(dest[...].astype(F32), (lent, lent))
    row, lane = iota((lent, lent), 0), iota((lent, lent), 1)
    down = jnp.sum(jnp.where(row == lane, across, 0.0), axis=1, keepdims=True)
    same = across == down
    before = jnp.sum(jnp.where(same & (lane < row), 1.0, 0.0), axis=1, keepdims=True)
    column = (replicas - 1 - down) * CAP + before
    column = jnp.broadcast_to(column, (lent, LANES)).astype(BF16)
    before = jnp.sum(jnp.where(same & (row < lane), 1.0, 0.0), axis=0, keepdims=True)
    line = dest[...] ^ replicas // 2
    line = jnp.broadcast_to(line.astype(F32), (lent, lent))
    line = (line * CAP + before).astype(BF16)
    expand = iota((lent * SLOT, lent), 0) // SLOT == iota((lent * SLOT, lent), 1)
    expand = jnp.where(expand, 1.0, 0.0).astype(BF16)
    column = jnp.dot(expand, column, preferred_element_type=F32).astype(jnp.int32)
    pick_ref[...] = column * SLOT + iota(column.shape, 0) % SLOT
    line = lax.dot_general(line, expand, NT, preferred_element_type=F32).astype(jnp.int32)
    drop_ref[...] = line * SLOT + iota(line.shape, 1) % SLOT
    meta_ref[3:4, :] = jnp.full((1, entries), ids_ref[0], jnp.int32)
    cosine, sine = rope_tables(ctx_row, requests)
    tables_ref[0] = cosine
    tables_ref[1] = sine
    slot = iota((inbox, requests), 0)
    lender = replicas - 1 - slot // CAP
    held, spans = claims(pool + lender * CAP + slot % CAP)
    away_ref[...] = held
    away_span = jnp.sum(spans, axis=1, keepdims=True)
    numbers = (iota((inbox, requests), 1) + 1).astype(F32)
    away_owner = jnp.sum(held.astype(F32) * numbers, axis=1, keepdims=True)
    low = iota(span_ref.shape, 1) < HEAD_DIM
    span_ref[...] = jnp.where(low, away_span, away_owner)
    for copy in large:
        copy.wait()


def query_kernel(
    count, meta_ref, *refs,
):
    pieces = refs[:count]
    (gain_ref, wq_ref, tables_ref, away_ref, span_ref,
     hidden_ref, normed_ref, packed_ref, send_ref, packs, sends) = refs[count:]
    requests = hidden_ref.shape[0]
    inbox = span_ref.shape[0]
    width = wq_ref.shape[1]
    chunks = -(-width // LANES)
    if count == 1:
        hidden = pieces[0][...]
    else:
        own, other = pieces[0][...], pieces[1][...]
        first = meta_ref[3:4, 0:1] == 0
        hidden = jnp.concatenate(
            [jnp.where(first, own, other), jnp.where(first, other, own)], axis=0
        )
    hidden_ref[...] = hidden
    normed = norm_rows(hidden.astype(F32), gain_ref[...])
    normed_ref[...] = normed
    queries = jnp.dot(normed, wq_ref[...], preferred_element_type=F32)
    if chunks * LANES > width:
        pad = jnp.zeros((requests, chunks * LANES - width), F32)
        queries = jnp.concatenate([queries, pad], axis=1)
    cosine, sine = tables_ref[0], tables_ref[1]
    zeros = jnp.zeros((requests, LANES), F32)
    nothing = jnp.zeros((inbox, LANES), F32)
    for j in range(SLOT):
        here = pl.ds(j, requests, stride=SLOT)
        there = pl.ds(j, inbox, stride=SLOT)
        if j < chunks:
            chunk = rotate(queries[:, j * LANES : (j + 1) * LANES], cosine, sine)
            chunk = (chunk.astype(BF16).astype(F32) * ATTN_SCALE).astype(BF16)
            packs[here, :] = chunk.astype(F32)
            sends[there, :] = jnp.dot(away_ref[...], chunk, preferred_element_type=F32)
        else:
            packs[here, :] = zeros
            sends[there, :] = span_ref[...] if j == META else nothing
    packed_ref[...] = packs[...]
    send_ref[...] = sends[...].astype(BF16)


def unpack(packed):
    low = iota(packed.shape, 1) < HEAD_DIM
    even = jnp.where(low, packed, 0.0)
    odd = jnp.where(low, pltpu.roll(packed, HEAD_DIM, 1), 0.0)
    return jnp.concatenate([even, odd], axis=0)


def head_rows(heads):
    return [(h // 2) + SLOT * (h % 2) for h in range(heads)]


def token_of_column(heads, kv_local, columns):
    row = iota((ROWS, columns), 0)
    column = iota((ROWS, columns), 1)
    wanted = jnp.full((ROWS, columns), kv_local, jnp.int32)
    for h, place in enumerate(head_rows(heads)):
        wanted = jnp.where(row == place, h // (heads // kv_local), wanted)
    return jnp.where(column % kv_local == wanted, column // kv_local, 1 << 20)


def score_page(query, block):
    return lax.dot_general(query, block, NT, preferred_element_type=F32)


def weigh_page(scores, tokens, span):
    scores = jnp.where(tokens < span, scores, NEG_FILL)
    top = jnp.max(scores, axis=1, keepdims=True)
    weights = jnp.exp(scores - top)
    return top, jnp.sum(weights, axis=1, keepdims=True), weights.astype(BF16)


def attend_pages(
    count, stage, copies, query_of, block_of, span_of, tokens, keep, last=None
):
    stages = [range(i, min(i + stage, count)) for i in range(0, count, stage)]

    def score_stage(pages):
        if copies is not None:
            copies[pages[0] // stage].wait()
        if last is not None and pages[-1] == count - 1:
            last.wait()
        return {p: score_page(query_of(p), block_of(p)) for p in pages}

    scores = score_stage(stages[0])
    for i, pages in enumerate(stages):
        if i + 1 < len(stages):
            ahead = score_stage(stages[i + 1])
        weighed = {p: weigh_page(scores[p], tokens, span_of(p)) for p in pages}
        outs = {
            p: jnp.dot(weighed[p][2], block_of(p), preferred_element_type=F32)
            for p in pages
        }
        for p in pages:
            keep(p, weighed[p][0], weighed[p][1], outs[p])
        if i + 1 < len(stages):
            scores = ahead


def spread_queries(target, packed):
    low = iota(packed.shape, 2) < HEAD_DIM
    target[:, 0:SLOT, :] = jnp.where(low, packed, 0.0)
    target[:, SLOT:ROWS, :] = jnp.where(low, pltpu.roll(packed, HEAD_DIM, 2), 0.0)


def merge_pages(places, top_of, sum_of, top, acc, scaled, start, before):
    requests = start.shape[0]
    for p, place in enumerate(places):
        top[place] = jnp.maximum(top[place], top_of(p))
    acc[0:requests] = start * jnp.exp(before - top[0:requests])
    for p, place in enumerate(places):
        scaled[p] = sum_of(p) * jnp.exp(top_of(p) - top[place])
    for p, place in enumerate(places):
        acc[place] = acc[place] + scaled[p]


def project_heads(values, weights_ref, heads):
    if heads == 1:
        return jnp.dot(values, weights_ref[...], preferred_element_type=F32)
    rows, depth = values.shape
    wide = 1024
    part = wide // heads
    repeat = iota((part, wide), 1) // heads == iota((part, wide), 0)
    repeat = jnp.where(repeat, 1.0, 0.0).astype(BF16)
    parts = [values[:, i : i + part] for i in range(0, depth, part)]
    spread = jnp.dot(
        jnp.concatenate(parts, axis=0), repeat, preferred_element_type=F32
    ).astype(BF16)
    lane = iota((1, wide), 1) % heads
    masks = [jnp.where(lane == k, 1.0, 0.0).astype(BF16) for k in range(heads)]
    total = jnp.zeros((heads * rows, LANES), F32)
    for i in range(len(parts)):
        piece = spread[i * rows : (i + 1) * rows]
        piece = jnp.concatenate([piece * mask for mask in masks], axis=0)
        total += jnp.dot(
            piece, weights_ref[i * wide : (i + 1) * wide, :], preferred_element_type=F32
        )
    return total


def local_kernel(
    heads, kv_local, meta_hbm, packed_hbm, normed_hbm, wkv_hbm, tables_hbm, cache_hbm,
    state_hbm,
    meta, packed, normed, raw, tables, pages, queries, fresh, tops, sums, top, acc,
    scaled, sems,
):
    requests = normed.shape[0]
    count, columns, _ = pages.shape
    small = [
        copy_of(meta_hbm, meta, sems.at[0]),
        copy_of(packed_hbm, packed, sems.at[1]),
        copy_of(normed_hbm, normed, sems.at[2]),
        copy_of(tables_hbm, tables, sems.at[3]),
    ]
    weights = copy_of(wkv_hbm, raw, sems.at[4])
    stage = next(n for n in (8, 5, 4, 2, 1) if count % n == 0)
    paging = page_copies(cache_hbm, pages, stage, sems, 6)
    for copy in small + paging + [weights]:
        copy.start()
    tokens = token_of_column(heads, kv_local, columns)
    lower = iota((ROWS, LANES), 1) < HEAD_DIM
    low = iota((requests, LANES), 1) < HEAD_DIM
    low16 = iota((requests, ROWS, LANES), 2) < HEAD_DIM
    top[...] = jnp.full(top.shape, NEG_FILL, F32)
    acc[...] = jnp.zeros(acc.shape, F32)
    for copy in small:
        copy.wait()
    spread_queries(queries, packed[...].reshape(requests, SLOT, LANES))

    def place_of(p):
        owner = meta[0, p]
        return jnp.where(owner < 0, requests, owner)

    places = [place_of(p) for p in range(count)]

    def keep(p, page_top, total, out):
        tops[p] = jnp.broadcast_to(page_top, (ROWS, LANES))
        sums[p] = jnp.where(lower, total, out)
        top[places[p]] = jnp.maximum(top[places[p]], tops[p])

    attend_pages(
        count,
        stage,
        paging,
        lambda p: queries[jnp.maximum(meta[0, p], 0)].astype(BF16),
        lambda p: pages[p],
        lambda p: meta[1, p],
        tokens,
        keep,
        weights,
    )
    cosine = jnp.where(low, tables[0], 1.0)
    sine = jnp.where(low, tables[1], 0.0)
    projected = project_heads(normed[...], raw, kv_local)
    new = [
        rotate(projected[k * requests : (k + 1) * requests], cosine, sine)
        .astype(BF16)
        .astype(F32)
        for k in range(kv_local)
    ]
    used = {place: h for h, place in enumerate(head_rows(heads))}
    for place in range(ROWS):
        value = jnp.zeros((requests, LANES), F32)
        if place in used:
            value = new[used[place] // (heads // kv_local)]
        fresh[pl.ds(place, requests, stride=ROWS), :] = value
    for p, place in enumerate(places):
        scaled[p] = sums[p] * jnp.exp(tops[p] - top[place])
    for p, place in enumerate(places):
        acc[place] = acc[place] + scaled[p]
    added = fresh[...].reshape(requests, ROWS, LANES)
    score = jnp.sum(queries[...] * added, axis=2, keepdims=True)
    score = jnp.broadcast_to(score, added.shape)
    before = top[0:requests]
    highest = jnp.maximum(before, score)
    whole = acc[0:requests] * jnp.exp(before - highest)
    whole = whole + jnp.where(low16, 1.0, added) * jnp.exp(score - highest)
    acc[0:requests] = jnp.where(
        low16, highest + jnp.log(whole), whole / pltpu.roll(whole, HEAD_DIM, 2)
    )
    parked = copy_of(acc.at[pl.ds(0, requests)], state_hbm, sems.at[5])
    parked.start()
    parked.wait()


def lent_kernel(
    heads, kv_local, asked_ref, pages, pick_ref, drop_ref, meta_ref, packed_ref,
    normed_ref, tables_ref, hidden_ref,
    reply_hbm, meta_hbm, packed_hbm, normed_hbm, tables_hbm, hidden_hbm,
    reply16, sems,
):
    outgoing, columns, _ = pages.shape
    parked = [
        copy_of(packed_ref, packed_hbm, sems.at[0]),
        copy_of(normed_ref, normed_hbm, sems.at[1]),
        copy_of(hidden_ref, hidden_hbm, sems.at[2]),
        copy_of(tables_ref, tables_hbm, sems.at[3]),
        copy_of(meta_ref, meta_hbm, sems.at[4]),
    ]
    for copy in parked:
        copy.start()
    slot_rows = asked_ref.shape[0]
    shape = (outgoing * SLOT, slot_rows)
    chosen = jnp.where(pick_ref[:, 0:1] == iota(shape, 1), 1.0, 0.0).astype(BF16)
    asked = jnp.dot(chosen, asked_ref[...], preferred_element_type=F32)
    tokens = token_of_column(heads, kv_local, columns).astype(F32)
    low = iota((SLOT, LANES), 1) < HEAD_DIM
    lane = iota((SLOT, LANES), 1)
    row = iota((SLOT, LANES), 0)

    def terms(total, offset):
        leading = total.astype(BF16).astype(F32)
        rest = total - leading
        second = rest.astype(BF16).astype(F32)
        third = rest - second
        spot = lane - offset - 3 * row
        placed = jnp.where(spot == 0, leading, 0.0)
        placed = jnp.where(spot == 1, second, placed)
        return jnp.where(spot == 2, third, placed)

    packed = [asked[j * SLOT : (j + 1) * SLOT] for j in range(outgoing)]
    replies = {}

    def keep(j, top, total, out):
        out = out / total
        logs = top + jnp.log(total)
        even = pltpu.roll(out[0:SLOT], HEAD_DIM, 1)
        both = jnp.where(low, even, out[SLOT:ROWS])
        line = jnp.sum(
            terms(logs[0:SLOT], 0) + terms(logs[SLOT:ROWS], HEAD_DIM), axis=0, keepdims=True
        )
        owner = packed[j][META : META + 1, LANES - 1 : LANES]
        line = jnp.where(lane[0:1, :] == LANES - 1, owner, line)
        replies[j] = jnp.where(row == META, line, both)

    attend_pages(
        outgoing,
        8,
        None,
        lambda j: unpack(packed[j]).astype(BF16),
        lambda j: pages[j],
        lambda j: packed[j][META : META + 1, 0:1],
        tokens,
        keep,
    )
    shape = (slot_rows, outgoing * SLOT)
    placed = jnp.where(drop_ref[0:1, :] == iota(shape, 0), 1.0, 0.0).astype(BF16)
    every = jnp.concatenate([replies[j] for j in range(outgoing)], axis=0).astype(BF16)
    reply = jnp.dot(placed, every, preferred_element_type=F32)
    reply16[...] = reply.astype(BF16)
    replying = copy_of(reply16, reply_hbm, sems.at[5])
    replying.start()
    for copy in parked + [replying]:
        copy.wait()


def combine_kernel(
    heads, meta_hbm, state_hbm, wo_hbm, hidden_hbm, gain_hbm, router_hbm, routes_hbm,
    wd_hbm, reply_ref,
    part_ref, meta_ref, hidden_ref, gain_ref, router_ref, routes_ref, wd_ref,
    state, wo, gain, tops, accs, scaled, reply, finals, sems,
):
    requests = state.shape[0]
    inbox = reply_ref.shape[0] // SLOT
    chunks = -(-heads // 2)
    arriving = copy_of(state_hbm, state, sems.at[0])
    weights = copies_of(wo_hbm, wo, sems, 1)
    gaining = copy_of(gain_hbm, gain, sems.at[5])
    later = [
        copy_of(meta_hbm, meta_ref, sems.at[6]),
        copy_of(hidden_hbm, hidden_ref, sems.at[7]),
        copy_of(router_hbm, router_ref, sems.at[8]),
        copy_of(routes_hbm, routes_ref, sems.at[9]),
        copy_of(wd_hbm.at[pl.ds(0, wd_ref.shape[0])], wd_ref, sems.at[10]),
    ]
    for copy in [arriving] + weights + [gaining] + later:
        copy.start()
    reply[...] = reply_ref[...].astype(F32)
    tops[...] = jnp.full(tops.shape, NEG_FILL, F32)
    accs[...] = jnp.zeros(accs.shape, F32)
    low = iota((SLOT, LANES), 1) < HEAD_DIM
    lane = iota((SLOT, LANES), 1)
    row = iota((SLOT, LANES), 0)
    mine = (lane % HEAD_DIM) // 3 == row

    def place_of(s):
        owner = reply[s * SLOT + META : s * SLOT + META + 1, :][0, LANES - 1]
        owner = owner.astype(jnp.int32) - 1
        return jnp.where(owner < 0, requests, owner)

    def logs_of(s):
        line = reply[s * SLOT + META : s * SLOT + META + 1, :]
        line = jnp.where(mine, jnp.broadcast_to(line, (SLOT, LANES)), 0.0)
        even = jnp.sum(jnp.where(low, line, 0.0), axis=1, keepdims=True)
        odd = jnp.sum(jnp.where(low, 0.0, line), axis=1, keepdims=True)
        logs = jnp.concatenate([even, odd], axis=0)
        return jnp.broadcast_to(logs, (ROWS, LANES))

    def sum_of(s):
        packed = reply[s * SLOT : (s + 1) * SLOT, :]
        even = jnp.where(low, 1.0, pltpu.roll(packed, HEAD_DIM, 1))
        odd = jnp.where(low, 1.0, packed)
        return jnp.concatenate([even, odd], axis=0)

    places = [place_of(s) for s in range(inbox)]
    logs = [logs_of(s) for s in range(inbox)]
    for s, place in enumerate(places):
        tops[place] = jnp.maximum(tops[place], logs[s])
    for s, place in enumerate(places):
        scaled[s] = sum_of(s) * jnp.exp(logs[s] - tops[place])
    for s, place in enumerate(places):
        accs[place] = accs[place] + scaled[s]
    arriving.wait()
    low16 = iota(state.shape, 2) < HEAD_DIM
    start = state[...]
    before = jnp.where(low16, start, pltpu.roll(start, HEAD_DIM, 2))
    remote = tops[0:requests]
    highest = jnp.maximum(before, remote)
    whole = accs[0:requests] * jnp.exp(remote - highest)
    whole = whole + jnp.where(low16, 1.0, start) * jnp.exp(before - highest)
    finals[...] = (whole / pltpu.roll(whole, HEAD_DIM, 2)).reshape(
        requests * ROWS, LANES
    )
    wide = iota((requests, LANES), 1) < HEAD_DIM
    parts = []
    for j in range(chunks):
        even = finals[pl.ds(j, requests, stride=ROWS), :]
        odd = finals[pl.ds(SLOT + j, requests, stride=ROWS), :]
        parts.append(jnp.where(wide, pltpu.roll(even, HEAD_DIM, 1), odd).astype(BF16))
    attention = jnp.concatenate(parts, axis=1)[:, : heads * HEAD_DIM]
    for copy in weights:
        copy.wait()
    part_ref[...] = jnp.dot(attention, wo[...], preferred_element_type=F32).astype(BF16)
    gaining.wait()
    gain_ref[...] = gain[...].reshape(1, gain.shape[0])
    for copy in later:
        copy.wait()


def load_kernel(wd_hbm, order_hbm, wd_ref, sem):
    del order_hbm
    rows = wd_ref.shape[0]
    copy = copy_of(wd_hbm.at[pl.ds(wd_hbm.shape[0] - rows, rows)], wd_ref, sem)
    copy.start()
    copy.wait()


def finish_kernel(attended_ref, own_ref, other_ref, attended_out, experts_out):
    attended_out[...] = attended_ref[...]
    experts_out[...] = (own_ref[...] + other_ref[...].astype(F32)).astype(BF16)


def own_rows(values, first):
    half = values.shape[0] // 2
    return jnp.where(first, values[:half], values[half:])


def residual_kernel(
    tp, count, meta_ref, hidden_ref, *refs,
):
    pieces = refs[:count]
    gain_ref, attended_ref, input_ref, again_ref = refs[count:]
    requests = hidden_ref.shape[0]
    if count == 2:
        summed = pieces[0][...].astype(F32) + pieces[1][...].astype(F32)
    else:
        summed = pieces[0][0:requests, :].astype(F32)
        for t in range(1, tp):
            part = pieces[0][t * requests : (t + 1) * requests, :]
            summed = summed + part.astype(F32)
    attended = (hidden_ref[...].astype(F32) + RESID_SCALE * summed).astype(BF16)
    if count == 2:
        attended_ref[...] = own_rows(attended, meta_ref[3:4, 0:1] == 0)
    else:
        attended_ref[...] = attended
    ffn_input = norm_rows(attended.astype(F32), gain_ref[...])
    input_ref[...] = ffn_input
    again_ref[...] = ffn_input


def gate_column(units, meta_ref, input_ref, router_ref, routes_ref):
    ffn_input = input_ref[...]
    requests = ffn_input.shape[0]
    logits = lax.dot_general(router_ref[...], ffn_input, NT, preferred_element_type=F32)
    expert = iota(logits.shape, 0)
    named = jnp.zeros(logits.shape, F32)
    for k in range(routes_ref.shape[0]):
        named = jnp.where(routes_ref[k : k + 1, :] == expert, 1.0, named)
    chosen = named > 0.5
    top = jnp.max(jnp.where(chosen, logits, NEG_FILL), axis=0, keepdims=True)
    weights = jnp.where(chosen, jnp.exp(logits - top), 0.0)
    total = jnp.sum(weights, axis=0, keepdims=True)
    mine = expert == meta_ref[3:4, 0:1] * units // FF
    line = jnp.sum(jnp.where(mine, weights, 0.0), axis=0, keepdims=True) / total
    diagonal = iota((requests, requests), 0) == iota((requests, requests), 1)
    line = jnp.where(diagonal, jnp.broadcast_to(line, (requests, requests)), 0.0)
    return jnp.sum(line, axis=1, keepdims=True)


def expert_kernel(
    units, meta_ref, lifted_ref, input_ref, router_ref, routes_ref, wd_ref, wd_rest_ref,
    *outs
):
    column = gate_column(units, meta_ref, input_ref, router_ref, routes_ref)
    gate = lifted_ref[0]
    active = gate / (1.0 + jnp.exp(-gate)) * lifted_ref[1] * column
    active = active.astype(BF16)
    half = wd_ref.shape[0]
    share = jnp.dot(active[:, :half], wd_ref[...], preferred_element_type=F32)
    share += jnp.dot(active[:, half:], wd_rest_ref[...], preferred_element_type=F32)
    if len(outs) == 2:
        first = meta_ref[3:4, 0:1] == 0
        outs[0][...] = own_rows(share, first)
        outs[1][...] = own_rows(share, jnp.logical_not(first)).astype(BF16)
    else:
        outs[0][...] = share.astype(BF16)


def call(body, outs, in_specs, scratch=(), limit=16, flops=0, moved=0):
    return pl.pallas_call(
        body,
        out_shape=outs,
        in_specs=in_specs,
        out_specs=[VMEM if isinstance(o, jax.ShapeDtypeStruct) else HBM for o in outs],
        scratch_shapes=list(scratch),
        compiler_params=pltpu.CompilerParams(vmem_limit_bytes=limit << 20),
        cost_estimate=pl.CostEstimate(
            flops=flops, bytes_accessed=moved, transcendentals=0
        ),
    )


def swap(values):
    return lax.ppermute(values, "tensor", [(0, 1), (1, 0)])


def on_device(
    hidden,
    attn_gain,
    w_query,
    w_keyvalue,
    w_output,
    cache,
    page_table,
    ctx_len,
    move_dest,
    ffn_gain,
    router,
    routes,
    w_in,
    w_down,
):
    replicas = lax.axis_size("replica")
    tp = lax.axis_size("tensor")
    rank = lax.axis_index("tensor").astype(jnp.int32)
    rows, width = hidden.shape
    pool, page_len, kv_local, _ = cache.shape
    outgoing = move_dest.shape[0]
    local_pages = pool - outgoing
    requests = page_table.shape[0]
    heads = w_query.shape[1] // HEAD_DIM
    inbox = replicas * CAP
    units = w_down.shape[0]
    assert FF % units == 0
    columns = page_len * kv_local
    entries = -(-(pool + inbox) // LANES) * LANES
    struct = jax.ShapeDtypeStruct
    pair = tp == 2
    ids = rank.reshape(1)

    def pin(values):
        return pltpu.with_memory_space_constraint(values, pltpu.HBM)

    def exchange(blocks, order):
        blocks = blocks.reshape(replicas, CAP * SLOT, LANES)
        blocks = lax.all_to_all(
            blocks,
            "replica",
            split_axis=0,
            concat_axis=0,
            tiled=True,
            axis_index_groups=[list(order)],
        )
        return blocks.reshape(inbox * SLOT, LANES)

    blocks = pin(cache.reshape(pool, columns, LANES))
    if pair:
        pieces = [hidden, swap(hidden)]
    else:
        pieces = [lax.all_gather(hidden, "tensor", axis=0, tiled=True)]
    meta_shape = (4, entries)
    tables_shape = (2, requests, LANES)
    own, wq, gain, tables, away, away_span, meta, lent, pick, drop = call(
        functools.partial(prepare_kernel, pool, replicas),
        [
            struct(hidden.shape, BF16),
            struct(w_query.shape, BF16),
            struct((1, width), F32),
            struct(tables_shape, F32),
            struct((inbox, requests), BF16),
            struct((inbox, LANES), F32),
            struct(meta_shape, jnp.int32),
            struct((outgoing, columns, LANES), BF16),
            struct((outgoing * SLOT, LANES), jnp.int32),
            struct((outgoing, outgoing * SLOT), jnp.int32),
        ],
        [SMEM] + [HBM] * 7,
        [
            pltpu.VMEM((1, requests), jnp.int32),
            pltpu.VMEM((page_table.shape[1], requests), jnp.int32),
            pltpu.VMEM((1, outgoing), jnp.int32),
            pltpu.VMEM((width,), F32),
            pltpu.SemaphoreType.DMA((10,)),
        ],
        moved=2 * w_query.size,
    )(
        ids,
        pin(hidden),
        pin(ctx_len.reshape(1, requests)),
        pin(page_table.T),
        pin(move_dest.reshape(1, outgoing)),
        pin(attn_gain),
        pin(w_query),
        blocks,
    )
    if pair:
        pieces[0] = own
    hidden_all, normed, packed, sends = call(
        functools.partial(query_kernel, len(pieces)),
        [
            struct((requests, width), BF16),
            struct((requests, width), BF16),
            struct((requests * SLOT, LANES), F32),
            struct((inbox * SLOT, LANES), BF16),
        ],
        [VMEM] * (len(pieces) + 6),
        [
            pltpu.VMEM((requests * SLOT, LANES), F32),
            pltpu.VMEM((inbox * SLOT, LANES), F32),
        ],
        flops=4 * requests * width * w_query.shape[1],
        moved=2 * w_query.size,
    )(meta, *pieces, gain, wq, tables, away, away_span)
    asked = exchange(sends, range(replicas)[::-1])
    replies, meta_far, packed_far, normed_far, tables_far, hidden_far = call(
        functools.partial(lent_kernel, heads, kv_local),
        [
            pltpu.HBM((inbox * SLOT, LANES), BF16),
            pltpu.HBM(meta_shape, jnp.int32),
            pltpu.HBM((requests * SLOT, LANES), F32),
            pltpu.HBM((requests, width), BF16),
            pltpu.HBM(tables_shape, F32),
            pltpu.HBM((requests, width), BF16),
        ],
        [VMEM] * 9,
        [
            pltpu.VMEM((inbox * SLOT, LANES), BF16),
            pltpu.SemaphoreType.DMA((6,)),
        ],
        flops=4 * ROWS * columns * LANES * outgoing,
        moved=2 * columns * LANES * outgoing,
    )(asked, lent, pick, drop, meta, packed, normed, tables, hidden_all)
    returned = exchange(replies, [r ^ replicas // 2 for r in range(replicas)])
    (state,) = call(
        functools.partial(local_kernel, heads, kv_local),
        [pltpu.HBM((requests, ROWS, LANES), F32)],
        [HBM] * 6,
        [
            pltpu.SMEM(meta_shape, jnp.int32),
            pltpu.VMEM((requests * SLOT, LANES), F32),
            pltpu.VMEM((requests, width), BF16),
            pltpu.VMEM((width * kv_local, LANES), BF16),
            pltpu.VMEM(tables_shape, F32),
            pltpu.VMEM((local_pages, columns, LANES), BF16),
            pltpu.VMEM((requests, ROWS, LANES), F32),
            pltpu.VMEM((requests * ROWS, LANES), F32),
            pltpu.VMEM((local_pages, ROWS, LANES), F32),
            pltpu.VMEM((local_pages, ROWS, LANES), F32),
            pltpu.VMEM((requests + 1, ROWS, LANES), F32),
            pltpu.VMEM((requests + 1, ROWS, LANES), F32),
            pltpu.VMEM((local_pages, ROWS, LANES), F32),
            pltpu.SemaphoreType.DMA((6 + local_pages,)),
        ],
        limit=24,
        flops=4 * ROWS * columns * LANES * local_pages,
        moved=2 * columns * LANES * local_pages,
    )(
        pin(meta_far),
        pin(packed_far),
        pin(normed_far),
        pin(w_keyvalue.reshape(width * kv_local, LANES)),
        pin(tables_far),
        blocks,
    )
    half = struct((units // 2, width), BF16)
    part, meta, hidden_all, gain, router_t, routes_t, wd = call(
        functools.partial(combine_kernel, heads),
        [
            struct((requests, width), BF16),
            struct(meta_shape, jnp.int32),
            struct((requests, width), BF16),
            struct((1, width), F32),
            struct(router.shape[::-1], BF16),
            struct(routes.shape[::-1], jnp.int32),
            half,
        ],
        [HBM] * 8 + [VMEM],
        [
            pltpu.VMEM((requests, ROWS, LANES), F32),
            pltpu.VMEM(w_output.shape, BF16),
            pltpu.VMEM((width,), F32),
            pltpu.VMEM((requests + 1, ROWS, LANES), F32),
            pltpu.VMEM((requests + 1, ROWS, LANES), F32),
            pltpu.VMEM((inbox, ROWS, LANES), F32),
            pltpu.VMEM((inbox * SLOT, LANES), F32),
            pltpu.VMEM((requests * ROWS, LANES), F32),
            pltpu.SemaphoreType.DMA((11,)),
        ],
        flops=2 * requests * w_output.size,
        moved=2 * w_output.size,
    )(
        pin(meta_far), pin(state), pin(w_output), pin(hidden_far), pin(ffn_gain),
        pin(router.T), pin(routes.T), pin(w_down), returned,
    )
    if pair:
        parts = [part, swap(part)]
    else:
        parts = [lax.all_gather(part, "tensor", axis=0, tiled=True)]
    (wd_rest,) = call(
        load_kernel,
        [half],
        [HBM, ANY],
        [pltpu.SemaphoreType.DMA],
        moved=w_down.size,
    )(pin(w_down), part)
    attended, ffn_input, ffn_again = call(
        functools.partial(residual_kernel, tp, len(parts)),
        [
            struct((rows if pair else requests, width), BF16),
            struct((requests, width), BF16),
            struct((requests, width), BF16),
        ],
        [VMEM] * (len(parts) + 3),
        flops=2 * requests * width,
        moved=8 * requests * width,
    )(meta, hidden_all, *parts, gain)
    lifted = jnp.einsum("rd,dsu->sru", ffn_input, w_in, preferred_element_type=F32)
    shapes = [struct((requests, width), BF16)]
    if pair:
        shapes = [struct((rows, width), F32), struct((rows, width), BF16)]
    shares = call(
        functools.partial(expert_kernel, units),
        shapes,
        [VMEM] * 7,
        flops=2 * requests * w_down.size,
        moved=2 * w_down.size,
    )(meta, lifted, ffn_again, router_t, routes_t, wd, wd_rest)
    if pair:
        out = struct((rows, width), BF16)
        return tuple(
            call(finish_kernel, [out, out], [VMEM] * 3)(attended, shares[0], swap(shares[1]))
        )
    shares = lax.all_gather(shares[0], "tensor", axis=0)
    mine = lax.dynamic_slice_in_dim(shares, rank * rows, rows, axis=1)
    experts_out = jnp.sum(mine.astype(F32), axis=0).astype(BF16)
    attended = lax.dynamic_slice_in_dim(attended, rank * rows, rows, axis=0)
    return attended, experts_out


def solution(mesh):
    placed = (
        P(("replica", "tensor"), None),
        P(),
        P(None, "tensor"),
        P(None, "tensor", None),
        P("tensor", None),
        P("replica", None, "tensor", None),
        P("replica", None),
        P("replica"),
        P("replica"),
        P(),
        P(),
        P("replica", None),
        P(None, None, "tensor"),
        P("tensor", None),
    )
    return jax.shard_map(
        on_device,
        mesh=mesh,
        in_specs=placed,
        out_specs=(P(("replica", "tensor"), None), P(("replica", "tensor"), None)),
        check_vma=False,
    )
```

```python
import functools
import math

import jax
import jax.numpy as jnp
from jax import lax
from jax.experimental import pallas as pl
from jax.experimental.pallas import tpu as pltpu
from jax.sharding import PartitionSpec as P

HEAD_DIM = 64
EXPERTS = 40
FF = 512
CAP = 2
LANES = 128
SLOT = 8
ROWS = 16
META = 6

ATTN_SCALE = 0.015625
RESID_SCALE = 0.22
ROPE_BASE = 10000.0
EPSILON = 1e-06
NEG_FILL = -1e30

F32 = jnp.float32
BF16 = jnp.bfloat16
VMEM = pl.BlockSpec(memory_space=pltpu.VMEM)
SMEM = pl.BlockSpec(memory_space=pltpu.SMEM)
ANY = pl.BlockSpec(memory_space=pl.ANY)
HBM = pl.BlockSpec(memory_space=pltpu.HBM)
NT = (((1,), (1,)), ((), ()))


def iota(shape, axis):
    return lax.broadcasted_iota(jnp.int32, shape, axis)


def norm_rows(values, gain):
    factor = lax.rsqrt(jnp.mean(values * values, axis=-1, keepdims=True) + EPSILON)
    return (values * factor * gain).astype(BF16)


def rope_tables(ctx_row, requests):
    diagonal = iota((requests, requests), 0) == iota((requests, requests), 1)
    ctx = jnp.broadcast_to(ctx_row.astype(F32), (requests, requests))
    ctx = jnp.sum(jnp.where(diagonal, ctx, 0.0), axis=1, keepdims=True)
    lane = iota((requests, LANES), 1)
    index = (lane % (HEAD_DIM // 2)).astype(F32)
    inverse = jnp.exp(index * (-2.0 * math.log(ROPE_BASE) / HEAD_DIM))
    angles = ctx * inverse
    sign = jnp.where(lane % HEAD_DIM < HEAD_DIM // 2, -1.0, 1.0)
    return jnp.cos(angles), jnp.sin(angles) * sign


def rotate(chunk, cosine, sine):
    lane = iota(chunk.shape, 1)
    ahead = pltpu.roll(chunk, LANES - HEAD_DIM // 2, 1)
    behind = pltpu.roll(chunk, HEAD_DIM // 2, 1)
    turned = jnp.where(lane % HEAD_DIM < HEAD_DIM // 2, ahead, behind)
    return chunk * cosine + turned * sine


def copy_of(source, target, sem):
    return pltpu.make_async_copy(source, target, sem)


def copies_of(source, target, sems, base):
    step = source.shape[0] // 4
    return [
        copy_of(
            source.at[pl.ds(i * step, step)], target.at[pl.ds(i * step, step)], sems.at[base + i]
        )
        for i in range(4)
    ]


def page_copies(cache_hbm, pages, stage, sems, base):
    starts = range(0, pages.shape[0], stage)
    return [
        copy_of(cache_hbm.at[pl.ds(p, stage)], pages.at[pl.ds(p, stage)], sems.at[base + i])
        for i, p in enumerate(starts)
    ]


def prepare_kernel(
    pool, replicas, ids_ref, hidden_hbm, ctx_hbm, table_hbm, dest_hbm, attn_gain_hbm,
    wq_hbm, cache_hbm,
    hidden_ref, wq_ref, gain_ref, tables_ref, away_ref, span_ref, meta_ref, lent_ref,
    pick_ref, drop_ref,
    ctx, table, dest, gain, sems,
):
    inbox = replicas * CAP
    requests = ctx.shape[1]
    entries = meta_ref.shape[1]
    small = [
        copy_of(ctx_hbm, ctx, sems.at[0]),
        copy_of(table_hbm, table, sems.at[1]),
        copy_of(dest_hbm, dest, sems.at[2]),
        copy_of(attn_gain_hbm, gain, sems.at[3]),
    ]
    large = [copy_of(hidden_hbm, hidden_ref, sems.at[4])]
    large += copies_of(wq_hbm, wq_ref, sems, 5)
    lending = pl.ds(pool - lent_ref.shape[0], lent_ref.shape[0])
    large.append(copy_of(cache_hbm.at[lending], lent_ref, sems.at[9]))
    for copy in small + large:
        copy.start()
    for copy in small:
        copy.wait()
    gain_ref[...] = gain[...].reshape(1, gain.shape[0])
    ctx_row = ctx[...]

    def claims(values):
        held = jnp.zeros(values.shape, F32)
        spans = jnp.zeros(values.shape, F32)
        for k in range(table.shape[0]):
            match = table[k : k + 1, :] == values
            filled = jnp.clip(ctx_row - k * 128, 0, 128).astype(F32)
            held = jnp.where(match, 1.0, held)
            spans = jnp.where(match, filled, spans)
        return held.astype(BF16), spans

    held, spans = claims(iota((entries, requests), 0))
    numbers = (iota((SLOT, requests), 1) + 1).astype(BF16)
    ones = jnp.ones((SLOT, requests), BF16)
    holder = lax.dot_general(numbers, held, NT, preferred_element_type=F32)
    covered = lax.dot_general(ones, spans.astype(BF16), NT, preferred_element_type=F32)
    meta_ref[0:1, :] = holder[0:1, :].astype(jnp.int32) - 1
    meta_ref[1:2, :] = covered[0:1, :].astype(jnp.int32)
    meta_ref[2:3, :] = jnp.zeros((1, entries), jnp.int32)
    lent = dest.shape[1]
    across = jnp.broadcast_to(dest[...].astype(F32), (lent, lent))
    row, lane = iota((lent, lent), 0), iota((lent, lent), 1)
    down = jnp.sum(jnp.where(row == lane, across, 0.0), axis=1, keepdims=True)
    same = across == down
    before = jnp.sum(jnp.where(same & (lane < row), 1.0, 0.0), axis=1, keepdims=True)
    column = (replicas - 1 - down) * CAP + before
    column = jnp.broadcast_to(column, (lent, LANES)).astype(BF16)
    before = jnp.sum(jnp.where(same & (row < lane), 1.0, 0.0), axis=0, keepdims=True)
    line = dest[...] ^ replicas // 2
    line = jnp.broadcast_to(line.astype(F32), (lent, lent))
    line = (line * CAP + before).astype(BF16)
    expand = iota((lent * SLOT, lent), 0) // SLOT == iota((lent * SLOT, lent), 1)
    expand = jnp.where(expand, 1.0, 0.0).astype(BF16)
    column = jnp.dot(expand, column, preferred_element_type=F32).astype(jnp.int32)
    pick_ref[...] = column * SLOT + iota(column.shape, 0) % SLOT
    line = lax.dot_general(line, expand, NT, preferred_element_type=F32).astype(jnp.int32)
    drop_ref[...] = line * SLOT + iota(line.shape, 1) % SLOT
    meta_ref[3:4, :] = jnp.full((1, entries), ids_ref[0], jnp.int32)
    cosine, sine = rope_tables(ctx_row, requests)
    tables_ref[0] = cosine
    tables_ref[1] = sine
    slot = iota((inbox, requests), 0)
    lender = replicas - 1 - slot // CAP
    held, spans = claims(pool + lender * CAP + slot % CAP)
    away_ref[...] = held
    away_span = jnp.sum(spans, axis=1, keepdims=True)
    span_ref[...] = jnp.broadcast_to(away_span, span_ref.shape)
    for copy in large:
        copy.wait()


def query_kernel(
    count, meta_ref, *refs,
):
    pieces = refs[:count]
    (gain_ref, wq_ref, tables_ref, away_ref, span_ref,
     hidden_ref, normed_ref, packed_ref, send_ref, packs, sends) = refs[count:]
    requests = hidden_ref.shape[0]
    inbox = span_ref.shape[0]
    width = wq_ref.shape[1]
    chunks = -(-width // LANES)
    if count == 1:
        hidden = pieces[0][...]
    else:
        own, other = pieces[0][...], pieces[1][...]
        first = meta_ref[3:4, 0:1] == 0
        hidden = jnp.concatenate(
            [jnp.where(first, own, other), jnp.where(first, other, own)], axis=0
        )
    hidden_ref[...] = hidden
    normed = norm_rows(hidden.astype(F32), gain_ref[...])
    normed_ref[...] = normed
    queries = jnp.dot(normed, wq_ref[...], preferred_element_type=F32)
    if chunks * LANES > width:
        pad = jnp.zeros((requests, chunks * LANES - width), F32)
        queries = jnp.concatenate([queries, pad], axis=1)
    cosine, sine = tables_ref[0], tables_ref[1]
    zeros = jnp.zeros((requests, LANES), F32)
    nothing = jnp.zeros((inbox, LANES), F32)
    for j in range(SLOT):
        here = pl.ds(j, requests, stride=SLOT)
        there = pl.ds(j, inbox, stride=SLOT)
        if j < chunks:
            chunk = rotate(queries[:, j * LANES : (j + 1) * LANES], cosine, sine)
            chunk = (chunk.astype(BF16).astype(F32) * ATTN_SCALE).astype(BF16)
            packs[here, :] = chunk.astype(F32)
            sends[there, :] = jnp.dot(away_ref[...], chunk, preferred_element_type=F32)
        else:
            packs[here, :] = zeros
            sends[there, :] = span_ref[...] if j == META else nothing
    packed_ref[...] = packs[...]
    send_ref[...] = sends[...].astype(BF16)


def unpack(packed):
    low = iota(packed.shape, 1) < HEAD_DIM
    even = jnp.where(low, packed, 0.0)
    odd = jnp.where(low, pltpu.roll(packed, HEAD_DIM, 1), 0.0)
    return jnp.concatenate([even, odd], axis=0)


def head_rows(heads):
    return [(h // 2) + SLOT * (h % 2) for h in range(heads)]


def token_of_column(heads, kv_local, columns):
    row = iota((ROWS, columns), 0)
    column = iota((ROWS, columns), 1)
    wanted = jnp.full((ROWS, columns), kv_local, jnp.int32)
    for h, place in enumerate(head_rows(heads)):
        wanted = jnp.where(row == place, h // (heads // kv_local), wanted)
    return jnp.where(column % kv_local == wanted, column // kv_local, 1 << 20)


def score_page(query, block):
    return lax.dot_general(query, block, NT, preferred_element_type=F32)


def weigh_page(scores, tokens, span):
    scores = jnp.where(tokens < span, scores, NEG_FILL)
    top = jnp.max(scores, axis=1, keepdims=True)
    weights = jnp.exp(scores - top)
    return top, jnp.sum(weights, axis=1, keepdims=True), weights.astype(BF16)


def attend_pages(
    count, stage, copies, query_of, block_of, span_of, tokens, keep, last=None
):
    stages = [range(i, min(i + stage, count)) for i in range(0, count, stage)]

    def score_stage(pages):
        if copies is not None:
            copies[pages[0] // stage].wait()
        if last is not None and pages[-1] == count - 1:
            last.wait()
        return {p: score_page(query_of(p), block_of(p)) for p in pages}

    scores = score_stage(stages[0])
    for i, pages in enumerate(stages):
        if i + 1 < len(stages):
            ahead = score_stage(stages[i + 1])
        weighed = {p: weigh_page(scores[p], tokens, span_of(p)) for p in pages}
        outs = {
            p: jnp.dot(weighed[p][2], block_of(p), preferred_element_type=F32)
            for p in pages
        }
        for p in pages:
            keep(p, weighed[p][0], weighed[p][1], outs[p])
        if i + 1 < len(stages):
            scores = ahead


def spread_queries(target, packed):
    low = iota(packed.shape, 2) < HEAD_DIM
    target[:, 0:SLOT, :] = jnp.where(low, packed, 0.0)
    target[:, SLOT:ROWS, :] = jnp.where(low, pltpu.roll(packed, HEAD_DIM, 2), 0.0)


def merge_pages(places, top_of, sum_of, top, acc, scaled, start, before):
    requests = start.shape[0]
    for p, place in enumerate(places):
        top[place] = jnp.maximum(top[place], top_of(p))
    acc[0:requests] = start * jnp.exp(before - top[0:requests])
    for p, place in enumerate(places):
        scaled[p] = sum_of(p) * jnp.exp(top_of(p) - top[place])
    for p, place in enumerate(places):
        acc[place] = acc[place] + scaled[p]


def project_heads(values, weights_ref, heads):
    if heads == 1:
        return jnp.dot(values, weights_ref[...], preferred_element_type=F32)
    rows, depth = values.shape
    wide = 1024
    part = wide // heads
    repeat = iota((part, wide), 1) // heads == iota((part, wide), 0)
    repeat = jnp.where(repeat, 1.0, 0.0).astype(BF16)
    parts = [values[:, i : i + part] for i in range(0, depth, part)]
    spread = jnp.dot(
        jnp.concatenate(parts, axis=0), repeat, preferred_element_type=F32
    ).astype(BF16)
    lane = iota((1, wide), 1) % heads
    masks = [jnp.where(lane == k, 1.0, 0.0).astype(BF16) for k in range(heads)]
    total = jnp.zeros((heads * rows, LANES), F32)
    for i in range(len(parts)):
        piece = spread[i * rows : (i + 1) * rows]
        piece = jnp.concatenate([piece * mask for mask in masks], axis=0)
        total += jnp.dot(
            piece, weights_ref[i * wide : (i + 1) * wide, :], preferred_element_type=F32
        )
    return total


def local_kernel(
    heads, kv_local, meta_hbm, packed_hbm, normed_hbm, wkv_hbm, tables_hbm, cache_hbm,
    state_hbm,
    meta, packed, normed, raw, tables, pages, queries, fresh, tops, sums, top, acc,
    scaled, sems,
):
    requests = normed.shape[0]
    count, columns, _ = pages.shape
    small = [
        copy_of(meta_hbm, meta, sems.at[0]),
        copy_of(packed_hbm, packed, sems.at[1]),
        copy_of(normed_hbm, normed, sems.at[2]),
        copy_of(tables_hbm, tables, sems.at[3]),
    ]
    weights = copy_of(wkv_hbm, raw, sems.at[4])
    stage = next(n for n in (10, 5, 4, 2, 1) if count % n == 0)
    paging = page_copies(cache_hbm, pages, stage, sems, 6)
    for copy in small + paging + [weights]:
        copy.start()
    tokens = token_of_column(heads, kv_local, columns)
    lower = iota((ROWS, LANES), 1) < HEAD_DIM
    low = iota((requests, LANES), 1) < HEAD_DIM
    low16 = iota((requests, ROWS, LANES), 2) < HEAD_DIM
    top[...] = jnp.full(top.shape, NEG_FILL, F32)
    acc[...] = jnp.zeros(acc.shape, F32)
    for copy in small:
        copy.wait()
    spread_queries(queries, packed[...].reshape(requests, SLOT, LANES))

    def place_of(p):
        owner = meta[0, p]
        return jnp.where(owner < 0, requests, owner)

    places = [place_of(p) for p in range(count)]

    def keep(p, page_top, total, out):
        tops[p] = jnp.broadcast_to(page_top, (ROWS, LANES))
        sums[p] = jnp.where(lower, total, out)
        top[places[p]] = jnp.maximum(top[places[p]], tops[p])

    attend_pages(
        count,
        stage,
        paging,
        lambda p: queries[jnp.maximum(meta[0, p], 0)].astype(BF16),
        lambda p: pages[p],
        lambda p: meta[1, p],
        tokens,
        keep,
        weights,
    )
    cosine = jnp.where(low, tables[0], 1.0)
    sine = jnp.where(low, tables[1], 0.0)
    projected = project_heads(normed[...], raw, kv_local)
    new = [
        rotate(projected[k * requests : (k + 1) * requests], cosine, sine)
        .astype(BF16)
        .astype(F32)
        for k in range(kv_local)
    ]
    used = {place: h for h, place in enumerate(head_rows(heads))}
    for place in range(ROWS):
        value = jnp.zeros((requests, LANES), F32)
        if place in used:
            value = new[used[place] // (heads // kv_local)]
        fresh[pl.ds(place, requests, stride=ROWS), :] = value
    for p, place in enumerate(places):
        scaled[p] = sums[p] * jnp.exp(tops[p] - top[place])
    for p, place in enumerate(places):
        acc[place] = acc[place] + scaled[p]
    added = fresh[...].reshape(requests, ROWS, LANES)
    score = jnp.sum(queries[...] * added, axis=2, keepdims=True)
    score = jnp.broadcast_to(score, added.shape)
    before = top[0:requests]
    highest = jnp.maximum(before, score)
    whole = acc[0:requests] * jnp.exp(before - highest)
    whole = whole + jnp.where(low16, 1.0, added) * jnp.exp(score - highest)
    acc[0:requests] = jnp.where(
        low16, highest + jnp.log(whole), whole / pltpu.roll(whole, HEAD_DIM, 2)
    )
    parked = copy_of(acc.at[pl.ds(0, requests)], state_hbm, sems.at[5])
    parked.start()
    parked.wait()


def lent_kernel(
    heads, kv_local, asked_ref, pages, pick_ref, drop_ref, meta_ref, packed_ref,
    normed_ref, tables_ref, hidden_ref,
    reply_hbm, meta_hbm, packed_hbm, normed_hbm, tables_hbm, hidden_hbm,
    reply16, sems,
):
    outgoing, columns, _ = pages.shape
    parked = [
        copy_of(packed_ref, packed_hbm, sems.at[0]),
        copy_of(normed_ref, normed_hbm, sems.at[1]),
        copy_of(hidden_ref, hidden_hbm, sems.at[2]),
        copy_of(tables_ref, tables_hbm, sems.at[3]),
        copy_of(meta_ref, meta_hbm, sems.at[4]),
    ]
    for copy in parked:
        copy.start()
    slot_rows = asked_ref.shape[0]
    shape = (outgoing * SLOT, slot_rows)
    chosen = jnp.where(pick_ref[:, 0:1] == iota(shape, 1), 1.0, 0.0).astype(BF16)
    asked = jnp.dot(chosen, asked_ref[...], preferred_element_type=F32)
    tokens = token_of_column(heads, kv_local, columns).astype(F32)
    low = iota((SLOT, LANES), 1) < HEAD_DIM
    lane = iota((SLOT, LANES), 1)
    row = iota((SLOT, LANES), 0)

    def terms(total, offset):
        leading = total.astype(BF16).astype(F32)
        rest = total - leading
        second = rest.astype(BF16).astype(F32)
        third = rest - second
        spot = lane - offset - 3 * row
        placed = jnp.where(spot == 0, leading, 0.0)
        placed = jnp.where(spot == 1, second, placed)
        return jnp.where(spot == 2, third, placed)

    packed = [asked[j * SLOT : (j + 1) * SLOT] for j in range(outgoing)]
    replies = {}

    def keep(j, top, total, out):
        out = out / total
        logs = top + jnp.log(total)
        even = pltpu.roll(out[0:SLOT], HEAD_DIM, 1)
        both = jnp.where(low, even, out[SLOT:ROWS])
        line = jnp.sum(
            terms(logs[0:SLOT], 0) + terms(logs[SLOT:ROWS], HEAD_DIM), axis=0, keepdims=True
        )
        replies[j] = jnp.where(row == META, line, both)

    attend_pages(
        outgoing,
        8,
        None,
        lambda j: unpack(packed[j]).astype(BF16),
        lambda j: pages[j],
        lambda j: packed[j][META : META + 1, 0:1],
        tokens,
        keep,
    )
    shape = (slot_rows, outgoing * SLOT)
    placed = jnp.where(drop_ref[0:1, :] == iota(shape, 0), 1.0, 0.0).astype(BF16)
    every = jnp.concatenate([replies[j] for j in range(outgoing)], axis=0).astype(BF16)
    reply = jnp.dot(placed, every, preferred_element_type=F32)
    reply16[...] = reply.astype(BF16)
    replying = copy_of(reply16, reply_hbm, sems.at[5])
    replying.start()
    for copy in parked + [replying]:
        copy.wait()


def combine_kernel(
    heads, pool, meta_hbm, state_hbm, wo_hbm, hidden_hbm, gain_hbm, router_hbm,
    routes_hbm, wd_hbm, reply_ref,
    part_ref, meta_ref, hidden_ref, gain_ref, router_ref, routes_ref, wd_ref,
    meta, state, wo, gain, tops, accs, scaled, reply, finals, sems,
):
    requests = state.shape[0]
    inbox = reply_ref.shape[0] // SLOT
    chunks = -(-heads // 2)
    numbers = copy_of(meta_hbm, meta, sems.at[11])
    arriving = copy_of(state_hbm, state, sems.at[0])
    weights = copies_of(wo_hbm, wo, sems, 1)
    gaining = copy_of(gain_hbm, gain, sems.at[5])
    later = [
        copy_of(meta_hbm, meta_ref, sems.at[6]),
        copy_of(hidden_hbm, hidden_ref, sems.at[7]),
        copy_of(router_hbm, router_ref, sems.at[8]),
        copy_of(routes_hbm, routes_ref, sems.at[9]),
        copy_of(wd_hbm.at[pl.ds(0, wd_ref.shape[0])], wd_ref, sems.at[10]),
    ]
    for copy in [numbers, arriving] + weights + [gaining] + later:
        copy.start()
    reply[...] = reply_ref[...].astype(F32)
    tops[...] = jnp.full(tops.shape, NEG_FILL, F32)
    accs[...] = jnp.zeros(accs.shape, F32)
    low = iota((SLOT, LANES), 1) < HEAD_DIM
    lane = iota((SLOT, LANES), 1)
    row = iota((SLOT, LANES), 0)
    mine = (lane % HEAD_DIM) // 3 == row

    def place_of(s):
        lender = s // CAP ^ (inbox // CAP // 2)
        owner = meta[0, pool + lender * CAP + s % CAP]
        return jnp.where(owner < 0, requests, owner)

    def logs_of(s):
        line = reply[s * SLOT + META : s * SLOT + META + 1, :]
        line = jnp.where(mine, jnp.broadcast_to(line, (SLOT, LANES)), 0.0)
        even = jnp.sum(jnp.where(low, line, 0.0), axis=1, keepdims=True)
        odd = jnp.sum(jnp.where(low, 0.0, line), axis=1, keepdims=True)
        logs = jnp.concatenate([even, odd], axis=0)
        return jnp.broadcast_to(logs, (ROWS, LANES))

    def sum_of(s):
        packed = reply[s * SLOT : (s + 1) * SLOT, :]
        even = jnp.where(low, 1.0, pltpu.roll(packed, HEAD_DIM, 1))
        odd = jnp.where(low, 1.0, packed)
        return jnp.concatenate([even, odd], axis=0)

    logs = [logs_of(s) for s in range(inbox)]
    numbers.wait()
    places = [place_of(s) for s in range(inbox)]
    for s, place in enumerate(places):
        tops[place] = jnp.maximum(tops[place], logs[s])
    for s, place in enumerate(places):
        scaled[s] = sum_of(s) * jnp.exp(logs[s] - tops[place])
    for s, place in enumerate(places):
        accs[place] = accs[place] + scaled[s]
    arriving.wait()
    low16 = iota(state.shape, 2) < HEAD_DIM
    start = state[...]
    before = jnp.where(low16, start, pltpu.roll(start, HEAD_DIM, 2))
    remote = tops[0:requests]
    highest = jnp.maximum(before, remote)
    whole = accs[0:requests] * jnp.exp(remote - highest)
    whole = whole + jnp.where(low16, 1.0, start) * jnp.exp(before - highest)
    finals[...] = (whole / pltpu.roll(whole, HEAD_DIM, 2)).reshape(
        requests * ROWS, LANES
    )
    wide = iota((requests, LANES), 1) < HEAD_DIM
    parts = []
    for j in range(chunks):
        even = finals[pl.ds(j, requests, stride=ROWS), :]
        odd = finals[pl.ds(SLOT + j, requests, stride=ROWS), :]
        parts.append(jnp.where(wide, pltpu.roll(even, HEAD_DIM, 1), odd).astype(BF16))
    attention = jnp.concatenate(parts, axis=1)[:, : heads * HEAD_DIM]
    for copy in weights:
        copy.wait()
    part_ref[...] = jnp.dot(attention, wo[...], preferred_element_type=F32).astype(BF16)
    gaining.wait()
    gain_ref[...] = gain[...].reshape(1, gain.shape[0])
    for copy in later:
        copy.wait()


def load_kernel(wd_hbm, order_hbm, wd_ref, sem):
    del order_hbm
    rows = wd_ref.shape[0]
    copy = copy_of(wd_hbm.at[pl.ds(wd_hbm.shape[0] - rows, rows)], wd_ref, sem)
    copy.start()
    copy.wait()


def finish_kernel(attended_ref, own_ref, other_ref, attended_out, experts_out):
    attended_out[...] = attended_ref[...]
    experts_out[...] = (own_ref[...] + other_ref[...].astype(F32)).astype(BF16)


def own_rows(values, first):
    half = values.shape[0] // 2
    return jnp.where(first, values[:half], values[half:])


def residual_kernel(
    tp, count, meta_ref, hidden_ref, *refs,
):
    pieces = refs[:count]
    gain_ref, attended_ref, input_ref, again_ref = refs[count:]
    requests = hidden_ref.shape[0]
    if count == 2:
        summed = pieces[0][...].astype(F32) + pieces[1][...].astype(F32)
    else:
        summed = pieces[0][0:requests, :].astype(F32)
        for t in range(1, tp):
            part = pieces[0][t * requests : (t + 1) * requests, :]
            summed = summed + part.astype(F32)
    attended = (hidden_ref[...].astype(F32) + RESID_SCALE * summed).astype(BF16)
    if count == 2:
        attended_ref[...] = own_rows(attended, meta_ref[3:4, 0:1] == 0)
    else:
        attended_ref[...] = attended
    ffn_input = norm_rows(attended.astype(F32), gain_ref[...])
    input_ref[...] = ffn_input
    again_ref[...] = ffn_input


def gate_column(units, meta_ref, input_ref, router_ref, routes_ref):
    ffn_input = input_ref[...]
    requests = ffn_input.shape[0]
    logits = lax.dot_general(router_ref[...], ffn_input, NT, preferred_element_type=F32)
    expert = iota(logits.shape, 0)
    named = jnp.zeros(logits.shape, F32)
    for k in range(routes_ref.shape[0]):
        named = jnp.where(routes_ref[k : k + 1, :] == expert, 1.0, named)
    chosen = named > 0.5
    top = jnp.max(jnp.where(chosen, logits, NEG_FILL), axis=0, keepdims=True)
    weights = jnp.where(chosen, jnp.exp(logits - top), 0.0)
    total = jnp.sum(weights, axis=0, keepdims=True)
    mine = expert == meta_ref[3:4, 0:1] * units // FF
    line = jnp.sum(jnp.where(mine, weights, 0.0), axis=0, keepdims=True) / total
    diagonal = iota((requests, requests), 0) == iota((requests, requests), 1)
    line = jnp.where(diagonal, jnp.broadcast_to(line, (requests, requests)), 0.0)
    return jnp.sum(line, axis=1, keepdims=True)


def expert_kernel(
    units, meta_ref, lifted_ref, input_ref, router_ref, routes_ref, wd_ref, wd_rest_ref,
    *outs
):
    column = gate_column(units, meta_ref, input_ref, router_ref, routes_ref)
    gate = lifted_ref[0]
    active = gate / (1.0 + jnp.exp(-gate)) * lifted_ref[1] * column
    active = active.astype(BF16)
    half = wd_ref.shape[0]
    share = jnp.dot(active[:, :half], wd_ref[...], preferred_element_type=F32)
    share += jnp.dot(active[:, half:], wd_rest_ref[...], preferred_element_type=F32)
    if len(outs) == 2:
        first = meta_ref[3:4, 0:1] == 0
        outs[0][...] = own_rows(share, first)
        outs[1][...] = own_rows(share, jnp.logical_not(first)).astype(BF16)
    else:
        outs[0][...] = share.astype(BF16)


def call(body, outs, in_specs, scratch=(), limit=16, flops=0, moved=0):
    return pl.pallas_call(
        body,
        out_shape=outs,
        in_specs=in_specs,
        out_specs=[VMEM if isinstance(o, jax.ShapeDtypeStruct) else HBM for o in outs],
        scratch_shapes=list(scratch),
        compiler_params=pltpu.CompilerParams(vmem_limit_bytes=limit << 20),
        cost_estimate=pl.CostEstimate(
            flops=flops, bytes_accessed=moved, transcendentals=0
        ),
    )


def swap(values):
    return lax.ppermute(values, "tensor", [(0, 1), (1, 0)])


def on_device(
    hidden,
    attn_gain,
    w_query,
    w_keyvalue,
    w_output,
    cache,
    page_table,
    ctx_len,
    move_dest,
    ffn_gain,
    router,
    routes,
    w_in,
    w_down,
):
    replicas = lax.axis_size("replica")
    tp = lax.axis_size("tensor")
    rank = lax.axis_index("tensor").astype(jnp.int32)
    rows, width = hidden.shape
    pool, page_len, kv_local, _ = cache.shape
    outgoing = move_dest.shape[0]
    local_pages = pool - outgoing
    requests = page_table.shape[0]
    heads = w_query.shape[1] // HEAD_DIM
    inbox = replicas * CAP
    units = w_down.shape[0]
    assert FF % units == 0
    columns = page_len * kv_local
    entries = -(-(pool + inbox) // LANES) * LANES
    struct = jax.ShapeDtypeStruct
    pair = tp == 2
    ids = rank.reshape(1)

    def pin(values):
        return pltpu.with_memory_space_constraint(values, pltpu.HBM)

    def exchange(blocks, order):
        blocks = blocks.reshape(replicas, CAP * SLOT, LANES)
        blocks = lax.all_to_all(
            blocks,
            "replica",
            split_axis=0,
            concat_axis=0,
            tiled=True,
            axis_index_groups=[list(order)],
        )
        return blocks.reshape(inbox * SLOT, LANES)

    blocks = pin(cache.reshape(pool, columns, LANES))
    if pair:
        pieces = [hidden, swap(hidden)]
    else:
        pieces = [lax.all_gather(hidden, "tensor", axis=0, tiled=True)]
    meta_shape = (4, entries)
    tables_shape = (2, requests, LANES)
    own, wq, gain, tables, away, away_span, meta, lent, pick, drop = call(
        functools.partial(prepare_kernel, pool, replicas),
        [
            struct(hidden.shape, BF16),
            struct(w_query.shape, BF16),
            struct((1, width), F32),
            struct(tables_shape, F32),
            struct((inbox, requests), BF16),
            struct((inbox, LANES), F32),
            struct(meta_shape, jnp.int32),
            struct((outgoing, columns, LANES), BF16),
            struct((outgoing * SLOT, LANES), jnp.int32),
            struct((outgoing, outgoing * SLOT), jnp.int32),
        ],
        [SMEM] + [HBM] * 7,
        [
            pltpu.VMEM((1, requests), jnp.int32),
            pltpu.VMEM((page_table.shape[1], requests), jnp.int32),
            pltpu.VMEM((1, outgoing), jnp.int32),
            pltpu.VMEM((width,), F32),
            pltpu.SemaphoreType.DMA((10,)),
        ],
        moved=2 * w_query.size,
    )(
        ids,
        pin(hidden),
        pin(ctx_len.reshape(1, requests)),
        pin(page_table.T),
        pin(move_dest.reshape(1, outgoing)),
        pin(attn_gain),
        pin(w_query),
        blocks,
    )
    if pair:
        pieces[0] = own
    hidden_all, normed, packed, sends = call(
        functools.partial(query_kernel, len(pieces)),
        [
            struct((requests, width), BF16),
            struct((requests, width), BF16),
            struct((requests * SLOT, LANES), F32),
            struct((inbox * SLOT, LANES), BF16),
        ],
        [VMEM] * (len(pieces) + 6),
        [
            pltpu.VMEM((requests * SLOT, LANES), F32),
            pltpu.VMEM((inbox * SLOT, LANES), F32),
        ],
        flops=4 * requests * width * w_query.shape[1],
        moved=2 * w_query.size,
    )(meta, *pieces, gain, wq, tables, away, away_span)
    asked = exchange(sends, range(replicas)[::-1])
    replies, meta_far, packed_far, normed_far, tables_far, hidden_far = call(
        functools.partial(lent_kernel, heads, kv_local),
        [
            pltpu.HBM((inbox * SLOT, LANES), BF16),
            pltpu.HBM(meta_shape, jnp.int32),
            pltpu.HBM((requests * SLOT, LANES), F32),
            pltpu.HBM((requests, width), BF16),
            pltpu.HBM(tables_shape, F32),
            pltpu.HBM((requests, width), BF16),
        ],
        [VMEM] * 9,
        [
            pltpu.VMEM((inbox * SLOT, LANES), BF16),
            pltpu.SemaphoreType.DMA((6,)),
        ],
        flops=4 * ROWS * columns * LANES * outgoing,
        moved=2 * columns * LANES * outgoing,
    )(asked, lent, pick, drop, meta, packed, normed, tables, hidden_all)
    returned = exchange(replies, [r ^ replicas // 2 for r in range(replicas)])
    (state,) = call(
        functools.partial(local_kernel, heads, kv_local),
        [pltpu.HBM((requests, ROWS, LANES), F32)],
        [HBM] * 6,
        [
            pltpu.SMEM(meta_shape, jnp.int32),
            pltpu.VMEM((requests * SLOT, LANES), F32),
            pltpu.VMEM((requests, width), BF16),
            pltpu.VMEM((width * kv_local, LANES), BF16),
            pltpu.VMEM(tables_shape, F32),
            pltpu.VMEM((local_pages, columns, LANES), BF16),
            pltpu.VMEM((requests, ROWS, LANES), F32),
            pltpu.VMEM((requests * ROWS, LANES), F32),
            pltpu.VMEM((local_pages, ROWS, LANES), F32),
            pltpu.VMEM((local_pages, ROWS, LANES), F32),
            pltpu.VMEM((requests + 1, ROWS, LANES), F32),
            pltpu.VMEM((requests + 1, ROWS, LANES), F32),
            pltpu.VMEM((local_pages, ROWS, LANES), F32),
            pltpu.SemaphoreType.DMA((6 + local_pages,)),
        ],
        limit=24,
        flops=4 * ROWS * columns * LANES * local_pages,
        moved=2 * columns * LANES * local_pages,
    )(
        pin(meta_far),
        pin(packed_far),
        pin(normed_far),
        pin(w_keyvalue.reshape(width * kv_local, LANES)),
        pin(tables_far),
        blocks,
    )
    half = struct((units // 2, width), BF16)
    part, meta, hidden_all, gain, router_t, routes_t, wd = call(
        functools.partial(combine_kernel, heads, pool),
        [
            struct((requests, width), BF16),
            struct(meta_shape, jnp.int32),
            struct((requests, width), BF16),
            struct((1, width), F32),
            struct(router.shape[::-1], BF16),
            struct(routes.shape[::-1], jnp.int32),
            half,
        ],
        [HBM] * 8 + [VMEM],
        [
            pltpu.SMEM(meta_shape, jnp.int32),
            pltpu.VMEM((requests, ROWS, LANES), F32),
            pltpu.VMEM(w_output.shape, BF16),
            pltpu.VMEM((width,), F32),
            pltpu.VMEM((requests + 1, ROWS, LANES), F32),
            pltpu.VMEM((requests + 1, ROWS, LANES), F32),
            pltpu.VMEM((inbox, ROWS, LANES), F32),
            pltpu.VMEM((inbox * SLOT, LANES), F32),
            pltpu.VMEM((requests * ROWS, LANES), F32),
            pltpu.SemaphoreType.DMA((12,)),
        ],
        flops=2 * requests * w_output.size,
        moved=2 * w_output.size,
    )(
        pin(meta_far), pin(state), pin(w_output), pin(hidden_far), pin(ffn_gain),
        pin(router.T), pin(routes.T), pin(w_down), returned,
    )
    if pair:
        parts = [part, swap(part)]
    else:
        parts = [lax.all_gather(part, "tensor", axis=0, tiled=True)]
    (wd_rest,) = call(
        load_kernel,
        [half],
        [HBM, ANY],
        [pltpu.SemaphoreType.DMA],
        moved=w_down.size,
    )(pin(w_down), part)
    attended, ffn_input, ffn_again = call(
        functools.partial(residual_kernel, tp, len(parts)),
        [
            struct((rows if pair else requests, width), BF16),
            struct((requests, width), BF16),
            struct((requests, width), BF16),
        ],
        [VMEM] * (len(parts) + 3),
        flops=2 * requests * width,
        moved=8 * requests * width,
    )(meta, hidden_all, *parts, gain)
    lifted = jnp.einsum("rd,dsu->sru", ffn_input, w_in, preferred_element_type=F32)
    shapes = [struct((requests, width), BF16)]
    if pair:
        shapes = [struct((rows, width), F32), struct((rows, width), BF16)]
    shares = call(
        functools.partial(expert_kernel, units),
        shapes,
        [VMEM] * 7,
        flops=2 * requests * w_down.size,
        moved=2 * w_down.size,
    )(meta, lifted, ffn_again, router_t, routes_t, wd, wd_rest)
    if pair:
        out = struct((rows, width), BF16)
        return tuple(
            call(finish_kernel, [out, out], [VMEM] * 3)(attended, shares[0], swap(shares[1]))
        )
    shares = lax.all_gather(shares[0], "tensor", axis=0)
    mine = lax.dynamic_slice_in_dim(shares, rank * rows, rows, axis=1)
    experts_out = jnp.sum(mine.astype(F32), axis=0).astype(BF16)
    attended = lax.dynamic_slice_in_dim(attended, rank * rows, rows, axis=0)
    return attended, experts_out


def solution(mesh):
    placed = (
        P(("replica", "tensor"), None),
        P(),
        P(None, "tensor"),
        P(None, "tensor", None),
        P("tensor", None),
        P("replica", None, "tensor", None),
        P("replica", None),
        P("replica"),
        P("replica"),
        P(),
        P(),
        P("replica", None),
        P(None, None, "tensor"),
        P("tensor", None),
    )
    return jax.shard_map(
        on_device,
        mesh=mesh,
        in_specs=placed,
        out_specs=(P(("replica", "tensor"), None), P(("replica", "tensor"), None)),
        check_vma=False,
    )
```

```python
import functools
import math

import jax
import jax.numpy as jnp
from jax import lax
from jax.experimental import pallas as pl
from jax.experimental.pallas import tpu as pltpu
from jax.sharding import PartitionSpec as P

HEAD_DIM = 64
EXPERTS = 40
FF = 512
CAP = 2
LANES = 128
SLOT = 8
ROWS = 16
META = 6

ATTN_SCALE = 0.015625
RESID_SCALE = 0.22
ROPE_BASE = 10000.0
EPSILON = 1e-06
NEG_FILL = -1e30

F32 = jnp.float32
BF16 = jnp.bfloat16
VMEM = pl.BlockSpec(memory_space=pltpu.VMEM)
SMEM = pl.BlockSpec(memory_space=pltpu.SMEM)
ANY = pl.BlockSpec(memory_space=pl.ANY)
HBM = pl.BlockSpec(memory_space=pltpu.HBM)
NT = (((1,), (1,)), ((), ()))


def iota(shape, axis):
    return lax.broadcasted_iota(jnp.int32, shape, axis)


def norm_rows(values, gain):
    factor = lax.rsqrt(jnp.mean(values * values, axis=-1, keepdims=True) + EPSILON)
    return (values * factor * gain).astype(BF16)


def rope_tables(ctx_row, requests):
    diagonal = iota((requests, requests), 0) == iota((requests, requests), 1)
    ctx = jnp.broadcast_to(ctx_row.astype(F32), (requests, requests))
    ctx = jnp.sum(jnp.where(diagonal, ctx, 0.0), axis=1, keepdims=True)
    lane = iota((requests, LANES), 1)
    index = (lane % (HEAD_DIM // 2)).astype(F32)
    inverse = jnp.exp(index * (-2.0 * math.log(ROPE_BASE) / HEAD_DIM))
    angles = ctx * inverse
    sign = jnp.where(lane % HEAD_DIM < HEAD_DIM // 2, -1.0, 1.0)
    return jnp.cos(angles), jnp.sin(angles) * sign


def rotate(chunk, cosine, sine):
    lane = iota(chunk.shape, 1)
    ahead = pltpu.roll(chunk, LANES - HEAD_DIM // 2, 1)
    behind = pltpu.roll(chunk, HEAD_DIM // 2, 1)
    turned = jnp.where(lane % HEAD_DIM < HEAD_DIM // 2, ahead, behind)
    return chunk * cosine + turned * sine


def copy_of(source, target, sem):
    return pltpu.make_async_copy(source, target, sem)


def copies_of(source, target, sems, base):
    step = source.shape[0] // 4
    return [
        copy_of(
            source.at[pl.ds(i * step, step)], target.at[pl.ds(i * step, step)], sems.at[base + i]
        )
        for i in range(4)
    ]


def page_copies(cache_hbm, pages, stages, sems, base):
    copies = []
    for i, stage in enumerate(stages):
        rows = pl.ds(stage[0], len(stage))
        copies.append(copy_of(cache_hbm.at[rows], pages.at[rows], sems.at[base + i]))
    return copies


def page_stages(count, first, rest):
    starts = [0] + list(range(min(first, count), count, rest))
    return [range(a, b) for a, b in zip(starts, starts[1:] + [count])]


def prepare_kernel(
    pool, replicas, ids_ref, hidden_hbm, ctx_hbm, table_hbm, dest_hbm, attn_gain_hbm,
    wq_hbm, cache_hbm,
    hidden_ref, wq_ref, gain_ref, tables_ref, away_ref, span_ref, meta_ref, lent_ref,
    pick_ref, drop_ref,
    ctx, table, dest, gain, sems,
):
    inbox = replicas * CAP
    requests = ctx.shape[1]
    entries = meta_ref.shape[1]
    small = [
        copy_of(ctx_hbm, ctx, sems.at[0]),
        copy_of(table_hbm, table, sems.at[1]),
        copy_of(dest_hbm, dest, sems.at[2]),
        copy_of(attn_gain_hbm, gain, sems.at[3]),
    ]
    large = [copy_of(hidden_hbm, hidden_ref, sems.at[4])]
    large += copies_of(wq_hbm, wq_ref, sems, 5)
    lending = pl.ds(pool - lent_ref.shape[0], lent_ref.shape[0])
    large.append(copy_of(cache_hbm.at[lending], lent_ref, sems.at[9]))
    for copy in small + large:
        copy.start()
    for copy in small:
        copy.wait()
    gain_ref[...] = gain[...].reshape(1, gain.shape[0])
    ctx_row = ctx[...]

    def claims(values):
        held = jnp.zeros(values.shape, F32)
        spans = jnp.zeros(values.shape, F32)
        for k in range(table.shape[0]):
            match = table[k : k + 1, :] == values
            filled = jnp.clip(ctx_row - k * 128, 0, 128).astype(F32)
            held = jnp.where(match, 1.0, held)
            spans = jnp.where(match, filled, spans)
        return held.astype(BF16), spans

    held, spans = claims(iota((entries, requests), 0))
    numbers = (iota((SLOT, requests), 1) + 1).astype(BF16)
    ones = jnp.ones((SLOT, requests), BF16)
    holder = lax.dot_general(numbers, held, NT, preferred_element_type=F32)
    covered = lax.dot_general(ones, spans.astype(BF16), NT, preferred_element_type=F32)
    meta_ref[0:1, :] = holder[0:1, :].astype(jnp.int32) - 1
    meta_ref[1:2, :] = covered[0:1, :].astype(jnp.int32)
    meta_ref[2:3, :] = jnp.zeros((1, entries), jnp.int32)
    lent = dest.shape[1]
    across = jnp.broadcast_to(dest[...].astype(F32), (lent, lent))
    row, lane = iota((lent, lent), 0), iota((lent, lent), 1)
    down = jnp.sum(jnp.where(row == lane, across, 0.0), axis=1, keepdims=True)
    same = across == down
    before = jnp.sum(jnp.where(same & (lane < row), 1.0, 0.0), axis=1, keepdims=True)
    column = (replicas - 1 - down) * CAP + before
    column = jnp.broadcast_to(column, (lent, LANES)).astype(BF16)
    before = jnp.sum(jnp.where(same & (row < lane), 1.0, 0.0), axis=0, keepdims=True)
    line = dest[...] ^ replicas // 2
    line = jnp.broadcast_to(line.astype(F32), (lent, lent))
    line = (line * CAP + before).astype(BF16)
    expand = iota((lent * SLOT, lent), 0) // SLOT == iota((lent * SLOT, lent), 1)
    expand = jnp.where(expand, 1.0, 0.0).astype(BF16)
    column = jnp.dot(expand, column, preferred_element_type=F32).astype(jnp.int32)
    pick_ref[...] = column * SLOT + iota(column.shape, 0) % SLOT
    line = lax.dot_general(line, expand, NT, preferred_element_type=F32).astype(jnp.int32)
    drop_ref[...] = line * SLOT + iota(line.shape, 1) % SLOT
    meta_ref[3:4, :] = jnp.full((1, entries), ids_ref[0], jnp.int32)
    cosine, sine = rope_tables(ctx_row, requests)
    tables_ref[0] = cosine
    tables_ref[1] = sine
    slot = iota((inbox, requests), 0)
    lender = replicas - 1 - slot // CAP
    held, spans = claims(pool + lender * CAP + slot % CAP)
    away_ref[...] = held
    away_span = jnp.sum(spans, axis=1, keepdims=True)
    span_ref[...] = jnp.broadcast_to(away_span, span_ref.shape)
    for copy in large:
        copy.wait()


def query_kernel(
    count, meta_ref, *refs,
):
    pieces = refs[:count]
    (gain_ref, wq_ref, tables_ref, away_ref, span_ref,
     hidden_ref, normed_ref, packed_ref, send_ref, packs, sends) = refs[count:]
    requests = hidden_ref.shape[0]
    inbox = span_ref.shape[0]
    width = wq_ref.shape[1]
    chunks = -(-width // LANES)
    if count == 1:
        hidden = pieces[0][...]
    else:
        own, other = pieces[0][...], pieces[1][...]
        first = meta_ref[3:4, 0:1] == 0
        hidden = jnp.concatenate(
            [jnp.where(first, own, other), jnp.where(first, other, own)], axis=0
        )
    hidden_ref[...] = hidden
    normed = norm_rows(hidden.astype(F32), gain_ref[...])
    normed_ref[...] = normed
    queries = jnp.dot(normed, wq_ref[...], preferred_element_type=F32)
    if chunks * LANES > width:
        pad = jnp.zeros((requests, chunks * LANES - width), F32)
        queries = jnp.concatenate([queries, pad], axis=1)
    cosine, sine = tables_ref[0], tables_ref[1]
    zeros = jnp.zeros((requests, LANES), F32)
    nothing = jnp.zeros((inbox, LANES), F32)
    for j in range(SLOT):
        here = pl.ds(j, requests, stride=SLOT)
        there = pl.ds(j, inbox, stride=SLOT)
        if j < chunks:
            chunk = rotate(queries[:, j * LANES : (j + 1) * LANES], cosine, sine)
            chunk = (chunk.astype(BF16).astype(F32) * ATTN_SCALE).astype(BF16)
            packs[here, :] = chunk.astype(F32)
            sends[there, :] = jnp.dot(away_ref[...], chunk, preferred_element_type=F32)
        else:
            packs[here, :] = zeros
            sends[there, :] = span_ref[...] if j == META else nothing
    packed_ref[...] = packs[...]
    send_ref[...] = sends[...].astype(BF16)


def unpack(packed):
    low = iota(packed.shape, 1) < HEAD_DIM
    even = jnp.where(low, packed, 0.0)
    odd = jnp.where(low, pltpu.roll(packed, HEAD_DIM, 1), 0.0)
    return jnp.concatenate([even, odd], axis=0)


def head_rows(heads):
    return [(h // 2) + SLOT * (h % 2) for h in range(heads)]


def token_of_column(heads, kv_local, columns):
    row = iota((ROWS, columns), 0)
    column = iota((ROWS, columns), 1)
    wanted = jnp.full((ROWS, columns), kv_local, jnp.int32)
    for h, place in enumerate(head_rows(heads)):
        wanted = jnp.where(row == place, h // (heads // kv_local), wanted)
    return jnp.where(column % kv_local == wanted, column // kv_local, 1 << 20)


def score_page(query, block):
    return lax.dot_general(query, block, NT, preferred_element_type=F32)


def weigh_page(scores, tokens, span):
    scores = jnp.where(tokens < span, scores, NEG_FILL)
    top = jnp.max(scores, axis=1, keepdims=True)
    weights = jnp.exp(scores - top)
    return top, jnp.sum(weights, axis=1, keepdims=True), weights.astype(BF16)


def attend_pages(
    stages, copies, query_of, block_of, span_of, tokens, keep, last=None
):
    def score_stage(i):
        if copies is not None:
            copies[i].wait()
        if last is not None and i == len(stages) - 1:
            last.wait()
        return {p: score_page(query_of(p), block_of(p)) for p in stages[i]}

    scores = score_stage(0)
    for i, pages in enumerate(stages):
        if i + 1 < len(stages):
            ahead = score_stage(i + 1)
        weighed = {p: weigh_page(scores[p], tokens, span_of(p)) for p in pages}
        outs = {
            p: jnp.dot(weighed[p][2], block_of(p), preferred_element_type=F32)
            for p in pages
        }
        for p in pages:
            keep(p, weighed[p][0], weighed[p][1], outs[p])
        if i + 1 < len(stages):
            scores = ahead


def spread_queries(target, packed):
    low = iota(packed.shape, 2) < HEAD_DIM
    target[:, 0:SLOT, :] = jnp.where(low, packed, 0.0)
    target[:, SLOT:ROWS, :] = jnp.where(low, pltpu.roll(packed, HEAD_DIM, 2), 0.0)


def merge_pages(places, top_of, sum_of, top, acc, scaled, start, before):
    requests = start.shape[0]
    for p, place in enumerate(places):
        top[place] = jnp.maximum(top[place], top_of(p))
    acc[0:requests] = start * jnp.exp(before - top[0:requests])
    for p, place in enumerate(places):
        scaled[p] = sum_of(p) * jnp.exp(top_of(p) - top[place])
    for p, place in enumerate(places):
        acc[place] = acc[place] + scaled[p]


def project_heads(values, weights_ref, heads):
    if heads == 1:
        return jnp.dot(values, weights_ref[...], preferred_element_type=F32)
    rows, depth = values.shape
    wide = 1024
    part = wide // heads
    repeat = iota((part, wide), 1) // heads == iota((part, wide), 0)
    repeat = jnp.where(repeat, 1.0, 0.0).astype(BF16)
    parts = [values[:, i : i + part] for i in range(0, depth, part)]
    spread = jnp.dot(
        jnp.concatenate(parts, axis=0), repeat, preferred_element_type=F32
    ).astype(BF16)
    lane = iota((1, wide), 1) % heads
    masks = [jnp.where(lane == k, 1.0, 0.0).astype(BF16) for k in range(heads)]
    total = jnp.zeros((heads * rows, LANES), F32)
    for i in range(len(parts)):
        piece = spread[i * rows : (i + 1) * rows]
        piece = jnp.concatenate([piece * mask for mask in masks], axis=0)
        total += jnp.dot(
            piece, weights_ref[i * wide : (i + 1) * wide, :], preferred_element_type=F32
        )
    return total


def local_kernel(
    heads, kv_local, meta_hbm, packed_hbm, normed_hbm, wkv_hbm, tables_hbm, cache_hbm,
    state_hbm,
    meta, packed, normed, raw, tables, pages, queries, fresh, tops, sums, top, acc,
    scaled, sems,
):
    requests = normed.shape[0]
    count, columns, _ = pages.shape
    small = [
        copy_of(meta_hbm, meta, sems.at[0]),
        copy_of(packed_hbm, packed, sems.at[1]),
        copy_of(normed_hbm, normed, sems.at[2]),
        copy_of(tables_hbm, tables, sems.at[3]),
    ]
    weights = copy_of(wkv_hbm, raw, sems.at[4])
    stages = page_stages(count, 4, 12)
    paging = page_copies(cache_hbm, pages, stages, sems, 10)
    for copy in small + paging + [weights]:
        copy.start()
    tokens = token_of_column(heads, kv_local, columns)
    lower = iota((ROWS, LANES), 1) < HEAD_DIM
    low = iota((requests, LANES), 1) < HEAD_DIM
    low16 = iota((requests, ROWS, LANES), 2) < HEAD_DIM
    top[...] = jnp.full(top.shape, NEG_FILL, F32)
    acc[...] = jnp.zeros(acc.shape, F32)
    for copy in small:
        copy.wait()
    spread_queries(queries, packed[...].reshape(requests, SLOT, LANES))

    def place_of(p):
        owner = meta[0, p]
        return jnp.where(owner < 0, requests, owner)

    places = [place_of(p) for p in range(count)]

    def keep(p, page_top, total, out):
        tops[p] = jnp.broadcast_to(page_top, (ROWS, LANES))
        sums[p] = jnp.where(lower, total, out)
        top[places[p]] = jnp.maximum(top[places[p]], tops[p])

    attend_pages(
        stages,
        paging,
        lambda p: queries[jnp.maximum(meta[0, p], 0)].astype(BF16),
        lambda p: pages[p],
        lambda p: meta[1, p],
        tokens,
        keep,
        weights,
    )
    cosine = jnp.where(low, tables[0], 1.0)
    sine = jnp.where(low, tables[1], 0.0)
    projected = project_heads(normed[...], raw, kv_local)
    new = [
        rotate(projected[k * requests : (k + 1) * requests], cosine, sine)
        .astype(BF16)
        .astype(F32)
        for k in range(kv_local)
    ]
    used = {place: h for h, place in enumerate(head_rows(heads))}
    for place in range(ROWS):
        value = jnp.zeros((requests, LANES), F32)
        if place in used:
            value = new[used[place] // (heads // kv_local)]
        fresh[pl.ds(place, requests, stride=ROWS), :] = value
    for p, place in enumerate(places):
        scaled[p] = sums[p] * jnp.exp(tops[p] - top[place])
    for p, place in enumerate(places):
        acc[place] = acc[place] + scaled[p]
    added = fresh[...].reshape(requests, ROWS, LANES)
    score = jnp.sum(queries[...] * added, axis=2, keepdims=True)
    score = jnp.broadcast_to(score, added.shape)
    parked = []
    step = requests // 4
    for i in range(4):
        rows = slice(i * step, (i + 1) * step)
        before, fresh_score = top[rows], score[rows]
        highest = jnp.maximum(before, fresh_score)
        whole = acc[rows] * jnp.exp(before - highest)
        whole += jnp.where(low16[rows], 1.0, added[rows]) * jnp.exp(fresh_score - highest)
        acc[rows] = jnp.where(
            low16[rows], highest + jnp.log(whole), whole / pltpu.roll(whole, HEAD_DIM, 2)
        )
        part = pl.ds(i * step, step)
        parked.append(copy_of(acc.at[part], state_hbm.at[part], sems.at[5 + i]))
        parked[i].start()
    for copy in parked:
        copy.wait()


def lent_kernel(
    heads, kv_local, asked_ref, pages, pick_ref, drop_ref, meta_ref, packed_ref,
    normed_ref, tables_ref, hidden_ref,
    reply_hbm, meta_hbm, packed_hbm, normed_hbm, tables_hbm, hidden_hbm,
    reply16, sems,
):
    outgoing, columns, _ = pages.shape
    parked = [
        copy_of(packed_ref, packed_hbm, sems.at[0]),
        copy_of(normed_ref, normed_hbm, sems.at[1]),
        copy_of(hidden_ref, hidden_hbm, sems.at[2]),
        copy_of(tables_ref, tables_hbm, sems.at[3]),
        copy_of(meta_ref, meta_hbm, sems.at[4]),
    ]
    for copy in parked:
        copy.start()
    slot_rows = asked_ref.shape[0]
    shape = (outgoing * SLOT, slot_rows)
    chosen = jnp.where(pick_ref[:, 0:1] == iota(shape, 1), 1.0, 0.0).astype(BF16)
    asked = jnp.dot(chosen, asked_ref[...], preferred_element_type=F32)
    tokens = token_of_column(heads, kv_local, columns).astype(F32)
    low = iota((SLOT, LANES), 1) < HEAD_DIM
    lane = iota((SLOT, LANES), 1)
    row = iota((SLOT, LANES), 0)

    def terms(total, offset):
        leading = total.astype(BF16).astype(F32)
        rest = total - leading
        second = rest.astype(BF16).astype(F32)
        third = rest - second
        spot = lane - offset - 3 * row
        placed = jnp.where(spot == 0, leading, 0.0)
        placed = jnp.where(spot == 1, second, placed)
        return jnp.where(spot == 2, third, placed)

    packed = [asked[j * SLOT : (j + 1) * SLOT] for j in range(outgoing)]
    replies = {}

    def keep(j, top, total, out):
        out = out / total
        logs = top + jnp.log(total)
        even = pltpu.roll(out[0:SLOT], HEAD_DIM, 1)
        both = jnp.where(low, even, out[SLOT:ROWS])
        line = jnp.sum(
            terms(logs[0:SLOT], 0) + terms(logs[SLOT:ROWS], HEAD_DIM), axis=0, keepdims=True
        )
        replies[j] = jnp.where(row == META, line, both)

    attend_pages(
        page_stages(outgoing, 8, 8),
        None,
        lambda j: unpack(packed[j]).astype(BF16),
        lambda j: pages[j],
        lambda j: packed[j][META : META + 1, 0:1],
        tokens,
        keep,
    )
    shape = (slot_rows, outgoing * SLOT)
    placed = jnp.where(drop_ref[0:1, :] == iota(shape, 0), 1.0, 0.0).astype(BF16)
    every = jnp.concatenate([replies[j] for j in range(outgoing)], axis=0).astype(BF16)
    reply = jnp.dot(placed, every, preferred_element_type=F32)
    reply16[...] = reply.astype(BF16)
    replying = copy_of(reply16, reply_hbm, sems.at[5])
    replying.start()
    for copy in parked + [replying]:
        copy.wait()


def combine_kernel(
    heads, pool, meta_hbm, state_hbm, wo_hbm, hidden_hbm, gain_hbm, router_hbm,
    routes_hbm, wd_hbm, reply_ref,
    part_ref, meta_ref, hidden_ref, gain_ref, router_ref, routes_ref, wd_ref,
    meta, state, wo, gain, tops, accs, scaled, reply, finals, sems,
):
    requests = state.shape[0]
    inbox = reply_ref.shape[0] // SLOT
    chunks = -(-heads // 2)
    numbers = copy_of(meta_hbm, meta, sems.at[11])
    arriving = copy_of(state_hbm, state, sems.at[0])
    weights = copies_of(wo_hbm, wo, sems, 1)
    gaining = copy_of(gain_hbm, gain, sems.at[5])
    later = [
        copy_of(meta_hbm, meta_ref, sems.at[6]),
        copy_of(hidden_hbm, hidden_ref, sems.at[7]),
        copy_of(router_hbm, router_ref, sems.at[8]),
        copy_of(routes_hbm, routes_ref, sems.at[9]),
        copy_of(wd_hbm.at[pl.ds(0, wd_ref.shape[0])], wd_ref, sems.at[10]),
    ]
    for copy in [numbers, arriving] + weights + [gaining] + later:
        copy.start()
    reply[...] = reply_ref[...].astype(F32)
    tops[...] = jnp.full(tops.shape, NEG_FILL, F32)
    accs[...] = jnp.zeros(accs.shape, F32)
    low = iota((SLOT, LANES), 1) < HEAD_DIM
    lane = iota((SLOT, LANES), 1)
    row = iota((SLOT, LANES), 0)
    mine = (lane % HEAD_DIM) // 3 == row

    def place_of(s):
        lender = s // CAP ^ (inbox // CAP // 2)
        owner = meta[0, pool + lender * CAP + s % CAP]
        return jnp.where(owner < 0, requests, owner)

    def logs_of(s):
        line = reply[s * SLOT + META : s * SLOT + META + 1, :]
        line = jnp.where(mine, jnp.broadcast_to(line, (SLOT, LANES)), 0.0)
        even = jnp.sum(jnp.where(low, line, 0.0), axis=1, keepdims=True)
        odd = jnp.sum(jnp.where(low, 0.0, line), axis=1, keepdims=True)
        logs = jnp.concatenate([even, odd], axis=0)
        return jnp.broadcast_to(logs, (ROWS, LANES))

    def sum_of(s):
        packed = reply[s * SLOT : (s + 1) * SLOT, :]
        even = jnp.where(low, 1.0, pltpu.roll(packed, HEAD_DIM, 1))
        odd = jnp.where(low, 1.0, packed)
        return jnp.concatenate([even, odd], axis=0)

    logs = [logs_of(s) for s in range(inbox)]
    numbers.wait()
    places = [place_of(s) for s in range(inbox)]
    for s, place in enumerate(places):
        tops[place] = jnp.maximum(tops[place], logs[s])
    for s, place in enumerate(places):
        scaled[s] = sum_of(s) * jnp.exp(logs[s] - tops[place])
    for s, place in enumerate(places):
        accs[place] = accs[place] + scaled[s]
    arriving.wait()
    low16 = iota(state.shape, 2) < HEAD_DIM
    start = state[...]
    before = jnp.where(low16, start, pltpu.roll(start, HEAD_DIM, 2))
    remote = tops[0:requests]
    highest = jnp.maximum(before, remote)
    whole = accs[0:requests] * jnp.exp(remote - highest)
    whole = whole + jnp.where(low16, 1.0, start) * jnp.exp(before - highest)
    finals[...] = (whole / pltpu.roll(whole, HEAD_DIM, 2)).reshape(
        requests * ROWS, LANES
    )
    wide = iota((requests, LANES), 1) < HEAD_DIM
    parts = []
    for j in range(chunks):
        even = finals[pl.ds(j, requests, stride=ROWS), :]
        odd = finals[pl.ds(SLOT + j, requests, stride=ROWS), :]
        parts.append(jnp.where(wide, pltpu.roll(even, HEAD_DIM, 1), odd).astype(BF16))
    attention = jnp.concatenate(parts, axis=1)[:, : heads * HEAD_DIM]
    for copy in weights:
        copy.wait()
    part_ref[...] = jnp.dot(attention, wo[...], preferred_element_type=F32).astype(BF16)
    gaining.wait()
    gain_ref[...] = gain[...].reshape(1, gain.shape[0])
    for copy in later:
        copy.wait()


def load_kernel(wd_hbm, order_hbm, wd_ref, sem):
    del order_hbm
    rows = wd_ref.shape[0]
    copy = copy_of(wd_hbm.at[pl.ds(wd_hbm.shape[0] - rows, rows)], wd_ref, sem)
    copy.start()
    copy.wait()


def finish_kernel(attended_ref, own_ref, other_ref, attended_out, experts_out):
    attended_out[...] = attended_ref[...]
    experts_out[...] = (own_ref[...] + other_ref[...].astype(F32)).astype(BF16)


def own_rows(values, first):
    half = values.shape[0] // 2
    return jnp.where(first, values[:half], values[half:])


def residual_kernel(
    tp, count, meta_ref, hidden_ref, *refs,
):
    pieces = refs[:count]
    gain_ref, attended_ref, input_ref, again_ref = refs[count:]
    requests = hidden_ref.shape[0]
    if count == 2:
        summed = pieces[0][...].astype(F32) + pieces[1][...].astype(F32)
    else:
        summed = pieces[0][0:requests, :].astype(F32)
        for t in range(1, tp):
            part = pieces[0][t * requests : (t + 1) * requests, :]
            summed = summed + part.astype(F32)
    attended = (hidden_ref[...].astype(F32) + RESID_SCALE * summed).astype(BF16)
    if count == 2:
        attended_ref[...] = own_rows(attended, meta_ref[3:4, 0:1] == 0)
    else:
        attended_ref[...] = attended
    ffn_input = norm_rows(attended.astype(F32), gain_ref[...])
    input_ref[...] = ffn_input
    again_ref[...] = ffn_input


def gate_column(units, meta_ref, input_ref, router_ref, routes_ref):
    ffn_input = input_ref[...]
    requests = ffn_input.shape[0]
    logits = lax.dot_general(router_ref[...], ffn_input, NT, preferred_element_type=F32)
    expert = iota(logits.shape, 0)
    named = jnp.zeros(logits.shape, F32)
    for k in range(routes_ref.shape[0]):
        named = jnp.where(routes_ref[k : k + 1, :] == expert, 1.0, named)
    chosen = named > 0.5
    top = jnp.max(jnp.where(chosen, logits, NEG_FILL), axis=0, keepdims=True)
    weights = jnp.where(chosen, jnp.exp(logits - top), 0.0)
    total = jnp.sum(weights, axis=0, keepdims=True)
    mine = expert == meta_ref[3:4, 0:1] * units // FF
    line = jnp.sum(jnp.where(mine, weights, 0.0), axis=0, keepdims=True) / total
    diagonal = iota((requests, requests), 0) == iota((requests, requests), 1)
    line = jnp.where(diagonal, jnp.broadcast_to(line, (requests, requests)), 0.0)
    return jnp.sum(line, axis=1, keepdims=True)


def expert_kernel(
    units, meta_ref, lifted_ref, input_ref, router_ref, routes_ref, wd_ref, wd_rest_ref,
    *outs
):
    column = gate_column(units, meta_ref, input_ref, router_ref, routes_ref)
    gate = lifted_ref[0]
    active = gate / (1.0 + jnp.exp(-gate)) * lifted_ref[1]
    active = active.astype(BF16)
    half = wd_ref.shape[0]
    share = jnp.dot(active[:, :half], wd_ref[...], preferred_element_type=F32)
    share += jnp.dot(active[:, half:], wd_rest_ref[...], preferred_element_type=F32)
    share *= column
    if len(outs) == 2:
        first = meta_ref[3:4, 0:1] == 0
        outs[0][...] = own_rows(share, first)
        outs[1][...] = own_rows(share, jnp.logical_not(first)).astype(BF16)
    else:
        outs[0][...] = share.astype(BF16)


def call(body, outs, in_specs, scratch=(), limit=16, flops=0, moved=0):
    return pl.pallas_call(
        body,
        out_shape=outs,
        in_specs=in_specs,
        out_specs=[VMEM if isinstance(o, jax.ShapeDtypeStruct) else HBM for o in outs],
        scratch_shapes=list(scratch),
        compiler_params=pltpu.CompilerParams(vmem_limit_bytes=limit << 20),
        cost_estimate=pl.CostEstimate(
            flops=flops, bytes_accessed=moved, transcendentals=0
        ),
    )


def swap(values):
    return lax.ppermute(values, "tensor", [(0, 1), (1, 0)])


def on_device(
    hidden,
    attn_gain,
    w_query,
    w_keyvalue,
    w_output,
    cache,
    page_table,
    ctx_len,
    move_dest,
    ffn_gain,
    router,
    routes,
    w_in,
    w_down,
):
    replicas = lax.axis_size("replica")
    tp = lax.axis_size("tensor")
    rank = lax.axis_index("tensor").astype(jnp.int32)
    rows, width = hidden.shape
    pool, page_len, kv_local, _ = cache.shape
    outgoing = move_dest.shape[0]
    local_pages = pool - outgoing
    requests = page_table.shape[0]
    heads = w_query.shape[1] // HEAD_DIM
    inbox = replicas * CAP
    units = w_down.shape[0]
    assert FF % units == 0
    columns = page_len * kv_local
    entries = -(-(pool + inbox) // LANES) * LANES
    struct = jax.ShapeDtypeStruct
    pair = tp == 2
    ids = rank.reshape(1)

    def pin(values):
        return pltpu.with_memory_space_constraint(values, pltpu.HBM)

    def exchange(blocks, order):
        blocks = blocks.reshape(replicas, CAP * SLOT, LANES)
        blocks = lax.all_to_all(
            blocks,
            "replica",
            split_axis=0,
            concat_axis=0,
            tiled=True,
            axis_index_groups=[list(order)],
        )
        return blocks.reshape(inbox * SLOT, LANES)

    blocks = pin(cache.reshape(pool, columns, LANES))
    if pair:
        pieces = [hidden, swap(hidden)]
    else:
        pieces = [lax.all_gather(hidden, "tensor", axis=0, tiled=True)]
    meta_shape = (4, entries)
    tables_shape = (2, requests, LANES)
    own, wq, gain, tables, away, away_span, meta, lent, pick, drop = call(
        functools.partial(prepare_kernel, pool, replicas),
        [
            struct(hidden.shape, BF16),
            struct(w_query.shape, BF16),
            struct((1, width), F32),
            struct(tables_shape, F32),
            struct((inbox, requests), BF16),
            struct((inbox, LANES), F32),
            struct(meta_shape, jnp.int32),
            struct((outgoing, columns, LANES), BF16),
            struct((outgoing * SLOT, LANES), jnp.int32),
            struct((outgoing, outgoing * SLOT), jnp.int32),
        ],
        [SMEM] + [HBM] * 7,
        [
            pltpu.VMEM((1, requests), jnp.int32),
            pltpu.VMEM((page_table.shape[1], requests), jnp.int32),
            pltpu.VMEM((1, outgoing), jnp.int32),
            pltpu.VMEM((width,), F32),
            pltpu.SemaphoreType.DMA((10,)),
        ],
        moved=2 * w_query.size,
    )(
        ids,
        pin(hidden),
        pin(ctx_len.reshape(1, requests)),
        pin(page_table.T),
        pin(move_dest.reshape(1, outgoing)),
        pin(attn_gain),
        pin(w_query),
        blocks,
    )
    if pair:
        pieces[0] = own
    hidden_all, normed, packed, sends = call(
        functools.partial(query_kernel, len(pieces)),
        [
            struct((requests, width), BF16),
            struct((requests, width), BF16),
            struct((requests * SLOT, LANES), F32),
            struct((inbox * SLOT, LANES), BF16),
        ],
        [VMEM] * (len(pieces) + 6),
        [
            pltpu.VMEM((requests * SLOT, LANES), F32),
            pltpu.VMEM((inbox * SLOT, LANES), F32),
        ],
        flops=4 * requests * width * w_query.shape[1],
        moved=2 * w_query.size,
    )(meta, *pieces, gain, wq, tables, away, away_span)
    asked = exchange(sends, range(replicas)[::-1])
    replies, meta_far, packed_far, normed_far, tables_far, hidden_far = call(
        functools.partial(lent_kernel, heads, kv_local),
        [
            pltpu.HBM((inbox * SLOT, LANES), BF16),
            pltpu.HBM(meta_shape, jnp.int32),
            pltpu.HBM((requests * SLOT, LANES), F32),
            pltpu.HBM((requests, width), BF16),
            pltpu.HBM(tables_shape, F32),
            pltpu.HBM((requests, width), BF16),
        ],
        [VMEM] * 9,
        [
            pltpu.VMEM((inbox * SLOT, LANES), BF16),
            pltpu.SemaphoreType.DMA((6,)),
        ],
        flops=4 * ROWS * columns * LANES * outgoing,
        moved=2 * columns * LANES * outgoing,
    )(asked, lent, pick, drop, meta, packed, normed, tables, hidden_all)
    returned = exchange(replies, [r ^ replicas // 2 for r in range(replicas)])
    (state,) = call(
        functools.partial(local_kernel, heads, kv_local),
        [pltpu.HBM((requests, ROWS, LANES), F32)],
        [HBM] * 6,
        [
            pltpu.SMEM(meta_shape, jnp.int32),
            pltpu.VMEM((requests * SLOT, LANES), F32),
            pltpu.VMEM((requests, width), BF16),
            pltpu.VMEM((width * kv_local, LANES), BF16),
            pltpu.VMEM(tables_shape, F32),
            pltpu.VMEM((local_pages, columns, LANES), BF16),
            pltpu.VMEM((requests, ROWS, LANES), F32),
            pltpu.VMEM((requests * ROWS, LANES), F32),
            pltpu.VMEM((local_pages, ROWS, LANES), F32),
            pltpu.VMEM((local_pages, ROWS, LANES), F32),
            pltpu.VMEM((requests + 1, ROWS, LANES), F32),
            pltpu.VMEM((requests + 1, ROWS, LANES), F32),
            pltpu.VMEM((local_pages, ROWS, LANES), F32),
            pltpu.SemaphoreType.DMA((10 + local_pages,)),
        ],
        limit=24,
        flops=4 * ROWS * columns * LANES * local_pages,
        moved=2 * columns * LANES * local_pages,
    )(
        pin(meta_far),
        pin(packed_far),
        pin(normed_far),
        pin(w_keyvalue.reshape(width * kv_local, LANES)),
        pin(tables_far),
        blocks,
    )
    half = struct((units // 2, width), BF16)
    part, meta, hidden_all, gain, router_t, routes_t, wd = call(
        functools.partial(combine_kernel, heads, pool),
        [
            struct((requests, width), BF16),
            struct(meta_shape, jnp.int32),
            struct((requests, width), BF16),
            struct((1, width), F32),
            struct(router.shape[::-1], BF16),
            struct(routes.shape[::-1], jnp.int32),
            half,
        ],
        [HBM] * 8 + [VMEM],
        [
            pltpu.SMEM(meta_shape, jnp.int32),
            pltpu.VMEM((requests, ROWS, LANES), F32),
            pltpu.VMEM(w_output.shape, BF16),
            pltpu.VMEM((width,), F32),
            pltpu.VMEM((requests + 1, ROWS, LANES), F32),
            pltpu.VMEM((requests + 1, ROWS, LANES), F32),
            pltpu.VMEM((inbox, ROWS, LANES), F32),
            pltpu.VMEM((inbox * SLOT, LANES), F32),
            pltpu.VMEM((requests * ROWS, LANES), F32),
            pltpu.SemaphoreType.DMA((12,)),
        ],
        flops=2 * requests * w_output.size,
        moved=2 * w_output.size,
    )(
        pin(meta_far), pin(state), pin(w_output), pin(hidden_far), pin(ffn_gain),
        pin(router.T), pin(routes.T), pin(w_down), returned,
    )
    if pair:
        parts = [part, swap(part)]
    else:
        parts = [lax.all_gather(part, "tensor", axis=0, tiled=True)]
    (wd_rest,) = call(
        load_kernel,
        [half],
        [HBM, ANY],
        [pltpu.SemaphoreType.DMA],
        moved=w_down.size,
    )(pin(w_down), part)
    attended, ffn_input, ffn_again = call(
        functools.partial(residual_kernel, tp, len(parts)),
        [
            struct((rows if pair else requests, width), BF16),
            struct((requests, width), BF16),
            struct((requests, width), BF16),
        ],
        [VMEM] * (len(parts) + 3),
        flops=2 * requests * width,
        moved=8 * requests * width,
    )(meta, hidden_all, *parts, gain)
    lifted = jnp.einsum("rd,dsu->sru", ffn_input, w_in, preferred_element_type=F32)
    shapes = [struct((requests, width), BF16)]
    if pair:
        shapes = [struct((rows, width), F32), struct((rows, width), BF16)]
    shares = call(
        functools.partial(expert_kernel, units),
        shapes,
        [VMEM] * 7,
        flops=2 * requests * w_down.size,
        moved=2 * w_down.size,
    )(meta, lifted, ffn_again, router_t, routes_t, wd, wd_rest)
    if pair:
        out = struct((rows, width), BF16)
        return tuple(
            call(finish_kernel, [out, out], [VMEM] * 3)(attended, shares[0], swap(shares[1]))
        )
    shares = lax.all_gather(shares[0], "tensor", axis=0)
    mine = lax.dynamic_slice_in_dim(shares, rank * rows, rows, axis=1)
    experts_out = jnp.sum(mine.astype(F32), axis=0).astype(BF16)
    attended = lax.dynamic_slice_in_dim(attended, rank * rows, rows, axis=0)
    return attended, experts_out


def solution(mesh):
    placed = (
        P(("replica", "tensor"), None),
        P(),
        P(None, "tensor"),
        P(None, "tensor", None),
        P("tensor", None),
        P("replica", None, "tensor", None),
        P("replica", None),
        P("replica"),
        P("replica"),
        P(),
        P(),
        P("replica", None),
        P(None, None, "tensor"),
        P("tensor", None),
    )
    return jax.shard_map(
        on_device,
        mesh=mesh,
        in_specs=placed,
        out_specs=(P(("replica", "tensor"), None), P(("replica", "tensor"), None)),
        check_vma=False,
    )
```

```python
import functools
import math

import jax
import jax.numpy as jnp
from jax import lax
from jax.experimental import pallas as pl
from jax.experimental.pallas import tpu as pltpu
from jax.sharding import PartitionSpec as P

HEAD_DIM = 64
EXPERTS = 40
FF = 512
CAP = 2
LANES = 128
SLOT = 8
ROWS = 16
META = 6

ATTN_SCALE = 0.015625
RESID_SCALE = 0.22
ROPE_BASE = 10000.0
EPSILON = 1e-06
NEG_FILL = -1e30

F32 = jnp.float32
BF16 = jnp.bfloat16
VMEM = pl.BlockSpec(memory_space=pltpu.VMEM)
SMEM = pl.BlockSpec(memory_space=pltpu.SMEM)
ANY = pl.BlockSpec(memory_space=pl.ANY)
HBM = pl.BlockSpec(memory_space=pltpu.HBM)
NT = (((1,), (1,)), ((), ()))


def iota(shape, axis):
    return lax.broadcasted_iota(jnp.int32, shape, axis)


def norm_rows(values, gain):
    factor = lax.rsqrt(jnp.mean(values * values, axis=-1, keepdims=True) + EPSILON)
    return (values * factor * gain).astype(BF16)


def rope_tables(ctx_row, requests):
    diagonal = iota((requests, requests), 0) == iota((requests, requests), 1)
    ctx = jnp.broadcast_to(ctx_row.astype(F32), (requests, requests))
    ctx = jnp.sum(jnp.where(diagonal, ctx, 0.0), axis=1, keepdims=True)
    lane = iota((requests, LANES), 1)
    index = (lane % (HEAD_DIM // 2)).astype(F32)
    inverse = jnp.exp(index * (-2.0 * math.log(ROPE_BASE) / HEAD_DIM))
    angles = ctx * inverse
    sign = jnp.where(lane % HEAD_DIM < HEAD_DIM // 2, -1.0, 1.0)
    return jnp.cos(angles), jnp.sin(angles) * sign


def rotate(chunk, cosine, sine):
    lane = iota(chunk.shape, 1)
    ahead = pltpu.roll(chunk, LANES - HEAD_DIM // 2, 1)
    behind = pltpu.roll(chunk, HEAD_DIM // 2, 1)
    turned = jnp.where(lane % HEAD_DIM < HEAD_DIM // 2, ahead, behind)
    return chunk * cosine + turned * sine


def copy_of(source, target, sem):
    return pltpu.make_async_copy(source, target, sem)


def copies_of(source, target, sems, base):
    step = source.shape[0] // 4
    return [
        copy_of(
            source.at[pl.ds(i * step, step)], target.at[pl.ds(i * step, step)], sems.at[base + i]
        )
        for i in range(4)
    ]


def page_copies(cache_hbm, pages, stages, sems, base):
    copies = []
    for i, stage in enumerate(stages):
        rows = pl.ds(stage[0], len(stage))
        copies.append(copy_of(cache_hbm.at[rows], pages.at[rows], sems.at[base + i]))
    return copies


def page_stages(count, stage, tail, last):
    head = max(count - tail, 0)
    starts = list(range(0, head, stage)) + list(range(head, count, last))
    return [range(a, b) for a, b in zip(starts, starts[1:] + [count])]


def prepare_kernel(
    pool, replicas, ids_ref, hidden_hbm, ctx_hbm, table_hbm, dest_hbm, attn_gain_hbm,
    wq_hbm, cache_hbm,
    hidden_ref, wq_ref, gain_ref, tables_ref, away_ref, span_ref, meta_ref, lent_ref,
    pick_ref, drop_ref,
    ctx, table, dest, gain, sems,
):
    inbox = replicas * CAP
    requests = ctx.shape[1]
    entries = meta_ref.shape[1]
    small = [
        copy_of(ctx_hbm, ctx, sems.at[0]),
        copy_of(table_hbm, table, sems.at[1]),
        copy_of(dest_hbm, dest, sems.at[2]),
        copy_of(attn_gain_hbm, gain, sems.at[3]),
    ]
    large = [copy_of(hidden_hbm, hidden_ref, sems.at[4])]
    large += copies_of(wq_hbm, wq_ref, sems, 5)
    lending = pl.ds(pool - lent_ref.shape[0], lent_ref.shape[0])
    large.append(copy_of(cache_hbm.at[lending], lent_ref, sems.at[9]))
    for copy in small + large:
        copy.start()
    for copy in small:
        copy.wait()
    gain_ref[...] = gain[...].reshape(1, gain.shape[0])
    ctx_row = ctx[...]

    def claims(values):
        held = jnp.zeros(values.shape, F32)
        spans = jnp.zeros(values.shape, F32)
        for k in range(table.shape[0]):
            match = table[k : k + 1, :] == values
            filled = jnp.clip(ctx_row - k * 128, 0, 128).astype(F32)
            held = jnp.where(match, 1.0, held)
            spans = jnp.where(match, filled, spans)
        return held.astype(BF16), spans

    held, spans = claims(iota((entries, requests), 0))
    numbers = (iota((SLOT, requests), 1) + 1).astype(BF16)
    ones = jnp.ones((SLOT, requests), BF16)
    holder = lax.dot_general(numbers, held, NT, preferred_element_type=F32)
    covered = lax.dot_general(ones, spans.astype(BF16), NT, preferred_element_type=F32)
    meta_ref[0:1, :] = holder[0:1, :].astype(jnp.int32) - 1
    meta_ref[1:2, :] = covered[0:1, :].astype(jnp.int32)
    meta_ref[2:3, :] = jnp.zeros((1, entries), jnp.int32)
    lent = dest.shape[1]
    across = jnp.broadcast_to(dest[...].astype(F32), (lent, lent))
    row, lane = iota((lent, lent), 0), iota((lent, lent), 1)
    down = jnp.sum(jnp.where(row == lane, across, 0.0), axis=1, keepdims=True)
    same = across == down
    before = jnp.sum(jnp.where(same & (lane < row), 1.0, 0.0), axis=1, keepdims=True)
    column = (replicas - 1 - down) * CAP + before
    column = jnp.broadcast_to(column, (lent, LANES)).astype(BF16)
    before = jnp.sum(jnp.where(same & (row < lane), 1.0, 0.0), axis=0, keepdims=True)
    line = dest[...] ^ replicas // 2
    line = jnp.broadcast_to(line.astype(F32), (lent, lent))
    line = (line * CAP + before).astype(BF16)
    expand = iota((lent * SLOT, lent), 0) // SLOT == iota((lent * SLOT, lent), 1)
    expand = jnp.where(expand, 1.0, 0.0).astype(BF16)
    column = jnp.dot(expand, column, preferred_element_type=F32).astype(jnp.int32)
    pick_ref[...] = column * SLOT + iota(column.shape, 0) % SLOT
    line = lax.dot_general(line, expand, NT, preferred_element_type=F32).astype(jnp.int32)
    drop_ref[...] = line * SLOT + iota(line.shape, 1) % SLOT
    meta_ref[3:4, :] = jnp.full((1, entries), ids_ref[0], jnp.int32)
    cosine, sine = rope_tables(ctx_row, requests)
    tables_ref[0] = cosine
    tables_ref[1] = sine
    slot = iota((inbox, requests), 0)
    lender = replicas - 1 - slot // CAP
    held, spans = claims(pool + lender * CAP + slot % CAP)
    away_ref[...] = held
    away_span = jnp.sum(spans, axis=1, keepdims=True)
    span_ref[...] = jnp.broadcast_to(away_span, span_ref.shape)
    for copy in large:
        copy.wait()


def query_kernel(
    count, meta_ref, *refs,
):
    pieces = refs[:count]
    (gain_ref, wq_ref, tables_ref, away_ref, span_ref,
     hidden_ref, normed_ref, packed_ref, send_ref, packs, sends) = refs[count:]
    requests = hidden_ref.shape[0]
    inbox = span_ref.shape[0]
    width = wq_ref.shape[1]
    chunks = -(-width // LANES)
    if count == 1:
        hidden = pieces[0][...]
    else:
        own, other = pieces[0][...], pieces[1][...]
        first = meta_ref[3:4, 0:1] == 0
        hidden = jnp.concatenate(
            [jnp.where(first, own, other), jnp.where(first, other, own)], axis=0
        )
    hidden_ref[...] = hidden
    normed = norm_rows(hidden.astype(F32), gain_ref[...])
    normed_ref[...] = normed
    queries = jnp.dot(normed, wq_ref[...], preferred_element_type=F32)
    if chunks * LANES > width:
        pad = jnp.zeros((requests, chunks * LANES - width), F32)
        queries = jnp.concatenate([queries, pad], axis=1)
    cosine, sine = tables_ref[0], tables_ref[1]
    zeros = jnp.zeros((requests, LANES), F32)
    nothing = jnp.zeros((inbox, LANES), F32)
    for j in range(SLOT):
        here = pl.ds(j, requests, stride=SLOT)
        there = pl.ds(j, inbox, stride=SLOT)
        if j < chunks:
            chunk = rotate(queries[:, j * LANES : (j + 1) * LANES], cosine, sine)
            chunk = (chunk.astype(BF16).astype(F32) * ATTN_SCALE).astype(BF16)
            packs[here, :] = chunk.astype(F32)
            sends[there, :] = jnp.dot(away_ref[...], chunk, preferred_element_type=F32)
        else:
            packs[here, :] = zeros
            sends[there, :] = span_ref[...] if j == META else nothing
    packed_ref[...] = packs[...]
    send_ref[...] = sends[...].astype(BF16)


def unpack(packed):
    low = iota(packed.shape, 1) < HEAD_DIM
    even = jnp.where(low, packed, 0.0)
    odd = jnp.where(low, pltpu.roll(packed, HEAD_DIM, 1), 0.0)
    return jnp.concatenate([even, odd], axis=0)


def head_rows(heads):
    return [(h // 2) + SLOT * (h % 2) for h in range(heads)]


def token_of_column(heads, kv_local, columns):
    row = iota((ROWS, columns), 0)
    column = iota((ROWS, columns), 1)
    wanted = jnp.full((ROWS, columns), kv_local, jnp.int32)
    for h, place in enumerate(head_rows(heads)):
        wanted = jnp.where(row == place, h // (heads // kv_local), wanted)
    return jnp.where(column % kv_local == wanted, column // kv_local, 1 << 20)


def score_page(query, block):
    return lax.dot_general(query, block, NT, preferred_element_type=F32)


def weigh_page(scores, tokens, span):
    scores = jnp.where(tokens < span, scores, NEG_FILL)
    top = jnp.max(scores, axis=1, keepdims=True)
    weights = jnp.exp(scores - top)
    return top, jnp.sum(weights, axis=1, keepdims=True), weights.astype(BF16)


def attend_pages(stages, copies, query_of, block_of, span_of, tokens, keep):
    def score_stage(i):
        if copies is not None:
            copies[i].wait()
        return {p: score_page(query_of(p), block_of(p)) for p in stages[i]}

    scores = score_stage(0)
    for i, pages in enumerate(stages):
        if i + 1 < len(stages):
            ahead = score_stage(i + 1)
        weighed = {p: weigh_page(scores[p], tokens, span_of(p)) for p in pages}
        outs = {
            p: jnp.dot(weighed[p][2], block_of(p), preferred_element_type=F32)
            for p in pages
        }
        for p in pages:
            keep(p, weighed[p][0], weighed[p][1], outs[p])
        if i + 1 < len(stages):
            scores = ahead


def spread_queries(target, packed):
    low = iota(packed.shape, 2) < HEAD_DIM
    target[:, 0:SLOT, :] = jnp.where(low, packed, 0.0)
    target[:, SLOT:ROWS, :] = jnp.where(low, pltpu.roll(packed, HEAD_DIM, 2), 0.0)


def merge_pages(places, top_of, sum_of, top, acc, scaled, start, before):
    requests = start.shape[0]
    for p, place in enumerate(places):
        top[place] = jnp.maximum(top[place], top_of(p))
    acc[0:requests] = start * jnp.exp(before - top[0:requests])
    for p, place in enumerate(places):
        scaled[p] = sum_of(p) * jnp.exp(top_of(p) - top[place])
    for p, place in enumerate(places):
        acc[place] = acc[place] + scaled[p]


def project_heads(values, weights_ref, heads, copies):
    rows, depth = values.shape
    wide = weights_ref.shape[0] // len(copies)
    part = wide // heads
    if heads == 1:
        for copy in copies:
            copy.wait()
        return jnp.dot(values, weights_ref[...], preferred_element_type=F32)
    repeat = iota((part, wide), 1) // heads == iota((part, wide), 0)
    repeat = jnp.where(repeat, 1.0, 0.0).astype(BF16)
    parts = [values[:, i : i + part] for i in range(0, depth, part)]
    spread = jnp.dot(
        jnp.concatenate(parts, axis=0), repeat, preferred_element_type=F32
    ).astype(BF16)
    lane = iota((1, wide), 1) % heads
    masks = [jnp.where(lane == k, 1.0, 0.0).astype(BF16) for k in range(heads)]
    total = jnp.zeros((heads * rows, LANES), F32)
    for i in range(len(parts)):
        piece = spread[i * rows : (i + 1) * rows]
        piece = jnp.concatenate([piece * mask for mask in masks], axis=0)
        copies[i].wait()
        total += jnp.dot(
            piece, weights_ref[i * wide : (i + 1) * wide, :], preferred_element_type=F32
        )
    return total


def local_kernel(
    heads, kv_local, meta_hbm, packed_hbm, normed_hbm, wkv_hbm, tables_hbm, cache_hbm,
    state_hbm,
    meta, packed, normed, raw, tables, pages, queries, fresh, scores, tops, sums, top,
    acc, scaled, sems,
):
    requests = normed.shape[0]
    count, columns, _ = pages.shape
    small = [
        copy_of(meta_hbm, meta, sems.at[0]),
        copy_of(packed_hbm, packed, sems.at[1]),
        copy_of(normed_hbm, normed, sems.at[2]),
        copy_of(tables_hbm, tables, sems.at[3]),
    ]
    parts = 6
    step = raw.shape[0] // parts
    weights = [
        copy_of(wkv_hbm.at[pl.ds(i * step, step)], raw.at[pl.ds(i * step, step)], sems.at[4 + i])
        for i in range(parts)
    ]
    stages = page_stages(count, 8, 8, 4)
    paging = page_copies(cache_hbm, pages, stages, sems, 14)
    for copy in small + weights + paging:
        copy.start()
    tokens = token_of_column(heads, kv_local, columns)
    lower = iota((ROWS, LANES), 1) < HEAD_DIM
    low = iota((requests, LANES), 1) < HEAD_DIM
    low16 = iota((requests, ROWS, LANES), 2) < HEAD_DIM
    for copy in small:
        copy.wait()
    spread_queries(queries, packed[...].reshape(requests, SLOT, LANES))
    cosine = jnp.where(low, tables[0], 1.0)
    sine = jnp.where(low, tables[1], 0.0)
    projected = project_heads(normed[...], raw, kv_local, weights)
    new = [
        rotate(projected[k * requests : (k + 1) * requests], cosine, sine)
        .astype(BF16)
        .astype(F32)
        for k in range(kv_local)
    ]
    used = {place: h for h, place in enumerate(head_rows(heads))}
    for place in range(ROWS):
        value = jnp.zeros((requests, LANES), F32)
        if place in used:
            value = new[used[place] // (heads // kv_local)]
        fresh[pl.ds(place, requests, stride=ROWS), :] = value
    added = fresh[...].reshape(requests, ROWS, LANES)
    score = jnp.sum(queries[...] * added, axis=2, keepdims=True)
    top[0:requests] = jnp.broadcast_to(score, added.shape)
    scores[...] = jnp.broadcast_to(score, added.shape)

    def place_of(p):
        owner = meta[0, p]
        return jnp.where(owner < 0, requests, owner)

    places = [place_of(p) for p in range(count)]

    def keep(p, page_top, total, out):
        tops[p] = jnp.broadcast_to(page_top, (ROWS, LANES))
        sums[p] = jnp.where(lower, total, out)
        top[places[p]] = jnp.maximum(top[places[p]], tops[p])

    attend_pages(
        stages,
        paging,
        lambda p: queries[jnp.maximum(meta[0, p], 0)].astype(BF16),
        lambda p: pages[p],
        lambda p: meta[1, p],
        tokens,
        keep,
    )
    start = jnp.where(low16, 1.0, fresh[...].reshape(requests, ROWS, LANES))
    acc[0:requests] = start * jnp.exp(scores[...] - top[0:requests])
    for p, place in enumerate(places):
        scaled[p] = sums[p] * jnp.exp(tops[p] - top[place])
    for p, place in enumerate(places):
        acc[place] = acc[place] + scaled[p]
    parked = []
    step = requests // 4
    for i in range(4):
        rows = slice(i * step, (i + 1) * step)
        whole = acc[rows]
        acc[rows] = jnp.where(
            low16[rows], top[rows] + jnp.log(whole), whole / pltpu.roll(whole, HEAD_DIM, 2)
        )
        part = pl.ds(i * step, step)
        parked.append(copy_of(acc.at[part], state_hbm.at[part], sems.at[10 + i]))
        parked[i].start()
    for copy in parked:
        copy.wait()


def lent_kernel(
    heads, kv_local, asked_ref, pages, pick_ref, drop_ref, meta_ref, packed_ref,
    normed_ref, tables_ref, hidden_ref,
    reply_hbm, meta_hbm, packed_hbm, normed_hbm, tables_hbm, hidden_hbm,
    reply16, sems,
):
    outgoing, columns, _ = pages.shape
    parked = [
        copy_of(packed_ref, packed_hbm, sems.at[0]),
        copy_of(normed_ref, normed_hbm, sems.at[1]),
        copy_of(hidden_ref, hidden_hbm, sems.at[2]),
        copy_of(tables_ref, tables_hbm, sems.at[3]),
        copy_of(meta_ref, meta_hbm, sems.at[4]),
    ]
    for copy in parked:
        copy.start()
    slot_rows = asked_ref.shape[0]
    shape = (outgoing * SLOT, slot_rows)
    chosen = jnp.where(pick_ref[:, 0:1] == iota(shape, 1), 1.0, 0.0).astype(BF16)
    asked = jnp.dot(chosen, asked_ref[...], preferred_element_type=F32)
    tokens = token_of_column(heads, kv_local, columns).astype(F32)
    low = iota((SLOT, LANES), 1) < HEAD_DIM
    lane = iota((SLOT, LANES), 1)
    row = iota((SLOT, LANES), 0)

    def terms(total, offset):
        leading = total.astype(BF16).astype(F32)
        rest = total - leading
        second = rest.astype(BF16).astype(F32)
        third = rest - second
        spot = lane - offset - 3 * row
        placed = jnp.where(spot == 0, leading, 0.0)
        placed = jnp.where(spot == 1, second, placed)
        return jnp.where(spot == 2, third, placed)

    packed = [asked[j * SLOT : (j + 1) * SLOT] for j in range(outgoing)]
    replies = {}

    def keep(j, top, total, out):
        out = out / total
        logs = top + jnp.log(total)
        even = pltpu.roll(out[0:SLOT], HEAD_DIM, 1)
        both = jnp.where(low, even, out[SLOT:ROWS])
        line = jnp.sum(
            terms(logs[0:SLOT], 0) + terms(logs[SLOT:ROWS], HEAD_DIM), axis=0, keepdims=True
        )
        replies[j] = jnp.where(row == META, line, both)

    attend_pages(
        page_stages(outgoing, 8, 0, 8),
        None,
        lambda j: unpack(packed[j]).astype(BF16),
        lambda j: pages[j],
        lambda j: packed[j][META : META + 1, 0:1],
        tokens,
        keep,
    )
    shape = (slot_rows, outgoing * SLOT)
    placed = jnp.where(drop_ref[0:1, :] == iota(shape, 0), 1.0, 0.0).astype(BF16)
    every = jnp.concatenate([replies[j] for j in range(outgoing)], axis=0).astype(BF16)
    reply = jnp.dot(placed, every, preferred_element_type=F32)
    reply16[...] = reply.astype(BF16)
    replying = copy_of(reply16, reply_hbm, sems.at[5])
    replying.start()
    for copy in parked + [replying]:
        copy.wait()


def combine_kernel(
    heads, pool, meta_hbm, state_hbm, wo_hbm, hidden_hbm, gain_hbm, router_hbm,
    routes_hbm, wd_hbm, reply_ref,
    part_ref, meta_ref, hidden_ref, gain_ref, router_ref, routes_ref, wd_ref,
    meta, state, wo, gain, tops, accs, scaled, reply, finals, sems,
):
    requests = state.shape[0]
    inbox = reply_ref.shape[0] // SLOT
    chunks = -(-heads // 2)
    numbers = copy_of(meta_hbm, meta, sems.at[11])
    arriving = copy_of(state_hbm, state, sems.at[0])
    weights = copies_of(wo_hbm, wo, sems, 1)
    gaining = copy_of(gain_hbm, gain, sems.at[5])
    later = [
        copy_of(meta_hbm, meta_ref, sems.at[6]),
        copy_of(hidden_hbm, hidden_ref, sems.at[7]),
        copy_of(router_hbm, router_ref, sems.at[8]),
        copy_of(routes_hbm, routes_ref, sems.at[9]),
        copy_of(wd_hbm.at[pl.ds(0, wd_ref.shape[0])], wd_ref, sems.at[10]),
    ]
    for copy in [numbers, arriving] + weights + [gaining] + later:
        copy.start()
    reply[...] = reply_ref[...].astype(F32)
    tops[...] = jnp.full(tops.shape, NEG_FILL, F32)
    accs[...] = jnp.zeros(accs.shape, F32)
    low = iota((SLOT, LANES), 1) < HEAD_DIM
    lane = iota((SLOT, LANES), 1)
    row = iota((SLOT, LANES), 0)
    mine = (lane % HEAD_DIM) // 3 == row

    def place_of(s):
        lender = s // CAP ^ (inbox // CAP // 2)
        owner = meta[0, pool + lender * CAP + s % CAP]
        return jnp.where(owner < 0, requests, owner)

    def logs_of(s):
        line = reply[s * SLOT + META : s * SLOT + META + 1, :]
        line = jnp.where(mine, jnp.broadcast_to(line, (SLOT, LANES)), 0.0)
        even = jnp.sum(jnp.where(low, line, 0.0), axis=1, keepdims=True)
        odd = jnp.sum(jnp.where(low, 0.0, line), axis=1, keepdims=True)
        logs = jnp.concatenate([even, odd], axis=0)
        return jnp.broadcast_to(logs, (ROWS, LANES))

    def sum_of(s):
        packed = reply[s * SLOT : (s + 1) * SLOT, :]
        even = jnp.where(low, 1.0, pltpu.roll(packed, HEAD_DIM, 1))
        odd = jnp.where(low, 1.0, packed)
        return jnp.concatenate([even, odd], axis=0)

    logs = [logs_of(s) for s in range(inbox)]
    numbers.wait()
    places = [place_of(s) for s in range(inbox)]
    for s, place in enumerate(places):
        tops[place] = jnp.maximum(tops[place], logs[s])
    for s, place in enumerate(places):
        scaled[s] = sum_of(s) * jnp.exp(logs[s] - tops[place])
    for s, place in enumerate(places):
        accs[place] = accs[place] + scaled[s]
    arriving.wait()
    low16 = iota(state.shape, 2) < HEAD_DIM
    start = state[...]
    before = jnp.where(low16, start, pltpu.roll(start, HEAD_DIM, 2))
    remote = tops[0:requests]
    highest = jnp.maximum(before, remote)
    whole = accs[0:requests] * jnp.exp(remote - highest)
    whole = whole + jnp.where(low16, 1.0, start) * jnp.exp(before - highest)
    finals[...] = (whole / pltpu.roll(whole, HEAD_DIM, 2)).reshape(
        requests * ROWS, LANES
    )
    wide = iota((requests, LANES), 1) < HEAD_DIM
    parts = []
    for j in range(chunks):
        even = finals[pl.ds(j, requests, stride=ROWS), :]
        odd = finals[pl.ds(SLOT + j, requests, stride=ROWS), :]
        parts.append(jnp.where(wide, pltpu.roll(even, HEAD_DIM, 1), odd).astype(BF16))
    attention = jnp.concatenate(parts, axis=1)[:, : heads * HEAD_DIM]
    for copy in weights:
        copy.wait()
    part_ref[...] = jnp.dot(attention, wo[...], preferred_element_type=F32).astype(BF16)
    gaining.wait()
    gain_ref[...] = gain[...].reshape(1, gain.shape[0])
    for copy in later:
        copy.wait()


def load_kernel(wd_hbm, order_hbm, wd_ref, sem):
    del order_hbm
    rows = wd_ref.shape[0]
    copy = copy_of(wd_hbm.at[pl.ds(wd_hbm.shape[0] - rows, rows)], wd_ref, sem)
    copy.start()
    copy.wait()


def finish_kernel(attended_ref, own_ref, other_ref, attended_out, experts_out):
    attended_out[...] = attended_ref[...]
    experts_out[...] = (own_ref[...] + other_ref[...].astype(F32)).astype(BF16)


def own_rows(values, first):
    half = values.shape[0] // 2
    return jnp.where(first, values[:half], values[half:])


def residual_kernel(
    tp, count, meta_ref, hidden_ref, *refs,
):
    pieces = refs[:count]
    gain_ref, attended_ref, input_ref, again_ref = refs[count:]
    requests = hidden_ref.shape[0]
    if count == 2:
        summed = pieces[0][...].astype(F32) + pieces[1][...].astype(F32)
    else:
        summed = pieces[0][0:requests, :].astype(F32)
        for t in range(1, tp):
            part = pieces[0][t * requests : (t + 1) * requests, :]
            summed = summed + part.astype(F32)
    attended = (hidden_ref[...].astype(F32) + RESID_SCALE * summed).astype(BF16)
    if count == 2:
        attended_ref[...] = own_rows(attended, meta_ref[3:4, 0:1] == 0)
    else:
        attended_ref[...] = attended
    ffn_input = norm_rows(attended.astype(F32), gain_ref[...])
    input_ref[...] = ffn_input
    again_ref[...] = ffn_input


def gate_column(units, meta_ref, input_ref, router_ref, routes_ref):
    ffn_input = input_ref[...]
    requests = ffn_input.shape[0]
    logits = lax.dot_general(router_ref[...], ffn_input, NT, preferred_element_type=F32)
    expert = iota(logits.shape, 0)
    named = jnp.zeros(logits.shape, F32)
    for k in range(routes_ref.shape[0]):
        named = jnp.where(routes_ref[k : k + 1, :] == expert, 1.0, named)
    chosen = named > 0.5
    top = jnp.max(jnp.where(chosen, logits, NEG_FILL), axis=0, keepdims=True)
    weights = jnp.where(chosen, jnp.exp(logits - top), 0.0)
    total = jnp.sum(weights, axis=0, keepdims=True)
    mine = expert == meta_ref[3:4, 0:1] * units // FF
    line = jnp.sum(jnp.where(mine, weights, 0.0), axis=0, keepdims=True) / total
    diagonal = iota((requests, requests), 0) == iota((requests, requests), 1)
    line = jnp.where(diagonal, jnp.broadcast_to(line, (requests, requests)), 0.0)
    return jnp.sum(line, axis=1, keepdims=True)


def expert_kernel(
    units, meta_ref, lifted_ref, input_ref, router_ref, routes_ref, wd_ref, wd_rest_ref,
    *outs
):
    column = gate_column(units, meta_ref, input_ref, router_ref, routes_ref)
    gate = lifted_ref[0]
    active = gate / (1.0 + jnp.exp(-gate)) * lifted_ref[1]
    active = active.astype(BF16)
    half = wd_ref.shape[0]
    share = jnp.dot(active[:, :half], wd_ref[...], preferred_element_type=F32)
    share += jnp.dot(active[:, half:], wd_rest_ref[...], preferred_element_type=F32)
    share *= column
    if len(outs) == 2:
        first = meta_ref[3:4, 0:1] == 0
        outs[0][...] = own_rows(share, first)
        outs[1][...] = own_rows(share, jnp.logical_not(first)).astype(BF16)
    else:
        outs[0][...] = share.astype(BF16)


def call(body, outs, in_specs, scratch=(), limit=16, flops=0, moved=0):
    return pl.pallas_call(
        body,
        out_shape=outs,
        in_specs=in_specs,
        out_specs=[VMEM if isinstance(o, jax.ShapeDtypeStruct) else HBM for o in outs],
        scratch_shapes=list(scratch),
        compiler_params=pltpu.CompilerParams(vmem_limit_bytes=limit << 20),
        cost_estimate=pl.CostEstimate(
            flops=flops, bytes_accessed=moved, transcendentals=0
        ),
    )


def swap(values):
    return lax.ppermute(values, "tensor", [(0, 1), (1, 0)])


def on_device(
    hidden,
    attn_gain,
    w_query,
    w_keyvalue,
    w_output,
    cache,
    page_table,
    ctx_len,
    move_dest,
    ffn_gain,
    router,
    routes,
    w_in,
    w_down,
):
    replicas = lax.axis_size("replica")
    tp = lax.axis_size("tensor")
    rank = lax.axis_index("tensor").astype(jnp.int32)
    rows, width = hidden.shape
    pool, page_len, kv_local, _ = cache.shape
    outgoing = move_dest.shape[0]
    local_pages = pool - outgoing
    requests = page_table.shape[0]
    heads = w_query.shape[1] // HEAD_DIM
    inbox = replicas * CAP
    units = w_down.shape[0]
    assert FF % units == 0
    columns = page_len * kv_local
    entries = -(-(pool + inbox) // LANES) * LANES
    struct = jax.ShapeDtypeStruct
    pair = tp == 2
    ids = rank.reshape(1)

    def pin(values):
        return pltpu.with_memory_space_constraint(values, pltpu.HBM)

    def exchange(blocks, order):
        blocks = blocks.reshape(replicas, CAP * SLOT, LANES)
        blocks = lax.all_to_all(
            blocks,
            "replica",
            split_axis=0,
            concat_axis=0,
            tiled=True,
            axis_index_groups=[list(order)],
        )
        return blocks.reshape(inbox * SLOT, LANES)

    blocks = pin(cache.reshape(pool, columns, LANES))
    if pair:
        pieces = [hidden, swap(hidden)]
    else:
        pieces = [lax.all_gather(hidden, "tensor", axis=0, tiled=True)]
    meta_shape = (4, entries)
    tables_shape = (2, requests, LANES)
    own, wq, gain, tables, away, away_span, meta, lent, pick, drop = call(
        functools.partial(prepare_kernel, pool, replicas),
        [
            struct(hidden.shape, BF16),
            struct(w_query.shape, BF16),
            struct((1, width), F32),
            struct(tables_shape, F32),
            struct((inbox, requests), BF16),
            struct((inbox, LANES), F32),
            struct(meta_shape, jnp.int32),
            struct((outgoing, columns, LANES), BF16),
            struct((outgoing * SLOT, LANES), jnp.int32),
            struct((outgoing, outgoing * SLOT), jnp.int32),
        ],
        [SMEM] + [HBM] * 7,
        [
            pltpu.VMEM((1, requests), jnp.int32),
            pltpu.VMEM((page_table.shape[1], requests), jnp.int32),
            pltpu.VMEM((1, outgoing), jnp.int32),
            pltpu.VMEM((width,), F32),
            pltpu.SemaphoreType.DMA((10,)),
        ],
        moved=2 * w_query.size,
    )(
        ids,
        pin(hidden),
        pin(ctx_len.reshape(1, requests)),
        pin(page_table.T),
        pin(move_dest.reshape(1, outgoing)),
        pin(attn_gain),
        pin(w_query),
        blocks,
    )
    if pair:
        pieces[0] = own
    hidden_all, normed, packed, sends = call(
        functools.partial(query_kernel, len(pieces)),
        [
            struct((requests, width), BF16),
            struct((requests, width), BF16),
            struct((requests * SLOT, LANES), F32),
            struct((inbox * SLOT, LANES), BF16),
        ],
        [VMEM] * (len(pieces) + 6),
        [
            pltpu.VMEM((requests * SLOT, LANES), F32),
            pltpu.VMEM((inbox * SLOT, LANES), F32),
        ],
        flops=4 * requests * width * w_query.shape[1],
        moved=2 * w_query.size,
    )(meta, *pieces, gain, wq, tables, away, away_span)
    asked = exchange(sends, range(replicas)[::-1])
    replies, meta_far, packed_far, normed_far, tables_far, hidden_far = call(
        functools.partial(lent_kernel, heads, kv_local),
        [
            pltpu.HBM((inbox * SLOT, LANES), BF16),
            pltpu.HBM(meta_shape, jnp.int32),
            pltpu.HBM((requests * SLOT, LANES), F32),
            pltpu.HBM((requests, width), BF16),
            pltpu.HBM(tables_shape, F32),
            pltpu.HBM((requests, width), BF16),
        ],
        [VMEM] * 9,
        [
            pltpu.VMEM((inbox * SLOT, LANES), BF16),
            pltpu.SemaphoreType.DMA((6,)),
        ],
        flops=4 * ROWS * columns * LANES * outgoing,
        moved=2 * columns * LANES * outgoing,
    )(asked, lent, pick, drop, meta, packed, normed, tables, hidden_all)
    returned = exchange(replies, [r ^ replicas // 2 for r in range(replicas)])
    (state,) = call(
        functools.partial(local_kernel, heads, kv_local),
        [pltpu.HBM((requests, ROWS, LANES), F32)],
        [HBM] * 6,
        [
            pltpu.SMEM(meta_shape, jnp.int32),
            pltpu.VMEM((requests * SLOT, LANES), F32),
            pltpu.VMEM((requests, width), BF16),
            pltpu.VMEM((width * kv_local, LANES), BF16),
            pltpu.VMEM(tables_shape, F32),
            pltpu.VMEM((local_pages, columns, LANES), BF16),
            pltpu.VMEM((requests, ROWS, LANES), F32),
            pltpu.VMEM((requests * ROWS, LANES), F32),
            pltpu.VMEM((requests, ROWS, LANES), F32),
            pltpu.VMEM((local_pages, ROWS, LANES), F32),
            pltpu.VMEM((local_pages, ROWS, LANES), F32),
            pltpu.VMEM((requests + 1, ROWS, LANES), F32),
            pltpu.VMEM((requests + 1, ROWS, LANES), F32),
            pltpu.VMEM((local_pages, ROWS, LANES), F32),
            pltpu.SemaphoreType.DMA((14 + local_pages,)),
        ],
        limit=24,
        flops=4 * ROWS * columns * LANES * local_pages,
        moved=2 * columns * LANES * local_pages,
    )(
        pin(meta_far),
        pin(packed_far),
        pin(normed_far),
        pin(w_keyvalue.reshape(width * kv_local, LANES)),
        pin(tables_far),
        blocks,
    )
    half = struct((units // 2, width), BF16)
    part, meta, hidden_all, gain, router_t, routes_t, wd = call(
        functools.partial(combine_kernel, heads, pool),
        [
            struct((requests, width), BF16),
            struct(meta_shape, jnp.int32),
            struct((requests, width), BF16),
            struct((1, width), F32),
            struct(router.shape[::-1], BF16),
            struct(routes.shape[::-1], jnp.int32),
            half,
        ],
        [HBM] * 8 + [VMEM],
        [
            pltpu.SMEM(meta_shape, jnp.int32),
            pltpu.VMEM((requests, ROWS, LANES), F32),
            pltpu.VMEM(w_output.shape, BF16),
            pltpu.VMEM((width,), F32),
            pltpu.VMEM((requests + 1, ROWS, LANES), F32),
            pltpu.VMEM((requests + 1, ROWS, LANES), F32),
            pltpu.VMEM((inbox, ROWS, LANES), F32),
            pltpu.VMEM((inbox * SLOT, LANES), F32),
            pltpu.VMEM((requests * ROWS, LANES), F32),
            pltpu.SemaphoreType.DMA((12,)),
        ],
        flops=2 * requests * w_output.size,
        moved=2 * w_output.size,
    )(
        pin(meta_far), pin(state), pin(w_output), pin(hidden_far), pin(ffn_gain),
        pin(router.T), pin(routes.T), pin(w_down), returned,
    )
    if pair:
        parts = [part, swap(part)]
    else:
        parts = [lax.all_gather(part, "tensor", axis=0, tiled=True)]
    (wd_rest,) = call(
        load_kernel,
        [half],
        [HBM, ANY],
        [pltpu.SemaphoreType.DMA],
        moved=w_down.size,
    )(pin(w_down), part)
    attended, ffn_input, ffn_again = call(
        functools.partial(residual_kernel, tp, len(parts)),
        [
            struct((rows if pair else requests, width), BF16),
            struct((requests, width), BF16),
            struct((requests, width), BF16),
        ],
        [VMEM] * (len(parts) + 3),
        flops=2 * requests * width,
        moved=8 * requests * width,
    )(meta, hidden_all, *parts, gain)
    lifted = jnp.einsum("rd,dsu->sru", ffn_input, w_in, preferred_element_type=F32)
    shapes = [struct((requests, width), BF16)]
    if pair:
        shapes = [struct((rows, width), F32), struct((rows, width), BF16)]
    shares = call(
        functools.partial(expert_kernel, units),
        shapes,
        [VMEM] * 7,
        flops=2 * requests * w_down.size,
        moved=2 * w_down.size,
    )(meta, lifted, ffn_again, router_t, routes_t, wd, wd_rest)
    if pair:
        out = struct((rows, width), BF16)
        return tuple(
            call(finish_kernel, [out, out], [VMEM] * 3)(attended, shares[0], swap(shares[1]))
        )
    shares = lax.all_gather(shares[0], "tensor", axis=0)
    mine = lax.dynamic_slice_in_dim(shares, rank * rows, rows, axis=1)
    experts_out = jnp.sum(mine.astype(F32), axis=0).astype(BF16)
    attended = lax.dynamic_slice_in_dim(attended, rank * rows, rows, axis=0)
    return attended, experts_out


def solution(mesh):
    placed = (
        P(("replica", "tensor"), None),
        P(),
        P(None, "tensor"),
        P(None, "tensor", None),
        P("tensor", None),
        P("replica", None, "tensor", None),
        P("replica", None),
        P("replica"),
        P("replica"),
        P(),
        P(),
        P("replica", None),
        P(None, None, "tensor"),
        P("tensor", None),
    )
    return jax.shard_map(
        on_device,
        mesh=mesh,
        in_specs=placed,
        out_specs=(P(("replica", "tensor"), None), P(("replica", "tensor"), None)),
        check_vma=False,
    )
```

```python
import functools
import math

import jax
import jax.numpy as jnp
from jax import lax
from jax.experimental import pallas as pl
from jax.experimental.pallas import tpu as pltpu
from jax.sharding import PartitionSpec as P

HEAD_DIM = 64
EXPERTS = 40
FF = 512
CAP = 2
LANES = 128
SLOT = 8
ROWS = 16
META = 6

ATTN_SCALE = 0.015625
RESID_SCALE = 0.22
ROPE_BASE = 10000.0
EPSILON = 1e-06
NEG_FILL = -1e30

F32 = jnp.float32
BF16 = jnp.bfloat16
VMEM = pl.BlockSpec(memory_space=pltpu.VMEM)
SMEM = pl.BlockSpec(memory_space=pltpu.SMEM)
ANY = pl.BlockSpec(memory_space=pl.ANY)
HBM = pl.BlockSpec(memory_space=pltpu.HBM)
NT = (((1,), (1,)), ((), ()))


def iota(shape, axis):
    return lax.broadcasted_iota(jnp.int32, shape, axis)


def norm_rows(values, gain):
    factor = lax.rsqrt(jnp.mean(values * values, axis=-1, keepdims=True) + EPSILON)
    return (values * factor * gain).astype(BF16)


def rope_tables(ctx_row, requests):
    diagonal = iota((requests, requests), 0) == iota((requests, requests), 1)
    ctx = jnp.broadcast_to(ctx_row.astype(F32), (requests, requests))
    ctx = jnp.sum(jnp.where(diagonal, ctx, 0.0), axis=1, keepdims=True)
    lane = iota((requests, LANES), 1)
    index = (lane % (HEAD_DIM // 2)).astype(F32)
    inverse = jnp.exp(index * (-2.0 * math.log(ROPE_BASE) / HEAD_DIM))
    angles = ctx * inverse
    sign = jnp.where(lane % HEAD_DIM < HEAD_DIM // 2, -1.0, 1.0)
    return jnp.cos(angles), jnp.sin(angles) * sign


def rotate(chunk, cosine, sine):
    lane = iota(chunk.shape, 1)
    ahead = pltpu.roll(chunk, LANES - HEAD_DIM // 2, 1)
    behind = pltpu.roll(chunk, HEAD_DIM // 2, 1)
    turned = jnp.where(lane % HEAD_DIM < HEAD_DIM // 2, ahead, behind)
    return chunk * cosine + turned * sine


def copy_of(source, target, sem):
    return pltpu.make_async_copy(source, target, sem)


def copies_of(source, target, sems, base):
    step = source.shape[0] // 4
    return [
        copy_of(
            source.at[pl.ds(i * step, step)], target.at[pl.ds(i * step, step)], sems.at[base + i]
        )
        for i in range(4)
    ]


def page_copies(cache_hbm, pages, stages, sems, base):
    copies = []
    for i, stage in enumerate(stages):
        rows = pl.ds(stage[0], len(stage))
        copies.append(copy_of(cache_hbm.at[rows], pages.at[rows], sems.at[base + i]))
    return copies


def page_stages(count, first, rest):
    starts = [0] + list(range(min(first, count), count, rest))
    return [range(a, b) for a, b in zip(starts, starts[1:] + [count])]


def prepare_kernel(
    pool, replicas, ids_ref, hidden_hbm, ctx_hbm, table_hbm, dest_hbm, attn_gain_hbm,
    wq_hbm, cache_hbm,
    hidden_ref, wq_ref, gain_ref, tables_ref, away_ref, span_ref, meta_ref, lent_ref,
    pick_ref, drop_ref,
    ctx, table, dest, gain, sems,
):
    inbox = replicas * CAP
    requests = ctx.shape[1]
    entries = meta_ref.shape[1]
    small = [
        copy_of(ctx_hbm, ctx, sems.at[0]),
        copy_of(table_hbm, table, sems.at[1]),
        copy_of(dest_hbm, dest, sems.at[2]),
        copy_of(attn_gain_hbm, gain, sems.at[3]),
    ]
    large = [copy_of(hidden_hbm, hidden_ref, sems.at[4])]
    large += copies_of(wq_hbm, wq_ref, sems, 5)
    lending = pl.ds(pool - lent_ref.shape[0], lent_ref.shape[0])
    large.append(copy_of(cache_hbm.at[lending], lent_ref, sems.at[9]))
    for copy in small + large:
        copy.start()
    for copy in small:
        copy.wait()
    gain_ref[...] = gain[...].reshape(1, gain.shape[0])
    ctx_row = ctx[...]

    def claims(values):
        held = jnp.zeros(values.shape, F32)
        spans = jnp.zeros(values.shape, F32)
        for k in range(table.shape[0]):
            match = table[k : k + 1, :] == values
            filled = jnp.clip(ctx_row - k * 128, 0, 128).astype(F32)
            held = jnp.where(match, 1.0, held)
            spans = jnp.where(match, filled, spans)
        return held.astype(BF16), spans

    held, spans = claims(iota((entries, requests), 0))
    numbers = (iota((SLOT, requests), 1) + 1).astype(BF16)
    ones = jnp.ones((SLOT, requests), BF16)
    holder = lax.dot_general(numbers, held, NT, preferred_element_type=F32)
    covered = lax.dot_general(ones, spans.astype(BF16), NT, preferred_element_type=F32)
    meta_ref[0:1, :] = holder[0:1, :].astype(jnp.int32) - 1
    meta_ref[1:2, :] = covered[0:1, :].astype(jnp.int32)
    meta_ref[2:3, :] = jnp.zeros((1, entries), jnp.int32)
    lent = dest.shape[1]
    across = jnp.broadcast_to(dest[...].astype(F32), (lent, lent))
    row, lane = iota((lent, lent), 0), iota((lent, lent), 1)
    down = jnp.sum(jnp.where(row == lane, across, 0.0), axis=1, keepdims=True)
    same = across == down
    before = jnp.sum(jnp.where(same & (lane < row), 1.0, 0.0), axis=1, keepdims=True)
    column = (replicas - 1 - down) * CAP + before
    column = jnp.broadcast_to(column, (lent, LANES)).astype(BF16)
    before = jnp.sum(jnp.where(same & (row < lane), 1.0, 0.0), axis=0, keepdims=True)
    line = dest[...] ^ replicas // 2
    line = jnp.broadcast_to(line.astype(F32), (lent, lent))
    line = (line * CAP + before).astype(BF16)
    expand = iota((lent * SLOT, lent), 0) // SLOT == iota((lent * SLOT, lent), 1)
    expand = jnp.where(expand, 1.0, 0.0).astype(BF16)
    column = jnp.dot(expand, column, preferred_element_type=F32).astype(jnp.int32)
    pick_ref[...] = column * SLOT + iota(column.shape, 0) % SLOT
    line = lax.dot_general(line, expand, NT, preferred_element_type=F32).astype(jnp.int32)
    drop_ref[...] = line * SLOT + iota(line.shape, 1) % SLOT
    meta_ref[3:4, :] = jnp.full((1, entries), ids_ref[0], jnp.int32)
    cosine, sine = rope_tables(ctx_row, requests)
    tables_ref[0] = cosine
    tables_ref[1] = sine
    slot = iota((inbox, requests), 0)
    lender = replicas - 1 - slot // CAP
    held, spans = claims(pool + lender * CAP + slot % CAP)
    away_ref[...] = held
    away_span = jnp.sum(spans, axis=1, keepdims=True)
    span_ref[...] = jnp.broadcast_to(away_span, span_ref.shape)
    for copy in large:
        copy.wait()


def query_kernel(
    count, meta_ref, *refs,
):
    pieces = refs[:count]
    (gain_ref, wq_ref, tables_ref, away_ref, span_ref,
     hidden_ref, normed_ref, packed_ref, send_ref, packs, sends) = refs[count:]
    requests = hidden_ref.shape[0]
    inbox = span_ref.shape[0]
    width = wq_ref.shape[1]
    chunks = -(-width // LANES)
    if count == 1:
        hidden = pieces[0][...]
    else:
        own, other = pieces[0][...], pieces[1][...]
        first = meta_ref[3:4, 0:1] == 0
        hidden = jnp.concatenate(
            [jnp.where(first, own, other), jnp.where(first, other, own)], axis=0
        )
    hidden_ref[...] = hidden
    normed = norm_rows(hidden.astype(F32), gain_ref[...])
    normed_ref[...] = normed
    queries = jnp.dot(normed, wq_ref[...], preferred_element_type=F32)
    if chunks * LANES > width:
        pad = jnp.zeros((requests, chunks * LANES - width), F32)
        queries = jnp.concatenate([queries, pad], axis=1)
    cosine, sine = tables_ref[0], tables_ref[1]
    zeros = jnp.zeros((requests, LANES), F32)
    nothing = jnp.zeros((inbox, LANES), F32)
    for j in range(SLOT):
        here = pl.ds(j, requests, stride=SLOT)
        there = pl.ds(j, inbox, stride=SLOT)
        if j < chunks:
            chunk = rotate(queries[:, j * LANES : (j + 1) * LANES], cosine, sine)
            chunk = (chunk.astype(BF16).astype(F32) * ATTN_SCALE).astype(BF16)
            packs[here, :] = chunk.astype(F32)
            sends[there, :] = jnp.dot(away_ref[...], chunk, preferred_element_type=F32)
        else:
            packs[here, :] = zeros
            sends[there, :] = span_ref[...] if j == META else nothing
    packed_ref[...] = packs[...]
    send_ref[...] = sends[...].astype(BF16)


def unpack(packed):
    low = iota(packed.shape, 1) < HEAD_DIM
    even = jnp.where(low, packed, 0.0)
    odd = jnp.where(low, pltpu.roll(packed, HEAD_DIM, 1), 0.0)
    return jnp.concatenate([even, odd], axis=0)


def head_rows(heads):
    return [(h // 2) + SLOT * (h % 2) for h in range(heads)]


def token_of_column(heads, kv_local, columns):
    row = iota((ROWS, columns), 0)
    column = iota((ROWS, columns), 1)
    wanted = jnp.full((ROWS, columns), kv_local, jnp.int32)
    for h, place in enumerate(head_rows(heads)):
        wanted = jnp.where(row == place, h // (heads // kv_local), wanted)
    return jnp.where(column % kv_local == wanted, column // kv_local, 1 << 20)


def score_page(query, block):
    return lax.dot_general(query, block, NT, preferred_element_type=F32)


def weigh_page(scores, tokens, span):
    scores = jnp.where(tokens < span, scores, NEG_FILL)
    top = jnp.max(scores, axis=1, keepdims=True)
    weights = jnp.exp(scores - top)
    return top, jnp.sum(weights, axis=1, keepdims=True), weights.astype(BF16)


def attend_pages(
    stages, copies, query_of, block_of, span_of, tokens, keep, last=None
):
    def score_stage(i):
        if copies is not None:
            copies[i].wait()
        if last is not None and i == len(stages) - 1:
            last.wait()
        return {p: score_page(query_of(p), block_of(p)) for p in stages[i]}

    scores = score_stage(0)
    for i, pages in enumerate(stages):
        if i + 1 < len(stages):
            ahead = score_stage(i + 1)
        weighed = {p: weigh_page(scores[p], tokens, span_of(p)) for p in pages}
        outs = {
            p: jnp.dot(weighed[p][2], block_of(p), preferred_element_type=F32)
            for p in pages
        }
        for p in pages:
            keep(p, weighed[p][0], weighed[p][1], outs[p])
        if i + 1 < len(stages):
            scores = ahead


def attend_pairs(stages, copies, query_of, block_of, span_of, tokens, keep, last):
    columns = tokens.shape[1]
    low = iota((columns, LANES), 1) < HEAD_DIM

    def score_stage(i):
        copies[i].wait()
        if i == len(stages) - 1:
            last.wait()
        scores, values = {}, {}
        for p in stages[i][::2]:
            one, two = block_of(p), block_of(p + 1)
            keys = jnp.where(low, one, pltpu.roll(two, HEAD_DIM, 1))
            values[p] = jnp.where(low, pltpu.roll(one, HEAD_DIM, 1), two)
            query = jnp.concatenate(
                [query_of(p), pltpu.roll(query_of(p + 1), HEAD_DIM, 1)], axis=0
            )
            scores[p] = score_page(query.astype(BF16), keys)
        return scores, values

    ahead = score_stage(0)
    for i, pages in enumerate(stages):
        scores, values = ahead
        if i + 1 < len(stages):
            ahead = score_stage(i + 1)
        for p in pages[::2]:
            one = weigh_page(scores[p][:ROWS], tokens, span_of(p))
            two = weigh_page(scores[p][ROWS:], tokens, span_of(p + 1))
            weights = jnp.concatenate([one[2], two[2]], axis=0)
            outs = jnp.dot(weights, values[p], preferred_element_type=F32)
            keep(p, one[0], one[1], pltpu.roll(outs[:ROWS], HEAD_DIM, 1))
            keep(p + 1, two[0], two[1], outs[ROWS:])


def spread_queries(target, packed):
    low = iota(packed.shape, 2) < HEAD_DIM
    target[:, 0:SLOT, :] = jnp.where(low, packed, 0.0)
    target[:, SLOT:ROWS, :] = jnp.where(low, pltpu.roll(packed, HEAD_DIM, 2), 0.0)


def merge_pages(places, top_of, sum_of, top, acc, scaled, start, before):
    requests = start.shape[0]
    for p, place in enumerate(places):
        top[place] = jnp.maximum(top[place], top_of(p))
    acc[0:requests] = start * jnp.exp(before - top[0:requests])
    for p, place in enumerate(places):
        scaled[p] = sum_of(p) * jnp.exp(top_of(p) - top[place])
    for p, place in enumerate(places):
        acc[place] = acc[place] + scaled[p]


def project_heads(values, weights_ref, heads):
    if heads == 1:
        return jnp.dot(values, weights_ref[...], preferred_element_type=F32)
    rows, depth = values.shape
    wide = 1024
    part = wide // heads
    repeat = iota((part, wide), 1) // heads == iota((part, wide), 0)
    repeat = jnp.where(repeat, 1.0, 0.0).astype(BF16)
    parts = [values[:, i : i + part] for i in range(0, depth, part)]
    spread = jnp.dot(
        jnp.concatenate(parts, axis=0), repeat, preferred_element_type=F32
    ).astype(BF16)
    lane = iota((1, wide), 1) % heads
    masks = [jnp.where(lane == k, 1.0, 0.0).astype(BF16) for k in range(heads)]
    total = jnp.zeros((heads * rows, LANES), F32)
    for i in range(len(parts)):
        piece = spread[i * rows : (i + 1) * rows]
        piece = jnp.concatenate([piece * mask for mask in masks], axis=0)
        total += jnp.dot(
            piece, weights_ref[i * wide : (i + 1) * wide, :], preferred_element_type=F32
        )
    return total


def local_kernel(
    heads, kv_local, meta_hbm, packed_hbm, normed_hbm, wkv_hbm, tables_hbm, cache_hbm,
    state_hbm,
    meta, packed, normed, raw, tables, pages, queries, fresh, tops, sums, top, acc,
    scaled, sems,
):
    requests = normed.shape[0]
    count, columns, _ = pages.shape
    small = [
        copy_of(meta_hbm, meta, sems.at[0]),
        copy_of(packed_hbm, packed, sems.at[1]),
        copy_of(normed_hbm, normed, sems.at[2]),
        copy_of(tables_hbm, tables, sems.at[3]),
    ]
    weights = copy_of(wkv_hbm, raw, sems.at[4])
    assert count % 2 == 0
    stages = page_stages(count, 4, 12)
    paging = page_copies(cache_hbm, pages, stages, sems, 10)
    for copy in small + paging + [weights]:
        copy.start()
    tokens = token_of_column(heads, kv_local, columns)
    lower = iota((ROWS, LANES), 1) < HEAD_DIM
    low = iota((requests, LANES), 1) < HEAD_DIM
    low16 = iota((requests, ROWS, LANES), 2) < HEAD_DIM
    top[...] = jnp.full(top.shape, NEG_FILL, F32)
    acc[...] = jnp.zeros(acc.shape, F32)
    for copy in small:
        copy.wait()
    spread_queries(queries, packed[...].reshape(requests, SLOT, LANES))

    def place_of(p):
        owner = meta[0, p]
        return jnp.where(owner < 0, requests, owner)

    places = [place_of(p) for p in range(count)]

    def keep(p, page_top, total, out):
        tops[p] = jnp.broadcast_to(page_top, (ROWS, LANES))
        sums[p] = jnp.where(lower, total, out)
        top[places[p]] = jnp.maximum(top[places[p]], tops[p])

    attend_pairs(
        stages,
        paging,
        lambda p: queries[jnp.maximum(meta[0, p], 0)],
        lambda p: pages[p],
        lambda p: meta[1, p],
        tokens,
        keep,
        weights,
    )
    cosine = jnp.where(low, tables[0], 1.0)
    sine = jnp.where(low, tables[1], 0.0)
    projected = project_heads(normed[...], raw, kv_local)
    new = [
        rotate(projected[k * requests : (k + 1) * requests], cosine, sine)
        .astype(BF16)
        .astype(F32)
        for k in range(kv_local)
    ]
    used = {place: h for h, place in enumerate(head_rows(heads))}
    for place in range(ROWS):
        value = jnp.zeros((requests, LANES), F32)
        if place in used:
            value = new[used[place] // (heads // kv_local)]
        fresh[pl.ds(place, requests, stride=ROWS), :] = value
    for p, place in enumerate(places):
        scaled[p] = sums[p] * jnp.exp(tops[p] - top[place])
    for p, place in enumerate(places):
        acc[place] = acc[place] + scaled[p]
    added = fresh[...].reshape(requests, ROWS, LANES)
    score = jnp.sum(queries[...] * added, axis=2, keepdims=True)
    score = jnp.broadcast_to(score, added.shape)
    parked = []
    step = requests // 4
    for i in range(4):
        rows = slice(i * step, (i + 1) * step)
        before, fresh_score = top[rows], score[rows]
        highest = jnp.maximum(before, fresh_score)
        whole = acc[rows] * jnp.exp(before - highest)
        whole += jnp.where(low16[rows], 1.0, added[rows]) * jnp.exp(fresh_score - highest)
        acc[rows] = jnp.where(
            low16[rows], highest + jnp.log(whole), whole / pltpu.roll(whole, HEAD_DIM, 2)
        )
        part = pl.ds(i * step, step)
        parked.append(copy_of(acc.at[part], state_hbm.at[part], sems.at[5 + i]))
        parked[i].start()
    for copy in parked:
        copy.wait()


def lent_kernel(
    heads, kv_local, asked_ref, pages, pick_ref, drop_ref, meta_ref, packed_ref,
    normed_ref, tables_ref, hidden_ref,
    reply_hbm, meta_hbm, packed_hbm, normed_hbm, tables_hbm, hidden_hbm,
    reply16, sems,
):
    outgoing, columns, _ = pages.shape
    parked = [
        copy_of(packed_ref, packed_hbm, sems.at[0]),
        copy_of(normed_ref, normed_hbm, sems.at[1]),
        copy_of(hidden_ref, hidden_hbm, sems.at[2]),
        copy_of(tables_ref, tables_hbm, sems.at[3]),
        copy_of(meta_ref, meta_hbm, sems.at[4]),
    ]
    for copy in parked:
        copy.start()
    slot_rows = asked_ref.shape[0]
    shape = (outgoing * SLOT, slot_rows)
    chosen = jnp.where(pick_ref[:, 0:1] == iota(shape, 1), 1.0, 0.0).astype(BF16)
    asked = jnp.dot(chosen, asked_ref[...], preferred_element_type=F32)
    tokens = token_of_column(heads, kv_local, columns).astype(F32)
    low = iota((SLOT, LANES), 1) < HEAD_DIM
    lane = iota((SLOT, LANES), 1)
    row = iota((SLOT, LANES), 0)

    def terms(total, offset):
        leading = total.astype(BF16).astype(F32)
        rest = total - leading
        second = rest.astype(BF16).astype(F32)
        third = rest - second
        spot = lane - offset - 3 * row
        placed = jnp.where(spot == 0, leading, 0.0)
        placed = jnp.where(spot == 1, second, placed)
        return jnp.where(spot == 2, third, placed)

    packed = [asked[j * SLOT : (j + 1) * SLOT] for j in range(outgoing)]
    replies = {}

    def keep(j, top, total, out):
        out = out / total
        logs = top + jnp.log(total)
        even = pltpu.roll(out[0:SLOT], HEAD_DIM, 1)
        both = jnp.where(low, even, out[SLOT:ROWS])
        line = jnp.sum(
            terms(logs[0:SLOT], 0) + terms(logs[SLOT:ROWS], HEAD_DIM), axis=0, keepdims=True
        )
        replies[j] = jnp.where(row == META, line, both)

    attend_pages(
        page_stages(outgoing, 8, 8),
        None,
        lambda j: unpack(packed[j]).astype(BF16),
        lambda j: pages[j],
        lambda j: packed[j][META : META + 1, 0:1],
        tokens,
        keep,
    )
    shape = (slot_rows, outgoing * SLOT)
    placed = jnp.where(drop_ref[0:1, :] == iota(shape, 0), 1.0, 0.0).astype(BF16)
    every = jnp.concatenate([replies[j] for j in range(outgoing)], axis=0).astype(BF16)
    reply = jnp.dot(placed, every, preferred_element_type=F32)
    reply16[...] = reply.astype(BF16)
    replying = copy_of(reply16, reply_hbm, sems.at[5])
    replying.start()
    for copy in parked + [replying]:
        copy.wait()


def combine_kernel(
    heads, pool, meta_hbm, state_hbm, wo_hbm, hidden_hbm, gain_hbm, router_hbm,
    routes_hbm, wd_hbm, reply_ref,
    part_ref, meta_ref, hidden_ref, gain_ref, router_ref, routes_ref, wd_ref,
    meta, state, wo, gain, tops, accs, scaled, reply, finals, sems,
):
    requests = state.shape[0]
    inbox = reply_ref.shape[0] // SLOT
    chunks = -(-heads // 2)
    numbers = copy_of(meta_hbm, meta, sems.at[11])
    arriving = copy_of(state_hbm, state, sems.at[0])
    weights = copies_of(wo_hbm, wo, sems, 1)
    gaining = copy_of(gain_hbm, gain, sems.at[5])
    later = [
        copy_of(meta_hbm, meta_ref, sems.at[6]),
        copy_of(hidden_hbm, hidden_ref, sems.at[7]),
        copy_of(router_hbm, router_ref, sems.at[8]),
        copy_of(routes_hbm, routes_ref, sems.at[9]),
        copy_of(wd_hbm.at[pl.ds(0, wd_ref.shape[0])], wd_ref, sems.at[10]),
    ]
    for copy in [numbers, arriving] + weights + [gaining] + later:
        copy.start()
    reply[...] = reply_ref[...].astype(F32)
    tops[...] = jnp.full(tops.shape, NEG_FILL, F32)
    accs[...] = jnp.zeros(accs.shape, F32)
    low = iota((SLOT, LANES), 1) < HEAD_DIM
    lane = iota((SLOT, LANES), 1)
    row = iota((SLOT, LANES), 0)
    mine = (lane % HEAD_DIM) // 3 == row

    def place_of(s):
        lender = s // CAP ^ (inbox // CAP // 2)
        owner = meta[0, pool + lender * CAP + s % CAP]
        return jnp.where(owner < 0, requests, owner)

    def logs_of(s):
        line = reply[s * SLOT + META : s * SLOT + META + 1, :]
        line = jnp.where(mine, jnp.broadcast_to(line, (SLOT, LANES)), 0.0)
        even = jnp.sum(jnp.where(low, line, 0.0), axis=1, keepdims=True)
        odd = jnp.sum(jnp.where(low, 0.0, line), axis=1, keepdims=True)
        logs = jnp.concatenate([even, odd], axis=0)
        return jnp.broadcast_to(logs, (ROWS, LANES))

    def sum_of(s):
        packed = reply[s * SLOT : (s + 1) * SLOT, :]
        even = jnp.where(low, 1.0, pltpu.roll(packed, HEAD_DIM, 1))
        odd = jnp.where(low, 1.0, packed)
        return jnp.concatenate([even, odd], axis=0)

    logs = [logs_of(s) for s in range(inbox)]
    numbers.wait()
    places = [place_of(s) for s in range(inbox)]
    for s, place in enumerate(places):
        tops[place] = jnp.maximum(tops[place], logs[s])
    for s, place in enumerate(places):
        scaled[s] = sum_of(s) * jnp.exp(logs[s] - tops[place])
    for s, place in enumerate(places):
        accs[place] = accs[place] + scaled[s]
    arriving.wait()
    low16 = iota(state.shape, 2) < HEAD_DIM
    start = state[...]
    before = jnp.where(low16, start, pltpu.roll(start, HEAD_DIM, 2))
    remote = tops[0:requests]
    highest = jnp.maximum(before, remote)
    whole = accs[0:requests] * jnp.exp(remote - highest)
    whole = whole + jnp.where(low16, 1.0, start) * jnp.exp(before - highest)
    finals[...] = (whole / pltpu.roll(whole, HEAD_DIM, 2)).reshape(
        requests * ROWS, LANES
    )
    wide = iota((requests, LANES), 1) < HEAD_DIM
    parts = []
    for j in range(chunks):
        even = finals[pl.ds(j, requests, stride=ROWS), :]
        odd = finals[pl.ds(SLOT + j, requests, stride=ROWS), :]
        parts.append(jnp.where(wide, pltpu.roll(even, HEAD_DIM, 1), odd).astype(BF16))
    attention = jnp.concatenate(parts, axis=1)[:, : heads * HEAD_DIM]
    for copy in weights:
        copy.wait()
    part_ref[...] = jnp.dot(attention, wo[...], preferred_element_type=F32).astype(BF16)
    gaining.wait()
    gain_ref[...] = gain[...].reshape(1, gain.shape[0])
    for copy in later:
        copy.wait()


def load_kernel(wd_hbm, order_hbm, wd_ref, sem):
    del order_hbm
    rows = wd_ref.shape[0]
    copy = copy_of(wd_hbm.at[pl.ds(wd_hbm.shape[0] - rows, rows)], wd_ref, sem)
    copy.start()
    copy.wait()


def finish_kernel(attended_ref, own_ref, other_ref, attended_out, experts_out):
    attended_out[...] = attended_ref[...]
    experts_out[...] = (own_ref[...] + other_ref[...].astype(F32)).astype(BF16)


def own_rows(values, first):
    half = values.shape[0] // 2
    return jnp.where(first, values[:half], values[half:])


def residual_kernel(
    tp, count, meta_ref, hidden_ref, *refs,
):
    pieces = refs[:count]
    gain_ref, attended_ref, input_ref, again_ref = refs[count:]
    requests = hidden_ref.shape[0]
    if count == 2:
        summed = pieces[0][...].astype(F32) + pieces[1][...].astype(F32)
    else:
        summed = pieces[0][0:requests, :].astype(F32)
        for t in range(1, tp):
            part = pieces[0][t * requests : (t + 1) * requests, :]
            summed = summed + part.astype(F32)
    attended = (hidden_ref[...].astype(F32) + RESID_SCALE * summed).astype(BF16)
    if count == 2:
        attended_ref[...] = own_rows(attended, meta_ref[3:4, 0:1] == 0)
    else:
        attended_ref[...] = attended
    ffn_input = norm_rows(attended.astype(F32), gain_ref[...])
    input_ref[...] = ffn_input
    again_ref[...] = ffn_input


def gate_column(units, meta_ref, input_ref, router_ref, routes_ref):
    ffn_input = input_ref[...]
    requests = ffn_input.shape[0]
    logits = lax.dot_general(router_ref[...], ffn_input, NT, preferred_element_type=F32)
    expert = iota(logits.shape, 0)
    named = jnp.zeros(logits.shape, F32)
    for k in range(routes_ref.shape[0]):
        named = jnp.where(routes_ref[k : k + 1, :] == expert, 1.0, named)
    chosen = named > 0.5
    top = jnp.max(jnp.where(chosen, logits, NEG_FILL), axis=0, keepdims=True)
    weights = jnp.where(chosen, jnp.exp(logits - top), 0.0)
    total = jnp.sum(weights, axis=0, keepdims=True)
    mine = expert == meta_ref[3:4, 0:1] * units // FF
    line = jnp.sum(jnp.where(mine, weights, 0.0), axis=0, keepdims=True) / total
    diagonal = iota((requests, requests), 0) == iota((requests, requests), 1)
    line = jnp.where(diagonal, jnp.broadcast_to(line, (requests, requests)), 0.0)
    return jnp.sum(line, axis=1, keepdims=True)


def expert_kernel(
    units, meta_ref, lifted_ref, input_ref, router_ref, routes_ref, wd_ref, wd_rest_ref,
    *outs
):
    column = gate_column(units, meta_ref, input_ref, router_ref, routes_ref)
    gate = lifted_ref[0]
    active = gate / (1.0 + jnp.exp(-gate)) * lifted_ref[1]
    active = active.astype(BF16)
    half = wd_ref.shape[0]
    share = jnp.dot(active[:, :half], wd_ref[...], preferred_element_type=F32)
    share += jnp.dot(active[:, half:], wd_rest_ref[...], preferred_element_type=F32)
    share *= column
    if len(outs) == 2:
        first = meta_ref[3:4, 0:1] == 0
        outs[0][...] = own_rows(share, first)
        outs[1][...] = own_rows(share, jnp.logical_not(first)).astype(BF16)
    else:
        outs[0][...] = share.astype(BF16)


def call(body, outs, in_specs, scratch=(), limit=16, flops=0, moved=0):
    return pl.pallas_call(
        body,
        out_shape=outs,
        in_specs=in_specs,
        out_specs=[VMEM if isinstance(o, jax.ShapeDtypeStruct) else HBM for o in outs],
        scratch_shapes=list(scratch),
        compiler_params=pltpu.CompilerParams(vmem_limit_bytes=limit << 20),
        cost_estimate=pl.CostEstimate(
            flops=flops, bytes_accessed=moved, transcendentals=0
        ),
    )


def swap(values):
    return lax.ppermute(values, "tensor", [(0, 1), (1, 0)])


def on_device(
    hidden,
    attn_gain,
    w_query,
    w_keyvalue,
    w_output,
    cache,
    page_table,
    ctx_len,
    move_dest,
    ffn_gain,
    router,
    routes,
    w_in,
    w_down,
):
    replicas = lax.axis_size("replica")
    tp = lax.axis_size("tensor")
    rank = lax.axis_index("tensor").astype(jnp.int32)
    rows, width = hidden.shape
    pool, page_len, kv_local, _ = cache.shape
    outgoing = move_dest.shape[0]
    local_pages = pool - outgoing
    requests = page_table.shape[0]
    heads = w_query.shape[1] // HEAD_DIM
    inbox = replicas * CAP
    units = w_down.shape[0]
    assert FF % units == 0
    columns = page_len * kv_local
    entries = -(-(pool + inbox) // LANES) * LANES
    struct = jax.ShapeDtypeStruct
    pair = tp == 2
    ids = rank.reshape(1)

    def pin(values):
        return pltpu.with_memory_space_constraint(values, pltpu.HBM)

    def exchange(blocks, order):
        blocks = blocks.reshape(replicas, CAP * SLOT, LANES)
        blocks = lax.all_to_all(
            blocks,
            "replica",
            split_axis=0,
            concat_axis=0,
            tiled=True,
            axis_index_groups=[list(order)],
        )
        return blocks.reshape(inbox * SLOT, LANES)

    blocks = pin(cache.reshape(pool, columns, LANES))
    if pair:
        pieces = [hidden, swap(hidden)]
    else:
        pieces = [lax.all_gather(hidden, "tensor", axis=0, tiled=True)]
    meta_shape = (4, entries)
    tables_shape = (2, requests, LANES)
    own, wq, gain, tables, away, away_span, meta, lent, pick, drop = call(
        functools.partial(prepare_kernel, pool, replicas),
        [
            struct(hidden.shape, BF16),
            struct(w_query.shape, BF16),
            struct((1, width), F32),
            struct(tables_shape, F32),
            struct((inbox, requests), BF16),
            struct((inbox, LANES), F32),
            struct(meta_shape, jnp.int32),
            struct((outgoing, columns, LANES), BF16),
            struct((outgoing * SLOT, LANES), jnp.int32),
            struct((outgoing, outgoing * SLOT), jnp.int32),
        ],
        [SMEM] + [HBM] * 7,
        [
            pltpu.VMEM((1, requests), jnp.int32),
            pltpu.VMEM((page_table.shape[1], requests), jnp.int32),
            pltpu.VMEM((1, outgoing), jnp.int32),
            pltpu.VMEM((width,), F32),
            pltpu.SemaphoreType.DMA((10,)),
        ],
        moved=2 * w_query.size,
    )(
        ids,
        pin(hidden),
        pin(ctx_len.reshape(1, requests)),
        pin(page_table.T),
        pin(move_dest.reshape(1, outgoing)),
        pin(attn_gain),
        pin(w_query),
        blocks,
    )
    if pair:
        pieces[0] = own
    hidden_all, normed, packed, sends = call(
        functools.partial(query_kernel, len(pieces)),
        [
            struct((requests, width), BF16),
            struct((requests, width), BF16),
            struct((requests * SLOT, LANES), F32),
            struct((inbox * SLOT, LANES), BF16),
        ],
        [VMEM] * (len(pieces) + 6),
        [
            pltpu.VMEM((requests * SLOT, LANES), F32),
            pltpu.VMEM((inbox * SLOT, LANES), F32),
        ],
        flops=4 * requests * width * w_query.shape[1],
        moved=2 * w_query.size,
    )(meta, *pieces, gain, wq, tables, away, away_span)
    asked = exchange(sends, range(replicas)[::-1])
    replies, meta_far, packed_far, normed_far, tables_far, hidden_far = call(
        functools.partial(lent_kernel, heads, kv_local),
        [
            pltpu.HBM((inbox * SLOT, LANES), BF16),
            pltpu.HBM(meta_shape, jnp.int32),
            pltpu.HBM((requests * SLOT, LANES), F32),
            pltpu.HBM((requests, width), BF16),
            pltpu.HBM(tables_shape, F32),
            pltpu.HBM((requests, width), BF16),
        ],
        [VMEM] * 9,
        [
            pltpu.VMEM((inbox * SLOT, LANES), BF16),
            pltpu.SemaphoreType.DMA((6,)),
        ],
        flops=4 * ROWS * columns * LANES * outgoing,
        moved=2 * columns * LANES * outgoing,
    )(asked, lent, pick, drop, meta, packed, normed, tables, hidden_all)
    returned = exchange(replies, [r ^ replicas // 2 for r in range(replicas)])
    (state,) = call(
        functools.partial(local_kernel, heads, kv_local),
        [pltpu.HBM((requests, ROWS, LANES), F32)],
        [HBM] * 6,
        [
            pltpu.SMEM(meta_shape, jnp.int32),
            pltpu.VMEM((requests * SLOT, LANES), F32),
            pltpu.VMEM((requests, width), BF16),
            pltpu.VMEM((width * kv_local, LANES), BF16),
            pltpu.VMEM(tables_shape, F32),
            pltpu.VMEM((local_pages, columns, LANES), BF16),
            pltpu.VMEM((requests, ROWS, LANES), F32),
            pltpu.VMEM((requests * ROWS, LANES), F32),
            pltpu.VMEM((local_pages, ROWS, LANES), F32),
            pltpu.VMEM((local_pages, ROWS, LANES), F32),
            pltpu.VMEM((requests + 1, ROWS, LANES), F32),
            pltpu.VMEM((requests + 1, ROWS, LANES), F32),
            pltpu.VMEM((local_pages, ROWS, LANES), F32),
            pltpu.SemaphoreType.DMA((10 + local_pages,)),
        ],
        limit=24,
        flops=4 * ROWS * columns * LANES * local_pages,
        moved=2 * columns * LANES * local_pages,
    )(
        pin(meta_far),
        pin(packed_far),
        pin(normed_far),
        pin(w_keyvalue.reshape(width * kv_local, LANES)),
        pin(tables_far),
        blocks,
    )
    half = struct((units // 2, width), BF16)
    part, meta, hidden_all, gain, router_t, routes_t, wd = call(
        functools.partial(combine_kernel, heads, pool),
        [
            struct((requests, width), BF16),
            struct(meta_shape, jnp.int32),
            struct((requests, width), BF16),
            struct((1, width), F32),
            struct(router.shape[::-1], BF16),
            struct(routes.shape[::-1], jnp.int32),
            half,
        ],
        [HBM] * 8 + [VMEM],
        [
            pltpu.SMEM(meta_shape, jnp.int32),
            pltpu.VMEM((requests, ROWS, LANES), F32),
            pltpu.VMEM(w_output.shape, BF16),
            pltpu.VMEM((width,), F32),
            pltpu.VMEM((requests + 1, ROWS, LANES), F32),
            pltpu.VMEM((requests + 1, ROWS, LANES), F32),
            pltpu.VMEM((inbox, ROWS, LANES), F32),
            pltpu.VMEM((inbox * SLOT, LANES), F32),
            pltpu.VMEM((requests * ROWS, LANES), F32),
            pltpu.SemaphoreType.DMA((12,)),
        ],
        flops=2 * requests * w_output.size,
        moved=2 * w_output.size,
    )(
        pin(meta_far), pin(state), pin(w_output), pin(hidden_far), pin(ffn_gain),
        pin(router.T), pin(routes.T), pin(w_down), returned,
    )
    if pair:
        parts = [part, swap(part)]
    else:
        parts = [lax.all_gather(part, "tensor", axis=0, tiled=True)]
    (wd_rest,) = call(
        load_kernel,
        [half],
        [HBM, ANY],
        [pltpu.SemaphoreType.DMA],
        moved=w_down.size,
    )(pin(w_down), part)
    attended, ffn_input, ffn_again = call(
        functools.partial(residual_kernel, tp, len(parts)),
        [
            struct((rows if pair else requests, width), BF16),
            struct((requests, width), BF16),
            struct((requests, width), BF16),
        ],
        [VMEM] * (len(parts) + 3),
        flops=2 * requests * width,
        moved=8 * requests * width,
    )(meta, hidden_all, *parts, gain)
    lifted = jnp.einsum("rd,dsu->sru", ffn_input, w_in, preferred_element_type=F32)
    shapes = [struct((requests, width), BF16)]
    if pair:
        shapes = [struct((rows, width), F32), struct((rows, width), BF16)]
    shares = call(
        functools.partial(expert_kernel, units),
        shapes,
        [VMEM] * 7,
        flops=2 * requests * w_down.size,
        moved=2 * w_down.size,
    )(meta, lifted, ffn_again, router_t, routes_t, wd, wd_rest)
    if pair:
        out = struct((rows, width), BF16)
        return tuple(
            call(finish_kernel, [out, out], [VMEM] * 3)(attended, shares[0], swap(shares[1]))
        )
    shares = lax.all_gather(shares[0], "tensor", axis=0)
    mine = lax.dynamic_slice_in_dim(shares, rank * rows, rows, axis=1)
    experts_out = jnp.sum(mine.astype(F32), axis=0).astype(BF16)
    attended = lax.dynamic_slice_in_dim(attended, rank * rows, rows, axis=0)
    return attended, experts_out


def solution(mesh):
    placed = (
        P(("replica", "tensor"), None),
        P(),
        P(None, "tensor"),
        P(None, "tensor", None),
        P("tensor", None),
        P("replica", None, "tensor", None),
        P("replica", None),
        P("replica"),
        P("replica"),
        P(),
        P(),
        P("replica", None),
        P(None, None, "tensor"),
        P("tensor", None),
    )
    return jax.shard_map(
        on_device,
        mesh=mesh,
        in_specs=placed,
        out_specs=(P(("replica", "tensor"), None), P(("replica", "tensor"), None)),
        check_vma=False,
    )
```

```python
import functools
import math

import jax
import jax.numpy as jnp
from jax import lax
from jax.experimental import pallas as pl
from jax.experimental.pallas import tpu as pltpu
from jax.sharding import PartitionSpec as P

HEAD_DIM = 64
EXPERTS = 40
FF = 512
CAP = 2
LANES = 128
SLOT = 8
ROWS = 16
META = 6

ATTN_SCALE = 0.015625
RESID_SCALE = 0.22
ROPE_BASE = 10000.0
EPSILON = 1e-06
NEG_FILL = -1e30

F32 = jnp.float32
BF16 = jnp.bfloat16
VMEM = pl.BlockSpec(memory_space=pltpu.VMEM)
SMEM = pl.BlockSpec(memory_space=pltpu.SMEM)
ANY = pl.BlockSpec(memory_space=pl.ANY)
HBM = pl.BlockSpec(memory_space=pltpu.HBM)
NT = (((1,), (1,)), ((), ()))


def iota(shape, axis):
    return lax.broadcasted_iota(jnp.int32, shape, axis)


def norm_rows(values, gain):
    factor = lax.rsqrt(jnp.mean(values * values, axis=-1, keepdims=True) + EPSILON)
    return (values * factor * gain).astype(BF16)


def rope_tables(ctx_row, requests):
    diagonal = iota((requests, requests), 0) == iota((requests, requests), 1)
    ctx = jnp.broadcast_to(ctx_row.astype(F32), (requests, requests))
    ctx = jnp.sum(jnp.where(diagonal, ctx, 0.0), axis=1, keepdims=True)
    lane = iota((requests, LANES), 1)
    index = (lane % (HEAD_DIM // 2)).astype(F32)
    inverse = jnp.exp(index * (-2.0 * math.log(ROPE_BASE) / HEAD_DIM))
    angles = ctx * inverse
    sign = jnp.where(lane % HEAD_DIM < HEAD_DIM // 2, -1.0, 1.0)
    return jnp.cos(angles), jnp.sin(angles) * sign


def rotate(chunk, cosine, sine):
    lane = iota(chunk.shape, 1)
    ahead = pltpu.roll(chunk, LANES - HEAD_DIM // 2, 1)
    behind = pltpu.roll(chunk, HEAD_DIM // 2, 1)
    turned = jnp.where(lane % HEAD_DIM < HEAD_DIM // 2, ahead, behind)
    return chunk * cosine + turned * sine


def copy_of(source, target, sem):
    return pltpu.make_async_copy(source, target, sem)


def copies_of(source, target, sems, base):
    step = source.shape[0] // 4
    return [
        copy_of(
            source.at[pl.ds(i * step, step)], target.at[pl.ds(i * step, step)], sems.at[base + i]
        )
        for i in range(4)
    ]


def page_copies(cache_hbm, pages, stages, sems, base):
    copies = []
    for i, stage in enumerate(stages):
        rows = pl.ds(stage[0], len(stage))
        copies.append(copy_of(cache_hbm.at[rows], pages.at[rows], sems.at[base + i]))
    return copies


def page_stages(count, first, rest):
    starts = [0] + list(range(min(first, count), count, rest))
    return [range(a, b) for a, b in zip(starts, starts[1:] + [count])]


def prepare_kernel(
    pool, replicas, ids_ref, hidden_hbm, ctx_hbm, table_hbm, dest_hbm, attn_gain_hbm,
    wq_hbm, cache_hbm,
    hidden_ref, wq_ref, gain_ref, tables_ref, away_ref, span_ref, meta_ref, lent_ref,
    pick_ref, drop_ref,
    ctx, table, dest, gain, sems,
):
    inbox = replicas * CAP
    requests = ctx.shape[1]
    entries = meta_ref.shape[1]
    small = [
        copy_of(ctx_hbm, ctx, sems.at[0]),
        copy_of(table_hbm, table, sems.at[1]),
        copy_of(dest_hbm, dest, sems.at[2]),
        copy_of(attn_gain_hbm, gain, sems.at[3]),
    ]
    large = [copy_of(hidden_hbm, hidden_ref, sems.at[4])]
    large += copies_of(wq_hbm, wq_ref, sems, 5)
    lending = pl.ds(pool - lent_ref.shape[0], lent_ref.shape[0])
    large.append(copy_of(cache_hbm.at[lending], lent_ref, sems.at[9]))
    for copy in small + large:
        copy.start()
    for copy in small:
        copy.wait()
    gain_ref[...] = gain[...].reshape(1, gain.shape[0])
    ctx_row = ctx[...]

    def claims(values):
        held = jnp.zeros(values.shape, F32)
        spans = jnp.zeros(values.shape, F32)
        for k in range(table.shape[0]):
            match = table[k : k + 1, :] == values
            filled = jnp.clip(ctx_row - k * 128, 0, 128).astype(F32)
            held = jnp.where(match, 1.0, held)
            spans = jnp.where(match, filled, spans)
        return held.astype(BF16), spans

    held, spans = claims(iota((entries, requests), 0))
    numbers = (iota((SLOT, requests), 1) + 1).astype(BF16)
    ones = jnp.ones((SLOT, requests), BF16)
    holder = lax.dot_general(numbers, held, NT, preferred_element_type=F32)
    covered = lax.dot_general(ones, spans.astype(BF16), NT, preferred_element_type=F32)
    meta_ref[0:1, :] = holder[0:1, :].astype(jnp.int32) - 1
    meta_ref[1:2, :] = covered[0:1, :].astype(jnp.int32)
    meta_ref[2:3, :] = jnp.zeros((1, entries), jnp.int32)
    lent = dest.shape[1]
    across = jnp.broadcast_to(dest[...].astype(F32), (lent, lent))
    row, lane = iota((lent, lent), 0), iota((lent, lent), 1)
    down = jnp.sum(jnp.where(row == lane, across, 0.0), axis=1, keepdims=True)
    same = across == down
    before = jnp.sum(jnp.where(same & (lane < row), 1.0, 0.0), axis=1, keepdims=True)
    column = (replicas - 1 - down) * CAP + before
    column = jnp.broadcast_to(column, (lent, LANES)).astype(BF16)
    before = jnp.sum(jnp.where(same & (row < lane), 1.0, 0.0), axis=0, keepdims=True)
    line = dest[...] ^ replicas // 2
    line = jnp.broadcast_to(line.astype(F32), (lent, lent))
    line = (line * CAP + before).astype(BF16)
    expand = iota((lent * SLOT, lent), 0) // SLOT == iota((lent * SLOT, lent), 1)
    expand = jnp.where(expand, 1.0, 0.0).astype(BF16)
    column = jnp.dot(expand, column, preferred_element_type=F32).astype(jnp.int32)
    pick_ref[...] = column * SLOT + iota(column.shape, 0) % SLOT
    line = lax.dot_general(line, expand, NT, preferred_element_type=F32).astype(jnp.int32)
    drop_ref[...] = line * SLOT + iota(line.shape, 1) % SLOT
    meta_ref[3:4, :] = jnp.full((1, entries), ids_ref[0], jnp.int32)
    cosine, sine = rope_tables(ctx_row, requests)
    tables_ref[0] = cosine
    tables_ref[1] = sine
    slot = iota((inbox, requests), 0)
    lender = replicas - 1 - slot // CAP
    held, spans = claims(pool + lender * CAP + slot % CAP)
    away_ref[...] = held
    away_span = jnp.sum(spans, axis=1, keepdims=True)
    span_ref[...] = jnp.broadcast_to(away_span, span_ref.shape)
    for copy in large:
        copy.wait()


def query_kernel(
    count, meta_ref, *refs,
):
    pieces = refs[:count]
    (gain_ref, wq_ref, tables_ref, away_ref, span_ref,
     hidden_ref, normed_ref, packed_ref, send_ref, packs, sends) = refs[count:]
    requests = hidden_ref.shape[0]
    inbox = span_ref.shape[0]
    width = wq_ref.shape[1]
    chunks = -(-width // LANES)
    if count == 1:
        hidden = pieces[0][...]
    else:
        own, other = pieces[0][...], pieces[1][...]
        first = meta_ref[3:4, 0:1] == 0
        hidden = jnp.concatenate(
            [jnp.where(first, own, other), jnp.where(first, other, own)], axis=0
        )
    hidden_ref[...] = hidden
    normed = norm_rows(hidden.astype(F32), gain_ref[...])
    normed_ref[...] = normed
    queries = jnp.dot(normed, wq_ref[...], preferred_element_type=F32)
    if chunks * LANES > width:
        pad = jnp.zeros((requests, chunks * LANES - width), F32)
        queries = jnp.concatenate([queries, pad], axis=1)
    cosine, sine = tables_ref[0], tables_ref[1]
    zeros = jnp.zeros((requests, LANES), F32)
    nothing = jnp.zeros((inbox, LANES), F32)
    for j in range(SLOT):
        here = pl.ds(j, requests, stride=SLOT)
        there = pl.ds(j, inbox, stride=SLOT)
        if j < chunks:
            chunk = rotate(queries[:, j * LANES : (j + 1) * LANES], cosine, sine)
            chunk = (chunk.astype(BF16).astype(F32) * ATTN_SCALE).astype(BF16)
            packs[here, :] = chunk.astype(F32)
            sends[there, :] = jnp.dot(away_ref[...], chunk, preferred_element_type=F32)
        else:
            packs[here, :] = zeros
            sends[there, :] = span_ref[...] if j == META else nothing
    packed_ref[...] = packs[...]
    send_ref[...] = sends[...].astype(BF16)


def unpack(packed):
    low = iota(packed.shape, 1) < HEAD_DIM
    even = jnp.where(low, packed, 0.0)
    odd = jnp.where(low, pltpu.roll(packed, HEAD_DIM, 1), 0.0)
    return jnp.concatenate([even, odd], axis=0)


def head_rows(heads):
    return [(h // 2) + SLOT * (h % 2) for h in range(heads)]


def token_of_column(heads, kv_local, columns):
    row = iota((ROWS, columns), 0)
    column = iota((ROWS, columns), 1)
    wanted = jnp.full((ROWS, columns), kv_local, jnp.int32)
    for h, place in enumerate(head_rows(heads)):
        wanted = jnp.where(row == place, h // (heads // kv_local), wanted)
    return jnp.where(column % kv_local == wanted, column // kv_local, 1 << 20)


def score_page(query, block):
    return lax.dot_general(query, block, NT, preferred_element_type=F32)


def weigh_page(scores, tokens, span):
    scores = jnp.where(tokens < span, scores, NEG_FILL)
    top = jnp.max(scores, axis=1, keepdims=True)
    weights = jnp.exp(scores - top)
    return top, jnp.sum(weights, axis=1, keepdims=True), weights.astype(BF16)


def attend_pages(
    stages, copies, query_of, block_of, span_of, tokens, keep, last=None
):
    def score_stage(i):
        if copies is not None:
            copies[i].wait()
        if last is not None and i == len(stages) - 1:
            last.wait()
        return {p: score_page(query_of(p), block_of(p)) for p in stages[i]}

    scores = score_stage(0)
    for i, pages in enumerate(stages):
        if i + 1 < len(stages):
            ahead = score_stage(i + 1)
        weighed = {p: weigh_page(scores[p], tokens, span_of(p)) for p in pages}
        outs = {
            p: jnp.dot(weighed[p][2], block_of(p), preferred_element_type=F32)
            for p in pages
        }
        for p in pages:
            keep(p, weighed[p][0], weighed[p][1], outs[p])
        if i + 1 < len(stages):
            scores = ahead


def spread_queries(target, packed):
    low = iota(packed.shape, 2) < HEAD_DIM
    target[:, 0:SLOT, :] = jnp.where(low, packed, 0.0)
    target[:, SLOT:ROWS, :] = jnp.where(low, pltpu.roll(packed, HEAD_DIM, 2), 0.0)


def merge_pages(places, top_of, sum_of, top, acc, scaled, start, before):
    requests = start.shape[0]
    for p, place in enumerate(places):
        top[place] = jnp.maximum(top[place], top_of(p))
    acc[0:requests] = start * jnp.exp(before - top[0:requests])
    for p, place in enumerate(places):
        scaled[p] = sum_of(p) * jnp.exp(top_of(p) - top[place])
    for p, place in enumerate(places):
        acc[place] = acc[place] + scaled[p]


def project_heads(values, weights_ref, heads):
    if heads == 1:
        return jnp.dot(values, weights_ref[...], preferred_element_type=F32)
    rows, depth = values.shape
    wide = 1024
    part = wide // heads
    repeat = iota((part, wide), 1) // heads == iota((part, wide), 0)
    repeat = jnp.where(repeat, 1.0, 0.0).astype(BF16)
    parts = [values[:, i : i + part] for i in range(0, depth, part)]
    spread = jnp.dot(
        jnp.concatenate(parts, axis=0), repeat, preferred_element_type=F32
    ).astype(BF16)
    lane = iota((1, wide), 1) % heads
    masks = [jnp.where(lane == k, 1.0, 0.0).astype(BF16) for k in range(heads)]
    total = jnp.zeros((heads * rows, LANES), F32)
    for i in range(len(parts)):
        piece = spread[i * rows : (i + 1) * rows]
        piece = jnp.concatenate([piece * mask for mask in masks], axis=0)
        total += jnp.dot(
            piece, weights_ref[i * wide : (i + 1) * wide, :], preferred_element_type=F32
        )
    return total


def local_kernel(
    heads, kv_local, meta_hbm, packed_hbm, normed_hbm, wkv_hbm, tables_hbm, cache_hbm,
    state_hbm,
    meta, packed, normed, raw, tables, pages, queries, fresh, tops, sums, top, acc,
    sems,
):
    requests = normed.shape[0]
    count, columns, _ = pages.shape
    small = [
        copy_of(meta_hbm, meta, sems.at[0]),
        copy_of(packed_hbm, packed, sems.at[1]),
        copy_of(normed_hbm, normed, sems.at[2]),
        copy_of(tables_hbm, tables, sems.at[3]),
    ]
    weights = copy_of(wkv_hbm, raw, sems.at[4])
    stage = next(n for n in (8, 5, 4, 2, 1) if count % n == 0)

    def paging(i):
        rows = pl.ds(i * stage, stage)
        return copy_of(cache_hbm.at[rows], pages.at[rows], sems.at[10 + i])

    for copy in small + [paging(i) for i in range(count // stage)] + [weights]:
        copy.start()
    tokens = token_of_column(heads, kv_local, columns)
    lower = iota((ROWS, LANES), 1) < HEAD_DIM
    low = iota((requests, LANES), 1) < HEAD_DIM
    low16 = iota((requests, ROWS, LANES), 2) < HEAD_DIM
    top[...] = jnp.full(top.shape, NEG_FILL, F32)
    acc[...] = jnp.zeros(acc.shape, F32)
    for copy in small:
        copy.wait()
    spread_queries(queries, packed[...].reshape(requests, SLOT, LANES))

    def place_of(p):
        owner = meta[0, p]
        return jnp.where(owner < 0, requests, owner)

    def work(i, carry):
        paging(i).wait()
        first = i * stage
        here = range(stage)
        asked = [
            queries[jnp.maximum(meta[0, first + u], 0)].astype(BF16) for u in here
        ]
        scores = [score_page(asked[u], pages[first + u]) for u in here]
        weighed = [weigh_page(scores[u], tokens, meta[1, first + u]) for u in here]
        outs = [
            jnp.dot(weighed[u][2], pages[first + u], preferred_element_type=F32)
            for u in here
        ]
        for u in here:
            tops[first + u] = jnp.broadcast_to(weighed[u][0], (ROWS, LANES))
            sums[first + u] = jnp.where(lower, weighed[u][1], outs[u])
        for u in here:
            place = place_of(first + u)
            page_top = jnp.broadcast_to(weighed[u][0], (ROWS, LANES))
            top[place] = jnp.maximum(top[place], page_top)
        return carry

    lax.fori_loop(0, count // stage, work, 0)
    weights.wait()
    cosine = jnp.where(low, tables[0], 1.0)
    sine = jnp.where(low, tables[1], 0.0)
    projected = project_heads(normed[...], raw, kv_local)
    new = [
        rotate(projected[k * requests : (k + 1) * requests], cosine, sine)
        .astype(BF16)
        .astype(F32)
        for k in range(kv_local)
    ]
    used = {place: h for h, place in enumerate(head_rows(heads))}
    for place in range(ROWS):
        value = jnp.zeros((requests, LANES), F32)
        if place in used:
            value = new[used[place] // (heads // kv_local)]
        fresh[pl.ds(place, requests, stride=ROWS), :] = value

    def merge(i, carry):
        here = [i * stage + u for u in range(stage)]
        places = [place_of(p) for p in here]
        parts = [
            sums[p] * jnp.exp(tops[p] - top[place]) for p, place in zip(here, places)
        ]
        for place, part in zip(places, parts):
            acc[place] = acc[place] + part
        return carry

    lax.fori_loop(0, count // stage, merge, 0)
    added = fresh[...].reshape(requests, ROWS, LANES)
    score = jnp.sum(queries[...] * added, axis=2, keepdims=True)
    score = jnp.broadcast_to(score, added.shape)
    parked = []
    step = requests // 4
    for i in range(4):
        rows = slice(i * step, (i + 1) * step)
        before, fresh_score = top[rows], score[rows]
        highest = jnp.maximum(before, fresh_score)
        whole = acc[rows] * jnp.exp(before - highest)
        whole += jnp.where(low16[rows], 1.0, added[rows]) * jnp.exp(fresh_score - highest)
        acc[rows] = jnp.where(
            low16[rows], highest + jnp.log(whole), whole / pltpu.roll(whole, HEAD_DIM, 2)
        )
        part = pl.ds(i * step, step)
        parked.append(copy_of(acc.at[part], state_hbm.at[part], sems.at[5 + i]))
        parked[i].start()
    for copy in parked:
        copy.wait()


def lent_kernel(
    heads, kv_local, asked_ref, pages, pick_ref, drop_ref, meta_ref, packed_ref,
    normed_ref, tables_ref, hidden_ref,
    reply_hbm, meta_hbm, packed_hbm, normed_hbm, tables_hbm, hidden_hbm,
    reply16, sems,
):
    outgoing, columns, _ = pages.shape
    parked = [
        copy_of(packed_ref, packed_hbm, sems.at[0]),
        copy_of(normed_ref, normed_hbm, sems.at[1]),
        copy_of(hidden_ref, hidden_hbm, sems.at[2]),
        copy_of(tables_ref, tables_hbm, sems.at[3]),
        copy_of(meta_ref, meta_hbm, sems.at[4]),
    ]
    for copy in parked:
        copy.start()
    slot_rows = asked_ref.shape[0]
    shape = (outgoing * SLOT, slot_rows)
    chosen = jnp.where(pick_ref[:, 0:1] == iota(shape, 1), 1.0, 0.0).astype(BF16)
    asked = jnp.dot(chosen, asked_ref[...], preferred_element_type=F32)
    tokens = token_of_column(heads, kv_local, columns).astype(F32)
    low = iota((SLOT, LANES), 1) < HEAD_DIM
    lane = iota((SLOT, LANES), 1)
    row = iota((SLOT, LANES), 0)

    def terms(total, offset):
        leading = total.astype(BF16).astype(F32)
        rest = total - leading
        second = rest.astype(BF16).astype(F32)
        third = rest - second
        spot = lane - offset - 3 * row
        placed = jnp.where(spot == 0, leading, 0.0)
        placed = jnp.where(spot == 1, second, placed)
        return jnp.where(spot == 2, third, placed)

    packed = [asked[j * SLOT : (j + 1) * SLOT] for j in range(outgoing)]
    replies = {}

    def keep(j, top, total, out):
        out = out / total
        logs = top + jnp.log(total)
        even = pltpu.roll(out[0:SLOT], HEAD_DIM, 1)
        both = jnp.where(low, even, out[SLOT:ROWS])
        line = jnp.sum(
            terms(logs[0:SLOT], 0) + terms(logs[SLOT:ROWS], HEAD_DIM), axis=0, keepdims=True
        )
        replies[j] = jnp.where(row == META, line, both)

    attend_pages(
        page_stages(outgoing, 8, 8),
        None,
        lambda j: unpack(packed[j]).astype(BF16),
        lambda j: pages[j],
        lambda j: packed[j][META : META + 1, 0:1],
        tokens,
        keep,
    )
    shape = (slot_rows, outgoing * SLOT)
    placed = jnp.where(drop_ref[0:1, :] == iota(shape, 0), 1.0, 0.0).astype(BF16)
    every = jnp.concatenate([replies[j] for j in range(outgoing)], axis=0).astype(BF16)
    reply = jnp.dot(placed, every, preferred_element_type=F32)
    reply16[...] = reply.astype(BF16)
    replying = copy_of(reply16, reply_hbm, sems.at[5])
    replying.start()
    for copy in parked + [replying]:
        copy.wait()


def combine_kernel(
    heads, pool, meta_hbm, state_hbm, wo_hbm, hidden_hbm, gain_hbm, router_hbm,
    routes_hbm, wd_hbm, reply_ref,
    part_ref, meta_ref, hidden_ref, gain_ref, router_ref, routes_ref, wd_ref,
    meta, state, wo, gain, tops, accs, scaled, reply, finals, sems,
):
    requests = state.shape[0]
    inbox = reply_ref.shape[0] // SLOT
    chunks = -(-heads // 2)
    numbers = copy_of(meta_hbm, meta, sems.at[11])
    arriving = copy_of(state_hbm, state, sems.at[0])
    weights = copies_of(wo_hbm, wo, sems, 1)
    gaining = copy_of(gain_hbm, gain, sems.at[5])
    later = [
        copy_of(meta_hbm, meta_ref, sems.at[6]),
        copy_of(hidden_hbm, hidden_ref, sems.at[7]),
        copy_of(router_hbm, router_ref, sems.at[8]),
        copy_of(routes_hbm, routes_ref, sems.at[9]),
        copy_of(wd_hbm.at[pl.ds(0, wd_ref.shape[0])], wd_ref, sems.at[10]),
    ]
    for copy in [numbers, arriving] + weights + [gaining] + later:
        copy.start()
    reply[...] = reply_ref[...].astype(F32)
    tops[...] = jnp.full(tops.shape, NEG_FILL, F32)
    accs[...] = jnp.zeros(accs.shape, F32)
    low = iota((SLOT, LANES), 1) < HEAD_DIM
    lane = iota((SLOT, LANES), 1)
    row = iota((SLOT, LANES), 0)
    mine = (lane % HEAD_DIM) // 3 == row

    def place_of(s):
        lender = s // CAP ^ (inbox // CAP // 2)
        owner = meta[0, pool + lender * CAP + s % CAP]
        return jnp.where(owner < 0, requests, owner)

    def logs_of(s):
        line = reply[s * SLOT + META : s * SLOT + META + 1, :]
        line = jnp.where(mine, jnp.broadcast_to(line, (SLOT, LANES)), 0.0)
        even = jnp.sum(jnp.where(low, line, 0.0), axis=1, keepdims=True)
        odd = jnp.sum(jnp.where(low, 0.0, line), axis=1, keepdims=True)
        logs = jnp.concatenate([even, odd], axis=0)
        return jnp.broadcast_to(logs, (ROWS, LANES))

    def sum_of(s):
        packed = reply[s * SLOT : (s + 1) * SLOT, :]
        even = jnp.where(low, 1.0, pltpu.roll(packed, HEAD_DIM, 1))
        odd = jnp.where(low, 1.0, packed)
        return jnp.concatenate([even, odd], axis=0)

    logs = [logs_of(s) for s in range(inbox)]
    numbers.wait()
    places = [place_of(s) for s in range(inbox)]
    for s, place in enumerate(places):
        tops[place] = jnp.maximum(tops[place], logs[s])
    for s, place in enumerate(places):
        scaled[s] = sum_of(s) * jnp.exp(logs[s] - tops[place])
    for s, place in enumerate(places):
        accs[place] = accs[place] + scaled[s]
    arriving.wait()
    low16 = iota(state.shape, 2) < HEAD_DIM
    start = state[...]
    before = jnp.where(low16, start, pltpu.roll(start, HEAD_DIM, 2))
    remote = tops[0:requests]
    highest = jnp.maximum(before, remote)
    whole = accs[0:requests] * jnp.exp(remote - highest)
    whole = whole + jnp.where(low16, 1.0, start) * jnp.exp(before - highest)
    finals[...] = (whole / pltpu.roll(whole, HEAD_DIM, 2)).reshape(
        requests * ROWS, LANES
    )
    wide = iota((requests, LANES), 1) < HEAD_DIM
    parts = []
    for j in range(chunks):
        even = finals[pl.ds(j, requests, stride=ROWS), :]
        odd = finals[pl.ds(SLOT + j, requests, stride=ROWS), :]
        parts.append(jnp.where(wide, pltpu.roll(even, HEAD_DIM, 1), odd).astype(BF16))
    attention = jnp.concatenate(parts, axis=1)[:, : heads * HEAD_DIM]
    for copy in weights:
        copy.wait()
    part_ref[...] = jnp.dot(attention, wo[...], preferred_element_type=F32).astype(BF16)
    gaining.wait()
    gain_ref[...] = gain[...].reshape(1, gain.shape[0])
    for copy in later:
        copy.wait()


def load_kernel(wd_hbm, order_hbm, wd_ref, sem):
    del order_hbm
    rows = wd_ref.shape[0]
    copy = copy_of(wd_hbm.at[pl.ds(wd_hbm.shape[0] - rows, rows)], wd_ref, sem)
    copy.start()
    copy.wait()


def finish_kernel(attended_ref, own_ref, other_ref, attended_out, experts_out):
    attended_out[...] = attended_ref[...]
    experts_out[...] = (own_ref[...] + other_ref[...].astype(F32)).astype(BF16)


def own_rows(values, first):
    half = values.shape[0] // 2
    return jnp.where(first, values[:half], values[half:])


def residual_kernel(
    tp, count, meta_ref, hidden_ref, *refs,
):
    pieces = refs[:count]
    gain_ref, attended_ref, input_ref, again_ref = refs[count:]
    requests = hidden_ref.shape[0]
    if count == 2:
        summed = pieces[0][...].astype(F32) + pieces[1][...].astype(F32)
    else:
        summed = pieces[0][0:requests, :].astype(F32)
        for t in range(1, tp):
            part = pieces[0][t * requests : (t + 1) * requests, :]
            summed = summed + part.astype(F32)
    attended = (hidden_ref[...].astype(F32) + RESID_SCALE * summed).astype(BF16)
    if count == 2:
        attended_ref[...] = own_rows(attended, meta_ref[3:4, 0:1] == 0)
    else:
        attended_ref[...] = attended
    ffn_input = norm_rows(attended.astype(F32), gain_ref[...])
    input_ref[...] = ffn_input
    again_ref[...] = ffn_input


def gate_column(units, meta_ref, input_ref, router_ref, routes_ref):
    ffn_input = input_ref[...]
    requests = ffn_input.shape[0]
    logits = lax.dot_general(router_ref[...], ffn_input, NT, preferred_element_type=F32)
    expert = iota(logits.shape, 0)
    named = jnp.zeros(logits.shape, F32)
    for k in range(routes_ref.shape[0]):
        named = jnp.where(routes_ref[k : k + 1, :] == expert, 1.0, named)
    chosen = named > 0.5
    top = jnp.max(jnp.where(chosen, logits, NEG_FILL), axis=0, keepdims=True)
    weights = jnp.where(chosen, jnp.exp(logits - top), 0.0)
    total = jnp.sum(weights, axis=0, keepdims=True)
    mine = expert == meta_ref[3:4, 0:1] * units // FF
    line = jnp.sum(jnp.where(mine, weights, 0.0), axis=0, keepdims=True) / total
    diagonal = iota((requests, requests), 0) == iota((requests, requests), 1)
    line = jnp.where(diagonal, jnp.broadcast_to(line, (requests, requests)), 0.0)
    return jnp.sum(line, axis=1, keepdims=True)


def expert_kernel(
    units, meta_ref, lifted_ref, input_ref, router_ref, routes_ref, wd_ref, wd_rest_ref,
    *outs
):
    column = gate_column(units, meta_ref, input_ref, router_ref, routes_ref)
    gate = lifted_ref[0]
    active = gate / (1.0 + jnp.exp(-gate)) * lifted_ref[1]
    active = active.astype(BF16)
    half = wd_ref.shape[0]
    share = jnp.dot(active[:, :half], wd_ref[...], preferred_element_type=F32)
    share += jnp.dot(active[:, half:], wd_rest_ref[...], preferred_element_type=F32)
    share *= column
    if len(outs) == 2:
        first = meta_ref[3:4, 0:1] == 0
        outs[0][...] = own_rows(share, first)
        outs[1][...] = own_rows(share, jnp.logical_not(first)).astype(BF16)
    else:
        outs[0][...] = share.astype(BF16)


def call(body, outs, in_specs, scratch=(), limit=16, flops=0, moved=0):
    return pl.pallas_call(
        body,
        out_shape=outs,
        in_specs=in_specs,
        out_specs=[VMEM if isinstance(o, jax.ShapeDtypeStruct) else HBM for o in outs],
        scratch_shapes=list(scratch),
        compiler_params=pltpu.CompilerParams(vmem_limit_bytes=limit << 20),
        cost_estimate=pl.CostEstimate(
            flops=flops, bytes_accessed=moved, transcendentals=0
        ),
    )


def swap(values):
    return lax.ppermute(values, "tensor", [(0, 1), (1, 0)])


def on_device(
    hidden,
    attn_gain,
    w_query,
    w_keyvalue,
    w_output,
    cache,
    page_table,
    ctx_len,
    move_dest,
    ffn_gain,
    router,
    routes,
    w_in,
    w_down,
):
    replicas = lax.axis_size("replica")
    tp = lax.axis_size("tensor")
    rank = lax.axis_index("tensor").astype(jnp.int32)
    rows, width = hidden.shape
    pool, page_len, kv_local, _ = cache.shape
    outgoing = move_dest.shape[0]
    local_pages = pool - outgoing
    requests = page_table.shape[0]
    heads = w_query.shape[1] // HEAD_DIM
    inbox = replicas * CAP
    units = w_down.shape[0]
    assert FF % units == 0
    columns = page_len * kv_local
    entries = -(-(pool + inbox) // LANES) * LANES
    struct = jax.ShapeDtypeStruct
    pair = tp == 2
    ids = rank.reshape(1)

    def pin(values):
        return pltpu.with_memory_space_constraint(values, pltpu.HBM)

    def exchange(blocks, order):
        blocks = blocks.reshape(replicas, CAP * SLOT, LANES)
        blocks = lax.all_to_all(
            blocks,
            "replica",
            split_axis=0,
            concat_axis=0,
            tiled=True,
            axis_index_groups=[list(order)],
        )
        return blocks.reshape(inbox * SLOT, LANES)

    blocks = pin(cache.reshape(pool, columns, LANES))
    if pair:
        pieces = [hidden, swap(hidden)]
    else:
        pieces = [lax.all_gather(hidden, "tensor", axis=0, tiled=True)]
    meta_shape = (4, entries)
    tables_shape = (2, requests, LANES)
    own, wq, gain, tables, away, away_span, meta, lent, pick, drop = call(
        functools.partial(prepare_kernel, pool, replicas),
        [
            struct(hidden.shape, BF16),
            struct(w_query.shape, BF16),
            struct((1, width), F32),
            struct(tables_shape, F32),
            struct((inbox, requests), BF16),
            struct((inbox, LANES), F32),
            struct(meta_shape, jnp.int32),
            struct((outgoing, columns, LANES), BF16),
            struct((outgoing * SLOT, LANES), jnp.int32),
            struct((outgoing, outgoing * SLOT), jnp.int32),
        ],
        [SMEM] + [HBM] * 7,
        [
            pltpu.VMEM((1, requests), jnp.int32),
            pltpu.VMEM((page_table.shape[1], requests), jnp.int32),
            pltpu.VMEM((1, outgoing), jnp.int32),
            pltpu.VMEM((width,), F32),
            pltpu.SemaphoreType.DMA((10,)),
        ],
        moved=2 * w_query.size,
    )(
        ids,
        pin(hidden),
        pin(ctx_len.reshape(1, requests)),
        pin(page_table.T),
        pin(move_dest.reshape(1, outgoing)),
        pin(attn_gain),
        pin(w_query),
        blocks,
    )
    if pair:
        pieces[0] = own
    hidden_all, normed, packed, sends = call(
        functools.partial(query_kernel, len(pieces)),
        [
            struct((requests, width), BF16),
            struct((requests, width), BF16),
            struct((requests * SLOT, LANES), F32),
            struct((inbox * SLOT, LANES), BF16),
        ],
        [VMEM] * (len(pieces) + 6),
        [
            pltpu.VMEM((requests * SLOT, LANES), F32),
            pltpu.VMEM((inbox * SLOT, LANES), F32),
        ],
        flops=4 * requests * width * w_query.shape[1],
        moved=2 * w_query.size,
    )(meta, *pieces, gain, wq, tables, away, away_span)
    asked = exchange(sends, range(replicas)[::-1])
    replies, meta_far, packed_far, normed_far, tables_far, hidden_far = call(
        functools.partial(lent_kernel, heads, kv_local),
        [
            pltpu.HBM((inbox * SLOT, LANES), BF16),
            pltpu.HBM(meta_shape, jnp.int32),
            pltpu.HBM((requests * SLOT, LANES), F32),
            pltpu.HBM((requests, width), BF16),
            pltpu.HBM(tables_shape, F32),
            pltpu.HBM((requests, width), BF16),
        ],
        [VMEM] * 9,
        [
            pltpu.VMEM((inbox * SLOT, LANES), BF16),
            pltpu.SemaphoreType.DMA((6,)),
        ],
        flops=4 * ROWS * columns * LANES * outgoing,
        moved=2 * columns * LANES * outgoing,
    )(asked, lent, pick, drop, meta, packed, normed, tables, hidden_all)
    returned = exchange(replies, [r ^ replicas // 2 for r in range(replicas)])
    (state,) = call(
        functools.partial(local_kernel, heads, kv_local),
        [pltpu.HBM((requests, ROWS, LANES), F32)],
        [HBM] * 6,
        [
            pltpu.SMEM(meta_shape, jnp.int32),
            pltpu.VMEM((requests * SLOT, LANES), F32),
            pltpu.VMEM((requests, width), BF16),
            pltpu.VMEM((width * kv_local, LANES), BF16),
            pltpu.VMEM(tables_shape, F32),
            pltpu.VMEM((local_pages, columns, LANES), BF16),
            pltpu.VMEM((requests, ROWS, LANES), F32),
            pltpu.VMEM((requests * ROWS, LANES), F32),
            pltpu.VMEM((local_pages, ROWS, LANES), F32),
            pltpu.VMEM((local_pages, ROWS, LANES), F32),
            pltpu.VMEM((requests + 1, ROWS, LANES), F32),
            pltpu.VMEM((requests + 1, ROWS, LANES), F32),
            pltpu.SemaphoreType.DMA((10 + local_pages,)),
        ],
        limit=24,
        flops=4 * ROWS * columns * LANES * local_pages,
        moved=2 * columns * LANES * local_pages,
    )(
        pin(meta_far),
        pin(packed_far),
        pin(normed_far),
        pin(w_keyvalue.reshape(width * kv_local, LANES)),
        pin(tables_far),
        blocks,
    )
    half = struct((units // 2, width), BF16)
    part, meta, hidden_all, gain, router_t, routes_t, wd = call(
        functools.partial(combine_kernel, heads, pool),
        [
            struct((requests, width), BF16),
            struct(meta_shape, jnp.int32),
            struct((requests, width), BF16),
            struct((1, width), F32),
            struct(router.shape[::-1], BF16),
            struct(routes.shape[::-1], jnp.int32),
            half,
        ],
        [HBM] * 8 + [VMEM],
        [
            pltpu.SMEM(meta_shape, jnp.int32),
            pltpu.VMEM((requests, ROWS, LANES), F32),
            pltpu.VMEM(w_output.shape, BF16),
            pltpu.VMEM((width,), F32),
            pltpu.VMEM((requests + 1, ROWS, LANES), F32),
            pltpu.VMEM((requests + 1, ROWS, LANES), F32),
            pltpu.VMEM((inbox, ROWS, LANES), F32),
            pltpu.VMEM((inbox * SLOT, LANES), F32),
            pltpu.VMEM((requests * ROWS, LANES), F32),
            pltpu.SemaphoreType.DMA((12,)),
        ],
        flops=2 * requests * w_output.size,
        moved=2 * w_output.size,
    )(
        pin(meta_far), pin(state), pin(w_output), pin(hidden_far), pin(ffn_gain),
        pin(router.T), pin(routes.T), pin(w_down), returned,
    )
    if pair:
        parts = [part, swap(part)]
    else:
        parts = [lax.all_gather(part, "tensor", axis=0, tiled=True)]
    (wd_rest,) = call(
        load_kernel,
        [half],
        [HBM, ANY],
        [pltpu.SemaphoreType.DMA],
        moved=w_down.size,
    )(pin(w_down), part)
    attended, ffn_input, ffn_again = call(
        functools.partial(residual_kernel, tp, len(parts)),
        [
            struct((rows if pair else requests, width), BF16),
            struct((requests, width), BF16),
            struct((requests, width), BF16),
        ],
        [VMEM] * (len(parts) + 3),
        flops=2 * requests * width,
        moved=8 * requests * width,
    )(meta, hidden_all, *parts, gain)
    lifted = jnp.einsum("rd,dsu->sru", ffn_input, w_in, preferred_element_type=F32)
    shapes = [struct((requests, width), BF16)]
    if pair:
        shapes = [struct((rows, width), F32), struct((rows, width), BF16)]
    shares = call(
        functools.partial(expert_kernel, units),
        shapes,
        [VMEM] * 7,
        flops=2 * requests * w_down.size,
        moved=2 * w_down.size,
    )(meta, lifted, ffn_again, router_t, routes_t, wd, wd_rest)
    if pair:
        out = struct((rows, width), BF16)
        return tuple(
            call(finish_kernel, [out, out], [VMEM] * 3)(attended, shares[0], swap(shares[1]))
        )
    shares = lax.all_gather(shares[0], "tensor", axis=0)
    mine = lax.dynamic_slice_in_dim(shares, rank * rows, rows, axis=1)
    experts_out = jnp.sum(mine.astype(F32), axis=0).astype(BF16)
    attended = lax.dynamic_slice_in_dim(attended, rank * rows, rows, axis=0)
    return attended, experts_out


def solution(mesh):
    placed = (
        P(("replica", "tensor"), None),
        P(),
        P(None, "tensor"),
        P(None, "tensor", None),
        P("tensor", None),
        P("replica", None, "tensor", None),
        P("replica", None),
        P("replica"),
        P("replica"),
        P(),
        P(),
        P("replica", None),
        P(None, None, "tensor"),
        P("tensor", None),
    )
    return jax.shard_map(
        on_device,
        mesh=mesh,
        in_specs=placed,
        out_specs=(P(("replica", "tensor"), None), P(("replica", "tensor"), None)),
        check_vma=False,
    )
```

```python
import functools
import math

import jax
import jax.numpy as jnp
from jax import lax
from jax.experimental import pallas as pl
from jax.experimental.pallas import tpu as pltpu
from jax.sharding import PartitionSpec as P

HEAD_DIM = 64
EXPERTS = 40
FF = 512
CAP = 2
LANES = 128
SLOT = 8
ROWS = 16
META = 6

ATTN_SCALE = 0.015625
RESID_SCALE = 0.22
ROPE_BASE = 10000.0
EPSILON = 1e-06
NEG_FILL = -1e30

F32 = jnp.float32
BF16 = jnp.bfloat16
VMEM = pl.BlockSpec(memory_space=pltpu.VMEM)
SMEM = pl.BlockSpec(memory_space=pltpu.SMEM)
ANY = pl.BlockSpec(memory_space=pl.ANY)
HBM = pl.BlockSpec(memory_space=pltpu.HBM)
NT = (((1,), (1,)), ((), ()))


def iota(shape, axis):
    return lax.broadcasted_iota(jnp.int32, shape, axis)


def norm_rows(values, gain):
    factor = lax.rsqrt(jnp.mean(values * values, axis=-1, keepdims=True) + EPSILON)
    return (values * factor * gain).astype(BF16)


def rope_tables(ctx_row, requests):
    diagonal = iota((requests, requests), 0) == iota((requests, requests), 1)
    ctx = jnp.broadcast_to(ctx_row.astype(F32), (requests, requests))
    ctx = jnp.sum(jnp.where(diagonal, ctx, 0.0), axis=1, keepdims=True)
    lane = iota((requests, LANES), 1)
    index = (lane % (HEAD_DIM // 2)).astype(F32)
    inverse = jnp.exp(index * (-2.0 * math.log(ROPE_BASE) / HEAD_DIM))
    angles = ctx * inverse
    sign = jnp.where(lane % HEAD_DIM < HEAD_DIM // 2, -1.0, 1.0)
    return jnp.cos(angles), jnp.sin(angles) * sign


def rotate(chunk, cosine, sine):
    lane = iota(chunk.shape, 1)
    ahead = pltpu.roll(chunk, LANES - HEAD_DIM // 2, 1)
    behind = pltpu.roll(chunk, HEAD_DIM // 2, 1)
    turned = jnp.where(lane % HEAD_DIM < HEAD_DIM // 2, ahead, behind)
    return chunk * cosine + turned * sine


def copy_of(source, target, sem):
    return pltpu.make_async_copy(source, target, sem)


def copies_of(source, target, sems, base):
    step = source.shape[0] // 4
    return [
        copy_of(
            source.at[pl.ds(i * step, step)], target.at[pl.ds(i * step, step)], sems.at[base + i]
        )
        for i in range(4)
    ]


def page_copies(cache_hbm, pages, stages, sems, base):
    copies = []
    for i, stage in enumerate(stages):
        rows = pl.ds(stage[0], len(stage))
        copies.append(copy_of(cache_hbm.at[rows], pages.at[rows], sems.at[base + i]))
    return copies


def page_stages(count, first, rest):
    starts = [0] + list(range(min(first, count), count, rest))
    return [range(a, b) for a, b in zip(starts, starts[1:] + [count])]


def prepare_kernel(
    pool, replicas, ids_ref, hidden_hbm, ctx_hbm, table_hbm, dest_hbm, attn_gain_hbm,
    wq_hbm, cache_hbm,
    hidden_ref, wq_ref, gain_ref, tables_ref, away_ref, span_ref, meta_ref, lent_ref,
    pick_ref, drop_ref,
    ctx, table, dest, gain, sems,
):
    inbox = replicas * CAP
    requests = ctx.shape[1]
    entries = meta_ref.shape[1]
    small = [
        copy_of(ctx_hbm, ctx, sems.at[0]),
        copy_of(table_hbm, table, sems.at[1]),
        copy_of(dest_hbm, dest, sems.at[2]),
        copy_of(attn_gain_hbm, gain, sems.at[3]),
    ]
    large = [copy_of(hidden_hbm, hidden_ref, sems.at[4])]
    large += copies_of(wq_hbm, wq_ref, sems, 5)
    lending = pl.ds(pool - lent_ref.shape[0], lent_ref.shape[0])
    large.append(copy_of(cache_hbm.at[lending], lent_ref, sems.at[9]))
    for copy in small + large:
        copy.start()
    for copy in small:
        copy.wait()
    gain_ref[...] = gain[...].reshape(1, gain.shape[0])
    ctx_row = ctx[...]

    def claims(values):
        held = jnp.zeros(values.shape, F32)
        spans = jnp.zeros(values.shape, F32)
        for k in range(table.shape[0]):
            match = table[k : k + 1, :] == values
            filled = jnp.clip(ctx_row - k * 128, 0, 128).astype(F32)
            held = jnp.where(match, 1.0, held)
            spans = jnp.where(match, filled, spans)
        return held.astype(BF16), spans

    held, spans = claims(iota((entries, requests), 0))
    numbers = (iota((SLOT, requests), 1) + 1).astype(BF16)
    ones = jnp.ones((SLOT, requests), BF16)
    holder = lax.dot_general(numbers, held, NT, preferred_element_type=F32)
    covered = lax.dot_general(ones, spans.astype(BF16), NT, preferred_element_type=F32)
    meta_ref[0:1, :] = holder[0:1, :].astype(jnp.int32) - 1
    meta_ref[1:2, :] = covered[0:1, :].astype(jnp.int32)
    meta_ref[2:3, :] = jnp.zeros((1, entries), jnp.int32)
    lent = dest.shape[1]
    across = jnp.broadcast_to(dest[...].astype(F32), (lent, lent))
    row, lane = iota((lent, lent), 0), iota((lent, lent), 1)
    down = jnp.sum(jnp.where(row == lane, across, 0.0), axis=1, keepdims=True)
    same = across == down
    before = jnp.sum(jnp.where(same & (lane < row), 1.0, 0.0), axis=1, keepdims=True)
    column = (replicas - 1 - down) * CAP + before
    column = jnp.broadcast_to(column, (lent, LANES)).astype(BF16)
    before = jnp.sum(jnp.where(same & (row < lane), 1.0, 0.0), axis=0, keepdims=True)
    line = dest[...] ^ replicas // 2
    line = jnp.broadcast_to(line.astype(F32), (lent, lent))
    line = (line * CAP + before).astype(BF16)
    expand = iota((lent * SLOT, lent), 0) // SLOT == iota((lent * SLOT, lent), 1)
    expand = jnp.where(expand, 1.0, 0.0).astype(BF16)
    column = jnp.dot(expand, column, preferred_element_type=F32).astype(jnp.int32)
    pick_ref[...] = column * SLOT + iota(column.shape, 0) % SLOT
    line = lax.dot_general(line, expand, NT, preferred_element_type=F32).astype(jnp.int32)
    drop_ref[...] = line * SLOT + iota(line.shape, 1) % SLOT
    meta_ref[3:4, :] = jnp.full((1, entries), ids_ref[0], jnp.int32)
    cosine, sine = rope_tables(ctx_row, requests)
    tables_ref[0] = cosine
    tables_ref[1] = sine
    slot = iota((inbox, requests), 0)
    lender = replicas - 1 - slot // CAP
    held, spans = claims(pool + lender * CAP + slot % CAP)
    away_ref[...] = held
    away_span = jnp.sum(spans, axis=1, keepdims=True)
    span_ref[...] = jnp.broadcast_to(away_span, span_ref.shape)
    for copy in large:
        copy.wait()


def query_kernel(
    count, meta_ref, *refs,
):
    pieces = refs[:count]
    (gain_ref, wq_ref, tables_ref, away_ref, span_ref,
     hidden_ref, normed_ref, packed_ref, send_ref, packs, sends) = refs[count:]
    requests = hidden_ref.shape[0]
    inbox = span_ref.shape[0]
    width = wq_ref.shape[1]
    chunks = -(-width // LANES)
    if count == 1:
        hidden = pieces[0][...]
    else:
        own, other = pieces[0][...], pieces[1][...]
        first = meta_ref[3:4, 0:1] == 0
        hidden = jnp.concatenate(
            [jnp.where(first, own, other), jnp.where(first, other, own)], axis=0
        )
    hidden_ref[...] = hidden
    normed = norm_rows(hidden.astype(F32), gain_ref[...])
    normed_ref[...] = normed
    queries = jnp.dot(normed, wq_ref[...], preferred_element_type=F32)
    if chunks * LANES > width:
        pad = jnp.zeros((requests, chunks * LANES - width), F32)
        queries = jnp.concatenate([queries, pad], axis=1)
    cosine, sine = tables_ref[0], tables_ref[1]
    zeros = jnp.zeros((requests, LANES), F32)
    nothing = jnp.zeros((inbox, LANES), F32)
    for j in range(SLOT):
        here = pl.ds(j, requests, stride=SLOT)
        there = pl.ds(j, inbox, stride=SLOT)
        if j < chunks:
            chunk = rotate(queries[:, j * LANES : (j + 1) * LANES], cosine, sine)
            chunk = (chunk.astype(BF16).astype(F32) * ATTN_SCALE).astype(BF16)
            packs[here, :] = chunk.astype(F32)
            sends[there, :] = jnp.dot(away_ref[...], chunk, preferred_element_type=F32)
        else:
            packs[here, :] = zeros
            sends[there, :] = span_ref[...] if j == META else nothing
    packed_ref[...] = packs[...]
    send_ref[...] = sends[...].astype(BF16)


def unpack(packed):
    low = iota(packed.shape, 1) < HEAD_DIM
    even = jnp.where(low, packed, 0.0)
    odd = jnp.where(low, pltpu.roll(packed, HEAD_DIM, 1), 0.0)
    return jnp.concatenate([even, odd], axis=0)


def head_rows(heads):
    return [(h // 2) + SLOT * (h % 2) for h in range(heads)]


def token_of_column(heads, kv_local, columns):
    row = iota((ROWS, columns), 0)
    column = iota((ROWS, columns), 1)
    wanted = jnp.full((ROWS, columns), kv_local, jnp.int32)
    for h, place in enumerate(head_rows(heads)):
        wanted = jnp.where(row == place, h // (heads // kv_local), wanted)
    return jnp.where(column % kv_local == wanted, column // kv_local, 1 << 20)


def score_page(query, block):
    return lax.dot_general(query, block, NT, preferred_element_type=F32)


def weigh_page(scores, tokens, span):
    scores = jnp.where(tokens < span, scores, NEG_FILL)
    top = jnp.max(scores, axis=1, keepdims=True)
    weights = jnp.exp(scores - top)
    return top, jnp.sum(weights, axis=1, keepdims=True), weights.astype(BF16)


def attend_pages(
    stages, copies, query_of, block_of, span_of, tokens, keep, last=None
):
    def score_stage(i):
        if copies is not None:
            copies[i].wait()
        return {p: score_page(query_of(p), block_of(p)) for p in stages[i]}

    scores = score_stage(0)
    for i, pages in enumerate(stages):
        if i + 1 < len(stages):
            ahead = score_stage(i + 1)
        elif last is not None:
            last.wait()
        weighed = {p: weigh_page(scores[p], tokens, span_of(p)) for p in pages}
        outs = {
            p: jnp.dot(weighed[p][2], block_of(p), preferred_element_type=F32)
            for p in pages
        }
        for p in pages:
            keep(p, weighed[p][0], weighed[p][1], outs[p])
        if i + 1 < len(stages):
            scores = ahead


def spread_queries(target, packed):
    low = iota(packed.shape, 2) < HEAD_DIM
    target[:, 0:SLOT, :] = jnp.where(low, packed, 0.0)
    target[:, SLOT:ROWS, :] = jnp.where(low, pltpu.roll(packed, HEAD_DIM, 2), 0.0)


def merge_pages(places, top_of, sum_of, top, acc, scaled, start, before):
    requests = start.shape[0]
    for p, place in enumerate(places):
        top[place] = jnp.maximum(top[place], top_of(p))
    acc[0:requests] = start * jnp.exp(before - top[0:requests])
    for p, place in enumerate(places):
        scaled[p] = sum_of(p) * jnp.exp(top_of(p) - top[place])
    for p, place in enumerate(places):
        acc[place] = acc[place] + scaled[p]


def project_heads(values, weights_ref, heads):
    if heads == 1:
        return jnp.dot(values, weights_ref[...], preferred_element_type=F32)
    rows, depth = values.shape
    wide = 1024
    part = wide // heads
    repeat = iota((part, wide), 1) // heads == iota((part, wide), 0)
    repeat = jnp.where(repeat, 1.0, 0.0).astype(BF16)
    parts = [values[:, i : i + part] for i in range(0, depth, part)]
    spread = jnp.dot(
        jnp.concatenate(parts, axis=0), repeat, preferred_element_type=F32
    ).astype(BF16)
    lane = iota((1, wide), 1) % heads
    masks = [jnp.where(lane == k, 1.0, 0.0).astype(BF16) for k in range(heads)]
    total = jnp.zeros((heads * rows, LANES), F32)
    for i in range(len(parts)):
        piece = spread[i * rows : (i + 1) * rows]
        piece = jnp.concatenate([piece * mask for mask in masks], axis=0)
        total += jnp.dot(
            piece, weights_ref[i * wide : (i + 1) * wide, :], preferred_element_type=F32
        )
    return total


def local_kernel(
    heads, kv_local, meta_hbm, packed_hbm, normed_hbm, wkv_hbm, tables_hbm, cache_hbm,
    state_hbm,
    meta, packed, normed, raw, tables, pages, queries, fresh, tops, sums, top, acc,
    scaled, sems,
):
    requests = normed.shape[0]
    count, columns, _ = pages.shape
    small = [
        copy_of(meta_hbm, meta, sems.at[0]),
        copy_of(packed_hbm, packed, sems.at[1]),
        copy_of(normed_hbm, normed, sems.at[2]),
        copy_of(tables_hbm, tables, sems.at[3]),
    ]
    weights = copy_of(wkv_hbm, raw, sems.at[4])
    stages = page_stages(count, 4, 12)
    paging = page_copies(cache_hbm, pages, stages, sems, 10)
    for copy in small + paging + [weights]:
        copy.start()
    tokens = token_of_column(heads, kv_local, columns)
    lower = iota((ROWS, LANES), 1) < HEAD_DIM
    low = iota((requests, LANES), 1) < HEAD_DIM
    low16 = iota((requests, ROWS, LANES), 2) < HEAD_DIM
    top[...] = jnp.full(top.shape, NEG_FILL, F32)
    acc[...] = jnp.zeros(acc.shape, F32)
    for copy in small:
        copy.wait()
    spread_queries(queries, packed[...].reshape(requests, SLOT, LANES))

    def place_of(p):
        owner = meta[0, p]
        return jnp.where(owner < 0, requests, owner)

    places = [place_of(p) for p in range(count)]

    def keep(p, page_top, total, out):
        tops[p] = jnp.broadcast_to(page_top, (ROWS, LANES))
        sums[p] = jnp.where(lower, total, out)
        top[places[p]] = jnp.maximum(top[places[p]], tops[p])

    attend_pages(
        stages,
        paging,
        lambda p: queries[jnp.maximum(meta[0, p], 0)].astype(BF16),
        lambda p: pages[p],
        lambda p: meta[1, p],
        tokens,
        keep,
        weights,
    )
    cosine = jnp.where(low, tables[0], 1.0)
    sine = jnp.where(low, tables[1], 0.0)
    projected = project_heads(normed[...], raw, kv_local)
    new = [
        rotate(projected[k * requests : (k + 1) * requests], cosine, sine)
        .astype(BF16)
        .astype(F32)
        for k in range(kv_local)
    ]
    used = {place: h for h, place in enumerate(head_rows(heads))}
    for place in range(ROWS):
        value = jnp.zeros((requests, LANES), F32)
        if place in used:
            value = new[used[place] // (heads // kv_local)]
        fresh[pl.ds(place, requests, stride=ROWS), :] = value
    for p, place in enumerate(places):
        scaled[p] = sums[p] * jnp.exp(tops[p] - top[place])
    for p, place in enumerate(places):
        acc[place] = acc[place] + scaled[p]
    added = fresh[...].reshape(requests, ROWS, LANES)
    score = jnp.sum(queries[...] * added, axis=2, keepdims=True)
    score = jnp.broadcast_to(score, added.shape)
    parked = []
    step = requests // 4
    for i in range(4):
        rows = slice(i * step, (i + 1) * step)
        before, fresh_score = top[rows], score[rows]
        highest = jnp.maximum(before, fresh_score)
        whole = acc[rows] * jnp.exp(before - highest)
        whole += jnp.where(low16[rows], 1.0, added[rows]) * jnp.exp(fresh_score - highest)
        acc[rows] = jnp.where(
            low16[rows], highest + jnp.log(whole), whole / pltpu.roll(whole, HEAD_DIM, 2)
        )
        part = pl.ds(i * step, step)
        parked.append(copy_of(acc.at[part], state_hbm.at[part], sems.at[5 + i]))
        parked[i].start()
    for copy in parked:
        copy.wait()


def lent_kernel(
    heads, kv_local, asked_ref, pages, pick_ref, drop_ref, meta_ref, packed_ref,
    normed_ref, tables_ref, hidden_ref,
    reply_hbm, meta_hbm, packed_hbm, normed_hbm, tables_hbm, hidden_hbm,
    reply16, sems,
):
    outgoing, columns, _ = pages.shape
    parked = [
        copy_of(packed_ref, packed_hbm, sems.at[0]),
        copy_of(normed_ref, normed_hbm, sems.at[1]),
        copy_of(hidden_ref, hidden_hbm, sems.at[2]),
        copy_of(tables_ref, tables_hbm, sems.at[3]),
        copy_of(meta_ref, meta_hbm, sems.at[4]),
    ]
    for copy in parked:
        copy.start()
    slot_rows = asked_ref.shape[0]
    shape = (outgoing * SLOT, slot_rows)
    chosen = jnp.where(pick_ref[:, 0:1] == iota(shape, 1), 1.0, 0.0).astype(BF16)
    asked = jnp.dot(chosen, asked_ref[...], preferred_element_type=F32)
    tokens = token_of_column(heads, kv_local, columns).astype(F32)
    low = iota((SLOT, LANES), 1) < HEAD_DIM
    lane = iota((SLOT, LANES), 1)
    row = iota((SLOT, LANES), 0)

    def terms(total, offset):
        leading = total.astype(BF16).astype(F32)
        rest = total - leading
        second = rest.astype(BF16).astype(F32)
        third = rest - second
        spot = lane - offset - 3 * row
        placed = jnp.where(spot == 0, leading, 0.0)
        placed = jnp.where(spot == 1, second, placed)
        return jnp.where(spot == 2, third, placed)

    packed = [asked[j * SLOT : (j + 1) * SLOT] for j in range(outgoing)]
    replies = {}

    def keep(j, top, total, out):
        out = out / total
        logs = top + jnp.log(total)
        even = pltpu.roll(out[0:SLOT], HEAD_DIM, 1)
        both = jnp.where(low, even, out[SLOT:ROWS])
        line = jnp.sum(
            terms(logs[0:SLOT], 0) + terms(logs[SLOT:ROWS], HEAD_DIM), axis=0, keepdims=True
        )
        replies[j] = jnp.where(row == META, line, both)

    attend_pages(
        page_stages(outgoing, 8, 8),
        None,
        lambda j: unpack(packed[j]).astype(BF16),
        lambda j: pages[j],
        lambda j: packed[j][META : META + 1, 0:1],
        tokens,
        keep,
    )
    shape = (slot_rows, outgoing * SLOT)
    placed = jnp.where(drop_ref[0:1, :] == iota(shape, 0), 1.0, 0.0).astype(BF16)
    every = jnp.concatenate([replies[j] for j in range(outgoing)], axis=0).astype(BF16)
    reply = jnp.dot(placed, every, preferred_element_type=F32)
    reply16[...] = reply.astype(BF16)
    replying = copy_of(reply16, reply_hbm, sems.at[5])
    replying.start()
    for copy in parked + [replying]:
        copy.wait()


def combine_kernel(
    heads, pool, meta_hbm, state_hbm, wo_hbm, hidden_hbm, gain_hbm, router_hbm,
    routes_hbm, wd_hbm, reply_ref,
    part_ref, meta_ref, hidden_ref, gain_ref, router_ref, routes_ref, wd_ref,
    meta, state, wo, gain, tops, accs, scaled, reply, finals, sems,
):
    requests = state.shape[0]
    inbox = reply_ref.shape[0] // SLOT
    chunks = -(-heads // 2)
    numbers = copy_of(meta_hbm, meta, sems.at[11])
    arriving = copy_of(state_hbm, state, sems.at[0])
    weights = copies_of(wo_hbm, wo, sems, 1)
    gaining = copy_of(gain_hbm, gain, sems.at[5])
    later = [
        copy_of(meta_hbm, meta_ref, sems.at[6]),
        copy_of(hidden_hbm, hidden_ref, sems.at[7]),
        copy_of(router_hbm, router_ref, sems.at[8]),
        copy_of(routes_hbm, routes_ref, sems.at[9]),
        copy_of(wd_hbm.at[pl.ds(0, wd_ref.shape[0])], wd_ref, sems.at[10]),
    ]
    for copy in [numbers, arriving] + weights + [gaining] + later:
        copy.start()
    reply[...] = reply_ref[...].astype(F32)
    tops[...] = jnp.full(tops.shape, NEG_FILL, F32)
    accs[...] = jnp.zeros(accs.shape, F32)
    low = iota((SLOT, LANES), 1) < HEAD_DIM
    lane = iota((SLOT, LANES), 1)
    row = iota((SLOT, LANES), 0)
    mine = (lane % HEAD_DIM) // 3 == row

    def place_of(s):
        lender = s // CAP ^ (inbox // CAP // 2)
        owner = meta[0, pool + lender * CAP + s % CAP]
        return jnp.where(owner < 0, requests, owner)

    def logs_of(s):
        line = reply[s * SLOT + META : s * SLOT + META + 1, :]
        line = jnp.where(mine, jnp.broadcast_to(line, (SLOT, LANES)), 0.0)
        even = jnp.sum(jnp.where(low, line, 0.0), axis=1, keepdims=True)
        odd = jnp.sum(jnp.where(low, 0.0, line), axis=1, keepdims=True)
        logs = jnp.concatenate([even, odd], axis=0)
        return jnp.broadcast_to(logs, (ROWS, LANES))

    def sum_of(s):
        packed = reply[s * SLOT : (s + 1) * SLOT, :]
        even = jnp.where(low, 1.0, pltpu.roll(packed, HEAD_DIM, 1))
        odd = jnp.where(low, 1.0, packed)
        return jnp.concatenate([even, odd], axis=0)

    logs = [logs_of(s) for s in range(inbox)]
    numbers.wait()
    places = [place_of(s) for s in range(inbox)]
    for s, place in enumerate(places):
        tops[place] = jnp.maximum(tops[place], logs[s])
    for s, place in enumerate(places):
        scaled[s] = sum_of(s) * jnp.exp(logs[s] - tops[place])
    for s, place in enumerate(places):
        accs[place] = accs[place] + scaled[s]
    arriving.wait()
    low16 = iota(state.shape, 2) < HEAD_DIM
    start = state[...]
    before = jnp.where(low16, start, pltpu.roll(start, HEAD_DIM, 2))
    remote = tops[0:requests]
    highest = jnp.maximum(before, remote)
    whole = accs[0:requests] * jnp.exp(remote - highest)
    whole = whole + jnp.where(low16, 1.0, start) * jnp.exp(before - highest)
    finals[...] = (whole / pltpu.roll(whole, HEAD_DIM, 2)).reshape(
        requests * ROWS, LANES
    )
    wide = iota((requests, LANES), 1) < HEAD_DIM
    parts = []
    for j in range(chunks):
        even = finals[pl.ds(j, requests, stride=ROWS), :]
        odd = finals[pl.ds(SLOT + j, requests, stride=ROWS), :]
        parts.append(jnp.where(wide, pltpu.roll(even, HEAD_DIM, 1), odd).astype(BF16))
    attention = jnp.concatenate(parts, axis=1)[:, : heads * HEAD_DIM]
    for copy in weights:
        copy.wait()
    part_ref[...] = jnp.dot(attention, wo[...], preferred_element_type=F32).astype(BF16)
    gaining.wait()
    gain_ref[...] = gain[...].reshape(1, gain.shape[0])
    for copy in later:
        copy.wait()


def load_kernel(wd_hbm, order_hbm, wd_ref, sem):
    del order_hbm
    rows = wd_ref.shape[0]
    copy = copy_of(wd_hbm.at[pl.ds(wd_hbm.shape[0] - rows, rows)], wd_ref, sem)
    copy.start()
    copy.wait()


def finish_kernel(attended_ref, own_ref, other_ref, attended_out, experts_out):
    attended_out[...] = attended_ref[...]
    experts_out[...] = (own_ref[...] + other_ref[...].astype(F32)).astype(BF16)


def own_rows(values, first):
    half = values.shape[0] // 2
    return jnp.where(first, values[:half], values[half:])


def residual_kernel(
    tp, count, meta_ref, hidden_ref, *refs,
):
    pieces = refs[:count]
    gain_ref, attended_ref, input_ref, again_ref = refs[count:]
    requests = hidden_ref.shape[0]
    if count == 2:
        summed = pieces[0][...].astype(F32) + pieces[1][...].astype(F32)
    else:
        summed = pieces[0][0:requests, :].astype(F32)
        for t in range(1, tp):
            part = pieces[0][t * requests : (t + 1) * requests, :]
            summed = summed + part.astype(F32)
    attended = (hidden_ref[...].astype(F32) + RESID_SCALE * summed).astype(BF16)
    if count == 2:
        attended_ref[...] = own_rows(attended, meta_ref[3:4, 0:1] == 0)
    else:
        attended_ref[...] = attended
    ffn_input = norm_rows(attended.astype(F32), gain_ref[...])
    input_ref[...] = ffn_input
    again_ref[...] = ffn_input


def gate_column(units, meta_ref, input_ref, router_ref, routes_ref):
    ffn_input = input_ref[...]
    requests = ffn_input.shape[0]
    logits = lax.dot_general(router_ref[...], ffn_input, NT, preferred_element_type=F32)
    expert = iota(logits.shape, 0)
    named = jnp.zeros(logits.shape, F32)
    for k in range(routes_ref.shape[0]):
        named = jnp.where(routes_ref[k : k + 1, :] == expert, 1.0, named)
    chosen = named > 0.5
    top = jnp.max(jnp.where(chosen, logits, NEG_FILL), axis=0, keepdims=True)
    weights = jnp.where(chosen, jnp.exp(logits - top), 0.0)
    total = jnp.sum(weights, axis=0, keepdims=True)
    mine = expert == meta_ref[3:4, 0:1] * units // FF
    line = jnp.sum(jnp.where(mine, weights, 0.0), axis=0, keepdims=True) / total
    diagonal = iota((requests, requests), 0) == iota((requests, requests), 1)
    line = jnp.where(diagonal, jnp.broadcast_to(line, (requests, requests)), 0.0)
    return jnp.sum(line, axis=1, keepdims=True)


def expert_kernel(
    units, meta_ref, lifted_ref, input_ref, router_ref, routes_ref, wd_ref, wd_rest_ref,
    *outs
):
    column = gate_column(units, meta_ref, input_ref, router_ref, routes_ref)
    gate = lifted_ref[0]
    active = gate / (1.0 + jnp.exp(-gate)) * lifted_ref[1]
    active = active.astype(BF16)
    half = wd_ref.shape[0]
    share = jnp.dot(active[:, :half], wd_ref[...], preferred_element_type=F32)
    share += jnp.dot(active[:, half:], wd_rest_ref[...], preferred_element_type=F32)
    share *= column
    if len(outs) == 2:
        first = meta_ref[3:4, 0:1] == 0
        outs[0][...] = own_rows(share, first)
        outs[1][...] = own_rows(share, jnp.logical_not(first)).astype(BF16)
    else:
        outs[0][...] = share.astype(BF16)


def call(body, outs, in_specs, scratch=(), limit=16, flops=0, moved=0):
    return pl.pallas_call(
        body,
        out_shape=outs,
        in_specs=in_specs,
        out_specs=[VMEM if isinstance(o, jax.ShapeDtypeStruct) else HBM for o in outs],
        scratch_shapes=list(scratch),
        compiler_params=pltpu.CompilerParams(vmem_limit_bytes=limit << 20),
        cost_estimate=pl.CostEstimate(
            flops=flops, bytes_accessed=moved, transcendentals=0
        ),
    )


def swap(values):
    return lax.ppermute(values, "tensor", [(0, 1), (1, 0)])


def on_device(
    hidden,
    attn_gain,
    w_query,
    w_keyvalue,
    w_output,
    cache,
    page_table,
    ctx_len,
    move_dest,
    ffn_gain,
    router,
    routes,
    w_in,
    w_down,
):
    replicas = lax.axis_size("replica")
    tp = lax.axis_size("tensor")
    rank = lax.axis_index("tensor").astype(jnp.int32)
    rows, width = hidden.shape
    pool, page_len, kv_local, _ = cache.shape
    outgoing = move_dest.shape[0]
    local_pages = pool - outgoing
    requests = page_table.shape[0]
    heads = w_query.shape[1] // HEAD_DIM
    inbox = replicas * CAP
    units = w_down.shape[0]
    assert FF % units == 0
    columns = page_len * kv_local
    entries = -(-(pool + inbox) // LANES) * LANES
    struct = jax.ShapeDtypeStruct
    pair = tp == 2
    ids = rank.reshape(1)

    def pin(values):
        return pltpu.with_memory_space_constraint(values, pltpu.HBM)

    def exchange(blocks, order):
        blocks = blocks.reshape(replicas, CAP * SLOT, LANES)
        blocks = lax.all_to_all(
            blocks,
            "replica",
            split_axis=0,
            concat_axis=0,
            tiled=True,
            axis_index_groups=[list(order)],
        )
        return blocks.reshape(inbox * SLOT, LANES)

    blocks = pin(cache.reshape(pool, columns, LANES))
    if pair:
        pieces = [hidden, swap(hidden)]
    else:
        pieces = [lax.all_gather(hidden, "tensor", axis=0, tiled=True)]
    meta_shape = (4, entries)
    tables_shape = (2, requests, LANES)
    own, wq, gain, tables, away, away_span, meta, lent, pick, drop = call(
        functools.partial(prepare_kernel, pool, replicas),
        [
            struct(hidden.shape, BF16),
            struct(w_query.shape, BF16),
            struct((1, width), F32),
            struct(tables_shape, F32),
            struct((inbox, requests), BF16),
            struct((inbox, LANES), F32),
            struct(meta_shape, jnp.int32),
            struct((outgoing, columns, LANES), BF16),
            struct((outgoing * SLOT, LANES), jnp.int32),
            struct((outgoing, outgoing * SLOT), jnp.int32),
        ],
        [SMEM] + [HBM] * 7,
        [
            pltpu.VMEM((1, requests), jnp.int32),
            pltpu.VMEM((page_table.shape[1], requests), jnp.int32),
            pltpu.VMEM((1, outgoing), jnp.int32),
            pltpu.VMEM((width,), F32),
            pltpu.SemaphoreType.DMA((10,)),
        ],
        moved=2 * w_query.size,
    )(
        ids,
        pin(hidden),
        pin(ctx_len.reshape(1, requests)),
        pin(page_table.T),
        pin(move_dest.reshape(1, outgoing)),
        pin(attn_gain),
        pin(w_query),
        blocks,
    )
    if pair:
        pieces[0] = own
    hidden_all, normed, packed, sends = call(
        functools.partial(query_kernel, len(pieces)),
        [
            struct((requests, width), BF16),
            struct((requests, width), BF16),
            struct((requests * SLOT, LANES), F32),
            struct((inbox * SLOT, LANES), BF16),
        ],
        [VMEM] * (len(pieces) + 6),
        [
            pltpu.VMEM((requests * SLOT, LANES), F32),
            pltpu.VMEM((inbox * SLOT, LANES), F32),
        ],
        flops=4 * requests * width * w_query.shape[1],
        moved=2 * w_query.size,
    )(meta, *pieces, gain, wq, tables, away, away_span)
    asked = exchange(sends, range(replicas)[::-1])
    replies, meta_far, packed_far, normed_far, tables_far, hidden_far = call(
        functools.partial(lent_kernel, heads, kv_local),
        [
            pltpu.HBM((inbox * SLOT, LANES), BF16),
            pltpu.HBM(meta_shape, jnp.int32),
            pltpu.HBM((requests * SLOT, LANES), F32),
            pltpu.HBM((requests, width), BF16),
            pltpu.HBM(tables_shape, F32),
            pltpu.HBM((requests, width), BF16),
        ],
        [VMEM] * 9,
        [
            pltpu.VMEM((inbox * SLOT, LANES), BF16),
            pltpu.SemaphoreType.DMA((6,)),
        ],
        flops=4 * ROWS * columns * LANES * outgoing,
        moved=2 * columns * LANES * outgoing,
    )(asked, lent, pick, drop, meta, packed, normed, tables, hidden_all)
    returned = exchange(replies, [r ^ replicas // 2 for r in range(replicas)])
    (state,) = call(
        functools.partial(local_kernel, heads, kv_local),
        [pltpu.HBM((requests, ROWS, LANES), F32)],
        [HBM] * 6,
        [
            pltpu.SMEM(meta_shape, jnp.int32),
            pltpu.VMEM((requests * SLOT, LANES), F32),
            pltpu.VMEM((requests, width), BF16),
            pltpu.VMEM((width * kv_local, LANES), BF16),
            pltpu.VMEM(tables_shape, F32),
            pltpu.VMEM((local_pages, columns, LANES), BF16),
            pltpu.VMEM((requests, ROWS, LANES), F32),
            pltpu.VMEM((requests * ROWS, LANES), F32),
            pltpu.VMEM((local_pages, ROWS, LANES), F32),
            pltpu.VMEM((local_pages, ROWS, LANES), F32),
            pltpu.VMEM((requests + 1, ROWS, LANES), F32),
            pltpu.VMEM((requests + 1, ROWS, LANES), F32),
            pltpu.VMEM((local_pages, ROWS, LANES), F32),
            pltpu.SemaphoreType.DMA((10 + local_pages,)),
        ],
        limit=24,
        flops=4 * ROWS * columns * LANES * local_pages,
        moved=2 * columns * LANES * local_pages,
    )(
        pin(meta_far),
        pin(packed_far),
        pin(normed_far),
        pin(w_keyvalue.reshape(width * kv_local, LANES)),
        pin(tables_far),
        blocks,
    )
    half = struct((units // 2, width), BF16)
    part, meta, hidden_all, gain, router_t, routes_t, wd = call(
        functools.partial(combine_kernel, heads, pool),
        [
            struct((requests, width), BF16),
            struct(meta_shape, jnp.int32),
            struct((requests, width), BF16),
            struct((1, width), F32),
            struct(router.shape[::-1], BF16),
            struct(routes.shape[::-1], jnp.int32),
            half,
        ],
        [HBM] * 8 + [VMEM],
        [
            pltpu.SMEM(meta_shape, jnp.int32),
            pltpu.VMEM((requests, ROWS, LANES), F32),
            pltpu.VMEM(w_output.shape, BF16),
            pltpu.VMEM((width,), F32),
            pltpu.VMEM((requests + 1, ROWS, LANES), F32),
            pltpu.VMEM((requests + 1, ROWS, LANES), F32),
            pltpu.VMEM((inbox, ROWS, LANES), F32),
            pltpu.VMEM((inbox * SLOT, LANES), F32),
            pltpu.VMEM((requests * ROWS, LANES), F32),
            pltpu.SemaphoreType.DMA((12,)),
        ],
        flops=2 * requests * w_output.size,
        moved=2 * w_output.size,
    )(
        pin(meta_far), pin(state), pin(w_output), pin(hidden_far), pin(ffn_gain),
        pin(router.T), pin(routes.T), pin(w_down), returned,
    )
    if pair:
        parts = [part, swap(part)]
    else:
        parts = [lax.all_gather(part, "tensor", axis=0, tiled=True)]
    (wd_rest,) = call(
        load_kernel,
        [half],
        [HBM, ANY],
        [pltpu.SemaphoreType.DMA],
        moved=w_down.size,
    )(pin(w_down), part)
    attended, ffn_input, ffn_again = call(
        functools.partial(residual_kernel, tp, len(parts)),
        [
            struct((rows if pair else requests, width), BF16),
            struct((requests, width), BF16),
            struct((requests, width), BF16),
        ],
        [VMEM] * (len(parts) + 3),
        flops=2 * requests * width,
        moved=8 * requests * width,
    )(meta, hidden_all, *parts, gain)
    lifted = jnp.einsum("rd,dsu->sru", ffn_input, w_in, preferred_element_type=F32)
    shapes = [struct((requests, width), BF16)]
    if pair:
        shapes = [struct((rows, width), F32), struct((rows, width), BF16)]
    shares = call(
        functools.partial(expert_kernel, units),
        shapes,
        [VMEM] * 7,
        flops=2 * requests * w_down.size,
        moved=2 * w_down.size,
    )(meta, lifted, ffn_again, router_t, routes_t, wd, wd_rest)
    if pair:
        out = struct((rows, width), BF16)
        return tuple(
            call(finish_kernel, [out, out], [VMEM] * 3)(attended, shares[0], swap(shares[1]))
        )
    shares = lax.all_gather(shares[0], "tensor", axis=0)
    mine = lax.dynamic_slice_in_dim(shares, rank * rows, rows, axis=1)
    experts_out = jnp.sum(mine.astype(F32), axis=0).astype(BF16)
    attended = lax.dynamic_slice_in_dim(attended, rank * rows, rows, axis=0)
    return attended, experts_out


def solution(mesh):
    placed = (
        P(("replica", "tensor"), None),
        P(),
        P(None, "tensor"),
        P(None, "tensor", None),
        P("tensor", None),
        P("replica", None, "tensor", None),
        P("replica", None),
        P("replica"),
        P("replica"),
        P(),
        P(),
        P("replica", None),
        P(None, None, "tensor"),
        P("tensor", None),
    )
    return jax.shard_map(
        on_device,
        mesh=mesh,
        in_specs=placed,
        out_specs=(P(("replica", "tensor"), None), P(("replica", "tensor"), None)),
        check_vma=False,
    )
```

```python
import functools
import math

import jax
import jax.numpy as jnp
from jax import lax
from jax.experimental import pallas as pl
from jax.experimental.pallas import tpu as pltpu
from jax.sharding import PartitionSpec as P

HEAD_DIM = 64
EXPERTS = 40
FF = 512
CAP = 2
LANES = 128
SLOT = 8
ROWS = 16
META = 6

ATTN_SCALE = 0.015625
RESID_SCALE = 0.22
ROPE_BASE = 10000.0
EPSILON = 1e-06
NEG_FILL = -1e30

F32 = jnp.float32
BF16 = jnp.bfloat16
VMEM = pl.BlockSpec(memory_space=pltpu.VMEM)
SMEM = pl.BlockSpec(memory_space=pltpu.SMEM)
ANY = pl.BlockSpec(memory_space=pl.ANY)
HBM = pl.BlockSpec(memory_space=pltpu.HBM)
NT = (((1,), (1,)), ((), ()))


def iota(shape, axis):
    return lax.broadcasted_iota(jnp.int32, shape, axis)


def norm_rows(values, gain):
    factor = lax.rsqrt(jnp.mean(values * values, axis=-1, keepdims=True) + EPSILON)
    return (values * factor * gain).astype(BF16)


def rope_tables(ctx_row, requests):
    diagonal = iota((requests, requests), 0) == iota((requests, requests), 1)
    ctx = jnp.broadcast_to(ctx_row.astype(F32), (requests, requests))
    ctx = jnp.sum(jnp.where(diagonal, ctx, 0.0), axis=1, keepdims=True)
    lane = iota((requests, LANES), 1)
    index = (lane % (HEAD_DIM // 2)).astype(F32)
    inverse = jnp.exp(index * (-2.0 * math.log(ROPE_BASE) / HEAD_DIM))
    angles = ctx * inverse
    sign = jnp.where(lane % HEAD_DIM < HEAD_DIM // 2, -1.0, 1.0)
    return jnp.cos(angles), jnp.sin(angles) * sign


def rotate(chunk, cosine, sine):
    lane = iota(chunk.shape, 1)
    ahead = pltpu.roll(chunk, LANES - HEAD_DIM // 2, 1)
    behind = pltpu.roll(chunk, HEAD_DIM // 2, 1)
    turned = jnp.where(lane % HEAD_DIM < HEAD_DIM // 2, ahead, behind)
    return chunk * cosine + turned * sine


def copy_of(source, target, sem):
    return pltpu.make_async_copy(source, target, sem)


def copies_of(source, target, sems, base):
    step = source.shape[0] // 4
    return [
        copy_of(
            source.at[pl.ds(i * step, step)], target.at[pl.ds(i * step, step)], sems.at[base + i]
        )
        for i in range(4)
    ]


def page_copies(cache_hbm, pages, stages, sems, base):
    copies = []
    for i, stage in enumerate(stages):
        rows = pl.ds(stage[0], len(stage))
        copies.append(copy_of(cache_hbm.at[rows], pages.at[rows], sems.at[base + i]))
    return copies


def page_stages(count, first, rest):
    starts = [0] + list(range(min(first, count), count, rest))
    return [range(a, b) for a, b in zip(starts, starts[1:] + [count])]


def prepare_kernel(
    pool, replicas, ids_ref, hidden_hbm, ctx_hbm, table_hbm, dest_hbm, attn_gain_hbm,
    wq_hbm, cache_hbm,
    hidden_ref, wq_ref, gain_ref, tables_ref, away_ref, span_ref, meta_ref, lent_ref,
    pick_ref, drop_ref,
    ctx, table, dest, gain, sems,
):
    inbox = replicas * CAP
    requests = ctx.shape[1]
    entries = meta_ref.shape[1]
    small = [
        copy_of(ctx_hbm, ctx, sems.at[0]),
        copy_of(table_hbm, table, sems.at[1]),
        copy_of(dest_hbm, dest, sems.at[2]),
        copy_of(attn_gain_hbm, gain, sems.at[3]),
    ]
    large = [copy_of(hidden_hbm, hidden_ref, sems.at[4])]
    large += copies_of(wq_hbm, wq_ref, sems, 5)
    lending = pl.ds(pool - lent_ref.shape[0], lent_ref.shape[0])
    large.append(copy_of(cache_hbm.at[lending], lent_ref, sems.at[9]))
    for copy in small + large:
        copy.start()
    for copy in small:
        copy.wait()
    gain_ref[...] = gain[...].reshape(1, gain.shape[0])
    ctx_row = ctx[...]

    def claims(values):
        held = jnp.zeros(values.shape, F32)
        spans = jnp.zeros(values.shape, F32)
        for k in range(table.shape[0]):
            match = table[k : k + 1, :] == values
            filled = jnp.clip(ctx_row - k * 128, 0, 128).astype(F32)
            held = jnp.where(match, 1.0, held)
            spans = jnp.where(match, filled, spans)
        return held.astype(BF16), spans

    held, spans = claims(iota((entries, requests), 0))
    numbers = (iota((SLOT, requests), 1) + 1).astype(BF16)
    ones = jnp.ones((SLOT, requests), BF16)
    holder = lax.dot_general(numbers, held, NT, preferred_element_type=F32)
    covered = lax.dot_general(ones, spans.astype(BF16), NT, preferred_element_type=F32)
    meta_ref[0:1, :] = holder[0:1, :].astype(jnp.int32) - 1
    meta_ref[1:2, :] = covered[0:1, :].astype(jnp.int32)
    meta_ref[2:3, :] = jnp.zeros((1, entries), jnp.int32)
    lent = dest.shape[1]
    across = jnp.broadcast_to(dest[...].astype(F32), (lent, lent))
    row, lane = iota((lent, lent), 0), iota((lent, lent), 1)
    down = jnp.sum(jnp.where(row == lane, across, 0.0), axis=1, keepdims=True)
    same = across == down
    before = jnp.sum(jnp.where(same & (lane < row), 1.0, 0.0), axis=1, keepdims=True)
    column = (replicas - 1 - down) * CAP + before
    column = jnp.broadcast_to(column, (lent, LANES)).astype(BF16)
    before = jnp.sum(jnp.where(same & (row < lane), 1.0, 0.0), axis=0, keepdims=True)
    line = dest[...] ^ replicas // 2
    line = jnp.broadcast_to(line.astype(F32), (lent, lent))
    line = (line * CAP + before).astype(BF16)
    expand = iota((lent * SLOT, lent), 0) // SLOT == iota((lent * SLOT, lent), 1)
    expand = jnp.where(expand, 1.0, 0.0).astype(BF16)
    column = jnp.dot(expand, column, preferred_element_type=F32).astype(jnp.int32)
    pick_ref[...] = column * SLOT + iota(column.shape, 0) % SLOT
    line = lax.dot_general(line, expand, NT, preferred_element_type=F32).astype(jnp.int32)
    drop_ref[...] = line * SLOT + iota(line.shape, 1) % SLOT
    meta_ref[3:4, :] = jnp.full((1, entries), ids_ref[0], jnp.int32)
    cosine, sine = rope_tables(ctx_row, requests)
    tables_ref[0] = cosine
    tables_ref[1] = sine
    slot = iota((inbox, requests), 0)
    lender = replicas - 1 - slot // CAP
    held, spans = claims(pool + lender * CAP + slot % CAP)
    away_ref[...] = held
    away_span = jnp.sum(spans, axis=1, keepdims=True)
    span_ref[...] = jnp.broadcast_to(away_span, span_ref.shape)
    for copy in large:
        copy.wait()


def query_kernel(
    count, meta_ref, *refs,
):
    pieces = refs[:count]
    (gain_ref, wq_ref, tables_ref, away_ref, span_ref,
     hidden_ref, normed_ref, packed_ref, send_ref, packs, sends) = refs[count:]
    requests = hidden_ref.shape[0]
    inbox = span_ref.shape[0]
    width = wq_ref.shape[1]
    chunks = -(-width // LANES)
    if count == 1:
        hidden = pieces[0][...]
    else:
        own, other = pieces[0][...], pieces[1][...]
        first = meta_ref[3:4, 0:1] == 0
        hidden = jnp.concatenate(
            [jnp.where(first, own, other), jnp.where(first, other, own)], axis=0
        )
    hidden_ref[...] = hidden
    normed = norm_rows(hidden.astype(F32), gain_ref[...])
    normed_ref[...] = normed
    queries = jnp.dot(normed, wq_ref[...], preferred_element_type=F32)
    if chunks * LANES > width:
        pad = jnp.zeros((requests, chunks * LANES - width), F32)
        queries = jnp.concatenate([queries, pad], axis=1)
    cosine, sine = tables_ref[0], tables_ref[1]
    zeros = jnp.zeros((requests, LANES), F32)
    nothing = jnp.zeros((inbox, LANES), F32)
    for j in range(SLOT):
        here = pl.ds(j, requests, stride=SLOT)
        there = pl.ds(j, inbox, stride=SLOT)
        if j < chunks:
            chunk = rotate(queries[:, j * LANES : (j + 1) * LANES], cosine, sine)
            chunk = (chunk.astype(BF16).astype(F32) * ATTN_SCALE).astype(BF16)
            packs[here, :] = chunk.astype(F32)
            sends[there, :] = jnp.dot(away_ref[...], chunk, preferred_element_type=F32)
        else:
            packs[here, :] = zeros
            sends[there, :] = span_ref[...] if j == META else nothing
    packed_ref[...] = packs[...]
    send_ref[...] = sends[...].astype(BF16)


def unpack(packed):
    low = iota(packed.shape, 1) < HEAD_DIM
    even = jnp.where(low, packed, 0.0)
    odd = jnp.where(low, pltpu.roll(packed, HEAD_DIM, 1), 0.0)
    return jnp.concatenate([even, odd], axis=0)


def head_rows(heads):
    return [(h // 2) + SLOT * (h % 2) for h in range(heads)]


def token_of_column(heads, kv_local, columns):
    row = iota((ROWS, columns), 0)
    column = iota((ROWS, columns), 1)
    wanted = jnp.full((ROWS, columns), kv_local, jnp.int32)
    for h, place in enumerate(head_rows(heads)):
        wanted = jnp.where(row == place, h // (heads // kv_local), wanted)
    return jnp.where(column % kv_local == wanted, column // kv_local, 1 << 20)


def score_page(query, block):
    return lax.dot_general(query, block, NT, preferred_element_type=F32)


def weigh_page(scores, tokens, span):
    scores = jnp.where(tokens < span, scores, NEG_FILL)
    top = jnp.max(scores, axis=1, keepdims=True)
    weights = jnp.exp(scores - top)
    return top, jnp.sum(weights, axis=1, keepdims=True), weights.astype(BF16)


def attend_pages(
    stages, copies, query_of, block_of, span_of, tokens, keep, last=None
):
    def score_stage(i):
        if copies is not None:
            copies[i].wait()
        if last is not None and i == len(stages) - 1:
            last.wait()
        return {p: score_page(query_of(p), block_of(p)) for p in stages[i]}

    scores = score_stage(0)
    for i, pages in enumerate(stages):
        if i + 1 < len(stages):
            ahead = score_stage(i + 1)
        weighed = {p: weigh_page(scores[p], tokens, span_of(p)) for p in pages}
        outs = {
            p: jnp.dot(weighed[p][2], block_of(p), preferred_element_type=F32)
            for p in pages
        }
        for p in pages:
            keep(p, weighed[p][0], weighed[p][1], outs[p])
        if i + 1 < len(stages):
            scores = ahead


def spread_queries(target, packed):
    low = iota(packed.shape, 2) < HEAD_DIM
    target[:, 0:SLOT, :] = jnp.where(low, packed, 0.0)
    target[:, SLOT:ROWS, :] = jnp.where(low, pltpu.roll(packed, HEAD_DIM, 2), 0.0)


def merge_pages(places, top_of, sum_of, top, acc, scaled, start, before):
    requests = start.shape[0]
    for p, place in enumerate(places):
        top[place] = jnp.maximum(top[place], top_of(p))
    acc[0:requests] = start * jnp.exp(before - top[0:requests])
    for p, place in enumerate(places):
        scaled[p] = sum_of(p) * jnp.exp(top_of(p) - top[place])
    for p, place in enumerate(places):
        acc[place] = acc[place] + scaled[p]


def project_heads(values, weights_ref, heads):
    if heads == 1:
        return jnp.dot(values, weights_ref[...], preferred_element_type=F32)
    rows, depth = values.shape
    wide = 1024
    part = wide // heads
    repeat = iota((part, wide), 1) // heads == iota((part, wide), 0)
    repeat = jnp.where(repeat, 1.0, 0.0).astype(BF16)
    parts = [values[:, i : i + part] for i in range(0, depth, part)]
    spread = jnp.dot(
        jnp.concatenate(parts, axis=0), repeat, preferred_element_type=F32
    ).astype(BF16)
    lane = iota((1, wide), 1) % heads
    masks = [jnp.where(lane == k, 1.0, 0.0).astype(BF16) for k in range(heads)]
    total = jnp.zeros((heads * rows, LANES), F32)
    for i in range(len(parts)):
        piece = spread[i * rows : (i + 1) * rows]
        piece = jnp.concatenate([piece * mask for mask in masks], axis=0)
        total += jnp.dot(
            piece, weights_ref[i * wide : (i + 1) * wide, :], preferred_element_type=F32
        )
    return total


def local_kernel(
    heads, kv_local, meta_hbm, packed_hbm, normed_hbm, wkv_hbm, tables_hbm, cache_hbm,
    state_hbm,
    meta, packed, normed, raw, tables, pages, queries, fresh, tops, sums, top, acc,
    scaled, sems,
):
    requests = normed.shape[0]
    count, columns, _ = pages.shape
    small = [
        copy_of(meta_hbm, meta, sems.at[0]),
        copy_of(packed_hbm, packed, sems.at[1]),
        copy_of(normed_hbm, normed, sems.at[2]),
        copy_of(tables_hbm, tables, sems.at[3]),
    ]
    weights = copy_of(wkv_hbm, raw, sems.at[4])
    stages = page_stages(count, 16, 24)
    paging = page_copies(cache_hbm, pages, stages, sems, 10)
    for copy in small + paging + [weights]:
        copy.start()
    tokens = token_of_column(heads, kv_local, columns)
    lower = iota((ROWS, LANES), 1) < HEAD_DIM
    low = iota((requests, LANES), 1) < HEAD_DIM
    low16 = iota((requests, ROWS, LANES), 2) < HEAD_DIM
    top[...] = jnp.full(top.shape, NEG_FILL, F32)
    acc[...] = jnp.zeros(acc.shape, F32)
    for copy in small:
        copy.wait()
    spread_queries(queries, packed[...].reshape(requests, SLOT, LANES))

    def place_of(p):
        owner = meta[0, p]
        return jnp.where(owner < 0, requests, owner)

    places = [place_of(p) for p in range(count)]

    def keep(p, page_top, total, out):
        tops[p] = jnp.broadcast_to(page_top, (ROWS, LANES))
        sums[p] = jnp.where(lower, total, out)
        top[places[p]] = jnp.maximum(top[places[p]], tops[p])

    attend_pages(
        stages,
        paging,
        lambda p: queries[jnp.maximum(meta[0, p], 0)].astype(BF16),
        lambda p: pages[p],
        lambda p: meta[1, p],
        tokens,
        keep,
        weights,
    )
    cosine = jnp.where(low, tables[0], 1.0)
    sine = jnp.where(low, tables[1], 0.0)
    projected = project_heads(normed[...], raw, kv_local)
    new = [
        rotate(projected[k * requests : (k + 1) * requests], cosine, sine)
        .astype(BF16)
        .astype(F32)
        for k in range(kv_local)
    ]
    used = {place: h for h, place in enumerate(head_rows(heads))}
    for place in range(ROWS):
        value = jnp.zeros((requests, LANES), F32)
        if place in used:
            value = new[used[place] // (heads // kv_local)]
        fresh[pl.ds(place, requests, stride=ROWS), :] = value
    for p, place in enumerate(places):
        scaled[p] = sums[p] * jnp.exp(tops[p] - top[place])
    for p, place in enumerate(places):
        acc[place] = acc[place] + scaled[p]
    added = fresh[...].reshape(requests, ROWS, LANES)
    score = jnp.sum(queries[...] * added, axis=2, keepdims=True)
    score = jnp.broadcast_to(score, added.shape)
    parked = []
    step = requests // 4
    for i in range(4):
        rows = slice(i * step, (i + 1) * step)
        before, fresh_score = top[rows], score[rows]
        highest = jnp.maximum(before, fresh_score)
        whole = acc[rows] * jnp.exp(before - highest)
        whole += jnp.where(low16[rows], 1.0, added[rows]) * jnp.exp(fresh_score - highest)
        acc[rows] = jnp.where(
            low16[rows], highest + jnp.log(whole), whole / pltpu.roll(whole, HEAD_DIM, 2)
        )
        part = pl.ds(i * step, step)
        parked.append(copy_of(acc.at[part], state_hbm.at[part], sems.at[5 + i]))
        parked[i].start()
    for copy in parked:
        copy.wait()


def lent_kernel(
    heads, kv_local, asked_ref, pages, pick_ref, drop_ref, meta_ref, packed_ref,
    normed_ref, tables_ref, hidden_ref,
    reply_hbm, meta_hbm, packed_hbm, normed_hbm, tables_hbm, hidden_hbm,
    reply16, sems,
):
    outgoing, columns, _ = pages.shape
    parked = [
        copy_of(packed_ref, packed_hbm, sems.at[0]),
        copy_of(normed_ref, normed_hbm, sems.at[1]),
        copy_of(hidden_ref, hidden_hbm, sems.at[2]),
        copy_of(tables_ref, tables_hbm, sems.at[3]),
        copy_of(meta_ref, meta_hbm, sems.at[4]),
    ]
    for copy in parked:
        copy.start()
    slot_rows = asked_ref.shape[0]
    shape = (outgoing * SLOT, slot_rows)
    chosen = jnp.where(pick_ref[:, 0:1] == iota(shape, 1), 1.0, 0.0).astype(BF16)
    asked = jnp.dot(chosen, asked_ref[...], preferred_element_type=F32)
    tokens = token_of_column(heads, kv_local, columns).astype(F32)
    low = iota((SLOT, LANES), 1) < HEAD_DIM
    lane = iota((SLOT, LANES), 1)
    row = iota((SLOT, LANES), 0)

    def terms(total, offset):
        leading = total.astype(BF16).astype(F32)
        rest = total - leading
        second = rest.astype(BF16).astype(F32)
        third = rest - second
        spot = lane - offset - 3 * row
        placed = jnp.where(spot == 0, leading, 0.0)
        placed = jnp.where(spot == 1, second, placed)
        return jnp.where(spot == 2, third, placed)

    packed = [asked[j * SLOT : (j + 1) * SLOT] for j in range(outgoing)]
    replies = {}

    def keep(j, top, total, out):
        out = out / total
        logs = top + jnp.log(total)
        even = pltpu.roll(out[0:SLOT], HEAD_DIM, 1)
        both = jnp.where(low, even, out[SLOT:ROWS])
        line = jnp.sum(
            terms(logs[0:SLOT], 0) + terms(logs[SLOT:ROWS], HEAD_DIM), axis=0, keepdims=True
        )
        replies[j] = jnp.where(row == META, line, both)

    attend_pages(
        page_stages(outgoing, 8, 8),
        None,
        lambda j: unpack(packed[j]).astype(BF16),
        lambda j: pages[j],
        lambda j: packed[j][META : META + 1, 0:1],
        tokens,
        keep,
    )
    shape = (slot_rows, outgoing * SLOT)
    placed = jnp.where(drop_ref[0:1, :] == iota(shape, 0), 1.0, 0.0).astype(BF16)
    every = jnp.concatenate([replies[j] for j in range(outgoing)], axis=0).astype(BF16)
    reply = jnp.dot(placed, every, preferred_element_type=F32)
    reply16[...] = reply.astype(BF16)
    replying = copy_of(reply16, reply_hbm, sems.at[5])
    replying.start()
    for copy in parked + [replying]:
        copy.wait()


def combine_kernel(
    heads, pool, meta_hbm, state_hbm, wo_hbm, hidden_hbm, gain_hbm, router_hbm,
    routes_hbm, wd_hbm, reply_ref,
    part_ref, meta_ref, hidden_ref, gain_ref, router_ref, routes_ref, wd_ref,
    meta, state, wo, gain, tops, accs, scaled, reply, finals, sems,
):
    requests = state.shape[0]
    inbox = reply_ref.shape[0] // SLOT
    chunks = -(-heads // 2)
    numbers = copy_of(meta_hbm, meta, sems.at[11])
    arriving = copy_of(state_hbm, state, sems.at[0])
    weights = copies_of(wo_hbm, wo, sems, 1)
    gaining = copy_of(gain_hbm, gain, sems.at[5])
    later = [
        copy_of(meta_hbm, meta_ref, sems.at[6]),
        copy_of(hidden_hbm, hidden_ref, sems.at[7]),
        copy_of(router_hbm, router_ref, sems.at[8]),
        copy_of(routes_hbm, routes_ref, sems.at[9]),
        copy_of(wd_hbm.at[pl.ds(0, wd_ref.shape[0])], wd_ref, sems.at[10]),
    ]
    for copy in [numbers, arriving] + weights + [gaining] + later:
        copy.start()
    reply[...] = reply_ref[...].astype(F32)
    tops[...] = jnp.full(tops.shape, NEG_FILL, F32)
    accs[...] = jnp.zeros(accs.shape, F32)
    low = iota((SLOT, LANES), 1) < HEAD_DIM
    lane = iota((SLOT, LANES), 1)
    row = iota((SLOT, LANES), 0)
    mine = (lane % HEAD_DIM) // 3 == row

    def place_of(s):
        lender = s // CAP ^ (inbox // CAP // 2)
        owner = meta[0, pool + lender * CAP + s % CAP]
        return jnp.where(owner < 0, requests, owner)

    def logs_of(s):
        line = reply[s * SLOT + META : s * SLOT + META + 1, :]
        line = jnp.where(mine, jnp.broadcast_to(line, (SLOT, LANES)), 0.0)
        even = jnp.sum(jnp.where(low, line, 0.0), axis=1, keepdims=True)
        odd = jnp.sum(jnp.where(low, 0.0, line), axis=1, keepdims=True)
        logs = jnp.concatenate([even, odd], axis=0)
        return jnp.broadcast_to(logs, (ROWS, LANES))

    def sum_of(s):
        packed = reply[s * SLOT : (s + 1) * SLOT, :]
        even = jnp.where(low, 1.0, pltpu.roll(packed, HEAD_DIM, 1))
        odd = jnp.where(low, 1.0, packed)
        return jnp.concatenate([even, odd], axis=0)

    logs = [logs_of(s) for s in range(inbox)]
    numbers.wait()
    places = [place_of(s) for s in range(inbox)]
    for s, place in enumerate(places):
        tops[place] = jnp.maximum(tops[place], logs[s])
    for s, place in enumerate(places):
        scaled[s] = sum_of(s) * jnp.exp(logs[s] - tops[place])
    for s, place in enumerate(places):
        accs[place] = accs[place] + scaled[s]
    arriving.wait()
    low16 = iota(state.shape, 2) < HEAD_DIM
    start = state[...]
    before = jnp.where(low16, start, pltpu.roll(start, HEAD_DIM, 2))
    remote = tops[0:requests]
    highest = jnp.maximum(before, remote)
    whole = accs[0:requests] * jnp.exp(remote - highest)
    whole = whole + jnp.where(low16, 1.0, start) * jnp.exp(before - highest)
    finals[...] = (whole / pltpu.roll(whole, HEAD_DIM, 2)).reshape(
        requests * ROWS, LANES
    )
    wide = iota((requests, LANES), 1) < HEAD_DIM
    parts = []
    for j in range(chunks):
        even = finals[pl.ds(j, requests, stride=ROWS), :]
        odd = finals[pl.ds(SLOT + j, requests, stride=ROWS), :]
        parts.append(jnp.where(wide, pltpu.roll(even, HEAD_DIM, 1), odd).astype(BF16))
    attention = jnp.concatenate(parts, axis=1)[:, : heads * HEAD_DIM]
    for copy in weights:
        copy.wait()
    part_ref[...] = jnp.dot(attention, wo[...], preferred_element_type=F32).astype(BF16)
    gaining.wait()
    gain_ref[...] = gain[...].reshape(1, gain.shape[0])
    for copy in later:
        copy.wait()


def load_kernel(wd_hbm, order_hbm, wd_ref, sem):
    del order_hbm
    rows = wd_ref.shape[0]
    copy = copy_of(wd_hbm.at[pl.ds(wd_hbm.shape[0] - rows, rows)], wd_ref, sem)
    copy.start()
    copy.wait()


def finish_kernel(attended_ref, own_ref, other_ref, attended_out, experts_out):
    attended_out[...] = attended_ref[...]
    experts_out[...] = (own_ref[...] + other_ref[...].astype(F32)).astype(BF16)


def own_rows(values, first):
    half = values.shape[0] // 2
    return jnp.where(first, values[:half], values[half:])


def residual_kernel(
    tp, count, meta_ref, hidden_ref, *refs,
):
    pieces = refs[:count]
    gain_ref, attended_ref, input_ref, again_ref = refs[count:]
    requests = hidden_ref.shape[0]
    if count == 2:
        summed = pieces[0][...].astype(F32) + pieces[1][...].astype(F32)
    else:
        summed = pieces[0][0:requests, :].astype(F32)
        for t in range(1, tp):
            part = pieces[0][t * requests : (t + 1) * requests, :]
            summed = summed + part.astype(F32)
    attended = (hidden_ref[...].astype(F32) + RESID_SCALE * summed).astype(BF16)
    if count == 2:
        attended_ref[...] = own_rows(attended, meta_ref[3:4, 0:1] == 0)
    else:
        attended_ref[...] = attended
    ffn_input = norm_rows(attended.astype(F32), gain_ref[...])
    input_ref[...] = ffn_input
    again_ref[...] = ffn_input


def gate_column(units, meta_ref, input_ref, router_ref, routes_ref):
    ffn_input = input_ref[...]
    requests = ffn_input.shape[0]
    logits = lax.dot_general(router_ref[...], ffn_input, NT, preferred_element_type=F32)
    expert = iota(logits.shape, 0)
    named = jnp.zeros(logits.shape, F32)
    for k in range(routes_ref.shape[0]):
        named = jnp.where(routes_ref[k : k + 1, :] == expert, 1.0, named)
    chosen = named > 0.5
    top = jnp.max(jnp.where(chosen, logits, NEG_FILL), axis=0, keepdims=True)
    weights = jnp.where(chosen, jnp.exp(logits - top), 0.0)
    total = jnp.sum(weights, axis=0, keepdims=True)
    mine = expert == meta_ref[3:4, 0:1] * units // FF
    line = jnp.sum(jnp.where(mine, weights, 0.0), axis=0, keepdims=True) / total
    diagonal = iota((requests, requests), 0) == iota((requests, requests), 1)
    line = jnp.where(diagonal, jnp.broadcast_to(line, (requests, requests)), 0.0)
    return jnp.sum(line, axis=1, keepdims=True)


def expert_kernel(
    units, meta_ref, lifted_ref, input_ref, router_ref, routes_ref, wd_ref, wd_rest_ref,
    *outs
):
    column = gate_column(units, meta_ref, input_ref, router_ref, routes_ref)
    gate = lifted_ref[0]
    active = gate / (1.0 + jnp.exp(-gate)) * lifted_ref[1]
    active = active.astype(BF16)
    half = wd_ref.shape[0]
    share = jnp.dot(active[:, :half], wd_ref[...], preferred_element_type=F32)
    share += jnp.dot(active[:, half:], wd_rest_ref[...], preferred_element_type=F32)
    share *= column
    if len(outs) == 2:
        first = meta_ref[3:4, 0:1] == 0
        outs[0][...] = own_rows(share, first)
        outs[1][...] = own_rows(share, jnp.logical_not(first)).astype(BF16)
    else:
        outs[0][...] = share.astype(BF16)


def call(body, outs, in_specs, scratch=(), limit=16, flops=0, moved=0):
    return pl.pallas_call(
        body,
        out_shape=outs,
        in_specs=in_specs,
        out_specs=[VMEM if isinstance(o, jax.ShapeDtypeStruct) else HBM for o in outs],
        scratch_shapes=list(scratch),
        compiler_params=pltpu.CompilerParams(vmem_limit_bytes=limit << 20),
        cost_estimate=pl.CostEstimate(
            flops=flops, bytes_accessed=moved, transcendentals=0
        ),
    )


def swap(values):
    return lax.ppermute(values, "tensor", [(0, 1), (1, 0)])


def on_device(
    hidden,
    attn_gain,
    w_query,
    w_keyvalue,
    w_output,
    cache,
    page_table,
    ctx_len,
    move_dest,
    ffn_gain,
    router,
    routes,
    w_in,
    w_down,
):
    replicas = lax.axis_size("replica")
    tp = lax.axis_size("tensor")
    rank = lax.axis_index("tensor").astype(jnp.int32)
    rows, width = hidden.shape
    pool, page_len, kv_local, _ = cache.shape
    outgoing = move_dest.shape[0]
    local_pages = pool - outgoing
    requests = page_table.shape[0]
    heads = w_query.shape[1] // HEAD_DIM
    inbox = replicas * CAP
    units = w_down.shape[0]
    assert FF % units == 0
    columns = page_len * kv_local
    entries = -(-(pool + inbox) // LANES) * LANES
    struct = jax.ShapeDtypeStruct
    pair = tp == 2
    ids = rank.reshape(1)

    def pin(values):
        return pltpu.with_memory_space_constraint(values, pltpu.HBM)

    def exchange(blocks, order):
        blocks = blocks.reshape(replicas, CAP * SLOT, LANES)
        blocks = lax.all_to_all(
            blocks,
            "replica",
            split_axis=0,
            concat_axis=0,
            tiled=True,
            axis_index_groups=[list(order)],
        )
        return blocks.reshape(inbox * SLOT, LANES)

    blocks = pin(cache.reshape(pool, columns, LANES))
    if pair:
        pieces = [hidden, swap(hidden)]
    else:
        pieces = [lax.all_gather(hidden, "tensor", axis=0, tiled=True)]
    meta_shape = (4, entries)
    tables_shape = (2, requests, LANES)
    own, wq, gain, tables, away, away_span, meta, lent, pick, drop = call(
        functools.partial(prepare_kernel, pool, replicas),
        [
            struct(hidden.shape, BF16),
            struct(w_query.shape, BF16),
            struct((1, width), F32),
            struct(tables_shape, F32),
            struct((inbox, requests), BF16),
            struct((inbox, LANES), F32),
            struct(meta_shape, jnp.int32),
            struct((outgoing, columns, LANES), BF16),
            struct((outgoing * SLOT, LANES), jnp.int32),
            struct((outgoing, outgoing * SLOT), jnp.int32),
        ],
        [SMEM] + [HBM] * 7,
        [
            pltpu.VMEM((1, requests), jnp.int32),
            pltpu.VMEM((page_table.shape[1], requests), jnp.int32),
            pltpu.VMEM((1, outgoing), jnp.int32),
            pltpu.VMEM((width,), F32),
            pltpu.SemaphoreType.DMA((10,)),
        ],
        moved=2 * w_query.size,
    )(
        ids,
        pin(hidden),
        pin(ctx_len.reshape(1, requests)),
        pin(page_table.T),
        pin(move_dest.reshape(1, outgoing)),
        pin(attn_gain),
        pin(w_query),
        blocks,
    )
    if pair:
        pieces[0] = own
    hidden_all, normed, packed, sends = call(
        functools.partial(query_kernel, len(pieces)),
        [
            struct((requests, width), BF16),
            struct((requests, width), BF16),
            struct((requests * SLOT, LANES), F32),
            struct((inbox * SLOT, LANES), BF16),
        ],
        [VMEM] * (len(pieces) + 6),
        [
            pltpu.VMEM((requests * SLOT, LANES), F32),
            pltpu.VMEM((inbox * SLOT, LANES), F32),
        ],
        flops=4 * requests * width * w_query.shape[1],
        moved=2 * w_query.size,
    )(meta, *pieces, gain, wq, tables, away, away_span)
    asked = exchange(sends, range(replicas)[::-1])
    replies, meta_far, packed_far, normed_far, tables_far, hidden_far = call(
        functools.partial(lent_kernel, heads, kv_local),
        [
            pltpu.HBM((inbox * SLOT, LANES), BF16),
            pltpu.HBM(meta_shape, jnp.int32),
            pltpu.HBM((requests * SLOT, LANES), F32),
            pltpu.HBM((requests, width), BF16),
            pltpu.HBM(tables_shape, F32),
            pltpu.HBM((requests, width), BF16),
        ],
        [VMEM] * 9,
        [
            pltpu.VMEM((inbox * SLOT, LANES), BF16),
            pltpu.SemaphoreType.DMA((6,)),
        ],
        flops=4 * ROWS * columns * LANES * outgoing,
        moved=2 * columns * LANES * outgoing,
    )(asked, lent, pick, drop, meta, packed, normed, tables, hidden_all)
    returned = exchange(replies, [r ^ replicas // 2 for r in range(replicas)])
    (state,) = call(
        functools.partial(local_kernel, heads, kv_local),
        [pltpu.HBM((requests, ROWS, LANES), F32)],
        [HBM] * 6,
        [
            pltpu.SMEM(meta_shape, jnp.int32),
            pltpu.VMEM((requests * SLOT, LANES), F32),
            pltpu.VMEM((requests, width), BF16),
            pltpu.VMEM((width * kv_local, LANES), BF16),
            pltpu.VMEM(tables_shape, F32),
            pltpu.VMEM((local_pages, columns, LANES), BF16),
            pltpu.VMEM((requests, ROWS, LANES), F32),
            pltpu.VMEM((requests * ROWS, LANES), F32),
            pltpu.VMEM((local_pages, ROWS, LANES), F32),
            pltpu.VMEM((local_pages, ROWS, LANES), F32),
            pltpu.VMEM((requests + 1, ROWS, LANES), F32),
            pltpu.VMEM((requests + 1, ROWS, LANES), F32),
            pltpu.VMEM((local_pages, ROWS, LANES), F32),
            pltpu.SemaphoreType.DMA((10 + local_pages,)),
        ],
        limit=24,
        flops=4 * ROWS * columns * LANES * local_pages,
        moved=2 * columns * LANES * local_pages,
    )(
        pin(meta_far),
        pin(packed_far),
        pin(normed_far),
        pin(w_keyvalue.reshape(width * kv_local, LANES)),
        pin(tables_far),
        blocks,
    )
    half = struct((units // 2, width), BF16)
    part, meta, hidden_all, gain, router_t, routes_t, wd = call(
        functools.partial(combine_kernel, heads, pool),
        [
            struct((requests, width), BF16),
            struct(meta_shape, jnp.int32),
            struct((requests, width), BF16),
            struct((1, width), F32),
            struct(router.shape[::-1], BF16),
            struct(routes.shape[::-1], jnp.int32),
            half,
        ],
        [HBM] * 8 + [VMEM],
        [
            pltpu.SMEM(meta_shape, jnp.int32),
            pltpu.VMEM((requests, ROWS, LANES), F32),
            pltpu.VMEM(w_output.shape, BF16),
            pltpu.VMEM((width,), F32),
            pltpu.VMEM((requests + 1, ROWS, LANES), F32),
            pltpu.VMEM((requests + 1, ROWS, LANES), F32),
            pltpu.VMEM((inbox, ROWS, LANES), F32),
            pltpu.VMEM((inbox * SLOT, LANES), F32),
            pltpu.VMEM((requests * ROWS, LANES), F32),
            pltpu.SemaphoreType.DMA((12,)),
        ],
        flops=2 * requests * w_output.size,
        moved=2 * w_output.size,
    )(
        pin(meta_far), pin(state), pin(w_output), pin(hidden_far), pin(ffn_gain),
        pin(router.T), pin(routes.T), pin(w_down), returned,
    )
    if pair:
        parts = [part, swap(part)]
    else:
        parts = [lax.all_gather(part, "tensor", axis=0, tiled=True)]
    (wd_rest,) = call(
        load_kernel,
        [half],
        [HBM, ANY],
        [pltpu.SemaphoreType.DMA],
        moved=w_down.size,
    )(pin(w_down), part)
    attended, ffn_input, ffn_again = call(
        functools.partial(residual_kernel, tp, len(parts)),
        [
            struct((rows if pair else requests, width), BF16),
            struct((requests, width), BF16),
            struct((requests, width), BF16),
        ],
        [VMEM] * (len(parts) + 3),
        flops=2 * requests * width,
        moved=8 * requests * width,
    )(meta, hidden_all, *parts, gain)
    lifted = jnp.einsum("rd,dsu->sru", ffn_input, w_in, preferred_element_type=F32)
    shapes = [struct((requests, width), BF16)]
    if pair:
        shapes = [struct((rows, width), F32), struct((rows, width), BF16)]
    shares = call(
        functools.partial(expert_kernel, units),
        shapes,
        [VMEM] * 7,
        flops=2 * requests * w_down.size,
        moved=2 * w_down.size,
    )(meta, lifted, ffn_again, router_t, routes_t, wd, wd_rest)
    if pair:
        out = struct((rows, width), BF16)
        return tuple(
            call(finish_kernel, [out, out], [VMEM] * 3)(attended, shares[0], swap(shares[1]))
        )
    shares = lax.all_gather(shares[0], "tensor", axis=0)
    mine = lax.dynamic_slice_in_dim(shares, rank * rows, rows, axis=1)
    experts_out = jnp.sum(mine.astype(F32), axis=0).astype(BF16)
    attended = lax.dynamic_slice_in_dim(attended, rank * rows, rows, axis=0)
    return attended, experts_out


def solution(mesh):
    placed = (
        P(("replica", "tensor"), None),
        P(),
        P(None, "tensor"),
        P(None, "tensor", None),
        P("tensor", None),
        P("replica", None, "tensor", None),
        P("replica", None),
        P("replica"),
        P("replica"),
        P(),
        P(),
        P("replica", None),
        P(None, None, "tensor"),
        P("tensor", None),
    )
    return jax.shard_map(
        on_device,
        mesh=mesh,
        in_specs=placed,
        out_specs=(P(("replica", "tensor"), None), P(("replica", "tensor"), None)),
        check_vma=False,
    )
```

```python
import functools
import math

import jax
import jax.numpy as jnp
from jax import lax
from jax.experimental import pallas as pl
from jax.experimental.pallas import tpu as pltpu
from jax.sharding import PartitionSpec as P

HEAD_DIM = 64
EXPERTS = 40
FF = 512
CAP = 2
LANES = 128
SLOT = 8
ROWS = 16
META = 6

ATTN_SCALE = 0.015625
RESID_SCALE = 0.22
ROPE_BASE = 10000.0
EPSILON = 1e-06
NEG_FILL = -1e30

F32 = jnp.float32
BF16 = jnp.bfloat16
VMEM = pl.BlockSpec(memory_space=pltpu.VMEM)
SMEM = pl.BlockSpec(memory_space=pltpu.SMEM)
ANY = pl.BlockSpec(memory_space=pl.ANY)
HBM = pl.BlockSpec(memory_space=pltpu.HBM)
NT = (((1,), (1,)), ((), ()))


def iota(shape, axis):
    return lax.broadcasted_iota(jnp.int32, shape, axis)


def norm_rows(values, gain):
    factor = lax.rsqrt(jnp.mean(values * values, axis=-1, keepdims=True) + EPSILON)
    return (values * factor * gain).astype(BF16)


def rope_tables(ctx_row, requests):
    diagonal = iota((requests, requests), 0) == iota((requests, requests), 1)
    ctx = jnp.broadcast_to(ctx_row.astype(F32), (requests, requests))
    ctx = jnp.sum(jnp.where(diagonal, ctx, 0.0), axis=1, keepdims=True)
    lane = iota((requests, LANES), 1)
    index = (lane % (HEAD_DIM // 2)).astype(F32)
    inverse = jnp.exp(index * (-2.0 * math.log(ROPE_BASE) / HEAD_DIM))
    angles = ctx * inverse
    sign = jnp.where(lane % HEAD_DIM < HEAD_DIM // 2, -1.0, 1.0)
    return jnp.cos(angles), jnp.sin(angles) * sign


def rotate(chunk, cosine, sine):
    lane = iota(chunk.shape, 1)
    ahead = pltpu.roll(chunk, LANES - HEAD_DIM // 2, 1)
    behind = pltpu.roll(chunk, HEAD_DIM // 2, 1)
    turned = jnp.where(lane % HEAD_DIM < HEAD_DIM // 2, ahead, behind)
    return chunk * cosine + turned * sine


def copy_of(source, target, sem):
    return pltpu.make_async_copy(source, target, sem)


def copies_of(source, target, sems, base):
    step = source.shape[0] // 4
    return [
        copy_of(
            source.at[pl.ds(i * step, step)], target.at[pl.ds(i * step, step)], sems.at[base + i]
        )
        for i in range(4)
    ]


def page_copies(cache_hbm, pages, stages, sems, base):
    copies = []
    for i, stage in enumerate(stages):
        rows = pl.ds(stage[0], len(stage))
        copies.append(copy_of(cache_hbm.at[rows], pages.at[rows], sems.at[base + i]))
    return copies


def page_stages(count, first, rest):
    starts = [0] + list(range(min(first, count), count, rest))
    return [range(a, b) for a, b in zip(starts, starts[1:] + [count])]


def prepare_kernel(
    pool, replicas, ids_ref, hidden_hbm, ctx_hbm, table_hbm, dest_hbm, attn_gain_hbm,
    wq_hbm, cache_hbm,
    hidden_ref, wq_ref, gain_ref, tables_ref, away_ref, span_ref, meta_ref, lent_ref,
    pick_ref, drop_ref,
    ctx, table, dest, gain, sems,
):
    inbox = replicas * CAP
    requests = ctx.shape[1]
    entries = meta_ref.shape[1]
    small = [
        copy_of(ctx_hbm, ctx, sems.at[0]),
        copy_of(table_hbm, table, sems.at[1]),
        copy_of(dest_hbm, dest, sems.at[2]),
        copy_of(attn_gain_hbm, gain, sems.at[3]),
    ]
    large = [copy_of(hidden_hbm, hidden_ref, sems.at[4])]
    large += copies_of(wq_hbm, wq_ref, sems, 5)
    lending = pl.ds(pool - lent_ref.shape[0], lent_ref.shape[0])
    large.append(copy_of(cache_hbm.at[lending], lent_ref, sems.at[9]))
    for copy in small + large:
        copy.start()
    for copy in small:
        copy.wait()
    gain_ref[...] = gain[...].reshape(1, gain.shape[0])
    ctx_row = ctx[...]

    def claims(values):
        held = jnp.zeros(values.shape, F32)
        spans = jnp.zeros(values.shape, F32)
        for k in range(table.shape[0]):
            match = table[k : k + 1, :] == values
            filled = jnp.clip(ctx_row - k * 128, 0, 128).astype(F32)
            held = jnp.where(match, 1.0, held)
            spans = jnp.where(match, filled, spans)
        return held.astype(BF16), spans

    held, spans = claims(iota((entries, requests), 0))
    numbers = (iota((SLOT, requests), 1) + 1).astype(BF16)
    ones = jnp.ones((SLOT, requests), BF16)
    holder = lax.dot_general(numbers, held, NT, preferred_element_type=F32)
    covered = lax.dot_general(ones, spans.astype(BF16), NT, preferred_element_type=F32)
    meta_ref[0:1, :] = holder[0:1, :].astype(jnp.int32) - 1
    meta_ref[1:2, :] = covered[0:1, :].astype(jnp.int32)
    meta_ref[2:3, :] = jnp.zeros((1, entries), jnp.int32)
    lent = dest.shape[1]
    across = jnp.broadcast_to(dest[...].astype(F32), (lent, lent))
    row, lane = iota((lent, lent), 0), iota((lent, lent), 1)
    down = jnp.sum(jnp.where(row == lane, across, 0.0), axis=1, keepdims=True)
    same = across == down
    before = jnp.sum(jnp.where(same & (lane < row), 1.0, 0.0), axis=1, keepdims=True)
    column = (replicas - 1 - down) * CAP + before
    column = jnp.broadcast_to(column, (lent, LANES)).astype(BF16)
    before = jnp.sum(jnp.where(same & (row < lane), 1.0, 0.0), axis=0, keepdims=True)
    line = dest[...] ^ replicas // 2
    line = jnp.broadcast_to(line.astype(F32), (lent, lent))
    line = (line * CAP + before).astype(BF16)
    expand = iota((lent * SLOT, lent), 0) // SLOT == iota((lent * SLOT, lent), 1)
    expand = jnp.where(expand, 1.0, 0.0).astype(BF16)
    column = jnp.dot(expand, column, preferred_element_type=F32).astype(jnp.int32)
    pick_ref[...] = column * SLOT + iota(column.shape, 0) % SLOT
    line = lax.dot_general(line, expand, NT, preferred_element_type=F32).astype(jnp.int32)
    drop_ref[...] = line * SLOT + iota(line.shape, 1) % SLOT
    meta_ref[3:4, :] = jnp.full((1, entries), ids_ref[0], jnp.int32)
    cosine, sine = rope_tables(ctx_row, requests)
    tables_ref[0] = cosine
    tables_ref[1] = sine
    slot = iota((inbox, requests), 0)
    lender = replicas - 1 - slot // CAP
    held, spans = claims(pool + lender * CAP + slot % CAP)
    away_ref[...] = held
    away_span = jnp.sum(spans, axis=1, keepdims=True)
    span_ref[...] = jnp.broadcast_to(away_span, span_ref.shape)
    for copy in large:
        copy.wait()


def query_kernel(
    count, meta_ref, *refs,
):
    pieces = refs[:count]
    (gain_ref, wq_ref, tables_ref, away_ref, span_ref,
     hidden_ref, normed_ref, packed_ref, send_ref, packs, sends) = refs[count:]
    requests = hidden_ref.shape[0]
    inbox = span_ref.shape[0]
    width = wq_ref.shape[1]
    chunks = -(-width // LANES)
    if count == 1:
        hidden = pieces[0][...]
    else:
        own, other = pieces[0][...], pieces[1][...]
        first = meta_ref[3:4, 0:1] == 0
        hidden = jnp.concatenate(
            [jnp.where(first, own, other), jnp.where(first, other, own)], axis=0
        )
    hidden_ref[...] = hidden
    normed = norm_rows(hidden.astype(F32), gain_ref[...])
    normed_ref[...] = normed
    queries = jnp.dot(normed, wq_ref[...], preferred_element_type=F32)
    if chunks * LANES > width:
        pad = jnp.zeros((requests, chunks * LANES - width), F32)
        queries = jnp.concatenate([queries, pad], axis=1)
    cosine, sine = tables_ref[0], tables_ref[1]
    zeros = jnp.zeros((requests, LANES), F32)
    nothing = jnp.zeros((inbox, LANES), F32)
    for j in range(SLOT):
        here = pl.ds(j, requests, stride=SLOT)
        there = pl.ds(j, inbox, stride=SLOT)
        if j < chunks:
            chunk = rotate(queries[:, j * LANES : (j + 1) * LANES], cosine, sine)
            chunk = (chunk.astype(BF16).astype(F32) * ATTN_SCALE).astype(BF16)
            packs[here, :] = chunk.astype(F32)
            sends[there, :] = jnp.dot(away_ref[...], chunk, preferred_element_type=F32)
        else:
            packs[here, :] = zeros
            sends[there, :] = span_ref[...] if j == META else nothing
    packed_ref[...] = packs[...]
    send_ref[...] = sends[...].astype(BF16)


def unpack(packed):
    low = iota(packed.shape, 1) < HEAD_DIM
    even = jnp.where(low, packed, 0.0)
    odd = jnp.where(low, pltpu.roll(packed, HEAD_DIM, 1), 0.0)
    return jnp.concatenate([even, odd], axis=0)


def head_rows(heads):
    return [(h // 2) + SLOT * (h % 2) for h in range(heads)]


def token_of_column(heads, kv_local, columns):
    row = iota((ROWS, columns), 0)
    column = iota((ROWS, columns), 1)
    wanted = jnp.full((ROWS, columns), kv_local, jnp.int32)
    for h, place in enumerate(head_rows(heads)):
        wanted = jnp.where(row == place, h // (heads // kv_local), wanted)
    return jnp.where(column % kv_local == wanted, column // kv_local, 1 << 20)


def score_page(query, block):
    return lax.dot_general(query, block, NT, preferred_element_type=F32)


def weigh_page(scores, tokens, span):
    scores = jnp.where(tokens < span, scores, NEG_FILL)
    top = jnp.max(scores, axis=1, keepdims=True)
    weights = jnp.exp(scores - top)
    return top, jnp.sum(weights, axis=1, keepdims=True), weights.astype(BF16)


def attend_pages(
    stages, copies, query_of, block_of, span_of, tokens, keep, last=None
):
    def score_stage(i):
        if copies is not None:
            copies[i].wait()
        if last is not None and i == len(stages) - 1:
            last.wait()
        return {p: score_page(query_of(p), block_of(p)) for p in stages[i]}

    scores = score_stage(0)
    for i, pages in enumerate(stages):
        if i + 1 < len(stages):
            ahead = score_stage(i + 1)
        weighed = {p: weigh_page(scores[p], tokens, span_of(p)) for p in pages}
        outs = {
            p: jnp.dot(weighed[p][2], block_of(p), preferred_element_type=F32)
            for p in pages
        }
        for p in pages:
            keep(p, weighed[p][0], weighed[p][1], outs[p])
        if i + 1 < len(stages):
            scores = ahead


def spread_queries(target, packed):
    low = iota(packed.shape, 2) < HEAD_DIM
    target[:, 0:SLOT, :] = jnp.where(low, packed, 0.0)
    target[:, SLOT:ROWS, :] = jnp.where(low, pltpu.roll(packed, HEAD_DIM, 2), 0.0)


def merge_pages(places, top_of, sum_of, top, acc, scaled, start, before):
    requests = start.shape[0]
    for p, place in enumerate(places):
        top[place] = jnp.maximum(top[place], top_of(p))
    acc[0:requests] = start * jnp.exp(before - top[0:requests])
    for p, place in enumerate(places):
        scaled[p] = sum_of(p) * jnp.exp(top_of(p) - top[place])
    for p, place in enumerate(places):
        acc[place] = acc[place] + scaled[p]


def project_heads(values, weights_ref, heads):
    if heads == 1:
        return jnp.dot(values, weights_ref[...], preferred_element_type=F32)
    rows, depth = values.shape
    wide = 1024
    part = wide // heads
    repeat = iota((part, wide), 1) // heads == iota((part, wide), 0)
    repeat = jnp.where(repeat, 1.0, 0.0).astype(BF16)
    parts = [values[:, i : i + part] for i in range(0, depth, part)]
    spread = jnp.dot(
        jnp.concatenate(parts, axis=0), repeat, preferred_element_type=F32
    ).astype(BF16)
    lane = iota((1, wide), 1) % heads
    masks = [jnp.where(lane == k, 1.0, 0.0).astype(BF16) for k in range(heads)]
    total = jnp.zeros((heads * rows, LANES), F32)
    for i in range(len(parts)):
        piece = spread[i * rows : (i + 1) * rows]
        piece = jnp.concatenate([piece * mask for mask in masks], axis=0)
        total += jnp.dot(
            piece, weights_ref[i * wide : (i + 1) * wide, :], preferred_element_type=F32
        )
    return total


def local_kernel(
    heads, kv_local, meta_hbm, packed_hbm, normed_hbm, wkv_hbm, tables_hbm, cache_hbm,
    state_hbm,
    meta, packed, normed, raw, tables, pages, queries, fresh, tops, sums, top, acc,
    scaled, sems,
):
    requests = normed.shape[0]
    count, columns, _ = pages.shape
    small = [
        copy_of(meta_hbm, meta, sems.at[0]),
        copy_of(packed_hbm, packed, sems.at[1]),
        copy_of(normed_hbm, normed, sems.at[2]),
        copy_of(tables_hbm, tables, sems.at[3]),
    ]
    weights = copy_of(wkv_hbm, raw, sems.at[4])
    stages = page_stages(count, 8, 8)
    paging = page_copies(cache_hbm, pages, stages, sems, 10)
    for copy in small + paging + [weights]:
        copy.start()
    tokens = token_of_column(heads, kv_local, columns)
    lower = iota((ROWS, LANES), 1) < HEAD_DIM
    low = iota((requests, LANES), 1) < HEAD_DIM
    low16 = iota((requests, ROWS, LANES), 2) < HEAD_DIM
    top[...] = jnp.full(top.shape, NEG_FILL, F32)
    acc[...] = jnp.zeros(acc.shape, F32)
    for copy in small:
        copy.wait()
    spread_queries(queries, packed[...].reshape(requests, SLOT, LANES))

    def place_of(p):
        owner = meta[0, p]
        return jnp.where(owner < 0, requests, owner)

    places = [place_of(p) for p in range(count)]

    def keep(p, page_top, total, out):
        tops[p] = jnp.broadcast_to(page_top, (ROWS, LANES))
        sums[p] = jnp.where(lower, total, out)
        top[places[p]] = jnp.maximum(top[places[p]], tops[p])

    attend_pages(
        stages,
        paging,
        lambda p: queries[jnp.maximum(meta[0, p], 0)].astype(BF16),
        lambda p: pages[p],
        lambda p: meta[1, p],
        tokens,
        keep,
        weights,
    )
    cosine = jnp.where(low, tables[0], 1.0)
    sine = jnp.where(low, tables[1], 0.0)
    projected = project_heads(normed[...], raw, kv_local)
    new = [
        rotate(projected[k * requests : (k + 1) * requests], cosine, sine)
        .astype(BF16)
        .astype(F32)
        for k in range(kv_local)
    ]
    used = {place: h for h, place in enumerate(head_rows(heads))}
    for place in range(ROWS):
        value = jnp.zeros((requests, LANES), F32)
        if place in used:
            value = new[used[place] // (heads // kv_local)]
        fresh[pl.ds(place, requests, stride=ROWS), :] = value
    for p, place in enumerate(places):
        scaled[p] = sums[p] * jnp.exp(tops[p] - top[place])
    for p, place in enumerate(places):
        acc[place] = acc[place] + scaled[p]
    added = fresh[...].reshape(requests, ROWS, LANES)
    score = jnp.sum(queries[...] * added, axis=2, keepdims=True)
    score = jnp.broadcast_to(score, added.shape)
    parked = []
    step = requests // 4
    for i in range(4):
        rows = slice(i * step, (i + 1) * step)
        before, fresh_score = top[rows], score[rows]
        highest = jnp.maximum(before, fresh_score)
        whole = acc[rows] * jnp.exp(before - highest)
        whole += jnp.where(low16[rows], 1.0, added[rows]) * jnp.exp(fresh_score - highest)
        acc[rows] = jnp.where(
            low16[rows], highest + jnp.log(whole), whole / pltpu.roll(whole, HEAD_DIM, 2)
        )
        part = pl.ds(i * step, step)
        parked.append(copy_of(acc.at[part], state_hbm.at[part], sems.at[5 + i]))
        parked[i].start()
    for copy in parked:
        copy.wait()


def lent_kernel(
    heads, kv_local, asked_ref, pages, pick_ref, drop_ref, meta_ref, packed_ref,
    normed_ref, tables_ref, hidden_ref,
    reply_hbm, meta_hbm, packed_hbm, normed_hbm, tables_hbm, hidden_hbm,
    reply16, sems,
):
    outgoing, columns, _ = pages.shape
    parked = [
        copy_of(packed_ref, packed_hbm, sems.at[0]),
        copy_of(normed_ref, normed_hbm, sems.at[1]),
        copy_of(hidden_ref, hidden_hbm, sems.at[2]),
        copy_of(tables_ref, tables_hbm, sems.at[3]),
        copy_of(meta_ref, meta_hbm, sems.at[4]),
    ]
    for copy in parked:
        copy.start()
    slot_rows = asked_ref.shape[0]
    shape = (outgoing * SLOT, slot_rows)
    chosen = jnp.where(pick_ref[:, 0:1] == iota(shape, 1), 1.0, 0.0).astype(BF16)
    asked = jnp.dot(chosen, asked_ref[...], preferred_element_type=F32)
    tokens = token_of_column(heads, kv_local, columns).astype(F32)
    low = iota((SLOT, LANES), 1) < HEAD_DIM
    lane = iota((SLOT, LANES), 1)
    row = iota((SLOT, LANES), 0)

    def terms(total, offset):
        leading = total.astype(BF16).astype(F32)
        rest = total - leading
        second = rest.astype(BF16).astype(F32)
        third = rest - second
        spot = lane - offset - 3 * row
        placed = jnp.where(spot == 0, leading, 0.0)
        placed = jnp.where(spot == 1, second, placed)
        return jnp.where(spot == 2, third, placed)

    packed = [asked[j * SLOT : (j + 1) * SLOT] for j in range(outgoing)]
    replies = {}

    def keep(j, top, total, out):
        out = out / total
        logs = top + jnp.log(total)
        even = pltpu.roll(out[0:SLOT], HEAD_DIM, 1)
        both = jnp.where(low, even, out[SLOT:ROWS])
        line = jnp.sum(
            terms(logs[0:SLOT], 0) + terms(logs[SLOT:ROWS], HEAD_DIM), axis=0, keepdims=True
        )
        replies[j] = jnp.where(row == META, line, both)

    attend_pages(
        page_stages(outgoing, 8, 8),
        None,
        lambda j: unpack(packed[j]).astype(BF16),
        lambda j: pages[j],
        lambda j: packed[j][META : META + 1, 0:1],
        tokens,
        keep,
    )
    shape = (slot_rows, outgoing * SLOT)
    placed = jnp.where(drop_ref[0:1, :] == iota(shape, 0), 1.0, 0.0).astype(BF16)
    every = jnp.concatenate([replies[j] for j in range(outgoing)], axis=0).astype(BF16)
    reply = jnp.dot(placed, every, preferred_element_type=F32)
    reply16[...] = reply.astype(BF16)
    replying = copy_of(reply16, reply_hbm, sems.at[5])
    replying.start()
    for copy in parked + [replying]:
        copy.wait()


def combine_kernel(
    heads, pool, meta_hbm, state_hbm, wo_hbm, hidden_hbm, gain_hbm, router_hbm,
    routes_hbm, wd_hbm, reply_ref,
    part_ref, meta_ref, hidden_ref, gain_ref, router_ref, routes_ref, wd_ref,
    meta, state, wo, gain, tops, accs, scaled, reply, finals, sems,
):
    requests = state.shape[0]
    inbox = reply_ref.shape[0] // SLOT
    chunks = -(-heads // 2)
    numbers = copy_of(meta_hbm, meta, sems.at[11])
    arriving = copy_of(state_hbm, state, sems.at[0])
    weights = copies_of(wo_hbm, wo, sems, 1)
    gaining = copy_of(gain_hbm, gain, sems.at[5])
    later = [
        copy_of(meta_hbm, meta_ref, sems.at[6]),
        copy_of(hidden_hbm, hidden_ref, sems.at[7]),
        copy_of(router_hbm, router_ref, sems.at[8]),
        copy_of(routes_hbm, routes_ref, sems.at[9]),
        copy_of(wd_hbm.at[pl.ds(0, wd_ref.shape[0])], wd_ref, sems.at[10]),
    ]
    for copy in [numbers, arriving] + weights + [gaining] + later:
        copy.start()
    reply[...] = reply_ref[...].astype(F32)
    tops[...] = jnp.full(tops.shape, NEG_FILL, F32)
    accs[...] = jnp.zeros(accs.shape, F32)
    low = iota((SLOT, LANES), 1) < HEAD_DIM
    lane = iota((SLOT, LANES), 1)
    row = iota((SLOT, LANES), 0)
    mine = (lane % HEAD_DIM) // 3 == row

    def place_of(s):
        lender = s // CAP ^ (inbox // CAP // 2)
        owner = meta[0, pool + lender * CAP + s % CAP]
        return jnp.where(owner < 0, requests, owner)

    def logs_of(s):
        line = reply[s * SLOT + META : s * SLOT + META + 1, :]
        line = jnp.where(mine, jnp.broadcast_to(line, (SLOT, LANES)), 0.0)
        even = jnp.sum(jnp.where(low, line, 0.0), axis=1, keepdims=True)
        odd = jnp.sum(jnp.where(low, 0.0, line), axis=1, keepdims=True)
        logs = jnp.concatenate([even, odd], axis=0)
        return jnp.broadcast_to(logs, (ROWS, LANES))

    def sum_of(s):
        packed = reply[s * SLOT : (s + 1) * SLOT, :]
        even = jnp.where(low, 1.0, pltpu.roll(packed, HEAD_DIM, 1))
        odd = jnp.where(low, 1.0, packed)
        return jnp.concatenate([even, odd], axis=0)

    logs = [logs_of(s) for s in range(inbox)]
    numbers.wait()
    places = [place_of(s) for s in range(inbox)]
    for s, place in enumerate(places):
        tops[place] = jnp.maximum(tops[place], logs[s])
    for s, place in enumerate(places):
        scaled[s] = sum_of(s) * jnp.exp(logs[s] - tops[place])
    for s, place in enumerate(places):
        accs[place] = accs[place] + scaled[s]
    arriving.wait()
    low16 = iota(state.shape, 2) < HEAD_DIM
    start = state[...]
    before = jnp.where(low16, start, pltpu.roll(start, HEAD_DIM, 2))
    remote = tops[0:requests]
    highest = jnp.maximum(before, remote)
    whole = accs[0:requests] * jnp.exp(remote - highest)
    whole = whole + jnp.where(low16, 1.0, start) * jnp.exp(before - highest)
    finals[...] = (whole / pltpu.roll(whole, HEAD_DIM, 2)).reshape(
        requests * ROWS, LANES
    )
    wide = iota((requests, LANES), 1) < HEAD_DIM
    parts = []
    for j in range(chunks):
        even = finals[pl.ds(j, requests, stride=ROWS), :]
        odd = finals[pl.ds(SLOT + j, requests, stride=ROWS), :]
        parts.append(jnp.where(wide, pltpu.roll(even, HEAD_DIM, 1), odd).astype(BF16))
    attention = jnp.concatenate(parts, axis=1)[:, : heads * HEAD_DIM]
    for copy in weights:
        copy.wait()
    part_ref[...] = jnp.dot(attention, wo[...], preferred_element_type=F32).astype(BF16)
    gaining.wait()
    gain_ref[...] = gain[...].reshape(1, gain.shape[0])
    for copy in later:
        copy.wait()


def load_kernel(wd_hbm, order_hbm, wd_ref, sem):
    del order_hbm
    rows = wd_ref.shape[0]
    copy = copy_of(wd_hbm.at[pl.ds(wd_hbm.shape[0] - rows, rows)], wd_ref, sem)
    copy.start()
    copy.wait()


def finish_kernel(attended_ref, own_ref, other_ref, attended_out, experts_out):
    attended_out[...] = attended_ref[...]
    experts_out[...] = (own_ref[...] + other_ref[...].astype(F32)).astype(BF16)


def own_rows(values, first):
    half = values.shape[0] // 2
    return jnp.where(first, values[:half], values[half:])


def residual_kernel(
    tp, count, meta_ref, hidden_ref, *refs,
):
    pieces = refs[:count]
    gain_ref, attended_ref, input_ref, again_ref = refs[count:]
    requests = hidden_ref.shape[0]
    if count == 2:
        summed = pieces[0][...].astype(F32) + pieces[1][...].astype(F32)
    else:
        summed = pieces[0][0:requests, :].astype(F32)
        for t in range(1, tp):
            part = pieces[0][t * requests : (t + 1) * requests, :]
            summed = summed + part.astype(F32)
    attended = (hidden_ref[...].astype(F32) + RESID_SCALE * summed).astype(BF16)
    if count == 2:
        attended_ref[...] = own_rows(attended, meta_ref[3:4, 0:1] == 0)
    else:
        attended_ref[...] = attended
    ffn_input = norm_rows(attended.astype(F32), gain_ref[...])
    input_ref[...] = ffn_input
    again_ref[...] = ffn_input


def gate_column(units, meta_ref, input_ref, router_ref, routes_ref):
    ffn_input = input_ref[...]
    requests = ffn_input.shape[0]
    logits = lax.dot_general(router_ref[...], ffn_input, NT, preferred_element_type=F32)
    expert = iota(logits.shape, 0)
    named = jnp.zeros(logits.shape, F32)
    for k in range(routes_ref.shape[0]):
        named = jnp.where(routes_ref[k : k + 1, :] == expert, 1.0, named)
    chosen = named > 0.5
    top = jnp.max(jnp.where(chosen, logits, NEG_FILL), axis=0, keepdims=True)
    weights = jnp.where(chosen, jnp.exp(logits - top), 0.0)
    total = jnp.sum(weights, axis=0, keepdims=True)
    mine = expert == meta_ref[3:4, 0:1] * units // FF
    line = jnp.sum(jnp.where(mine, weights, 0.0), axis=0, keepdims=True) / total
    diagonal = iota((requests, requests), 0) == iota((requests, requests), 1)
    line = jnp.where(diagonal, jnp.broadcast_to(line, (requests, requests)), 0.0)
    return jnp.sum(line, axis=1, keepdims=True)


def expert_kernel(
    units, meta_ref, lifted_ref, input_ref, router_ref, routes_ref, wd_ref, wd_rest_ref,
    *outs
):
    column = gate_column(units, meta_ref, input_ref, router_ref, routes_ref)
    gate = lifted_ref[0]
    active = gate / (1.0 + jnp.exp(-gate)) * lifted_ref[1]
    active = active.astype(BF16)
    half = wd_ref.shape[0]
    share = jnp.dot(active[:, :half], wd_ref[...], preferred_element_type=F32)
    share += jnp.dot(active[:, half:], wd_rest_ref[...], preferred_element_type=F32)
    share *= column
    if len(outs) == 2:
        first = meta_ref[3:4, 0:1] == 0
        outs[0][...] = own_rows(share, first)
        outs[1][...] = own_rows(share, jnp.logical_not(first)).astype(BF16)
    else:
        outs[0][...] = share.astype(BF16)


def call(body, outs, in_specs, scratch=(), limit=16, flops=0, moved=0):
    return pl.pallas_call(
        body,
        out_shape=outs,
        in_specs=in_specs,
        out_specs=[VMEM if isinstance(o, jax.ShapeDtypeStruct) else HBM for o in outs],
        scratch_shapes=list(scratch),
        compiler_params=pltpu.CompilerParams(vmem_limit_bytes=limit << 20),
        cost_estimate=pl.CostEstimate(
            flops=flops, bytes_accessed=moved, transcendentals=0
        ),
    )


def swap(values):
    return lax.ppermute(values, "tensor", [(0, 1), (1, 0)])


def on_device(
    hidden,
    attn_gain,
    w_query,
    w_keyvalue,
    w_output,
    cache,
    page_table,
    ctx_len,
    move_dest,
    ffn_gain,
    router,
    routes,
    w_in,
    w_down,
):
    replicas = lax.axis_size("replica")
    tp = lax.axis_size("tensor")
    rank = lax.axis_index("tensor").astype(jnp.int32)
    rows, width = hidden.shape
    pool, page_len, kv_local, _ = cache.shape
    outgoing = move_dest.shape[0]
    local_pages = pool - outgoing
    requests = page_table.shape[0]
    heads = w_query.shape[1] // HEAD_DIM
    inbox = replicas * CAP
    units = w_down.shape[0]
    assert FF % units == 0
    columns = page_len * kv_local
    entries = -(-(pool + inbox) // LANES) * LANES
    struct = jax.ShapeDtypeStruct
    pair = tp == 2
    ids = rank.reshape(1)

    def pin(values):
        return pltpu.with_memory_space_constraint(values, pltpu.HBM)

    def exchange(blocks, order):
        blocks = blocks.reshape(replicas, CAP * SLOT, LANES)
        blocks = lax.all_to_all(
            blocks,
            "replica",
            split_axis=0,
            concat_axis=0,
            tiled=True,
            axis_index_groups=[list(order)],
        )
        return blocks.reshape(inbox * SLOT, LANES)

    blocks = pin(cache.reshape(pool, columns, LANES))
    if pair:
        pieces = [hidden, swap(hidden)]
    else:
        pieces = [lax.all_gather(hidden, "tensor", axis=0, tiled=True)]
    meta_shape = (4, entries)
    tables_shape = (2, requests, LANES)
    own, wq, gain, tables, away, away_span, meta, lent, pick, drop = call(
        functools.partial(prepare_kernel, pool, replicas),
        [
            struct(hidden.shape, BF16),
            struct(w_query.shape, BF16),
            struct((1, width), F32),
            struct(tables_shape, F32),
            struct((inbox, requests), BF16),
            struct((inbox, LANES), F32),
            struct(meta_shape, jnp.int32),
            struct((outgoing, columns, LANES), BF16),
            struct((outgoing * SLOT, LANES), jnp.int32),
            struct((outgoing, outgoing * SLOT), jnp.int32),
        ],
        [SMEM] + [HBM] * 7,
        [
            pltpu.VMEM((1, requests), jnp.int32),
            pltpu.VMEM((page_table.shape[1], requests), jnp.int32),
            pltpu.VMEM((1, outgoing), jnp.int32),
            pltpu.VMEM((width,), F32),
            pltpu.SemaphoreType.DMA((10,)),
        ],
        moved=2 * w_query.size,
    )(
        ids,
        pin(hidden),
        pin(ctx_len.reshape(1, requests)),
        pin(page_table.T),
        pin(move_dest.reshape(1, outgoing)),
        pin(attn_gain),
        pin(w_query),
        blocks,
    )
    if pair:
        pieces[0] = own
    hidden_all, normed, packed, sends = call(
        functools.partial(query_kernel, len(pieces)),
        [
            struct((requests, width), BF16),
            struct((requests, width), BF16),
            struct((requests * SLOT, LANES), F32),
            struct((inbox * SLOT, LANES), BF16),
        ],
        [VMEM] * (len(pieces) + 6),
        [
            pltpu.VMEM((requests * SLOT, LANES), F32),
            pltpu.VMEM((inbox * SLOT, LANES), F32),
        ],
        flops=4 * requests * width * w_query.shape[1],
        moved=2 * w_query.size,
    )(meta, *pieces, gain, wq, tables, away, away_span)
    asked = exchange(sends, range(replicas)[::-1])
    replies, meta_far, packed_far, normed_far, tables_far, hidden_far = call(
        functools.partial(lent_kernel, heads, kv_local),
        [
            pltpu.HBM((inbox * SLOT, LANES), BF16),
            pltpu.HBM(meta_shape, jnp.int32),
            pltpu.HBM((requests * SLOT, LANES), F32),
            pltpu.HBM((requests, width), BF16),
            pltpu.HBM(tables_shape, F32),
            pltpu.HBM((requests, width), BF16),
        ],
        [VMEM] * 9,
        [
            pltpu.VMEM((inbox * SLOT, LANES), BF16),
            pltpu.SemaphoreType.DMA((6,)),
        ],
        flops=4 * ROWS * columns * LANES * outgoing,
        moved=2 * columns * LANES * outgoing,
    )(asked, lent, pick, drop, meta, packed, normed, tables, hidden_all)
    returned = exchange(replies, [r ^ replicas // 2 for r in range(replicas)])
    (state,) = call(
        functools.partial(local_kernel, heads, kv_local),
        [pltpu.HBM((requests, ROWS, LANES), F32)],
        [HBM] * 6,
        [
            pltpu.SMEM(meta_shape, jnp.int32),
            pltpu.VMEM((requests * SLOT, LANES), F32),
            pltpu.VMEM((requests, width), BF16),
            pltpu.VMEM((width * kv_local, LANES), BF16),
            pltpu.VMEM(tables_shape, F32),
            pltpu.VMEM((local_pages, columns, LANES), BF16),
            pltpu.VMEM((requests, ROWS, LANES), F32),
            pltpu.VMEM((requests * ROWS, LANES), F32),
            pltpu.VMEM((local_pages, ROWS, LANES), F32),
            pltpu.VMEM((local_pages, ROWS, LANES), F32),
            pltpu.VMEM((requests + 1, ROWS, LANES), F32),
            pltpu.VMEM((requests + 1, ROWS, LANES), F32),
            pltpu.VMEM((local_pages, ROWS, LANES), F32),
            pltpu.SemaphoreType.DMA((10 + local_pages,)),
        ],
        limit=24,
        flops=4 * ROWS * columns * LANES * local_pages,
        moved=2 * columns * LANES * local_pages,
    )(
        pin(meta_far),
        pin(packed_far),
        pin(normed_far),
        pin(w_keyvalue.reshape(width * kv_local, LANES)),
        pin(tables_far),
        blocks,
    )
    half = struct((units // 2, width), BF16)
    part, meta, hidden_all, gain, router_t, routes_t, wd = call(
        functools.partial(combine_kernel, heads, pool),
        [
            struct((requests, width), BF16),
            struct(meta_shape, jnp.int32),
            struct((requests, width), BF16),
            struct((1, width), F32),
            struct(router.shape[::-1], BF16),
            struct(routes.shape[::-1], jnp.int32),
            half,
        ],
        [HBM] * 8 + [VMEM],
        [
            pltpu.SMEM(meta_shape, jnp.int32),
            pltpu.VMEM((requests, ROWS, LANES), F32),
            pltpu.VMEM(w_output.shape, BF16),
            pltpu.VMEM((width,), F32),
            pltpu.VMEM((requests + 1, ROWS, LANES), F32),
            pltpu.VMEM((requests + 1, ROWS, LANES), F32),
            pltpu.VMEM((inbox, ROWS, LANES), F32),
            pltpu.VMEM((inbox * SLOT, LANES), F32),
            pltpu.VMEM((requests * ROWS, LANES), F32),
            pltpu.SemaphoreType.DMA((12,)),
        ],
        flops=2 * requests * w_output.size,
        moved=2 * w_output.size,
    )(
        pin(meta_far), pin(state), pin(w_output), pin(hidden_far), pin(ffn_gain),
        pin(router.T), pin(routes.T), pin(w_down), returned,
    )
    if pair:
        parts = [part, swap(part)]
    else:
        parts = [lax.all_gather(part, "tensor", axis=0, tiled=True)]
    (wd_rest,) = call(
        load_kernel,
        [half],
        [HBM, ANY],
        [pltpu.SemaphoreType.DMA],
        moved=w_down.size,
    )(pin(w_down), part)
    attended, ffn_input, ffn_again = call(
        functools.partial(residual_kernel, tp, len(parts)),
        [
            struct((rows if pair else requests, width), BF16),
            struct((requests, width), BF16),
            struct((requests, width), BF16),
        ],
        [VMEM] * (len(parts) + 3),
        flops=2 * requests * width,
        moved=8 * requests * width,
    )(meta, hidden_all, *parts, gain)
    lifted = jnp.einsum("rd,dsu->sru", ffn_input, w_in, preferred_element_type=F32)
    shapes = [struct((requests, width), BF16)]
    if pair:
        shapes = [struct((rows, width), F32), struct((rows, width), BF16)]
    shares = call(
        functools.partial(expert_kernel, units),
        shapes,
        [VMEM] * 7,
        flops=2 * requests * w_down.size,
        moved=2 * w_down.size,
    )(meta, lifted, ffn_again, router_t, routes_t, wd, wd_rest)
    if pair:
        out = struct((rows, width), BF16)
        return tuple(
            call(finish_kernel, [out, out], [VMEM] * 3)(attended, shares[0], swap(shares[1]))
        )
    shares = lax.all_gather(shares[0], "tensor", axis=0)
    mine = lax.dynamic_slice_in_dim(shares, rank * rows, rows, axis=1)
    experts_out = jnp.sum(mine.astype(F32), axis=0).astype(BF16)
    attended = lax.dynamic_slice_in_dim(attended, rank * rows, rows, axis=0)
    return attended, experts_out


def solution(mesh):
    placed = (
        P(("replica", "tensor"), None),
        P(),
        P(None, "tensor"),
        P(None, "tensor", None),
        P("tensor", None),
        P("replica", None, "tensor", None),
        P("replica", None),
        P("replica"),
        P("replica"),
        P(),
        P(),
        P("replica", None),
        P(None, None, "tensor"),
        P("tensor", None),
    )
    return jax.shard_map(
        on_device,
        mesh=mesh,
        in_specs=placed,
        out_specs=(P(("replica", "tensor"), None), P(("replica", "tensor"), None)),
        check_vma=False,
    )
```

```python
import functools
import math

import jax
import jax.numpy as jnp
from jax import lax
from jax.experimental import pallas as pl
from jax.experimental.pallas import tpu as pltpu
from jax.sharding import PartitionSpec as P

HEAD_DIM = 64
EXPERTS = 40
FF = 512
CAP = 2
LANES = 128
SLOT = 8
ROWS = 16
META = 6

ATTN_SCALE = 0.015625
RESID_SCALE = 0.22
ROPE_BASE = 10000.0
EPSILON = 1e-06
NEG_FILL = -1e30

F32 = jnp.float32
BF16 = jnp.bfloat16
VMEM = pl.BlockSpec(memory_space=pltpu.VMEM)
SMEM = pl.BlockSpec(memory_space=pltpu.SMEM)
ANY = pl.BlockSpec(memory_space=pl.ANY)
HBM = pl.BlockSpec(memory_space=pltpu.HBM)
NT = (((1,), (1,)), ((), ()))


def iota(shape, axis):
    return lax.broadcasted_iota(jnp.int32, shape, axis)


def norm_rows(values, gain):
    factor = lax.rsqrt(jnp.mean(values * values, axis=-1, keepdims=True) + EPSILON)
    return (values * factor * gain).astype(BF16)


def rope_tables(ctx_row, requests):
    diagonal = iota((requests, requests), 0) == iota((requests, requests), 1)
    ctx = jnp.broadcast_to(ctx_row.astype(F32), (requests, requests))
    ctx = jnp.sum(jnp.where(diagonal, ctx, 0.0), axis=1, keepdims=True)
    lane = iota((requests, LANES), 1)
    index = (lane % (HEAD_DIM // 2)).astype(F32)
    inverse = jnp.exp(index * (-2.0 * math.log(ROPE_BASE) / HEAD_DIM))
    angles = ctx * inverse
    sign = jnp.where(lane % HEAD_DIM < HEAD_DIM // 2, -1.0, 1.0)
    return jnp.cos(angles), jnp.sin(angles) * sign


def rotate(chunk, cosine, sine):
    lane = iota(chunk.shape, 1)
    ahead = pltpu.roll(chunk, LANES - HEAD_DIM // 2, 1)
    behind = pltpu.roll(chunk, HEAD_DIM // 2, 1)
    turned = jnp.where(lane % HEAD_DIM < HEAD_DIM // 2, ahead, behind)
    return chunk * cosine + turned * sine


def copy_of(source, target, sem):
    return pltpu.make_async_copy(source, target, sem)


def copies_of(source, target, sems, base):
    step = source.shape[0] // 4
    return [
        copy_of(
            source.at[pl.ds(i * step, step)], target.at[pl.ds(i * step, step)], sems.at[base + i]
        )
        for i in range(4)
    ]


def page_copies(cache_hbm, pages, stages, sems, base):
    copies = []
    for i, stage in enumerate(stages):
        rows = pl.ds(stage[0], len(stage))
        copies.append(copy_of(cache_hbm.at[rows], pages.at[rows], sems.at[base + i]))
    return copies


def page_stages(count, first, rest):
    starts = [0] + list(range(min(first, count), count, rest))
    return [range(a, b) for a, b in zip(starts, starts[1:] + [count])]


def prepare_kernel(
    pool, replicas, ids_ref, hidden_hbm, ctx_hbm, table_hbm, dest_hbm, attn_gain_hbm,
    wq_hbm, cache_hbm,
    hidden_ref, wq_ref, gain_ref, tables_ref, away_ref, span_ref, meta_ref, lent_ref,
    pick_ref, drop_ref,
    ctx, table, dest, gain, sems,
):
    inbox = replicas * CAP
    requests = ctx.shape[1]
    entries = meta_ref.shape[1]
    small = [
        copy_of(ctx_hbm, ctx, sems.at[0]),
        copy_of(table_hbm, table, sems.at[1]),
        copy_of(dest_hbm, dest, sems.at[2]),
        copy_of(attn_gain_hbm, gain, sems.at[3]),
    ]
    large = [copy_of(hidden_hbm, hidden_ref, sems.at[4])]
    large += copies_of(wq_hbm, wq_ref, sems, 5)
    lending = pl.ds(pool - lent_ref.shape[0], lent_ref.shape[0])
    large.append(copy_of(cache_hbm.at[lending], lent_ref, sems.at[9]))
    for copy in small + large:
        copy.start()
    for copy in small:
        copy.wait()
    gain_ref[...] = gain[...].reshape(1, gain.shape[0])
    ctx_row = ctx[...]

    def claims(values):
        held = jnp.zeros(values.shape, F32)
        spans = jnp.zeros(values.shape, F32)
        for k in range(table.shape[0]):
            match = table[k : k + 1, :] == values
            filled = jnp.clip(ctx_row - k * 128, 0, 128).astype(F32)
            held = jnp.where(match, 1.0, held)
            spans = jnp.where(match, filled, spans)
        return held.astype(BF16), spans

    held, spans = claims(iota((entries, requests), 0))
    numbers = (iota((SLOT, requests), 1) + 1).astype(BF16)
    ones = jnp.ones((SLOT, requests), BF16)
    holder = lax.dot_general(numbers, held, NT, preferred_element_type=F32)
    covered = lax.dot_general(ones, spans.astype(BF16), NT, preferred_element_type=F32)
    meta_ref[0:1, :] = holder[0:1, :].astype(jnp.int32) - 1
    meta_ref[1:2, :] = covered[0:1, :].astype(jnp.int32)
    meta_ref[2:3, :] = jnp.zeros((1, entries), jnp.int32)
    lent = dest.shape[1]
    across = jnp.broadcast_to(dest[...].astype(F32), (lent, lent))
    row, lane = iota((lent, lent), 0), iota((lent, lent), 1)
    down = jnp.sum(jnp.where(row == lane, across, 0.0), axis=1, keepdims=True)
    same = across == down
    before = jnp.sum(jnp.where(same & (lane < row), 1.0, 0.0), axis=1, keepdims=True)
    column = (replicas - 1 - down) * CAP + before
    column = jnp.broadcast_to(column, (lent, LANES)).astype(BF16)
    before = jnp.sum(jnp.where(same & (row < lane), 1.0, 0.0), axis=0, keepdims=True)
    line = dest[...] ^ replicas // 2
    line = jnp.broadcast_to(line.astype(F32), (lent, lent))
    line = (line * CAP + before).astype(BF16)
    expand = iota((lent * SLOT, lent), 0) // SLOT == iota((lent * SLOT, lent), 1)
    expand = jnp.where(expand, 1.0, 0.0).astype(BF16)
    column = jnp.dot(expand, column, preferred_element_type=F32).astype(jnp.int32)
    pick_ref[...] = column * SLOT + iota(column.shape, 0) % SLOT
    line = lax.dot_general(line, expand, NT, preferred_element_type=F32).astype(jnp.int32)
    drop_ref[...] = line * SLOT + iota(line.shape, 1) % SLOT
    meta_ref[3:4, :] = jnp.full((1, entries), ids_ref[0], jnp.int32)
    cosine, sine = rope_tables(ctx_row, requests)
    tables_ref[0] = cosine
    tables_ref[1] = sine
    slot = iota((inbox, requests), 0)
    lender = replicas - 1 - slot // CAP
    held, spans = claims(pool + lender * CAP + slot % CAP)
    away_ref[...] = held
    away_span = jnp.sum(spans, axis=1, keepdims=True)
    span_ref[...] = jnp.broadcast_to(away_span, span_ref.shape)
    for copy in large:
        copy.wait()


def query_kernel(
    count, meta_ref, *refs,
):
    pieces = refs[:count]
    (gain_ref, wq_ref, tables_ref, away_ref, span_ref,
     hidden_ref, normed_ref, packed_ref, send_ref, packs, sends) = refs[count:]
    requests = hidden_ref.shape[0]
    inbox = span_ref.shape[0]
    width = wq_ref.shape[1]
    chunks = -(-width // LANES)
    if count == 1:
        hidden = pieces[0][...]
    else:
        own, other = pieces[0][...], pieces[1][...]
        first = meta_ref[3:4, 0:1] == 0
        hidden = jnp.concatenate(
            [jnp.where(first, own, other), jnp.where(first, other, own)], axis=0
        )
    hidden_ref[...] = hidden
    normed = norm_rows(hidden.astype(F32), gain_ref[...])
    normed_ref[...] = normed
    queries = jnp.dot(normed, wq_ref[...], preferred_element_type=F32)
    if chunks * LANES > width:
        pad = jnp.zeros((requests, chunks * LANES - width), F32)
        queries = jnp.concatenate([queries, pad], axis=1)
    cosine, sine = tables_ref[0], tables_ref[1]
    zeros = jnp.zeros((requests, LANES), F32)
    nothing = jnp.zeros((inbox, LANES), F32)
    for j in range(SLOT):
        here = pl.ds(j, requests, stride=SLOT)
        there = pl.ds(j, inbox, stride=SLOT)
        if j < chunks:
            chunk = rotate(queries[:, j * LANES : (j + 1) * LANES], cosine, sine)
            chunk = (chunk.astype(BF16).astype(F32) * ATTN_SCALE).astype(BF16)
            packs[here, :] = chunk.astype(F32)
            sends[there, :] = jnp.dot(away_ref[...], chunk, preferred_element_type=F32)
        else:
            packs[here, :] = zeros
            sends[there, :] = span_ref[...] if j == META else nothing
    packed_ref[...] = packs[...]
    send_ref[...] = sends[...].astype(BF16)


def unpack(packed):
    low = iota(packed.shape, 1) < HEAD_DIM
    even = jnp.where(low, packed, 0.0)
    odd = jnp.where(low, pltpu.roll(packed, HEAD_DIM, 1), 0.0)
    return jnp.concatenate([even, odd], axis=0)


def head_rows(heads):
    return [(h // 2) + SLOT * (h % 2) for h in range(heads)]


def token_of_column(heads, kv_local, columns):
    row = iota((ROWS, columns), 0)
    column = iota((ROWS, columns), 1)
    wanted = jnp.full((ROWS, columns), kv_local, jnp.int32)
    for h, place in enumerate(head_rows(heads)):
        wanted = jnp.where(row == place, h // (heads // kv_local), wanted)
    return jnp.where(column % kv_local == wanted, column // kv_local, 1 << 20)


def score_page(query, block):
    return lax.dot_general(query, block, NT, preferred_element_type=F32)


def weigh_page(scores, tokens, span):
    scores = jnp.where(tokens < span, scores, NEG_FILL)
    top = jnp.max(scores, axis=1, keepdims=True)
    weights = jnp.exp(scores - top)
    return top, jnp.sum(weights, axis=1, keepdims=True), weights.astype(BF16)


def attend_pages(
    stages, copies, query_of, block_of, span_of, tokens, keep, last=None
):
    def score_stage(i):
        if copies is not None:
            copies[i].wait()
        if last is not None and i == len(stages) - 1:
            last.wait()
        return {p: score_page(query_of(p), block_of(p)) for p in stages[i]}

    scores = score_stage(0)
    for i, pages in enumerate(stages):
        if i + 1 < len(stages):
            ahead = score_stage(i + 1)
        weighed = {p: weigh_page(scores[p], tokens, span_of(p)) for p in pages}
        outs = {
            p: jnp.dot(weighed[p][2], block_of(p), preferred_element_type=F32)
            for p in pages
        }
        for p in pages:
            keep(p, weighed[p][0], weighed[p][1], outs[p])
        if i + 1 < len(stages):
            scores = ahead


def spread_queries(target, packed):
    low = iota(packed.shape, 2) < HEAD_DIM
    target[:, 0:SLOT, :] = jnp.where(low, packed, 0.0)
    target[:, SLOT:ROWS, :] = jnp.where(low, pltpu.roll(packed, HEAD_DIM, 2), 0.0)


def merge_pages(places, top_of, sum_of, top, acc, scaled, start, before):
    requests = start.shape[0]
    for p, place in enumerate(places):
        top[place] = jnp.maximum(top[place], top_of(p))
    acc[0:requests] = start * jnp.exp(before - top[0:requests])
    for p, place in enumerate(places):
        scaled[p] = sum_of(p) * jnp.exp(top_of(p) - top[place])
    for p, place in enumerate(places):
        acc[place] = acc[place] + scaled[p]


WIDE = 1024


def repeat_lanes(values, heads, out_ref):
    part = WIDE // heads
    repeat = iota((part, WIDE), 1) // heads == iota((part, WIDE), 0)
    repeat = jnp.where(repeat, 1.0, 0.0).astype(BF16)
    parts = [values[:, i : i + part] for i in range(0, values.shape[1], part)]
    out_ref[...] = jnp.dot(
        jnp.concatenate(parts, axis=0), repeat, preferred_element_type=F32
    ).astype(BF16)


def project_heads(values, spread_ref, weights_ref, heads):
    if heads == 1:
        return jnp.dot(values, weights_ref[...], preferred_element_type=F32)
    rows = values.shape[0]
    lane = iota((1, WIDE), 1) % heads
    masks = [jnp.where(lane == k, 1.0, 0.0).astype(BF16) for k in range(heads)]
    total = jnp.zeros((heads * rows, LANES), F32)
    for i in range(weights_ref.shape[0] // WIDE):
        piece = spread_ref[i * rows : (i + 1) * rows, :]
        piece = jnp.concatenate([piece * mask for mask in masks], axis=0)
        total += jnp.dot(
            piece, weights_ref[i * WIDE : (i + 1) * WIDE, :], preferred_element_type=F32
        )
    return total


def local_kernel(
    heads, kv_local, meta_hbm, packed_hbm, normed_hbm, wkv_hbm, tables_hbm, cache_hbm,
    state_hbm,
    meta, packed, normed, raw, spread, tables, pages, queries, fresh, tops, sums, top, acc,
    scaled, sems,
):
    requests = normed.shape[0]
    count, columns, _ = pages.shape
    small = [
        copy_of(meta_hbm, meta, sems.at[0]),
        copy_of(packed_hbm, packed, sems.at[1]),
        copy_of(normed_hbm, normed, sems.at[2]),
        copy_of(tables_hbm, tables, sems.at[3]),
    ]
    weights = copy_of(wkv_hbm, raw, sems.at[4])
    stages = page_stages(count, 4, 12)
    paging = page_copies(cache_hbm, pages, stages, sems, 10)
    for copy in small + paging + [weights]:
        copy.start()
    tokens = token_of_column(heads, kv_local, columns)
    lower = iota((ROWS, LANES), 1) < HEAD_DIM
    low = iota((requests, LANES), 1) < HEAD_DIM
    low16 = iota((requests, ROWS, LANES), 2) < HEAD_DIM
    top[...] = jnp.full(top.shape, NEG_FILL, F32)
    acc[...] = jnp.zeros(acc.shape, F32)
    for copy in small:
        copy.wait()
    spread_queries(queries, packed[...].reshape(requests, SLOT, LANES))
    if kv_local > 1:
        repeat_lanes(normed[...], kv_local, spread)

    def place_of(p):
        owner = meta[0, p]
        return jnp.where(owner < 0, requests, owner)

    places = [place_of(p) for p in range(count)]

    def keep(p, page_top, total, out):
        tops[p] = jnp.broadcast_to(page_top, (ROWS, LANES))
        sums[p] = jnp.where(lower, total, out)
        top[places[p]] = jnp.maximum(top[places[p]], tops[p])

    attend_pages(
        stages,
        paging,
        lambda p: queries[jnp.maximum(meta[0, p], 0)].astype(BF16),
        lambda p: pages[p],
        lambda p: meta[1, p],
        tokens,
        keep,
        weights,
    )
    cosine = jnp.where(low, tables[0], 1.0)
    sine = jnp.where(low, tables[1], 0.0)
    projected = project_heads(normed[...], spread, raw, kv_local)
    new = [
        rotate(projected[k * requests : (k + 1) * requests], cosine, sine)
        .astype(BF16)
        .astype(F32)
        for k in range(kv_local)
    ]
    used = {place: h for h, place in enumerate(head_rows(heads))}
    for place in range(ROWS):
        value = jnp.zeros((requests, LANES), F32)
        if place in used:
            value = new[used[place] // (heads // kv_local)]
        fresh[pl.ds(place, requests, stride=ROWS), :] = value
    for p, place in enumerate(places):
        scaled[p] = sums[p] * jnp.exp(tops[p] - top[place])
    for p, place in enumerate(places):
        acc[place] = acc[place] + scaled[p]
    added = fresh[...].reshape(requests, ROWS, LANES)
    score = jnp.sum(queries[...] * added, axis=2, keepdims=True)
    score = jnp.broadcast_to(score, added.shape)
    parked = []
    step = requests // 4
    for i in range(4):
        rows = slice(i * step, (i + 1) * step)
        before, fresh_score = top[rows], score[rows]
        highest = jnp.maximum(before, fresh_score)
        whole = acc[rows] * jnp.exp(before - highest)
        whole += jnp.where(low16[rows], 1.0, added[rows]) * jnp.exp(fresh_score - highest)
        acc[rows] = jnp.where(
            low16[rows], highest + jnp.log(whole), whole / pltpu.roll(whole, HEAD_DIM, 2)
        )
        part = pl.ds(i * step, step)
        parked.append(copy_of(acc.at[part], state_hbm.at[part], sems.at[5 + i]))
        parked[i].start()
    for copy in parked:
        copy.wait()


def lent_kernel(
    heads, kv_local, asked_ref, pages, pick_ref, drop_ref, meta_ref, packed_ref,
    normed_ref, tables_ref, hidden_ref,
    reply_hbm, meta_hbm, packed_hbm, normed_hbm, tables_hbm, hidden_hbm,
    reply16, sems,
):
    outgoing, columns, _ = pages.shape
    parked = [
        copy_of(packed_ref, packed_hbm, sems.at[0]),
        copy_of(normed_ref, normed_hbm, sems.at[1]),
        copy_of(hidden_ref, hidden_hbm, sems.at[2]),
        copy_of(tables_ref, tables_hbm, sems.at[3]),
        copy_of(meta_ref, meta_hbm, sems.at[4]),
    ]
    for copy in parked:
        copy.start()
    slot_rows = asked_ref.shape[0]
    shape = (outgoing * SLOT, slot_rows)
    chosen = jnp.where(pick_ref[:, 0:1] == iota(shape, 1), 1.0, 0.0).astype(BF16)
    asked = jnp.dot(chosen, asked_ref[...], preferred_element_type=F32)
    tokens = token_of_column(heads, kv_local, columns).astype(F32)
    low = iota((SLOT, LANES), 1) < HEAD_DIM
    lane = iota((SLOT, LANES), 1)
    row = iota((SLOT, LANES), 0)

    def terms(total, offset):
        leading = total.astype(BF16).astype(F32)
        rest = total - leading
        second = rest.astype(BF16).astype(F32)
        third = rest - second
        spot = lane - offset - 3 * row
        placed = jnp.where(spot == 0, leading, 0.0)
        placed = jnp.where(spot == 1, second, placed)
        return jnp.where(spot == 2, third, placed)

    packed = [asked[j * SLOT : (j + 1) * SLOT] for j in range(outgoing)]
    replies = {}

    def keep(j, top, total, out):
        out = out / total
        logs = top + jnp.log(total)
        even = pltpu.roll(out[0:SLOT], HEAD_DIM, 1)
        both = jnp.where(low, even, out[SLOT:ROWS])
        line = jnp.sum(
            terms(logs[0:SLOT], 0) + terms(logs[SLOT:ROWS], HEAD_DIM), axis=0, keepdims=True
        )
        replies[j] = jnp.where(row == META, line, both)

    attend_pages(
        page_stages(outgoing, 8, 8),
        None,
        lambda j: unpack(packed[j]).astype(BF16),
        lambda j: pages[j],
        lambda j: packed[j][META : META + 1, 0:1],
        tokens,
        keep,
    )
    shape = (slot_rows, outgoing * SLOT)
    placed = jnp.where(drop_ref[0:1, :] == iota(shape, 0), 1.0, 0.0).astype(BF16)
    every = jnp.concatenate([replies[j] for j in range(outgoing)], axis=0).astype(BF16)
    reply = jnp.dot(placed, every, preferred_element_type=F32)
    reply16[...] = reply.astype(BF16)
    replying = copy_of(reply16, reply_hbm, sems.at[5])
    replying.start()
    for copy in parked + [replying]:
        copy.wait()


def combine_kernel(
    heads, pool, meta_hbm, state_hbm, wo_hbm, hidden_hbm, gain_hbm, router_hbm,
    routes_hbm, wd_hbm, reply_ref,
    part_ref, meta_ref, hidden_ref, gain_ref, router_ref, routes_ref, wd_ref,
    meta, state, wo, gain, tops, accs, scaled, reply, finals, sems,
):
    requests = state.shape[0]
    inbox = reply_ref.shape[0] // SLOT
    chunks = -(-heads // 2)
    numbers = copy_of(meta_hbm, meta, sems.at[11])
    arriving = copy_of(state_hbm, state, sems.at[0])
    weights = copies_of(wo_hbm, wo, sems, 1)
    gaining = copy_of(gain_hbm, gain, sems.at[5])
    later = [
        copy_of(meta_hbm, meta_ref, sems.at[6]),
        copy_of(hidden_hbm, hidden_ref, sems.at[7]),
        copy_of(router_hbm, router_ref, sems.at[8]),
        copy_of(routes_hbm, routes_ref, sems.at[9]),
        copy_of(wd_hbm.at[pl.ds(0, wd_ref.shape[0])], wd_ref, sems.at[10]),
    ]
    for copy in [numbers, arriving] + weights + [gaining] + later:
        copy.start()
    reply[...] = reply_ref[...].astype(F32)
    tops[...] = jnp.full(tops.shape, NEG_FILL, F32)
    accs[...] = jnp.zeros(accs.shape, F32)
    low = iota((SLOT, LANES), 1) < HEAD_DIM
    lane = iota((SLOT, LANES), 1)
    row = iota((SLOT, LANES), 0)
    mine = (lane % HEAD_DIM) // 3 == row

    def place_of(s):
        lender = s // CAP ^ (inbox // CAP // 2)
        owner = meta[0, pool + lender * CAP + s % CAP]
        return jnp.where(owner < 0, requests, owner)

    def logs_of(s):
        line = reply[s * SLOT + META : s * SLOT + META + 1, :]
        line = jnp.where(mine, jnp.broadcast_to(line, (SLOT, LANES)), 0.0)
        even = jnp.sum(jnp.where(low, line, 0.0), axis=1, keepdims=True)
        odd = jnp.sum(jnp.where(low, 0.0, line), axis=1, keepdims=True)
        logs = jnp.concatenate([even, odd], axis=0)
        return jnp.broadcast_to(logs, (ROWS, LANES))

    def sum_of(s):
        packed = reply[s * SLOT : (s + 1) * SLOT, :]
        even = jnp.where(low, 1.0, pltpu.roll(packed, HEAD_DIM, 1))
        odd = jnp.where(low, 1.0, packed)
        return jnp.concatenate([even, odd], axis=0)

    logs = [logs_of(s) for s in range(inbox)]
    numbers.wait()
    places = [place_of(s) for s in range(inbox)]
    for s, place in enumerate(places):
        tops[place] = jnp.maximum(tops[place], logs[s])
    for s, place in enumerate(places):
        scaled[s] = sum_of(s) * jnp.exp(logs[s] - tops[place])
    for s, place in enumerate(places):
        accs[place] = accs[place] + scaled[s]
    arriving.wait()
    low16 = iota(state.shape, 2) < HEAD_DIM
    start = state[...]
    before = jnp.where(low16, start, pltpu.roll(start, HEAD_DIM, 2))
    remote = tops[0:requests]
    highest = jnp.maximum(before, remote)
    whole = accs[0:requests] * jnp.exp(remote - highest)
    whole = whole + jnp.where(low16, 1.0, start) * jnp.exp(before - highest)
    finals[...] = (whole / pltpu.roll(whole, HEAD_DIM, 2)).reshape(
        requests * ROWS, LANES
    )
    wide = iota((requests, LANES), 1) < HEAD_DIM
    parts = []
    for j in range(chunks):
        even = finals[pl.ds(j, requests, stride=ROWS), :]
        odd = finals[pl.ds(SLOT + j, requests, stride=ROWS), :]
        parts.append(jnp.where(wide, pltpu.roll(even, HEAD_DIM, 1), odd).astype(BF16))
    attention = jnp.concatenate(parts, axis=1)[:, : heads * HEAD_DIM]
    for copy in weights:
        copy.wait()
    part_ref[...] = jnp.dot(attention, wo[...], preferred_element_type=F32).astype(BF16)
    gaining.wait()
    gain_ref[...] = gain[...].reshape(1, gain.shape[0])
    for copy in later:
        copy.wait()


def load_kernel(wd_hbm, order_hbm, wd_ref, sem):
    del order_hbm
    rows = wd_ref.shape[0]
    copy = copy_of(wd_hbm.at[pl.ds(wd_hbm.shape[0] - rows, rows)], wd_ref, sem)
    copy.start()
    copy.wait()


def finish_kernel(attended_ref, own_ref, other_ref, attended_out, experts_out):
    attended_out[...] = attended_ref[...]
    experts_out[...] = (own_ref[...] + other_ref[...].astype(F32)).astype(BF16)


def own_rows(values, first):
    half = values.shape[0] // 2
    return jnp.where(first, values[:half], values[half:])


def residual_kernel(
    tp, count, meta_ref, hidden_ref, *refs,
):
    pieces = refs[:count]
    gain_ref, attended_ref, input_ref, again_ref = refs[count:]
    requests = hidden_ref.shape[0]
    if count == 2:
        summed = pieces[0][...].astype(F32) + pieces[1][...].astype(F32)
    else:
        summed = pieces[0][0:requests, :].astype(F32)
        for t in range(1, tp):
            part = pieces[0][t * requests : (t + 1) * requests, :]
            summed = summed + part.astype(F32)
    attended = (hidden_ref[...].astype(F32) + RESID_SCALE * summed).astype(BF16)
    if count == 2:
        attended_ref[...] = own_rows(attended, meta_ref[3:4, 0:1] == 0)
    else:
        attended_ref[...] = attended
    ffn_input = norm_rows(attended.astype(F32), gain_ref[...])
    input_ref[...] = ffn_input
    again_ref[...] = ffn_input


def gate_column(units, meta_ref, input_ref, router_ref, routes_ref):
    ffn_input = input_ref[...]
    requests = ffn_input.shape[0]
    logits = lax.dot_general(router_ref[...], ffn_input, NT, preferred_element_type=F32)
    expert = iota(logits.shape, 0)
    named = jnp.zeros(logits.shape, F32)
    for k in range(routes_ref.shape[0]):
        named = jnp.where(routes_ref[k : k + 1, :] == expert, 1.0, named)
    chosen = named > 0.5
    top = jnp.max(jnp.where(chosen, logits, NEG_FILL), axis=0, keepdims=True)
    weights = jnp.where(chosen, jnp.exp(logits - top), 0.0)
    total = jnp.sum(weights, axis=0, keepdims=True)
    mine = expert == meta_ref[3:4, 0:1] * units // FF
    line = jnp.sum(jnp.where(mine, weights, 0.0), axis=0, keepdims=True) / total
    diagonal = iota((requests, requests), 0) == iota((requests, requests), 1)
    line = jnp.where(diagonal, jnp.broadcast_to(line, (requests, requests)), 0.0)
    return jnp.sum(line, axis=1, keepdims=True)


def expert_kernel(
    units, meta_ref, lifted_ref, input_ref, router_ref, routes_ref, wd_ref, wd_rest_ref,
    *outs
):
    column = gate_column(units, meta_ref, input_ref, router_ref, routes_ref)
    gate = lifted_ref[0]
    active = gate / (1.0 + jnp.exp(-gate)) * lifted_ref[1]
    active = active.astype(BF16)
    half = wd_ref.shape[0]
    share = jnp.dot(active[:, :half], wd_ref[...], preferred_element_type=F32)
    share += jnp.dot(active[:, half:], wd_rest_ref[...], preferred_element_type=F32)
    share *= column
    if len(outs) == 2:
        first = meta_ref[3:4, 0:1] == 0
        outs[0][...] = own_rows(share, first)
        outs[1][...] = own_rows(share, jnp.logical_not(first)).astype(BF16)
    else:
        outs[0][...] = share.astype(BF16)


def call(body, outs, in_specs, scratch=(), limit=16, flops=0, moved=0):
    return pl.pallas_call(
        body,
        out_shape=outs,
        in_specs=in_specs,
        out_specs=[VMEM if isinstance(o, jax.ShapeDtypeStruct) else HBM for o in outs],
        scratch_shapes=list(scratch),
        compiler_params=pltpu.CompilerParams(vmem_limit_bytes=limit << 20),
        cost_estimate=pl.CostEstimate(
            flops=flops, bytes_accessed=moved, transcendentals=0
        ),
    )


def swap(values):
    return lax.ppermute(values, "tensor", [(0, 1), (1, 0)])


def on_device(
    hidden,
    attn_gain,
    w_query,
    w_keyvalue,
    w_output,
    cache,
    page_table,
    ctx_len,
    move_dest,
    ffn_gain,
    router,
    routes,
    w_in,
    w_down,
):
    replicas = lax.axis_size("replica")
    tp = lax.axis_size("tensor")
    rank = lax.axis_index("tensor").astype(jnp.int32)
    rows, width = hidden.shape
    pool, page_len, kv_local, _ = cache.shape
    outgoing = move_dest.shape[0]
    local_pages = pool - outgoing
    requests = page_table.shape[0]
    heads = w_query.shape[1] // HEAD_DIM
    inbox = replicas * CAP
    units = w_down.shape[0]
    assert FF % units == 0
    columns = page_len * kv_local
    entries = -(-(pool + inbox) // LANES) * LANES
    struct = jax.ShapeDtypeStruct
    pair = tp == 2
    ids = rank.reshape(1)

    def pin(values):
        return pltpu.with_memory_space_constraint(values, pltpu.HBM)

    def exchange(blocks, order):
        blocks = blocks.reshape(replicas, CAP * SLOT, LANES)
        blocks = lax.all_to_all(
            blocks,
            "replica",
            split_axis=0,
            concat_axis=0,
            tiled=True,
            axis_index_groups=[list(order)],
        )
        return blocks.reshape(inbox * SLOT, LANES)

    blocks = pin(cache.reshape(pool, columns, LANES))
    if pair:
        pieces = [hidden, swap(hidden)]
    else:
        pieces = [lax.all_gather(hidden, "tensor", axis=0, tiled=True)]
    meta_shape = (4, entries)
    tables_shape = (2, requests, LANES)
    own, wq, gain, tables, away, away_span, meta, lent, pick, drop = call(
        functools.partial(prepare_kernel, pool, replicas),
        [
            struct(hidden.shape, BF16),
            struct(w_query.shape, BF16),
            struct((1, width), F32),
            struct(tables_shape, F32),
            struct((inbox, requests), BF16),
            struct((inbox, LANES), F32),
            struct(meta_shape, jnp.int32),
            struct((outgoing, columns, LANES), BF16),
            struct((outgoing * SLOT, LANES), jnp.int32),
            struct((outgoing, outgoing * SLOT), jnp.int32),
        ],
        [SMEM] + [HBM] * 7,
        [
            pltpu.VMEM((1, requests), jnp.int32),
            pltpu.VMEM((page_table.shape[1], requests), jnp.int32),
            pltpu.VMEM((1, outgoing), jnp.int32),
            pltpu.VMEM((width,), F32),
            pltpu.SemaphoreType.DMA((10,)),
        ],
        moved=2 * w_query.size,
    )(
        ids,
        pin(hidden),
        pin(ctx_len.reshape(1, requests)),
        pin(page_table.T),
        pin(move_dest.reshape(1, outgoing)),
        pin(attn_gain),
        pin(w_query),
        blocks,
    )
    if pair:
        pieces[0] = own
    hidden_all, normed, packed, sends = call(
        functools.partial(query_kernel, len(pieces)),
        [
            struct((requests, width), BF16),
            struct((requests, width), BF16),
            struct((requests * SLOT, LANES), F32),
            struct((inbox * SLOT, LANES), BF16),
        ],
        [VMEM] * (len(pieces) + 6),
        [
            pltpu.VMEM((requests * SLOT, LANES), F32),
            pltpu.VMEM((inbox * SLOT, LANES), F32),
        ],
        flops=4 * requests * width * w_query.shape[1],
        moved=2 * w_query.size,
    )(meta, *pieces, gain, wq, tables, away, away_span)
    asked = exchange(sends, range(replicas)[::-1])
    replies, meta_far, packed_far, normed_far, tables_far, hidden_far = call(
        functools.partial(lent_kernel, heads, kv_local),
        [
            pltpu.HBM((inbox * SLOT, LANES), BF16),
            pltpu.HBM(meta_shape, jnp.int32),
            pltpu.HBM((requests * SLOT, LANES), F32),
            pltpu.HBM((requests, width), BF16),
            pltpu.HBM(tables_shape, F32),
            pltpu.HBM((requests, width), BF16),
        ],
        [VMEM] * 9,
        [
            pltpu.VMEM((inbox * SLOT, LANES), BF16),
            pltpu.SemaphoreType.DMA((6,)),
        ],
        flops=4 * ROWS * columns * LANES * outgoing,
        moved=2 * columns * LANES * outgoing,
    )(asked, lent, pick, drop, meta, packed, normed, tables, hidden_all)
    returned = exchange(replies, [r ^ replicas // 2 for r in range(replicas)])
    (state,) = call(
        functools.partial(local_kernel, heads, kv_local),
        [pltpu.HBM((requests, ROWS, LANES), F32)],
        [HBM] * 6,
        [
            pltpu.SMEM(meta_shape, jnp.int32),
            pltpu.VMEM((requests * SLOT, LANES), F32),
            pltpu.VMEM((requests, width), BF16),
            pltpu.VMEM((width * kv_local, LANES), BF16),
            pltpu.VMEM((requests * width * kv_local // WIDE, WIDE), BF16),
            pltpu.VMEM(tables_shape, F32),
            pltpu.VMEM((local_pages, columns, LANES), BF16),
            pltpu.VMEM((requests, ROWS, LANES), F32),
            pltpu.VMEM((requests * ROWS, LANES), F32),
            pltpu.VMEM((local_pages, ROWS, LANES), F32),
            pltpu.VMEM((local_pages, ROWS, LANES), F32),
            pltpu.VMEM((requests + 1, ROWS, LANES), F32),
            pltpu.VMEM((requests + 1, ROWS, LANES), F32),
            pltpu.VMEM((local_pages, ROWS, LANES), F32),
            pltpu.SemaphoreType.DMA((10 + local_pages,)),
        ],
        limit=24,
        flops=4 * ROWS * columns * LANES * local_pages,
        moved=2 * columns * LANES * local_pages,
    )(
        pin(meta_far),
        pin(packed_far),
        pin(normed_far),
        pin(w_keyvalue.reshape(width * kv_local, LANES)),
        pin(tables_far),
        blocks,
    )
    half = struct((units // 2, width), BF16)
    part, meta, hidden_all, gain, router_t, routes_t, wd = call(
        functools.partial(combine_kernel, heads, pool),
        [
            struct((requests, width), BF16),
            struct(meta_shape, jnp.int32),
            struct((requests, width), BF16),
            struct((1, width), F32),
            struct(router.shape[::-1], BF16),
            struct(routes.shape[::-1], jnp.int32),
            half,
        ],
        [HBM] * 8 + [VMEM],
        [
            pltpu.SMEM(meta_shape, jnp.int32),
            pltpu.VMEM((requests, ROWS, LANES), F32),
            pltpu.VMEM(w_output.shape, BF16),
            pltpu.VMEM((width,), F32),
            pltpu.VMEM((requests + 1, ROWS, LANES), F32),
            pltpu.VMEM((requests + 1, ROWS, LANES), F32),
            pltpu.VMEM((inbox, ROWS, LANES), F32),
            pltpu.VMEM((inbox * SLOT, LANES), F32),
            pltpu.VMEM((requests * ROWS, LANES), F32),
            pltpu.SemaphoreType.DMA((12,)),
        ],
        flops=2 * requests * w_output.size,
        moved=2 * w_output.size,
    )(
        pin(meta_far), pin(state), pin(w_output), pin(hidden_far), pin(ffn_gain),
        pin(router.T), pin(routes.T), pin(w_down), returned,
    )
    if pair:
        parts = [part, swap(part)]
    else:
        parts = [lax.all_gather(part, "tensor", axis=0, tiled=True)]
    (wd_rest,) = call(
        load_kernel,
        [half],
        [HBM, ANY],
        [pltpu.SemaphoreType.DMA],
        moved=w_down.size,
    )(pin(w_down), part)
    attended, ffn_input, ffn_again = call(
        functools.partial(residual_kernel, tp, len(parts)),
        [
            struct((rows if pair else requests, width), BF16),
            struct((requests, width), BF16),
            struct((requests, width), BF16),
        ],
        [VMEM] * (len(parts) + 3),
        flops=2 * requests * width,
        moved=8 * requests * width,
    )(meta, hidden_all, *parts, gain)
    lifted = jnp.einsum("rd,dsu->sru", ffn_input, w_in, preferred_element_type=F32)
    shapes = [struct((requests, width), BF16)]
    if pair:
        shapes = [struct((rows, width), F32), struct((rows, width), BF16)]
    shares = call(
        functools.partial(expert_kernel, units),
        shapes,
        [VMEM] * 7,
        flops=2 * requests * w_down.size,
        moved=2 * w_down.size,
    )(meta, lifted, ffn_again, router_t, routes_t, wd, wd_rest)
    if pair:
        out = struct((rows, width), BF16)
        return tuple(
            call(finish_kernel, [out, out], [VMEM] * 3)(attended, shares[0], swap(shares[1]))
        )
    shares = lax.all_gather(shares[0], "tensor", axis=0)
    mine = lax.dynamic_slice_in_dim(shares, rank * rows, rows, axis=1)
    experts_out = jnp.sum(mine.astype(F32), axis=0).astype(BF16)
    attended = lax.dynamic_slice_in_dim(attended, rank * rows, rows, axis=0)
    return attended, experts_out


def solution(mesh):
    placed = (
        P(("replica", "tensor"), None),
        P(),
        P(None, "tensor"),
        P(None, "tensor", None),
        P("tensor", None),
        P("replica", None, "tensor", None),
        P("replica", None),
        P("replica"),
        P("replica"),
        P(),
        P(),
        P("replica", None),
        P(None, None, "tensor"),
        P("tensor", None),
    )
    return jax.shard_map(
        on_device,
        mesh=mesh,
        in_specs=placed,
        out_specs=(P(("replica", "tensor"), None), P(("replica", "tensor"), None)),
        check_vma=False,
    )
```
